32 devices in a mesh: dp: 4 (over z), tensor: 4 (over y, x), seq: 2 (over core).
Axes of the slice: x: 2, y: 2, z: 4, core: 2. Of those that a mesh axis runs over, the one named last changes fastest.
Arguments:
- token_ids: int32 [4, 1024], P('dp', 'seq'), may hold values from 0 to 50303
- labels: int32 [4, 1024], P('dp', 'seq'), may hold values from 0 to 50303
- real_counts: int32 [8], P(('dp', 'seq')), may hold values from 1 to 512, as said below
- owners: int32 [179], replicated, may hold values from 0 to 3, as said below
- master: float32 [268, 384, 768], P('dp', ('tensor', 'seq')), may hold values from -0.4330127 to 0.4330127
- first_moment: float32 [268, 384, 768], P('dp', ('tensor', 'seq')), may hold values from -9.536743e-07 to 9.536743e-07
- second_moment: float32 [268, 384, 768], P('dp', ('tensor', 'seq')), may hold values from 4.9252455e-14 to 3.9780828e-13
- gains: float32 [5, 768], replicated, may hold values from 0.25 to 1.75
- gains_first: float32 [5, 768], replicated, may hold values from -9.536743e-06 to 9.536743e-06
- gains_second: float32 [5, 768], replicated, may hold values from 4.9252455e-12 to 3.9780828e-11
- mix: float32 [5], replicated, may hold values from -0.5 to 1.3
- mix_first: float32 [5], replicated, may hold values from -9.1552734e-05 to 9.1552734e-05
- mix_second: float32 [5], replicated, may hold values from 4.925245e-10 to 3.9780828e-09
Outputs:
- new_master: float32 [268, 384, 768], P('dp', ('tensor', 'seq'))
- new_first: float32 [268, 384, 768], P('dp', ('tensor', 'seq'))
- new_second: float32 [268, 384, 768], P('dp', ('tensor', 'seq'))
- new_gains: float32 [5, 768], replicated
- new_gains_first: float32 [5, 768], replicated
- new_gains_second: float32 [5, 768], replicated
- new_mix: float32 [5], replicated
- new_mix_first: float32 [5], replicated
- new_mix_second: float32 [5], replicated
- loss_sum: float32 [], replicated
- token_count: float32 [], replicated
- clip_norm: float32 [], replicated
The draws below stay inside these ranges and needn't reach their ends.
Inputs may be any that keep to these rules, and one draw needn't show every extreme that they name: `owners`: each owner holds at most 67 row blocks and some owner holds exactly 67. `real_counts`: some device has all 512 tokens real.
All inputs are finite; a program needn't handle non-finite values.
Results may differ from the reference program's by a relative error of at most 0.023.
Values may be sent and summed in bfloat16 or wider, within the bound.
A program may use at most 384 MiB of HBM per device.

```python
import math
import jax
import jax.numpy as jnp
import numpy as np
from jax import lax

D = 768
HEADS = 12
HEAD_DIM = 64
FF = 3072
VOCAB = 50304
LAYERS = 2
SEQ_LEN = 1024
SEQS_DP = 1
BLOCK_ROWS = 96
STEP_COUNT = 10
GROUPS = 4
TENSORS = 4
SEQS = 4
HALF_LEN = 512
TOK_DEV = 512
ROW_BLOCKS = 179
OWNER_SLOTS = 67
PARAMS_ALL = 52789248
MIX_WEIGHTS = 5
N_DP = 4
N_TENSOR = 4


def owner_layout(key):
    heavy = jax.random.randint(jax.random.fold_in(key, 11), (), 0, GROUPS)
    offset = jax.random.randint(jax.random.fold_in(key, 12), (), 0, GROUPS - 1)
    order = jax.random.permutation(jax.random.fold_in(key, 13), ROW_BLOCKS)
    position = jnp.argsort(order).astype(jnp.int32)
    rest = (position - OWNER_SLOTS + offset) % (GROUPS - 1)
    other = rest + jnp.where(rest >= heavy, 1, 0)
    return jnp.where(position < OWNER_SLOTS, heavy, other).astype(jnp.int32)


def draw_owners(key, part):
    return owner_layout(key)


def draw_master(key, part):
    owners = owner_layout(key)
    key = jax.random.fold_in(key, 2)
    ranks = jnp.arange(ROW_BLOCKS)
    same = (owners[None, :] == owners[:, None]) & (ranks[None, :] < ranks[:, None])
    slot_rank = jnp.sum(jnp.where(same, 1, 0), axis=1).astype(jnp.int32)
    rise = 2.0
    head_rows = 3 * D // TENSORS
    out_rows = D // TENSORS
    unit_rows = FF // TENSORS
    layer_rows = head_rows + out_rows + 2 * unit_rows
    vocab_rows = VOCAB // TENSORS
    row_index = jnp.arange(ROW_BLOCKS * BLOCK_ROWS)[None, :]
    tensor_index = jnp.arange(TENSORS)[:, None]
    within = row_index % layer_rows
    layer_scale = jnp.where(within < head_rows, D ** (-0.5), jnp.where(within < head_rows + out_rows, 2.0 * D ** (-0.5), jnp.where(within < head_rows + out_rows + unit_rows, D ** (-0.5), 1.5 * FF ** (-0.5))))
    vocab_index = (tensor_index * vocab_rows + row_index - LAYERS * layer_rows).astype(jnp.float32)
    vocab_scale = (1.0 + rise * vocab_index / VOCAB) * D ** (-0.5)
    scales = jnp.where(row_index < LAYERS * layer_rows, layer_scale, vocab_scale).astype(jnp.float32)
    entries = jax.random.truncated_normal(jax.random.fold_in(key, 1), -4.0, 4.0, (TENSORS, ROW_BLOCKS * BLOCK_ROWS, D), jnp.float32)
    logical = (entries * scales[:, :, None]).reshape(TENSORS, ROW_BLOCKS, BLOCK_ROWS, D).transpose(1, 0, 2, 3)
    logical = logical.reshape(ROW_BLOCKS, TENSORS * BLOCK_ROWS, D)
    filler = jax.random.truncated_normal(jax.random.fold_in(key, 2), -4.0, 4.0, (GROUPS * OWNER_SLOTS, TENSORS * BLOCK_ROWS, D), jnp.float32) * D ** (-0.5)
    return filler.at[owners * OWNER_SLOTS + slot_rank].set(logical)


def draw_real_counts(key, part):
    key = jax.random.fold_in(key, 3)
    index = jnp.arange(GROUPS * 2)
    group = index // 2
    side = index % 2
    weight = (GROUPS - 1 + 2 * group) * (1 + 2 * side)
    ceiling = jnp.maximum(TOK_DEV * weight // (9 * (GROUPS - 1)), 1)
    bottom = jnp.minimum(ceiling // 2 + 1, ceiling)
    counts = jax.random.randint(key, (GROUPS * 2,), bottom, ceiling + 1)
    return jnp.where(index == GROUPS * 2 - 1, TOK_DEV, counts).astype(jnp.int32)


def draw_mix(key, part):
    key = jax.random.fold_in(key, 4)
    diagonal = np.zeros((MIX_WEIGHTS,), np.float32)
    for block in range(1, LAYERS + 1):
        diagonal[block * (block + 1) // 2 - 1 + block] = 1.0
    strong = jax.random.uniform(jax.random.fold_in(key, 1), (MIX_WEIGHTS,), jnp.float32, 0.7, 1.3)
    weak = jax.random.uniform(jax.random.fold_in(key, 2), (MIX_WEIGHTS,), jnp.float32, -0.5, 0.5)
    return jnp.where(jnp.asarray(diagonal) > 0.5, strong, weak)


def touch_ends(drawn, key, low, largest):
    spot = [jax.random.randint(jax.random.fold_in(key, axis), (), 0, length) for axis, length in enumerate(drawn.shape)]
    widest = drawn.shape.index(max(drawn.shape))
    neighbour = spot[:widest] + [(spot[widest] + 1) % drawn.shape[widest]] + spot[widest + 1:]
    return drawn.at[tuple(spot)].set(low).at[tuple(neighbour)].set(largest)


def block_scale(key, dims, cuts, smallest, largest):
    loudness, own = 1.0, jax.random.fold_in(key, 6)
    for dim, blocks in cuts:
        draws = jnp.exp(jax.random.uniform(jax.random.fold_in(own, dim), (blocks,), jnp.float32, smallest / len(cuts), largest / len(cuts)))
        loudness = loudness * jnp.repeat(draws, dims[dim] // blocks).reshape([-1 if axis == dim else 1 for axis in range(len(dims))])
    return loudness


def rank_table(count, slope):
    portions = [(1 << 20) // math.isqrt(standing ** slope) + 1 for standing in range(1, count + 1)]
    width = 1 + sum(portions) // (1 << 30)
    return np.cumsum(np.array([max(1, weight // width) for weight in portions]))


def skewed_ids(rng, shape, number_of, slope):
    grid = rank_table(number_of, slope)
    pick = jax.random.randint(jax.random.fold_in(rng, 1), shape, 0, int(grid[number_of - 1]))
    grade = jnp.searchsorted(jnp.asarray(grid, jnp.int32), pick, side="right")
    return jax.random.permutation(jax.random.fold_in(rng, 2), number_of)[grade].astype(jnp.int32)


def normal_values(key, shape, width, bound, cuts=(), held_as=jnp.bfloat16):
    values = width * jax.random.normal(key, shape, jnp.float32)
    if cuts:
        values = values * block_scale(key, shape, cuts, -0.22, 0.18)
    return jnp.clip(values, -bound, bound).astype(held_as)


def setup_inputs(seed: int = 0) -> dict:
    streams_of = jax.random.split(jax.random.key(seed), 14)
    token_ids = touch_ends(skewed_ids(streams_of[0], (SEQS, SEQ_LEN), VOCAB, 2), jax.random.fold_in(streams_of[0], 3), 0, VOCAB - 1).astype(jnp.int32)
    labels = touch_ends(skewed_ids(streams_of[1], (SEQS, SEQ_LEN), VOCAB, 2), jax.random.fold_in(streams_of[1], 3), 0, VOCAB - 1).astype(jnp.int32)
    real_counts = draw_real_counts(jax.random.fold_in(streams_of[13], 71), 0)
    owners = draw_owners(jax.random.fold_in(streams_of[13], 71), 0)
    master = draw_master(jax.random.fold_in(streams_of[13], 71), 0)
    first_moment = normal_values(streams_of[5], (N_DP * OWNER_SLOTS, N_TENSOR * BLOCK_ROWS, D), (0.0011 / PARAMS_ALL ** 0.5), 9.5367431640625e-07, ((0, 4), (1, 8)), jnp.float32)
    second_moment = jnp.clip(jnp.exp(math.log(3.9780827828898857e-13) - 2.089011 * jax.random.uniform(streams_of[6], (N_DP * OWNER_SLOTS, N_TENSOR * BLOCK_ROWS, D), jnp.float32) ** block_scale(streams_of[6], (N_DP * OWNER_SLOTS, N_TENSOR * BLOCK_ROWS, D), ((0, 4), (1, 8)), -0.2, 0.2)), 4.92524552771819e-14, 3.9780827828898857e-13)
    gains = jnp.clip(1.0 + 0.15 * jax.random.normal(streams_of[7], (2 * LAYERS + 1, D), jnp.float32), 0.25, 1.75)
    gains_first = normal_values(streams_of[8], (2 * LAYERS + 1, D), (0.011 / PARAMS_ALL ** 0.5), 9.5367431640625e-06, (), jnp.float32)
    gains_second = jnp.clip(jnp.exp(jax.random.uniform(streams_of[9], (2 * LAYERS + 1, D), jnp.float32, math.log(4.9252455412707175e-12), math.log(3.9780827937319074e-11))), 4.9252455412707175e-12, 3.9780827937319074e-11)
    mix = draw_mix(jax.random.fold_in(streams_of[13], 71), 0)
    mix_first = normal_values(streams_of[11], (MIX_WEIGHTS,), (0.11 / PARAMS_ALL ** 0.5), 9.1552734375e-05, (), jnp.float32)
    mix_second = jnp.clip(jnp.exp(jax.random.uniform(streams_of[12], (MIX_WEIGHTS,), jnp.float32, math.log(4.925245211673257e-10), math.log(3.978082752098544e-09))), 4.925245211673257e-10, 3.978082752098544e-09)
    return {"token_ids": token_ids, "labels": labels, "real_counts": real_counts, "owners": owners, "master": master, "first_moment": first_moment, "second_moment": second_moment, "gains": gains, "gains_first": gains_first, "gains_second": gains_second, "mix": mix, "mix_first": mix_first, "mix_second": mix_second}


EPS_NORM = 1e-05
CLIP_NORM = 0.01
BETA_ONE = 0.9
BETA_TWO = 0.95
ADAM_EPS = 1e-08
RATE_MATRIX = 0.04
RATE_SMALL = 0.4
DECAY_MATRIX = 0.1
HIGHEST = lax.Precision.HIGHEST

@jax.custom_vjp
def low(v):
    return lax.optimization_barrier(v.astype(jnp.bfloat16)).astype(jnp.float32)

@jax.custom_vjp
def low_back(v):
    return v

def low_keep(v):
    return (low(v), None)

def low_pass(kept, grad):
    return (grad,)

def back_keep(v):
    return (v, None)

def back_low(kept, grad):
    return (low(grad),)
low.defvjp(low_keep, low_pass)
low_back.defvjp(back_keep, back_low)

def matmul(left, right):
    return jnp.dot(left, right, precision=HIGHEST, preferred_element_type=jnp.float32)

def layer_norm(stream, gain):
    center = stream - lax.optimization_barrier(jnp.mean(stream, -1, keepdims=True))
    spread = lax.optimization_barrier(jnp.mean(center * center, -1, keepdims=True))
    return center * lax.rsqrt(spread + EPS_NORM) * gain

def rotary(positions):
    steps_half = jnp.arange(HEAD_DIM // 2).astype(jnp.float32)
    freqs = 10000.0 ** (-2.0 * steps_half / HEAD_DIM)
    angles = positions.astype(jnp.float32)[:, None] * freqs[None, :]
    return (jnp.cos(angles)[:, None, :], jnp.sin(angles)[:, None, :])

def rotate(tensor, cosine, sine):
    first, second = jnp.split(tensor, 2, axis=-1)
    return jnp.concatenate([first * cosine - second * sine, second * cosine + first * sine], axis=-1)

def slot_table(owners):
    ranks = jnp.arange(owners.shape[0])
    same = (owners[None, :] == owners[:, None]) & (ranks[None, :] < ranks[:, None])
    return lax.optimization_barrier(jnp.sum(jnp.where(same, 1, 0), axis=1)).astype(jnp.int32)

def unpack(master, owners):
    layout = master[owners * OWNER_SLOTS + slot_table(owners)]
    layout = layout.reshape(ROW_BLOCKS, N_TENSOR, BLOCK_ROWS, D).transpose(1, 0, 2, 3)
    layout = layout.reshape(N_TENSOR, ROW_BLOCKS * BLOCK_ROWS, D)
    head_rows = 3 * D // N_TENSOR
    out_rows = D // N_TENSOR
    unit_rows = FF // N_TENSOR
    layer_rows = head_rows + out_rows + 2 * unit_rows
    stacked = layout[:, :LAYERS * layer_rows].reshape(N_TENSOR, LAYERS, layer_rows, D)
    joined = stacked[:, :, :head_rows].reshape(N_TENSOR, LAYERS, 3, D // N_TENSOR, D)
    joined = joined.transpose(1, 2, 0, 3, 4).reshape(LAYERS, 3 * D, D)

    def take_part(start, extent, total):
        return stacked[:, :, start:start + extent].transpose(1, 0, 2, 3).reshape(LAYERS, total, D)
    out_w = take_part(head_rows, out_rows, D)
    up_w = take_part(head_rows + out_rows, unit_rows, FF)
    down_w = take_part(head_rows + out_rows + unit_rows, unit_rows, FF)
    table = layout[:, LAYERS * layer_rows:].reshape(VOCAB, D)
    return (joined, out_w, up_w, down_w, table)

def head_loss(rows_final, labels_block, keep_block, table):
    logits = low_back(matmul(rows_final, table.T))
    spread = jax.scipy.special.logsumexp(logits, axis=-1)
    target = jnp.take_along_axis(logits, labels_block[:, None], axis=-1)[:, 0]
    return jnp.sum((spread - target) * keep_block)

def sequence_loss(weights, token_row, label_row, keep_row):
    qkv_w, out_w, up_w, down_w, table, gains, mix = weights
    cosine, sine = rotary(jnp.arange(SEQ_LEN))
    causal = jnp.arange(SEQ_LEN)[None, :] <= jnp.arange(SEQ_LEN)[:, None]
    states = [table[token_row]]
    stream = states[0]
    for level in range(LAYERS):
        normed = low(layer_norm(stream, gains[2 * level]))
        joined = low_back(matmul(normed, qkv_w[level].T))
        queries = low(rotate(joined[:, :D].reshape(SEQ_LEN, HEADS, HEAD_DIM), cosine, sine))
        keys_all = low(rotate(joined[:, D:2 * D].reshape(SEQ_LEN, HEADS, HEAD_DIM), cosine, sine))
        values_all = low(joined[:, 2 * D:].reshape(SEQ_LEN, HEADS, HEAD_DIM))
        scores = jnp.einsum('qhd,khd->hqk', queries, keys_all, precision=HIGHEST) * HEAD_DIM ** (-0.5)
        scores = low_back(scores)
        probs = jax.nn.softmax(jnp.where(causal[None], scores, -1e+30), axis=-1)
        attended = jnp.einsum('hqk,khd->qhd', low(probs), values_all, precision=HIGHEST).reshape(SEQ_LEN, D)
        attended = low(low_back(attended))
        inner = stream + low_back(matmul(attended, out_w[level]))
        normed_two = low(layer_norm(inner, gains[2 * level + 1]))
        hidden = low_back(matmul(normed_two, up_w[level].T))
        inner = inner + low_back(matmul(low(jax.nn.gelu(hidden, approximate=True)), down_w[level]))
        states.append(inner)
        base = (level + 1) * (level + 2) // 2 - 1
        stream = mix[base] * states[0]
        for source in range(1, level + 2):
            stream = stream + mix[base + source] * states[source]
    final = low(layer_norm(stream, gains[2 * LAYERS]))
    block_len = min(256, SEQ_LEN)

    def head_block(total, item):
        return (total + jax.checkpoint(head_loss)(item[0], item[1], item[2], table), None)
    items = (final.reshape(-1, block_len, D), label_row.reshape(-1, block_len), keep_row.reshape(-1, block_len))
    total, _ = lax.scan(head_block, jnp.zeros((), jnp.float32), items)
    return total

def adam_update(weight, first, second, grad, rate, decay):
    first = BETA_ONE * first + (1.0 - BETA_ONE) * grad
    second = BETA_TWO * second + (1.0 - BETA_TWO) * grad * grad
    first_hat = first / (1.0 - BETA_ONE ** STEP_COUNT)
    second_hat = second / (1.0 - BETA_TWO ** STEP_COUNT)
    weight = weight - rate * (first_hat / (jnp.sqrt(second_hat) + ADAM_EPS) + decay * weight)
    return (weight, first, second)

def reference(token_ids, labels, real_counts, owners, master, first_moment, second_moment, gains, gains_first, gains_second, mix, mix_first, mix_second):
    seq_index = jnp.arange(SEQS)[:, None]
    place = jnp.arange(SEQ_LEN)[None, :]
    group = seq_index // SEQS_DP
    within = seq_index % SEQS_DP
    local_row = within * HALF_LEN + place % HALF_LEN
    limit = real_counts[(group * 2 + place // HALF_LEN).astype(jnp.int32)]
    keep = jnp.where(local_row < limit, 1.0, 0.0).astype(jnp.float32)

    def total_loss(master_w, gain_w, mix_w):
        qkv_w, out_w, up_w, down_w, table = unpack(master_w, owners)
        weights = (low(qkv_w), low(out_w), low(up_w), low(down_w), low(table), gain_w, mix_w)

        def one_sequence(total, item):
            return (total + jax.checkpoint(sequence_loss)(weights, item[0], item[1], item[2]), None)
        total, _ = lax.scan(one_sequence, jnp.zeros((), jnp.float32), (token_ids, labels, keep))
        return total
    loss_sum, pullback = jax.vjp(total_loss, master, gains, mix)
    grad_master, grad_gains, grad_mix = pullback(jnp.ones((), jnp.float32))
    token_count = jnp.sum(real_counts).astype(jnp.float32)
    grad_master = grad_master / token_count
    grad_gains = grad_gains / token_count
    grad_mix = grad_mix / token_count
    squares = jnp.sum(grad_master * grad_master) + jnp.sum(grad_gains * grad_gains) + jnp.sum(grad_mix * grad_mix)
    clip_norm = jnp.sqrt(squares)
    factor = jnp.minimum(1.0, CLIP_NORM / clip_norm)
    new_master, new_first, new_second = adam_update(master, first_moment, second_moment, grad_master * factor, RATE_MATRIX, DECAY_MATRIX)
    new_gains, new_gains_first, new_gains_second = adam_update(gains, gains_first, gains_second, grad_gains * factor, RATE_SMALL, 0.0)
    new_mix, new_mix_first, new_mix_second = adam_update(mix, mix_first, mix_second, grad_mix * factor, RATE_SMALL, 0.0)
    return (new_master, new_first, new_second, new_gains, new_gains_first, new_gains_second, new_mix, new_mix_first, new_mix_second, loss_sum, token_count, clip_norm)
```

```python
from functools import partial

import jax
import jax.numpy as jnp
from jax import lax
from jax.experimental import pallas as pl
from jax.experimental.pallas import tpu as pltpu
from jax.sharding import PartitionSpec as P

D = 768
HEADS = 12
HEAD_DIM = 64
FF = 3072
VOCAB = 50304
LAYERS = 2
STEP_COUNT = 10
MIX_WEIGHTS = 5


EPS_NORM = 1e-05
CLIP_NORM = 0.01
BETA_ONE = 0.9
BETA_TWO = 0.95
ADAM_EPS = 1e-08
RATE_MATRIX = 0.04
RATE_SMALL = 0.4
DECAY_MATRIX = 0.1


def from_behind(block, axis, distance):
    devices = range(lax.axis_size(axis))
    route = [(i - distance, i) for i in devices if i - distance in devices]
    return lax.ppermute(block, axis, route)


def contract_last(left, right):
    return lax.dot_general(
        left, right, (((1,), (1,)), ((), ())), preferred_element_type=jnp.float32
    )


def contract_first(left, right):
    return lax.dot_general(
        left, right, (((0,), (0,)), ((), ())), preferred_element_type=jnp.float32
    )


def normalize(stream):
    center = stream - jnp.mean(stream, -1, keepdims=True)
    inverse = lax.rsqrt(jnp.mean(center * center, -1, keepdims=True) + EPS_NORM)
    return (center * inverse, inverse)


def norm_back(grad_normed, gain, scaled, inverse):
    grad_scaled = grad_normed * gain
    grad_stream = inverse * (
        grad_scaled
        - jnp.mean(grad_scaled, -1, keepdims=True)
        - scaled * jnp.mean(grad_scaled * scaled, -1, keepdims=True)
    )
    return (grad_stream, jnp.sum(grad_normed * scaled, axis=0))


def rotary(positions):
    steps_half = jnp.arange(HEAD_DIM // 2).astype(jnp.float32)
    freqs = 10000.0 ** (-2.0 * steps_half / HEAD_DIM)
    angles = positions.astype(jnp.float32)[:, None] * freqs[None, :]
    return (jnp.cos(angles)[:, None, :], jnp.sin(angles)[:, None, :])


def rotate(tensor, cosine, sine):
    first, second = jnp.split(tensor, 2, axis=-1)
    return jnp.concatenate(
        [first * cosine - second * sine, second * cosine + first * sine], axis=-1
    )


def slot_table(owners):
    ranks = jnp.arange(owners.shape[0])
    same = (owners[None, :] == owners[:, None]) & (ranks[None, :] < ranks[:, None])
    return jnp.sum(jnp.where(same, 1, 0), axis=1).astype(jnp.int32)


def attention_scores(queries, keys_all, allowed):
    raw = jnp.einsum(
        "bqhd,bkhd->bhqk", queries, keys_all, preferred_element_type=jnp.float32
    ) * HEAD_DIM ** (-0.5)
    return jnp.where(allowed[None, None], raw, -1e30)


def adam_update(weight, first, second, grad, rate, decay):
    first = BETA_ONE * first + (1.0 - BETA_ONE) * grad
    second = BETA_TWO * second + (1.0 - BETA_TWO) * grad * grad
    first_hat = first / (1.0 - BETA_ONE**STEP_COUNT)
    second_hat = second / (1.0 - BETA_TWO**STEP_COUNT)
    weight = weight - rate * (first_hat / (jnp.sqrt(second_hat) + ADAM_EPS) + decay * weight)
    return (weight, first, second)


MESH = pl.DeviceIdType.MESH
ROW_STEP = 256
TILE_GROUPS = 4
LANES = 128


def meet(peers):
    gate = pltpu.get_barrier_semaphore()
    for peer in peers:
        pl.semaphore_signal(gate, inc=1, device_id=peer, device_id_type=MESH)
    pl.semaphore_wait(gate, len(peers))


def others(axis):
    count, me = lax.axis_size(axis), lax.axis_index(axis)
    return [lax.rem(me + step, count) for step in range(1, count)]


def behind(axis, step):
    count, me = lax.axis_size(axis), lax.axis_index(axis)
    return lax.rem(me + count - step, count)


def send(source, target, send_sem, recv_sem, device):
    copy = pltpu.make_async_remote_copy(
        src_ref=source,
        dst_ref=target,
        send_sem=send_sem,
        recv_sem=recv_sem,
        device_id=device,
        device_id_type=MESH,
    )
    copy.start()
    return copy


def layer_norm_parts(stream):
    center = stream - jnp.mean(stream, -1, keepdims=True)
    inverse = lax.rsqrt(jnp.mean(center * center, -1, keepdims=True) + EPS_NORM)
    return center * inverse, inverse


def norm_pull(grad_normed, gain, stream):
    scaled, inverse = layer_norm_parts(stream)
    grad_scaled = grad_normed * gain
    grad_stream = inverse * (
        grad_scaled
        - jnp.mean(grad_scaled, -1, keepdims=True)
        - scaled * jnp.mean(grad_scaled * scaled, -1, keepdims=True)
    )
    return grad_stream, jnp.sum(grad_normed * scaled, axis=0, keepdims=True)


def tensor_step(name, function, partial, extras, scalars, outs, gather, collective_id):
    parts = lax.axis_size("tensor")
    share = extras[0].shape[0]
    reduce = partial is not None

    def kernel(*refs):
        refs = list(refs)
        partial_ref = refs.pop(0) if reduce else None
        extra_refs = [refs.pop(0) for _ in extras]
        scalar_refs = [refs.pop(0) for _ in scalars]
        out_refs = [refs.pop(0) for _ in outs]
        full = refs.pop(0) if gather else None
        outgoing = refs.pop(0) if reduce else None
        arrived = refs.pop(0) if reduce else None
        send_sems, recv_sems = refs
        me = lax.axis_index("tensor")
        peers = others("tensor")
        meet([{"tensor": peer} for peer in peers])
        total = None
        if reduce:
            copies = []
            for step, peer in enumerate(peers):
                rows = pl.ds(pl.multiple_of(peer * share, share), share)
                outgoing[step] = partial_ref[rows, :].astype(jnp.bfloat16)
                copies.append(
                    send(
                        outgoing.at[step],
                        arrived.at[step],
                        send_sems.at[0, step],
                        recv_sems.at[0, step],
                        {"tensor": peer},
                    )
                )
            total = partial_ref[pl.ds(pl.multiple_of(me * share, share), share), :]
            for step, copy in enumerate(copies):
                copy.wait()
                total = total + arrived[step].astype(jnp.float32)
        results = function(total, *[ref[...] for ref in extra_refs], *scalar_refs)
        for ref, value in zip(out_refs, results):
            ref[...] = value.astype(ref.dtype)
        if gather:
            full[me] = results[len(outs)].astype(jnp.bfloat16)
            copies = [
                send(
                    full.at[me],
                    full.at[me],
                    send_sems.at[1, step],
                    recv_sems.at[1, step],
                    {"tensor": peer},
                )
                for step, peer in enumerate(peers)
            ]
            for copy in copies:
                copy.wait()

    vmem = pl.BlockSpec(memory_space=pltpu.VMEM)
    smem = pl.BlockSpec(memory_space=pltpu.SMEM)
    shapes = [jax.ShapeDtypeStruct(shape, dtype) for shape, dtype in outs]
    if gather:
        shapes.append(jax.ShapeDtypeStruct((parts, share, D), jnp.bfloat16))
    buffers = [pltpu.VMEM((parts - 1, share, D), jnp.bfloat16)] * (2 if reduce else 0)
    operands = ([partial] if reduce else []) + list(extras) + list(scalars)
    return pl.pallas_call(
        kernel,
        name=name,
        out_shape=shapes,
        in_specs=[vmem] * (len(operands) - len(scalars)) + [smem] * len(scalars),
        out_specs=[vmem] * len(shapes),
        scratch_shapes=buffers + [pltpu.SemaphoreType.DMA((2, parts - 1))] * 2,
        compiler_params=pltpu.CompilerParams(
            collective_id=collective_id, has_side_effects=True, vmem_limit_bytes=40 << 20
        ),
    )(*operands)


def reduce_all(terms, collective_id):
    _, tensors, groups, count, _ = terms.shape

    def kernel(
        terms_ref, out_ref, near, own, mid, mid_in, far, far_in,
        own_sems, near_send, near_recv, mid_send, mid_recv, far_send, far_recv,
    ):
        group, part, side = lax.axis_index("dp"), lax.axis_index("tensor"), lax.axis_index("seq")
        twin = 1 - side
        parts = others("tensor")
        order = others("dp") + [group]
        meet(
            [{"seq": twin}]
            + [{"tensor": peer} for peer in parts]
            + [{"dp": peer} for peer in order[:-1]]
        )
        waits, near_copies, own_copies = [], [], []
        for place, target in enumerate(order):
            near_copies.append(
                send(
                    terms_ref.at[twin, :, target],
                    near.at[place],
                    near_send.at[place],
                    near_recv.at[place],
                    {"seq": twin},
                )
            )
            copy = pltpu.make_async_copy(
                terms_ref.at[side, :, target], own.at[place], own_sems.at[place]
            )
            copy.start()
            own_copies.append(copy)
        mid_copies = []
        for place in range(groups):
            near_copies[place].wait_recv()
            own_copies[place].wait()
            for slot in range(tensors):
                mid[place, slot] = (
                    own[place, slot].astype(jnp.float32) + near[place, slot].astype(jnp.float32)
                ).astype(jnp.bfloat16)
            mid_copies.append(
                [
                    send(
                        mid.at[place, peer],
                        mid_in.at[place, step],
                        mid_send.at[place, step],
                        mid_recv.at[place, step],
                        {"tensor": peer},
                    )
                    for step, peer in enumerate(parts)
                ]
            )
        far_copies = []
        for place, target in enumerate(order):
            total = mid[place, part].astype(jnp.float32)
            for step in range(tensors - 1):
                mid_copies[place][step].wait_recv()
                total = total + mid_in[place, step].astype(jnp.float32)
            if place < groups - 1:
                far[place] = total.astype(jnp.bfloat16)
                far_copies.append(
                    send(
                        far.at[place],
                        far_in.at[place],
                        far_send.at[place],
                        far_recv.at[place],
                        {"dp": target},
                    )
                )
        for place, copy in enumerate(far_copies):
            copy.wait_recv()
            total = total + far_in[place].astype(jnp.float32)
        out_ref[...] = total
        for copy in near_copies + far_copies + [c for row in mid_copies for c in row]:
            copy.wait_send()

    block = (count, D)
    dma = pltpu.SemaphoreType.DMA
    return pl.pallas_call(
        kernel,
        name="reduce_all",
        out_shape=jax.ShapeDtypeStruct(block, jnp.float32),
        in_specs=[pl.BlockSpec(memory_space=pl.ANY)],
        out_specs=pl.BlockSpec(memory_space=pltpu.VMEM),
        scratch_shapes=[pltpu.VMEM((groups, tensors) + block, jnp.bfloat16)] * 3
        + [
            pltpu.VMEM((groups, tensors - 1) + block, jnp.bfloat16),
            pltpu.VMEM((groups,) + block, jnp.bfloat16),
            pltpu.VMEM((groups,) + block, jnp.bfloat16),
            dma((groups,)),
            dma((groups,)),
            dma((groups,)),
            dma((groups, tensors - 1)),
            dma((groups, tensors - 1)),
            dma((groups,)),
            dma((groups,)),
        ],
        compiler_params=pltpu.CompilerParams(
            collective_id=collective_id, has_side_effects=True, vmem_limit_bytes=56 << 20
        ),
    )(terms)


def gather_all(block, collective_id):
    tensors, groups = lax.axis_size("tensor"), lax.axis_size("dp")

    def kernel(block_ref, out, own_sem, far_send, far_recv, mid_send, mid_recv, near_send, near_recv):
        group, part, side = lax.axis_index("dp"), lax.axis_index("tensor"), lax.axis_index("seq")
        twin = 1 - side
        parts = others("tensor")
        meet(
            [{"seq": twin}]
            + [{"tensor": peer} for peer in parts]
            + [{"dp": peer} for peer in others("dp")]
        )
        far_copies = [
            send(
                block_ref,
                out.at[side, part, group],
                far_send.at[step],
                far_recv.at[step],
                {"dp": peer},
            )
            for step, peer in enumerate(others("dp"))
        ]
        own = pltpu.make_async_copy(block_ref, out.at[side, part, group], own_sem)
        own.start()
        own.wait()
        mid_copies, near_copies = [], []
        for place in range(groups):
            source = behind("dp", place)
            if place:
                far_copies[place - 1].wait_recv()
            held = out.at[side, part, source]
            mid_copies.append(
                [
                    send(held, held, mid_send.at[place, step], mid_recv.at[place, step], {"tensor": peer})
                    for step, peer in enumerate(parts)
                ]
            )
            near_copies.append(
                send(held, held, near_send.at[place, 0], near_recv.at[place, 0], {"seq": twin})
            )
        for place in range(groups):
            source = behind("dp", place)
            for step in range(tensors - 1):
                mid_copies[place][step].wait_recv()
                held = out.at[side, behind("tensor", step + 1), source]
                near_copies.append(
                    send(
                        held,
                        held,
                        near_send.at[place, step + 1],
                        near_recv.at[place, step + 1],
                        {"seq": twin},
                    )
                )
        for copy in near_copies:
            copy.wait_recv()
        for copy in near_copies + far_copies + [c for row in mid_copies for c in row]:
            copy.wait_send()

    dma = pltpu.SemaphoreType.DMA
    return pl.pallas_call(
        kernel,
        name="gather_all",
        out_shape=jax.ShapeDtypeStruct((2, tensors, groups) + block.shape, block.dtype),
        in_specs=[pl.BlockSpec(memory_space=pl.ANY)],
        out_specs=pl.BlockSpec(memory_space=pl.ANY),
        scratch_shapes=[
            dma,
            dma((groups - 1,)),
            dma((groups - 1,)),
            dma((groups, tensors - 1)),
            dma((groups, tensors - 1)),
            dma((groups, tensors)),
            dma((groups, tensors)),
        ],
        compiler_params=pltpu.CompilerParams(collective_id=collective_id, has_side_effects=True),
    )(block)


def reduce_rows(terms, collective_id):
    count, groups = terms.shape[3], terms.shape[2]
    pieces = max(1, groups // 4)
    part = count // pieces
    sums = [
        reduce_all(terms[:, :, :, i * part : (i + 1) * part] if pieces > 1 else terms, collective_id)
        for i in range(pieces)
    ]
    return jnp.concatenate(sums, axis=0) if pieces > 1 else sums[0]


def join_stats(stats, collective_id):
    _, tensors, groups, _, _ = stats.shape

    def join(left, right):
        top = jnp.maximum(left[..., 0:1, :], right[..., 0:1, :])
        total = left[..., 1:2, :] * jnp.exp(left[..., 0:1, :] - top) + right[..., 1:2, :] * jnp.exp(
            right[..., 0:1, :] - top
        )
        return jnp.concatenate(
            [top, total, left[..., 2:3, :] + right[..., 2:3, :], left[..., 3:, :]], axis=-2
        )

    def kernel(
        stats_ref, home, full, near, mid, mid_in, far, far_in,
        near_send, near_recv, mid_send, mid_recv, far_send, far_recv,
    ):
        group, part, side = lax.axis_index("dp"), lax.axis_index("tensor"), lax.axis_index("seq")
        twin = 1 - side
        parts, groups_else = others("tensor"), others("dp")
        meet(
            [{"seq": twin}]
            + [{"tensor": peer} for peer in parts]
            + [{"dp": peer} for peer in groups_else]
        )
        copy = send(stats_ref.at[twin], near, near_send.at[0], near_recv.at[0], {"seq": twin})
        copy.wait()
        for slot in range(tensors):
            for spot in range(groups):
                mid[slot, spot] = join(stats_ref[side, slot, spot], near[slot, spot])
        copies = [
            send(mid.at[peer], mid_in.at[step], mid_send.at[0, step], mid_recv.at[0, step], {"tensor": peer})
            for step, peer in enumerate(parts)
        ]
        for copy in copies:
            copy.wait()
        for spot in range(groups):
            total = mid[part, spot]
            for step in range(tensors - 1):
                total = join(total, mid_in[step, spot])
            far[spot] = total
        copies = [
            send(far.at[peer], far_in.at[step], far_send.at[0, step], far_recv.at[0, step], {"dp": peer})
            for step, peer in enumerate(groups_else)
        ]
        total = far[group]
        for step, copy in enumerate(copies):
            copy.wait()
            total = join(total, far_in[step])
        log_total = total[0:1] + jnp.log(total[1:2])
        home[...] = jnp.concatenate([log_total, total[2:3], total[2:]], axis=0)
        full[side, part, group] = jnp.broadcast_to(log_total, (8, LANES))
        held = full.at[side, part, group]
        copies = [
            send(held, held, far_send.at[1, step], far_recv.at[1, step], {"dp": peer})
            for step, peer in enumerate(groups_else)
        ]
        for copy in copies:
            copy.wait()
        held = full.at[side, part]
        copies = [
            send(held, held, mid_send.at[1, step], mid_recv.at[1, step], {"tensor": peer})
            for step, peer in enumerate(parts)
        ]
        for copy in copies:
            copy.wait()
        held = full.at[side]
        send(held, held, near_send.at[1], near_recv.at[1], {"seq": twin}).wait()

    tile = (8, LANES)
    dma = pltpu.SemaphoreType.DMA
    vmem = pl.BlockSpec(memory_space=pltpu.VMEM)
    return pl.pallas_call(
        kernel,
        name="join_stats",
        out_shape=[
            jax.ShapeDtypeStruct(tile, jnp.float32),
            jax.ShapeDtypeStruct(stats.shape, jnp.float32),
        ],
        in_specs=[vmem],
        out_specs=[vmem, vmem],
        scratch_shapes=[
            pltpu.VMEM((tensors, groups) + tile, jnp.float32),
            pltpu.VMEM((tensors, groups) + tile, jnp.float32),
            pltpu.VMEM((tensors - 1, groups) + tile, jnp.float32),
            pltpu.VMEM((groups,) + tile, jnp.float32),
            pltpu.VMEM((groups - 1,) + tile, jnp.float32),
            dma((2,)),
            dma((2,)),
            dma((2, tensors - 1)),
            dma((2, tensors - 1)),
            dma((2, groups - 1)),
            dma((2, groups - 1)),
        ],
        compiler_params=pltpu.CompilerParams(collective_id=collective_id, has_side_effects=True),
    )(stats)


def sum_small(block, collective_id):
    tensors, groups = lax.axis_size("tensor"), lax.axis_size("dp")

    def kernel(block_ref, out, near, mid, far, near_send, near_recv, mid_send, mid_recv, far_send, far_recv):
        group, part, side = lax.axis_index("dp"), lax.axis_index("tensor"), lax.axis_index("seq")
        parts, groups_else = others("tensor"), others("dp")
        meet(
            [{"seq": 1 - side}]
            + [{"tensor": peer} for peer in parts]
            + [{"dp": peer} for peer in groups_else]
        )
        stages = [
            ("seq", near, side, [1 - side], near_send, near_recv),
            ("tensor", mid, part, parts, mid_send, mid_recv),
            ("dp", far, group, groups_else, far_send, far_recv),
        ]
        total = block_ref[...]
        for axis, slots, me, peers, send_sems, recv_sems in stages:
            slots[me] = total
            copies = [
                send(slots.at[me], slots.at[me], send_sems.at[step], recv_sems.at[step], {axis: peer})
                for step, peer in enumerate(peers)
            ]
            for copy in copies:
                copy.wait()
            total = slots[0]
            for index in range(1, slots.shape[0]):
                total = total + slots[index]
        out[...] = total

    dma = pltpu.SemaphoreType.DMA
    vmem = pl.BlockSpec(memory_space=pltpu.VMEM)
    return pl.pallas_call(
        kernel,
        name="sum_small",
        out_shape=jax.ShapeDtypeStruct(block.shape, jnp.float32),
        in_specs=[vmem],
        out_specs=vmem,
        scratch_shapes=[
            pltpu.VMEM((2,) + block.shape, jnp.float32),
            pltpu.VMEM((tensors,) + block.shape, jnp.float32),
            pltpu.VMEM((groups,) + block.shape, jnp.float32),
            dma((1,)),
            dma((1,)),
            dma((tensors - 1,)),
            dma((tensors - 1,)),
            dma((groups - 1,)),
            dma((groups - 1,)),
        ],
        compiler_params=pltpu.CompilerParams(collective_id=collective_id, has_side_effects=True),
    )(block)


def row_of(groups_ref):
    return jnp.concatenate([groups_ref[0, g : g + 1, :] for g in range(TILE_GROUPS)], axis=1)


def stat_row(stat_ref, row):
    return jnp.concatenate([stat_ref[g, row : row + 1, :] for g in range(TILE_GROUPS)], axis=1)


def chunk_of(step):
    return pl.ds(pl.multiple_of(step * ROW_STEP, ROW_STEP), ROW_STEP)


def whole(shape):
    return pl.BlockSpec(shape, lambda step, span: (0,) * len(shape), pipeline_mode=pl.Buffered(1))


TILE = TILE_GROUPS * LANES
TOKENS_SPEC = pl.BlockSpec((1, TILE_GROUPS, LANES), lambda step, span: (step, 0, 0))
STATS_SPEC = pl.BlockSpec((TILE_GROUPS, 8, LANES), lambda step, span: (step, 0, 0))
ROWS_SPEC = pl.BlockSpec((TILE, D), lambda step, span: (step, 0))


def local_call(name, kernel, steps, span, operands, in_specs, out_shape, out_specs, scratch):
    return pl.pallas_call(
        kernel,
        name=name,
        grid_spec=pltpu.PrefetchScalarGridSpec(
            num_scalar_prefetch=1,
            grid=(steps,),
            in_specs=in_specs,
            out_specs=out_specs,
            scratch_shapes=scratch,
        ),
        out_shape=out_shape,
        compiler_params=pltpu.CompilerParams(vmem_limit_bytes=56 << 20),
    )(span, *operands)


def look_up(span, row_ids, tokens, table_t):
    rows = table_t.shape[1]
    steps = tokens.shape[0]

    def kernel(span_ref, ids_ref, tokens_ref, table_ref, out_ref, acc):
        acc[...] = jnp.zeros_like(acc)
        wanted = row_of(tokens_ref)

        def one(step, carry):
            chunk = chunk_of(step)
            hits = jnp.where(ids_ref[chunk, :] == wanted, 1.0, 0.0).astype(jnp.bfloat16)
            acc[...] += jnp.dot(table_ref[:, chunk], hits, preferred_element_type=jnp.float32)
            return carry

        lax.fori_loop(span_ref[0], span_ref[1], one, 0)
        out_ref[...] = acc[...].T.astype(jnp.bfloat16)

    return local_call(
        "look_up",
        kernel,
        steps,
        span,
        (row_ids, tokens, table_t),
        [whole((rows, 1)), TOKENS_SPEC, whole((D, rows))],
        jax.ShapeDtypeStruct((steps * TILE, D), jnp.bfloat16),
        ROWS_SPEC,
        [pltpu.VMEM((D, TILE), jnp.float32)],
    )


def head_forward(span, row_ids, labels, table, final):
    rows = table.shape[0]
    steps = labels.shape[0]

    def kernel(span_ref, ids_ref, labels_ref, table_ref, final_ref, powers_ref, stats_ref, scores):
        wanted = row_of(labels_ref)
        hidden = final_ref[...]

        def first(step, carry):
            top, target = carry
            chunk = chunk_of(step)
            ids = ids_ref[chunk, :]
            raw = contract_last(table_ref[chunk, :], hidden)
            raw = jnp.where(ids >= 0, raw, -1e30)
            scores[chunk, :] = raw
            top = jnp.maximum(top, jnp.max(raw, axis=0, keepdims=True))
            target = target + jnp.sum(jnp.where(ids == wanted, raw, 0.0), axis=0, keepdims=True)
            return (top, target)

        blank = jnp.zeros((1, TILE), jnp.float32)
        top, target = lax.fori_loop(span_ref[0], span_ref[1], first, (blank - 1e30, blank))

        def second(step, total):
            chunk = chunk_of(step)
            powers = jnp.exp(scores[chunk, :] - top)
            powers_ref[chunk, :] = powers.astype(jnp.bfloat16)
            return total + jnp.sum(powers, axis=0, keepdims=True)

        total = lax.fori_loop(span_ref[0], span_ref[1], second, blank)
        rest = jnp.zeros((5, LANES), jnp.float32)
        for g in range(TILE_GROUPS):
            lanes = slice(g * LANES, (g + 1) * LANES)
            stats_ref[g] = jnp.concatenate(
                [top[:, lanes], total[:, lanes], target[:, lanes], rest], axis=0
            )

    return local_call(
        "head_forward",
        kernel,
        steps,
        span,
        (row_ids, labels, table, final),
        [whole((rows, 1)), TOKENS_SPEC, whole((rows, D)), ROWS_SPEC],
        [
            jax.ShapeDtypeStruct((rows, steps * TILE), jnp.bfloat16),
            jax.ShapeDtypeStruct((steps * TILE_GROUPS, 8, LANES), jnp.float32),
        ],
        [pl.BlockSpec((rows, TILE), lambda step, span: (0, step)), STATS_SPEC],
        [pltpu.VMEM((rows, TILE), jnp.float32)],
    )


def head_backward(span, row_ids, labels, keep, stats, log_totals, table_t, final, powers):
    rows = table_t.shape[1]
    steps = labels.shape[0]

    def kernel(
        span_ref, ids_ref, labels_ref, keep_ref, stats_ref, logs_ref, table_ref, final_ref,
        powers_ref, grad_final_ref, grad_table_ref, acc,
    ):
        @pl.when(pl.program_id(0) == 0)
        def _():
            grad_table_ref[...] = jnp.zeros_like(grad_table_ref)

        acc[...] = jnp.zeros_like(acc)
        wanted, kept = row_of(labels_ref), row_of(keep_ref)
        scale = jnp.exp(stat_row(stats_ref, 0) - stat_row(logs_ref, 0)) * kept
        hidden = final_ref[...]

        def one(step, carry):
            chunk = chunk_of(step)
            grads = powers_ref[chunk, :].astype(jnp.float32) * scale
            grads = grads - jnp.where(ids_ref[chunk, :] == wanted, kept, 0.0)
            grads = grads.astype(jnp.bfloat16)
            grad_table_ref[chunk, :] += jnp.dot(grads, hidden, preferred_element_type=jnp.float32)
            acc[...] += jnp.dot(table_ref[:, chunk], grads, preferred_element_type=jnp.float32)
            return carry

        lax.fori_loop(span_ref[0], span_ref[1], one, 0)
        grad_final_ref[...] = acc[...].T.astype(jnp.bfloat16)

    return local_call(
        "head_backward",
        kernel,
        steps,
        span,
        (row_ids, labels, keep, stats, log_totals, table_t, final, powers),
        [
            whole((rows, 1)),
            TOKENS_SPEC,
            TOKENS_SPEC,
            STATS_SPEC,
            STATS_SPEC,
            whole((D, rows)),
            ROWS_SPEC,
            pl.BlockSpec((rows, TILE), lambda step, span: (0, step)),
        ],
        [
            jax.ShapeDtypeStruct((steps * TILE, D), jnp.bfloat16),
            jax.ShapeDtypeStruct((rows, D), jnp.float32),
        ],
        [ROWS_SPEC, whole((rows, D))],
        [pltpu.VMEM((D, TILE), jnp.float32)],
    )


def look_back(span, row_ids, tokens, grad_start, grad_table):
    rows = grad_table.shape[0]
    steps = tokens.shape[0]

    def kernel(span_ref, ids_ref, tokens_ref, grad_ref, table_ref, out_ref):
        @pl.when(pl.program_id(0) == 0)
        def _():
            out_ref[...] = table_ref[...]

        wanted = row_of(tokens_ref)
        grads = grad_ref[...]

        def one(step, carry):
            chunk = chunk_of(step)
            hits = jnp.where(ids_ref[chunk, :] == wanted, 1.0, 0.0).astype(jnp.bfloat16)
            out_ref[chunk, :] += jnp.dot(hits, grads, preferred_element_type=jnp.float32)
            return carry

        lax.fori_loop(span_ref[0], span_ref[1], one, 0)

    return local_call(
        "look_back",
        kernel,
        steps,
        span,
        (row_ids, tokens, grad_start, grad_table),
        [whole((rows, 1)), TOKENS_SPEC, ROWS_SPEC, whole((rows, D))],
        jax.ShapeDtypeStruct((rows, D), jnp.float32),
        whole((rows, D)),
        [],
    )


def attend(joined, geometry):
    cosine, sine, allowed, seq_count, half_len, local_heads = geometry
    width = local_heads * HEAD_DIM
    shape_four = (seq_count, half_len, local_heads, HEAD_DIM)
    queries = (
        rotate(joined[:, :width].reshape(-1, local_heads, HEAD_DIM), cosine, sine)
        .astype(jnp.bfloat16)
        .reshape(shape_four)
    )
    own_keys = (
        rotate(joined[:, width : 2 * width].reshape(-1, local_heads, HEAD_DIM), cosine, sine)
        .astype(jnp.bfloat16)
        .reshape(shape_four)
    )
    own_values = joined[:, 2 * width :].astype(jnp.bfloat16).reshape(shape_four)
    far_keys, far_values = from_behind((own_keys, own_values), "seq", 1)
    keys_all = jnp.concatenate([far_keys, own_keys], axis=1)
    values_all = jnp.concatenate([far_values, own_values], axis=1)
    scores = attention_scores(queries, keys_all, allowed)
    peak = jnp.max(scores, -1, keepdims=True)
    log_total = peak + jnp.log(jnp.sum(jnp.exp(scores - peak), -1, keepdims=True))
    probs = jnp.exp(scores - log_total).astype(jnp.bfloat16)
    attended = jnp.einsum("bhqk,bkhd->bqhd", probs, values_all, preferred_element_type=jnp.float32)
    attended = attended.astype(jnp.bfloat16).reshape(-1, width)
    return attended, (queries, keys_all, values_all, log_total)


def attend_back(grad_attended, kept, geometry):
    queries, keys_all, values_all, log_total = kept
    cosine, sine, allowed, seq_count, half_len, local_heads = geometry
    width = local_heads * HEAD_DIM
    grad_attended = grad_attended.reshape(seq_count, half_len, local_heads, HEAD_DIM)
    probs = jnp.exp(attention_scores(queries, keys_all, allowed) - log_total)
    grad_probs = jnp.einsum(
        "bqhd,bkhd->bhqk", grad_attended, values_all, preferred_element_type=jnp.float32
    )
    grad_scores = (probs * (grad_probs - jnp.sum(probs * grad_probs, -1, keepdims=True))).astype(
        jnp.bfloat16
    )
    scale = HEAD_DIM ** (-0.5)
    grad_queries = (
        jnp.einsum("bhqk,bkhd->bqhd", grad_scores, keys_all, preferred_element_type=jnp.float32)
        * scale
    )
    grad_keys = (
        jnp.einsum("bhqk,bqhd->bkhd", grad_scores, queries, preferred_element_type=jnp.float32)
        * scale
    )
    grad_values = jnp.einsum(
        "bhqk,bqhd->bkhd",
        probs.astype(jnp.bfloat16),
        grad_attended,
        preferred_element_type=jnp.float32,
    )
    back_keys, back_values = (
        from_behind(grad_keys[:, :half_len].astype(jnp.bfloat16), "seq", -1).astype(jnp.float32),
        from_behind(grad_values[:, :half_len].astype(jnp.bfloat16), "seq", -1).astype(jnp.float32),
    )
    grad_keys = grad_keys[:, half_len:] + back_keys
    grad_values = grad_values[:, half_len:] + back_values
    return jnp.concatenate(
        [
            rotate(grad_queries.reshape(-1, local_heads, HEAD_DIM), cosine, -sine).reshape(
                -1, width
            ),
            rotate(grad_keys.reshape(-1, local_heads, HEAD_DIM), cosine, -sine).reshape(-1, width),
            grad_values.reshape(-1, width),
        ],
        axis=1,
    ).astype(jnp.bfloat16)


def body(
    token_ids,
    labels,
    real_counts,
    owners,
    master,
    first_moment,
    second_moment,
    gains,
    gains_first,
    gains_second,
    mix,
    mix_first,
    mix_second,
):
    tensors = lax.axis_size("tensor")
    groups = lax.axis_size("dp")
    group = lax.axis_index("dp")
    tensor_part = lax.axis_index("tensor")
    seq_part = lax.axis_index("seq")
    slots, half_rows, _ = master.shape
    seq_count, half_len = token_ids.shape
    row_count = seq_count * half_len
    share = row_count // tensors
    head_rows = 3 * D // tensors
    out_rows = D // tensors
    unit_rows = FF // tensors
    layer_rows = head_rows + out_rows + 2 * unit_rows
    layer_blocks = layer_rows // (2 * half_rows)
    blocks = LAYERS * layer_blocks
    vocab_rows = VOCAB // tensors
    local_heads = HEADS // tensors

    slot_rank = slot_table(owners)
    block_ids = jnp.arange(owners.shape[0], dtype=jnp.int32)
    mine = owners == group
    match = (jnp.arange(slots)[:, None] == slot_rank[None, :]) & mine[None, :]
    slot_block = jnp.sum(jnp.where(match, block_ids[None, :] + 1, 0), axis=1) - 1
    row_ids = (
        tensor_part * vocab_rows
        + (slot_block[:, None] - blocks) * (2 * half_rows)
        + seq_part * half_rows
        + jnp.arange(half_rows, dtype=jnp.int32)[None, :]
    )
    row_ids = jnp.where(slot_block[:, None] >= blocks, row_ids, -1).reshape(-1, 1)
    rows = slots * half_rows
    padded = -(-rows // ROW_STEP) * ROW_STEP
    row_ids = jnp.pad(row_ids, ((0, padded - rows), (0, 0)), constant_values=-1)
    held = jnp.sum(jnp.where(mine, 1, 0)) * half_rows
    first_held = jnp.sum(jnp.where(mine & (block_ids < blocks), 1, 0)) * half_rows
    span = jnp.stack([first_held // ROW_STEP, (held + ROW_STEP - 1) // ROW_STEP]).astype(jnp.int32)

    packed = jnp.concatenate([token_ids.reshape(-1), labels.reshape(-1), real_counts])
    packed = lax.all_gather(packed, ("dp", "seq")).reshape(groups, 2, -1)

    def by_home(tokens):
        tokens = tokens.reshape(groups, 2, tensors, share).transpose(1, 2, 0, 3)
        return tokens.reshape(-1, TILE_GROUPS, LANES)

    ids_all = by_home(packed[:, :, :row_count])
    labels_all = by_home(packed[:, :, row_count : 2 * row_count])
    counts_all = packed[:, :, 2 * row_count]
    token_count = jnp.sum(counts_all).astype(jnp.float32)
    keep_all = by_home(
        jnp.where(jnp.arange(row_count)[None, None, :] < counts_all[:, :, None], 1.0, 0.0)
    )
    order = (2, tensors, groups, share)

    master_low = master.astype(jnp.bfloat16)
    table = jnp.pad(master_low.reshape(rows, D), ((0, padded - rows), (0, 0)))
    table_t = table.T

    weights_all = []
    for level in range(LAYERS):
        chosen = slice(level * layer_blocks, (level + 1) * layer_blocks)
        own = jnp.where(
            mine[chosen][:, None, None], jnp.take(master_low, slot_rank[chosen], axis=0), 0.0
        ).astype(jnp.bfloat16)
        own = lax.psum(own, "dp")
        own = lax.all_gather(own, "seq", axis=1).reshape(layer_rows, D)
        cut_one, cut_two = head_rows + out_rows, head_rows + out_rows + unit_rows
        weights_all.append(
            (own[:head_rows], own[head_rows:cut_one], own[cut_one:cut_two], own[cut_two:])
        )

    positions = seq_part * half_len + jnp.arange(row_count) % half_len
    cosine, sine = rotary(positions)
    query_pos = seq_part * half_len + jnp.arange(half_len)
    key_pos = jnp.concatenate([(seq_part - 1) * half_len + jnp.arange(half_len), query_pos])
    allowed = (key_pos[None, :] <= query_pos[:, None]) & (key_pos[None, :] >= 0)
    geometry = (cosine, sine, allowed, seq_count, half_len, local_heads)

    looked = look_up(span, row_ids, ids_all, table_t).reshape(order + (D,))
    start = reduce_rows(looked, 0)
    gain = [gains[i : i + 1] for i in range(2 * LAYERS + 1)]
    piece = ((share, D), jnp.float32)

    def normed_of(total, stream, gain_row):
        return (layer_norm_parts(stream)[0] * gain_row,)

    def inner_of(total, stream, gain_row):
        inner = stream + total
        return (inner, layer_norm_parts(inner)[0] * gain_row)

    def outcome_of(base, total, inner, gain_row, *rest):
        states, scalars = rest[:-1], rest[-1]
        outcome = inner + total
        stream = scalars[base + len(states)] * outcome
        for source, state in enumerate(states):
            stream = stream + scalars[base + source] * state
        return (outcome, stream, layer_norm_parts(stream)[0] * gain_row)

    (normed,) = tensor_step("normed", normed_of, None, (start, gain[0]), (), [], True, 1)
    states, streams, inners, kept_all = [start], [start], [], []
    for level in range(LAYERS):
        qkv_w, out_w, up_w, down_w = weights_all[level]
        normed = normed.reshape(row_count, D)
        attended, kept = attend(contract_last(normed, qkv_w), geometry)
        inner, normed_two = tensor_step(
            "inner",
            inner_of,
            jnp.dot(attended, out_w, preferred_element_type=jnp.float32),
            (streams[level], gain[2 * level + 1]),
            (),
            [piece],
            True,
            2,
        )
        normed_two = normed_two.reshape(row_count, D)
        hidden = contract_last(normed_two, up_w)
        activated = jax.nn.gelu(hidden, approximate=True).astype(jnp.bfloat16)
        last = level == LAYERS - 1
        results = tensor_step(
            f"outcome_{level}",
            partial(outcome_of, (level + 1) * (level + 2) // 2 - 1),
            jnp.dot(activated, down_w, preferred_element_type=jnp.float32),
            [inner, gain[2 * level + 2]] + states,
            (mix,),
            [piece, piece] + ([((share, D), jnp.bfloat16)] if last else []),
            not last,
            3 + level,
        )
        inners.append(inner)
        kept_all.append((normed, kept, attended, normed_two, hidden, activated))
        states.append(results[0])
        streams.append(results[1])
        normed = results[2]

    final_all = gather_all(normed, 3 + LAYERS).reshape(-1, D)
    powers, stats = head_forward(span, row_ids, labels_all, table, final_all)
    home, log_totals = join_stats(
        stats.reshape((2, tensors, groups, 8, LANES)), 4 + LAYERS
    )
    keep = jnp.where(
        tensor_part * share + jnp.arange(share) < real_counts[0], 1.0, 0.0
    ).astype(jnp.float32)
    loss_local = jnp.sum((home[0] - home[1]) * keep)
    grad_final, grad_table = head_backward(
        span,
        row_ids,
        labels_all,
        keep_all,
        stats,
        log_totals.reshape(-1, 8, LANES),
        table_t,
        final_all,
        powers,
    )
    grad_final = reduce_rows(grad_final.reshape(order + (D,)), 0)

    row = ((1, D), jnp.float32)

    def top_of(total, grad, stream, gain_row, scalars):
        grad_top, grad_gain = norm_pull(grad, gain_row, stream)
        grad_state = scalars[MIX_WEIGHTS - 1] * grad_top
        return (grad_top, grad_state, grad_gain, grad_state)

    def inner_back(total, grad_out, inner, gain_row):
        grad, grad_gain = norm_pull(total, gain_row, inner)
        grad = grad_out + grad
        return (grad, grad_gain, grad)

    def stream_back(block, total, grad_inner, stream, gain_row, *rest):
        grad_ys, scalars = rest[:-1], rest[-1]
        grad, grad_gain = norm_pull(total, gain_row, stream)
        grad = grad_inner + grad
        state = grad if block == 0 else scalars[block * (block + 1) // 2 - 1 + block] * grad
        for offset, grad_y in enumerate(grad_ys):
            later = block + 1 + offset
            state = state + scalars[later * (later + 1) // 2 - 1 + block] * grad_y
        return (grad, state, grad_gain, state)

    grad_ys = [None] * (LAYERS + 1)
    gain_grads = [None] * (2 * LAYERS + 1)
    layer_grads = [None] * LAYERS
    grad_ys[LAYERS], grad_state, gain_grads[2 * LAYERS], grad_branch = tensor_step(
        "top_back",
        top_of,
        None,
        (grad_final, streams[LAYERS], gain[2 * LAYERS]),
        (mix,),
        [piece, piece, row],
        True,
        5 + LAYERS,
    )
    for level in reversed(range(LAYERS)):
        qkv_w, out_w, up_w, down_w = weights_all[level]
        normed, kept, attended, normed_two, hidden, activated = kept_all[level]
        grad_branch = grad_branch.reshape(row_count, D)
        grad_act = contract_last(grad_branch, down_w)
        _, gelu_pull = jax.vjp(partial(jax.nn.gelu, approximate=True), hidden)
        grad_hidden = gelu_pull(grad_act)[0].astype(jnp.bfloat16)
        grad_inner, gain_grads[2 * level + 1], grad_attn = tensor_step(
            "inner_back",
            inner_back,
            jnp.dot(grad_hidden, up_w, preferred_element_type=jnp.float32),
            (grad_state, inners[level], gain[2 * level + 1]),
            (),
            [piece, row],
            True,
            6 + LAYERS,
        )
        grad_attn = grad_attn.reshape(row_count, D)
        grad_attended = contract_last(grad_attn, out_w).astype(jnp.bfloat16)
        grad_joined = attend_back(grad_attended, kept, geometry)
        results = tensor_step(
            f"stream_back_{level}",
            partial(stream_back, level),
            jnp.dot(grad_joined, qkv_w, preferred_element_type=jnp.float32),
            [grad_inner, streams[level], gain[2 * level]] + grad_ys[level + 1 :],
            (mix,),
            [piece, piece, row] + ([] if level else [((share, D), jnp.bfloat16)]),
            level > 0,
            7 + LAYERS + level,
        )
        grad_ys[level], grad_state, gain_grads[2 * level] = results[:3]
        branch_before, grad_branch = grad_branch, results[3]
        grads = jnp.concatenate(
            [
                contract_first(grad_joined, normed),
                contract_first(attended, grad_attn),
                contract_first(grad_hidden, normed_two),
                contract_first(activated, branch_before),
            ],
            axis=0,
        ).astype(jnp.bfloat16)
        grads = lax.psum_scatter(
            grads.reshape(layer_blocks, 2, half_rows, D), "seq", scatter_dimension=1, tiled=False
        )
        layer_grads[level] = lax.psum(grads, "dp")

    grad_mix = [None] * MIX_WEIGHTS
    for later in range(1, LAYERS + 1):
        for block in range(later + 1):
            grad_mix[later * (later + 1) // 2 - 1 + block] = jnp.sum(grad_ys[later] * states[block])

    grad_start_all = gather_all(grad_branch, 3 + LAYERS).reshape(-1, D)
    grad_table = look_back(span, row_ids, ids_all, grad_start_all, grad_table)
    layer_grad = jnp.concatenate(layer_grads, axis=0)
    placed = jnp.take(layer_grad, jnp.clip(slot_block, 0, blocks - 1), axis=0).astype(jnp.float32)
    owned = jnp.where(
        ((slot_block >= 0) & (slot_block < blocks))[:, None, None],
        placed,
        grad_table[:rows].reshape(slots, half_rows, D),
    )
    small = jnp.concatenate([jnp.stack(grad_mix), loss_local[None], jnp.sum(owned * owned)[None]])
    small = jnp.concatenate(
        [
            jnp.concatenate(gain_grads, axis=0),
            jnp.pad(small, (0, D - small.shape[0]))[None],
            jnp.zeros((7 - 2 * LAYERS - 1, D), jnp.float32),
        ],
        axis=0,
    )
    small = sum_small(small, 7 + 2 * LAYERS)
    gain_total = small[: 2 * LAYERS + 1]
    mix_total = small[2 * LAYERS + 1, :MIX_WEIGHTS]
    loss_sum = small[2 * LAYERS + 1, MIX_WEIGHTS]
    squares = small[2 * LAYERS + 1, MIX_WEIGHTS + 1]
    clip_norm = (
        jnp.sqrt(squares + jnp.sum(gain_total * gain_total) + jnp.sum(mix_total * mix_total))
        / token_count
    )
    factor = jnp.minimum(1.0, CLIP_NORM / clip_norm) / token_count
    new_master, new_first, new_second = adam_update(
        master, first_moment, second_moment, owned * factor, RATE_MATRIX, DECAY_MATRIX
    )
    new_gains, new_gains_first, new_gains_second = adam_update(
        gains, gains_first, gains_second, gain_total * factor, RATE_SMALL, 0.0
    )
    new_mix, new_mix_first, new_mix_second = adam_update(
        mix, mix_first, mix_second, mix_total * factor, RATE_SMALL, 0.0
    )
    return (
        new_master,
        new_first,
        new_second,
        new_gains,
        new_gains_first,
        new_gains_second,
        new_mix,
        new_mix_first,
        new_mix_second,
        loss_sum,
        token_count,
        clip_norm,
    )


def solution(mesh):
    return jax.shard_map(
        body,
        mesh=mesh,
        in_specs=(
            P("dp", "seq"),
            P("dp", "seq"),
            P(("dp", "seq")),
            P(),
            P("dp", ("tensor", "seq"), None),
            P("dp", ("tensor", "seq"), None),
            P("dp", ("tensor", "seq"), None),
            P(),
            P(),
            P(),
            P(),
            P(),
            P(),
        ),
        out_specs=(
            P("dp", ("tensor", "seq"), None),
            P("dp", ("tensor", "seq"), None),
            P("dp", ("tensor", "seq"), None),
            P(),
            P(),
            P(),
            P(),
            P(),
            P(),
            P(),
            P(),
            P(),
        ),
        check_vma=False,
    )
```

```python
from functools import partial

import jax
import jax.numpy as jnp
from jax import lax
from jax.experimental import pallas as pl
from jax.experimental.pallas import tpu as pltpu
from jax.sharding import PartitionSpec as P

D = 768
HEADS = 12
HEAD_DIM = 64
FF = 3072
VOCAB = 50304
LAYERS = 2
STEP_COUNT = 10
MIX_WEIGHTS = 5


EPS_NORM = 1e-05
CLIP_NORM = 0.01
BETA_ONE = 0.9
BETA_TWO = 0.95
ADAM_EPS = 1e-08
RATE_MATRIX = 0.04
RATE_SMALL = 0.4
DECAY_MATRIX = 0.1


def from_behind(block, axis, distance):
    devices = range(lax.axis_size(axis))
    route = [(i - distance, i) for i in devices if i - distance in devices]
    return lax.ppermute(block, axis, route)


def contract_last(left, right):
    return lax.dot_general(
        left, right, (((1,), (1,)), ((), ())), preferred_element_type=jnp.float32
    )


def contract_first(left, right):
    return lax.dot_general(
        left, right, (((0,), (0,)), ((), ())), preferred_element_type=jnp.float32
    )


def normalize(stream):
    center = stream - jnp.mean(stream, -1, keepdims=True)
    inverse = lax.rsqrt(jnp.mean(center * center, -1, keepdims=True) + EPS_NORM)
    return (center * inverse, inverse)


def norm_back(grad_normed, gain, scaled, inverse):
    grad_scaled = grad_normed * gain
    grad_stream = inverse * (
        grad_scaled
        - jnp.mean(grad_scaled, -1, keepdims=True)
        - scaled * jnp.mean(grad_scaled * scaled, -1, keepdims=True)
    )
    return (grad_stream, jnp.sum(grad_normed * scaled, axis=0))


def rotary(positions):
    steps_half = jnp.arange(HEAD_DIM // 2).astype(jnp.float32)
    freqs = 10000.0 ** (-2.0 * steps_half / HEAD_DIM)
    angles = positions.astype(jnp.float32)[:, None] * freqs[None, :]
    return (jnp.cos(angles)[:, None, :], jnp.sin(angles)[:, None, :])


def rotate(tensor, cosine, sine):
    first, second = jnp.split(tensor, 2, axis=-1)
    return jnp.concatenate(
        [first * cosine - second * sine, second * cosine + first * sine], axis=-1
    )


def slot_table(owners):
    ranks = jnp.arange(owners.shape[0])
    same = (owners[None, :] == owners[:, None]) & (ranks[None, :] < ranks[:, None])
    return jnp.sum(jnp.where(same, 1, 0), axis=1).astype(jnp.int32)


def attention_scores(queries, keys_all, allowed):
    raw = jnp.einsum(
        "bqhd,bkhd->bhqk", queries, keys_all, preferred_element_type=jnp.float32
    ) * HEAD_DIM ** (-0.5)
    return jnp.where(allowed[None, None], raw, -1e30)


def adam_update(weight, first, second, grad, rate, decay):
    first = BETA_ONE * first + (1.0 - BETA_ONE) * grad
    second = BETA_TWO * second + (1.0 - BETA_TWO) * grad * grad
    first_hat = first / (1.0 - BETA_ONE**STEP_COUNT)
    second_hat = second / (1.0 - BETA_TWO**STEP_COUNT)
    weight = weight - rate * (first_hat / (jnp.sqrt(second_hat) + ADAM_EPS) + decay * weight)
    return (weight, first, second)


MESH = pl.DeviceIdType.MESH
ROW_STEP = 400
TILE_GROUPS = 8
LANES = 128


def meet(peers):
    gate = pltpu.get_barrier_semaphore()
    for peer in peers:
        pl.semaphore_signal(gate, inc=1, device_id=peer, device_id_type=MESH)
    pl.semaphore_wait(gate, len(peers))


def others(axis):
    count, me = lax.axis_size(axis), lax.axis_index(axis)
    return [lax.rem(me + step, count) for step in range(1, count)]


def behind(axis, step):
    count, me = lax.axis_size(axis), lax.axis_index(axis)
    return lax.rem(me + count - step, count)


def send(source, target, send_sem, recv_sem, device):
    copy = pltpu.make_async_remote_copy(
        src_ref=source,
        dst_ref=target,
        send_sem=send_sem,
        recv_sem=recv_sem,
        device_id=device,
        device_id_type=MESH,
    )
    copy.start()
    return copy


def layer_norm_parts(stream):
    center = stream - jnp.mean(stream, -1, keepdims=True)
    inverse = lax.rsqrt(jnp.mean(center * center, -1, keepdims=True) + EPS_NORM)
    return center * inverse, inverse


def norm_pull(grad_normed, gain, stream):
    scaled, inverse = layer_norm_parts(stream)
    grad_scaled = grad_normed * gain
    grad_stream = inverse * (
        grad_scaled
        - jnp.mean(grad_scaled, -1, keepdims=True)
        - scaled * jnp.mean(grad_scaled * scaled, -1, keepdims=True)
    )
    return grad_stream, jnp.sum(grad_normed * scaled, axis=0, keepdims=True)


def tensor_step(
    name, function, partial, extras, scalars, outs, gather, collective_id, beside=None, rider=None
):
    parts = lax.axis_size("tensor")
    share = extras[0].shape[0]
    reduce = partial is not None
    if beside:
        count, half_rows = rider.shape[0], rider.shape[-2]
        half = (count, half_rows, D)

    def kernel(*refs):
        refs = list(refs)
        partial_ref = refs.pop(0) if reduce else None
        extra_refs = [refs.pop(0) for _ in extras]
        scalar_refs = [refs.pop(0) for _ in scalars]
        rider_ref = refs.pop(0) if beside else None
        out_refs = [refs.pop(0) for _ in outs]
        full = refs.pop(0) if gather else None
        joined = refs.pop(0) if beside else None
        outgoing = refs.pop(0) if reduce else None
        arrived = refs.pop(0) if reduce else None
        send_sems, recv_sems = refs[:2]
        me = lax.axis_index("tensor")
        peers = others("tensor")
        side = lax.axis_index("seq")
        twin = [{"seq": 1 - side}] if beside else []
        meet([{"tensor": peer} for peer in peers] + twin)
        if beside == "share":
            _, _, own_sem, twin_send, twin_recv = refs
            own_copy = pltpu.make_async_copy(rider_ref, joined.at[:, side], own_sem)
            own_copy.start()
            twin_copy = send(rider_ref, joined.at[:, side], twin_send, twin_recv, twin[0])
        if beside == "fold":
            _, _, own_sem, twin_send, twin_recv, near = refs
            own_copy = pltpu.make_async_copy(rider_ref.at[:, side], joined, own_sem)
            own_copy.start()
            twin_copy = send(rider_ref.at[:, 1 - side], near, twin_send, twin_recv, twin[0])
        total = None
        if reduce:
            copies = []
            for step, peer in enumerate(peers):
                rows = pl.ds(pl.multiple_of(peer * share, share), share)
                outgoing[step] = partial_ref[rows, :].astype(jnp.bfloat16)
                copies.append(
                    send(
                        outgoing.at[step],
                        arrived.at[step],
                        send_sems.at[0, step],
                        recv_sems.at[0, step],
                        {"tensor": peer},
                    )
                )
            total = partial_ref[pl.ds(pl.multiple_of(me * share, share), share), :]
            for step, copy in enumerate(copies):
                copy.wait()
                total = total + arrived[step].astype(jnp.float32)
        results = function(total, *[ref[...] for ref in extra_refs], *scalar_refs)
        for ref, value in zip(out_refs, results):
            ref[...] = value.astype(ref.dtype)
        if gather:
            full[me] = results[len(outs)].astype(jnp.bfloat16)
            copies = [
                send(
                    full.at[me],
                    full.at[me],
                    send_sems.at[1, step],
                    recv_sems.at[1, step],
                    {"tensor": peer},
                )
                for step, peer in enumerate(peers)
            ]
        if beside:
            own_copy.wait()
            twin_copy.wait()
        if beside == "fold":

            def add_block(block, carry):
                value = joined[block].astype(jnp.float32) + near[block].astype(jnp.float32)
                joined[block] = value.astype(jnp.bfloat16)
                return carry

            lax.fori_loop(0, count, add_block, 0)
        if gather:
            for copy in copies:
                copy.wait()

    vmem = pl.BlockSpec(memory_space=pltpu.VMEM)
    anywhere = pl.BlockSpec(memory_space=pl.ANY)
    smem = pl.BlockSpec(memory_space=pltpu.SMEM)
    shapes = [jax.ShapeDtypeStruct(shape, dtype) for shape, dtype in outs]
    if gather:
        shapes.append(jax.ShapeDtypeStruct((parts, share, D), jnp.bfloat16))
    buffers = [pltpu.VMEM((parts - 1, share, D), jnp.bfloat16)] * (2 if reduce else 0)
    operands = ([partial] if reduce else []) + list(extras) + list(scalars)
    in_specs = [vmem] * (len(operands) - len(scalars)) + [smem] * len(scalars)
    out_specs = [vmem] * len(shapes)
    dma = pltpu.SemaphoreType.DMA
    buffers += [dma((2, parts - 1))] * 2
    if beside:
        operands.append(rider)
        in_specs.append(anywhere)
        buffers += [dma] * 3
        folds = beside == "fold"
        kept = half if folds else (count, 2, half_rows, D)
        shapes.append(jax.ShapeDtypeStruct(kept, jnp.bfloat16))
        out_specs.append(vmem if folds else anywhere)
        buffers += [pltpu.VMEM(half, jnp.bfloat16)] * folds
    return pl.pallas_call(
        kernel,
        name=name,
        out_shape=shapes,
        in_specs=in_specs,
        out_specs=out_specs,
        scratch_shapes=buffers,
        compiler_params=pltpu.CompilerParams(
            collective_id=collective_id, has_side_effects=True, vmem_limit_bytes=40 << 20
        ),
    )(*operands)


def reduce_all(terms, collective_id):
    _, tensors, groups, count, _ = terms.shape

    def kernel(
        terms_ref, out_ref, near, own, mid, mid_in, far, far_in,
        own_sems, near_send, near_recv, mid_send, mid_recv, far_send, far_recv,
    ):
        group, part, side = lax.axis_index("dp"), lax.axis_index("tensor"), lax.axis_index("seq")
        twin = 1 - side
        parts = others("tensor")
        order = others("dp") + [group]
        meet(
            [{"seq": twin}]
            + [{"tensor": peer} for peer in parts]
            + [{"dp": peer} for peer in order[:-1]]
        )
        waits, near_copies, own_copies = [], [], []
        for place, target in enumerate(order):
            near_copies.append(
                send(
                    terms_ref.at[twin, :, target],
                    near.at[place],
                    near_send.at[place],
                    near_recv.at[place],
                    {"seq": twin},
                )
            )
            copy = pltpu.make_async_copy(
                terms_ref.at[side, :, target], own.at[place], own_sems.at[place]
            )
            copy.start()
            own_copies.append(copy)
        mid_copies = []
        for place in range(groups):
            near_copies[place].wait_recv()
            own_copies[place].wait()
            for slot in range(tensors):
                mid[place, slot] = (
                    own[place, slot].astype(jnp.float32) + near[place, slot].astype(jnp.float32)
                ).astype(jnp.bfloat16)
            mid_copies.append(
                [
                    send(
                        mid.at[place, peer],
                        mid_in.at[place, step],
                        mid_send.at[place, step],
                        mid_recv.at[place, step],
                        {"tensor": peer},
                    )
                    for step, peer in enumerate(parts)
                ]
            )
        far_copies = []
        for place, target in enumerate(order):
            total = mid[place, part].astype(jnp.float32)
            for step in range(tensors - 1):
                mid_copies[place][step].wait_recv()
                total = total + mid_in[place, step].astype(jnp.float32)
            if place < groups - 1:
                far[place] = total.astype(jnp.bfloat16)
                far_copies.append(
                    send(
                        far.at[place],
                        far_in.at[place],
                        far_send.at[place],
                        far_recv.at[place],
                        {"dp": target},
                    )
                )
        for place, copy in enumerate(far_copies):
            copy.wait_recv()
            total = total + far_in[place].astype(jnp.float32)
        out_ref[...] = total
        for copy in near_copies + far_copies + [c for row in mid_copies for c in row]:
            copy.wait_send()

    block = (count, D)
    dma = pltpu.SemaphoreType.DMA
    return pl.pallas_call(
        kernel,
        name="reduce_all",
        out_shape=jax.ShapeDtypeStruct(block, jnp.float32),
        in_specs=[pl.BlockSpec(memory_space=pl.ANY)],
        out_specs=pl.BlockSpec(memory_space=pltpu.VMEM),
        scratch_shapes=[pltpu.VMEM((groups, tensors) + block, jnp.bfloat16)] * 3
        + [
            pltpu.VMEM((groups, tensors - 1) + block, jnp.bfloat16),
            pltpu.VMEM((groups,) + block, jnp.bfloat16),
            pltpu.VMEM((groups,) + block, jnp.bfloat16),
            dma((groups,)),
            dma((groups,)),
            dma((groups,)),
            dma((groups, tensors - 1)),
            dma((groups, tensors - 1)),
            dma((groups,)),
            dma((groups,)),
        ],
        compiler_params=pltpu.CompilerParams(
            collective_id=collective_id, has_side_effects=True, vmem_limit_bytes=56 << 20
        ),
    )(terms)


def gather_all(block, collective_id):
    tensors, groups = lax.axis_size("tensor"), lax.axis_size("dp")

    def kernel(block_ref, out, own_sem, far_send, far_recv, mid_send, mid_recv, near_send, near_recv):
        group, part, side = lax.axis_index("dp"), lax.axis_index("tensor"), lax.axis_index("seq")
        twin = 1 - side
        parts = others("tensor")
        meet(
            [{"seq": twin}]
            + [{"tensor": peer} for peer in parts]
            + [{"dp": peer} for peer in others("dp")]
        )
        far_copies = [
            send(
                block_ref,
                out.at[side, part, group],
                far_send.at[step],
                far_recv.at[step],
                {"dp": peer},
            )
            for step, peer in enumerate(others("dp"))
        ]
        own = pltpu.make_async_copy(block_ref, out.at[side, part, group], own_sem)
        own.start()
        own.wait()
        mid_copies, near_copies = [], []
        for place in range(groups):
            source = behind("dp", place)
            if place:
                far_copies[place - 1].wait_recv()
            held = out.at[side, part, source]
            mid_copies.append(
                [
                    send(held, held, mid_send.at[place, step], mid_recv.at[place, step], {"tensor": peer})
                    for step, peer in enumerate(parts)
                ]
            )
            near_copies.append(
                send(held, held, near_send.at[place, 0], near_recv.at[place, 0], {"seq": twin})
            )
        for place in range(groups):
            source = behind("dp", place)
            for step in range(tensors - 1):
                mid_copies[place][step].wait_recv()
                held = out.at[side, behind("tensor", step + 1), source]
                near_copies.append(
                    send(
                        held,
                        held,
                        near_send.at[place, step + 1],
                        near_recv.at[place, step + 1],
                        {"seq": twin},
                    )
                )
        for copy in near_copies:
            copy.wait_recv()
        for copy in near_copies + far_copies + [c for row in mid_copies for c in row]:
            copy.wait_send()

    dma = pltpu.SemaphoreType.DMA
    return pl.pallas_call(
        kernel,
        name="gather_all",
        out_shape=jax.ShapeDtypeStruct((2, tensors, groups) + block.shape, block.dtype),
        in_specs=[pl.BlockSpec(memory_space=pl.ANY)],
        out_specs=pl.BlockSpec(memory_space=pl.ANY),
        scratch_shapes=[
            dma,
            dma((groups - 1,)),
            dma((groups - 1,)),
            dma((groups, tensors - 1)),
            dma((groups, tensors - 1)),
            dma((groups, tensors)),
            dma((groups, tensors)),
        ],
        compiler_params=pltpu.CompilerParams(collective_id=collective_id, has_side_effects=True),
    )(block)


def reduce_rows(terms, collective_id):
    count, groups = terms.shape[3], terms.shape[2]
    pieces = max(1, groups // 4)
    part = count // pieces
    sums = [
        reduce_all(terms[:, :, :, i * part : (i + 1) * part] if pieces > 1 else terms, collective_id)
        for i in range(pieces)
    ]
    return jnp.concatenate(sums, axis=0) if pieces > 1 else sums[0]


def join_stats(stats, collective_id):
    _, tensors, groups, _, _ = stats.shape

    def join(left, right):
        top = jnp.maximum(left[..., 0:1, :], right[..., 0:1, :])
        total = left[..., 1:2, :] * jnp.exp(left[..., 0:1, :] - top) + right[..., 1:2, :] * jnp.exp(
            right[..., 0:1, :] - top
        )
        return jnp.concatenate(
            [top, total, left[..., 2:3, :] + right[..., 2:3, :], left[..., 3:, :]], axis=-2
        )

    def kernel(
        stats_ref, home, full, near, mid, mid_in, far, far_in,
        near_send, near_recv, mid_send, mid_recv, far_send, far_recv,
    ):
        group, part, side = lax.axis_index("dp"), lax.axis_index("tensor"), lax.axis_index("seq")
        twin = 1 - side
        parts, groups_else = others("tensor"), others("dp")
        meet(
            [{"seq": twin}]
            + [{"tensor": peer} for peer in parts]
            + [{"dp": peer} for peer in groups_else]
        )
        copy = send(stats_ref.at[twin], near, near_send.at[0], near_recv.at[0], {"seq": twin})
        copy.wait()
        for slot in range(tensors):
            for spot in range(groups):
                mid[slot, spot] = join(stats_ref[side, slot, spot], near[slot, spot])
        copies = [
            send(mid.at[peer], mid_in.at[step], mid_send.at[0, step], mid_recv.at[0, step], {"tensor": peer})
            for step, peer in enumerate(parts)
        ]
        for copy in copies:
            copy.wait()
        for spot in range(groups):
            total = mid[part, spot]
            for step in range(tensors - 1):
                total = join(total, mid_in[step, spot])
            far[spot] = total
        copies = [
            send(far.at[peer], far_in.at[step], far_send.at[0, step], far_recv.at[0, step], {"dp": peer})
            for step, peer in enumerate(groups_else)
        ]
        total = far[group]
        for step, copy in enumerate(copies):
            copy.wait()
            total = join(total, far_in[step])
        log_total = total[0:1] + jnp.log(total[1:2])
        home[...] = jnp.concatenate([log_total, total[2:3], total[2:]], axis=0)
        full[side, part, group] = jnp.broadcast_to(log_total, (8, LANES))
        held = full.at[side, part, group]
        copies = [
            send(held, held, far_send.at[1, step], far_recv.at[1, step], {"dp": peer})
            for step, peer in enumerate(groups_else)
        ]
        for copy in copies:
            copy.wait()
        held = full.at[side, part]
        copies = [
            send(held, held, mid_send.at[1, step], mid_recv.at[1, step], {"tensor": peer})
            for step, peer in enumerate(parts)
        ]
        for copy in copies:
            copy.wait()
        held = full.at[side]
        send(held, held, near_send.at[1], near_recv.at[1], {"seq": twin}).wait()

    tile = (8, LANES)
    dma = pltpu.SemaphoreType.DMA
    vmem = pl.BlockSpec(memory_space=pltpu.VMEM)
    return pl.pallas_call(
        kernel,
        name="join_stats",
        out_shape=[
            jax.ShapeDtypeStruct(tile, jnp.float32),
            jax.ShapeDtypeStruct(stats.shape, jnp.float32),
        ],
        in_specs=[vmem],
        out_specs=[vmem, vmem],
        scratch_shapes=[
            pltpu.VMEM((tensors, groups) + tile, jnp.float32),
            pltpu.VMEM((tensors, groups) + tile, jnp.float32),
            pltpu.VMEM((tensors - 1, groups) + tile, jnp.float32),
            pltpu.VMEM((groups,) + tile, jnp.float32),
            pltpu.VMEM((groups - 1,) + tile, jnp.float32),
            dma((2,)),
            dma((2,)),
            dma((2, tensors - 1)),
            dma((2, tensors - 1)),
            dma((2, groups - 1)),
            dma((2, groups - 1)),
        ],
        compiler_params=pltpu.CompilerParams(collective_id=collective_id, has_side_effects=True),
    )(stats)


def spread_tokens(block, collective_id):
    tensors, groups = lax.axis_size("tensor"), lax.axis_size("dp")
    rows = 2 * tensors * groups

    def kernel(block_ref, ids, targets, kept, count, held, own_sem, send_sems, recv_sems):
        group, side = lax.axis_index("dp"), lax.axis_index("seq")
        peers = [
            {"dp": lax.rem(group + step // 2, groups), "seq": lax.rem(side + step % 2, 2)}
            for step in range(1, 2 * groups)
        ]
        meet(peers)
        copies = [
            send(block_ref, held.at[group, side], send_sems.at[step], recv_sems.at[step], peer)
            for step, peer in enumerate(peers)
        ]
        own = pltpu.make_async_copy(block_ref, held.at[group, side], own_sem)
        own.start()
        own.wait()
        for copy in copies:
            copy.wait()
        lane = lax.broadcasted_iota(jnp.int32, (1, LANES), 1)
        total = jnp.zeros((1, LANES), jnp.int32)
        for half in range(2):
            for source in range(groups):
                limit = held[source, half, 2 * tensors : 2 * tensors + 1, :]
                total = total + limit
                for part in range(tensors):
                    row = (half * tensors + part) * groups + source
                    tile, place = row // TILE_GROUPS, slice(row % TILE_GROUPS, row % TILE_GROUPS + 1)
                    ids[tile, place, :] = held[source, half, part : part + 1, :]
                    targets[tile, place, :] = held[source, half, tensors + part : tensors + part + 1, :]
                    kept[tile, place, :] = jnp.where(lane + part * LANES < limit, 1.0, 0.0)
        count[...] = total.astype(jnp.float32)

    dma = pltpu.SemaphoreType.DMA
    vmem = pl.BlockSpec(memory_space=pltpu.VMEM)
    shape = (rows // TILE_GROUPS, TILE_GROUPS, LANES)
    return pl.pallas_call(
        kernel,
        name="spread_tokens",
        out_shape=[
            jax.ShapeDtypeStruct(shape, jnp.int32),
            jax.ShapeDtypeStruct(shape, jnp.int32),
            jax.ShapeDtypeStruct(shape, jnp.float32),
            jax.ShapeDtypeStruct((1, LANES), jnp.float32),
        ],
        in_specs=[vmem],
        out_specs=[vmem] * 4,
        scratch_shapes=[
            pltpu.VMEM((groups, 2) + block.shape, jnp.int32),
            dma,
            dma((2 * groups - 1,)),
            dma((2 * groups - 1,)),
        ],
        compiler_params=pltpu.CompilerParams(collective_id=collective_id, has_side_effects=True),
    )(block)


def finish(gain_grads, states, grad_ys, home, keep, table_squares, layer_squares, count, smalls, collective_id):
    tensors, groups = lax.axis_size("tensor"), lax.axis_size("dp")
    block = (8, D)
    gain_rows = 2 * LAYERS + 1
    operands = list(gain_grads) + list(states) + list(grad_ys) + [
        home, keep, table_squares, layer_squares, count
    ] + list(smalls)

    def kernel(*refs):
        refs = list(refs)
        gain_refs = [refs.pop(0) for _ in gain_grads]
        state_refs = [refs.pop(0) for _ in states]
        grad_refs = [refs.pop(0) for _ in grad_ys]
        home_ref, keep_ref, table_ref, layer_ref, count_ref = [refs.pop(0) for _ in range(5)]
        small_refs = [refs.pop(0) for _ in smalls]
        out_refs = [refs.pop(0) for _ in range(8)]
        near, mid, far, near_send, near_recv, mid_send, mid_recv, far_send, far_recv = refs
        group, part, side = lax.axis_index("dp"), lax.axis_index("tensor"), lax.axis_index("seq")
        parts, groups_else = others("tensor"), others("dp")
        meet(
            [{"seq": 1 - side}]
            + [{"tensor": peer} for peer in parts]
            + [{"dp": peer} for peer in groups_else]
        )
        values = []
        for later in range(1, LAYERS + 1):
            grad = grad_refs[later - 1][...]
            for level in range(later + 1):
                values.append(jnp.sum(grad * state_refs[level][...], keepdims=True))
        loss = (home_ref[0:1, :] - home_ref[1:2, :]) * keep_ref[...]
        values.append(jnp.sum(loss, keepdims=True))
        values.append(jnp.sum(table_ref[...], keepdims=True) + layer_ref[...])
        lane = lax.broadcasted_iota(jnp.int32, (1, D), 1)
        row = jnp.zeros((1, D), jnp.float32)
        for place, value in enumerate(values):
            row = jnp.where(lane == place, value, row)
        blank = jnp.zeros((8 - gain_rows - 1, D), jnp.float32)
        total = jnp.concatenate([ref[...] for ref in gain_refs] + [row, blank], axis=0)
        stages = [
            ("seq", near, side, [1 - side], near_send, near_recv),
            ("tensor", mid, part, parts, mid_send, mid_recv),
            ("dp", far, group, groups_else, far_send, far_recv),
        ]
        for axis, slots, me, peers, send_sems, recv_sems in stages:
            slots[me] = total
            copies = [
                send(slots.at[me], slots.at[me], send_sems.at[step], recv_sems.at[step], {axis: peer})
                for step, peer in enumerate(peers)
            ]
            for copy in copies:
                copy.wait()
            total = slots[0]
            for index in range(1, slots.shape[0]):
                total = total + slots[index]
        gain_total = total[:gain_rows]
        row = total[gain_rows : gain_rows + 1]

        def pick(place):
            return jnp.sum(jnp.where(lane == place, row, 0.0), axis=1, keepdims=True)

        mix_squares = jnp.sum(jnp.where(lane < MIX_WEIGHTS, row * row, 0.0), axis=1, keepdims=True)
        gain_squares = jnp.sum(gain_total * gain_total, keepdims=True)
        tokens = count_ref[:, 0:1]
        clip_norm = jnp.sqrt(pick(MIX_WEIGHTS + 1) + gain_squares + mix_squares) / tokens
        factor = jnp.minimum(1.0, CLIP_NORM / clip_norm) / tokens
        gain_news = adam_update(
            *[ref[...] for ref in small_refs[:3]], gain_total * factor, RATE_SMALL, 0.0
        )
        mix_news = adam_update(
            *[ref[...] for ref in small_refs[3:]], row[:, :MIX_WEIGHTS] * factor, RATE_SMALL, 0.0
        )
        for ref, value in zip(out_refs[:6], gain_news + mix_news):
            ref[...] = value
        ends = jnp.where(lane == 0, pick(MIX_WEIGHTS), jnp.where(lane == 1, clip_norm, factor))
        out_refs[6][...] = ends[:, :LANES]
        out_refs[7][...] = jnp.broadcast_to(factor, (8, LANES))

    dma = pltpu.SemaphoreType.DMA
    vmem = pl.BlockSpec(memory_space=pltpu.VMEM)
    return pl.pallas_call(
        kernel,
        name="finish",
        out_shape=[jax.ShapeDtypeStruct(value.shape, jnp.float32) for value in smalls]
        + [
            jax.ShapeDtypeStruct((1, LANES), jnp.float32),
            jax.ShapeDtypeStruct((8, LANES), jnp.float32),
        ],
        in_specs=[vmem] * len(operands),
        out_specs=[vmem] * 8,
        scratch_shapes=[
            pltpu.VMEM((2,) + block, jnp.float32),
            pltpu.VMEM((tensors,) + block, jnp.float32),
            pltpu.VMEM((groups,) + block, jnp.float32),
            dma((1,)),
            dma((1,)),
            dma((tensors - 1,)),
            dma((tensors - 1,)),
            dma((groups - 1,)),
            dma((groups - 1,)),
        ],
        compiler_params=pltpu.CompilerParams(collective_id=collective_id, has_side_effects=True),
    )(*operands)


def update_slots(plan, factor, master, first, second, layer_grads, grad_table):
    slots, half_rows, _ = master.shape

    def kernel(plan_ref, factor_ref, master_ref, first_ref, second_ref, *rest):
        layer_refs, (table_ref, new_master, new_first, new_second) = rest[:LAYERS], rest[LAYERS:]
        kind = plan_ref[0, pl.program_id(0)]
        grad = table_ref[...]
        for level in range(LAYERS):
            grad = jnp.where(kind == level, layer_refs[level][0].astype(jnp.float32), grad)
        grad = jnp.where(kind >= 0, grad * factor_ref[0:1, 0:1], 0.0)
        values = adam_update(
            master_ref[0], first_ref[0], second_ref[0], grad, RATE_MATRIX, DECAY_MATRIX
        )
        for ref, value in zip((new_master, new_first, new_second), values):
            ref[0] = value

    slot = pl.BlockSpec((1, half_rows, D), lambda step, plan: (step, 0, 0))
    return pl.pallas_call(
        kernel,
        name="update_slots",
        grid_spec=pltpu.PrefetchScalarGridSpec(
            num_scalar_prefetch=1,
            grid=(slots,),
            in_specs=[pl.BlockSpec((8, LANES), lambda step, plan: (0, 0)), slot, slot, slot]
            + [
                pl.BlockSpec(
                    (1, half_rows, D), lambda step, plan, level=level: (plan[1 + level, step], 0, 0)
                )
                for level in range(LAYERS)
            ]
            + [pl.BlockSpec((half_rows, D), lambda step, plan: (step, 0))],
            out_specs=[slot] * 3,
        ),
        out_shape=[jax.ShapeDtypeStruct(master.shape, jnp.float32)] * 3,
        compiler_params=pltpu.CompilerParams(vmem_limit_bytes=32 << 20),
    )(plan, factor, master, first, second, *layer_grads, grad_table)


def row_of(groups_ref):
    return jnp.concatenate([groups_ref[0, g : g + 1, :] for g in range(TILE_GROUPS)], axis=1)


def stat_row(stat_ref, row):
    return jnp.concatenate([stat_ref[g, row : row + 1, :] for g in range(TILE_GROUPS)], axis=1)


def chunk_of(span_ref, step):
    return pl.ds(pl.multiple_of(span_ref[0] + step * ROW_STEP, 16), ROW_STEP)


def chunks_of(span_ref):
    return (span_ref[1] - span_ref[0] + ROW_STEP - 1) // ROW_STEP


def whole(shape):
    return pl.BlockSpec(shape, lambda step, span: (0,) * len(shape), pipeline_mode=pl.Buffered(1))


TILE = TILE_GROUPS * LANES
TOKENS_SPEC = pl.BlockSpec((1, TILE_GROUPS, LANES), lambda step, span: (step, 0, 0))
STATS_SPEC = pl.BlockSpec((TILE_GROUPS, 8, LANES), lambda step, span: (step, 0, 0))
ROWS_SPEC = pl.BlockSpec((TILE, D), lambda step, span: (step, 0))


def local_call(name, kernel, steps, span, operands, in_specs, out_shape, out_specs, scratch):
    return pl.pallas_call(
        kernel,
        name=name,
        grid_spec=pltpu.PrefetchScalarGridSpec(
            num_scalar_prefetch=1,
            grid=(steps,),
            in_specs=in_specs,
            out_specs=out_specs,
            scratch_shapes=scratch,
        ),
        out_shape=out_shape,
        compiler_params=pltpu.CompilerParams(vmem_limit_bytes=60 << 20),
    )(span, *operands)


def look_up(span, row_ids, tokens, table):
    rows = table.shape[0]
    steps = tokens.shape[0]

    def kernel(span_ref, ids_ref, tokens_ref, table_ref, out_ref, acc):
        acc[...] = jnp.zeros_like(acc)
        wanted = row_of(tokens_ref)

        def one(step, carry):
            chunk = chunk_of(span_ref, step)
            hits = jnp.where(ids_ref[chunk, :] == wanted, 1.0, 0.0).astype(jnp.bfloat16)
            acc[...] += contract_first(hits, table_ref[chunk, :])
            return carry

        lax.fori_loop(0, chunks_of(span_ref), one, 0)
        out_ref[...] = acc[...].astype(jnp.bfloat16)

    return local_call(
        "look_up",
        kernel,
        steps,
        span,
        (row_ids, tokens, table),
        [whole((rows, 1)), TOKENS_SPEC, whole((rows, D))],
        jax.ShapeDtypeStruct((steps * TILE, D), jnp.bfloat16),
        ROWS_SPEC,
        [pltpu.VMEM((TILE, D), jnp.float32)],
    )


def head_forward(span, row_ids, labels, table, final):
    rows = table.shape[0]
    steps = labels.shape[0]

    def kernel(span_ref, ids_ref, labels_ref, table_ref, final_ref, powers_ref, stats_ref, scores):
        wanted = row_of(labels_ref)
        hidden = final_ref[...]

        def first(step, carry):
            top, target = carry
            chunk = chunk_of(span_ref, step)
            ids = ids_ref[chunk, :]
            raw = contract_last(table_ref[chunk, :], hidden)
            raw = jnp.where(ids >= 0, raw, -1e30)
            scores[chunk, :] = raw
            top = jnp.maximum(top, jnp.max(raw, axis=0, keepdims=True))
            target = target + jnp.sum(jnp.where(ids == wanted, raw, 0.0), axis=0, keepdims=True)
            return (top, target)

        blank = jnp.zeros((1, TILE), jnp.float32)
        top, target = lax.fori_loop(0, chunks_of(span_ref), first, (blank - 1e30, blank))

        def second(step, total):
            chunk = chunk_of(span_ref, step)
            powers = jnp.exp(scores[chunk, :] - top)
            powers_ref[chunk, :] = powers.astype(jnp.bfloat16)
            return total + jnp.sum(powers, axis=0, keepdims=True)

        total = lax.fori_loop(0, chunks_of(span_ref), second, blank)
        rest = jnp.zeros((5, LANES), jnp.float32)
        for g in range(TILE_GROUPS):
            lanes = slice(g * LANES, (g + 1) * LANES)
            stats_ref[g] = jnp.concatenate(
                [top[:, lanes], total[:, lanes], target[:, lanes], rest], axis=0
            )

    return local_call(
        "head_forward",
        kernel,
        steps,
        span,
        (row_ids, labels, table, final),
        [whole((rows, 1)), TOKENS_SPEC, whole((rows, D)), ROWS_SPEC],
        [
            jax.ShapeDtypeStruct((rows, steps * TILE), jnp.bfloat16),
            jax.ShapeDtypeStruct((steps * TILE_GROUPS, 8, LANES), jnp.float32),
        ],
        [pl.BlockSpec((rows, TILE), lambda step, span: (0, step)), STATS_SPEC],
        [pltpu.VMEM((rows, TILE), jnp.float32)],
    )


def head_backward(span, row_ids, labels, keep, stats, log_totals, table, final, powers):
    rows = table.shape[0]
    steps = labels.shape[0]

    def kernel(
        span_ref, ids_ref, labels_ref, keep_ref, stats_ref, logs_ref, table_ref, final_ref,
        powers_ref, grad_final_ref, grad_table_ref, acc,
    ):
        @pl.when(pl.program_id(0) == 0)
        def _():
            grad_table_ref[...] = jnp.zeros_like(grad_table_ref)

        acc[...] = jnp.zeros_like(acc)
        wanted, kept = row_of(labels_ref), row_of(keep_ref)
        scale = jnp.exp(stat_row(stats_ref, 0) - stat_row(logs_ref, 0)) * kept
        hidden = final_ref[...]

        def one(step, carry):
            chunk = chunk_of(span_ref, step)
            grads = powers_ref[chunk, :].astype(jnp.float32) * scale
            grads = grads - jnp.where(ids_ref[chunk, :] == wanted, kept, 0.0)
            grads = grads.astype(jnp.bfloat16)
            grad_table_ref[chunk, :] += jnp.dot(grads, hidden, preferred_element_type=jnp.float32)
            acc[...] += contract_first(grads, table_ref[chunk, :])
            return carry

        lax.fori_loop(0, chunks_of(span_ref), one, 0)
        grad_final_ref[...] = acc[...].astype(jnp.bfloat16)

    return local_call(
        "head_backward",
        kernel,
        steps,
        span,
        (row_ids, labels, keep, stats, log_totals, table, final, powers),
        [
            whole((rows, 1)),
            TOKENS_SPEC,
            TOKENS_SPEC,
            STATS_SPEC,
            STATS_SPEC,
            whole((rows, D)),
            ROWS_SPEC,
            pl.BlockSpec((rows, TILE), lambda step, span: (0, step)),
        ],
        [
            jax.ShapeDtypeStruct((steps * TILE, D), jnp.bfloat16),
            jax.ShapeDtypeStruct((rows, D), jnp.float32),
        ],
        [ROWS_SPEC, whole((rows, D))],
        [pltpu.VMEM((TILE, D), jnp.float32)],
    )


def look_back(span, row_ids, tokens, grad_start, grad_table):
    rows = grad_table.shape[0]
    steps = tokens.shape[0]

    def kernel(span_ref, ids_ref, tokens_ref, grad_ref, table_ref, out_ref, squares_ref):
        @pl.when(pl.program_id(0) == 0)
        def _():
            out_ref[...] = table_ref[...]

        wanted = row_of(tokens_ref)
        grads = grad_ref[...]

        def one(step, carry):
            chunk = chunk_of(span_ref, step)
            hits = jnp.where(ids_ref[chunk, :] == wanted, 1.0, 0.0).astype(jnp.bfloat16)
            out_ref[chunk, :] += jnp.dot(hits, grads, preferred_element_type=jnp.float32)
            return carry

        lax.fori_loop(0, chunks_of(span_ref), one, 0)

        @pl.when(pl.program_id(0) == steps - 1)
        def _():
            def square(step, total):
                values = out_ref[chunk_of(span_ref, step), :]
                values = (values * values).reshape(ROW_STEP // 8, 8, D).sum(axis=0)
                return total + values

            squares_ref[...] = lax.fori_loop(
                0, chunks_of(span_ref), square, jnp.zeros((8, D), jnp.float32)
            )

    return local_call(
        "look_back",
        kernel,
        steps,
        span,
        (row_ids, tokens, grad_start, grad_table),
        [whole((rows, 1)), TOKENS_SPEC, ROWS_SPEC, whole((rows, D))],
        [
            jax.ShapeDtypeStruct((rows, D), jnp.float32),
            jax.ShapeDtypeStruct((8, D), jnp.float32),
        ],
        [whole((rows, D)), whole((8, D))],
        [],
    )


def attend(joined, geometry):
    cosine, sine, allowed, seq_count, half_len, local_heads = geometry
    width = local_heads * HEAD_DIM
    shape_four = (seq_count, half_len, local_heads, HEAD_DIM)
    queries = (
        rotate(joined[:, :width].reshape(-1, local_heads, HEAD_DIM), cosine, sine)
        .astype(jnp.bfloat16)
        .reshape(shape_four)
    )
    own_keys = (
        rotate(joined[:, width : 2 * width].reshape(-1, local_heads, HEAD_DIM), cosine, sine)
        .astype(jnp.bfloat16)
        .reshape(shape_four)
    )
    own_values = joined[:, 2 * width :].astype(jnp.bfloat16).reshape(shape_four)
    far_keys, far_values = from_behind((own_keys, own_values), "seq", 1)
    keys_all = jnp.concatenate([far_keys, own_keys], axis=1)
    values_all = jnp.concatenate([far_values, own_values], axis=1)
    scores = attention_scores(queries, keys_all, allowed)
    peak = jnp.max(scores, -1, keepdims=True)
    log_total = peak + jnp.log(jnp.sum(jnp.exp(scores - peak), -1, keepdims=True))
    probs = jnp.exp(scores - log_total).astype(jnp.bfloat16)
    attended = jnp.einsum("bhqk,bkhd->bqhd", probs, values_all, preferred_element_type=jnp.float32)
    attended = attended.astype(jnp.bfloat16).reshape(-1, width)
    return attended, (queries, keys_all, values_all, log_total)


def attend_back(grad_attended, kept, geometry):
    queries, keys_all, values_all, log_total = kept
    cosine, sine, allowed, seq_count, half_len, local_heads = geometry
    width = local_heads * HEAD_DIM
    grad_attended = grad_attended.reshape(seq_count, half_len, local_heads, HEAD_DIM)
    probs = jnp.exp(attention_scores(queries, keys_all, allowed) - log_total)
    grad_probs = jnp.einsum(
        "bqhd,bkhd->bhqk", grad_attended, values_all, preferred_element_type=jnp.float32
    )
    grad_scores = (probs * (grad_probs - jnp.sum(probs * grad_probs, -1, keepdims=True))).astype(
        jnp.bfloat16
    )
    scale = HEAD_DIM ** (-0.5)
    grad_queries = (
        jnp.einsum("bhqk,bkhd->bqhd", grad_scores, keys_all, preferred_element_type=jnp.float32)
        * scale
    )
    grad_keys = (
        jnp.einsum("bhqk,bqhd->bkhd", grad_scores, queries, preferred_element_type=jnp.float32)
        * scale
    )
    grad_values = jnp.einsum(
        "bhqk,bqhd->bkhd",
        probs.astype(jnp.bfloat16),
        grad_attended,
        preferred_element_type=jnp.float32,
    )
    back_keys, back_values = (
        from_behind(grad_keys[:, :half_len].astype(jnp.bfloat16), "seq", -1).astype(jnp.float32),
        from_behind(grad_values[:, :half_len].astype(jnp.bfloat16), "seq", -1).astype(jnp.float32),
    )
    grad_keys = grad_keys[:, half_len:] + back_keys
    grad_values = grad_values[:, half_len:] + back_values
    return jnp.concatenate(
        [
            rotate(grad_queries.reshape(-1, local_heads, HEAD_DIM), cosine, -sine).reshape(
                -1, width
            ),
            rotate(grad_keys.reshape(-1, local_heads, HEAD_DIM), cosine, -sine).reshape(-1, width),
            grad_values.reshape(-1, width),
        ],
        axis=1,
    ).astype(jnp.bfloat16)


def body(
    token_ids,
    labels,
    real_counts,
    owners,
    master,
    first_moment,
    second_moment,
    gains,
    gains_first,
    gains_second,
    mix,
    mix_first,
    mix_second,
):
    tensors = lax.axis_size("tensor")
    groups = lax.axis_size("dp")
    group = lax.axis_index("dp")
    tensor_part = lax.axis_index("tensor")
    seq_part = lax.axis_index("seq")
    slots, half_rows, _ = master.shape
    seq_count, half_len = token_ids.shape
    row_count = seq_count * half_len
    share = row_count // tensors
    head_rows = 3 * D // tensors
    out_rows = D // tensors
    unit_rows = FF // tensors
    layer_rows = head_rows + out_rows + 2 * unit_rows
    layer_blocks = layer_rows // (2 * half_rows)
    blocks = LAYERS * layer_blocks
    vocab_rows = VOCAB // tensors
    local_heads = HEADS // tensors

    slot_rank = slot_table(owners)
    block_ids = jnp.arange(owners.shape[0], dtype=jnp.int32)
    mine = owners == group
    match = (jnp.arange(slots)[:, None] == slot_rank[None, :]) & mine[None, :]
    slot_block = jnp.sum(jnp.where(match, block_ids[None, :] + 1, 0), axis=1) - 1
    row_ids = (
        tensor_part * vocab_rows
        + (slot_block[:, None] - blocks) * (2 * half_rows)
        + seq_part * half_rows
        + jnp.arange(half_rows, dtype=jnp.int32)[None, :]
    )
    row_ids = jnp.where(slot_block[:, None] >= blocks, row_ids, -1).reshape(-1, 1)
    spare = -(-ROW_STEP // half_rows)
    row_ids = jnp.pad(row_ids, ((0, spare * half_rows), (0, 0)), constant_values=-1)
    held = jnp.sum(jnp.where(mine, 1, 0)) * half_rows
    first_held = jnp.sum(jnp.where(mine & (block_ids < blocks), 1, 0)) * half_rows
    span = jnp.stack([first_held, held]).astype(jnp.int32)
    level_of = jnp.where(slot_block < 0, -1, jnp.minimum(slot_block // layer_blocks, LAYERS))
    plan = jnp.stack(
        [level_of]
        + [
            jnp.where(level_of == level, slot_block - level * layer_blocks, 0)
            for level in range(LAYERS)
        ]
    ).astype(jnp.int32)

    packed = jnp.concatenate(
        [
            token_ids.reshape(tensors, LANES),
            labels.reshape(tensors, LANES),
            jnp.broadcast_to(real_counts[:, None], (16 - 2 * tensors, LANES)),
        ],
        axis=0,
    )
    ids_all, labels_all, keep_all, count = spread_tokens(packed, 15)
    order = (2, tensors, groups, share)

    table_slots = jnp.pad(master.astype(jnp.bfloat16), ((0, spare), (0, 0), (0, 0)))
    table = table_slots.reshape(-1, D)

    halves = []
    for level in range(LAYERS):
        chosen = slice(level * layer_blocks, (level + 1) * layer_blocks)
        own = jnp.where(
            mine[chosen][:, None, None], jnp.take(table_slots, slot_rank[chosen], axis=0), 0.0
        ).astype(jnp.bfloat16)
        if level:
            own, halves[-1] = lax.optimization_barrier((own, halves[-1]))
        halves.append(lax.psum(own, "dp"))

    def cut(joined):
        joined = joined.reshape(layer_rows, D)
        cut_one, cut_two = head_rows + out_rows, head_rows + out_rows + unit_rows
        return (joined[:head_rows], joined[head_rows:cut_one], joined[cut_one:cut_two], joined[cut_two:])

    positions = seq_part * half_len + jnp.arange(row_count) % half_len
    cosine, sine = rotary(positions)
    query_pos = seq_part * half_len + jnp.arange(half_len)
    key_pos = jnp.concatenate([(seq_part - 1) * half_len + jnp.arange(half_len), query_pos])
    allowed = (key_pos[None, :] <= query_pos[:, None]) & (key_pos[None, :] >= 0)
    geometry = (cosine, sine, allowed, seq_count, half_len, local_heads)

    looked = look_up(span, row_ids, ids_all, table).reshape(order + (D,))
    start = reduce_rows(looked, 0)
    gain = [gains[i : i + 1] for i in range(2 * LAYERS + 1)]
    piece = ((share, D), jnp.float32)

    def normed_of(total, stream, gain_row):
        return (layer_norm_parts(stream)[0] * gain_row,)

    def inner_of(total, stream, gain_row):
        inner = stream + total
        return (inner, layer_norm_parts(inner)[0] * gain_row)

    def outcome_of(base, total, inner, gain_row, *rest):
        states, scalars = rest[:-1], rest[-1]
        outcome = inner + total
        stream = scalars[base + len(states)] * outcome
        for source, state in enumerate(states):
            stream = stream + scalars[base + source] * state
        return (outcome, stream, layer_norm_parts(stream)[0] * gain_row)

    normed, joined = tensor_step(
        "normed", normed_of, None, (start, gain[0]), (), [], True, 1, "share", halves[0]
    )
    weights_all = [cut(joined)]
    states, streams, inners, kept_all = [start], [start], [], []
    for level in range(LAYERS):
        qkv_w, out_w, up_w, down_w = weights_all[level]
        normed = normed.reshape(row_count, D)
        attended, kept = attend(contract_last(normed, qkv_w), geometry)
        inner, normed_two = tensor_step(
            "inner",
            inner_of,
            jnp.dot(attended, out_w, preferred_element_type=jnp.float32),
            (streams[level], gain[2 * level + 1]),
            (),
            [piece],
            True,
            2,
        )
        normed_two = normed_two.reshape(row_count, D)
        hidden = contract_last(normed_two, up_w)
        activated = jax.nn.gelu(hidden, approximate=True).astype(jnp.bfloat16)
        last = level == LAYERS - 1
        results = tensor_step(
            f"outcome_{level}",
            partial(outcome_of, (level + 1) * (level + 2) // 2 - 1),
            jnp.dot(activated, down_w, preferred_element_type=jnp.float32),
            [inner, gain[2 * level + 2]] + states,
            (mix,),
            [piece, piece] + ([((share, D), jnp.bfloat16)] if last else []),
            not last,
            3 + level,
            *((None, None) if last else ("share", halves[level + 1])),
        )
        if not last:
            weights_all.append(cut(results[3]))
        inners.append(inner)
        kept_all.append((normed, kept, attended, normed_two, hidden, activated))
        states.append(results[0])
        streams.append(results[1])
        normed = results[2]

    final_all = gather_all(normed, 3 + LAYERS).reshape(-1, D)
    powers, stats = head_forward(span, row_ids, labels_all, table, final_all)
    home, log_totals = join_stats(
        stats.reshape((2, tensors, groups, 8, LANES)), 4 + LAYERS
    )
    grad_final, grad_table = head_backward(
        span,
        row_ids,
        labels_all,
        keep_all,
        stats,
        log_totals.reshape(-1, 8, LANES),
        table,
        final_all,
        powers,
    )
    grad_final = reduce_rows(grad_final.reshape(order + (D,)), 0)

    row = ((1, D), jnp.float32)

    def top_of(total, grad, stream, gain_row, scalars):
        grad_top, grad_gain = norm_pull(grad, gain_row, stream)
        grad_state = scalars[MIX_WEIGHTS - 1] * grad_top
        return (grad_top, grad_state, grad_gain, grad_state)

    def inner_back(total, grad_out, inner, gain_row):
        grad, grad_gain = norm_pull(total, gain_row, inner)
        grad = grad_out + grad
        return (grad, grad_gain, grad)

    def stream_back(block, total, grad_inner, stream, gain_row, *rest):
        grad_ys, scalars = rest[:-1], rest[-1]
        grad, grad_gain = norm_pull(total, gain_row, stream)
        grad = grad_inner + grad
        state = grad if block == 0 else scalars[block * (block + 1) // 2 - 1 + block] * grad
        for offset, grad_y in enumerate(grad_ys):
            later = block + 1 + offset
            state = state + scalars[later * (later + 1) // 2 - 1 + block] * grad_y
        return (grad, state, grad_gain, state)

    grad_ys = [None] * (LAYERS + 1)
    gain_grads = [None] * (2 * LAYERS + 1)
    layer_grads = [None] * LAYERS
    grad_ys[LAYERS], grad_state, gain_grads[2 * LAYERS], grad_branch = tensor_step(
        "top_back",
        top_of,
        None,
        (grad_final, streams[LAYERS], gain[2 * LAYERS]),
        (mix,),
        [piece, piece, row],
        True,
        5 + LAYERS,
    )
    for level in reversed(range(LAYERS)):
        qkv_w, out_w, up_w, down_w = weights_all[level]
        normed, kept, attended, normed_two, hidden, activated = kept_all[level]
        grad_branch = grad_branch.reshape(row_count, D)
        grad_act = contract_last(grad_branch, down_w)
        _, gelu_pull = jax.vjp(partial(jax.nn.gelu, approximate=True), hidden)
        grad_hidden = gelu_pull(grad_act)[0].astype(jnp.bfloat16)
        grad_inner, gain_grads[2 * level + 1], grad_attn = tensor_step(
            "inner_back",
            inner_back,
            jnp.dot(grad_hidden, up_w, preferred_element_type=jnp.float32),
            (grad_state, inners[level], gain[2 * level + 1]),
            (),
            [piece, row],
            True,
            6 + LAYERS,
        )
        grad_attn = grad_attn.reshape(row_count, D)
        grad_attended = contract_last(grad_attn, out_w).astype(jnp.bfloat16)
        grad_joined = attend_back(grad_attended, kept, geometry)
        grads = jnp.concatenate(
            [
                contract_first(grad_joined, normed),
                contract_first(attended, grad_attn),
                contract_first(grad_hidden, normed_two),
                contract_first(activated, grad_branch),
            ],
            axis=0,
        ).astype(jnp.bfloat16)
        results = tensor_step(
            f"stream_back_{level}",
            partial(stream_back, level),
            jnp.dot(grad_joined, qkv_w, preferred_element_type=jnp.float32),
            [grad_inner, streams[level], gain[2 * level]] + grad_ys[level + 1 :],
            (mix,),
            [piece, piece, row] + ([] if level else [((share, D), jnp.bfloat16)]),
            level > 0,
            7 + LAYERS + level,
            "fold",
            grads.reshape(layer_blocks, 2, half_rows, D),
        )
        grad_ys[level], grad_state, gain_grads[2 * level], grad_branch, folded = results
        if level < LAYERS - 1:
            folded, layer_grads[level + 1] = lax.optimization_barrier(
                (folded, layer_grads[level + 1])
            )
        layer_grads[level] = lax.psum(folded, "dp")

    grad_start_all = gather_all(grad_branch, 3 + LAYERS).reshape(-1, D)
    grad_table, table_squares = look_back(span, row_ids, ids_all, grad_start_all, grad_table)
    layer_squares = jnp.zeros((), jnp.float32)
    for level in range(LAYERS):
        chosen = slice(level * layer_blocks, (level + 1) * layer_blocks)
        values = layer_grads[level].astype(jnp.float32)
        layer_squares += jnp.sum(jnp.where(mine[chosen][:, None, None], values * values, 0.0))
    keep = jnp.where(
        tensor_part * share + jnp.arange(share) < real_counts[0], 1.0, 0.0
    ).astype(jnp.float32)
    news = finish(
        gain_grads,
        states,
        grad_ys[1:],
        home,
        keep[None],
        table_squares,
        layer_squares.reshape(1, 1),
        count,
        (gains, gains_first, gains_second, mix[None], mix_first[None], mix_second[None]),
        7 + 2 * LAYERS,
    )
    new_gains, new_gains_first, new_gains_second = news[:3]
    new_mix, new_mix_first, new_mix_second = [value[0] for value in news[3:6]]
    loss_sum, clip_norm = news[6][0, 0], news[6][0, 1]
    token_count = count[0, 0]
    new_master, new_first, new_second = update_slots(
        plan, news[7], master, first_moment, second_moment, layer_grads, grad_table
    )
    return (
        new_master,
        new_first,
        new_second,
        new_gains,
        new_gains_first,
        new_gains_second,
        new_mix,
        new_mix_first,
        new_mix_second,
        loss_sum,
        token_count,
        clip_norm,
    )


def solution(mesh):
    return jax.shard_map(
        body,
        mesh=mesh,
        in_specs=(
            P("dp", "seq"),
            P("dp", "seq"),
            P(("dp", "seq")),
            P(),
            P("dp", ("tensor", "seq"), None),
            P("dp", ("tensor", "seq"), None),
            P("dp", ("tensor", "seq"), None),
            P(),
            P(),
            P(),
            P(),
            P(),
            P(),
        ),
        out_specs=(
            P("dp", ("tensor", "seq"), None),
            P("dp", ("tensor", "seq"), None),
            P("dp", ("tensor", "seq"), None),
            P(),
            P(),
            P(),
            P(),
            P(),
            P(),
            P(),
            P(),
            P(),
        ),
        check_vma=False,
    )
```

```python
from functools import partial

import jax
import jax.numpy as jnp
from jax import lax
from jax.experimental import pallas as pl
from jax.experimental.pallas import tpu as pltpu
from jax.sharding import PartitionSpec as P

D = 768
HEADS = 12
HEAD_DIM = 64
FF = 3072
VOCAB = 50304
LAYERS = 2
STEP_COUNT = 10
MIX_WEIGHTS = 5


EPS_NORM = 1e-05
CLIP_NORM = 0.01
BETA_ONE = 0.9
BETA_TWO = 0.95
ADAM_EPS = 1e-08
RATE_MATRIX = 0.04
RATE_SMALL = 0.4
DECAY_MATRIX = 0.1


def from_behind(block, axis, distance):
    devices = range(lax.axis_size(axis))
    route = [(i - distance, i) for i in devices if i - distance in devices]
    return lax.ppermute(block, axis, route)


def contract_last(left, right):
    return lax.dot_general(
        left, right, (((1,), (1,)), ((), ())), preferred_element_type=jnp.float32
    )


def contract_first(left, right):
    return lax.dot_general(
        left, right, (((0,), (0,)), ((), ())), preferred_element_type=jnp.float32
    )


def normalize(stream):
    center = stream - jnp.mean(stream, -1, keepdims=True)
    inverse = lax.rsqrt(jnp.mean(center * center, -1, keepdims=True) + EPS_NORM)
    return (center * inverse, inverse)


def norm_back(grad_normed, gain, scaled, inverse):
    grad_scaled = grad_normed * gain
    grad_stream = inverse * (
        grad_scaled
        - jnp.mean(grad_scaled, -1, keepdims=True)
        - scaled * jnp.mean(grad_scaled * scaled, -1, keepdims=True)
    )
    return (grad_stream, jnp.sum(grad_normed * scaled, axis=0))


def rotary(positions):
    steps_half = jnp.arange(HEAD_DIM // 2).astype(jnp.float32)
    freqs = 10000.0 ** (-2.0 * steps_half / HEAD_DIM)
    angles = positions.astype(jnp.float32)[:, None] * freqs[None, :]
    return (jnp.cos(angles)[:, None, :], jnp.sin(angles)[:, None, :])


def rotate(tensor, cosine, sine):
    first, second = jnp.split(tensor, 2, axis=-1)
    return jnp.concatenate(
        [first * cosine - second * sine, second * cosine + first * sine], axis=-1
    )


def slot_table(owners):
    ranks = jnp.arange(owners.shape[0])
    same = (owners[None, :] == owners[:, None]) & (ranks[None, :] < ranks[:, None])
    return jnp.sum(jnp.where(same, 1, 0), axis=1).astype(jnp.int32)


def attention_scores(queries, keys_all, allowed):
    raw = jnp.einsum(
        "bqhd,bkhd->bhqk", queries, keys_all, preferred_element_type=jnp.float32
    ) * HEAD_DIM ** (-0.5)
    return jnp.where(allowed[None, None], raw, -1e30)


def adam_update(weight, first, second, grad, rate, decay):
    first = BETA_ONE * first + (1.0 - BETA_ONE) * grad
    second = BETA_TWO * second + (1.0 - BETA_TWO) * grad * grad
    first_hat = first / (1.0 - BETA_ONE**STEP_COUNT)
    second_hat = second / (1.0 - BETA_TWO**STEP_COUNT)
    weight = weight - rate * (first_hat / (jnp.sqrt(second_hat) + ADAM_EPS) + decay * weight)
    return (weight, first, second)


MESH = pl.DeviceIdType.MESH
ROW_STEP = 400
TILE_GROUPS = 8
LANES = 128


def meet(peers):
    gate = pltpu.get_barrier_semaphore()
    for peer in peers:
        pl.semaphore_signal(gate, inc=1, device_id=peer, device_id_type=MESH)
    pl.semaphore_wait(gate, len(peers))


def others(axis):
    count, me = lax.axis_size(axis), lax.axis_index(axis)
    return [lax.rem(me + step, count) for step in range(1, count)]


def behind(axis, step):
    count, me = lax.axis_size(axis), lax.axis_index(axis)
    return lax.rem(me + count - step, count)


def send(source, target, send_sem, recv_sem, device):
    copy = pltpu.make_async_remote_copy(
        src_ref=source,
        dst_ref=target,
        send_sem=send_sem,
        recv_sem=recv_sem,
        device_id=device,
        device_id_type=MESH,
    )
    copy.start()
    return copy


def layer_norm_parts(stream):
    center = stream - jnp.mean(stream, -1, keepdims=True)
    inverse = lax.rsqrt(jnp.mean(center * center, -1, keepdims=True) + EPS_NORM)
    return center * inverse, inverse


def norm_pull(grad_normed, gain, stream):
    scaled, inverse = layer_norm_parts(stream)
    grad_scaled = grad_normed * gain
    grad_stream = inverse * (
        grad_scaled
        - jnp.mean(grad_scaled, -1, keepdims=True)
        - scaled * jnp.mean(grad_scaled * scaled, -1, keepdims=True)
    )
    return grad_stream, jnp.sum(grad_normed * scaled, axis=0, keepdims=True)


def tensor_step(
    name, function, partial, extras, scalars, outs, gather, collective_id, beside=None, rider=None
):
    parts = lax.axis_size("tensor")
    share = extras[0].shape[0]
    reduce = partial is not None
    if beside:
        count, half_rows = rider.shape[0], rider.shape[-2]
        half = (count, half_rows, D)

    def kernel(*refs):
        refs = list(refs)
        partial_ref = refs.pop(0) if reduce else None
        extra_refs = [refs.pop(0) for _ in extras]
        scalar_refs = [refs.pop(0) for _ in scalars]
        rider_ref = refs.pop(0) if beside else None
        out_refs = [refs.pop(0) for _ in outs]
        full = refs.pop(0) if gather else None
        joined = refs.pop(0) if beside else None
        outgoing = refs.pop(0) if reduce else None
        arrived = refs.pop(0) if reduce else None
        send_sems, recv_sems = refs[:2]
        me = lax.axis_index("tensor")
        peers = others("tensor")
        side = lax.axis_index("seq")
        twin = [{"seq": 1 - side}] if beside else []
        meet([{"tensor": peer} for peer in peers] + twin)
        if beside == "share":
            _, _, own_sem, twin_send, twin_recv = refs
            own_copy = pltpu.make_async_copy(rider_ref, joined.at[:, side], own_sem)
            own_copy.start()
            twin_copy = send(rider_ref, joined.at[:, side], twin_send, twin_recv, twin[0])
        if beside == "fold":
            _, _, own_sem, twin_send, twin_recv, near = refs
            own_copy = pltpu.make_async_copy(rider_ref.at[:, side], joined, own_sem)
            own_copy.start()
            twin_copy = send(rider_ref.at[:, 1 - side], near, twin_send, twin_recv, twin[0])
        total = None
        if reduce:
            copies = []
            for step, peer in enumerate(peers):
                rows = pl.ds(pl.multiple_of(peer * share, share), share)
                outgoing[step] = partial_ref[rows, :].astype(jnp.bfloat16)
                copies.append(
                    send(
                        outgoing.at[step],
                        arrived.at[step],
                        send_sems.at[0, step],
                        recv_sems.at[0, step],
                        {"tensor": peer},
                    )
                )
            total = partial_ref[pl.ds(pl.multiple_of(me * share, share), share), :]
            for step, copy in enumerate(copies):
                copy.wait()
                total = total + arrived[step].astype(jnp.float32)
        results = function(total, *[ref[...] for ref in extra_refs], *scalar_refs)
        for ref, value in zip(out_refs, results):
            ref[...] = value.astype(ref.dtype)
        if gather:
            full[me] = results[len(outs)].astype(jnp.bfloat16)
            copies = [
                send(
                    full.at[me],
                    full.at[me],
                    send_sems.at[1, step],
                    recv_sems.at[1, step],
                    {"tensor": peer},
                )
                for step, peer in enumerate(peers)
            ]
        if beside:
            own_copy.wait()
            twin_copy.wait()
        if beside == "fold":

            def add_block(block, carry):
                value = joined[block].astype(jnp.float32) + near[block].astype(jnp.float32)
                joined[block] = value.astype(jnp.bfloat16)
                return carry

            lax.fori_loop(0, count, add_block, 0)
        if gather:
            for copy in copies:
                copy.wait()

    vmem = pl.BlockSpec(memory_space=pltpu.VMEM)
    anywhere = pl.BlockSpec(memory_space=pl.ANY)
    smem = pl.BlockSpec(memory_space=pltpu.SMEM)
    shapes = [jax.ShapeDtypeStruct(shape, dtype) for shape, dtype in outs]
    if gather:
        shapes.append(jax.ShapeDtypeStruct((parts, share, D), jnp.bfloat16))
    buffers = [pltpu.VMEM((parts - 1, share, D), jnp.bfloat16)] * (2 if reduce else 0)
    operands = ([partial] if reduce else []) + list(extras) + list(scalars)
    in_specs = [vmem] * (len(operands) - len(scalars)) + [smem] * len(scalars)
    out_specs = [vmem] * len(shapes)
    dma = pltpu.SemaphoreType.DMA
    buffers += [dma((2, parts - 1))] * 2
    if beside:
        operands.append(rider)
        in_specs.append(anywhere)
        buffers += [dma] * 3
        folds = beside == "fold"
        kept = half if folds else (count, 2, half_rows, D)
        shapes.append(jax.ShapeDtypeStruct(kept, jnp.bfloat16))
        out_specs.append(vmem if folds else anywhere)
        buffers += [pltpu.VMEM(half, jnp.bfloat16)] * folds
    return pl.pallas_call(
        kernel,
        name=name,
        out_shape=shapes,
        in_specs=in_specs,
        out_specs=out_specs,
        scratch_shapes=buffers,
        compiler_params=pltpu.CompilerParams(
            collective_id=collective_id, has_side_effects=True, vmem_limit_bytes=40 << 20
        ),
    )(*operands)


LINE_BLOCKS = 2


class Line:
    def __init__(self, rider, share):
        self.groups = lax.axis_size("dp")
        self.half = rider.shape
        self.chunks = rider.shape[0] // LINE_BLOCKS
        self.share = share
        count, half_rows, _ = rider.shape
        dma = pltpu.SemaphoreType.DMA
        out = (count, 2, half_rows, D) if share else rider.shape
        self.out_shape = jax.ShapeDtypeStruct(out, jnp.bfloat16)
        self.out_spec = pl.BlockSpec(memory_space=pl.ANY if share else pltpu.VMEM)
        self.scratch = [
            pltpu.VMEM(self.half, jnp.bfloat16),
            pltpu.VMEM((2,) + self.half, jnp.bfloat16),
            pltpu.VMEM((2,) + self.half, jnp.bfloat16),
            dma,
            dma((2, self.chunks)),
            dma((2, self.chunks)),
        ]
        if share:
            self.scratch += [pltpu.VMEM(self.half, jnp.bfloat16)] + [dma((self.chunks,))] * 3

    def neighbours(self, signal):
        group = lax.axis_index("dp")

        @pl.when(group > 0)
        def _():
            signal({"dp": group - 1})

        @pl.when(group < self.groups - 1)
        def _():
            signal({"dp": group + 1})

    def bind(self, rider_ref, out_ref, refs):
        self.rider, self.out = rider_ref, out_ref
        self.own, self.came, self.going, self.own_sem, self.send_sems, self.recv_sems = refs[:6]
        self.total = out_ref
        if self.share:
            self.total, self.keep_sems, self.twin_send, self.twin_recv = refs[6:]
        self.group = lax.axis_index("dp")
        self.first = jnp.where(self.group < self.groups // 2, 0, 1)

    def at(self, chunk):
        return pl.ds(chunk * LINE_BLOCKS, LINE_BLOCKS)

    def comes(self, way):
        return jnp.where(way == 0, self.group > 0, self.group < self.groups - 1)

    def goes(self, way):
        return jnp.where(way == 0, self.group < self.groups - 1, self.group > 0)

    def copy(self, source, way, chunk):
        target = jnp.where(way == 0, self.group + 1, self.group - 1)
        return pltpu.make_async_remote_copy(
            src_ref=source,
            dst_ref=self.came.at[way, self.at(chunk)],
            send_sem=self.send_sems.at[way, chunk],
            recv_sem=self.recv_sems.at[way, chunk],
            device_id={"dp": target},
            device_id_type=MESH,
        )

    def begin(self):
        copy = pltpu.make_async_copy(self.rider, self.own, self.own_sem)
        copy.start()
        copy.wait()
        for way in range(2):

            @pl.when(jnp.logical_not(self.comes(way)))
            def _():
                self.came[way] = jnp.zeros(self.half, jnp.bfloat16)
                self.going[way] = self.own[...]

                def start(chunk, carry):
                    self.copy(self.going.at[way, self.at(chunk)], way, chunk).start()
                    return carry

                lax.fori_loop(0, self.chunks, start, 0)

    def twin_copy(self, chunk):
        side = lax.axis_index("seq")
        return pltpu.make_async_remote_copy(
            src_ref=self.total.at[self.at(chunk)],
            dst_ref=self.out.at[self.at(chunk), side],
            send_sem=self.twin_send.at[chunk],
            recv_sem=self.twin_recv.at[chunk],
            device_id={"seq": 1 - side},
            device_id_type=MESH,
        )

    def keep_copy(self, chunk):
        return pltpu.make_async_copy(
            self.total.at[self.at(chunk)],
            self.out.at[self.at(chunk), lax.axis_index("seq")],
            self.keep_sems.at[chunk],
        )

    def step(self, chunk):
        rows = self.at(chunk)
        own = self.own[rows].astype(jnp.float32)
        for turn in range(2):
            way = self.first if turn == 0 else 1 - self.first

            @pl.when(self.comes(way))
            def _():
                copy = self.copy(self.going.at[way, rows], way, chunk)
                copy.wait_recv()

                @pl.when(self.goes(way))
                def _():
                    value = own + self.came[way, rows].astype(jnp.float32)
                    self.going[way, rows] = value.astype(jnp.bfloat16)
                    copy.start()

        value = own + self.came[0, rows].astype(jnp.float32) + self.came[1, rows].astype(jnp.float32)
        self.total[rows] = value.astype(jnp.bfloat16)
        if self.share:
            self.keep_copy(chunk).start()
            self.twin_copy(chunk).start()

    def steps(self, start, stop):
        def one(chunk, carry):
            self.step(chunk)
            return carry

        lax.fori_loop(start, stop, one, 0)

    def end(self):
        def one(chunk, carry):
            for way in range(2):

                @pl.when(self.goes(way))
                def _():
                    self.copy(self.going.at[way, self.at(chunk)], way, chunk).wait_send()

            if self.share:
                self.keep_copy(chunk).wait()
                self.twin_copy(chunk).wait()
            return carry

        lax.fori_loop(0, self.chunks, one, 0)


def reduce_all(terms, collective_id, rider=None):
    _, tensors, groups, count, _ = terms.shape
    line = None if rider is None else Line(rider, True)

    def kernel(*refs):
        refs = list(refs)
        terms_ref = refs.pop(0)
        rider_ref = refs.pop(0) if line else None
        out_ref = refs.pop(0)
        joined_ref = refs.pop(0) if line else None
        (
            near, own, mid, mid_in, far, far_in,
            own_sems, near_send, near_recv, mid_send, mid_recv, far_send, far_recv,
        ) = refs[:13]
        if line:
            line.bind(rider_ref, joined_ref, refs[13:])
        group, part, side = lax.axis_index("dp"), lax.axis_index("tensor"), lax.axis_index("seq")
        twin = 1 - side
        parts = others("tensor")
        order = others("dp") + [group]
        meet(
            [{"seq": twin}]
            + [{"tensor": peer} for peer in parts]
            + [{"dp": peer} for peer in order[:-1]]
        )
        waits, near_copies, own_copies = [], [], []
        for place, target in enumerate(order):
            near_copies.append(
                send(
                    terms_ref.at[twin, :, target],
                    near.at[place],
                    near_send.at[place],
                    near_recv.at[place],
                    {"seq": twin},
                )
            )
            copy = pltpu.make_async_copy(
                terms_ref.at[side, :, target], own.at[place], own_sems.at[place]
            )
            copy.start()
            own_copies.append(copy)
        if line:
            line.begin()
        mid_copies = []
        for place in range(groups):
            near_copies[place].wait_recv()
            own_copies[place].wait()
            for slot in range(tensors):
                mid[place, slot] = (
                    own[place, slot].astype(jnp.float32) + near[place, slot].astype(jnp.float32)
                ).astype(jnp.bfloat16)
            mid_copies.append(
                [
                    send(
                        mid.at[place, peer],
                        mid_in.at[place, step],
                        mid_send.at[place, step],
                        mid_recv.at[place, step],
                        {"tensor": peer},
                    )
                    for step, peer in enumerate(parts)
                ]
            )
        far_copies = []
        for place, target in enumerate(order):
            if line:
                line.steps(line.chunks * place // groups, line.chunks * (place + 1) // groups)
            total = mid[place, part].astype(jnp.float32)
            for step in range(tensors - 1):
                mid_copies[place][step].wait_recv()
                total = total + mid_in[place, step].astype(jnp.float32)
            if place < groups - 1:
                far[place] = total.astype(jnp.bfloat16)
                far_copies.append(
                    send(
                        far.at[place],
                        far_in.at[place],
                        far_send.at[place],
                        far_recv.at[place],
                        {"dp": target},
                    )
                )
        for place, copy in enumerate(far_copies):
            copy.wait_recv()
            total = total + far_in[place].astype(jnp.float32)
        out_ref[...] = total
        for copy in near_copies + far_copies + [c for row in mid_copies for c in row]:
            copy.wait_send()
        if line:
            line.end()

    block = (count, D)
    dma = pltpu.SemaphoreType.DMA
    return pl.pallas_call(
        kernel,
        name="reduce_all",
        out_shape=[jax.ShapeDtypeStruct(block, jnp.float32)] + ([line.out_shape] if line else []),
        in_specs=[pl.BlockSpec(memory_space=pl.ANY)] * (2 if line else 1),
        out_specs=[pl.BlockSpec(memory_space=pltpu.VMEM)] + ([line.out_spec] if line else []),
        scratch_shapes=[pltpu.VMEM((groups, tensors) + block, jnp.bfloat16)] * 3
        + [
            pltpu.VMEM((groups, tensors - 1) + block, jnp.bfloat16),
            pltpu.VMEM((groups,) + block, jnp.bfloat16),
            pltpu.VMEM((groups,) + block, jnp.bfloat16),
            dma((groups,)),
            dma((groups,)),
            dma((groups,)),
            dma((groups, tensors - 1)),
            dma((groups, tensors - 1)),
            dma((groups,)),
            dma((groups,)),
        ]
        + (line.scratch if line else []),
        compiler_params=pltpu.CompilerParams(
            collective_id=collective_id, has_side_effects=True, vmem_limit_bytes=56 << 20
        ),
    )(terms, *([rider] if line else []))


def gather_all(block, collective_id, rider=None):
    tensors, groups = lax.axis_size("tensor"), lax.axis_size("dp")
    line = None if rider is None else Line(rider, False)

    def kernel(*refs):
        refs = list(refs)
        block_ref = refs.pop(0)
        rider_ref = refs.pop(0) if line else None
        out = refs.pop(0)
        summed_ref = refs.pop(0) if line else None
        own_sem, far_send, far_recv, mid_send, mid_recv, near_send, near_recv = refs[:7]
        if line:
            line.bind(rider_ref, summed_ref, refs[7:])
        group, part, side = lax.axis_index("dp"), lax.axis_index("tensor"), lax.axis_index("seq")
        twin = 1 - side
        parts = others("tensor")
        meet(
            [{"seq": twin}]
            + [{"tensor": peer} for peer in parts]
            + [{"dp": peer} for peer in others("dp")]
        )
        far_copies = [
            send(
                block_ref,
                out.at[side, part, group],
                far_send.at[step],
                far_recv.at[step],
                {"dp": peer},
            )
            for step, peer in enumerate(others("dp"))
        ]
        own = pltpu.make_async_copy(block_ref, out.at[side, part, group], own_sem)
        own.start()
        own.wait()
        if line:
            line.begin()
        mid_copies, near_copies = [], []
        for place in range(groups):
            if line and place:
                line.steps(
                    line.chunks * (place - 1) // groups // 2, line.chunks * place // groups // 2
                )
            source = behind("dp", place)
            if place:
                far_copies[place - 1].wait_recv()
            held = out.at[side, part, source]
            mid_copies.append(
                [
                    send(held, held, mid_send.at[place, step], mid_recv.at[place, step], {"tensor": peer})
                    for step, peer in enumerate(parts)
                ]
            )
            near_copies.append(
                send(held, held, near_send.at[place, 0], near_recv.at[place, 0], {"seq": twin})
            )
        if line:
            done = line.chunks * (groups - 1) // groups // 2
        for place in range(groups):
            if line:
                left = line.chunks - done
                line.steps(done + left * place // groups, done + left * (place + 1) // groups)
            source = behind("dp", place)
            for step in range(tensors - 1):
                mid_copies[place][step].wait_recv()
                held = out.at[side, behind("tensor", step + 1), source]
                near_copies.append(
                    send(
                        held,
                        held,
                        near_send.at[place, step + 1],
                        near_recv.at[place, step + 1],
                        {"seq": twin},
                    )
                )
        for copy in near_copies:
            copy.wait_recv()
        for copy in near_copies + far_copies + [c for row in mid_copies for c in row]:
            copy.wait_send()
        if line:
            line.end()

    dma = pltpu.SemaphoreType.DMA
    anywhere = pl.BlockSpec(memory_space=pl.ANY)
    return pl.pallas_call(
        kernel,
        name="gather_all",
        out_shape=[jax.ShapeDtypeStruct((2, tensors, groups) + block.shape, block.dtype)]
        + ([line.out_shape] if line else []),
        in_specs=[anywhere] * (2 if line else 1),
        out_specs=[anywhere] + ([line.out_spec] if line else []),
        scratch_shapes=[
            dma,
            dma((groups - 1,)),
            dma((groups - 1,)),
            dma((groups, tensors - 1)),
            dma((groups, tensors - 1)),
            dma((groups, tensors)),
            dma((groups, tensors)),
        ]
        + (line.scratch if line else []),
        compiler_params=pltpu.CompilerParams(
            collective_id=collective_id, has_side_effects=True, vmem_limit_bytes=40 << 20
        ),
    )(block, *([rider] if line else []))


def reduce_rows(terms, ids, rider=None):
    count, groups = terms.shape[3], terms.shape[2]
    pieces = max(1, groups // 4)
    part = count // pieces
    sums, joined = [], None
    for i in range(pieces):
        piece = terms[:, :, :, i * part : (i + 1) * part] if pieces > 1 else terms
        if i == 0 and rider is not None:
            total, joined = reduce_all(piece, ids[1], rider)
        else:
            (total,) = reduce_all(piece, ids[0])
        sums.append(total)
    return jnp.concatenate(sums, axis=0) if pieces > 1 else sums[0], joined


def join_stats(stats, collective_id):
    _, tensors, groups, _, _ = stats.shape

    def join(left, right):
        top = jnp.maximum(left[..., 0:1, :], right[..., 0:1, :])
        total = left[..., 1:2, :] * jnp.exp(left[..., 0:1, :] - top) + right[..., 1:2, :] * jnp.exp(
            right[..., 0:1, :] - top
        )
        return jnp.concatenate(
            [top, total, left[..., 2:3, :] + right[..., 2:3, :], left[..., 3:, :]], axis=-2
        )

    def kernel(
        stats_ref, home, full, near, mid, mid_in, far, far_in,
        near_send, near_recv, mid_send, mid_recv, far_send, far_recv,
    ):
        group, part, side = lax.axis_index("dp"), lax.axis_index("tensor"), lax.axis_index("seq")
        twin = 1 - side
        parts, groups_else = others("tensor"), others("dp")
        meet(
            [{"seq": twin}]
            + [{"tensor": peer} for peer in parts]
            + [{"dp": peer} for peer in groups_else]
        )
        copy = send(stats_ref.at[twin], near, near_send.at[0], near_recv.at[0], {"seq": twin})
        copy.wait()
        for slot in range(tensors):
            for spot in range(groups):
                mid[slot, spot] = join(stats_ref[side, slot, spot], near[slot, spot])
        copies = [
            send(mid.at[peer], mid_in.at[step], mid_send.at[0, step], mid_recv.at[0, step], {"tensor": peer})
            for step, peer in enumerate(parts)
        ]
        for copy in copies:
            copy.wait()
        for spot in range(groups):
            total = mid[part, spot]
            for step in range(tensors - 1):
                total = join(total, mid_in[step, spot])
            far[spot] = total
        copies = [
            send(far.at[peer], far_in.at[step], far_send.at[0, step], far_recv.at[0, step], {"dp": peer})
            for step, peer in enumerate(groups_else)
        ]
        total = far[group]
        for step, copy in enumerate(copies):
            copy.wait()
            total = join(total, far_in[step])
        log_total = total[0:1] + jnp.log(total[1:2])
        home[...] = jnp.concatenate([log_total, total[2:3], total[2:]], axis=0)
        full[side, part, group] = jnp.broadcast_to(log_total, (8, LANES))
        held = full.at[side, part, group]
        copies = [
            send(held, held, far_send.at[1, step], far_recv.at[1, step], {"dp": peer})
            for step, peer in enumerate(groups_else)
        ]
        for copy in copies:
            copy.wait()
        held = full.at[side, part]
        copies = [
            send(held, held, mid_send.at[1, step], mid_recv.at[1, step], {"tensor": peer})
            for step, peer in enumerate(parts)
        ]
        for copy in copies:
            copy.wait()
        held = full.at[side]
        send(held, held, near_send.at[1], near_recv.at[1], {"seq": twin}).wait()

    tile = (8, LANES)
    dma = pltpu.SemaphoreType.DMA
    vmem = pl.BlockSpec(memory_space=pltpu.VMEM)
    return pl.pallas_call(
        kernel,
        name="join_stats",
        out_shape=[
            jax.ShapeDtypeStruct(tile, jnp.float32),
            jax.ShapeDtypeStruct(stats.shape, jnp.float32),
        ],
        in_specs=[vmem],
        out_specs=[vmem, vmem],
        scratch_shapes=[
            pltpu.VMEM((tensors, groups) + tile, jnp.float32),
            pltpu.VMEM((tensors, groups) + tile, jnp.float32),
            pltpu.VMEM((tensors - 1, groups) + tile, jnp.float32),
            pltpu.VMEM((groups,) + tile, jnp.float32),
            pltpu.VMEM((groups - 1,) + tile, jnp.float32),
            dma((2,)),
            dma((2,)),
            dma((2, tensors - 1)),
            dma((2, tensors - 1)),
            dma((2, groups - 1)),
            dma((2, groups - 1)),
        ],
        compiler_params=pltpu.CompilerParams(collective_id=collective_id, has_side_effects=True),
    )(stats)


def spread_tokens(block, collective_id):
    tensors, groups = lax.axis_size("tensor"), lax.axis_size("dp")
    rows = 2 * tensors * groups

    def kernel(block_ref, ids, targets, kept, count, held, own_sem, send_sems, recv_sems):
        group, side = lax.axis_index("dp"), lax.axis_index("seq")
        peers = [
            {"dp": lax.rem(group + step // 2, groups), "seq": lax.rem(side + step % 2, 2)}
            for step in range(1, 2 * groups)
        ]
        meet(peers)
        copies = [
            send(block_ref, held.at[group, side], send_sems.at[step], recv_sems.at[step], peer)
            for step, peer in enumerate(peers)
        ]
        own = pltpu.make_async_copy(block_ref, held.at[group, side], own_sem)
        own.start()
        own.wait()
        for copy in copies:
            copy.wait()
        lane = lax.broadcasted_iota(jnp.int32, (1, LANES), 1)
        total = jnp.zeros((1, LANES), jnp.int32)
        for half in range(2):
            for source in range(groups):
                limit = held[source, half, 2 * tensors : 2 * tensors + 1, :]
                total = total + limit
                for part in range(tensors):
                    row = (half * tensors + part) * groups + source
                    tile, place = row // TILE_GROUPS, slice(row % TILE_GROUPS, row % TILE_GROUPS + 1)
                    ids[tile, place, :] = held[source, half, part : part + 1, :]
                    targets[tile, place, :] = held[source, half, tensors + part : tensors + part + 1, :]
                    kept[tile, place, :] = jnp.where(lane + part * LANES < limit, 1.0, 0.0)
        count[...] = total.astype(jnp.float32)

    dma = pltpu.SemaphoreType.DMA
    vmem = pl.BlockSpec(memory_space=pltpu.VMEM)
    shape = (rows // TILE_GROUPS, TILE_GROUPS, LANES)
    return pl.pallas_call(
        kernel,
        name="spread_tokens",
        out_shape=[
            jax.ShapeDtypeStruct(shape, jnp.int32),
            jax.ShapeDtypeStruct(shape, jnp.int32),
            jax.ShapeDtypeStruct(shape, jnp.float32),
            jax.ShapeDtypeStruct((1, LANES), jnp.float32),
        ],
        in_specs=[vmem],
        out_specs=[vmem] * 4,
        scratch_shapes=[
            pltpu.VMEM((groups, 2) + block.shape, jnp.int32),
            dma,
            dma((2 * groups - 1,)),
            dma((2 * groups - 1,)),
        ],
        compiler_params=pltpu.CompilerParams(collective_id=collective_id, has_side_effects=True),
    )(block)


def finish(gain_grads, states, grad_ys, home, keep, table_squares, layer_squares, count, smalls, collective_id):
    tensors, groups = lax.axis_size("tensor"), lax.axis_size("dp")
    block = (8, D)
    gain_rows = 2 * LAYERS + 1
    operands = list(gain_grads) + list(states) + list(grad_ys) + [
        home, keep, table_squares, layer_squares, count
    ] + list(smalls)

    def kernel(*refs):
        refs = list(refs)
        gain_refs = [refs.pop(0) for _ in gain_grads]
        state_refs = [refs.pop(0) for _ in states]
        grad_refs = [refs.pop(0) for _ in grad_ys]
        home_ref, keep_ref, table_ref, layer_ref, count_ref = [refs.pop(0) for _ in range(5)]
        small_refs = [refs.pop(0) for _ in smalls]
        out_refs = [refs.pop(0) for _ in range(8)]
        near, mid, far, near_send, near_recv, mid_send, mid_recv, far_send, far_recv = refs
        group, part, side = lax.axis_index("dp"), lax.axis_index("tensor"), lax.axis_index("seq")
        parts, groups_else = others("tensor"), others("dp")
        meet(
            [{"seq": 1 - side}]
            + [{"tensor": peer} for peer in parts]
            + [{"dp": peer} for peer in groups_else]
        )
        values = []
        for later in range(1, LAYERS + 1):
            grad = grad_refs[later - 1][...]
            for level in range(later + 1):
                values.append(jnp.sum(grad * state_refs[level][...], keepdims=True))
        loss = (home_ref[0:1, :] - home_ref[1:2, :]) * keep_ref[...]
        values.append(jnp.sum(loss, keepdims=True))
        values.append(jnp.sum(table_ref[...], keepdims=True) + layer_ref[...])
        lane = lax.broadcasted_iota(jnp.int32, (1, D), 1)
        row = jnp.zeros((1, D), jnp.float32)
        for place, value in enumerate(values):
            row = jnp.where(lane == place, value, row)
        blank = jnp.zeros((8 - gain_rows - 1, D), jnp.float32)
        total = jnp.concatenate([ref[...] for ref in gain_refs] + [row, blank], axis=0)
        stages = [
            ("seq", near, side, [1 - side], near_send, near_recv),
            ("tensor", mid, part, parts, mid_send, mid_recv),
            ("dp", far, group, groups_else, far_send, far_recv),
        ]
        for axis, slots, me, peers, send_sems, recv_sems in stages:
            slots[me] = total
            copies = [
                send(slots.at[me], slots.at[me], send_sems.at[step], recv_sems.at[step], {axis: peer})
                for step, peer in enumerate(peers)
            ]
            for copy in copies:
                copy.wait()
            total = slots[0]
            for index in range(1, slots.shape[0]):
                total = total + slots[index]
        gain_total = total[:gain_rows]
        row = total[gain_rows : gain_rows + 1]

        def pick(place):
            return jnp.sum(jnp.where(lane == place, row, 0.0), axis=1, keepdims=True)

        mix_squares = jnp.sum(jnp.where(lane < MIX_WEIGHTS, row * row, 0.0), axis=1, keepdims=True)
        gain_squares = jnp.sum(gain_total * gain_total, keepdims=True)
        tokens = count_ref[:, 0:1]
        clip_norm = jnp.sqrt(pick(MIX_WEIGHTS + 1) + gain_squares + mix_squares) / tokens
        factor = jnp.minimum(1.0, CLIP_NORM / clip_norm) / tokens
        gain_news = adam_update(
            *[ref[...] for ref in small_refs[:3]], gain_total * factor, RATE_SMALL, 0.0
        )
        mix_news = adam_update(
            *[ref[...] for ref in small_refs[3:]], row[:, :MIX_WEIGHTS] * factor, RATE_SMALL, 0.0
        )
        for ref, value in zip(out_refs[:6], gain_news + mix_news):
            ref[...] = value
        ends = jnp.where(lane == 0, pick(MIX_WEIGHTS), jnp.where(lane == 1, clip_norm, factor))
        out_refs[6][...] = ends[:, :LANES]
        out_refs[7][...] = jnp.broadcast_to(factor, (8, LANES))

    dma = pltpu.SemaphoreType.DMA
    vmem = pl.BlockSpec(memory_space=pltpu.VMEM)
    return pl.pallas_call(
        kernel,
        name="finish",
        out_shape=[jax.ShapeDtypeStruct(value.shape, jnp.float32) for value in smalls]
        + [
            jax.ShapeDtypeStruct((1, LANES), jnp.float32),
            jax.ShapeDtypeStruct((8, LANES), jnp.float32),
        ],
        in_specs=[vmem] * len(operands),
        out_specs=[vmem] * 8,
        scratch_shapes=[
            pltpu.VMEM((2,) + block, jnp.float32),
            pltpu.VMEM((tensors,) + block, jnp.float32),
            pltpu.VMEM((groups,) + block, jnp.float32),
            dma((1,)),
            dma((1,)),
            dma((tensors - 1,)),
            dma((tensors - 1,)),
            dma((groups - 1,)),
            dma((groups - 1,)),
        ],
        compiler_params=pltpu.CompilerParams(collective_id=collective_id, has_side_effects=True),
    )(*operands)


SLOT_STEP = 4


def update_slots(plan, factor, master, first, second, layer_grads, grad_table):
    slots, half_rows, _ = master.shape
    steps = -(-slots // SLOT_STEP)
    plan = jnp.pad(plan, ((0, 0), (0, steps * SLOT_STEP - slots)))

    def kernel(plan_ref, factor_ref, master_ref, first_ref, second_ref, *rest):
        layer_refs = rest[: LAYERS * SLOT_STEP]
        table_ref, new_master, new_first, new_second = rest[LAYERS * SLOT_STEP :]
        for place in range(SLOT_STEP):
            kind = plan_ref[0, pl.program_id(0) * SLOT_STEP + place]
            grad = table_ref[place * half_rows : (place + 1) * half_rows, :]
            for level in range(LAYERS):
                layer = layer_refs[level * SLOT_STEP + place][0].astype(jnp.float32)
                grad = jnp.where(kind == level, layer, grad)
            grad = jnp.where(kind >= 0, grad * factor_ref[0:1, 0:1], 0.0)
            values = adam_update(
                master_ref[place],
                first_ref[place],
                second_ref[place],
                grad,
                RATE_MATRIX,
                DECAY_MATRIX,
            )
            for ref, value in zip((new_master, new_first, new_second), values):
                ref[place] = value

    slot = pl.BlockSpec((SLOT_STEP, half_rows, D), lambda step, plan: (step, 0, 0))
    return pl.pallas_call(
        kernel,
        name="update_slots",
        grid_spec=pltpu.PrefetchScalarGridSpec(
            num_scalar_prefetch=1,
            grid=(steps,),
            in_specs=[pl.BlockSpec((8, LANES), lambda step, plan: (0, 0)), slot, slot, slot]
            + [
                pl.BlockSpec(
                    (1, half_rows, D),
                    lambda step, plan, level=level, place=place: (
                        plan[1 + level, step * SLOT_STEP + place],
                        0,
                        0,
                    ),
                )
                for level in range(LAYERS)
                for place in range(SLOT_STEP)
            ]
            + [pl.BlockSpec((SLOT_STEP * half_rows, D), lambda step, plan: (step, 0))],
            out_specs=[slot] * 3,
        ),
        out_shape=[jax.ShapeDtypeStruct(master.shape, jnp.float32)] * 3,
        compiler_params=pltpu.CompilerParams(vmem_limit_bytes=48 << 20),
    )(
        plan,
        factor,
        master,
        first,
        second,
        *[grads for grads in layer_grads for _ in range(SLOT_STEP)],
        grad_table,
    )


def row_of(groups_ref):
    return jnp.concatenate([groups_ref[0, g : g + 1, :] for g in range(TILE_GROUPS)], axis=1)


def stat_row(stat_ref, row):
    return jnp.concatenate([stat_ref[g, row : row + 1, :] for g in range(TILE_GROUPS)], axis=1)


def chunk_of(span_ref, step):
    return pl.ds(pl.multiple_of(span_ref[0] + step * ROW_STEP, 16), ROW_STEP)


def chunks_of(span_ref):
    return (span_ref[1] - span_ref[0] + ROW_STEP - 1) // ROW_STEP


def whole(shape):
    return pl.BlockSpec(shape, lambda step, span: (0,) * len(shape), pipeline_mode=pl.Buffered(1))


TILE = TILE_GROUPS * LANES
TOKENS_SPEC = pl.BlockSpec((1, TILE_GROUPS, LANES), lambda step, span: (step, 0, 0))
STATS_SPEC = pl.BlockSpec((TILE_GROUPS, 8, LANES), lambda step, span: (step, 0, 0))
ROWS_SPEC = pl.BlockSpec((TILE, D), lambda step, span: (step, 0))


def local_call(name, kernel, steps, span, operands, in_specs, out_shape, out_specs, scratch):
    return pl.pallas_call(
        kernel,
        name=name,
        grid_spec=pltpu.PrefetchScalarGridSpec(
            num_scalar_prefetch=1,
            grid=(steps,),
            in_specs=in_specs,
            out_specs=out_specs,
            scratch_shapes=scratch,
        ),
        out_shape=out_shape,
        compiler_params=pltpu.CompilerParams(vmem_limit_bytes=60 << 20),
    )(span, *operands)


def look_up(span, row_ids, tokens, table):
    rows = table.shape[0]
    steps = tokens.shape[0]

    def kernel(span_ref, ids_ref, tokens_ref, table_ref, out_ref, acc):
        acc[...] = jnp.zeros_like(acc)
        wanted = row_of(tokens_ref)

        def one(step, carry):
            chunk = chunk_of(span_ref, step)
            hits = jnp.where(ids_ref[chunk, :] == wanted, 1.0, 0.0).astype(jnp.bfloat16)
            acc[...] += contract_first(hits, table_ref[chunk, :])
            return carry

        lax.fori_loop(0, chunks_of(span_ref), one, 0)
        out_ref[...] = acc[...].astype(jnp.bfloat16)

    return local_call(
        "look_up",
        kernel,
        steps,
        span,
        (row_ids, tokens, table),
        [whole((rows, 1)), TOKENS_SPEC, whole((rows, D))],
        jax.ShapeDtypeStruct((steps * TILE, D), jnp.bfloat16),
        ROWS_SPEC,
        [pltpu.VMEM((TILE, D), jnp.float32)],
    )


def head_forward(span, row_ids, labels, table, final):
    rows = table.shape[0]
    steps = labels.shape[0]

    def kernel(span_ref, ids_ref, labels_ref, table_ref, final_ref, powers_ref, stats_ref, scores):
        wanted = row_of(labels_ref)
        hidden = final_ref[...]

        def first(step, carry):
            top, target = carry
            chunk = chunk_of(span_ref, step)
            ids = ids_ref[chunk, :]
            raw = contract_last(table_ref[chunk, :], hidden)
            raw = jnp.where(ids >= 0, raw, -1e30)
            scores[chunk, :] = raw
            top = jnp.maximum(top, jnp.max(raw, axis=0, keepdims=True))
            target = target + jnp.sum(jnp.where(ids == wanted, raw, 0.0), axis=0, keepdims=True)
            return (top, target)

        blank = jnp.zeros((1, TILE), jnp.float32)
        top, target = lax.fori_loop(0, chunks_of(span_ref), first, (blank - 1e30, blank))

        def second(step, total):
            chunk = chunk_of(span_ref, step)
            powers = jnp.exp(scores[chunk, :] - top)
            powers_ref[chunk, :] = powers.astype(jnp.bfloat16)
            return total + jnp.sum(powers, axis=0, keepdims=True)

        total = lax.fori_loop(0, chunks_of(span_ref), second, blank)
        rest = jnp.zeros((5, LANES), jnp.float32)
        for g in range(TILE_GROUPS):
            lanes = slice(g * LANES, (g + 1) * LANES)
            stats_ref[g] = jnp.concatenate(
                [top[:, lanes], total[:, lanes], target[:, lanes], rest], axis=0
            )

    return local_call(
        "head_forward",
        kernel,
        steps,
        span,
        (row_ids, labels, table, final),
        [whole((rows, 1)), TOKENS_SPEC, whole((rows, D)), ROWS_SPEC],
        [
            jax.ShapeDtypeStruct((rows, steps * TILE), jnp.bfloat16),
            jax.ShapeDtypeStruct((steps * TILE_GROUPS, 8, LANES), jnp.float32),
        ],
        [pl.BlockSpec((rows, TILE), lambda step, span: (0, step)), STATS_SPEC],
        [pltpu.VMEM((rows, TILE), jnp.float32)],
    )


def head_backward(span, row_ids, labels, keep, stats, log_totals, table, final, powers):
    rows = table.shape[0]
    steps = labels.shape[0]

    def kernel(
        span_ref, ids_ref, labels_ref, keep_ref, stats_ref, logs_ref, table_ref, final_ref,
        powers_ref, grad_final_ref, grad_table_ref, acc,
    ):
        @pl.when(pl.program_id(0) == 0)
        def _():
            grad_table_ref[...] = jnp.zeros_like(grad_table_ref)

        acc[...] = jnp.zeros_like(acc)
        wanted, kept = row_of(labels_ref), row_of(keep_ref)
        scale = jnp.exp(stat_row(stats_ref, 0) - stat_row(logs_ref, 0)) * kept
        hidden = final_ref[...]

        def one(step, carry):
            chunk = chunk_of(span_ref, step)
            grads = powers_ref[chunk, :].astype(jnp.float32) * scale
            grads = grads - jnp.where(ids_ref[chunk, :] == wanted, kept, 0.0)
            grads = grads.astype(jnp.bfloat16)
            grad_table_ref[chunk, :] += jnp.dot(grads, hidden, preferred_element_type=jnp.float32)
            acc[...] += contract_first(grads, table_ref[chunk, :])
            return carry

        lax.fori_loop(0, chunks_of(span_ref), one, 0)
        grad_final_ref[...] = acc[...].astype(jnp.bfloat16)

    return local_call(
        "head_backward",
        kernel,
        steps,
        span,
        (row_ids, labels, keep, stats, log_totals, table, final, powers),
        [
            whole((rows, 1)),
            TOKENS_SPEC,
            TOKENS_SPEC,
            STATS_SPEC,
            STATS_SPEC,
            whole((rows, D)),
            ROWS_SPEC,
            pl.BlockSpec((rows, TILE), lambda step, span: (0, step)),
        ],
        [
            jax.ShapeDtypeStruct((steps * TILE, D), jnp.bfloat16),
            jax.ShapeDtypeStruct((rows, D), jnp.float32),
        ],
        [ROWS_SPEC, whole((rows, D))],
        [pltpu.VMEM((TILE, D), jnp.float32)],
    )


def look_back(span, row_ids, tokens, grad_start, grad_table):
    rows = grad_table.shape[0]
    steps = tokens.shape[0]

    def kernel(span_ref, ids_ref, tokens_ref, grad_ref, table_ref, out_ref, squares_ref):
        @pl.when(pl.program_id(0) == 0)
        def _():
            out_ref[...] = table_ref[...]

        wanted = row_of(tokens_ref)
        grads = grad_ref[...]

        def one(step, carry):
            chunk = chunk_of(span_ref, step)
            hits = jnp.where(ids_ref[chunk, :] == wanted, 1.0, 0.0).astype(jnp.bfloat16)
            out_ref[chunk, :] += jnp.dot(hits, grads, preferred_element_type=jnp.float32)
            return carry

        lax.fori_loop(0, chunks_of(span_ref), one, 0)

        @pl.when(pl.program_id(0) == steps - 1)
        def _():
            def square(step, total):
                values = out_ref[chunk_of(span_ref, step), :]
                values = (values * values).reshape(ROW_STEP // 8, 8, D).sum(axis=0)
                return total + values

            squares_ref[...] = lax.fori_loop(
                0, chunks_of(span_ref), square, jnp.zeros((8, D), jnp.float32)
            )

    return local_call(
        "look_back",
        kernel,
        steps,
        span,
        (row_ids, tokens, grad_start, grad_table),
        [whole((rows, 1)), TOKENS_SPEC, ROWS_SPEC, whole((rows, D))],
        [
            jax.ShapeDtypeStruct((rows, D), jnp.float32),
            jax.ShapeDtypeStruct((8, D), jnp.float32),
        ],
        [whole((rows, D)), whole((8, D))],
        [],
    )


def attend(joined, geometry):
    cosine, sine, allowed, seq_count, half_len, local_heads = geometry
    width = local_heads * HEAD_DIM
    shape_four = (seq_count, half_len, local_heads, HEAD_DIM)
    queries = (
        rotate(joined[:, :width].reshape(-1, local_heads, HEAD_DIM), cosine, sine)
        .astype(jnp.bfloat16)
        .reshape(shape_four)
    )
    own_keys = (
        rotate(joined[:, width : 2 * width].reshape(-1, local_heads, HEAD_DIM), cosine, sine)
        .astype(jnp.bfloat16)
        .reshape(shape_four)
    )
    own_values = joined[:, 2 * width :].astype(jnp.bfloat16).reshape(shape_four)
    far_keys, far_values = from_behind((own_keys, own_values), "seq", 1)
    keys_all = jnp.concatenate([far_keys, own_keys], axis=1)
    values_all = jnp.concatenate([far_values, own_values], axis=1)
    scores = attention_scores(queries, keys_all, allowed)
    peak = jnp.max(scores, -1, keepdims=True)
    log_total = peak + jnp.log(jnp.sum(jnp.exp(scores - peak), -1, keepdims=True))
    probs = jnp.exp(scores - log_total).astype(jnp.bfloat16)
    attended = jnp.einsum("bhqk,bkhd->bqhd", probs, values_all, preferred_element_type=jnp.float32)
    attended = attended.astype(jnp.bfloat16).reshape(-1, width)
    return attended, (queries, keys_all, values_all, log_total)


def attend_back(grad_attended, kept, geometry):
    queries, keys_all, values_all, log_total = kept
    cosine, sine, allowed, seq_count, half_len, local_heads = geometry
    width = local_heads * HEAD_DIM
    grad_attended = grad_attended.reshape(seq_count, half_len, local_heads, HEAD_DIM)
    probs = jnp.exp(attention_scores(queries, keys_all, allowed) - log_total)
    grad_probs = jnp.einsum(
        "bqhd,bkhd->bhqk", grad_attended, values_all, preferred_element_type=jnp.float32
    )
    grad_scores = (probs * (grad_probs - jnp.sum(probs * grad_probs, -1, keepdims=True))).astype(
        jnp.bfloat16
    )
    scale = HEAD_DIM ** (-0.5)
    grad_queries = (
        jnp.einsum("bhqk,bkhd->bqhd", grad_scores, keys_all, preferred_element_type=jnp.float32)
        * scale
    )
    grad_keys = (
        jnp.einsum("bhqk,bqhd->bkhd", grad_scores, queries, preferred_element_type=jnp.float32)
        * scale
    )
    grad_values = jnp.einsum(
        "bhqk,bqhd->bkhd",
        probs.astype(jnp.bfloat16),
        grad_attended,
        preferred_element_type=jnp.float32,
    )
    back_keys, back_values = (
        from_behind(grad_keys[:, :half_len].astype(jnp.bfloat16), "seq", -1).astype(jnp.float32),
        from_behind(grad_values[:, :half_len].astype(jnp.bfloat16), "seq", -1).astype(jnp.float32),
    )
    grad_keys = grad_keys[:, half_len:] + back_keys
    grad_values = grad_values[:, half_len:] + back_values
    return jnp.concatenate(
        [
            rotate(grad_queries.reshape(-1, local_heads, HEAD_DIM), cosine, -sine).reshape(
                -1, width
            ),
            rotate(grad_keys.reshape(-1, local_heads, HEAD_DIM), cosine, -sine).reshape(-1, width),
            grad_values.reshape(-1, width),
        ],
        axis=1,
    ).astype(jnp.bfloat16)


def body(
    token_ids,
    labels,
    real_counts,
    owners,
    master,
    first_moment,
    second_moment,
    gains,
    gains_first,
    gains_second,
    mix,
    mix_first,
    mix_second,
):
    tensors = lax.axis_size("tensor")
    groups = lax.axis_size("dp")
    group = lax.axis_index("dp")
    tensor_part = lax.axis_index("tensor")
    seq_part = lax.axis_index("seq")
    slots, half_rows, _ = master.shape
    seq_count, half_len = token_ids.shape
    row_count = seq_count * half_len
    share = row_count // tensors
    head_rows = 3 * D // tensors
    out_rows = D // tensors
    unit_rows = FF // tensors
    layer_rows = head_rows + out_rows + 2 * unit_rows
    layer_blocks = layer_rows // (2 * half_rows)
    blocks = LAYERS * layer_blocks
    vocab_rows = VOCAB // tensors
    local_heads = HEADS // tensors

    slot_rank = slot_table(owners)
    block_ids = jnp.arange(owners.shape[0], dtype=jnp.int32)
    mine = owners == group
    match = (jnp.arange(slots)[:, None] == slot_rank[None, :]) & mine[None, :]
    slot_block = jnp.sum(jnp.where(match, block_ids[None, :] + 1, 0), axis=1) - 1
    row_ids = (
        tensor_part * vocab_rows
        + (slot_block[:, None] - blocks) * (2 * half_rows)
        + seq_part * half_rows
        + jnp.arange(half_rows, dtype=jnp.int32)[None, :]
    )
    row_ids = jnp.where(slot_block[:, None] >= blocks, row_ids, -1).reshape(-1, 1)
    spare = -(-ROW_STEP // half_rows)
    row_ids = jnp.pad(row_ids, ((0, spare * half_rows), (0, 0)), constant_values=-1)
    held = jnp.sum(jnp.where(mine, 1, 0)) * half_rows
    first_held = jnp.sum(jnp.where(mine & (block_ids < blocks), 1, 0)) * half_rows
    span = jnp.stack([first_held, held]).astype(jnp.int32)
    level_of = jnp.where(slot_block < 0, -1, jnp.minimum(slot_block // layer_blocks, LAYERS))
    plan = jnp.stack(
        [level_of]
        + [
            jnp.where(level_of == level, slot_block - level * layer_blocks, 0)
            for level in range(LAYERS)
        ]
    ).astype(jnp.int32)

    packed = jnp.concatenate(
        [
            token_ids.reshape(tensors, LANES),
            labels.reshape(tensors, LANES),
            jnp.broadcast_to(real_counts[:, None], (16 - 2 * tensors, LANES)),
        ],
        axis=0,
    )
    ids_all, labels_all, keep_all, count = spread_tokens(packed, 15)
    order = (2, tensors, groups, share)

    table_slots = jnp.pad(master.astype(jnp.bfloat16), ((0, spare), (0, 0), (0, 0)))
    table = table_slots.reshape(-1, D)

    halves = []
    for level in range(LAYERS):
        chosen = slice(level * layer_blocks, (level + 1) * layer_blocks)
        halves.append(
            jnp.where(
                mine[chosen][:, None, None], jnp.take(table_slots, slot_rank[chosen], axis=0), 0.0
            ).astype(jnp.bfloat16)
        )
    halves[1:] = [lax.psum(half, "dp") for half in halves[1:]]

    def cut(joined):
        joined = joined.reshape(layer_rows, D)
        cut_one, cut_two = head_rows + out_rows, head_rows + out_rows + unit_rows
        return (joined[:head_rows], joined[head_rows:cut_one], joined[cut_one:cut_two], joined[cut_two:])

    positions = seq_part * half_len + jnp.arange(row_count) % half_len
    cosine, sine = rotary(positions)
    query_pos = seq_part * half_len + jnp.arange(half_len)
    key_pos = jnp.concatenate([(seq_part - 1) * half_len + jnp.arange(half_len), query_pos])
    allowed = (key_pos[None, :] <= query_pos[:, None]) & (key_pos[None, :] >= 0)
    geometry = (cosine, sine, allowed, seq_count, half_len, local_heads)

    looked = look_up(span, row_ids, ids_all, table).reshape(order + (D,))
    start, joined = reduce_rows(looked, (0, 14), halves[0])
    weights_all = [cut(joined)]
    gain = [gains[i : i + 1] for i in range(2 * LAYERS + 1)]
    piece = ((share, D), jnp.float32)

    def normed_of(total, stream, gain_row):
        return (layer_norm_parts(stream)[0] * gain_row,)

    def inner_of(total, stream, gain_row):
        inner = stream + total
        return (inner, layer_norm_parts(inner)[0] * gain_row)

    def outcome_of(base, total, inner, gain_row, *rest):
        states, scalars = rest[:-1], rest[-1]
        outcome = inner + total
        stream = scalars[base + len(states)] * outcome
        for source, state in enumerate(states):
            stream = stream + scalars[base + source] * state
        return (outcome, stream, layer_norm_parts(stream)[0] * gain_row)

    (normed,) = tensor_step("normed", normed_of, None, (start, gain[0]), (), [], True, 1)
    states, streams, inners, kept_all = [start], [start], [], []
    for level in range(LAYERS):
        qkv_w, out_w, up_w, down_w = weights_all[level]
        normed = normed.reshape(row_count, D)
        attended, kept = attend(contract_last(normed, qkv_w), geometry)
        inner, normed_two = tensor_step(
            "inner",
            inner_of,
            jnp.dot(attended, out_w, preferred_element_type=jnp.float32),
            (streams[level], gain[2 * level + 1]),
            (),
            [piece],
            True,
            2,
        )
        normed_two = normed_two.reshape(row_count, D)
        hidden = contract_last(normed_two, up_w)
        activated = jax.nn.gelu(hidden, approximate=True).astype(jnp.bfloat16)
        last = level == LAYERS - 1
        results = tensor_step(
            f"outcome_{level}",
            partial(outcome_of, (level + 1) * (level + 2) // 2 - 1),
            jnp.dot(activated, down_w, preferred_element_type=jnp.float32),
            [inner, gain[2 * level + 2]] + states,
            (mix,),
            [piece, piece] + ([((share, D), jnp.bfloat16)] if last else []),
            not last,
            3 + level,
            *((None, None) if last else ("share", halves[level + 1])),
        )
        if not last:
            weights_all.append(cut(results[3]))
        inners.append(inner)
        kept_all.append((normed, kept, attended, normed_two, hidden, activated))
        states.append(results[0])
        streams.append(results[1])
        normed = results[2]

    final_all = gather_all(normed, 3 + LAYERS)[0].reshape(-1, D)
    powers, stats = head_forward(span, row_ids, labels_all, table, final_all)
    home, log_totals = join_stats(
        stats.reshape((2, tensors, groups, 8, LANES)), 4 + LAYERS
    )
    grad_final, grad_table = head_backward(
        span,
        row_ids,
        labels_all,
        keep_all,
        stats,
        log_totals.reshape(-1, 8, LANES),
        table,
        final_all,
        powers,
    )
    grad_final, _ = reduce_rows(grad_final.reshape(order + (D,)), (0, 14))

    row = ((1, D), jnp.float32)

    def top_of(total, grad, stream, gain_row, scalars):
        grad_top, grad_gain = norm_pull(grad, gain_row, stream)
        grad_state = scalars[MIX_WEIGHTS - 1] * grad_top
        return (grad_top, grad_state, grad_gain, grad_state)

    def inner_back(total, grad_out, inner, gain_row):
        grad, grad_gain = norm_pull(total, gain_row, inner)
        grad = grad_out + grad
        return (grad, grad_gain, grad)

    def stream_back(block, total, grad_inner, stream, gain_row, *rest):
        grad_ys, scalars = rest[:-1], rest[-1]
        grad, grad_gain = norm_pull(total, gain_row, stream)
        grad = grad_inner + grad
        state = grad if block == 0 else scalars[block * (block + 1) // 2 - 1 + block] * grad
        for offset, grad_y in enumerate(grad_ys):
            later = block + 1 + offset
            state = state + scalars[later * (later + 1) // 2 - 1 + block] * grad_y
        return (grad, state, grad_gain, state)

    grad_ys = [None] * (LAYERS + 1)
    gain_grads = [None] * (2 * LAYERS + 1)
    layer_grads = [None] * LAYERS
    grad_ys[LAYERS], grad_state, gain_grads[2 * LAYERS], grad_branch = tensor_step(
        "top_back",
        top_of,
        None,
        (grad_final, streams[LAYERS], gain[2 * LAYERS]),
        (mix,),
        [piece, piece, row],
        True,
        5 + LAYERS,
    )
    for level in reversed(range(LAYERS)):
        qkv_w, out_w, up_w, down_w = weights_all[level]
        normed, kept, attended, normed_two, hidden, activated = kept_all[level]
        grad_branch = grad_branch.reshape(row_count, D)
        grad_act = contract_last(grad_branch, down_w)
        _, gelu_pull = jax.vjp(partial(jax.nn.gelu, approximate=True), hidden)
        grad_hidden = gelu_pull(grad_act)[0].astype(jnp.bfloat16)
        grad_inner, gain_grads[2 * level + 1], grad_attn = tensor_step(
            "inner_back",
            inner_back,
            jnp.dot(grad_hidden, up_w, preferred_element_type=jnp.float32),
            (grad_state, inners[level], gain[2 * level + 1]),
            (),
            [piece, row],
            True,
            6 + LAYERS,
        )
        grad_attn = grad_attn.reshape(row_count, D)
        grad_attended = contract_last(grad_attn, out_w).astype(jnp.bfloat16)
        grad_joined = attend_back(grad_attended, kept, geometry)
        grads = jnp.concatenate(
            [
                contract_first(grad_joined, normed),
                contract_first(attended, grad_attn),
                contract_first(grad_hidden, normed_two),
                contract_first(activated, grad_branch),
            ],
            axis=0,
        ).astype(jnp.bfloat16)
        results = tensor_step(
            f"stream_back_{level}",
            partial(stream_back, level),
            jnp.dot(grad_joined, qkv_w, preferred_element_type=jnp.float32),
            [grad_inner, streams[level], gain[2 * level]] + grad_ys[level + 1 :],
            (mix,),
            [piece, piece, row] + ([] if level else [((share, D), jnp.bfloat16)]),
            level > 0,
            7 + LAYERS + level,
            "fold",
            grads.reshape(layer_blocks, 2, half_rows, D),
        )
        grad_ys[level], grad_state, gain_grads[2 * level], grad_branch, folded = results
        layer_grads[level] = lax.psum(folded, "dp") if level else folded

    grad_start_all, layer_grads[0] = gather_all(grad_branch, 13, layer_grads[0])
    grad_start_all = grad_start_all.reshape(-1, D)
    grad_table, table_squares = look_back(span, row_ids, ids_all, grad_start_all, grad_table)
    layer_squares = jnp.zeros((), jnp.float32)
    for level in range(LAYERS):
        chosen = slice(level * layer_blocks, (level + 1) * layer_blocks)
        values = layer_grads[level].astype(jnp.float32)
        layer_squares += jnp.sum(jnp.where(mine[chosen][:, None, None], values * values, 0.0))
    keep = jnp.where(
        tensor_part * share + jnp.arange(share) < real_counts[0], 1.0, 0.0
    ).astype(jnp.float32)
    news = finish(
        gain_grads,
        states,
        grad_ys[1:],
        home,
        keep[None],
        table_squares,
        layer_squares.reshape(1, 1),
        count,
        (gains, gains_first, gains_second, mix[None], mix_first[None], mix_second[None]),
        7 + 2 * LAYERS,
    )
    new_gains, new_gains_first, new_gains_second = news[:3]
    new_mix, new_mix_first, new_mix_second = [value[0] for value in news[3:6]]
    loss_sum, clip_norm = news[6][0, 0], news[6][0, 1]
    token_count = count[0, 0]
    new_master, new_first, new_second = update_slots(
        plan, news[7], master, first_moment, second_moment, layer_grads, grad_table
    )
    return (
        new_master,
        new_first,
        new_second,
        new_gains,
        new_gains_first,
        new_gains_second,
        new_mix,
        new_mix_first,
        new_mix_second,
        loss_sum,
        token_count,
        clip_norm,
    )


def solution(mesh):
    return jax.shard_map(
        body,
        mesh=mesh,
        in_specs=(
            P("dp", "seq"),
            P("dp", "seq"),
            P(("dp", "seq")),
            P(),
            P("dp", ("tensor", "seq"), None),
            P("dp", ("tensor", "seq"), None),
            P("dp", ("tensor", "seq"), None),
            P(),
            P(),
            P(),
            P(),
            P(),
            P(),
        ),
        out_specs=(
            P("dp", ("tensor", "seq"), None),
            P("dp", ("tensor", "seq"), None),
            P("dp", ("tensor", "seq"), None),
            P(),
            P(),
            P(),
            P(),
            P(),
            P(),
            P(),
            P(),
            P(),
        ),
        check_vma=False,
    )
```

```python
from functools import partial

import jax
import jax.numpy as jnp
from jax import lax
from jax.experimental import pallas as pl
from jax.experimental.pallas import tpu as pltpu
from jax.sharding import PartitionSpec as P

D = 768
HEADS = 12
HEAD_DIM = 64
FF = 3072
VOCAB = 50304
LAYERS = 2
STEP_COUNT = 10
MIX_WEIGHTS = 5


EPS_NORM = 1e-05
CLIP_NORM = 0.01
BETA_ONE = 0.9
BETA_TWO = 0.95
ADAM_EPS = 1e-08
RATE_MATRIX = 0.04
RATE_SMALL = 0.4
DECAY_MATRIX = 0.1


def contract_last(left, right):
    return lax.dot_general(
        left, right, (((1,), (1,)), ((), ())), preferred_element_type=jnp.float32
    )


def contract_first(left, right):
    return lax.dot_general(
        left, right, (((0,), (0,)), ((), ())), preferred_element_type=jnp.float32
    )


def slot_table(owners):
    ranks = jnp.arange(owners.shape[0])
    same = (owners[None, :] == owners[:, None]) & (ranks[None, :] < ranks[:, None])
    return jnp.sum(jnp.where(same, 1, 0), axis=1).astype(jnp.int32)


def adam_update(weight, first, second, grad, rate, decay):
    first = BETA_ONE * first + (1.0 - BETA_ONE) * grad
    second = BETA_TWO * second + (1.0 - BETA_TWO) * grad * grad
    first_hat = first / (1.0 - BETA_ONE**STEP_COUNT)
    second_hat = second / (1.0 - BETA_TWO**STEP_COUNT)
    weight = weight - rate * (first_hat / (jnp.sqrt(second_hat) + ADAM_EPS) + decay * weight)
    return (weight, first, second)


MESH = pl.DeviceIdType.MESH
ROW_STEP = 400
TILE_GROUPS = 8
LANES = 128
SHORT = pl.CostEstimate(flops=1000, bytes_accessed=1000, transcendentals=0)


def meet(peers):
    gate = pltpu.get_barrier_semaphore()
    for peer in peers:
        pl.semaphore_signal(gate, inc=1, device_id=peer, device_id_type=MESH)
    pl.semaphore_wait(gate, len(peers))


def others(axis):
    count, me = lax.axis_size(axis), lax.axis_index(axis)
    return [lax.rem(me + step, count) for step in range(1, count)]


def behind(axis, step):
    count, me = lax.axis_size(axis), lax.axis_index(axis)
    return lax.rem(me + count - step, count)


def send(source, target, send_sem, recv_sem, device):
    copy = pltpu.make_async_remote_copy(
        src_ref=source,
        dst_ref=target,
        send_sem=send_sem,
        recv_sem=recv_sem,
        device_id=device,
        device_id_type=MESH,
    )
    copy.start()
    return copy


def layer_norm_parts(stream):
    center = stream - jnp.mean(stream, -1, keepdims=True)
    inverse = lax.rsqrt(jnp.mean(center * center, -1, keepdims=True) + EPS_NORM)
    return center * inverse, inverse


def norm_pull(grad_normed, gain, stream):
    scaled, inverse = layer_norm_parts(stream)
    grad_scaled = grad_normed * gain
    grad_stream = inverse * (
        grad_scaled
        - jnp.mean(grad_scaled, -1, keepdims=True)
        - scaled * jnp.mean(grad_scaled * scaled, -1, keepdims=True)
    )
    return grad_stream, jnp.sum(grad_normed * scaled, axis=0, keepdims=True)


class Work:
    def __init__(self, before, during, operands, specs, outs, scratch, after=None, twins=False):
        self.before, self.during, self.after, self.twins = before, during, after, twins
        self.operands, self.specs, self.outs, self.scratch = operands, specs, outs, scratch


def tensor_step(name, function, work, extras, scalars, outs, gather, collective_id, rider=None):
    parts = lax.axis_size("tensor")
    share = extras[0].shape[0]
    reduce = work is not None
    work = work or Work(None, None, [], [], [], [])

    def kernel(*refs):
        refs = list(refs)

        def take(count):
            return [refs.pop(0) for _ in range(count)]

        work_refs = take(len(work.operands))
        extra_refs = take(len(extras))
        scalar_refs = take(len(scalars))
        (rider_ref,) = take(1) if rider is not None else [None]
        out_refs = take(len(outs))
        (full,) = take(1) if gather else [None]
        work_outs = take(len(work.outs))
        (joined,) = take(1) if rider is not None else [None]
        send_sems, recv_sems = take(2)
        partial_ref, outgoing, arrived = take(3) if reduce else [None] * 3
        own_sem, twin_send, twin_recv = take(3) if rider is not None else [None] * 3
        me, side = lax.axis_index("tensor"), lax.axis_index("seq")
        peers = others("tensor")
        twin = {"seq": 1 - side}
        twins = work.twins or rider is not None
        meet([{"tensor": peer} for peer in peers] + [twin] * twins)
        if rider is not None:
            own_copy = pltpu.make_async_copy(rider_ref, joined.at[:, side], own_sem)
            own_copy.start()
            twin_copy = send(rider_ref, joined.at[:, side], twin_send, twin_recv, twin)
        total = None
        if reduce:
            work.before(work_refs, work_outs, refs, partial_ref)
            copies = []
            for step, peer in enumerate(peers):
                rows = pl.ds(pl.multiple_of(peer * share, share), share)
                outgoing[step] = partial_ref[rows, :].astype(jnp.bfloat16)
                copies.append(
                    send(
                        outgoing.at[step],
                        arrived.at[step],
                        send_sems.at[0, step],
                        recv_sems.at[0, step],
                        {"tensor": peer},
                    )
                )
            if work.during:
                work.during(work_refs, work_outs, refs)
            total = partial_ref[pl.ds(pl.multiple_of(me * share, share), share), :]
            for step, copy in enumerate(copies):
                copy.wait()
                total = total + arrived[step].astype(jnp.float32)
        results = function(total, *[ref[...] for ref in extra_refs], *scalar_refs)
        for ref, value in zip(out_refs, results):
            ref[...] = value.astype(ref.dtype)
        if gather:
            full[me] = results[len(outs)].astype(jnp.bfloat16)
            copies = [
                send(
                    full.at[me],
                    full.at[me],
                    send_sems.at[1, step],
                    recv_sems.at[1, step],
                    {"tensor": peer},
                )
                for step, peer in enumerate(peers)
            ]
        if work.after:
            work.after(work_refs, work_outs, refs)
        if rider is not None:
            own_copy.wait()
            twin_copy.wait()
        if gather:
            for copy in copies:
                copy.wait()

    vmem = pl.BlockSpec(memory_space=pltpu.VMEM)
    anywhere = pl.BlockSpec(memory_space=pl.ANY)
    smem = pl.BlockSpec(memory_space=pltpu.SMEM)
    shapes = [jax.ShapeDtypeStruct(shape, dtype) for shape, dtype in outs]
    if gather:
        shapes.append(jax.ShapeDtypeStruct((parts, share, D), jnp.bfloat16))
    shapes += [jax.ShapeDtypeStruct(shape, dtype) for shape, dtype in work.outs]
    out_specs = [vmem] * len(shapes)
    operands = list(work.operands) + list(extras) + list(scalars)
    in_specs = list(work.specs) + [vmem] * len(extras) + [smem] * len(scalars)
    dma = pltpu.SemaphoreType.DMA
    buffers = [dma((2, parts - 1))] * 2
    if reduce:
        buffers += [pltpu.VMEM((parts * share, D), jnp.float32)]
        buffers += [pltpu.VMEM((parts - 1, share, D), jnp.bfloat16)] * 2
    if rider is not None:
        operands.append(rider)
        in_specs.append(anywhere)
        count, half_rows, _ = rider.shape
        shapes.append(jax.ShapeDtypeStruct((count, 2, half_rows, D), jnp.bfloat16))
        out_specs.append(anywhere)
        buffers += [dma] * 3
    return pl.pallas_call(
        kernel,
        name=name,
        grid=(1,),
        out_shape=shapes,
        in_specs=in_specs,
        out_specs=out_specs,
        scratch_shapes=buffers + list(work.scratch),
        cost_estimate=SHORT,
        compiler_params=pltpu.CompilerParams(
            collective_id=collective_id, has_side_effects=True, vmem_limit_bytes=50 << 20
        ),
    )(*operands)


VMEM_SPEC = pl.BlockSpec(memory_space=pltpu.VMEM)


def part_spec(rows, index):
    return pl.BlockSpec((rows, D), lambda step: (index, 0), pipeline_mode=pl.Buffered(1))


def turn(block, cosine, sine):
    half = HEAD_DIM // 2
    first, second = block[:half], block[half:]
    return jnp.concatenate(
        [first * cosine - second * sine, second * cosine + first * sine], axis=0
    )


def times(left, right):
    return jnp.dot(left, right, preferred_element_type=jnp.float32)


def scores_of(keys_values, head, queries, side):
    span = slice(head * HEAD_DIM, (head + 1) * HEAD_DIM)
    count = queries.shape[1]
    scale = HEAD_DIM ** (-0.5)
    far = contract_first(keys_values[0, 0, span, :], queries) * scale
    own = contract_first(keys_values[1, 0, span, :], queries) * scale
    key = lax.broadcasted_iota(jnp.int32, (count, count), 0)
    query = lax.broadcasted_iota(jnp.int32, (count, count), 1)
    own = jnp.where(key <= query, own, -1e30)
    far = jnp.where(query + side * (2 * count) >= 2 * count, far, -1e30)
    return far, own


def attention_work(normed, table, cosine, sine):
    parts, share, _ = normed.shape
    count = parts * share
    width = D // parts
    heads = width // HEAD_DIM

    def before(ins, outs, scratch, partial_ref):
        normed_ref, qkv_ref, out_ref, cosine_ref, sine_ref = ins
        queries_ref, both, logs_ref, attended_ref = outs
        send_sem, recv_sem = scratch
        side = lax.axis_index("seq")
        cosine, sine = cosine_ref[...], sine_ref[...]
        rows = normed_ref[...].reshape(count, D)
        joined = contract_last(qkv_ref[...], rows)
        for head in range(heads):
            span = slice(head * HEAD_DIM, (head + 1) * HEAD_DIM)
            keys = joined[width + head * HEAD_DIM : width + (head + 1) * HEAD_DIM]
            both[1, 0, span, :] = turn(keys, cosine, sine).astype(jnp.bfloat16)
        both[1, 1] = joined[2 * width :].astype(jnp.bfloat16)
        copy = pltpu.make_async_remote_copy(
            src_ref=both.at[1],
            dst_ref=both.at[0],
            send_sem=send_sem,
            recv_sem=recv_sem,
            device_id={"seq": 1 - side},
            device_id_type=MESH,
        )

        copy.start()
        for head in range(heads):
            span = slice(head * HEAD_DIM, (head + 1) * HEAD_DIM)
            queries_ref[span, :] = turn(joined[span], cosine, sine).astype(jnp.bfloat16)

        copy.wait()
        for head in range(heads):
            span = slice(head * HEAD_DIM, (head + 1) * HEAD_DIM)
            far, own = scores_of(both, head, queries_ref[span, :], side)
            peak = jnp.maximum(
                jnp.max(far, axis=0, keepdims=True), jnp.max(own, axis=0, keepdims=True)
            )
            far, own = jnp.exp(far - peak), jnp.exp(own - peak)
            total = jnp.sum(far, axis=0, keepdims=True) + jnp.sum(own, axis=0, keepdims=True)
            logs_ref[head] = peak + jnp.log(total)
            inverse = 1.0 / total
            attended = times(both[0, 1, span, :], (far * inverse).astype(jnp.bfloat16))
            attended += times(both[1, 1, span, :], (own * inverse).astype(jnp.bfloat16))
            attended_ref[span, :] = attended.astype(jnp.bfloat16)
        partial_ref[...] = contract_first(attended_ref[...], out_ref[...])

    low = jnp.bfloat16
    return Work(
        before,
        None,
        [normed, table, table, cosine, sine],
        [VMEM_SPEC, part_spec(3 * width, 0), part_spec(width, 3), VMEM_SPEC, VMEM_SPEC],
        [
            ((width, count), low),
            ((2, 2, width, count), low),
            ((heads, 1, count), jnp.float32),
            ((width, count), low),
        ],
        [pltpu.SemaphoreType.DMA, pltpu.SemaphoreType.DMA],
        twins=True,
    )


def attention_back_work(grad, normed, table, kept, cosine, sine, unit_grads):
    parts, share, _ = normed.shape
    count = parts * share
    width = D // parts
    heads = width // HEAD_DIM
    queries, both, logs, attended = kept
    half_rows = unit_grads[0].shape[2]
    joined_blocks, out_blocks = 3 * width // (2 * half_rows), width // (2 * half_rows)
    unit_blocks = unit_grads[0].shape[0]
    starts = [0, joined_blocks, joined_blocks + out_blocks, joined_blocks + out_blocks + unit_blocks]
    sizes = [joined_blocks, out_blocks, unit_blocks, unit_blocks]
    blocks = sum(sizes)

    def twin_copy(source, target, send_sem, recv_sem):
        return pltpu.make_async_remote_copy(
            src_ref=source,
            dst_ref=target,
            send_sem=send_sem,
            recv_sem=recv_sem,
            device_id={"seq": 1 - lax.axis_index("seq")},
            device_id_type=MESH,
        )

    def fold_copy(index, source, refs):
        near, fold_send, fold_recv = refs
        side = lax.axis_index("seq")
        rows = pl.ds(starts[index], sizes[index])
        return twin_copy(
            source.at[:, 1 - side], near.at[rows], fold_send.at[index], fold_recv.at[index]
        )

    def before(ins, outs, scratch, partial_ref):
        grad_ref, _, qkv_ref, out_ref, queries_ref, both, logs_ref, _, cosine_ref, sine_ref = ins[:10]
        back, came, grad_joined, send_sem, recv_sem = scratch[:5]
        side = lax.axis_index("seq")
        for index, source in zip((2, 3), ins[10:]):
            fold_copy(index, source, scratch[7:]).start()
        cosine, sine = cosine_ref[...], -sine_ref[...]
        scale = HEAD_DIM ** (-0.5)
        grads = contract_last(out_ref[...], grad_ref[...].reshape(count, D)).astype(jnp.bfloat16)
        own_grads = []
        for head in range(heads):
            span = slice(head * HEAD_DIM, (head + 1) * HEAD_DIM)
            head_queries, head_grads = queries_ref[span, :], grads[span]
            far, own = scores_of(both, head, head_queries, side)
            far, own = jnp.exp(far - logs_ref[head]), jnp.exp(own - logs_ref[head])
            far_grad = contract_first(both[0, 1, span, :], head_grads)
            own_grad = contract_first(both[1, 1, span, :], head_grads)
            mean = jnp.sum(far * far_grad, axis=0, keepdims=True)
            mean += jnp.sum(own * own_grad, axis=0, keepdims=True)
            far_grad = (far * (far_grad - mean)).astype(jnp.bfloat16)
            own_grad = (own * (own_grad - mean)).astype(jnp.bfloat16)
            far, own = far.astype(jnp.bfloat16), own.astype(jnp.bfloat16)
            back[0, span, :] = (contract_last(head_queries, far_grad) * scale).astype(jnp.bfloat16)
            back[1, span, :] = contract_last(head_grads, far).astype(jnp.bfloat16)
            query_grad = times(both[0, 0, span, :], far_grad) + times(both[1, 0, span, :], own_grad)
            grad_joined[span, :] = turn(query_grad * scale, cosine, sine).astype(jnp.bfloat16)
            own_grads.append(
                (contract_last(head_queries, own_grad) * scale, contract_last(head_grads, own))
            )
        copy = twin_copy(back, came, send_sem, recv_sem)
        copy.start()
        copy.wait()
        for head, (key_grad, value_grad) in enumerate(own_grads):
            span = slice(head * HEAD_DIM, (head + 1) * HEAD_DIM)
            key_grad = key_grad + came[0, span, :].astype(jnp.float32)
            value_grad = value_grad + came[1, span, :].astype(jnp.float32)
            start = width + head * HEAD_DIM
            grad_joined[start : start + HEAD_DIM, :] = turn(key_grad, cosine, sine).astype(
                jnp.bfloat16
            )
            start += width
            grad_joined[start : start + HEAD_DIM, :] = value_grad.astype(jnp.bfloat16)
        partial_ref[...] = contract_first(grad_joined[...], qkv_ref[...])

    def during(ins, outs, scratch):
        grad_ref, normed_ref, attended_ref = ins[0], ins[1], ins[7]
        grad_joined, joined_part, out_part = scratch[2], scratch[5], scratch[6]
        value = times(grad_joined[...], normed_ref[...].reshape(count, D))
        joined_part[...] = value.astype(jnp.bfloat16).reshape(joined_part.shape)
        fold_copy(0, joined_part, scratch[7:]).start()
        value = times(attended_ref[...], grad_ref[...].reshape(count, D))
        out_part[...] = value.astype(jnp.bfloat16).reshape(out_part.shape)
        fold_copy(1, out_part, scratch[7:]).start()

    def after(ins, outs, scratch):
        side = lax.axis_index("seq")
        (folded,) = outs
        near = scratch[7]
        sources = [scratch[5], scratch[6], ins[10], ins[11]]
        for index in (2, 3, 0, 1):
            source, start = sources[index], starts[index]
            fold_copy(index, source, scratch[7:]).wait()

            def add_block(block, carry):
                value = source[block, side].astype(jnp.float32)
                value = value + near[start + block].astype(jnp.float32)
                folded[start + block] = value.astype(jnp.bfloat16)
                return carry

            lax.fori_loop(0, sizes[index], add_block, 0)

    low = jnp.bfloat16
    dma = pltpu.SemaphoreType.DMA
    return Work(
        before,
        during,
        [grad, normed, table, table, queries, both, logs, attended, cosine, sine] + list(unit_grads),
        [VMEM_SPEC, VMEM_SPEC, part_spec(3 * width, 0), part_spec(width, 3)] + [VMEM_SPEC] * 8,
        [((blocks, half_rows, D), low)],
        [
            pltpu.VMEM((2, width, count), low),
            pltpu.VMEM((2, width, count), low),
            pltpu.VMEM((3 * width, count), low),
            dma,
            dma,
            pltpu.VMEM((joined_blocks, 2, half_rows, D), low),
            pltpu.VMEM((out_blocks, 2, half_rows, D), low),
            pltpu.VMEM((blocks, half_rows, D), low),
            dma((4,)),
            dma((4,)),
        ],
        after,
        True,
    )


def gelu(hidden):
    return jax.nn.gelu(hidden, approximate=True)


def unit_work(normed, table):
    parts, share, _ = normed.shape
    count = parts * share
    units = FF // parts

    def before(ins, outs, scratch, partial_ref):
        normed_ref, up_ref, down_ref = ins
        hidden_ref, activated_ref = outs
        hidden = contract_last(up_ref[...], normed_ref[...].reshape(count, D))
        hidden_ref[...] = hidden
        activated_ref[...] = gelu(hidden).astype(jnp.bfloat16)
        partial_ref[...] = contract_first(activated_ref[...], down_ref[...])

    return Work(
        before,
        None,
        [normed, table, table],
        [VMEM_SPEC, part_spec(units, 1), part_spec(units, 2)],
        [((units, count), jnp.float32), ((units, count), jnp.bfloat16)],
        [],
    )


def unit_back_work(grad, normed, table, kept, half_rows):
    parts, share, _ = normed.shape
    count = parts * share
    units = FF // parts
    hidden, activated = kept

    def before(ins, outs, scratch, partial_ref):
        grad_ref, _, up_ref, down_ref, hidden_ref, _ = ins
        (grad_hidden,) = scratch
        grad_act = contract_last(down_ref[...], grad_ref[...].reshape(count, D))
        _, pull = jax.vjp(gelu, hidden_ref[...])
        grad_hidden[...] = pull(grad_act)[0].astype(jnp.bfloat16)
        partial_ref[...] = contract_first(grad_hidden[...], up_ref[...])

    def during(ins, outs, scratch):
        grad_ref, normed_ref, _, _, _, activated_ref = ins
        up_grad, down_grad = outs
        (grad_hidden,) = scratch
        value = times(grad_hidden[...], normed_ref[...].reshape(count, D))
        up_grad[...] = value.astype(jnp.bfloat16).reshape(up_grad.shape)
        value = times(activated_ref[...], grad_ref[...].reshape(count, D))
        down_grad[...] = value.astype(jnp.bfloat16).reshape(down_grad.shape)

    grads = ((units // (2 * half_rows), 2, half_rows, D), jnp.bfloat16)
    return Work(
        before,
        during,
        [grad, normed, table, table, hidden, activated],
        [VMEM_SPEC, VMEM_SPEC, part_spec(units, 1), part_spec(units, 2), VMEM_SPEC, VMEM_SPEC],
        [grads, grads],
        [pltpu.VMEM((units, count), jnp.bfloat16)],
    )


LINE_BLOCKS = 2
LINE_LAG = 2


class Line:
    def __init__(self, rider, share):
        self.groups = lax.axis_size("dp")
        self.half = rider.shape
        self.chunks = rider.shape[0] // LINE_BLOCKS
        self.share = share
        count, half_rows, _ = rider.shape
        dma = pltpu.SemaphoreType.DMA
        out = (count, 2, half_rows, D) if share else rider.shape
        self.out_shape = jax.ShapeDtypeStruct(out, jnp.bfloat16)
        self.out_spec = pl.BlockSpec(memory_space=pl.ANY if share else pltpu.VMEM)
        self.scratch = [
            pltpu.VMEM(self.half, jnp.bfloat16),
            pltpu.VMEM((2,) + self.half, jnp.bfloat16),
            pltpu.VMEM((2,) + self.half, jnp.bfloat16),
            dma,
            dma((2, self.chunks)),
            dma((2, self.chunks)),
        ]
        if share:
            self.scratch += [pltpu.VMEM(self.half, jnp.bfloat16)] + [dma((self.chunks,))] * 3

    def bind(self, rider_ref, out_ref, refs):
        self.rider, self.out = rider_ref, out_ref
        self.own, self.came, self.going, self.own_sem, self.send_sems, self.recv_sems = refs[:6]
        self.total = out_ref
        if self.share:
            self.total, self.keep_sems, self.twin_send, self.twin_recv = refs[6:]
        self.done = 0
        self.group = lax.axis_index("dp")
        self.first = jnp.where(self.group < self.groups // 2, 0, 1)

    def at(self, chunk):
        return pl.ds(chunk * LINE_BLOCKS, LINE_BLOCKS)

    def comes(self, way):
        return jnp.where(way == 0, self.group > 0, self.group < self.groups - 1)

    def goes(self, way):
        return jnp.where(way == 0, self.group < self.groups - 1, self.group > 0)

    def copy(self, source, way, chunk):
        target = jnp.where(way == 0, self.group + 1, self.group - 1)
        return pltpu.make_async_remote_copy(
            src_ref=source,
            dst_ref=self.came.at[way, self.at(chunk)],
            send_sem=self.send_sems.at[way, chunk],
            recv_sem=self.recv_sems.at[way, chunk],
            device_id={"dp": target},
            device_id_type=MESH,
        )

    def begin(self):
        copy = pltpu.make_async_copy(self.rider, self.own, self.own_sem)
        copy.start()
        copy.wait()
        for way in range(2):

            @pl.when(jnp.logical_not(self.comes(way)))
            def _():
                self.came[way] = jnp.zeros(self.half, jnp.bfloat16)
                self.going[way] = self.own[...]

                def start(chunk, carry):
                    self.copy(self.going.at[way, self.at(chunk)], way, chunk).start()
                    return carry

                lax.fori_loop(0, self.chunks, start, 0)

    def twin_copy(self, chunk):
        side = lax.axis_index("seq")
        return pltpu.make_async_remote_copy(
            src_ref=self.total.at[self.at(chunk)],
            dst_ref=self.out.at[self.at(chunk), side],
            send_sem=self.twin_send.at[chunk],
            recv_sem=self.twin_recv.at[chunk],
            device_id={"seq": 1 - side},
            device_id_type=MESH,
        )

    def keep_copy(self, chunk):
        return pltpu.make_async_copy(
            self.total.at[self.at(chunk)],
            self.out.at[self.at(chunk), lax.axis_index("seq")],
            self.keep_sems.at[chunk],
        )

    def pass_on(self, way, chunk):
        rows = self.at(chunk)

        @pl.when(self.comes(way))
        def _():
            copy = self.copy(self.going.at[way, rows], way, chunk)
            copy.wait_recv()

            @pl.when(self.goes(way))
            def _():
                value = self.own[rows].astype(jnp.float32) + self.came[way, rows].astype(jnp.float32)
                self.going[way, rows] = value.astype(jnp.bfloat16)
                copy.start()

    def step(self, index):
        @pl.when(index < self.chunks)
        def _():
            self.pass_on(self.first, index)

        @pl.when(index >= LINE_LAG)
        def _():
            chunk = index - LINE_LAG
            rows = self.at(chunk)
            self.pass_on(1 - self.first, chunk)
            value = self.own[rows].astype(jnp.float32)
            value = value + self.came[0, rows].astype(jnp.float32)
            value = value + self.came[1, rows].astype(jnp.float32)
            self.total[rows] = value.astype(jnp.bfloat16)
            if self.share:
                self.keep_copy(chunk).start()
                self.twin_copy(chunk).start()

    def steps(self, count=None):
        stop = self.chunks + LINE_LAG if count is None else self.done + count

        def one(index, carry):
            self.step(index)
            return carry

        lax.fori_loop(self.done, stop, one, 0)
        self.done = stop

    def end(self):
        def one(chunk, carry):
            for way in range(2):

                @pl.when(self.goes(way))
                def _():
                    self.copy(self.going.at[way, self.at(chunk)], way, chunk).wait_send()

            if self.share:
                self.keep_copy(chunk).wait()
                self.twin_copy(chunk).wait()
            return carry

        lax.fori_loop(0, self.chunks, one, 0)


def reduce_all(terms, collective_id, rider=None):
    _, tensors, groups, count, _ = terms.shape
    line = None if rider is None else Line(rider, True)

    def kernel(*refs):
        refs = list(refs)
        terms_ref = refs.pop(0)
        rider_ref = refs.pop(0) if line else None
        out_ref = refs.pop(0)
        joined_ref = refs.pop(0) if line else None
        (
            near, own, mid, mid_in, far, far_in,
            own_sems, near_send, near_recv, mid_send, mid_recv, far_send, far_recv,
        ) = refs[:13]
        if line:
            line.bind(rider_ref, joined_ref, refs[13:])
        group, part, side = lax.axis_index("dp"), lax.axis_index("tensor"), lax.axis_index("seq")
        twin = 1 - side
        parts = others("tensor")
        order = others("dp") + [group]
        meet(
            [{"seq": twin}]
            + [{"tensor": peer} for peer in parts]
            + [{"dp": peer} for peer in order[:-1]]
        )
        waits, near_copies, own_copies = [], [], []
        for place, target in enumerate(order):
            near_copies.append(
                send(
                    terms_ref.at[twin, :, target],
                    near.at[place],
                    near_send.at[place],
                    near_recv.at[place],
                    {"seq": twin},
                )
            )
            copy = pltpu.make_async_copy(
                terms_ref.at[side, :, target], own.at[place], own_sems.at[place]
            )
            copy.start()
            own_copies.append(copy)
        if line:
            line.begin()
        mid_copies = []
        for place in range(groups):
            near_copies[place].wait_recv()
            own_copies[place].wait()
            if line and place < 4:
                line.steps(1)
            for slot in range(tensors):
                mid[place, slot] = (
                    own[place, slot].astype(jnp.float32) + near[place, slot].astype(jnp.float32)
                ).astype(jnp.bfloat16)
            mid_copies.append(
                [
                    send(
                        mid.at[place, peer],
                        mid_in.at[place, step],
                        mid_send.at[place, step],
                        mid_recv.at[place, step],
                        {"tensor": peer},
                    )
                    for step, peer in enumerate(parts)
                ]
            )
        far_copies = []
        for place, target in enumerate(order):
            if line and place < 4:
                line.steps(2)
            total = mid[place, part].astype(jnp.float32)
            for step in range(tensors - 1):
                mid_copies[place][step].wait_recv()
                total = total + mid_in[place, step].astype(jnp.float32)
            if place < groups - 1:
                far[place] = total.astype(jnp.bfloat16)
                far_copies.append(
                    send(
                        far.at[place],
                        far_in.at[place],
                        far_send.at[place],
                        far_recv.at[place],
                        {"dp": target},
                    )
                )
        if line:
            line.steps()
        for place, copy in enumerate(far_copies):
            copy.wait_recv()
            total = total + far_in[place].astype(jnp.float32)
        out_ref[...] = total
        for copy in near_copies + far_copies + [c for row in mid_copies for c in row]:
            copy.wait_send()
        if line:
            line.end()

    block = (count, D)
    dma = pltpu.SemaphoreType.DMA
    return pl.pallas_call(
        kernel,
        name="reduce_all",
        out_shape=[jax.ShapeDtypeStruct(block, jnp.float32)] + ([line.out_shape] if line else []),
        in_specs=[pl.BlockSpec(memory_space=pl.ANY)] * (2 if line else 1),
        out_specs=[pl.BlockSpec(memory_space=pltpu.VMEM)] + ([line.out_spec] if line else []),
        scratch_shapes=[pltpu.VMEM((groups, tensors) + block, jnp.bfloat16)] * 3
        + [
            pltpu.VMEM((groups, tensors - 1) + block, jnp.bfloat16),
            pltpu.VMEM((groups,) + block, jnp.bfloat16),
            pltpu.VMEM((groups,) + block, jnp.bfloat16),
            dma((groups,)),
            dma((groups,)),
            dma((groups,)),
            dma((groups, tensors - 1)),
            dma((groups, tensors - 1)),
            dma((groups,)),
            dma((groups,)),
        ]
        + (line.scratch if line else []),
        cost_estimate=SHORT,
        compiler_params=pltpu.CompilerParams(
            collective_id=collective_id, has_side_effects=True, vmem_limit_bytes=56 << 20
        ),
    )(terms, *([rider] if line else []))


def gather_all(block, collective_id, rider=None):
    tensors, groups = lax.axis_size("tensor"), lax.axis_size("dp")
    line = None if rider is None else Line(rider, False)

    def kernel(*refs):
        refs = list(refs)
        block_ref = refs.pop(0)
        rider_ref = refs.pop(0) if line else None
        out = refs.pop(0)
        summed_ref = refs.pop(0) if line else None
        own_sem, far_send, far_recv, mid_send, mid_recv, near_send, near_recv = refs[:7]
        if line:
            line.bind(rider_ref, summed_ref, refs[7:])
        group, part, side = lax.axis_index("dp"), lax.axis_index("tensor"), lax.axis_index("seq")
        twin = 1 - side
        parts = others("tensor")
        meet(
            [{"seq": twin}]
            + [{"tensor": peer} for peer in parts]
            + [{"dp": peer} for peer in others("dp")]
        )
        far_copies = [
            send(
                block_ref,
                out.at[side, part, group],
                far_send.at[step],
                far_recv.at[step],
                {"dp": peer},
            )
            for step, peer in enumerate(others("dp"))
        ]
        own = pltpu.make_async_copy(block_ref, out.at[side, part, group], own_sem)
        own.start()
        own.wait()
        if line:
            line.begin()
        mid_copies, near_copies = [], []
        for place in range(groups):
            if line and 0 < place < 4:
                line.steps(1)
            source = behind("dp", place)
            if place:
                far_copies[place - 1].wait_recv()
            held = out.at[side, part, source]
            mid_copies.append(
                [
                    send(held, held, mid_send.at[place, step], mid_recv.at[place, step], {"tensor": peer})
                    for step, peer in enumerate(parts)
                ]
            )
            near_copies.append(
                send(held, held, near_send.at[place, 0], near_recv.at[place, 0], {"seq": twin})
            )
        for place in range(groups):
            if line and place < 4:
                line.steps(2)
            source = behind("dp", place)
            for step in range(tensors - 1):
                mid_copies[place][step].wait_recv()
                held = out.at[side, behind("tensor", step + 1), source]
                near_copies.append(
                    send(
                        held,
                        held,
                        near_send.at[place, step + 1],
                        near_recv.at[place, step + 1],
                        {"seq": twin},
                    )
                )
        if line:
            line.steps()
        for copy in near_copies:
            copy.wait_recv()
        for copy in near_copies + far_copies + [c for row in mid_copies for c in row]:
            copy.wait_send()
        if line:
            line.end()

    dma = pltpu.SemaphoreType.DMA
    anywhere = pl.BlockSpec(memory_space=pl.ANY)
    return pl.pallas_call(
        kernel,
        name="gather_all",
        out_shape=[jax.ShapeDtypeStruct((2, tensors, groups) + block.shape, block.dtype)]
        + ([line.out_shape] if line else []),
        in_specs=[anywhere] * (2 if line else 1),
        out_specs=[anywhere] + ([line.out_spec] if line else []),
        scratch_shapes=[
            dma,
            dma((groups - 1,)),
            dma((groups - 1,)),
            dma((groups, tensors - 1)),
            dma((groups, tensors - 1)),
            dma((groups, tensors)),
            dma((groups, tensors)),
        ]
        + (line.scratch if line else []),
        cost_estimate=SHORT,
        compiler_params=pltpu.CompilerParams(
            collective_id=collective_id, has_side_effects=True, vmem_limit_bytes=40 << 20
        ),
    )(block, *([rider] if line else []))


def reduce_rows(terms, ids, rider=None):
    count, groups = terms.shape[3], terms.shape[2]
    pieces = max(1, groups // 4)
    part = count // pieces
    sums, joined = [], None
    for i in range(pieces):
        piece = terms[:, :, :, i * part : (i + 1) * part] if pieces > 1 else terms
        if i == 0 and rider is not None:
            total, joined = reduce_all(piece, ids[1], rider)
        else:
            (total,) = reduce_all(piece, ids[0])
        sums.append(total)
    return jnp.concatenate(sums, axis=0) if pieces > 1 else sums[0], joined


def join_stats(stats, collective_id):
    _, tensors, groups, _, _ = stats.shape

    def join(left, right):
        top = jnp.maximum(left[..., 0:1, :], right[..., 0:1, :])
        total = left[..., 1:2, :] * jnp.exp(left[..., 0:1, :] - top) + right[..., 1:2, :] * jnp.exp(
            right[..., 0:1, :] - top
        )
        return jnp.concatenate(
            [top, total, left[..., 2:3, :] + right[..., 2:3, :], left[..., 3:, :]], axis=-2
        )

    def kernel(
        stats_ref, home, full, near, mid, mid_in, far, far_in,
        near_send, near_recv, mid_send, mid_recv, far_send, far_recv,
    ):
        group, part, side = lax.axis_index("dp"), lax.axis_index("tensor"), lax.axis_index("seq")
        twin = 1 - side
        parts, groups_else = others("tensor"), others("dp")
        meet(
            [{"seq": twin}]
            + [{"tensor": peer} for peer in parts]
            + [{"dp": peer} for peer in groups_else]
        )
        copy = send(stats_ref.at[twin], near, near_send.at[0], near_recv.at[0], {"seq": twin})
        copy.wait()
        for slot in range(tensors):
            for spot in range(groups):
                mid[slot, spot] = join(stats_ref[side, slot, spot], near[slot, spot])
        copies = [
            send(mid.at[peer], mid_in.at[step], mid_send.at[0, step], mid_recv.at[0, step], {"tensor": peer})
            for step, peer in enumerate(parts)
        ]
        for copy in copies:
            copy.wait()
        for spot in range(groups):
            total = mid[part, spot]
            for step in range(tensors - 1):
                total = join(total, mid_in[step, spot])
            far[spot] = total
        copies = [
            send(far.at[peer], far_in.at[step], far_send.at[0, step], far_recv.at[0, step], {"dp": peer})
            for step, peer in enumerate(groups_else)
        ]
        total = far[group]
        for step, copy in enumerate(copies):
            copy.wait()
            total = join(total, far_in[step])
        log_total = total[0:1] + jnp.log(total[1:2])
        home[...] = jnp.concatenate([log_total, total[2:3], total[2:]], axis=0)
        full[side, part, group] = jnp.broadcast_to(log_total, (8, LANES))
        held = full.at[side, part, group]
        copies = [
            send(held, held, far_send.at[1, step], far_recv.at[1, step], {"dp": peer})
            for step, peer in enumerate(groups_else)
        ]
        for copy in copies:
            copy.wait()
        held = full.at[side, part]
        copies = [
            send(held, held, mid_send.at[1, step], mid_recv.at[1, step], {"tensor": peer})
            for step, peer in enumerate(parts)
        ]
        for copy in copies:
            copy.wait()
        held = full.at[side]
        send(held, held, near_send.at[1], near_recv.at[1], {"seq": twin}).wait()

    tile = (8, LANES)
    dma = pltpu.SemaphoreType.DMA
    vmem = pl.BlockSpec(memory_space=pltpu.VMEM)
    return pl.pallas_call(
        kernel,
        name="join_stats",
        out_shape=[
            jax.ShapeDtypeStruct(tile, jnp.float32),
            jax.ShapeDtypeStruct(stats.shape, jnp.float32),
        ],
        in_specs=[vmem],
        out_specs=[vmem, vmem],
        scratch_shapes=[
            pltpu.VMEM((tensors, groups) + tile, jnp.float32),
            pltpu.VMEM((tensors, groups) + tile, jnp.float32),
            pltpu.VMEM((tensors - 1, groups) + tile, jnp.float32),
            pltpu.VMEM((groups,) + tile, jnp.float32),
            pltpu.VMEM((groups - 1,) + tile, jnp.float32),
            dma((2,)),
            dma((2,)),
            dma((2, tensors - 1)),
            dma((2, tensors - 1)),
            dma((2, groups - 1)),
            dma((2, groups - 1)),
        ],
        cost_estimate=SHORT,
        compiler_params=pltpu.CompilerParams(collective_id=collective_id, has_side_effects=True),
    )(stats)


def spread_tokens(block, collective_id):
    tensors, groups = lax.axis_size("tensor"), lax.axis_size("dp")
    rows = 2 * tensors * groups

    def kernel(block_ref, ids, targets, kept, count, held, own_sem, send_sems, recv_sems):
        group, side = lax.axis_index("dp"), lax.axis_index("seq")
        peers = [
            {"dp": lax.rem(group + step // 2, groups), "seq": lax.rem(side + step % 2, 2)}
            for step in range(1, 2 * groups)
        ]
        meet(peers)
        copies = [
            send(block_ref, held.at[group, side], send_sems.at[step], recv_sems.at[step], peer)
            for step, peer in enumerate(peers)
        ]
        own = pltpu.make_async_copy(block_ref, held.at[group, side], own_sem)
        own.start()
        own.wait()
        for copy in copies:
            copy.wait()
        lane = lax.broadcasted_iota(jnp.int32, (1, LANES), 1)
        total = jnp.zeros((1, LANES), jnp.int32)
        for half in range(2):
            for source in range(groups):
                limit = held[source, half, 2 * tensors : 2 * tensors + 1, :]
                total = total + limit
                for part in range(tensors):
                    row = (half * tensors + part) * groups + source
                    tile, place = row // TILE_GROUPS, slice(row % TILE_GROUPS, row % TILE_GROUPS + 1)
                    ids[tile, place, :] = held[source, half, part : part + 1, :]
                    targets[tile, place, :] = held[source, half, tensors + part : tensors + part + 1, :]
                    kept[tile, place, :] = jnp.where(lane + part * LANES < limit, 1.0, 0.0)
        count[...] = total.astype(jnp.float32)

    dma = pltpu.SemaphoreType.DMA
    vmem = pl.BlockSpec(memory_space=pltpu.VMEM)
    shape = (rows // TILE_GROUPS, TILE_GROUPS, LANES)
    return pl.pallas_call(
        kernel,
        name="spread_tokens",
        out_shape=[
            jax.ShapeDtypeStruct(shape, jnp.int32),
            jax.ShapeDtypeStruct(shape, jnp.int32),
            jax.ShapeDtypeStruct(shape, jnp.float32),
            jax.ShapeDtypeStruct((1, LANES), jnp.float32),
        ],
        in_specs=[vmem],
        out_specs=[vmem] * 4,
        scratch_shapes=[
            pltpu.VMEM((groups, 2) + block.shape, jnp.int32),
            dma,
            dma((2 * groups - 1,)),
            dma((2 * groups - 1,)),
        ],
        cost_estimate=SHORT,
        compiler_params=pltpu.CompilerParams(collective_id=collective_id, has_side_effects=True),
    )(block)


def finish(gain_grads, states, grad_ys, home, keep, table_squares, layer_squares, count, smalls, collective_id):
    tensors, groups = lax.axis_size("tensor"), lax.axis_size("dp")
    block = (8, D)
    gain_rows = 2 * LAYERS + 1
    operands = list(gain_grads) + list(states) + list(grad_ys) + [
        home, keep, table_squares, layer_squares, count
    ] + list(smalls)

    def kernel(*refs):
        refs = list(refs)
        gain_refs = [refs.pop(0) for _ in gain_grads]
        state_refs = [refs.pop(0) for _ in states]
        grad_refs = [refs.pop(0) for _ in grad_ys]
        home_ref, keep_ref, table_ref, layer_ref, count_ref = [refs.pop(0) for _ in range(5)]
        small_refs = [refs.pop(0) for _ in smalls]
        out_refs = [refs.pop(0) for _ in range(8)]
        near, mid, far, near_send, near_recv, mid_send, mid_recv, far_send, far_recv = refs
        group, part, side = lax.axis_index("dp"), lax.axis_index("tensor"), lax.axis_index("seq")
        parts, groups_else = others("tensor"), others("dp")
        meet(
            [{"seq": 1 - side}]
            + [{"tensor": peer} for peer in parts]
            + [{"dp": peer} for peer in groups_else]
        )
        values = []
        for later in range(1, LAYERS + 1):
            grad = grad_refs[later - 1][...]
            for level in range(later + 1):
                values.append(jnp.sum(grad * state_refs[level][...], keepdims=True))
        loss = (home_ref[0:1, :] - home_ref[1:2, :]) * keep_ref[...]
        values.append(jnp.sum(loss, keepdims=True))
        values.append(jnp.sum(table_ref[...], keepdims=True) + layer_ref[...])
        lane = lax.broadcasted_iota(jnp.int32, (1, D), 1)
        row = jnp.zeros((1, D), jnp.float32)
        for place, value in enumerate(values):
            row = jnp.where(lane == place, value, row)
        blank = jnp.zeros((8 - gain_rows - 1, D), jnp.float32)
        total = jnp.concatenate([ref[...] for ref in gain_refs] + [row, blank], axis=0)
        stages = [
            ("seq", near, side, [1 - side], near_send, near_recv),
            ("tensor", mid, part, parts, mid_send, mid_recv),
            ("dp", far, group, groups_else, far_send, far_recv),
        ]
        for axis, slots, me, peers, send_sems, recv_sems in stages:
            slots[me] = total
            copies = [
                send(slots.at[me], slots.at[me], send_sems.at[step], recv_sems.at[step], {axis: peer})
                for step, peer in enumerate(peers)
            ]
            for copy in copies:
                copy.wait()
            total = slots[0]
            for index in range(1, slots.shape[0]):
                total = total + slots[index]
        gain_total = total[:gain_rows]
        row = total[gain_rows : gain_rows + 1]

        def pick(place):
            return jnp.sum(jnp.where(lane == place, row, 0.0), axis=1, keepdims=True)

        mix_squares = jnp.sum(jnp.where(lane < MIX_WEIGHTS, row * row, 0.0), axis=1, keepdims=True)
        gain_squares = jnp.sum(gain_total * gain_total, keepdims=True)
        tokens = count_ref[:, 0:1]
        clip_norm = jnp.sqrt(pick(MIX_WEIGHTS + 1) + gain_squares + mix_squares) / tokens
        factor = jnp.minimum(1.0, CLIP_NORM / clip_norm) / tokens
        gain_news = adam_update(
            *[ref[...] for ref in small_refs[:3]], gain_total * factor, RATE_SMALL, 0.0
        )
        mix_news = adam_update(
            *[ref[...] for ref in small_refs[3:]], row[:, :MIX_WEIGHTS] * factor, RATE_SMALL, 0.0
        )
        for ref, value in zip(out_refs[:6], gain_news + mix_news):
            ref[...] = value
        ends = jnp.where(lane == 0, pick(MIX_WEIGHTS), jnp.where(lane == 1, clip_norm, factor))
        out_refs[6][...] = ends[:, :LANES]
        out_refs[7][...] = jnp.broadcast_to(factor, (8, LANES))

    dma = pltpu.SemaphoreType.DMA
    vmem = pl.BlockSpec(memory_space=pltpu.VMEM)
    return pl.pallas_call(
        kernel,
        name="finish",
        out_shape=[jax.ShapeDtypeStruct(value.shape, jnp.float32) for value in smalls]
        + [
            jax.ShapeDtypeStruct((1, LANES), jnp.float32),
            jax.ShapeDtypeStruct((8, LANES), jnp.float32),
        ],
        in_specs=[vmem] * len(operands),
        out_specs=[vmem] * 8,
        scratch_shapes=[
            pltpu.VMEM((2,) + block, jnp.float32),
            pltpu.VMEM((tensors,) + block, jnp.float32),
            pltpu.VMEM((groups,) + block, jnp.float32),
            dma((1,)),
            dma((1,)),
            dma((tensors - 1,)),
            dma((tensors - 1,)),
            dma((groups - 1,)),
            dma((groups - 1,)),
        ],
        cost_estimate=SHORT,
        compiler_params=pltpu.CompilerParams(collective_id=collective_id, has_side_effects=True),
    )(*operands)


SLOT_STEP = 4


def update_slots(plan, factor, master, first, second, layer_grads, grad_table):
    slots, half_rows, _ = master.shape
    steps = -(-slots // SLOT_STEP)
    plan = jnp.pad(plan, ((0, 0), (0, steps * SLOT_STEP - slots)))

    def kernel(plan_ref, factor_ref, master_ref, first_ref, second_ref, *rest):
        layer_refs = rest[: LAYERS * SLOT_STEP]
        table_ref, new_master, new_first, new_second = rest[LAYERS * SLOT_STEP :]
        for place in range(SLOT_STEP):
            kind = plan_ref[0, pl.program_id(0) * SLOT_STEP + place]
            grad = table_ref[place * half_rows : (place + 1) * half_rows, :]
            for level in range(LAYERS):
                layer = layer_refs[level * SLOT_STEP + place][0].astype(jnp.float32)
                grad = jnp.where(kind == level, layer, grad)
            grad = jnp.where(kind >= 0, grad * factor_ref[0:1, 0:1], 0.0)
            values = adam_update(
                master_ref[place],
                first_ref[place],
                second_ref[place],
                grad,
                RATE_MATRIX,
                DECAY_MATRIX,
            )
            for ref, value in zip((new_master, new_first, new_second), values):
                ref[place] = value

    slot = pl.BlockSpec((SLOT_STEP, half_rows, D), lambda step, plan: (step, 0, 0))
    return pl.pallas_call(
        kernel,
        name="update_slots",
        grid_spec=pltpu.PrefetchScalarGridSpec(
            num_scalar_prefetch=1,
            grid=(steps,),
            in_specs=[pl.BlockSpec((8, LANES), lambda step, plan: (0, 0)), slot, slot, slot]
            + [
                pl.BlockSpec(
                    (1, half_rows, D),
                    lambda step, plan, level=level, place=place: (
                        plan[1 + level, step * SLOT_STEP + place],
                        0,
                        0,
                    ),
                )
                for level in range(LAYERS)
                for place in range(SLOT_STEP)
            ]
            + [pl.BlockSpec((SLOT_STEP * half_rows, D), lambda step, plan: (step, 0))],
            out_specs=[slot] * 3,
        ),
        out_shape=[jax.ShapeDtypeStruct(master.shape, jnp.float32)] * 3,
        cost_estimate=SHORT,
        compiler_params=pltpu.CompilerParams(vmem_limit_bytes=48 << 20),
    )(
        plan,
        factor,
        master,
        first,
        second,
        *[grads for grads in layer_grads for _ in range(SLOT_STEP)],
        grad_table,
    )


def row_of(groups_ref):
    return jnp.concatenate([groups_ref[0, g : g + 1, :] for g in range(TILE_GROUPS)], axis=1)


def stat_row(stat_ref, row):
    return jnp.concatenate([stat_ref[g, row : row + 1, :] for g in range(TILE_GROUPS)], axis=1)


def chunk_of(span_ref, step):
    return pl.ds(pl.multiple_of(span_ref[0] + step * ROW_STEP, 16), ROW_STEP)


def chunks_of(span_ref):
    return (span_ref[1] - span_ref[0] + ROW_STEP - 1) // ROW_STEP


def whole(shape):
    return pl.BlockSpec(shape, lambda step, span: (0,) * len(shape), pipeline_mode=pl.Buffered(1))


TILE = TILE_GROUPS * LANES
TOKENS_SPEC = pl.BlockSpec((1, TILE_GROUPS, LANES), lambda step, span: (step, 0, 0))
STATS_SPEC = pl.BlockSpec((TILE_GROUPS, 8, LANES), lambda step, span: (step, 0, 0))
ROWS_SPEC = pl.BlockSpec((TILE, D), lambda step, span: (step, 0))


def local_call(name, kernel, steps, span, operands, in_specs, out_shape, out_specs, scratch):
    return pl.pallas_call(
        kernel,
        name=name,
        grid_spec=pltpu.PrefetchScalarGridSpec(
            num_scalar_prefetch=1,
            grid=(steps,),
            in_specs=in_specs,
            out_specs=out_specs,
            scratch_shapes=scratch,
        ),
        out_shape=out_shape,
        cost_estimate=SHORT,
        compiler_params=pltpu.CompilerParams(vmem_limit_bytes=60 << 20),
    )(span, *operands)


def look_up(span, row_ids, tokens, table):
    rows = table.shape[0]
    steps = tokens.shape[0]

    def kernel(span_ref, ids_ref, tokens_ref, table_ref, out_ref, acc):
        acc[...] = jnp.zeros_like(acc)
        wanted = row_of(tokens_ref)

        def one(step, carry):
            chunk = chunk_of(span_ref, step)
            hits = jnp.where(ids_ref[chunk, :] == wanted, 1.0, 0.0).astype(jnp.bfloat16)
            acc[...] += contract_first(hits, table_ref[chunk, :])
            return carry

        lax.fori_loop(0, chunks_of(span_ref), one, 0)
        out_ref[...] = acc[...].astype(jnp.bfloat16)

    return local_call(
        "look_up",
        kernel,
        steps,
        span,
        (row_ids, tokens, table),
        [whole((rows, 1)), TOKENS_SPEC, whole((rows, D))],
        jax.ShapeDtypeStruct((steps * TILE, D), jnp.bfloat16),
        ROWS_SPEC,
        [pltpu.VMEM((TILE, D), jnp.float32)],
    )


def head_forward(span, row_ids, labels, table, final):
    rows = table.shape[0]
    steps = labels.shape[0]

    def kernel(span_ref, ids_ref, labels_ref, table_ref, final_ref, powers_ref, stats_ref, scores):
        wanted = row_of(labels_ref)
        hidden = final_ref[...]

        def first(step, carry):
            top, target = carry
            chunk = chunk_of(span_ref, step)
            ids = ids_ref[chunk, :]
            raw = contract_last(table_ref[chunk, :], hidden)
            raw = jnp.where(ids >= 0, raw, -1e30)
            scores[chunk, :] = raw
            top = jnp.maximum(top, jnp.max(raw, axis=0, keepdims=True))
            target = target + jnp.sum(jnp.where(ids == wanted, raw, 0.0), axis=0, keepdims=True)
            return (top, target)

        blank = jnp.zeros((1, TILE), jnp.float32)
        top, target = lax.fori_loop(0, chunks_of(span_ref), first, (blank - 1e30, blank))

        def second(step, total):
            chunk = chunk_of(span_ref, step)
            powers = jnp.exp(scores[chunk, :] - top)
            powers_ref[chunk, :] = powers.astype(jnp.bfloat16)
            return total + jnp.sum(powers, axis=0, keepdims=True)

        total = lax.fori_loop(0, chunks_of(span_ref), second, blank)
        rest = jnp.zeros((5, LANES), jnp.float32)
        for g in range(TILE_GROUPS):
            lanes = slice(g * LANES, (g + 1) * LANES)
            stats_ref[g] = jnp.concatenate(
                [top[:, lanes], total[:, lanes], target[:, lanes], rest], axis=0
            )

    return local_call(
        "head_forward",
        kernel,
        steps,
        span,
        (row_ids, labels, table, final),
        [whole((rows, 1)), TOKENS_SPEC, whole((rows, D)), ROWS_SPEC],
        [
            jax.ShapeDtypeStruct((rows, steps * TILE), jnp.bfloat16),
            jax.ShapeDtypeStruct((steps * TILE_GROUPS, 8, LANES), jnp.float32),
        ],
        [pl.BlockSpec((rows, TILE), lambda step, span: (0, step)), STATS_SPEC],
        [pltpu.VMEM((rows, TILE), jnp.float32)],
    )


def head_backward(span, row_ids, labels, keep, stats, log_totals, table, final, powers):
    rows = table.shape[0]
    steps = labels.shape[0]

    def kernel(
        span_ref, ids_ref, labels_ref, keep_ref, stats_ref, logs_ref, table_ref, final_ref,
        powers_ref, grad_final_ref, grad_table_ref, acc,
    ):
        @pl.when(pl.program_id(0) == 0)
        def _():
            grad_table_ref[...] = jnp.zeros_like(grad_table_ref)

        acc[...] = jnp.zeros_like(acc)
        wanted, kept = row_of(labels_ref), row_of(keep_ref)
        scale = jnp.exp(stat_row(stats_ref, 0) - stat_row(logs_ref, 0)) * kept
        hidden = final_ref[...]

        def one(step, carry):
            chunk = chunk_of(span_ref, step)
            grads = powers_ref[chunk, :].astype(jnp.float32) * scale
            grads = grads - jnp.where(ids_ref[chunk, :] == wanted, kept, 0.0)
            grads = grads.astype(jnp.bfloat16)
            grad_table_ref[chunk, :] += jnp.dot(grads, hidden, preferred_element_type=jnp.float32)
            acc[...] += contract_first(grads, table_ref[chunk, :])
            return carry

        lax.fori_loop(0, chunks_of(span_ref), one, 0)
        grad_final_ref[...] = acc[...].astype(jnp.bfloat16)

    return local_call(
        "head_backward",
        kernel,
        steps,
        span,
        (row_ids, labels, keep, stats, log_totals, table, final, powers),
        [
            whole((rows, 1)),
            TOKENS_SPEC,
            TOKENS_SPEC,
            STATS_SPEC,
            STATS_SPEC,
            whole((rows, D)),
            ROWS_SPEC,
            pl.BlockSpec((rows, TILE), lambda step, span: (0, step)),
        ],
        [
            jax.ShapeDtypeStruct((steps * TILE, D), jnp.bfloat16),
            jax.ShapeDtypeStruct((rows, D), jnp.float32),
        ],
        [ROWS_SPEC, whole((rows, D))],
        [pltpu.VMEM((TILE, D), jnp.float32)],
    )


def look_back(span, row_ids, tokens, grad_start, grad_table):
    rows = grad_table.shape[0]
    steps = tokens.shape[0]

    def kernel(span_ref, ids_ref, tokens_ref, grad_ref, table_ref, out_ref, squares_ref):
        @pl.when(pl.program_id(0) == 0)
        def _():
            out_ref[...] = table_ref[...]

        wanted = row_of(tokens_ref)
        grads = grad_ref[...]

        def one(step, carry):
            chunk = chunk_of(span_ref, step)
            hits = jnp.where(ids_ref[chunk, :] == wanted, 1.0, 0.0).astype(jnp.bfloat16)
            out_ref[chunk, :] += jnp.dot(hits, grads, preferred_element_type=jnp.float32)
            return carry

        lax.fori_loop(0, chunks_of(span_ref), one, 0)

        @pl.when(pl.program_id(0) == steps - 1)
        def _():
            def square(step, total):
                values = out_ref[chunk_of(span_ref, step), :]
                values = (values * values).reshape(ROW_STEP // 8, 8, D).sum(axis=0)
                return total + values

            squares_ref[...] = lax.fori_loop(
                0, chunks_of(span_ref), square, jnp.zeros((8, D), jnp.float32)
            )

    return local_call(
        "look_back",
        kernel,
        steps,
        span,
        (row_ids, tokens, grad_start, grad_table),
        [whole((rows, 1)), TOKENS_SPEC, ROWS_SPEC, whole((rows, D))],
        [
            jax.ShapeDtypeStruct((rows, D), jnp.float32),
            jax.ShapeDtypeStruct((8, D), jnp.float32),
        ],
        [whole((rows, D)), whole((8, D))],
        [],
    )


def body(
    token_ids,
    labels,
    real_counts,
    owners,
    master,
    first_moment,
    second_moment,
    gains,
    gains_first,
    gains_second,
    mix,
    mix_first,
    mix_second,
):
    tensors = lax.axis_size("tensor")
    groups = lax.axis_size("dp")
    group = lax.axis_index("dp")
    tensor_part = lax.axis_index("tensor")
    seq_part = lax.axis_index("seq")
    slots, half_rows, _ = master.shape
    seq_count, half_len = token_ids.shape
    row_count = seq_count * half_len
    share = row_count // tensors
    head_rows = 3 * D // tensors
    out_rows = D // tensors
    unit_rows = FF // tensors
    layer_rows = head_rows + out_rows + 2 * unit_rows
    layer_blocks = layer_rows // (2 * half_rows)
    blocks = LAYERS * layer_blocks
    vocab_rows = VOCAB // tensors
    local_heads = HEADS // tensors

    slot_rank = slot_table(owners)
    block_ids = jnp.arange(owners.shape[0], dtype=jnp.int32)
    mine = owners == group
    match = (jnp.arange(slots)[:, None] == slot_rank[None, :]) & mine[None, :]
    slot_block = jnp.sum(jnp.where(match, block_ids[None, :] + 1, 0), axis=1) - 1
    row_ids = (
        tensor_part * vocab_rows
        + (slot_block[:, None] - blocks) * (2 * half_rows)
        + seq_part * half_rows
        + jnp.arange(half_rows, dtype=jnp.int32)[None, :]
    )
    row_ids = jnp.where(slot_block[:, None] >= blocks, row_ids, -1).reshape(-1, 1)
    spare = -(-ROW_STEP // half_rows)
    row_ids = jnp.pad(row_ids, ((0, spare * half_rows), (0, 0)), constant_values=-1)
    held = jnp.sum(jnp.where(mine, 1, 0)) * half_rows
    first_held = jnp.sum(jnp.where(mine & (block_ids < blocks), 1, 0)) * half_rows
    span = jnp.stack([first_held, held]).astype(jnp.int32)
    level_of = jnp.where(slot_block < 0, -1, jnp.minimum(slot_block // layer_blocks, LAYERS))
    plan = jnp.stack(
        [level_of]
        + [
            jnp.where(level_of == level, slot_block - level * layer_blocks, 0)
            for level in range(LAYERS)
        ]
    ).astype(jnp.int32)

    packed = jnp.concatenate(
        [
            token_ids.reshape(tensors, LANES),
            labels.reshape(tensors, LANES),
            jnp.broadcast_to(real_counts[:, None], (16 - 2 * tensors, LANES)),
        ],
        axis=0,
    )
    ids_all, labels_all, keep_all, count = spread_tokens(packed, 15)
    order = (2, tensors, groups, share)

    table_slots = jnp.pad(master.astype(jnp.bfloat16), ((0, spare), (0, 0), (0, 0)))
    table = table_slots.reshape(-1, D)

    halves = jnp.where(
        mine[:blocks][:, None, None], jnp.take(table_slots, slot_rank[:blocks], axis=0), 0.0
    ).astype(jnp.bfloat16)
    halves = [halves[i * layer_blocks : (i + 1) * layer_blocks] for i in range(LAYERS)]
    halves[1:] = [lax.psum(half, "dp") for half in halves[1:]]

    positions = seq_part * half_len + jnp.arange(row_count) % half_len
    steps_half = jnp.arange(HEAD_DIM // 2).astype(jnp.float32)
    freqs = 10000.0 ** (-2.0 * steps_half / HEAD_DIM)
    angles = freqs[:, None] * positions.astype(jnp.float32)[None, :]
    cosine, sine = jnp.cos(angles), jnp.sin(angles)

    looked = look_up(span, row_ids, ids_all, table).reshape(order + (D,))
    start, joined = reduce_rows(looked, (0, 14), halves[0])
    tables = [joined.reshape(layer_rows, D)]
    gain = [gains[i : i + 1] for i in range(2 * LAYERS + 1)]
    piece = ((share, D), jnp.float32)

    def normed_of(total, stream, gain_row):
        return (layer_norm_parts(stream)[0] * gain_row,)

    def inner_of(total, stream, gain_row):
        inner = stream + total
        return (inner, layer_norm_parts(inner)[0] * gain_row)

    def outcome_of(base, total, inner, gain_row, *rest):
        states, scalars = rest[:-1], rest[-1]
        outcome = inner + total
        stream = scalars[base + len(states)] * outcome
        for source, state in enumerate(states):
            stream = stream + scalars[base + source] * state
        return (outcome, stream, layer_norm_parts(stream)[0] * gain_row)

    (normed,) = tensor_step("normed", normed_of, None, (start, gain[0]), (), [], True, 1)
    states, streams, inners, kept_all = [start], [start], [], []
    for level in range(LAYERS):
        inner, normed_two, *kept = tensor_step(
            f"inner_{level}",
            inner_of,
            attention_work(normed, tables[level], cosine, sine),
            (streams[level], gain[2 * level + 1]),
            (),
            [piece],
            True,
            2 if level == 0 else 15 + level,
        )
        last = level == LAYERS - 1
        outcome, stream, normed_next, hidden, activated, *joined = tensor_step(
            f"outcome_{level}",
            partial(outcome_of, (level + 1) * (level + 2) // 2 - 1),
            unit_work(normed_two, tables[level]),
            [inner, gain[2 * level + 2]] + states,
            (mix,),
            [piece, piece] + ([((share, D), jnp.bfloat16)] if last else []),
            not last,
            3 + level,
            None if last else halves[level + 1],
        )
        tables += [table_next.reshape(layer_rows, D) for table_next in joined]
        inners.append(inner)
        kept_all.append((normed, kept, normed_two, (hidden, activated)))
        states.append(outcome)
        streams.append(stream)
        normed = normed_next

    final_all = gather_all(normed, 3 + LAYERS)[0].reshape(-1, D)
    powers, stats = head_forward(span, row_ids, labels_all, table, final_all)
    home, log_totals = join_stats(
        stats.reshape((2, tensors, groups, 8, LANES)), 4 + LAYERS
    )
    grad_final, grad_table = head_backward(
        span,
        row_ids,
        labels_all,
        keep_all,
        stats,
        log_totals.reshape(-1, 8, LANES),
        table,
        final_all,
        powers,
    )
    grad_final, _ = reduce_rows(grad_final.reshape(order + (D,)), (0, 14))

    row = ((1, D), jnp.float32)

    def top_of(total, grad, stream, gain_row, scalars):
        grad_top, grad_gain = norm_pull(grad, gain_row, stream)
        grad_state = scalars[MIX_WEIGHTS - 1] * grad_top
        return (grad_top, grad_state, grad_gain, grad_state)

    def inner_back(total, grad_out, inner, gain_row):
        grad, grad_gain = norm_pull(total, gain_row, inner)
        grad = grad_out + grad
        return (grad, grad_gain, grad)

    def stream_back(block, total, grad_inner, stream, gain_row, *rest):
        grad_ys, scalars = rest[:-1], rest[-1]
        grad, grad_gain = norm_pull(total, gain_row, stream)
        grad = grad_inner + grad
        state = grad if block == 0 else scalars[block * (block + 1) // 2 - 1 + block] * grad
        for offset, grad_y in enumerate(grad_ys):
            later = block + 1 + offset
            state = state + scalars[later * (later + 1) // 2 - 1 + block] * grad_y
        return (grad, state, grad_gain, state)

    grad_ys = [None] * (LAYERS + 1)
    gain_grads = [None] * (2 * LAYERS + 1)
    layer_grads = [None] * LAYERS
    grad_ys[LAYERS], grad_state, gain_grads[2 * LAYERS], grad_branch = tensor_step(
        "top_back",
        top_of,
        None,
        (grad_final, streams[LAYERS], gain[2 * LAYERS]),
        (mix,),
        [piece, piece, row],
        True,
        5 + LAYERS,
    )
    for level in reversed(range(LAYERS)):
        normed, kept, normed_two, unit_kept = kept_all[level]
        grad_inner, gain_grads[2 * level + 1], grad_attn, *unit_grads = tensor_step(
            f"inner_back_{level}",
            inner_back,
            unit_back_work(grad_branch, normed_two, tables[level], unit_kept, half_rows),
            (grad_state, inners[level], gain[2 * level + 1]),
            (),
            [piece, row],
            True,
            6 + LAYERS if level == 0 else 19 + level,
        )
        grad_ys[level], grad_state, gain_grads[2 * level], grad_branch, folded = tensor_step(
            f"stream_back_{level}",
            partial(stream_back, level),
            attention_back_work(
                grad_attn, normed, tables[level], kept, cosine, sine, unit_grads
            ),
            [grad_inner, streams[level], gain[2 * level]] + grad_ys[level + 1 :],
            (mix,),
            [piece, piece, row] + ([] if level else [((share, D), jnp.bfloat16)]),
            level > 0,
            7 + LAYERS + level,
        )
        layer_grads[level] = lax.psum(folded, "dp") if level else folded

    grad_start_all, layer_grads[0] = gather_all(grad_branch, 13, layer_grads[0])
    grad_start_all = grad_start_all.reshape(-1, D)
    grad_table, table_squares = look_back(span, row_ids, ids_all, grad_start_all, grad_table)
    layer_squares = jnp.zeros((), jnp.float32)
    for level in range(LAYERS):
        chosen = slice(level * layer_blocks, (level + 1) * layer_blocks)
        values = layer_grads[level].astype(jnp.float32)
        layer_squares += jnp.sum(jnp.where(mine[chosen][:, None, None], values * values, 0.0))
    keep = jnp.where(
        tensor_part * share + jnp.arange(share) < real_counts[0], 1.0, 0.0
    ).astype(jnp.float32)
    news = finish(
        gain_grads,
        states,
        grad_ys[1:],
        home,
        keep[None],
        table_squares,
        layer_squares.reshape(1, 1),
        count,
        (gains, gains_first, gains_second, mix[None], mix_first[None], mix_second[None]),
        7 + 2 * LAYERS,
    )
    new_gains, new_gains_first, new_gains_second = news[:3]
    new_mix, new_mix_first, new_mix_second = [value[0] for value in news[3:6]]
    loss_sum, clip_norm = news[6][0, 0], news[6][0, 1]
    token_count = count[0, 0]
    new_master, new_first, new_second = update_slots(
        plan, news[7], master, first_moment, second_moment, layer_grads, grad_table
    )
    return (
        new_master,
        new_first,
        new_second,
        new_gains,
        new_gains_first,
        new_gains_second,
        new_mix,
        new_mix_first,
        new_mix_second,
        loss_sum,
        token_count,
        clip_norm,
    )


def solution(mesh):
    return jax.shard_map(
        body,
        mesh=mesh,
        in_specs=(
            P("dp", "seq"),
            P("dp", "seq"),
            P(("dp", "seq")),
            P(),
            P("dp", ("tensor", "seq"), None),
            P("dp", ("tensor", "seq"), None),
            P("dp", ("tensor", "seq"), None),
            P(),
            P(),
            P(),
            P(),
            P(),
            P(),
        ),
        out_specs=(
            P("dp", ("tensor", "seq"), None),
            P("dp", ("tensor", "seq"), None),
            P("dp", ("tensor", "seq"), None),
            P(),
            P(),
            P(),
            P(),
            P(),
            P(),
            P(),
            P(),
            P(),
        ),
        check_vma=False,
    )
```

```python
from functools import partial

import jax
import jax.numpy as jnp
from jax import lax
from jax.experimental import pallas as pl
from jax.experimental.pallas import tpu as pltpu
from jax.sharding import PartitionSpec as P

D = 768
HEADS = 12
HEAD_DIM = 64
FF = 3072
VOCAB = 50304
LAYERS = 2
STEP_COUNT = 10
MIX_WEIGHTS = 5


EPS_NORM = 1e-05
CLIP_NORM = 0.01
BETA_ONE = 0.9
BETA_TWO = 0.95
ADAM_EPS = 1e-08
RATE_MATRIX = 0.04
RATE_SMALL = 0.4
DECAY_MATRIX = 0.1


def contract_last(left, right):
    return lax.dot_general(
        left, right, (((1,), (1,)), ((), ())), preferred_element_type=jnp.float32
    )


def contract_first(left, right):
    return lax.dot_general(
        left, right, (((0,), (0,)), ((), ())), preferred_element_type=jnp.float32
    )


def slot_table(owners):
    ranks = jnp.arange(owners.shape[0])
    same = (owners[None, :] == owners[:, None]) & (ranks[None, :] < ranks[:, None])
    return jnp.sum(jnp.where(same, 1, 0), axis=1).astype(jnp.int32)


def adam_update(weight, first, second, grad, rate, decay):
    first = BETA_ONE * first + (1.0 - BETA_ONE) * grad
    second = BETA_TWO * second + (1.0 - BETA_TWO) * grad * grad
    first_hat = first / (1.0 - BETA_ONE**STEP_COUNT)
    second_hat = second / (1.0 - BETA_TWO**STEP_COUNT)
    weight = weight - rate * (first_hat / (jnp.sqrt(second_hat) + ADAM_EPS) + decay * weight)
    return (weight, first, second)


MESH = pl.DeviceIdType.MESH
ROW_STEP = 400
TILE_GROUPS = 8
LANES = 128
SHORT = pl.CostEstimate(flops=1000, bytes_accessed=1000, transcendentals=0)


def meet(peers):
    gate = pltpu.get_barrier_semaphore()
    for peer in peers:
        pl.semaphore_signal(gate, inc=1, device_id=peer, device_id_type=MESH)
    pl.semaphore_wait(gate, len(peers))


def others(axis):
    count, me = lax.axis_size(axis), lax.axis_index(axis)
    return [lax.rem(me + step, count) for step in range(1, count)]


def behind(axis, step):
    count, me = lax.axis_size(axis), lax.axis_index(axis)
    return lax.rem(me + count - step, count)


def send(source, target, send_sem, recv_sem, device):
    copy = pltpu.make_async_remote_copy(
        src_ref=source,
        dst_ref=target,
        send_sem=send_sem,
        recv_sem=recv_sem,
        device_id=device,
        device_id_type=MESH,
    )
    copy.start()
    return copy


def layer_norm_parts(stream):
    center = stream - jnp.mean(stream, -1, keepdims=True)
    inverse = lax.rsqrt(jnp.mean(center * center, -1, keepdims=True) + EPS_NORM)
    return center * inverse, inverse


def norm_pull(grad_normed, gain, stream):
    scaled, inverse = layer_norm_parts(stream)
    grad_scaled = grad_normed * gain
    grad_stream = inverse * (
        grad_scaled
        - jnp.mean(grad_scaled, -1, keepdims=True)
        - scaled * jnp.mean(grad_scaled * scaled, -1, keepdims=True)
    )
    return grad_stream, jnp.sum(grad_normed * scaled, axis=0, keepdims=True)


class Work:
    def __init__(self, before, during, operands, specs, outs, scratch, after=None, twins=False):
        self.before, self.during, self.after, self.twins = before, during, after, twins
        self.operands, self.specs, self.outs, self.scratch = operands, specs, outs, scratch


def tensor_step(name, function, work, extras, scalars, outs, gather, collective_id, line=None):
    parts = lax.axis_size("tensor")
    share = extras[0].shape[0]
    reduce = work is not None
    work = work or Work(None, None, [], [], [], [])

    def kernel(*refs):
        refs = list(refs)

        def take(count):
            return [refs.pop(0) for _ in range(count)]

        work_refs = take(len(work.operands))
        extra_refs = take(len(extras))
        scalar_refs = take(len(scalars))
        source_refs = take(len(line.operands)) if line else []
        out_refs = take(len(outs))
        (full,) = take(1) if gather else [None]
        work_outs = take(len(work.outs))
        (joined,) = take(1) if line else [None]
        send_sems, recv_sems = take(2)
        partial_ref, outgoing, arrived = take(3) if reduce else [None] * 3
        if line:
            line.bind(source_refs, joined, take(len(line.scratch)))
            line.load()

        def tick(count=1):
            if line:
                line.steps(count)

        me, side = lax.axis_index("tensor"), lax.axis_index("seq")
        peers = others("tensor")
        twin = {"seq": 1 - side}
        twins = work.twins or (line and line.share)
        meet(
            [{"tensor": peer} for peer in peers]
            + [twin] * bool(twins)
            + ([{"dp": peer} for peer in others("dp")] if line else [])
        )
        if line:
            line.begin()
        total = None
        if reduce:
            work.before(work_refs, work_outs, refs, partial_ref, tick)
            copies = []
            for step, peer in enumerate(peers):
                rows = pl.ds(pl.multiple_of(peer * share, share), share)
                outgoing[step] = partial_ref[rows, :].astype(jnp.bfloat16)
                copies.append(
                    send(
                        outgoing.at[step],
                        arrived.at[step],
                        send_sems.at[0, step],
                        recv_sems.at[0, step],
                        {"tensor": peer},
                    )
                )
            if work.during:
                work.during(work_refs, work_outs, refs)
            tick(4)
            total = partial_ref[pl.ds(pl.multiple_of(me * share, share), share), :]
            for step, copy in enumerate(copies):
                copy.wait()
                total = total + arrived[step].astype(jnp.float32)
        results = function(total, *[ref[...] for ref in extra_refs], *scalar_refs)
        for ref, value in zip(out_refs, results):
            ref[...] = value.astype(ref.dtype)
        if gather:
            full[me] = results[len(outs)].astype(jnp.bfloat16)
            copies = [
                send(
                    full.at[me],
                    full.at[me],
                    send_sems.at[1, step],
                    recv_sems.at[1, step],
                    {"tensor": peer},
                )
                for step, peer in enumerate(peers)
            ]
        if work.after:
            work.after(work_refs, work_outs, refs)
        tick(None)
        if gather:
            for copy in copies:
                copy.wait()
        if line:
            line.end()

    vmem = pl.BlockSpec(memory_space=pltpu.VMEM)
    smem = pl.BlockSpec(memory_space=pltpu.SMEM)
    shapes = [jax.ShapeDtypeStruct(shape, dtype) for shape, dtype in outs]
    if gather:
        shapes.append(jax.ShapeDtypeStruct((parts, share, D), jnp.bfloat16))
    shapes += [jax.ShapeDtypeStruct(shape, dtype) for shape, dtype in work.outs]
    out_specs = [vmem] * len(shapes)
    operands = list(work.operands) + list(extras) + list(scalars)
    in_specs = list(work.specs) + [vmem] * len(extras) + [smem] * len(scalars)
    dma = pltpu.SemaphoreType.DMA
    buffers = [dma((2, parts - 1))] * 2
    if reduce:
        buffers += [pltpu.VMEM((parts * share, D), jnp.float32)]
        buffers += [pltpu.VMEM((parts - 1, share, D), jnp.bfloat16)] * 2
    if line:
        operands += line.operands
        in_specs += line.in_specs
        shapes.append(line.out_shape)
        out_specs.append(line.out_spec)
        buffers += line.scratch
    return pl.pallas_call(
        kernel,
        name=name,
        grid=(1,),
        out_shape=shapes,
        in_specs=in_specs,
        out_specs=out_specs,
        scratch_shapes=buffers + list(work.scratch),
        cost_estimate=SHORT,
        compiler_params=pltpu.CompilerParams(
            collective_id=collective_id, has_side_effects=True, vmem_limit_bytes=50 << 20
        ),
    )(*operands)


VMEM_SPEC = pl.BlockSpec(memory_space=pltpu.VMEM)


def part_spec(rows, index):
    return pl.BlockSpec((rows, D), lambda step: (index, 0), pipeline_mode=pl.Buffered(1))


def turn(block, cosine, sine):
    half = HEAD_DIM // 2
    first, second = block[:half], block[half:]
    return jnp.concatenate(
        [first * cosine - second * sine, second * cosine + first * sine], axis=0
    )


def times(left, right):
    return jnp.dot(left, right, preferred_element_type=jnp.float32)


def scores_of(keys_values, head, queries, side):
    span = slice(head * HEAD_DIM, (head + 1) * HEAD_DIM)
    count = queries.shape[1]
    scale = HEAD_DIM ** (-0.5)
    far = contract_first(keys_values[0, 0, span, :], queries) * scale
    own = contract_first(keys_values[1, 0, span, :], queries) * scale
    key = lax.broadcasted_iota(jnp.int32, (count, count), 0)
    query = lax.broadcasted_iota(jnp.int32, (count, count), 1)
    own = jnp.where(key <= query, own, -1e30)
    far = jnp.where(query + side * (2 * count) >= 2 * count, far, -1e30)
    return far, own


def attention_work(normed, table, cosine, sine):
    parts, share, _ = normed.shape
    count = parts * share
    width = D // parts
    heads = width // HEAD_DIM

    def before(ins, outs, scratch, partial_ref, tick):
        normed_ref, qkv_ref, out_ref, cosine_ref, sine_ref = ins
        queries_ref, both, logs_ref, attended_ref = outs
        send_sem, recv_sem = scratch
        side = lax.axis_index("seq")
        cosine, sine = cosine_ref[...], sine_ref[...]
        rows = normed_ref[...].reshape(count, D)
        joined = contract_last(qkv_ref[...], rows)
        for head in range(heads):
            span = slice(head * HEAD_DIM, (head + 1) * HEAD_DIM)
            keys = joined[width + head * HEAD_DIM : width + (head + 1) * HEAD_DIM]
            both[1, 0, span, :] = turn(keys, cosine, sine).astype(jnp.bfloat16)
        both[1, 1] = joined[2 * width :].astype(jnp.bfloat16)
        copy = pltpu.make_async_remote_copy(
            src_ref=both.at[1],
            dst_ref=both.at[0],
            send_sem=send_sem,
            recv_sem=recv_sem,
            device_id={"seq": 1 - side},
            device_id_type=MESH,
        )

        copy.start()
        for head in range(heads):
            span = slice(head * HEAD_DIM, (head + 1) * HEAD_DIM)
            queries_ref[span, :] = turn(joined[span], cosine, sine).astype(jnp.bfloat16)

        copy.wait()
        for head in range(heads):
            span = slice(head * HEAD_DIM, (head + 1) * HEAD_DIM)
            far, own = scores_of(both, head, queries_ref[span, :], side)
            peak = jnp.maximum(
                jnp.max(far, axis=0, keepdims=True), jnp.max(own, axis=0, keepdims=True)
            )
            far, own = jnp.exp(far - peak), jnp.exp(own - peak)
            total = jnp.sum(far, axis=0, keepdims=True) + jnp.sum(own, axis=0, keepdims=True)
            logs_ref[head] = peak + jnp.log(total)
            inverse = 1.0 / total
            attended = times(both[0, 1, span, :], (far * inverse).astype(jnp.bfloat16))
            attended += times(both[1, 1, span, :], (own * inverse).astype(jnp.bfloat16))
            attended_ref[span, :] = attended.astype(jnp.bfloat16)
            tick()
        partial_ref[...] = contract_first(attended_ref[...], out_ref[...])

    low = jnp.bfloat16
    return Work(
        before,
        None,
        [normed, table, table, cosine, sine],
        [VMEM_SPEC, part_spec(3 * width, 0), part_spec(width, 3), VMEM_SPEC, VMEM_SPEC],
        [
            ((width, count), low),
            ((2, 2, width, count), low),
            ((heads, 1, count), jnp.float32),
            ((width, count), low),
        ],
        [pltpu.SemaphoreType.DMA, pltpu.SemaphoreType.DMA],
        twins=True,
    )


def fold_copy(own, near, send_sems, recv_sems, index):
    side = lax.axis_index("seq")
    return pltpu.make_async_remote_copy(
        src_ref=own.at[index, :, 1 - side],
        dst_ref=near.at[index],
        send_sem=send_sems.at[index],
        recv_sem=recv_sems.at[index],
        device_id={"seq": 1 - side},
        device_id_type=MESH,
    )


def add_halves(own, near, out, start):
    side = lax.axis_index("seq")

    def one(block, carry):
        value = own[block, side].astype(jnp.float32) + near[block].astype(jnp.float32)
        out[start + block] = value.astype(jnp.bfloat16)
        return carry

    lax.fori_loop(0, near.shape[0], one, 0)


def attention_back_work(grad, normed, table, kept, cosine, sine, half_rows):
    parts, share, _ = normed.shape
    count = parts * share
    width = D // parts
    heads = width // HEAD_DIM
    queries, both, logs, attended = kept
    blocks = 4 * width // (2 * half_rows)

    def before(ins, outs, scratch, partial_ref, tick):
        grad_ref, _, qkv_ref, out_ref, queries_ref, both, logs_ref, _, cosine_ref, sine_ref = ins
        back, came, grad_joined, send_sem, recv_sem = scratch[:5]
        side = lax.axis_index("seq")
        cosine, sine = cosine_ref[...], -sine_ref[...]
        scale = HEAD_DIM ** (-0.5)
        grads = contract_last(out_ref[...], grad_ref[...].reshape(count, D)).astype(jnp.bfloat16)
        own_grads = []
        for head in range(heads):
            span = slice(head * HEAD_DIM, (head + 1) * HEAD_DIM)
            head_queries, head_grads = queries_ref[span, :], grads[span]
            far, own = scores_of(both, head, head_queries, side)
            far, own = jnp.exp(far - logs_ref[head]), jnp.exp(own - logs_ref[head])
            far_grad = contract_first(both[0, 1, span, :], head_grads)
            own_grad = contract_first(both[1, 1, span, :], head_grads)
            mean = jnp.sum(far * far_grad, axis=0, keepdims=True)
            mean += jnp.sum(own * own_grad, axis=0, keepdims=True)
            far_grad = (far * (far_grad - mean)).astype(jnp.bfloat16)
            own_grad = (own * (own_grad - mean)).astype(jnp.bfloat16)
            far, own = far.astype(jnp.bfloat16), own.astype(jnp.bfloat16)
            back[0, span, :] = (contract_last(head_queries, far_grad) * scale).astype(jnp.bfloat16)
            back[1, span, :] = contract_last(head_grads, far).astype(jnp.bfloat16)
            query_grad = times(both[0, 0, span, :], far_grad) + times(both[1, 0, span, :], own_grad)
            grad_joined[span, :] = turn(query_grad * scale, cosine, sine).astype(jnp.bfloat16)
            own_grads.append(
                (contract_last(head_queries, own_grad) * scale, contract_last(head_grads, own))
            )
            tick()
        copy = send(back, came, send_sem, recv_sem, {"seq": 1 - side})
        copy.wait()
        for head, (key_grad, value_grad) in enumerate(own_grads):
            span = slice(head * HEAD_DIM, (head + 1) * HEAD_DIM)
            key_grad = key_grad + came[0, span, :].astype(jnp.float32)
            value_grad = value_grad + came[1, span, :].astype(jnp.float32)
            start = width + head * HEAD_DIM
            grad_joined[start : start + HEAD_DIM, :] = turn(key_grad, cosine, sine).astype(
                jnp.bfloat16
            )
            start += width
            grad_joined[start : start + HEAD_DIM, :] = value_grad.astype(jnp.bfloat16)
        partial_ref[...] = contract_first(grad_joined[...], qkv_ref[...])

    def during(ins, outs, scratch):
        grad_ref, normed_ref, attended_ref = ins[0], ins[1], ins[7]
        grad_joined = scratch[2]
        own, near, fold_send, fold_recv = scratch[5:]
        value = times(grad_joined[...], normed_ref[...].reshape(count, D)).astype(jnp.bfloat16)
        part = 3 * blocks // 4
        own[0, :part] = value.reshape(part, 2, half_rows, D)
        value = times(attended_ref[...], grad_ref[...].reshape(count, D)).astype(jnp.bfloat16)
        own[0, part:] = value.reshape(blocks - part, 2, half_rows, D)
        fold_copy(own, near, fold_send, fold_recv, 0).start()

    def after(ins, outs, scratch):
        own, near, fold_send, fold_recv = scratch[5:]
        fold_copy(own, near, fold_send, fold_recv, 0).wait()
        add_halves(own.at[0], near.at[0], outs[0], 0)

    low = jnp.bfloat16
    dma = pltpu.SemaphoreType.DMA
    return Work(
        before,
        during,
        [grad, normed, table, table, queries, both, logs, attended, cosine, sine],
        [VMEM_SPEC, VMEM_SPEC, part_spec(3 * width, 0), part_spec(width, 3)] + [VMEM_SPEC] * 6,
        [((blocks, half_rows, D), low)],
        [
            pltpu.VMEM((2, width, count), low),
            pltpu.VMEM((2, width, count), low),
            pltpu.VMEM((3 * width, count), low),
            dma,
            dma,
            pltpu.VMEM((1, blocks, 2, half_rows, D), low),
            pltpu.VMEM((1, blocks, half_rows, D), low),
            dma((1,)),
            dma((1,)),
        ],
        after,
        True,
    )


def gelu(hidden):
    return jax.nn.gelu(hidden, approximate=True)


def unit_work(normed, up, down):
    parts, share, _ = normed.shape
    count = parts * share
    units = FF // parts

    def before(ins, outs, scratch, partial_ref, tick):
        normed_ref, up_ref, down_ref = ins
        hidden_ref, activated_ref = outs
        hidden = contract_last(up_ref[...], normed_ref[...].reshape(count, D))
        hidden_ref[...] = hidden
        activated_ref[...] = gelu(hidden).astype(jnp.bfloat16)
        tick(2)
        partial_ref[...] = contract_first(activated_ref[...], down_ref[...])

    return Work(
        before,
        None,
        [normed, up[0], down[0]],
        [VMEM_SPEC, part_spec(units, up[1]), part_spec(units, down[1])],
        [((units, count), jnp.float32), ((units, count), jnp.bfloat16)],
        [],
    )


def unit_back_work(grad, normed, up, down, kept, half_rows):
    parts, share, _ = normed.shape
    count = parts * share
    units = FF // parts
    hidden, activated = kept
    blocks = units // (2 * half_rows)

    def before(ins, outs, scratch, partial_ref, tick):
        grad_ref, _, up_ref, down_ref, hidden_ref, _ = ins
        grad_hidden = scratch[0]
        grad_act = contract_last(down_ref[...], grad_ref[...].reshape(count, D))
        _, pull = jax.vjp(gelu, hidden_ref[...])
        grad_hidden[...] = pull(grad_act)[0].astype(jnp.bfloat16)
        tick(2)
        partial_ref[...] = contract_first(grad_hidden[...], up_ref[...])

    def during(ins, outs, scratch):
        grad_ref, normed_ref, _, _, _, activated_ref = ins
        grad_hidden, own, near, fold_send, fold_recv = scratch
        value = times(grad_hidden[...], normed_ref[...].reshape(count, D))
        own[0] = value.astype(jnp.bfloat16).reshape(own.shape[1:])
        fold_copy(own, near, fold_send, fold_recv, 0).start()
        value = times(activated_ref[...], grad_ref[...].reshape(count, D))
        own[1] = value.astype(jnp.bfloat16).reshape(own.shape[1:])
        fold_copy(own, near, fold_send, fold_recv, 1).start()

    def after(ins, outs, scratch):
        _, own, near, fold_send, fold_recv = scratch
        for index in range(2):
            fold_copy(own, near, fold_send, fold_recv, index).wait()
            add_halves(own.at[index], near.at[index], outs[0], index * blocks)

    low, dma = jnp.bfloat16, pltpu.SemaphoreType.DMA
    return Work(
        before,
        during,
        [grad, normed, up[0], down[0], hidden, activated],
        [VMEM_SPEC, VMEM_SPEC, part_spec(units, up[1]), part_spec(units, down[1])]
        + [VMEM_SPEC] * 2,
        [((2 * blocks, half_rows, D), low)],
        [
            pltpu.VMEM((units, count), low),
            pltpu.VMEM((2, blocks, 2, half_rows, D), low),
            pltpu.VMEM((2, blocks, half_rows, D), low),
            dma((2,)),
            dma((2,)),
        ],
        after,
        True,
    )


LINE_BLOCKS = 2
LINE_LAG = 2


class Line:
    def __init__(self, sources, share):
        self.groups = lax.axis_size("dp")
        self.sources, self.share = sources, share
        count = sum(size for _, _, size in sources)
        _, half_rows, _ = sources[0][0].shape
        self.half = (count, half_rows, D)
        self.chunks = count // LINE_BLOCKS
        self.operands = [array for array, _, _ in sources]
        self.in_specs = [pl.BlockSpec(memory_space=pl.ANY)] * len(sources)
        dma = pltpu.SemaphoreType.DMA
        out = (count, 2, half_rows, D) if share else self.half
        self.out_shape = jax.ShapeDtypeStruct(out, jnp.bfloat16)
        self.out_spec = pl.BlockSpec(memory_space=pl.ANY if share else pltpu.VMEM)
        self.scratch = [
            pltpu.VMEM(self.half, jnp.bfloat16),
            pltpu.VMEM((2,) + self.half, jnp.bfloat16),
            pltpu.VMEM((2,) + self.half, jnp.bfloat16),
            dma((len(sources),)),
            dma((2, self.chunks)),
            dma((2, self.chunks)),
        ]
        if share:
            self.scratch += [pltpu.VMEM(self.half, jnp.bfloat16)] + [dma((self.chunks,))] * 3

    def bind(self, source_refs, out_ref, refs):
        self.source_refs, self.out = source_refs, out_ref
        self.own, self.came, self.going, self.own_sems, self.send_sems, self.recv_sems = refs[:6]
        self.total = out_ref
        if self.share:
            self.total, self.keep_sems, self.twin_send, self.twin_recv = refs[6:]
        self.done = 0
        self.group = lax.axis_index("dp")
        self.first = jnp.where(self.group < self.groups // 2, 0, 1)

    def at(self, chunk):
        return pl.ds(chunk * LINE_BLOCKS, LINE_BLOCKS)

    def comes(self, way):
        return jnp.where(way == 0, self.group > 0, self.group < self.groups - 1)

    def goes(self, way):
        return jnp.where(way == 0, self.group < self.groups - 1, self.group > 0)

    def copy(self, source, way, chunk):
        target = jnp.where(way == 0, self.group + 1, self.group - 1)
        return pltpu.make_async_remote_copy(
            src_ref=source,
            dst_ref=self.came.at[way, self.at(chunk)],
            send_sem=self.send_sems.at[way, chunk],
            recv_sem=self.recv_sems.at[way, chunk],
            device_id={"dp": target},
            device_id_type=MESH,
        )

    def load(self):
        self.loads, place = [], 0
        for index, (ref, (_, start, size)) in enumerate(zip(self.source_refs, self.sources)):
            copy = pltpu.make_async_copy(
                ref.at[pl.ds(start, size)], self.own.at[pl.ds(place, size)], self.own_sems.at[index]
            )
            copy.start()
            self.loads.append(copy)
            place += size

    def begin(self):
        for copy in self.loads:
            copy.wait()
        for way in range(2):

            @pl.when(jnp.logical_not(self.comes(way)))
            def _():
                self.came[way] = jnp.zeros(self.half, jnp.bfloat16)
                self.going[way] = self.own[...]

                def start(chunk, carry):
                    self.copy(self.going.at[way, self.at(chunk)], way, chunk).start()
                    return carry

                lax.fori_loop(0, self.chunks, start, 0)

    def twin_copy(self, chunk):
        side = lax.axis_index("seq")
        return pltpu.make_async_remote_copy(
            src_ref=self.total.at[self.at(chunk)],
            dst_ref=self.out.at[self.at(chunk), side],
            send_sem=self.twin_send.at[chunk],
            recv_sem=self.twin_recv.at[chunk],
            device_id={"seq": 1 - side},
            device_id_type=MESH,
        )

    def keep_copy(self, chunk):
        return pltpu.make_async_copy(
            self.total.at[self.at(chunk)],
            self.out.at[self.at(chunk), lax.axis_index("seq")],
            self.keep_sems.at[chunk],
        )

    def pass_on(self, way, chunk):
        rows = self.at(chunk)

        @pl.when(self.comes(way))
        def _():
            copy = self.copy(self.going.at[way, rows], way, chunk)
            copy.wait_recv()

            @pl.when(self.goes(way))
            def _():
                value = self.own[rows].astype(jnp.float32) + self.came[way, rows].astype(jnp.float32)
                self.going[way, rows] = value.astype(jnp.bfloat16)
                copy.start()

    def step(self, index):
        @pl.when(index < self.chunks)
        def _():
            self.pass_on(self.first, index)

        @pl.when(index >= LINE_LAG)
        def _():
            chunk = index - LINE_LAG
            rows = self.at(chunk)
            self.pass_on(1 - self.first, chunk)
            value = self.own[rows].astype(jnp.float32)
            value = value + self.came[0, rows].astype(jnp.float32)
            value = value + self.came[1, rows].astype(jnp.float32)
            self.total[rows] = value.astype(jnp.bfloat16)
            if self.share:
                self.keep_copy(chunk).start()
                self.twin_copy(chunk).start()

    def steps(self, count=None):
        last = self.chunks + LINE_LAG
        stop = last if count is None else min(self.done + count, last)

        def one(index, carry):
            self.step(index)
            return carry

        lax.fori_loop(self.done, stop, one, 0)
        self.done = stop

    def end(self):
        def one(chunk, carry):
            for way in range(2):

                @pl.when(self.goes(way))
                def _():
                    self.copy(self.going.at[way, self.at(chunk)], way, chunk).wait_send()

            if self.share:
                self.keep_copy(chunk).wait()
                self.twin_copy(chunk).wait()
            return carry

        lax.fori_loop(0, self.chunks, one, 0)


def reduce_all(terms, collective_id, line=None):
    _, tensors, groups, count, _ = terms.shape
    half = count // 2

    def kernel(*refs):
        refs = list(refs)
        terms_ref = refs.pop(0)
        source_refs = [refs.pop(0) for _ in line.operands] if line else []
        out_ref = refs.pop(0)
        joined_ref = refs.pop(0) if line else None
        (
            near, own, mid, sums, mid_in, far, far_in,
            own_sems, near_send, near_recv, mid_send, mid_recv, far_send, far_recv,
        ) = refs[:14]
        if line:
            line.bind(source_refs, joined_ref, refs[14:])
            line.load()
        group, part, side = lax.axis_index("dp"), lax.axis_index("tensor"), lax.axis_index("seq")
        twin = 1 - side
        parts = others("tensor")
        order = others("dp") + [group]
        meet(
            [{"seq": twin}]
            + [{"tensor": peer} for peer in parts]
            + [{"dp": peer} for peer in order[:-1]]
        )
        waits, near_copies, own_copies = [], [], []
        for place, target in enumerate(order):
            near_copies.append(
                send(
                    terms_ref.at[twin, :, target],
                    near.at[place],
                    near_send.at[place],
                    near_recv.at[place],
                    {"seq": twin},
                )
            )
            copy = pltpu.make_async_copy(
                terms_ref.at[side, :, target], own.at[place], own_sems.at[place]
            )
            copy.start()
            own_copies.append(copy)
        if line:
            line.begin()
        beside = lax.rem(part + 1, 2) + part - lax.rem(part, 2)
        across = lax.rem(part + 2, 4)
        corner = 3 - part
        upper, lower = pl.ds(0, half), pl.ds(half, half)
        first_copies, second_copies = [], []

        def hand(place, index, source, target):
            return send(
                source,
                mid_in.at[place, index],
                mid_send.at[place, index],
                mid_recv.at[place, index],
                {"tensor": target},
            )

        for place in range(groups):
            near_copies[place].wait_recv()
            own_copies[place].wait()
            if line and place < 4:
                line.steps(1)
            for slot in range(tensors):
                mid[place, slot] = (
                    own[place, slot].astype(jnp.float32) + near[place, slot].astype(jnp.float32)
                ).astype(jnp.bfloat16)
            first_copies.append(
                [
                    hand(place, 0, mid.at[place, corner, upper], beside),
                    hand(place, 1, mid.at[place, corner, lower], across),
                    hand(place, 2, mid.at[place, beside, upper], beside),
                    hand(place, 3, mid.at[place, across, lower], across),
                ]
            )
        for place in range(groups):
            if line and place < 4:
                line.steps(1)
            copies = []
            for index, slot, rows, target in ((0, across, upper, across), (1, beside, lower, beside)):
                first_copies[place][index].wait_recv()
                value = mid[place, slot, rows].astype(jnp.float32)
                value = value + mid_in[place, index].astype(jnp.float32)
                sums[place, index] = value.astype(jnp.bfloat16)
                copies.append(hand(place, 4 + index, sums.at[place, index], target))
            second_copies.append(copies)
        far_copies = []
        for place, target in enumerate(order):
            if line and place < 4:
                line.steps(1)
            copies = first_copies[place][2:] + second_copies[place]
            for copy in copies:
                copy.wait_recv()

            def joined(index):
                return mid_in[place, index].astype(jnp.float32)

            halves = [joined(2) + joined(4), joined(3) + joined(5)]
            total = mid[place, part].astype(jnp.float32) + jnp.concatenate(halves, axis=0)
            if place < groups - 1:
                far[place] = total.astype(jnp.bfloat16)
                far_copies.append(
                    send(
                        far.at[place],
                        far_in.at[place],
                        far_send.at[place],
                        far_recv.at[place],
                        {"dp": target},
                    )
                )
        if line:
            line.steps()
        for place, copy in enumerate(far_copies):
            copy.wait_recv()
            total = total + far_in[place].astype(jnp.float32)
        out_ref[...] = total
        for copy in near_copies + far_copies + [
            copy for row in first_copies + second_copies for copy in row
        ]:
            copy.wait_send()
        if line:
            line.end()

    block = (count, D)
    dma = pltpu.SemaphoreType.DMA
    return pl.pallas_call(
        kernel,
        name="reduce_all",
        out_shape=[jax.ShapeDtypeStruct(block, jnp.float32)] + ([line.out_shape] if line else []),
        in_specs=[pl.BlockSpec(memory_space=pl.ANY)] + (line.in_specs if line else []),
        out_specs=[pl.BlockSpec(memory_space=pltpu.VMEM)] + ([line.out_spec] if line else []),
        scratch_shapes=[pltpu.VMEM((groups, tensors) + block, jnp.bfloat16)] * 3
        + [
            pltpu.VMEM((groups, 2, half, D), jnp.bfloat16),
            pltpu.VMEM((groups, 6, half, D), jnp.bfloat16),
            pltpu.VMEM((groups,) + block, jnp.bfloat16),
            pltpu.VMEM((groups,) + block, jnp.bfloat16),
            dma((groups,)),
            dma((groups,)),
            dma((groups,)),
            dma((groups, 6)),
            dma((groups, 6)),
            dma((groups,)),
            dma((groups,)),
        ]
        + (line.scratch if line else []),
        cost_estimate=SHORT,
        compiler_params=pltpu.CompilerParams(
            collective_id=collective_id, has_side_effects=True, vmem_limit_bytes=56 << 20
        ),
    )(terms, *(line.operands if line else []))


def gather_all(block, collective_id, line=None):
    tensors, groups = lax.axis_size("tensor"), lax.axis_size("dp")
    half = block.shape[0] // 2

    def kernel(*refs):
        refs = list(refs)
        block_ref = refs.pop(0)
        source_refs = [refs.pop(0) for _ in line.operands] if line else []
        out = refs.pop(0)
        summed_ref = refs.pop(0) if line else None
        own_sem, far_send, far_recv, mid_send, mid_recv, near_send, near_recv = refs[:7]
        if line:
            line.bind(source_refs, summed_ref, refs[7:])
            line.load()
        group, part, side = lax.axis_index("dp"), lax.axis_index("tensor"), lax.axis_index("seq")
        twin = 1 - side
        meet(
            [{"seq": twin}]
            + [{"tensor": peer} for peer in others("tensor")]
            + [{"dp": peer} for peer in others("dp")]
        )
        far_copies = [
            send(
                block_ref,
                out.at[side, part, group],
                far_send.at[step],
                far_recv.at[step],
                {"dp": peer},
            )
            for step, peer in enumerate(others("dp"))
        ]
        own = pltpu.make_async_copy(block_ref, out.at[side, part, group], own_sem)
        own.start()
        if line:
            line.begin()
        beside = lax.rem(part + 1, 2) + part - lax.rem(part, 2)
        across = lax.rem(part + 2, 4)
        corner = 3 - part
        upper, lower = pl.ds(0, half), pl.ds(half, half)
        first_copies, second_copies, near_copies = [], [], []
        for place in range(groups):
            source = behind("dp", place)
            if place:
                if line and place < 4:
                    line.steps(1)
                far_copies[place - 1].wait_recv()
            held = out.at[side, part, source] if place else block_ref

            def hand(index, piece, slot, rows, target):
                return send(
                    piece,
                    out.at[side, slot, source, rows],
                    mid_send.at[place, index],
                    mid_recv.at[place, index],
                    {"tensor": target},
                )

            first = [
                hand(0, held.at[upper], part, upper, beside),
                hand(1, held.at[lower], part, lower, across),
                hand(2, held.at[lower], part, lower, beside),
                hand(3, held.at[upper], part, upper, across),
            ]
            near_copies.append(
                send(
                    held,
                    out.at[side, part, source],
                    near_send.at[place, 0],
                    near_recv.at[place, 0],
                    {"seq": twin},
                )
            )
            first[0].wait_recv()
            second = [hand(4, out.at[side, beside, source, upper], beside, upper, across)]
            first[1].wait_recv()
            second.append(hand(5, out.at[side, across, source, lower], across, lower, beside))
            first_copies.append(first)
            second_copies.append(second)
        for place in range(groups):
            if line and place < 4:
                line.steps(2)
            source = behind("dp", place)
            ready = [
                (beside, first_copies[place][2:3]),
                (across, first_copies[place][3:4]),
                (corner, second_copies[place]),
            ]
            for step, (slot, copies) in enumerate(ready):
                for copy in copies:
                    copy.wait_recv()
                held = out.at[side, slot, source]
                near_copies.append(
                    send(
                        held,
                        held,
                        near_send.at[place, step + 1],
                        near_recv.at[place, step + 1],
                        {"seq": twin},
                    )
                )
        if line:
            line.steps()
        for copy in near_copies:
            copy.wait_recv()
        for copy in near_copies + far_copies + [
            copy for row in first_copies + second_copies for copy in row
        ]:
            copy.wait_send()
        own.wait()
        if line:
            line.end()

    dma = pltpu.SemaphoreType.DMA
    anywhere = pl.BlockSpec(memory_space=pl.ANY)
    return pl.pallas_call(
        kernel,
        name="gather_all",
        out_shape=[jax.ShapeDtypeStruct((2, tensors, groups) + block.shape, block.dtype)]
        + ([line.out_shape] if line else []),
        in_specs=[VMEM_SPEC] + (line.in_specs if line else []),
        out_specs=[anywhere] + ([line.out_spec] if line else []),
        scratch_shapes=[
            dma,
            dma((groups - 1,)),
            dma((groups - 1,)),
            dma((groups, 6)),
            dma((groups, 6)),
            dma((groups, tensors)),
            dma((groups, tensors)),
        ]
        + (line.scratch if line else []),
        cost_estimate=SHORT,
        compiler_params=pltpu.CompilerParams(
            collective_id=collective_id, has_side_effects=True, vmem_limit_bytes=40 << 20
        ),
    )(block, *(line.operands if line else []))


def reduce_rows(terms, ids, line=None):
    count, groups = terms.shape[3], terms.shape[2]
    pieces = max(1, groups // 4)
    part = count // pieces
    sums, joined = [], None
    for i in range(pieces):
        piece = terms[:, :, :, i * part : (i + 1) * part] if pieces > 1 else terms
        if i == 0 and line:
            total, joined = reduce_all(piece, ids[1], line)
        else:
            (total,) = reduce_all(piece, ids[0])
        sums.append(total)
    return jnp.concatenate(sums, axis=0) if pieces > 1 else sums[0], joined


def join_stats(stats, collective_id):
    _, tensors, groups, _, _ = stats.shape

    def join(left, right):
        top = jnp.maximum(left[..., 0:1, :], right[..., 0:1, :])
        total = left[..., 1:2, :] * jnp.exp(left[..., 0:1, :] - top) + right[..., 1:2, :] * jnp.exp(
            right[..., 0:1, :] - top
        )
        return jnp.concatenate(
            [top, total, left[..., 2:3, :] + right[..., 2:3, :], left[..., 3:, :]], axis=-2
        )

    def kernel(
        stats_ref, home, full, near, mid, mid_in, far, far_in,
        near_send, near_recv, mid_send, mid_recv, far_send, far_recv,
    ):
        group, part, side = lax.axis_index("dp"), lax.axis_index("tensor"), lax.axis_index("seq")
        twin = 1 - side
        parts, groups_else = others("tensor"), others("dp")
        meet(
            [{"seq": twin}]
            + [{"tensor": peer} for peer in parts]
            + [{"dp": peer} for peer in groups_else]
        )
        copy = send(stats_ref.at[twin], near, near_send.at[0], near_recv.at[0], {"seq": twin})
        copy.wait()
        for slot in range(tensors):
            for spot in range(groups):
                mid[slot, spot] = join(stats_ref[side, slot, spot], near[slot, spot])
        copies = [
            send(mid.at[peer], mid_in.at[step], mid_send.at[0, step], mid_recv.at[0, step], {"tensor": peer})
            for step, peer in enumerate(parts)
        ]
        for copy in copies:
            copy.wait()
        for spot in range(groups):
            total = mid[part, spot]
            for step in range(tensors - 1):
                total = join(total, mid_in[step, spot])
            far[spot] = total
        copies = [
            send(far.at[peer], far_in.at[step], far_send.at[0, step], far_recv.at[0, step], {"dp": peer})
            for step, peer in enumerate(groups_else)
        ]
        total = far[group]
        for step, copy in enumerate(copies):
            copy.wait()
            total = join(total, far_in[step])
        log_total = total[0:1] + jnp.log(total[1:2])
        home[...] = jnp.concatenate([log_total, total[2:3], total[2:]], axis=0)
        full[side, part, group] = jnp.broadcast_to(log_total, (8, LANES))
        held = full.at[side, part, group]
        copies = [
            send(held, held, far_send.at[1, step], far_recv.at[1, step], {"dp": peer})
            for step, peer in enumerate(groups_else)
        ]
        for copy in copies:
            copy.wait()
        held = full.at[side, part]
        copies = [
            send(held, held, mid_send.at[1, step], mid_recv.at[1, step], {"tensor": peer})
            for step, peer in enumerate(parts)
        ]
        for copy in copies:
            copy.wait()
        held = full.at[side]
        send(held, held, near_send.at[1], near_recv.at[1], {"seq": twin}).wait()

    tile = (8, LANES)
    dma = pltpu.SemaphoreType.DMA
    vmem = pl.BlockSpec(memory_space=pltpu.VMEM)
    return pl.pallas_call(
        kernel,
        name="join_stats",
        out_shape=[
            jax.ShapeDtypeStruct(tile, jnp.float32),
            jax.ShapeDtypeStruct(stats.shape, jnp.float32),
        ],
        in_specs=[vmem],
        out_specs=[vmem, vmem],
        scratch_shapes=[
            pltpu.VMEM((tensors, groups) + tile, jnp.float32),
            pltpu.VMEM((tensors, groups) + tile, jnp.float32),
            pltpu.VMEM((tensors - 1, groups) + tile, jnp.float32),
            pltpu.VMEM((groups,) + tile, jnp.float32),
            pltpu.VMEM((groups - 1,) + tile, jnp.float32),
            dma((2,)),
            dma((2,)),
            dma((2, tensors - 1)),
            dma((2, tensors - 1)),
            dma((2, groups - 1)),
            dma((2, groups - 1)),
        ],
        cost_estimate=SHORT,
        compiler_params=pltpu.CompilerParams(collective_id=collective_id, has_side_effects=True),
    )(stats)


def spread_tokens(block, collective_id):
    tensors, groups = lax.axis_size("tensor"), lax.axis_size("dp")
    rows = 2 * tensors * groups

    def kernel(block_ref, ids, targets, kept, count, held, own_sem, send_sems, recv_sems):
        group, side = lax.axis_index("dp"), lax.axis_index("seq")
        peers = [
            {"dp": lax.rem(group + step // 2, groups), "seq": lax.rem(side + step % 2, 2)}
            for step in range(1, 2 * groups)
        ]
        meet(peers)
        copies = [
            send(block_ref, held.at[group, side], send_sems.at[step], recv_sems.at[step], peer)
            for step, peer in enumerate(peers)
        ]
        own = pltpu.make_async_copy(block_ref, held.at[group, side], own_sem)
        own.start()
        own.wait()
        for copy in copies:
            copy.wait()
        lane = lax.broadcasted_iota(jnp.int32, (1, LANES), 1)
        total = jnp.zeros((1, LANES), jnp.int32)
        for half in range(2):
            for source in range(groups):
                limit = held[source, half, 2 * tensors : 2 * tensors + 1, :]
                total = total + limit
                for part in range(tensors):
                    row = (half * tensors + part) * groups + source
                    tile, place = row // TILE_GROUPS, slice(row % TILE_GROUPS, row % TILE_GROUPS + 1)
                    ids[tile, place, :] = held[source, half, part : part + 1, :]
                    targets[tile, place, :] = held[source, half, tensors + part : tensors + part + 1, :]
                    kept[tile, place, :] = jnp.where(lane + part * LANES < limit, 1.0, 0.0)
        count[...] = total.astype(jnp.float32)

    dma = pltpu.SemaphoreType.DMA
    vmem = pl.BlockSpec(memory_space=pltpu.VMEM)
    shape = (rows // TILE_GROUPS, TILE_GROUPS, LANES)
    return pl.pallas_call(
        kernel,
        name="spread_tokens",
        out_shape=[
            jax.ShapeDtypeStruct(shape, jnp.int32),
            jax.ShapeDtypeStruct(shape, jnp.int32),
            jax.ShapeDtypeStruct(shape, jnp.float32),
            jax.ShapeDtypeStruct((1, LANES), jnp.float32),
        ],
        in_specs=[vmem],
        out_specs=[vmem] * 4,
        scratch_shapes=[
            pltpu.VMEM((groups, 2) + block.shape, jnp.int32),
            dma,
            dma((2 * groups - 1,)),
            dma((2 * groups - 1,)),
        ],
        cost_estimate=SHORT,
        compiler_params=pltpu.CompilerParams(collective_id=collective_id, has_side_effects=True),
    )(block)


def finish(gain_grads, states, grad_ys, home, keep, table_squares, layer_squares, count, smalls, collective_id):
    tensors, groups = lax.axis_size("tensor"), lax.axis_size("dp")
    block = (8, D)
    gain_rows = 2 * LAYERS + 1
    operands = list(gain_grads) + list(states) + list(grad_ys) + [
        home, keep, table_squares, layer_squares, count
    ] + list(smalls)

    def kernel(*refs):
        refs = list(refs)
        gain_refs = [refs.pop(0) for _ in gain_grads]
        state_refs = [refs.pop(0) for _ in states]
        grad_refs = [refs.pop(0) for _ in grad_ys]
        home_ref, keep_ref, table_ref, layer_ref, count_ref = [refs.pop(0) for _ in range(5)]
        small_refs = [refs.pop(0) for _ in smalls]
        out_refs = [refs.pop(0) for _ in range(8)]
        near, mid, far, near_send, near_recv, mid_send, mid_recv, far_send, far_recv = refs
        group, part, side = lax.axis_index("dp"), lax.axis_index("tensor"), lax.axis_index("seq")
        parts, groups_else = others("tensor"), others("dp")
        meet(
            [{"seq": 1 - side}]
            + [{"tensor": peer} for peer in parts]
            + [{"dp": peer} for peer in groups_else]
        )
        values = []
        for later in range(1, LAYERS + 1):
            grad = grad_refs[later - 1][...]
            for level in range(later + 1):
                values.append(jnp.sum(grad * state_refs[level][...], keepdims=True))
        loss = (home_ref[0:1, :] - home_ref[1:2, :]) * keep_ref[...]
        values.append(jnp.sum(loss, keepdims=True))
        values.append(jnp.sum(table_ref[...], keepdims=True) + layer_ref[...])
        lane = lax.broadcasted_iota(jnp.int32, (1, D), 1)
        row = jnp.zeros((1, D), jnp.float32)
        for place, value in enumerate(values):
            row = jnp.where(lane == place, value, row)
        blank = jnp.zeros((8 - gain_rows - 1, D), jnp.float32)
        total = jnp.concatenate([ref[...] for ref in gain_refs] + [row, blank], axis=0)
        stages = [
            ("seq", near, side, [1 - side], near_send, near_recv),
            ("tensor", mid, part, parts, mid_send, mid_recv),
            ("dp", far, group, groups_else, far_send, far_recv),
        ]
        for axis, slots, me, peers, send_sems, recv_sems in stages:
            slots[me] = total
            copies = [
                send(slots.at[me], slots.at[me], send_sems.at[step], recv_sems.at[step], {axis: peer})
                for step, peer in enumerate(peers)
            ]
            for copy in copies:
                copy.wait()
            total = slots[0]
            for index in range(1, slots.shape[0]):
                total = total + slots[index]
        gain_total = total[:gain_rows]
        row = total[gain_rows : gain_rows + 1]

        def pick(place):
            return jnp.sum(jnp.where(lane == place, row, 0.0), axis=1, keepdims=True)

        mix_squares = jnp.sum(jnp.where(lane < MIX_WEIGHTS, row * row, 0.0), axis=1, keepdims=True)
        gain_squares = jnp.sum(gain_total * gain_total, keepdims=True)
        tokens = count_ref[:, 0:1]
        clip_norm = jnp.sqrt(pick(MIX_WEIGHTS + 1) + gain_squares + mix_squares) / tokens
        factor = jnp.minimum(1.0, CLIP_NORM / clip_norm) / tokens
        gain_news = adam_update(
            *[ref[...] for ref in small_refs[:3]], gain_total * factor, RATE_SMALL, 0.0
        )
        mix_news = adam_update(
            *[ref[...] for ref in small_refs[3:]], row[:, :MIX_WEIGHTS] * factor, RATE_SMALL, 0.0
        )
        for ref, value in zip(out_refs[:6], gain_news + mix_news):
            ref[...] = value
        ends = jnp.where(lane == 0, pick(MIX_WEIGHTS), jnp.where(lane == 1, clip_norm, factor))
        out_refs[6][...] = ends[:, :LANES]
        out_refs[7][...] = jnp.broadcast_to(factor, (8, LANES))

    dma = pltpu.SemaphoreType.DMA
    vmem = pl.BlockSpec(memory_space=pltpu.VMEM)
    return pl.pallas_call(
        kernel,
        name="finish",
        out_shape=[jax.ShapeDtypeStruct(value.shape, jnp.float32) for value in smalls]
        + [
            jax.ShapeDtypeStruct((1, LANES), jnp.float32),
            jax.ShapeDtypeStruct((8, LANES), jnp.float32),
        ],
        in_specs=[vmem] * len(operands),
        out_specs=[vmem] * 8,
        scratch_shapes=[
            pltpu.VMEM((2,) + block, jnp.float32),
            pltpu.VMEM((tensors,) + block, jnp.float32),
            pltpu.VMEM((groups,) + block, jnp.float32),
            dma((1,)),
            dma((1,)),
            dma((tensors - 1,)),
            dma((tensors - 1,)),
            dma((groups - 1,)),
            dma((groups - 1,)),
        ],
        cost_estimate=SHORT,
        compiler_params=pltpu.CompilerParams(collective_id=collective_id, has_side_effects=True),
    )(*operands)


SLOT_STEP = 4


def update_slots(plan, factor, master, first, second, layer_grads, grad_table):
    slots, half_rows, _ = master.shape
    steps = -(-slots // SLOT_STEP)
    plan = jnp.pad(plan, ((0, 0), (0, steps * SLOT_STEP - slots)))

    def kernel(plan_ref, factor_ref, master_ref, first_ref, second_ref, *rest):
        layer_refs = rest[:SLOT_STEP]
        table_ref, new_master, new_first, new_second = rest[SLOT_STEP:]
        for place in range(SLOT_STEP):
            kind = plan_ref[0, pl.program_id(0) * SLOT_STEP + place]
            grad = table_ref[place * half_rows : (place + 1) * half_rows, :]
            grad = jnp.where(kind == 0, layer_refs[place][0].astype(jnp.float32), grad)
            grad = jnp.where(kind >= 0, grad * factor_ref[0:1, 0:1], 0.0)
            values = adam_update(
                master_ref[place],
                first_ref[place],
                second_ref[place],
                grad,
                RATE_MATRIX,
                DECAY_MATRIX,
            )
            for ref, value in zip((new_master, new_first, new_second), values):
                ref[place] = value

    slot = pl.BlockSpec((SLOT_STEP, half_rows, D), lambda step, plan: (step, 0, 0))
    return pl.pallas_call(
        kernel,
        name="update_slots",
        grid_spec=pltpu.PrefetchScalarGridSpec(
            num_scalar_prefetch=1,
            grid=(steps,),
            in_specs=[pl.BlockSpec((8, LANES), lambda step, plan: (0, 0)), slot, slot, slot]
            + [
                pl.BlockSpec(
                    (1, half_rows, D),
                    lambda step, plan, place=place: (plan[1, step * SLOT_STEP + place], 0, 0),
                )
                for place in range(SLOT_STEP)
            ]
            + [pl.BlockSpec((SLOT_STEP * half_rows, D), lambda step, plan: (step, 0))],
            out_specs=[slot] * 3,
        ),
        out_shape=[jax.ShapeDtypeStruct(master.shape, jnp.float32)] * 3,
        cost_estimate=SHORT,
        compiler_params=pltpu.CompilerParams(vmem_limit_bytes=48 << 20),
    )(
        plan,
        factor,
        master,
        first,
        second,
        *[layer_grads] * SLOT_STEP,
        grad_table,
    )


def row_of(groups_ref):
    return jnp.concatenate([groups_ref[0, g : g + 1, :] for g in range(TILE_GROUPS)], axis=1)


def stat_row(stat_ref, row):
    return jnp.concatenate([stat_ref[g, row : row + 1, :] for g in range(TILE_GROUPS)], axis=1)


def chunk_of(span_ref, step):
    return pl.ds(pl.multiple_of(span_ref[0] + step * ROW_STEP, 16), ROW_STEP)


def chunks_of(span_ref):
    return (span_ref[1] - span_ref[0] + ROW_STEP - 1) // ROW_STEP


def whole(shape):
    return pl.BlockSpec(shape, lambda step, span: (0,) * len(shape), pipeline_mode=pl.Buffered(1))


TILE = TILE_GROUPS * LANES
TOKENS_SPEC = pl.BlockSpec((1, TILE_GROUPS, LANES), lambda step, span: (step, 0, 0))
STATS_SPEC = pl.BlockSpec((TILE_GROUPS, 8, LANES), lambda step, span: (step, 0, 0))
ROWS_SPEC = pl.BlockSpec((TILE, D), lambda step, span: (step, 0))


def local_call(name, kernel, steps, span, operands, in_specs, out_shape, out_specs, scratch):
    return pl.pallas_call(
        kernel,
        name=name,
        grid_spec=pltpu.PrefetchScalarGridSpec(
            num_scalar_prefetch=1,
            grid=(steps,),
            in_specs=in_specs,
            out_specs=out_specs,
            scratch_shapes=scratch,
        ),
        out_shape=out_shape,
        cost_estimate=SHORT,
        compiler_params=pltpu.CompilerParams(vmem_limit_bytes=60 << 20),
    )(span, *operands)


def look_up(span, row_ids, tokens, table):
    rows = table.shape[0]
    steps = tokens.shape[0]

    def kernel(span_ref, ids_ref, tokens_ref, table_ref, out_ref, acc):
        acc[...] = jnp.zeros_like(acc)
        wanted = row_of(tokens_ref)

        def one(step, carry):
            chunk = chunk_of(span_ref, step)
            hits = jnp.where(ids_ref[chunk, :] == wanted, 1.0, 0.0).astype(jnp.bfloat16)
            acc[...] += contract_first(hits, table_ref[chunk, :])
            return carry

        lax.fori_loop(0, chunks_of(span_ref), one, 0)
        out_ref[...] = acc[...].astype(jnp.bfloat16)

    return local_call(
        "look_up",
        kernel,
        steps,
        span,
        (row_ids, tokens, table),
        [whole((rows, 1)), TOKENS_SPEC, whole((rows, D))],
        jax.ShapeDtypeStruct((steps * TILE, D), jnp.bfloat16),
        ROWS_SPEC,
        [pltpu.VMEM((TILE, D), jnp.float32)],
    )


def head_forward(span, row_ids, labels, table, final):
    rows = table.shape[0]
    steps = labels.shape[0]

    def kernel(span_ref, ids_ref, labels_ref, table_ref, final_ref, powers_ref, stats_ref, scores):
        wanted = row_of(labels_ref)
        hidden = final_ref[...]

        def first(step, carry):
            top, target = carry
            chunk = chunk_of(span_ref, step)
            ids = ids_ref[chunk, :]
            raw = contract_last(table_ref[chunk, :], hidden)
            raw = jnp.where(ids >= 0, raw, -1e30)
            scores[chunk, :] = raw
            top = jnp.maximum(top, jnp.max(raw, axis=0, keepdims=True))
            target = target + jnp.sum(jnp.where(ids == wanted, raw, 0.0), axis=0, keepdims=True)
            return (top, target)

        blank = jnp.zeros((1, TILE), jnp.float32)
        top, target = lax.fori_loop(0, chunks_of(span_ref), first, (blank - 1e30, blank))

        def second(step, total):
            chunk = chunk_of(span_ref, step)
            powers = jnp.exp(scores[chunk, :] - top)
            powers_ref[chunk, :] = powers.astype(jnp.bfloat16)
            return total + jnp.sum(powers, axis=0, keepdims=True)

        total = lax.fori_loop(0, chunks_of(span_ref), second, blank)
        rest = jnp.zeros((5, LANES), jnp.float32)
        for g in range(TILE_GROUPS):
            lanes = slice(g * LANES, (g + 1) * LANES)
            stats_ref[g] = jnp.concatenate(
                [top[:, lanes], total[:, lanes], target[:, lanes], rest], axis=0
            )

    return local_call(
        "head_forward",
        kernel,
        steps,
        span,
        (row_ids, labels, table, final),
        [whole((rows, 1)), TOKENS_SPEC, whole((rows, D)), ROWS_SPEC],
        [
            jax.ShapeDtypeStruct((rows, steps * TILE), jnp.bfloat16),
            jax.ShapeDtypeStruct((steps * TILE_GROUPS, 8, LANES), jnp.float32),
        ],
        [pl.BlockSpec((rows, TILE), lambda step, span: (0, step)), STATS_SPEC],
        [pltpu.VMEM((rows, TILE), jnp.float32)],
    )


def head_backward(span, row_ids, labels, keep, stats, log_totals, table, final, powers):
    rows = table.shape[0]
    steps = labels.shape[0]

    def kernel(
        span_ref, ids_ref, labels_ref, keep_ref, stats_ref, logs_ref, table_ref, final_ref,
        powers_ref, grad_final_ref, grad_table_ref, acc,
    ):
        @pl.when(pl.program_id(0) == 0)
        def _():
            grad_table_ref[...] = jnp.zeros_like(grad_table_ref)

        acc[...] = jnp.zeros_like(acc)
        wanted, kept = row_of(labels_ref), row_of(keep_ref)
        scale = jnp.exp(stat_row(stats_ref, 0) - stat_row(logs_ref, 0)) * kept
        hidden = final_ref[...]

        def one(step, carry):
            chunk = chunk_of(span_ref, step)
            grads = powers_ref[chunk, :].astype(jnp.float32) * scale
            grads = grads - jnp.where(ids_ref[chunk, :] == wanted, kept, 0.0)
            grads = grads.astype(jnp.bfloat16)
            grad_table_ref[chunk, :] += jnp.dot(grads, hidden, preferred_element_type=jnp.float32)
            acc[...] += contract_first(grads, table_ref[chunk, :])
            return carry

        lax.fori_loop(0, chunks_of(span_ref), one, 0)
        grad_final_ref[...] = acc[...].astype(jnp.bfloat16)

    return local_call(
        "head_backward",
        kernel,
        steps,
        span,
        (row_ids, labels, keep, stats, log_totals, table, final, powers),
        [
            whole((rows, 1)),
            TOKENS_SPEC,
            TOKENS_SPEC,
            STATS_SPEC,
            STATS_SPEC,
            whole((rows, D)),
            ROWS_SPEC,
            pl.BlockSpec((rows, TILE), lambda step, span: (0, step)),
        ],
        [
            jax.ShapeDtypeStruct((steps * TILE, D), jnp.bfloat16),
            jax.ShapeDtypeStruct((rows, D), jnp.float32),
        ],
        [ROWS_SPEC, whole((rows, D))],
        [pltpu.VMEM((TILE, D), jnp.float32)],
    )


def look_back(span, row_ids, tokens, grad_start, grad_table):
    rows = grad_table.shape[0]
    steps = tokens.shape[0]

    def kernel(span_ref, ids_ref, tokens_ref, grad_ref, table_ref, out_ref, squares_ref):
        @pl.when(pl.program_id(0) == 0)
        def _():
            out_ref[...] = table_ref[...]

        wanted = row_of(tokens_ref)
        grads = grad_ref[...]

        def one(step, carry):
            chunk = chunk_of(span_ref, step)
            hits = jnp.where(ids_ref[chunk, :] == wanted, 1.0, 0.0).astype(jnp.bfloat16)
            out_ref[chunk, :] += jnp.dot(hits, grads, preferred_element_type=jnp.float32)
            return carry

        lax.fori_loop(0, chunks_of(span_ref), one, 0)

        @pl.when(pl.program_id(0) == steps - 1)
        def _():
            def square(step, total):
                values = out_ref[chunk_of(span_ref, step), :]
                values = (values * values).reshape(ROW_STEP // 8, 8, D).sum(axis=0)
                return total + values

            squares_ref[...] = lax.fori_loop(
                0, chunks_of(span_ref), square, jnp.zeros((8, D), jnp.float32)
            )

    return local_call(
        "look_back",
        kernel,
        steps,
        span,
        (row_ids, tokens, grad_start, grad_table),
        [whole((rows, 1)), TOKENS_SPEC, ROWS_SPEC, whole((rows, D))],
        [
            jax.ShapeDtypeStruct((rows, D), jnp.float32),
            jax.ShapeDtypeStruct((8, D), jnp.float32),
        ],
        [whole((rows, D)), whole((8, D))],
        [],
    )


def body(
    token_ids,
    labels,
    real_counts,
    owners,
    master,
    first_moment,
    second_moment,
    gains,
    gains_first,
    gains_second,
    mix,
    mix_first,
    mix_second,
):
    tensors = lax.axis_size("tensor")
    groups = lax.axis_size("dp")
    group = lax.axis_index("dp")
    tensor_part = lax.axis_index("tensor")
    seq_part = lax.axis_index("seq")
    slots, half_rows, _ = master.shape
    seq_count, half_len = token_ids.shape
    row_count = seq_count * half_len
    share = row_count // tensors
    head_rows = 3 * D // tensors
    out_rows = D // tensors
    unit_rows = FF // tensors
    layer_rows = head_rows + out_rows + 2 * unit_rows
    layer_blocks = layer_rows // (2 * half_rows)
    blocks = LAYERS * layer_blocks
    vocab_rows = VOCAB // tensors
    local_heads = HEADS // tensors

    slot_rank = slot_table(owners)
    block_ids = jnp.arange(owners.shape[0], dtype=jnp.int32)
    mine = owners == group
    match = (jnp.arange(slots)[:, None] == slot_rank[None, :]) & mine[None, :]
    slot_block = jnp.sum(jnp.where(match, block_ids[None, :] + 1, 0), axis=1) - 1
    row_ids = (
        tensor_part * vocab_rows
        + (slot_block[:, None] - blocks) * (2 * half_rows)
        + seq_part * half_rows
        + jnp.arange(half_rows, dtype=jnp.int32)[None, :]
    )
    row_ids = jnp.where(slot_block[:, None] >= blocks, row_ids, -1).reshape(-1, 1)
    spare = -(-ROW_STEP // half_rows)
    row_ids = jnp.pad(row_ids, ((0, spare * half_rows), (0, 0)), constant_values=-1)
    held = jnp.sum(jnp.where(mine, 1, 0)) * half_rows
    first_held = jnp.sum(jnp.where(mine & (block_ids < blocks), 1, 0)) * half_rows
    span = jnp.stack([first_held, held]).astype(jnp.int32)
    plan = jnp.stack(
        [
            jnp.where(slot_block < 0, -1, jnp.where(slot_block < blocks, 0, 1)),
            jnp.where(slot_block < blocks, jnp.maximum(slot_block, 0), 0),
        ]
    ).astype(jnp.int32)

    packed = jnp.concatenate(
        [
            token_ids.reshape(tensors, LANES),
            labels.reshape(tensors, LANES),
            jnp.broadcast_to(real_counts[:, None], (16 - 2 * tensors, LANES)),
        ],
        axis=0,
    )
    ids_all, labels_all, keep_all, count = spread_tokens(packed, 15)
    order = (2, tensors, groups, share)

    table_slots = jnp.pad(master.astype(jnp.bfloat16), ((0, spare), (0, 0), (0, 0)))
    table = table_slots.reshape(-1, D)

    halves = jnp.where(
        mine[:blocks][:, None, None], jnp.take(table_slots, slot_rank[:blocks], axis=0), 0.0
    ).astype(jnp.bfloat16)
    third = layer_blocks // 3

    def weights_line(start, size):
        return Line([(halves, start * third, size * third)], True)

    def as_table(joined):
        return joined.reshape(-1, D)

    positions = seq_part * half_len + jnp.arange(row_count) % half_len
    steps_half = jnp.arange(HEAD_DIM // 2).astype(jnp.float32)
    freqs = 10000.0 ** (-2.0 * steps_half / HEAD_DIM)
    angles = freqs[:, None] * positions.astype(jnp.float32)[None, :]
    cosine, sine = jnp.cos(angles), jnp.sin(angles)

    looked = look_up(span, row_ids, ids_all, table).reshape(order + (D,))
    start, joined = reduce_rows(looked, (0, 14), weights_line(0, 2))
    table_one = as_table(joined)
    attention_table, up = table_one, (table_one, 1)
    tables = []
    gain = [gains[i : i + 1] for i in range(2 * LAYERS + 1)]
    piece = ((share, D), jnp.float32)

    def normed_of(total, stream, gain_row):
        return (layer_norm_parts(stream)[0] * gain_row,)

    def inner_of(total, stream, gain_row):
        inner = stream + total
        return (inner, layer_norm_parts(inner)[0] * gain_row)

    def outcome_of(base, total, inner, gain_row, *rest):
        states, scalars = rest[:-1], rest[-1]
        outcome = inner + total
        stream = scalars[base + len(states)] * outcome
        for source, state in enumerate(states):
            stream = stream + scalars[base + source] * state
        return (outcome, stream, layer_norm_parts(stream)[0] * gain_row)

    (normed,) = tensor_step("normed", normed_of, None, (start, gain[0]), (), [], True, 1)
    states, streams, inners, kept_all = [start], [start], [], []
    for level in range(LAYERS):
        here = 3 * level
        inner, normed_two, queries, both, logs, attended, joined = tensor_step(
            f"inner_{level}",
            inner_of,
            attention_work(normed, attention_table, cosine, sine),
            (streams[level], gain[2 * level + 1]),
            (),
            [piece],
            True,
            2 if level == 0 else 15 + level,
            weights_line(here + 1, 2) if level else weights_line(here + 2, 1),
        )
        kept = (queries, both, logs, attended)
        joined = as_table(joined)
        if level:
            up, down = (joined, 0), (joined, 1)
        else:
            down = (joined, 0)
        tables.append((attention_table, up, down))
        last = level == LAYERS - 1
        outcome, stream, normed_next, hidden, activated, *joined = tensor_step(
            f"outcome_{level}",
            partial(outcome_of, (level + 1) * (level + 2) // 2 - 1),
            unit_work(normed_two, up, down),
            [inner, gain[2 * level + 2]] + states,
            (mix,),
            [piece, piece] + ([((share, D), jnp.bfloat16)] if last else []),
            not last,
            3 + level,
            None if last else weights_line(here + 3, 1),
        )
        if not last:
            attention_table = as_table(joined[0])
        inners.append(inner)
        kept_all.append((normed, kept, normed_two, (hidden, activated)))
        states.append(outcome)
        streams.append(stream)
        normed = normed_next

    final_all = gather_all(normed, 3 + LAYERS)[0].reshape(-1, D)
    powers, stats = head_forward(span, row_ids, labels_all, table, final_all)
    home, log_totals = join_stats(
        stats.reshape((2, tensors, groups, 8, LANES)), 4 + LAYERS
    )
    grad_final, grad_table = head_backward(
        span,
        row_ids,
        labels_all,
        keep_all,
        stats,
        log_totals.reshape(-1, 8, LANES),
        table,
        final_all,
        powers,
    )
    grad_final, _ = reduce_rows(grad_final.reshape(order + (D,)), (0, 14))

    row = ((1, D), jnp.float32)

    def top_of(total, grad, stream, gain_row, scalars):
        grad_top, grad_gain = norm_pull(grad, gain_row, stream)
        grad_state = scalars[MIX_WEIGHTS - 1] * grad_top
        return (grad_top, grad_state, grad_gain, grad_state)

    def inner_back(total, grad_out, inner, gain_row):
        grad, grad_gain = norm_pull(total, gain_row, inner)
        grad = grad_out + grad
        return (grad, grad_gain, grad)

    def stream_back(block, total, grad_inner, stream, gain_row, *rest):
        grad_ys, scalars = rest[:-1], rest[-1]
        grad, grad_gain = norm_pull(total, gain_row, stream)
        grad = grad_inner + grad
        state = grad if block == 0 else scalars[block * (block + 1) // 2 - 1 + block] * grad
        for offset, grad_y in enumerate(grad_ys):
            later = block + 1 + offset
            state = state + scalars[later * (later + 1) // 2 - 1 + block] * grad_y
        return (grad, state, grad_gain, state)

    grad_ys = [None] * (LAYERS + 1)
    gain_grads = [None] * (2 * LAYERS + 1)
    layer_grads, attention_grads = [None] * (3 * LAYERS), None
    grad_ys[LAYERS], grad_state, gain_grads[2 * LAYERS], grad_branch = tensor_step(
        "top_back",
        top_of,
        None,
        (grad_final, streams[LAYERS], gain[2 * LAYERS]),
        (mix,),
        [piece, piece, row],
        True,
        5 + LAYERS,
    )
    for level in reversed(range(LAYERS)):
        normed, kept, normed_two, unit_kept = kept_all[level]
        attention_table, up, down = tables[level]
        grad_inner, gain_grads[2 * level + 1], grad_attn, unit_grads, *summed = tensor_step(
            f"inner_back_{level}",
            inner_back,
            unit_back_work(grad_branch, normed_two, up, down, unit_kept, half_rows),
            (grad_state, inners[level], gain[2 * level + 1]),
            (),
            [piece, row],
            True,
            6 + LAYERS if level == 0 else 19 + level,
            None if attention_grads is None else Line([(attention_grads, 0, third)], False),
        )
        if summed:
            layer_grads[3 * (level + 1)] = summed[0]
        carried = 1 if level == 0 else 2
        grad_ys[level], grad_state, gain_grads[2 * level], grad_branch, attention_grads, summed = (
            tensor_step(
                f"stream_back_{level}",
                partial(stream_back, level),
                attention_back_work(
                    grad_attn, normed, attention_table, kept, cosine, sine, half_rows
                ),
                [grad_inner, streams[level], gain[2 * level]] + grad_ys[level + 1 :],
                (mix,),
                [piece, piece, row] + ([] if level else [((share, D), jnp.bfloat16)]),
                level > 0,
                7 + LAYERS + level,
                Line([(unit_grads, 0, carried * third)], False),
            )
        )
        layer_grads[3 * level + 1] = summed

    grad_start_all, summed = gather_all(
        grad_branch, 13, Line([(attention_grads, 0, third), (unit_grads, third, third)], False)
    )
    layer_grads[0], layer_grads[2] = summed[:third], summed[third:]
    layer_grads = jnp.concatenate([grads for grads in layer_grads if grads is not None], axis=0)
    grad_start_all = grad_start_all.reshape(-1, D)
    grad_table, table_squares = look_back(span, row_ids, ids_all, grad_start_all, grad_table)
    values = layer_grads.astype(jnp.float32)
    layer_squares = jnp.sum(jnp.where(mine[:blocks][:, None, None], values * values, 0.0))
    keep = jnp.where(
        tensor_part * share + jnp.arange(share) < real_counts[0], 1.0, 0.0
    ).astype(jnp.float32)
    news = finish(
        gain_grads,
        states,
        grad_ys[1:],
        home,
        keep[None],
        table_squares,
        layer_squares.reshape(1, 1),
        count,
        (gains, gains_first, gains_second, mix[None], mix_first[None], mix_second[None]),
        7 + 2 * LAYERS,
    )
    new_gains, new_gains_first, new_gains_second = news[:3]
    new_mix, new_mix_first, new_mix_second = [value[0] for value in news[3:6]]
    loss_sum, clip_norm = news[6][0, 0], news[6][0, 1]
    token_count = count[0, 0]
    new_master, new_first, new_second = update_slots(
        plan, news[7], master, first_moment, second_moment, layer_grads, grad_table
    )
    return (
        new_master,
        new_first,
        new_second,
        new_gains,
        new_gains_first,
        new_gains_second,
        new_mix,
        new_mix_first,
        new_mix_second,
        loss_sum,
        token_count,
        clip_norm,
    )


def solution(mesh):
    return jax.shard_map(
        body,
        mesh=mesh,
        in_specs=(
            P("dp", "seq"),
            P("dp", "seq"),
            P(("dp", "seq")),
            P(),
            P("dp", ("tensor", "seq"), None),
            P("dp", ("tensor", "seq"), None),
            P("dp", ("tensor", "seq"), None),
            P(),
            P(),
            P(),
            P(),
            P(),
            P(),
        ),
        out_specs=(
            P("dp", ("tensor", "seq"), None),
            P("dp", ("tensor", "seq"), None),
            P("dp", ("tensor", "seq"), None),
            P(),
            P(),
            P(),
            P(),
            P(),
            P(),
            P(),
            P(),
            P(),
        ),
        check_vma=False,
    )
```

```python
from functools import partial

import jax
import jax.numpy as jnp
from jax import lax
from jax.experimental import pallas as pl
from jax.experimental.pallas import tpu as pltpu
from jax.sharding import PartitionSpec as P

D = 768
HEADS = 12
HEAD_DIM = 64
FF = 3072
VOCAB = 50304
LAYERS = 2
STEP_COUNT = 10
MIX_WEIGHTS = 5


EPS_NORM = 1e-05
CLIP_NORM = 0.01
BETA_ONE = 0.9
BETA_TWO = 0.95
ADAM_EPS = 1e-08
RATE_MATRIX = 0.04
RATE_SMALL = 0.4
DECAY_MATRIX = 0.1


def contract_last(left, right):
    return lax.dot_general(
        left, right, (((1,), (1,)), ((), ())), preferred_element_type=jnp.float32
    )


def contract_first(left, right):
    return lax.dot_general(
        left, right, (((0,), (0,)), ((), ())), preferred_element_type=jnp.float32
    )


def slot_table(owners):
    ranks = jnp.arange(owners.shape[0])
    same = (owners[None, :] == owners[:, None]) & (ranks[None, :] < ranks[:, None])
    return jnp.sum(jnp.where(same, 1, 0), axis=1).astype(jnp.int32)


def adam_update(weight, first, second, grad, rate, decay):
    first = BETA_ONE * first + (1.0 - BETA_ONE) * grad
    second = BETA_TWO * second + (1.0 - BETA_TWO) * grad * grad
    first_hat = first / (1.0 - BETA_ONE**STEP_COUNT)
    second_hat = second / (1.0 - BETA_TWO**STEP_COUNT)
    weight = weight - rate * (first_hat / (jnp.sqrt(second_hat) + ADAM_EPS) + decay * weight)
    return (weight, first, second)


MESH = pl.DeviceIdType.MESH
ROW_STEP = 400
TILE_GROUPS = 8
LANES = 128
SHORT = pl.CostEstimate(flops=1000, bytes_accessed=1000, transcendentals=0)


def meet(peers):
    gate = pltpu.get_barrier_semaphore()
    for peer in peers:
        pl.semaphore_signal(gate, inc=1, device_id=peer, device_id_type=MESH)
    pl.semaphore_wait(gate, len(peers))


def others(axis):
    count, me = lax.axis_size(axis), lax.axis_index(axis)
    return [lax.rem(me + step, count) for step in range(1, count)]


def behind(axis, step):
    count, me = lax.axis_size(axis), lax.axis_index(axis)
    return lax.rem(me + count - step, count)


def send(source, target, send_sem, recv_sem, device):
    copy = pltpu.make_async_remote_copy(
        src_ref=source,
        dst_ref=target,
        send_sem=send_sem,
        recv_sem=recv_sem,
        device_id=device,
        device_id_type=MESH,
    )
    copy.start()
    return copy


def layer_norm_parts(stream):
    center = stream - jnp.mean(stream, -1, keepdims=True)
    inverse = lax.rsqrt(jnp.mean(center * center, -1, keepdims=True) + EPS_NORM)
    return center * inverse, inverse


def norm_pull(grad_normed, gain, stream):
    scaled, inverse = layer_norm_parts(stream)
    grad_scaled = grad_normed * gain
    grad_stream = inverse * (
        grad_scaled
        - jnp.mean(grad_scaled, -1, keepdims=True)
        - scaled * jnp.mean(grad_scaled * scaled, -1, keepdims=True)
    )
    return grad_stream, jnp.sum(grad_normed * scaled, axis=0, keepdims=True)


class Work:
    def __init__(self, before, during, operands, specs, outs, scratch, after=None, twins=False):
        self.before, self.during, self.after, self.twins = before, during, after, twins
        self.operands, self.specs, self.outs, self.scratch = operands, specs, outs, scratch


def tensor_step(name, function, work, extras, scalars, outs, gather, collective_id, line=None):
    parts = lax.axis_size("tensor")
    share = extras[0].shape[0]
    reduce = work is not None
    work = work or Work(None, None, [], [], [], [])

    def kernel(*refs):
        refs = list(refs)

        def take(count):
            return [refs.pop(0) for _ in range(count)]

        work_refs = take(len(work.operands))
        extra_refs = take(len(extras))
        scalar_refs = take(len(scalars))
        source_refs = take(len(line.operands)) if line else []
        out_refs = take(len(outs))
        (full,) = take(1) if gather else [None]
        work_outs = take(len(work.outs))
        (joined,) = take(1) if line else [None]
        send_sems, recv_sems = take(2)
        partial_ref, outgoing, arrived = take(3) if reduce else [None] * 3
        if line:
            line.bind(source_refs, joined, take(len(line.scratch)))
            line.load()

        def tick(count=1):
            if line:
                line.steps(count)

        me, side = lax.axis_index("tensor"), lax.axis_index("seq")
        peers = others("tensor")
        twin = {"seq": 1 - side}
        twins = work.twins or (line and line.share)
        meet(
            [{"tensor": peer} for peer in peers]
            + [twin] * bool(twins)
            + ([{"dp": peer} for peer in others("dp")] if line else [])
        )
        if line:
            line.begin()
        total = None
        if reduce:
            work.before(work_refs, work_outs, refs, partial_ref, tick)
            copies = []
            for step, peer in enumerate(peers):
                rows = pl.ds(pl.multiple_of(peer * share, share), share)
                outgoing[step] = partial_ref[rows, :].astype(jnp.bfloat16)
                copies.append(
                    send(
                        outgoing.at[step],
                        arrived.at[step],
                        send_sems.at[0, step],
                        recv_sems.at[0, step],
                        {"tensor": peer},
                    )
                )
            if work.during:
                work.during(work_refs, work_outs, refs)
            tick(6)
            total = partial_ref[pl.ds(pl.multiple_of(me * share, share), share), :]
            for step, copy in enumerate(copies):
                copy.wait()
                total = total + arrived[step].astype(jnp.float32)
        results = function(total, *[ref[...] for ref in extra_refs], *scalar_refs)
        for ref, value in zip(out_refs, results):
            ref[...] = value.astype(ref.dtype)
        if gather:
            full[me] = results[len(outs)].astype(jnp.bfloat16)
            copies = [
                send(
                    full.at[me],
                    full.at[me],
                    send_sems.at[1, step],
                    recv_sems.at[1, step],
                    {"tensor": peer},
                )
                for step, peer in enumerate(peers)
            ]
        if work.after:
            work.after(work_refs, work_outs, refs)
        tick(None)
        if gather:
            for copy in copies:
                copy.wait()
        if line:
            line.end()

    vmem = pl.BlockSpec(memory_space=pltpu.VMEM)
    smem = pl.BlockSpec(memory_space=pltpu.SMEM)
    shapes = [jax.ShapeDtypeStruct(shape, dtype) for shape, dtype in outs]
    if gather:
        shapes.append(jax.ShapeDtypeStruct((parts, share, D), jnp.bfloat16))
    shapes += [jax.ShapeDtypeStruct(shape, dtype) for shape, dtype in work.outs]
    out_specs = [vmem] * len(shapes)
    operands = list(work.operands) + list(extras) + list(scalars)
    in_specs = list(work.specs) + [vmem] * len(extras) + [smem] * len(scalars)
    dma = pltpu.SemaphoreType.DMA
    buffers = [dma((2, parts - 1))] * 2
    if reduce:
        buffers += [pltpu.VMEM((parts * share, D), jnp.float32)]
        buffers += [pltpu.VMEM((parts - 1, share, D), jnp.bfloat16)] * 2
    if line:
        operands += line.operands
        in_specs += line.in_specs
        shapes.append(line.out_shape)
        out_specs.append(line.out_spec)
        buffers += line.scratch
    return pl.pallas_call(
        kernel,
        name=name,
        grid=(1,),
        out_shape=shapes,
        in_specs=in_specs,
        out_specs=out_specs,
        scratch_shapes=buffers + list(work.scratch),
        cost_estimate=SHORT,
        compiler_params=pltpu.CompilerParams(
            collective_id=collective_id, has_side_effects=True, vmem_limit_bytes=50 << 20
        ),
    )(*operands)


VMEM_SPEC = pl.BlockSpec(memory_space=pltpu.VMEM)


def part_spec(rows, index):
    return pl.BlockSpec((rows, D), lambda step: (index, 0), pipeline_mode=pl.Buffered(1))


def turn(block, cosine, sine):
    half = HEAD_DIM // 2
    first, second = block[:half], block[half:]
    return jnp.concatenate(
        [first * cosine - second * sine, second * cosine + first * sine], axis=0
    )


def times(left, right):
    return jnp.dot(left, right, preferred_element_type=jnp.float32)


def scores_of(keys_values, head, queries, side):
    span = slice(head * HEAD_DIM, (head + 1) * HEAD_DIM)
    count = queries.shape[1]
    scale = HEAD_DIM ** (-0.5)
    far = contract_first(keys_values[0, 0, span, :], queries) * scale
    own = contract_first(keys_values[1, 0, span, :], queries) * scale
    key = lax.broadcasted_iota(jnp.int32, (count, count), 0)
    query = lax.broadcasted_iota(jnp.int32, (count, count), 1)
    own = jnp.where(key <= query, own, -1e30)
    far = jnp.where(query + side * (2 * count) >= 2 * count, far, -1e30)
    return far, own


def attention_work(normed, table, cosine, sine):
    parts, share, _ = normed.shape
    count = parts * share
    width = D // parts
    heads = width // HEAD_DIM

    def before(ins, outs, scratch, partial_ref, tick):
        normed_ref, qkv_ref, out_ref, cosine_ref, sine_ref = ins
        queries_ref, both, logs_ref, attended_ref = outs
        send_sem, recv_sem = scratch
        side = lax.axis_index("seq")
        cosine, sine = cosine_ref[...], sine_ref[...]
        rows = normed_ref[...].reshape(count, D)
        joined = contract_last(qkv_ref[...], rows)
        for head in range(heads):
            span = slice(head * HEAD_DIM, (head + 1) * HEAD_DIM)
            keys = joined[width + head * HEAD_DIM : width + (head + 1) * HEAD_DIM]
            both[1, 0, span, :] = turn(keys, cosine, sine).astype(jnp.bfloat16)
        both[1, 1] = joined[2 * width :].astype(jnp.bfloat16)
        copy = pltpu.make_async_remote_copy(
            src_ref=both.at[1],
            dst_ref=both.at[0],
            send_sem=send_sem,
            recv_sem=recv_sem,
            device_id={"seq": 1 - side},
            device_id_type=MESH,
        )

        copy.start()
        for head in range(heads):
            span = slice(head * HEAD_DIM, (head + 1) * HEAD_DIM)
            queries_ref[span, :] = turn(joined[span], cosine, sine).astype(jnp.bfloat16)

        copy.wait()
        for head in range(heads):
            span = slice(head * HEAD_DIM, (head + 1) * HEAD_DIM)
            far, own = scores_of(both, head, queries_ref[span, :], side)
            peak = jnp.maximum(
                jnp.max(far, axis=0, keepdims=True), jnp.max(own, axis=0, keepdims=True)
            )
            far, own = jnp.exp(far - peak), jnp.exp(own - peak)
            total = jnp.sum(far, axis=0, keepdims=True) + jnp.sum(own, axis=0, keepdims=True)
            logs_ref[head] = peak + jnp.log(total)
            inverse = 1.0 / total
            attended = times(both[0, 1, span, :], (far * inverse).astype(jnp.bfloat16))
            attended += times(both[1, 1, span, :], (own * inverse).astype(jnp.bfloat16))
            attended_ref[span, :] = attended.astype(jnp.bfloat16)
            tick(2)
        partial_ref[...] = contract_first(attended_ref[...], out_ref[...])

    low = jnp.bfloat16
    return Work(
        before,
        None,
        [normed, table, table, cosine, sine],
        [VMEM_SPEC, part_spec(3 * width, 0), part_spec(width, 3), VMEM_SPEC, VMEM_SPEC],
        [
            ((width, count), low),
            ((2, 2, width, count), low),
            ((heads, 1, count), jnp.float32),
            ((width, count), low),
        ],
        [pltpu.SemaphoreType.DMA, pltpu.SemaphoreType.DMA],
        twins=True,
    )


def fold_copy(own, near, send_sems, recv_sems, index):
    side = lax.axis_index("seq")
    return pltpu.make_async_remote_copy(
        src_ref=own.at[index, :, 1 - side],
        dst_ref=near.at[index],
        send_sem=send_sems.at[index],
        recv_sem=recv_sems.at[index],
        device_id={"seq": 1 - side},
        device_id_type=MESH,
    )


def add_halves(own, near, out, start):
    side = lax.axis_index("seq")

    def one(block, carry):
        value = own[block, side].astype(jnp.float32) + near[block].astype(jnp.float32)
        out[start + block] = value.astype(jnp.bfloat16)
        return carry

    lax.fori_loop(0, near.shape[0], one, 0)


def attention_back_work(grad, normed, table, kept, cosine, sine, half_rows):
    parts, share, _ = normed.shape
    count = parts * share
    width = D // parts
    heads = width // HEAD_DIM
    queries, both, logs, attended = kept
    blocks = 4 * width // (2 * half_rows)

    def before(ins, outs, scratch, partial_ref, tick):
        grad_ref, _, qkv_ref, out_ref, queries_ref, both, logs_ref, _, cosine_ref, sine_ref = ins
        back, came, grad_joined, send_sem, recv_sem = scratch[:5]
        side = lax.axis_index("seq")
        cosine, sine = cosine_ref[...], -sine_ref[...]
        scale = HEAD_DIM ** (-0.5)
        grads = contract_last(out_ref[...], grad_ref[...].reshape(count, D)).astype(jnp.bfloat16)
        own_grads = []
        for head in range(heads):
            span = slice(head * HEAD_DIM, (head + 1) * HEAD_DIM)
            head_queries, head_grads = queries_ref[span, :], grads[span]
            far, own = scores_of(both, head, head_queries, side)
            far, own = jnp.exp(far - logs_ref[head]), jnp.exp(own - logs_ref[head])
            far_grad = contract_first(both[0, 1, span, :], head_grads)
            own_grad = contract_first(both[1, 1, span, :], head_grads)
            mean = jnp.sum(far * far_grad, axis=0, keepdims=True)
            mean += jnp.sum(own * own_grad, axis=0, keepdims=True)
            far_grad = (far * (far_grad - mean)).astype(jnp.bfloat16)
            own_grad = (own * (own_grad - mean)).astype(jnp.bfloat16)
            far, own = far.astype(jnp.bfloat16), own.astype(jnp.bfloat16)
            back[0, span, :] = (contract_last(head_queries, far_grad) * scale).astype(jnp.bfloat16)
            back[1, span, :] = contract_last(head_grads, far).astype(jnp.bfloat16)
            query_grad = times(both[0, 0, span, :], far_grad) + times(both[1, 0, span, :], own_grad)
            grad_joined[span, :] = turn(query_grad * scale, cosine, sine).astype(jnp.bfloat16)
            own_grads.append(
                (contract_last(head_queries, own_grad) * scale, contract_last(head_grads, own))
            )
            tick(2)
        copy = send(back, came, send_sem, recv_sem, {"seq": 1 - side})
        copy.wait()
        for head, (key_grad, value_grad) in enumerate(own_grads):
            span = slice(head * HEAD_DIM, (head + 1) * HEAD_DIM)
            key_grad = key_grad + came[0, span, :].astype(jnp.float32)
            value_grad = value_grad + came[1, span, :].astype(jnp.float32)
            start = width + head * HEAD_DIM
            grad_joined[start : start + HEAD_DIM, :] = turn(key_grad, cosine, sine).astype(
                jnp.bfloat16
            )
            start += width
            grad_joined[start : start + HEAD_DIM, :] = value_grad.astype(jnp.bfloat16)
        partial_ref[...] = contract_first(grad_joined[...], qkv_ref[...])

    def during(ins, outs, scratch):
        grad_ref, normed_ref, attended_ref = ins[0], ins[1], ins[7]
        grad_joined = scratch[2]
        own, near, fold_send, fold_recv = scratch[5:]
        value = times(grad_joined[...], normed_ref[...].reshape(count, D)).astype(jnp.bfloat16)
        part = 3 * blocks // 4
        own[0, :part] = value.reshape(part, 2, half_rows, D)
        value = times(attended_ref[...], grad_ref[...].reshape(count, D)).astype(jnp.bfloat16)
        own[0, part:] = value.reshape(blocks - part, 2, half_rows, D)
        fold_copy(own, near, fold_send, fold_recv, 0).start()

    def after(ins, outs, scratch):
        own, near, fold_send, fold_recv = scratch[5:]
        fold_copy(own, near, fold_send, fold_recv, 0).wait()
        add_halves(own.at[0], near.at[0], outs[0], 0)

    low = jnp.bfloat16
    dma = pltpu.SemaphoreType.DMA
    return Work(
        before,
        during,
        [grad, normed, table, table, queries, both, logs, attended, cosine, sine],
        [VMEM_SPEC, VMEM_SPEC, part_spec(3 * width, 0), part_spec(width, 3)] + [VMEM_SPEC] * 6,
        [((blocks, half_rows, D), low)],
        [
            pltpu.VMEM((2, width, count), low),
            pltpu.VMEM((2, width, count), low),
            pltpu.VMEM((3 * width, count), low),
            dma,
            dma,
            pltpu.VMEM((1, blocks, 2, half_rows, D), low),
            pltpu.VMEM((1, blocks, half_rows, D), low),
            dma((1,)),
            dma((1,)),
        ],
        after,
        True,
    )


def gelu(hidden):
    return jax.nn.gelu(hidden, approximate=True)


def unit_work(normed, up, down):
    parts, share, _ = normed.shape
    count = parts * share
    units = FF // parts

    def before(ins, outs, scratch, partial_ref, tick):
        normed_ref, up_ref, down_ref = ins
        hidden_ref, activated_ref = outs
        hidden = contract_last(up_ref[...], normed_ref[...].reshape(count, D))
        hidden_ref[...] = hidden
        activated_ref[...] = gelu(hidden).astype(jnp.bfloat16)
        tick(2)
        partial_ref[...] = contract_first(activated_ref[...], down_ref[...])

    return Work(
        before,
        None,
        [normed, up[0], down[0]],
        [VMEM_SPEC, part_spec(units, up[1]), part_spec(units, down[1])],
        [((units, count), jnp.float32), ((units, count), jnp.bfloat16)],
        [],
    )


def unit_back_work(grad, normed, up, down, kept, half_rows):
    parts, share, _ = normed.shape
    count = parts * share
    units = FF // parts
    hidden, activated = kept
    blocks = units // (2 * half_rows)

    def before(ins, outs, scratch, partial_ref, tick):
        grad_ref, _, up_ref, down_ref, hidden_ref, _ = ins
        grad_hidden = scratch[0]
        grad_act = contract_last(down_ref[...], grad_ref[...].reshape(count, D))
        _, pull = jax.vjp(gelu, hidden_ref[...])
        grad_hidden[...] = pull(grad_act)[0].astype(jnp.bfloat16)
        tick(2)
        partial_ref[...] = contract_first(grad_hidden[...], up_ref[...])

    def during(ins, outs, scratch):
        grad_ref, normed_ref, _, _, _, activated_ref = ins
        grad_hidden, own, near, fold_send, fold_recv = scratch
        value = times(grad_hidden[...], normed_ref[...].reshape(count, D))
        own[0] = value.astype(jnp.bfloat16).reshape(own.shape[1:])
        fold_copy(own, near, fold_send, fold_recv, 0).start()
        value = times(activated_ref[...], grad_ref[...].reshape(count, D))
        own[1] = value.astype(jnp.bfloat16).reshape(own.shape[1:])
        fold_copy(own, near, fold_send, fold_recv, 1).start()

    def after(ins, outs, scratch):
        _, own, near, fold_send, fold_recv = scratch
        for index in range(2):
            fold_copy(own, near, fold_send, fold_recv, index).wait()
            add_halves(own.at[index], near.at[index], outs[0], index * blocks)

    low, dma = jnp.bfloat16, pltpu.SemaphoreType.DMA
    return Work(
        before,
        during,
        [grad, normed, up[0], down[0], hidden, activated],
        [VMEM_SPEC, VMEM_SPEC, part_spec(units, up[1]), part_spec(units, down[1])]
        + [VMEM_SPEC] * 2,
        [((2 * blocks, half_rows, D), low)],
        [
            pltpu.VMEM((units, count), low),
            pltpu.VMEM((2, blocks, 2, half_rows, D), low),
            pltpu.VMEM((2, blocks, half_rows, D), low),
            dma((2,)),
            dma((2,)),
        ],
        after,
        True,
    )


LINE_BLOCKS = 1
LINE_LAG = 3


class Line:
    def __init__(self, sources, share):
        self.groups = lax.axis_size("dp")
        self.sources, self.share = sources, share
        count = sum(size for _, _, size in sources)
        _, half_rows, _ = sources[0][0].shape
        self.half = (count, half_rows, D)
        self.chunks = count // LINE_BLOCKS
        self.operands = [array for array, _, _ in sources]
        self.in_specs = [pl.BlockSpec(memory_space=pl.ANY)] * len(sources)
        dma = pltpu.SemaphoreType.DMA
        out = (count, 2, half_rows, D) if share else self.half
        self.out_shape = jax.ShapeDtypeStruct(out, jnp.bfloat16)
        self.out_spec = pl.BlockSpec(memory_space=pl.ANY if share else pltpu.VMEM)
        self.scratch = [
            pltpu.VMEM(self.half, jnp.bfloat16),
            pltpu.VMEM((2,) + self.half, jnp.bfloat16),
            pltpu.VMEM((2,) + self.half, jnp.bfloat16),
            dma((len(sources),)),
            dma((2, self.chunks)),
            dma((2, self.chunks)),
        ]
        if share:
            self.scratch += [pltpu.VMEM(self.half, jnp.bfloat16)] + [dma((self.chunks,))] * 3

    def bind(self, source_refs, out_ref, refs):
        self.source_refs, self.out = source_refs, out_ref
        self.own, self.came, self.going, self.own_sems, self.send_sems, self.recv_sems = refs[:6]
        self.total = out_ref
        if self.share:
            self.total, self.keep_sems, self.twin_send, self.twin_recv = refs[6:]
        self.done = 0
        self.group = lax.axis_index("dp")
        self.first = jnp.where(self.group < self.groups // 2, 0, 1)

    def at(self, chunk):
        return pl.ds(chunk * LINE_BLOCKS, LINE_BLOCKS)

    def comes(self, way):
        return jnp.where(way == 0, self.group > 0, self.group < self.groups - 1)

    def goes(self, way):
        return jnp.where(way == 0, self.group < self.groups - 1, self.group > 0)

    def copy(self, source, way, chunk):
        target = jnp.where(way == 0, self.group + 1, self.group - 1)
        return pltpu.make_async_remote_copy(
            src_ref=source,
            dst_ref=self.came.at[way, self.at(chunk)],
            send_sem=self.send_sems.at[way, chunk],
            recv_sem=self.recv_sems.at[way, chunk],
            device_id={"dp": target},
            device_id_type=MESH,
        )

    def load(self):
        self.loads, place = [], 0
        for index, (ref, (_, start, size)) in enumerate(zip(self.source_refs, self.sources)):
            copy = pltpu.make_async_copy(
                ref.at[pl.ds(start, size)], self.own.at[pl.ds(place, size)], self.own_sems.at[index]
            )
            copy.start()
            self.loads.append(copy)
            place += size

    def begin(self):
        for copy in self.loads:
            copy.wait()
        for way in range(2):

            @pl.when(jnp.logical_not(self.comes(way)))
            def _():
                self.came[way] = jnp.zeros(self.half, jnp.bfloat16)

                def start(chunk, carry):
                    self.copy(self.own.at[self.at(chunk)], way, chunk).start()
                    return carry

                lax.fori_loop(0, self.chunks, start, 0)

    def twin_copy(self, chunk):
        side = lax.axis_index("seq")
        return pltpu.make_async_remote_copy(
            src_ref=self.total.at[self.at(chunk)],
            dst_ref=self.out.at[self.at(chunk), side],
            send_sem=self.twin_send.at[chunk],
            recv_sem=self.twin_recv.at[chunk],
            device_id={"seq": 1 - side},
            device_id_type=MESH,
        )

    def keep_copy(self, chunk):
        return pltpu.make_async_copy(
            self.total.at[self.at(chunk)],
            self.out.at[self.at(chunk), lax.axis_index("seq")],
            self.keep_sems.at[chunk],
        )

    def pass_on(self, way, chunk):
        rows = self.at(chunk)

        @pl.when(self.comes(way))
        def _():
            copy = self.copy(self.going.at[way, rows], way, chunk)
            copy.wait_recv()

            @pl.when(self.goes(way))
            def _():
                value = self.own[rows].astype(jnp.float32) + self.came[way, rows].astype(jnp.float32)
                self.going[way, rows] = value.astype(jnp.bfloat16)
                copy.start()

    def step(self, index):
        @pl.when(index < self.chunks)
        def _():
            self.pass_on(self.first, index)

        @pl.when(index >= LINE_LAG)
        def _():
            chunk = index - LINE_LAG
            rows = self.at(chunk)
            self.pass_on(1 - self.first, chunk)
            value = self.own[rows].astype(jnp.float32)
            value = value + self.came[0, rows].astype(jnp.float32)
            value = value + self.came[1, rows].astype(jnp.float32)
            self.total[rows] = value.astype(jnp.bfloat16)
            if self.share:
                self.keep_copy(chunk).start()
                self.twin_copy(chunk).start()

    def steps(self, count=None):
        last = self.chunks + LINE_LAG
        stop = last if count is None else min(self.done + count, last)

        def one(index, carry):
            self.step(index)
            return carry

        lax.fori_loop(self.done, stop, one, 0)
        self.done = stop

    def end(self):
        def one(chunk, carry):
            for way in range(2):

                @pl.when(self.goes(way))
                def _():
                    self.copy(self.going.at[way, self.at(chunk)], way, chunk).wait_send()

            if self.share:
                self.keep_copy(chunk).wait()
                self.twin_copy(chunk).wait()
            return carry

        lax.fori_loop(0, self.chunks, one, 0)


def reduce_all(terms, collective_id, line=None):
    _, tensors, groups, count, _ = terms.shape
    half = count // 2

    def kernel(*refs):
        refs = list(refs)
        terms_ref = refs.pop(0)
        source_refs = [refs.pop(0) for _ in line.operands] if line else []
        out_ref = refs.pop(0)
        joined_ref = refs.pop(0) if line else None
        (
            near, own, mid, sums, mid_in, far, far_in,
            own_sems, near_send, near_recv, mid_send, mid_recv, far_send, far_recv,
        ) = refs[:14]
        if line:
            line.bind(source_refs, joined_ref, refs[14:])
            line.load()
        group, part, side = lax.axis_index("dp"), lax.axis_index("tensor"), lax.axis_index("seq")
        twin = 1 - side
        parts = others("tensor")
        order = others("dp") + [group]
        meet(
            [{"seq": twin}]
            + [{"tensor": peer} for peer in parts]
            + [{"dp": peer} for peer in order[:-1]]
        )
        waits, near_copies, own_copies = [], [], []
        for place, target in enumerate(order):
            near_copies.append(
                send(
                    terms_ref.at[twin, :, target],
                    near.at[place],
                    near_send.at[place],
                    near_recv.at[place],
                    {"seq": twin},
                )
            )
            copy = pltpu.make_async_copy(
                terms_ref.at[side, :, target], own.at[place], own_sems.at[place]
            )
            copy.start()
            own_copies.append(copy)
        if line:
            line.begin()
        beside = lax.rem(part + 1, 2) + part - lax.rem(part, 2)
        across = lax.rem(part + 2, 4)
        corner = 3 - part
        upper, lower = pl.ds(0, half), pl.ds(half, half)
        first_copies, second_copies = [], []

        def hand(place, index, source, target):
            return send(
                source,
                mid_in.at[place, index],
                mid_send.at[place, index],
                mid_recv.at[place, index],
                {"tensor": target},
            )

        for place in range(groups):
            near_copies[place].wait_recv()
            own_copies[place].wait()
            for slot in range(tensors):
                mid[place, slot] = (
                    own[place, slot].astype(jnp.float32) + near[place, slot].astype(jnp.float32)
                ).astype(jnp.bfloat16)
            first_copies.append(
                [
                    hand(place, 0, mid.at[place, corner, upper], beside),
                    hand(place, 1, mid.at[place, corner, lower], across),
                    hand(place, 2, mid.at[place, beside, upper], beside),
                    hand(place, 3, mid.at[place, across, lower], across),
                ]
            )
        for place in range(groups):
            if line and 0 < place < 4:
                line.steps(2)
            copies = []
            for index, slot, rows, target in ((0, across, upper, across), (1, beside, lower, beside)):
                first_copies[place][index].wait_recv()
                value = mid[place, slot, rows].astype(jnp.float32)
                value = value + mid_in[place, index].astype(jnp.float32)
                sums[place, index] = value.astype(jnp.bfloat16)
                copies.append(hand(place, 4 + index, sums.at[place, index], target))
            second_copies.append(copies)
        far_copies = []
        for place, target in enumerate(order):
            if line and place < 4:
                line.steps(2)
            copies = first_copies[place][2:] + second_copies[place]
            for copy in copies:
                copy.wait_recv()

            def joined(index):
                return mid_in[place, index].astype(jnp.float32)

            halves = [joined(2) + joined(4), joined(3) + joined(5)]
            total = mid[place, part].astype(jnp.float32) + jnp.concatenate(halves, axis=0)
            if place < groups - 1:
                far[place] = total.astype(jnp.bfloat16)
                far_copies.append(
                    send(
                        far.at[place],
                        far_in.at[place],
                        far_send.at[place],
                        far_recv.at[place],
                        {"dp": target},
                    )
                )
        if line:
            line.steps()
        for place, copy in enumerate(far_copies):
            copy.wait_recv()
            total = total + far_in[place].astype(jnp.float32)
        out_ref[...] = total
        for copy in near_copies + far_copies + [
            copy for row in first_copies + second_copies for copy in row
        ]:
            copy.wait_send()
        if line:
            line.end()

    block = (count, D)
    dma = pltpu.SemaphoreType.DMA
    return pl.pallas_call(
        kernel,
        name="reduce_all",
        out_shape=[jax.ShapeDtypeStruct(block, jnp.float32)] + ([line.out_shape] if line else []),
        in_specs=[pl.BlockSpec(memory_space=pl.ANY)] + (line.in_specs if line else []),
        out_specs=[pl.BlockSpec(memory_space=pltpu.VMEM)] + ([line.out_spec] if line else []),
        scratch_shapes=[pltpu.VMEM((groups, tensors) + block, jnp.bfloat16)] * 3
        + [
            pltpu.VMEM((groups, 2, half, D), jnp.bfloat16),
            pltpu.VMEM((groups, 6, half, D), jnp.bfloat16),
            pltpu.VMEM((groups,) + block, jnp.bfloat16),
            pltpu.VMEM((groups,) + block, jnp.bfloat16),
            dma((groups,)),
            dma((groups,)),
            dma((groups,)),
            dma((groups, 6)),
            dma((groups, 6)),
            dma((groups,)),
            dma((groups,)),
        ]
        + (line.scratch if line else []),
        cost_estimate=SHORT,
        compiler_params=pltpu.CompilerParams(
            collective_id=collective_id, has_side_effects=True, vmem_limit_bytes=56 << 20
        ),
    )(terms, *(line.operands if line else []))


def gather_all(block, collective_id, line=None):
    tensors, groups = lax.axis_size("tensor"), lax.axis_size("dp")
    half = block.shape[0] // 2

    def kernel(*refs):
        refs = list(refs)
        block_ref = refs.pop(0)
        source_refs = [refs.pop(0) for _ in line.operands] if line else []
        out = refs.pop(0)
        summed_ref = refs.pop(0) if line else None
        own_sem, far_send, far_recv, mid_send, mid_recv, near_send, near_recv = refs[:7]
        if line:
            line.bind(source_refs, summed_ref, refs[7:])
            line.load()
        group, part, side = lax.axis_index("dp"), lax.axis_index("tensor"), lax.axis_index("seq")
        twin = 1 - side
        meet(
            [{"seq": twin}]
            + [{"tensor": peer} for peer in others("tensor")]
            + [{"dp": peer} for peer in others("dp")]
        )
        far_copies = [
            send(
                block_ref,
                out.at[side, part, group],
                far_send.at[step],
                far_recv.at[step],
                {"dp": peer},
            )
            for step, peer in enumerate(others("dp"))
        ]
        own = pltpu.make_async_copy(block_ref, out.at[side, part, group], own_sem)
        own.start()
        if line:
            line.begin()
        beside = lax.rem(part + 1, 2) + part - lax.rem(part, 2)
        across = lax.rem(part + 2, 4)
        corner = 3 - part
        upper, lower = pl.ds(0, half), pl.ds(half, half)
        first_copies, second_copies, near_copies = [], [], []
        for place in range(groups):
            source = behind("dp", place)
            if place:
                far_copies[place - 1].wait_recv()
            held = out.at[side, part, source] if place else block_ref

            def hand(index, piece, slot, rows, target):
                return send(
                    piece,
                    out.at[side, slot, source, rows],
                    mid_send.at[place, index],
                    mid_recv.at[place, index],
                    {"tensor": target},
                )

            first = [
                hand(0, held.at[upper], part, upper, beside),
                hand(1, held.at[lower], part, lower, across),
                hand(2, held.at[lower], part, lower, beside),
                hand(3, held.at[upper], part, upper, across),
            ]
            near_copies.append(
                send(
                    held,
                    out.at[side, part, source],
                    near_send.at[place, 0],
                    near_recv.at[place, 0],
                    {"seq": twin},
                )
            )
            first[0].wait_recv()
            second = [hand(4, out.at[side, beside, source, upper], beside, upper, across)]
            first[1].wait_recv()
            second.append(hand(5, out.at[side, across, source, lower], across, lower, beside))
            first_copies.append(first)
            second_copies.append(second)
        for place in range(groups):
            if line and place < 4:
                line.steps(2)
            source = behind("dp", place)
            ready = [
                (beside, first_copies[place][2:3]),
                (across, first_copies[place][3:4]),
                (corner, second_copies[place]),
            ]
            for step, (slot, copies) in enumerate(ready):
                for copy in copies:
                    copy.wait_recv()
                held = out.at[side, slot, source]
                near_copies.append(
                    send(
                        held,
                        held,
                        near_send.at[place, step + 1],
                        near_recv.at[place, step + 1],
                        {"seq": twin},
                    )
                )
        if line:
            line.steps()
        for copy in near_copies:
            copy.wait_recv()
        for copy in near_copies + far_copies + [
            copy for row in first_copies + second_copies for copy in row
        ]:
            copy.wait_send()
        own.wait()
        if line:
            line.end()

    dma = pltpu.SemaphoreType.DMA
    anywhere = pl.BlockSpec(memory_space=pl.ANY)
    return pl.pallas_call(
        kernel,
        name="gather_all",
        out_shape=[jax.ShapeDtypeStruct((2, tensors, groups) + block.shape, block.dtype)]
        + ([line.out_shape] if line else []),
        in_specs=[VMEM_SPEC] + (line.in_specs if line else []),
        out_specs=[pl.BlockSpec(memory_space=pltpu.HBM)] + ([line.out_spec] if line else []),
        scratch_shapes=[
            dma,
            dma((groups - 1,)),
            dma((groups - 1,)),
            dma((groups, 6)),
            dma((groups, 6)),
            dma((groups, tensors)),
            dma((groups, tensors)),
        ]
        + (line.scratch if line else []),
        cost_estimate=SHORT,
        compiler_params=pltpu.CompilerParams(
            collective_id=collective_id, has_side_effects=True, vmem_limit_bytes=40 << 20
        ),
    )(block, *(line.operands if line else []))


def reduce_rows(terms, ids, line=None):
    count, groups = terms.shape[3], terms.shape[2]
    pieces = max(1, groups // 4)
    part = count // pieces
    sums, joined = [], None
    for i in range(pieces):
        piece = terms[:, :, :, i * part : (i + 1) * part] if pieces > 1 else terms
        if i == 0 and line:
            total, joined = reduce_all(piece, ids[1], line)
        else:
            (total,) = reduce_all(piece, ids[0])
        sums.append(total)
    return jnp.concatenate(sums, axis=0) if pieces > 1 else sums[0], joined


def join_stats(stats, collective_id):
    _, tensors, groups, _, _ = stats.shape

    def join(left, right):
        top = jnp.maximum(left[..., 0:1, :], right[..., 0:1, :])
        total = left[..., 1:2, :] * jnp.exp(left[..., 0:1, :] - top) + right[..., 1:2, :] * jnp.exp(
            right[..., 0:1, :] - top
        )
        return jnp.concatenate(
            [top, total, left[..., 2:3, :] + right[..., 2:3, :], left[..., 3:, :]], axis=-2
        )

    def kernel(
        stats_ref, home, full, near, mid, mid_in, far, far_in,
        near_send, near_recv, mid_send, mid_recv, far_send, far_recv,
    ):
        group, part, side = lax.axis_index("dp"), lax.axis_index("tensor"), lax.axis_index("seq")
        twin = 1 - side
        parts, groups_else = others("tensor"), others("dp")
        meet(
            [{"seq": twin}]
            + [{"tensor": peer} for peer in parts]
            + [{"dp": peer} for peer in groups_else]
        )
        copy = send(stats_ref.at[twin], near, near_send.at[0], near_recv.at[0], {"seq": twin})
        copy.wait()
        for slot in range(tensors):
            for spot in range(groups):
                mid[slot, spot] = join(stats_ref[side, slot, spot], near[slot, spot])
        copies = [
            send(mid.at[peer], mid_in.at[step], mid_send.at[0, step], mid_recv.at[0, step], {"tensor": peer})
            for step, peer in enumerate(parts)
        ]
        for copy in copies:
            copy.wait()
        for spot in range(groups):
            total = mid[part, spot]
            for step in range(tensors - 1):
                total = join(total, mid_in[step, spot])
            far[spot] = total
        copies = [
            send(far.at[peer], far_in.at[step], far_send.at[0, step], far_recv.at[0, step], {"dp": peer})
            for step, peer in enumerate(groups_else)
        ]
        total = far[group]
        for step, copy in enumerate(copies):
            copy.wait()
            total = join(total, far_in[step])
        log_total = total[0:1] + jnp.log(total[1:2])
        home[...] = jnp.concatenate([log_total, total[2:3], total[2:]], axis=0)
        full[side, part, group] = jnp.broadcast_to(log_total, (8, LANES))
        held = full.at[side, part, group]
        copies = [
            send(held, held, far_send.at[1, step], far_recv.at[1, step], {"dp": peer})
            for step, peer in enumerate(groups_else)
        ]
        for copy in copies:
            copy.wait()
        held = full.at[side, part]
        copies = [
            send(held, held, mid_send.at[1, step], mid_recv.at[1, step], {"tensor": peer})
            for step, peer in enumerate(parts)
        ]
        for copy in copies:
            copy.wait()
        held = full.at[side]
        send(held, held, near_send.at[1], near_recv.at[1], {"seq": twin}).wait()

    tile = (8, LANES)
    dma = pltpu.SemaphoreType.DMA
    vmem = pl.BlockSpec(memory_space=pltpu.VMEM)
    return pl.pallas_call(
        kernel,
        name="join_stats",
        out_shape=[
            jax.ShapeDtypeStruct(tile, jnp.float32),
            jax.ShapeDtypeStruct(stats.shape, jnp.float32),
        ],
        in_specs=[vmem],
        out_specs=[vmem, vmem],
        scratch_shapes=[
            pltpu.VMEM((tensors, groups) + tile, jnp.float32),
            pltpu.VMEM((tensors, groups) + tile, jnp.float32),
            pltpu.VMEM((tensors - 1, groups) + tile, jnp.float32),
            pltpu.VMEM((groups,) + tile, jnp.float32),
            pltpu.VMEM((groups - 1,) + tile, jnp.float32),
            dma((2,)),
            dma((2,)),
            dma((2, tensors - 1)),
            dma((2, tensors - 1)),
            dma((2, groups - 1)),
            dma((2, groups - 1)),
        ],
        cost_estimate=SHORT,
        compiler_params=pltpu.CompilerParams(collective_id=collective_id, has_side_effects=True),
    )(stats)


def spread_tokens(block, collective_id):
    tensors, groups = lax.axis_size("tensor"), lax.axis_size("dp")
    rows = 2 * tensors * groups

    def kernel(block_ref, ids, targets, kept, count, held, own_sem, send_sems, recv_sems):
        group, side = lax.axis_index("dp"), lax.axis_index("seq")
        peers = [
            {"dp": lax.rem(group + step // 2, groups), "seq": lax.rem(side + step % 2, 2)}
            for step in range(1, 2 * groups)
        ]
        meet(peers)
        copies = [
            send(block_ref, held.at[group, side], send_sems.at[step], recv_sems.at[step], peer)
            for step, peer in enumerate(peers)
        ]
        own = pltpu.make_async_copy(block_ref, held.at[group, side], own_sem)
        own.start()
        own.wait()
        for copy in copies:
            copy.wait()
        lane = lax.broadcasted_iota(jnp.int32, (1, LANES), 1)
        total = jnp.zeros((1, LANES), jnp.int32)
        for half in range(2):
            for source in range(groups):
                limit = held[source, half, 2 * tensors : 2 * tensors + 1, :]
                total = total + limit
                for part in range(tensors):
                    row = (half * tensors + part) * groups + source
                    tile, place = row // TILE_GROUPS, slice(row % TILE_GROUPS, row % TILE_GROUPS + 1)
                    ids[tile, place, :] = held[source, half, part : part + 1, :]
                    targets[tile, place, :] = held[source, half, tensors + part : tensors + part + 1, :]
                    kept[tile, place, :] = jnp.where(lane + part * LANES < limit, 1.0, 0.0)
        count[...] = total.astype(jnp.float32)

    dma = pltpu.SemaphoreType.DMA
    vmem = pl.BlockSpec(memory_space=pltpu.VMEM)
    shape = (rows // TILE_GROUPS, TILE_GROUPS, LANES)
    return pl.pallas_call(
        kernel,
        name="spread_tokens",
        out_shape=[
            jax.ShapeDtypeStruct(shape, jnp.int32),
            jax.ShapeDtypeStruct(shape, jnp.int32),
            jax.ShapeDtypeStruct(shape, jnp.float32),
            jax.ShapeDtypeStruct((1, LANES), jnp.float32),
        ],
        in_specs=[vmem],
        out_specs=[vmem] * 4,
        scratch_shapes=[
            pltpu.VMEM((groups, 2) + block.shape, jnp.int32),
            dma,
            dma((2 * groups - 1,)),
            dma((2 * groups - 1,)),
        ],
        cost_estimate=SHORT,
        compiler_params=pltpu.CompilerParams(collective_id=collective_id, has_side_effects=True),
    )(block)


def finish(gain_grads, states, grad_ys, home, keep, table_squares, layer_squares, count, smalls, collective_id):
    tensors, groups = lax.axis_size("tensor"), lax.axis_size("dp")
    block = (8, D)
    gain_rows = 2 * LAYERS + 1
    operands = list(gain_grads) + list(states) + list(grad_ys) + [
        home, keep, table_squares, layer_squares, count
    ] + list(smalls)

    def kernel(*refs):
        refs = list(refs)
        gain_refs = [refs.pop(0) for _ in gain_grads]
        state_refs = [refs.pop(0) for _ in states]
        grad_refs = [refs.pop(0) for _ in grad_ys]
        home_ref, keep_ref, table_ref, layer_ref, count_ref = [refs.pop(0) for _ in range(5)]
        small_refs = [refs.pop(0) for _ in smalls]
        out_refs = [refs.pop(0) for _ in range(8)]
        near, mid, far, near_send, near_recv, mid_send, mid_recv, far_send, far_recv = refs
        group, part, side = lax.axis_index("dp"), lax.axis_index("tensor"), lax.axis_index("seq")
        parts, groups_else = others("tensor"), others("dp")
        meet(
            [{"seq": 1 - side}]
            + [{"tensor": peer} for peer in parts]
            + [{"dp": peer} for peer in groups_else]
        )
        values = []
        for later in range(1, LAYERS + 1):
            grad = grad_refs[later - 1][...]
            for level in range(later + 1):
                values.append(jnp.sum(grad * state_refs[level][...], keepdims=True))
        loss = (home_ref[0:1, :] - home_ref[1:2, :]) * keep_ref[...]
        values.append(jnp.sum(loss, keepdims=True))
        values.append(jnp.sum(table_ref[...], keepdims=True) + layer_ref[...])
        lane = lax.broadcasted_iota(jnp.int32, (1, D), 1)
        row = jnp.zeros((1, D), jnp.float32)
        for place, value in enumerate(values):
            row = jnp.where(lane == place, value, row)
        blank = jnp.zeros((8 - gain_rows - 1, D), jnp.float32)
        total = jnp.concatenate([ref[...] for ref in gain_refs] + [row, blank], axis=0)
        stages = [
            ("seq", near, side, [1 - side], near_send, near_recv),
            ("tensor", mid, part, parts, mid_send, mid_recv),
            ("dp", far, group, groups_else, far_send, far_recv),
        ]
        for axis, slots, me, peers, send_sems, recv_sems in stages:
            slots[me] = total
            copies = [
                send(slots.at[me], slots.at[me], send_sems.at[step], recv_sems.at[step], {axis: peer})
                for step, peer in enumerate(peers)
            ]
            for copy in copies:
                copy.wait()
            total = slots[0]
            for index in range(1, slots.shape[0]):
                total = total + slots[index]
        gain_total = total[:gain_rows]
        row = total[gain_rows : gain_rows + 1]

        def pick(place):
            return jnp.sum(jnp.where(lane == place, row, 0.0), axis=1, keepdims=True)

        mix_squares = jnp.sum(jnp.where(lane < MIX_WEIGHTS, row * row, 0.0), axis=1, keepdims=True)
        gain_squares = jnp.sum(gain_total * gain_total, keepdims=True)
        tokens = count_ref[:, 0:1]
        clip_norm = jnp.sqrt(pick(MIX_WEIGHTS + 1) + gain_squares + mix_squares) / tokens
        factor = jnp.minimum(1.0, CLIP_NORM / clip_norm) / tokens
        gain_news = adam_update(
            *[ref[...] for ref in small_refs[:3]], gain_total * factor, RATE_SMALL, 0.0
        )
        mix_news = adam_update(
            *[ref[...] for ref in small_refs[3:]], row[:, :MIX_WEIGHTS] * factor, RATE_SMALL, 0.0
        )
        for ref, value in zip(out_refs[:6], gain_news + mix_news):
            ref[...] = value
        ends = jnp.where(lane == 0, pick(MIX_WEIGHTS), jnp.where(lane == 1, clip_norm, factor))
        out_refs[6][...] = ends[:, :LANES]
        out_refs[7][...] = jnp.broadcast_to(factor, (8, LANES))

    dma = pltpu.SemaphoreType.DMA
    vmem = pl.BlockSpec(memory_space=pltpu.VMEM)
    return pl.pallas_call(
        kernel,
        name="finish",
        out_shape=[jax.ShapeDtypeStruct(value.shape, jnp.float32) for value in smalls]
        + [
            jax.ShapeDtypeStruct((1, LANES), jnp.float32),
            jax.ShapeDtypeStruct((8, LANES), jnp.float32),
        ],
        in_specs=[vmem] * len(operands),
        out_specs=[vmem] * 8,
        scratch_shapes=[
            pltpu.VMEM((2,) + block, jnp.float32),
            pltpu.VMEM((tensors,) + block, jnp.float32),
            pltpu.VMEM((groups,) + block, jnp.float32),
            dma((1,)),
            dma((1,)),
            dma((tensors - 1,)),
            dma((tensors - 1,)),
            dma((groups - 1,)),
            dma((groups - 1,)),
        ],
        cost_estimate=SHORT,
        compiler_params=pltpu.CompilerParams(collective_id=collective_id, has_side_effects=True),
    )(*operands)


SLOT_STEP = 4


def update_slots(plan, factor, master, first, second, layer_grads, grad_table):
    slots, half_rows, _ = master.shape
    steps = -(-slots // SLOT_STEP)
    plan = jnp.pad(plan, ((0, 0), (0, steps * SLOT_STEP - slots)))

    def kernel(plan_ref, factor_ref, master_ref, first_ref, second_ref, *rest):
        layer_refs = rest[:SLOT_STEP]
        table_ref, new_master, new_first, new_second = rest[SLOT_STEP:]
        for place in range(SLOT_STEP):
            kind = plan_ref[0, pl.program_id(0) * SLOT_STEP + place]
            grad = table_ref[place * half_rows : (place + 1) * half_rows, :]
            grad = jnp.where(kind == 0, layer_refs[place][0].astype(jnp.float32), grad)
            grad = jnp.where(kind >= 0, grad * factor_ref[0:1, 0:1], 0.0)
            values = adam_update(
                master_ref[place],
                first_ref[place],
                second_ref[place],
                grad,
                RATE_MATRIX,
                DECAY_MATRIX,
            )
            for ref, value in zip((new_master, new_first, new_second), values):
                ref[place] = value

    slot = pl.BlockSpec((SLOT_STEP, half_rows, D), lambda step, plan: (step, 0, 0))
    return pl.pallas_call(
        kernel,
        name="update_slots",
        grid_spec=pltpu.PrefetchScalarGridSpec(
            num_scalar_prefetch=1,
            grid=(steps,),
            in_specs=[pl.BlockSpec((8, LANES), lambda step, plan: (0, 0)), slot, slot, slot]
            + [
                pl.BlockSpec(
                    (1, half_rows, D),
                    lambda step, plan, place=place: (plan[1, step * SLOT_STEP + place], 0, 0),
                )
                for place in range(SLOT_STEP)
            ]
            + [pl.BlockSpec((SLOT_STEP * half_rows, D), lambda step, plan: (step, 0))],
            out_specs=[slot] * 3,
        ),
        out_shape=[jax.ShapeDtypeStruct(master.shape, jnp.float32)] * 3,
        cost_estimate=SHORT,
        compiler_params=pltpu.CompilerParams(vmem_limit_bytes=48 << 20),
    )(
        plan,
        factor,
        master,
        first,
        second,
        *[layer_grads] * SLOT_STEP,
        grad_table,
    )


def row_of(groups_ref):
    return jnp.concatenate([groups_ref[0, g : g + 1, :] for g in range(TILE_GROUPS)], axis=1)


def stat_row(stat_ref, row):
    return jnp.concatenate([stat_ref[g, row : row + 1, :] for g in range(TILE_GROUPS)], axis=1)


def chunk_of(span_ref, step):
    return pl.ds(pl.multiple_of(span_ref[0] + step * ROW_STEP, 16), ROW_STEP)


def chunks_of(span_ref):
    return (span_ref[1] - span_ref[0] + ROW_STEP - 1) // ROW_STEP


def whole(shape):
    return pl.BlockSpec(shape, lambda step, span: (0,) * len(shape), pipeline_mode=pl.Buffered(1))


TILE = TILE_GROUPS * LANES
TOKENS_SPEC = pl.BlockSpec((1, TILE_GROUPS, LANES), lambda step, span: (step, 0, 0))
STATS_SPEC = pl.BlockSpec((TILE_GROUPS, 8, LANES), lambda step, span: (step, 0, 0))
ROWS_SPEC = pl.BlockSpec((TILE, D), lambda step, span: (step, 0))


def local_call(name, kernel, steps, span, operands, in_specs, out_shape, out_specs, scratch):
    return pl.pallas_call(
        kernel,
        name=name,
        grid_spec=pltpu.PrefetchScalarGridSpec(
            num_scalar_prefetch=1,
            grid=(steps,),
            in_specs=in_specs,
            out_specs=out_specs,
            scratch_shapes=scratch,
        ),
        out_shape=out_shape,
        cost_estimate=SHORT,
        compiler_params=pltpu.CompilerParams(vmem_limit_bytes=60 << 20),
    )(span, *operands)


def look_up(span, row_ids, tokens, table):
    rows = table.shape[0]
    steps = tokens.shape[0]

    def kernel(span_ref, ids_ref, tokens_ref, table_ref, out_ref, acc):
        acc[...] = jnp.zeros_like(acc)
        wanted = row_of(tokens_ref)

        def one(step, carry):
            chunk = chunk_of(span_ref, step)
            hits = jnp.where(ids_ref[chunk, :] == wanted, 1.0, 0.0).astype(jnp.bfloat16)
            acc[...] += contract_first(hits, table_ref[chunk, :])
            return carry

        lax.fori_loop(0, chunks_of(span_ref), one, 0)
        out_ref[...] = acc[...].astype(jnp.bfloat16)

    return local_call(
        "look_up",
        kernel,
        steps,
        span,
        (row_ids, tokens, table),
        [whole((rows, 1)), TOKENS_SPEC, whole((rows, D))],
        jax.ShapeDtypeStruct((steps * TILE, D), jnp.bfloat16),
        ROWS_SPEC,
        [pltpu.VMEM((TILE, D), jnp.float32)],
    )


def head_forward(span, row_ids, labels, table, final):
    rows = table.shape[0]
    steps = labels.shape[0]

    def kernel(span_ref, ids_ref, labels_ref, table_ref, final_ref, powers_ref, stats_ref, scores):
        wanted = row_of(labels_ref)
        hidden = final_ref[...]

        def first(step, carry):
            top, target = carry
            chunk = chunk_of(span_ref, step)
            ids = ids_ref[chunk, :]
            raw = contract_last(table_ref[chunk, :], hidden)
            raw = jnp.where(ids >= 0, raw, -1e30)
            scores[chunk, :] = raw
            top = jnp.maximum(top, jnp.max(raw, axis=0, keepdims=True))
            target = target + jnp.sum(jnp.where(ids == wanted, raw, 0.0), axis=0, keepdims=True)
            return (top, target)

        blank = jnp.zeros((1, TILE), jnp.float32)
        top, target = lax.fori_loop(0, chunks_of(span_ref), first, (blank - 1e30, blank))

        def second(step, total):
            chunk = chunk_of(span_ref, step)
            powers = jnp.exp(scores[chunk, :] - top)
            powers_ref[chunk, :] = powers.astype(jnp.bfloat16)
            return total + jnp.sum(powers, axis=0, keepdims=True)

        total = lax.fori_loop(0, chunks_of(span_ref), second, blank)
        rest = jnp.zeros((5, LANES), jnp.float32)
        for g in range(TILE_GROUPS):
            lanes = slice(g * LANES, (g + 1) * LANES)
            stats_ref[g] = jnp.concatenate(
                [top[:, lanes], total[:, lanes], target[:, lanes], rest], axis=0
            )

    return local_call(
        "head_forward",
        kernel,
        steps,
        span,
        (row_ids, labels, table, final),
        [whole((rows, 1)), TOKENS_SPEC, whole((rows, D)), ROWS_SPEC],
        [
            jax.ShapeDtypeStruct((rows, steps * TILE), jnp.bfloat16),
            jax.ShapeDtypeStruct((steps * TILE_GROUPS, 8, LANES), jnp.float32),
        ],
        [pl.BlockSpec((rows, TILE), lambda step, span: (0, step)), STATS_SPEC],
        [pltpu.VMEM((rows, TILE), jnp.float32)],
    )


def head_backward(span, row_ids, labels, keep, stats, log_totals, table, final, powers):
    rows = table.shape[0]
    steps = labels.shape[0]

    def kernel(
        span_ref, ids_ref, labels_ref, keep_ref, stats_ref, logs_ref, table_ref, final_ref,
        powers_ref, grad_final_ref, grad_table_ref, acc,
    ):
        @pl.when(pl.program_id(0) == 0)
        def _():
            grad_table_ref[...] = jnp.zeros_like(grad_table_ref)

        acc[...] = jnp.zeros_like(acc)
        wanted, kept = row_of(labels_ref), row_of(keep_ref)
        scale = jnp.exp(stat_row(stats_ref, 0) - stat_row(logs_ref, 0)) * kept
        hidden = final_ref[...]

        def one(step, carry):
            chunk = chunk_of(span_ref, step)
            grads = powers_ref[chunk, :].astype(jnp.float32) * scale
            grads = grads - jnp.where(ids_ref[chunk, :] == wanted, kept, 0.0)
            grads = grads.astype(jnp.bfloat16)
            grad_table_ref[chunk, :] += jnp.dot(grads, hidden, preferred_element_type=jnp.float32)
            acc[...] += contract_first(grads, table_ref[chunk, :])
            return carry

        lax.fori_loop(0, chunks_of(span_ref), one, 0)
        grad_final_ref[...] = acc[...].astype(jnp.bfloat16)

    return local_call(
        "head_backward",
        kernel,
        steps,
        span,
        (row_ids, labels, keep, stats, log_totals, table, final, powers),
        [
            whole((rows, 1)),
            TOKENS_SPEC,
            TOKENS_SPEC,
            STATS_SPEC,
            STATS_SPEC,
            whole((rows, D)),
            ROWS_SPEC,
            pl.BlockSpec((rows, TILE), lambda step, span: (0, step)),
        ],
        [
            jax.ShapeDtypeStruct((steps * TILE, D), jnp.bfloat16),
            jax.ShapeDtypeStruct((rows, D), jnp.float32),
        ],
        [ROWS_SPEC, whole((rows, D))],
        [pltpu.VMEM((TILE, D), jnp.float32)],
    )


def look_back(span, row_ids, tokens, grad_start, grad_table):
    rows = grad_table.shape[0]
    steps = tokens.shape[0]

    def kernel(span_ref, ids_ref, tokens_ref, grad_ref, table_ref, out_ref, squares_ref):
        @pl.when(pl.program_id(0) == 0)
        def _():
            out_ref[...] = table_ref[...]

        wanted = row_of(tokens_ref)
        grads = grad_ref[...]

        def one(step, carry):
            chunk = chunk_of(span_ref, step)
            hits = jnp.where(ids_ref[chunk, :] == wanted, 1.0, 0.0).astype(jnp.bfloat16)
            out_ref[chunk, :] += jnp.dot(hits, grads, preferred_element_type=jnp.float32)
            return carry

        lax.fori_loop(0, chunks_of(span_ref), one, 0)

        @pl.when(pl.program_id(0) == steps - 1)
        def _():
            def square(step, total):
                values = out_ref[chunk_of(span_ref, step), :]
                values = (values * values).reshape(ROW_STEP // 8, 8, D).sum(axis=0)
                return total + values

            squares_ref[...] = lax.fori_loop(
                0, chunks_of(span_ref), square, jnp.zeros((8, D), jnp.float32)
            )

    return local_call(
        "look_back",
        kernel,
        steps,
        span,
        (row_ids, tokens, grad_start, grad_table),
        [whole((rows, 1)), TOKENS_SPEC, ROWS_SPEC, whole((rows, D))],
        [
            jax.ShapeDtypeStruct((rows, D), jnp.float32),
            jax.ShapeDtypeStruct((8, D), jnp.float32),
        ],
        [whole((rows, D)), whole((8, D))],
        [],
    )


def body(
    token_ids,
    labels,
    real_counts,
    owners,
    master,
    first_moment,
    second_moment,
    gains,
    gains_first,
    gains_second,
    mix,
    mix_first,
    mix_second,
):
    tensors = lax.axis_size("tensor")
    groups = lax.axis_size("dp")
    group = lax.axis_index("dp")
    tensor_part = lax.axis_index("tensor")
    seq_part = lax.axis_index("seq")
    slots, half_rows, _ = master.shape
    seq_count, half_len = token_ids.shape
    row_count = seq_count * half_len
    share = row_count // tensors
    head_rows = 3 * D // tensors
    out_rows = D // tensors
    unit_rows = FF // tensors
    layer_rows = head_rows + out_rows + 2 * unit_rows
    layer_blocks = layer_rows // (2 * half_rows)
    blocks = LAYERS * layer_blocks
    vocab_rows = VOCAB // tensors
    local_heads = HEADS // tensors

    slot_rank = slot_table(owners)
    block_ids = jnp.arange(owners.shape[0], dtype=jnp.int32)
    mine = owners == group
    match = (jnp.arange(slots)[:, None] == slot_rank[None, :]) & mine[None, :]
    slot_block = jnp.sum(jnp.where(match, block_ids[None, :] + 1, 0), axis=1) - 1
    row_ids = (
        tensor_part * vocab_rows
        + (slot_block[:, None] - blocks) * (2 * half_rows)
        + seq_part * half_rows
        + jnp.arange(half_rows, dtype=jnp.int32)[None, :]
    )
    row_ids = jnp.where(slot_block[:, None] >= blocks, row_ids, -1).reshape(-1, 1)
    spare = -(-ROW_STEP // half_rows)
    row_ids = jnp.pad(row_ids, ((0, spare * half_rows), (0, 0)), constant_values=-1)
    held = jnp.sum(jnp.where(mine, 1, 0)) * half_rows
    first_held = jnp.sum(jnp.where(mine & (block_ids < blocks), 1, 0)) * half_rows
    span = jnp.stack([first_held, held]).astype(jnp.int32)
    plan = jnp.stack(
        [
            jnp.where(slot_block < 0, -1, jnp.where(slot_block < blocks, 0, 1)),
            jnp.where(slot_block < blocks, jnp.maximum(slot_block, 0), 0),
        ]
    ).astype(jnp.int32)

    packed = jnp.concatenate(
        [
            token_ids.reshape(tensors, LANES),
            labels.reshape(tensors, LANES),
            jnp.broadcast_to(real_counts[:, None], (16 - 2 * tensors, LANES)),
        ],
        axis=0,
    )
    ids_all, labels_all, keep_all, count = spread_tokens(packed, 15)
    order = (2, tensors, groups, share)

    table_slots = jnp.pad(master.astype(jnp.bfloat16), ((0, spare), (0, 0), (0, 0)))
    table = table_slots.reshape(-1, D)

    halves = jnp.where(
        mine[:blocks][:, None, None], jnp.take(table_slots, slot_rank[:blocks], axis=0), 0.0
    ).astype(jnp.bfloat16)
    third = layer_blocks // 3

    def weights_line(*starts):
        return Line([(halves, start * third, third) for start in starts], True)

    def as_table(joined):
        return joined.reshape(-1, D)

    positions = seq_part * half_len + jnp.arange(row_count) % half_len
    steps_half = jnp.arange(HEAD_DIM // 2).astype(jnp.float32)
    freqs = 10000.0 ** (-2.0 * steps_half / HEAD_DIM)
    angles = freqs[:, None] * positions.astype(jnp.float32)[None, :]
    cosine, sine = jnp.cos(angles), jnp.sin(angles)

    looked = look_up(span, row_ids, ids_all, table).reshape(order + (D,))
    start, joined = reduce_rows(looked, (0, 14), weights_line(0, 1))
    table_one = as_table(joined)
    attention_table, up = table_one, (table_one, 1)
    tables = []
    gain = [gains[i : i + 1] for i in range(2 * LAYERS + 1)]
    piece = ((share, D), jnp.float32)

    def normed_of(total, stream, gain_row):
        return (layer_norm_parts(stream)[0] * gain_row,)

    def inner_of(total, stream, gain_row):
        inner = stream + total
        return (inner, layer_norm_parts(inner)[0] * gain_row)

    def outcome_of(base, total, inner, gain_row, *rest):
        states, scalars = rest[:-1], rest[-1]
        outcome = inner + total
        stream = scalars[base + len(states)] * outcome
        for source, state in enumerate(states):
            stream = stream + scalars[base + source] * state
        return (outcome, stream, layer_norm_parts(stream)[0] * gain_row)

    (normed,) = tensor_step("normed", normed_of, None, (start, gain[0]), (), [], True, 1)
    states, streams, inners, kept_all = [start], [start], [], []
    for level in range(LAYERS):
        here, last = 3 * level, level == LAYERS - 1
        carried = [] if last else [here + 3]
        carried += [here + 1, here + 2] if level else [here + 2]
        inner, normed_two, queries, both, logs, attended, joined = tensor_step(
            f"inner_{level}",
            inner_of,
            attention_work(normed, attention_table, cosine, sine),
            (streams[level], gain[2 * level + 1]),
            (),
            [piece],
            True,
            2 if level == 0 else 15 + level,
            weights_line(*carried),
        )
        kept = (queries, both, logs, attended)
        joined = as_table(joined)
        down = (joined, len(carried) - 1)
        up = (joined, len(carried) - 2) if level else up
        tables.append((attention_table, up, down))
        attention_table = joined
        outcome, stream, normed_next, hidden, activated = tensor_step(
            f"outcome_{level}",
            partial(outcome_of, (level + 1) * (level + 2) // 2 - 1),
            unit_work(normed_two, up, down),
            [inner, gain[2 * level + 2]] + states,
            (mix,),
            [piece, piece] + ([((share, D), jnp.bfloat16)] if last else []),
            not last,
            3 + level,
        )
        inners.append(inner)
        kept_all.append((normed, kept, normed_two, (hidden, activated)))
        states.append(outcome)
        streams.append(stream)
        normed = normed_next

    final_all = gather_all(normed, 3 + LAYERS)[0].reshape(-1, D)
    powers, stats = head_forward(span, row_ids, labels_all, table, final_all)
    home, log_totals = join_stats(
        stats.reshape((2, tensors, groups, 8, LANES)), 4 + LAYERS
    )
    grad_final, grad_table = head_backward(
        span,
        row_ids,
        labels_all,
        keep_all,
        stats,
        log_totals.reshape(-1, 8, LANES),
        table,
        final_all,
        powers,
    )
    grad_final, _ = reduce_rows(grad_final.reshape(order + (D,)), (0, 14))

    row = ((1, D), jnp.float32)

    def top_of(total, grad, stream, gain_row, scalars):
        grad_top, grad_gain = norm_pull(grad, gain_row, stream)
        grad_state = scalars[MIX_WEIGHTS - 1] * grad_top
        return (grad_top, grad_state, grad_gain, grad_state)

    def inner_back(total, grad_out, inner, gain_row):
        grad, grad_gain = norm_pull(total, gain_row, inner)
        grad = grad_out + grad
        return (grad, grad_gain, grad)

    def stream_back(block, total, grad_inner, stream, gain_row, *rest):
        grad_ys, scalars = rest[:-1], rest[-1]
        grad, grad_gain = norm_pull(total, gain_row, stream)
        grad = grad_inner + grad
        state = grad if block == 0 else scalars[block * (block + 1) // 2 - 1 + block] * grad
        for offset, grad_y in enumerate(grad_ys):
            later = block + 1 + offset
            state = state + scalars[later * (later + 1) // 2 - 1 + block] * grad_y
        return (grad, state, grad_gain, state)

    grad_ys = [None] * (LAYERS + 1)
    gain_grads = [None] * (2 * LAYERS + 1)
    layer_grads, attention_grads = [None] * (3 * LAYERS), None
    grad_ys[LAYERS], grad_state, gain_grads[2 * LAYERS], grad_branch = tensor_step(
        "top_back",
        top_of,
        None,
        (grad_final, streams[LAYERS], gain[2 * LAYERS]),
        (mix,),
        [piece, piece, row],
        True,
        5 + LAYERS,
    )
    for level in reversed(range(LAYERS)):
        normed, kept, normed_two, unit_kept = kept_all[level]
        attention_table, up, down = tables[level]
        grad_inner, gain_grads[2 * level + 1], grad_attn, unit_grads, *summed = tensor_step(
            f"inner_back_{level}",
            inner_back,
            unit_back_work(grad_branch, normed_two, up, down, unit_kept, half_rows),
            (grad_state, inners[level], gain[2 * level + 1]),
            (),
            [piece, row],
            True,
            6 + LAYERS if level == 0 else 19 + level,
            None if attention_grads is None else Line([(attention_grads, 0, third)], False),
        )
        if summed:
            layer_grads[3 * (level + 1)] = summed[0]
        grad_ys[level], grad_state, gain_grads[2 * level], grad_branch, attention_grads, summed = (
            tensor_step(
                f"stream_back_{level}",
                partial(stream_back, level),
                attention_back_work(
                    grad_attn, normed, attention_table, kept, cosine, sine, half_rows
                ),
                [grad_inner, streams[level], gain[2 * level]] + grad_ys[level + 1 :],
                (mix,),
                [piece, piece, row] + ([] if level else [((share, D), jnp.bfloat16)]),
                level > 0,
                7 + LAYERS + level,
                Line([(unit_grads, 0, 2 * third)], False),
            )
        )
        layer_grads[3 * level + 1] = summed

    grad_start_all, layer_grads[0] = gather_all(
        grad_branch, 13, Line([(attention_grads, 0, third)], False)
    )
    layer_grads = jnp.concatenate([grads for grads in layer_grads if grads is not None], axis=0)
    grad_start_all = grad_start_all.reshape(-1, D)
    grad_table, table_squares = look_back(span, row_ids, ids_all, grad_start_all, grad_table)
    values = layer_grads.astype(jnp.float32)
    layer_squares = jnp.sum(jnp.where(mine[:blocks][:, None, None], values * values, 0.0))
    keep = jnp.where(
        tensor_part * share + jnp.arange(share) < real_counts[0], 1.0, 0.0
    ).astype(jnp.float32)
    news = finish(
        gain_grads,
        states,
        grad_ys[1:],
        home,
        keep[None],
        table_squares,
        layer_squares.reshape(1, 1),
        count,
        (gains, gains_first, gains_second, mix[None], mix_first[None], mix_second[None]),
        7 + 2 * LAYERS,
    )
    new_gains, new_gains_first, new_gains_second = news[:3]
    new_mix, new_mix_first, new_mix_second = [value[0] for value in news[3:6]]
    loss_sum, clip_norm = news[6][0, 0], news[6][0, 1]
    token_count = count[0, 0]
    new_master, new_first, new_second = update_slots(
        plan, news[7], master, first_moment, second_moment, layer_grads, grad_table
    )
    return (
        new_master,
        new_first,
        new_second,
        new_gains,
        new_gains_first,
        new_gains_second,
        new_mix,
        new_mix_first,
        new_mix_second,
        loss_sum,
        token_count,
        clip_norm,
    )


def solution(mesh):
    return jax.shard_map(
        body,
        mesh=mesh,
        in_specs=(
            P("dp", "seq"),
            P("dp", "seq"),
            P(("dp", "seq")),
            P(),
            P("dp", ("tensor", "seq"), None),
            P("dp", ("tensor", "seq"), None),
            P("dp", ("tensor", "seq"), None),
            P(),
            P(),
            P(),
            P(),
            P(),
            P(),
        ),
        out_specs=(
            P("dp", ("tensor", "seq"), None),
            P("dp", ("tensor", "seq"), None),
            P("dp", ("tensor", "seq"), None),
            P(),
            P(),
            P(),
            P(),
            P(),
            P(),
            P(),
            P(),
            P(),
        ),
        check_vma=False,
    )
```

```python
from functools import partial

import jax
import jax.numpy as jnp
from jax import lax
from jax.experimental import pallas as pl
from jax.experimental.pallas import tpu as pltpu
from jax.sharding import PartitionSpec as P

D = 768
HEADS = 12
HEAD_DIM = 64
FF = 3072
VOCAB = 50304
LAYERS = 2
STEP_COUNT = 10
MIX_WEIGHTS = 5


EPS_NORM = 1e-05
CLIP_NORM = 0.01
BETA_ONE = 0.9
BETA_TWO = 0.95
ADAM_EPS = 1e-08
RATE_MATRIX = 0.04
RATE_SMALL = 0.4
DECAY_MATRIX = 0.1


def contract_last(left, right):
    return lax.dot_general(
        left, right, (((1,), (1,)), ((), ())), preferred_element_type=jnp.float32
    )


def contract_first(left, right):
    return lax.dot_general(
        left, right, (((0,), (0,)), ((), ())), preferred_element_type=jnp.float32
    )


def slot_table(owners):
    ranks = jnp.arange(owners.shape[0])
    same = (owners[None, :] == owners[:, None]) & (ranks[None, :] < ranks[:, None])
    return jnp.sum(jnp.where(same, 1, 0), axis=1).astype(jnp.int32)


def adam_update(weight, first, second, grad, rate, decay):
    first = BETA_ONE * first + (1.0 - BETA_ONE) * grad
    second = BETA_TWO * second + (1.0 - BETA_TWO) * grad * grad
    first_hat = first / (1.0 - BETA_ONE**STEP_COUNT)
    second_hat = second / (1.0 - BETA_TWO**STEP_COUNT)
    weight = weight - rate * (first_hat / (jnp.sqrt(second_hat) + ADAM_EPS) + decay * weight)
    return (weight, first, second)


MESH = pl.DeviceIdType.MESH
ROW_STEP = 400
TILE_GROUPS = 8
LANES = 128
SHORT = pl.CostEstimate(flops=1000, bytes_accessed=1000, transcendentals=0)


def meet(peers):
    gate = pltpu.get_barrier_semaphore()
    for peer in peers:
        pl.semaphore_signal(gate, inc=1, device_id=peer, device_id_type=MESH)
    pl.semaphore_wait(gate, len(peers))


def others(axis):
    count, me = lax.axis_size(axis), lax.axis_index(axis)
    return [lax.rem(me + step, count) for step in range(1, count)]


def behind(axis, step):
    count, me = lax.axis_size(axis), lax.axis_index(axis)
    return lax.rem(me + count - step, count)


def send(source, target, send_sem, recv_sem, device):
    copy = pltpu.make_async_remote_copy(
        src_ref=source,
        dst_ref=target,
        send_sem=send_sem,
        recv_sem=recv_sem,
        device_id=device,
        device_id_type=MESH,
    )
    copy.start()
    return copy


def layer_norm_parts(stream):
    center = stream - jnp.mean(stream, -1, keepdims=True)
    inverse = lax.rsqrt(jnp.mean(center * center, -1, keepdims=True) + EPS_NORM)
    return center * inverse, inverse


def norm_pull(grad_normed, gain, stream):
    scaled, inverse = layer_norm_parts(stream)
    grad_scaled = grad_normed * gain
    grad_stream = inverse * (
        grad_scaled
        - jnp.mean(grad_scaled, -1, keepdims=True)
        - scaled * jnp.mean(grad_scaled * scaled, -1, keepdims=True)
    )
    return grad_stream, jnp.sum(grad_normed * scaled, axis=0, keepdims=True)


class Work:
    def __init__(self, before, during, operands, specs, outs, scratch, after=None, twins=False):
        self.before, self.during, self.after, self.twins = before, during, after, twins
        self.operands, self.specs, self.outs, self.scratch = operands, specs, outs, scratch


def tensor_step(name, function, work, extras, scalars, outs, gather, collective_id, line=None):
    parts = lax.axis_size("tensor")
    share = extras[0].shape[0]
    reduce = work is not None
    work = work or Work(None, None, [], [], [], [])

    def kernel(*refs):
        refs = list(refs)

        def take(count):
            return [refs.pop(0) for _ in range(count)]

        work_refs = take(len(work.operands))
        extra_refs = take(len(extras))
        scalar_refs = take(len(scalars))
        source_refs = take(len(line.operands)) if line else []
        out_refs = take(len(outs))
        (full,) = take(1) if gather else [None]
        work_outs = take(len(work.outs))
        (joined,) = take(1) if line else [None]
        send_sems, recv_sems = take(2)
        partial_ref, outgoing, arrived = take(3) if reduce else [None] * 3
        if line:
            line.bind(source_refs, joined, take(len(line.scratch)))
            line.load()

        def tick(count=1):
            if line:
                line.steps(count)

        me, side = lax.axis_index("tensor"), lax.axis_index("seq")
        peers = others("tensor")
        twin = {"seq": 1 - side}
        twins = work.twins or (line and line.share)
        meet(
            [{"tensor": peer} for peer in peers]
            + [twin] * bool(twins)
            + ([{"dp": peer} for peer in others("dp")] if line else [])
        )
        if line:
            line.begin()
        total = None
        if reduce:
            work.before(work_refs, work_outs, refs, partial_ref, tick)
            copies = []
            for step, peer in enumerate(peers):
                rows = pl.ds(pl.multiple_of(peer * share, share), share)
                outgoing[step] = partial_ref[rows, :].astype(jnp.bfloat16)
                copies.append(
                    send(
                        outgoing.at[step],
                        arrived.at[step],
                        send_sems.at[0, step],
                        recv_sems.at[0, step],
                        {"tensor": peer},
                    )
                )
            if work.during:
                work.during(work_refs, work_outs, refs)
            tick(6)
            total = partial_ref[pl.ds(pl.multiple_of(me * share, share), share), :]
            for step, copy in enumerate(copies):
                copy.wait()
                total = total + arrived[step].astype(jnp.float32)
        results = function(total, *[ref[...] for ref in extra_refs], *scalar_refs)
        for ref, value in zip(out_refs, results):
            ref[...] = value.astype(ref.dtype)
        if gather:
            full[me] = results[len(outs)].astype(jnp.bfloat16)
            copies = [
                send(
                    full.at[me],
                    full.at[me],
                    send_sems.at[1, step],
                    recv_sems.at[1, step],
                    {"tensor": peer},
                )
                for step, peer in enumerate(peers)
            ]
        if work.after:
            work.after(work_refs, work_outs, refs)
        tick(None)
        if gather:
            for copy in copies:
                copy.wait()
        if line:
            line.end()

    vmem = pl.BlockSpec(memory_space=pltpu.VMEM)
    smem = pl.BlockSpec(memory_space=pltpu.SMEM)
    shapes = [jax.ShapeDtypeStruct(shape, dtype) for shape, dtype in outs]
    if gather:
        shapes.append(jax.ShapeDtypeStruct((parts, share, D), jnp.bfloat16))
    shapes += [jax.ShapeDtypeStruct(shape, dtype) for shape, dtype in work.outs]
    out_specs = [vmem] * len(shapes)
    operands = list(work.operands) + list(extras) + list(scalars)
    in_specs = list(work.specs) + [vmem] * len(extras) + [smem] * len(scalars)
    dma = pltpu.SemaphoreType.DMA
    buffers = [dma((2, parts - 1))] * 2
    if reduce:
        buffers += [pltpu.VMEM((parts * share, D), jnp.float32)]
        buffers += [pltpu.VMEM((parts - 1, share, D), jnp.bfloat16)] * 2
    if line:
        operands += line.operands
        in_specs += line.in_specs
        shapes.append(line.out_shape)
        out_specs.append(line.out_spec)
        buffers += line.scratch
    return pl.pallas_call(
        kernel,
        name=name,
        grid=(1,),
        out_shape=shapes,
        in_specs=in_specs,
        out_specs=out_specs,
        scratch_shapes=buffers + list(work.scratch),
        cost_estimate=SHORT,
        compiler_params=pltpu.CompilerParams(
            collective_id=collective_id, has_side_effects=True, vmem_limit_bytes=50 << 20
        ),
    )(*operands)


VMEM_SPEC = pl.BlockSpec(memory_space=pltpu.VMEM)


def part_spec(rows, index):
    return pl.BlockSpec((rows, D), lambda step: (index, 0), pipeline_mode=pl.Buffered(1))


def turn(block, cosine, sine):
    half = HEAD_DIM // 2
    first, second = block[:half], block[half:]
    return jnp.concatenate(
        [first * cosine - second * sine, second * cosine + first * sine], axis=0
    )


def times(left, right):
    return jnp.dot(left, right, preferred_element_type=jnp.float32)


def scores_of(keys_values, head, queries, side):
    span = slice(head * HEAD_DIM, (head + 1) * HEAD_DIM)
    count = queries.shape[1]
    scale = HEAD_DIM ** (-0.5)
    far = contract_first(keys_values[0, 0, span, :], queries) * scale
    own = contract_first(keys_values[1, 0, span, :], queries) * scale
    key = lax.broadcasted_iota(jnp.int32, (count, count), 0)
    query = lax.broadcasted_iota(jnp.int32, (count, count), 1)
    own = jnp.where(key <= query, own, -1e30)
    far = jnp.where(query + side * (2 * count) >= 2 * count, far, -1e30)
    return far, own


def attention_work(normed, table, cosine, sine):
    parts, share, _ = normed.shape
    count = parts * share
    width = D // parts
    heads = width // HEAD_DIM

    def before(ins, outs, scratch, partial_ref, tick):
        normed_ref, qkv_ref, out_ref, cosine_ref, sine_ref = ins
        queries_ref, both, logs_ref, attended_ref = outs
        send_sem, recv_sem = scratch
        side = lax.axis_index("seq")
        cosine, sine = cosine_ref[...], sine_ref[...]
        rows = normed_ref[...].reshape(count, D)
        joined = contract_last(qkv_ref[...], rows)
        for head in range(heads):
            span = slice(head * HEAD_DIM, (head + 1) * HEAD_DIM)
            keys = joined[width + head * HEAD_DIM : width + (head + 1) * HEAD_DIM]
            both[1, 0, span, :] = turn(keys, cosine, sine).astype(jnp.bfloat16)
        both[1, 1] = joined[2 * width :].astype(jnp.bfloat16)
        copy = pltpu.make_async_remote_copy(
            src_ref=both.at[1],
            dst_ref=both.at[0],
            send_sem=send_sem,
            recv_sem=recv_sem,
            device_id={"seq": 1 - side},
            device_id_type=MESH,
        )

        copy.start()
        for head in range(heads):
            span = slice(head * HEAD_DIM, (head + 1) * HEAD_DIM)
            queries_ref[span, :] = turn(joined[span], cosine, sine).astype(jnp.bfloat16)

        copy.wait()
        for head in range(heads):
            span = slice(head * HEAD_DIM, (head + 1) * HEAD_DIM)
            far, own = scores_of(both, head, queries_ref[span, :], side)
            peak = jnp.maximum(
                jnp.max(far, axis=0, keepdims=True), jnp.max(own, axis=0, keepdims=True)
            )
            far, own = jnp.exp(far - peak), jnp.exp(own - peak)
            total = jnp.sum(far, axis=0, keepdims=True) + jnp.sum(own, axis=0, keepdims=True)
            logs_ref[head] = peak + jnp.log(total)
            inverse = 1.0 / total
            attended = times(both[0, 1, span, :], (far * inverse).astype(jnp.bfloat16))
            attended += times(both[1, 1, span, :], (own * inverse).astype(jnp.bfloat16))
            attended_ref[span, :] = attended.astype(jnp.bfloat16)
            tick(2)
        partial_ref[...] = contract_first(attended_ref[...], out_ref[...])

    low = jnp.bfloat16
    return Work(
        before,
        None,
        [normed, table, table, cosine, sine],
        [VMEM_SPEC, part_spec(3 * width, 0), part_spec(width, 3), VMEM_SPEC, VMEM_SPEC],
        [
            ((width, count), low),
            ((2, 2, width, count), low),
            ((heads, 1, count), jnp.float32),
            ((width, count), low),
        ],
        [pltpu.SemaphoreType.DMA, pltpu.SemaphoreType.DMA],
        twins=True,
    )


def fold_copy(own, near, send_sems, recv_sems, index):
    side = lax.axis_index("seq")
    return pltpu.make_async_remote_copy(
        src_ref=own.at[index, :, 1 - side],
        dst_ref=near.at[index],
        send_sem=send_sems.at[index],
        recv_sem=recv_sems.at[index],
        device_id={"seq": 1 - side},
        device_id_type=MESH,
    )


def add_halves(own, near, out, start):
    side = lax.axis_index("seq")

    def one(block, carry):
        value = own[block, side].astype(jnp.float32) + near[block].astype(jnp.float32)
        out[start + block] = value.astype(jnp.bfloat16)
        return carry

    lax.fori_loop(0, near.shape[0], one, 0)


def attention_back_work(grad, normed, table, kept, cosine, sine, half_rows):
    parts, share, _ = normed.shape
    count = parts * share
    width = D // parts
    heads = width // HEAD_DIM
    queries, both, logs, attended = kept
    blocks = 4 * width // (2 * half_rows)

    def before(ins, outs, scratch, partial_ref, tick):
        grad_ref, _, qkv_ref, out_ref, queries_ref, both, logs_ref, _, cosine_ref, sine_ref = ins
        back, came, grad_joined, send_sem, recv_sem = scratch[:5]
        side = lax.axis_index("seq")
        cosine, sine = cosine_ref[...], -sine_ref[...]
        scale = HEAD_DIM ** (-0.5)
        grads = contract_last(out_ref[...], grad_ref[...].reshape(count, D)).astype(jnp.bfloat16)
        own_grads = []
        for head in range(heads):
            span = slice(head * HEAD_DIM, (head + 1) * HEAD_DIM)
            head_queries, head_grads = queries_ref[span, :], grads[span]
            far, own = scores_of(both, head, head_queries, side)
            far, own = jnp.exp(far - logs_ref[head]), jnp.exp(own - logs_ref[head])
            far_grad = contract_first(both[0, 1, span, :], head_grads)
            own_grad = contract_first(both[1, 1, span, :], head_grads)
            mean = jnp.sum(far * far_grad, axis=0, keepdims=True)
            mean += jnp.sum(own * own_grad, axis=0, keepdims=True)
            far_grad = (far * (far_grad - mean)).astype(jnp.bfloat16)
            own_grad = (own * (own_grad - mean)).astype(jnp.bfloat16)
            far, own = far.astype(jnp.bfloat16), own.astype(jnp.bfloat16)
            back[0, span, :] = (contract_last(head_queries, far_grad) * scale).astype(jnp.bfloat16)
            back[1, span, :] = contract_last(head_grads, far).astype(jnp.bfloat16)
            query_grad = times(both[0, 0, span, :], far_grad) + times(both[1, 0, span, :], own_grad)
            grad_joined[span, :] = turn(query_grad * scale, cosine, sine).astype(jnp.bfloat16)
            own_grads.append(
                (contract_last(head_queries, own_grad) * scale, contract_last(head_grads, own))
            )
            tick(2)
        copy = send(back, came, send_sem, recv_sem, {"seq": 1 - side})
        copy.wait()
        for head, (key_grad, value_grad) in enumerate(own_grads):
            span = slice(head * HEAD_DIM, (head + 1) * HEAD_DIM)
            key_grad = key_grad + came[0, span, :].astype(jnp.float32)
            value_grad = value_grad + came[1, span, :].astype(jnp.float32)
            start = width + head * HEAD_DIM
            grad_joined[start : start + HEAD_DIM, :] = turn(key_grad, cosine, sine).astype(
                jnp.bfloat16
            )
            start += width
            grad_joined[start : start + HEAD_DIM, :] = value_grad.astype(jnp.bfloat16)
        partial_ref[...] = contract_first(grad_joined[...], qkv_ref[...])

    def during(ins, outs, scratch):
        grad_ref, normed_ref, attended_ref = ins[0], ins[1], ins[7]
        grad_joined = scratch[2]
        own, near, fold_send, fold_recv = scratch[5:]
        value = times(grad_joined[...], normed_ref[...].reshape(count, D)).astype(jnp.bfloat16)
        part = 3 * blocks // 4
        own[0, :part] = value.reshape(part, 2, half_rows, D)
        value = times(attended_ref[...], grad_ref[...].reshape(count, D)).astype(jnp.bfloat16)
        own[0, part:] = value.reshape(blocks - part, 2, half_rows, D)
        fold_copy(own, near, fold_send, fold_recv, 0).start()

    def after(ins, outs, scratch):
        own, near, fold_send, fold_recv = scratch[5:]
        fold_copy(own, near, fold_send, fold_recv, 0).wait()
        add_halves(own.at[0], near.at[0], outs[0], 0)

    low = jnp.bfloat16
    dma = pltpu.SemaphoreType.DMA
    return Work(
        before,
        during,
        [grad, normed, table, table, queries, both, logs, attended, cosine, sine],
        [VMEM_SPEC, VMEM_SPEC, part_spec(3 * width, 0), part_spec(width, 3)] + [VMEM_SPEC] * 6,
        [((blocks, half_rows, D), low)],
        [
            pltpu.VMEM((2, width, count), low),
            pltpu.VMEM((2, width, count), low),
            pltpu.VMEM((3 * width, count), low),
            dma,
            dma,
            pltpu.VMEM((1, blocks, 2, half_rows, D), low),
            pltpu.VMEM((1, blocks, half_rows, D), low),
            dma((1,)),
            dma((1,)),
        ],
        after,
        True,
    )


def gelu(hidden):
    return jax.nn.gelu(hidden, approximate=True)


def unit_work(normed, up, down):
    parts, share, _ = normed.shape
    count = parts * share
    units = FF // parts

    def before(ins, outs, scratch, partial_ref, tick):
        normed_ref, up_ref, down_ref = ins
        hidden_ref, activated_ref = outs
        hidden = contract_last(up_ref[...], normed_ref[...].reshape(count, D))
        hidden_ref[...] = hidden
        activated_ref[...] = gelu(hidden).astype(jnp.bfloat16)
        tick(2)
        partial_ref[...] = contract_first(activated_ref[...], down_ref[...])

    return Work(
        before,
        None,
        [normed, up[0], down[0]],
        [VMEM_SPEC, part_spec(units, up[1]), part_spec(units, down[1])],
        [((units, count), jnp.float32), ((units, count), jnp.bfloat16)],
        [],
    )


def unit_back_work(grad, normed, up, down, kept, half_rows):
    parts, share, _ = normed.shape
    count = parts * share
    units = FF // parts
    hidden, activated = kept
    blocks = units // (2 * half_rows)

    def before(ins, outs, scratch, partial_ref, tick):
        grad_ref, _, up_ref, down_ref, hidden_ref, _ = ins
        grad_hidden = scratch[0]
        grad_act = contract_last(down_ref[...], grad_ref[...].reshape(count, D))
        _, pull = jax.vjp(gelu, hidden_ref[...])
        grad_hidden[...] = pull(grad_act)[0].astype(jnp.bfloat16)
        tick(2)
        partial_ref[...] = contract_first(grad_hidden[...], up_ref[...])

    def during(ins, outs, scratch):
        grad_ref, normed_ref, _, _, _, activated_ref = ins
        grad_hidden, own, near, fold_send, fold_recv = scratch
        value = times(grad_hidden[...], normed_ref[...].reshape(count, D))
        own[0] = value.astype(jnp.bfloat16).reshape(own.shape[1:])
        fold_copy(own, near, fold_send, fold_recv, 0).start()
        value = times(activated_ref[...], grad_ref[...].reshape(count, D))
        own[1] = value.astype(jnp.bfloat16).reshape(own.shape[1:])
        fold_copy(own, near, fold_send, fold_recv, 1).start()

    def after(ins, outs, scratch):
        _, own, near, fold_send, fold_recv = scratch
        for index in range(2):
            fold_copy(own, near, fold_send, fold_recv, index).wait()
            add_halves(own.at[index], near.at[index], outs[0], index * blocks)

    low, dma = jnp.bfloat16, pltpu.SemaphoreType.DMA
    return Work(
        before,
        during,
        [grad, normed, up[0], down[0], hidden, activated],
        [VMEM_SPEC, VMEM_SPEC, part_spec(units, up[1]), part_spec(units, down[1])]
        + [VMEM_SPEC] * 2,
        [((2 * blocks, half_rows, D), low)],
        [
            pltpu.VMEM((units, count), low),
            pltpu.VMEM((2, blocks, 2, half_rows, D), low),
            pltpu.VMEM((2, blocks, half_rows, D), low),
            dma((2,)),
            dma((2,)),
        ],
        after,
        True,
    )


LINE_BLOCKS = 1
LINE_LAG = 3


class Line:
    def __init__(self, sources, share):
        self.groups = lax.axis_size("dp")
        self.sources, self.share = sources, share
        count = sum(size for _, _, size in sources)
        _, half_rows, _ = sources[0][0].shape
        self.half = (count, half_rows, D)
        self.chunks = count // LINE_BLOCKS
        self.operands = [array for array, _, _ in sources]
        self.in_specs = [pl.BlockSpec(memory_space=pl.ANY)] * len(sources)
        dma = pltpu.SemaphoreType.DMA
        out = (count, 2, half_rows, D) if share else self.half
        self.out_shape = jax.ShapeDtypeStruct(out, jnp.bfloat16)
        self.out_spec = pl.BlockSpec(memory_space=pl.ANY if share else pltpu.VMEM)
        self.scratch = [
            pltpu.VMEM(self.half, jnp.bfloat16),
            pltpu.VMEM((2,) + self.half, jnp.bfloat16),
            pltpu.VMEM((2,) + self.half, jnp.bfloat16),
            dma((len(sources),)),
            dma((2, self.chunks)),
            dma((2, self.chunks)),
        ]
        if share:
            self.scratch += [pltpu.VMEM(self.half, jnp.bfloat16)] + [dma((self.chunks,))] * 3

    def bind(self, source_refs, out_ref, refs):
        self.source_refs, self.out = source_refs, out_ref
        self.own, self.came, self.going, self.own_sems, self.send_sems, self.recv_sems = refs[:6]
        self.total = out_ref
        if self.share:
            self.total, self.keep_sems, self.twin_send, self.twin_recv = refs[6:]
        self.done = 0
        self.group = lax.axis_index("dp")
        self.first = jnp.where(self.group < self.groups // 2, 0, 1)

    def at(self, chunk):
        return pl.ds(chunk * LINE_BLOCKS, LINE_BLOCKS)

    def comes(self, way):
        return jnp.where(way == 0, self.group > 0, self.group < self.groups - 1)

    def goes(self, way):
        return jnp.where(way == 0, self.group < self.groups - 1, self.group > 0)

    def copy(self, source, way, chunk):
        target = jnp.where(way == 0, self.group + 1, self.group - 1)
        return pltpu.make_async_remote_copy(
            src_ref=source,
            dst_ref=self.came.at[way, self.at(chunk)],
            send_sem=self.send_sems.at[way, chunk],
            recv_sem=self.recv_sems.at[way, chunk],
            device_id={"dp": target},
            device_id_type=MESH,
        )

    def load(self):
        self.loads, place = [], 0
        for index, (ref, (_, start, size)) in enumerate(zip(self.source_refs, self.sources)):
            copy = pltpu.make_async_copy(
                ref.at[pl.ds(start, size)], self.own.at[pl.ds(place, size)], self.own_sems.at[index]
            )
            copy.start()
            self.loads.append(copy)
            place += size

    def begin(self):
        for copy in self.loads:
            copy.wait()
        for way in range(2):

            @pl.when(jnp.logical_not(self.comes(way)))
            def _():
                self.came[way] = jnp.zeros(self.half, jnp.bfloat16)

                def start(chunk, carry):
                    self.copy(self.own.at[self.at(chunk)], way, chunk).start()
                    return carry

                lax.fori_loop(0, self.chunks, start, 0)

    def twin_copy(self, chunk):
        side = lax.axis_index("seq")
        return pltpu.make_async_remote_copy(
            src_ref=self.total.at[self.at(chunk)],
            dst_ref=self.out.at[self.at(chunk), side],
            send_sem=self.twin_send.at[chunk],
            recv_sem=self.twin_recv.at[chunk],
            device_id={"seq": 1 - side},
            device_id_type=MESH,
        )

    def keep_copy(self, chunk):
        return pltpu.make_async_copy(
            self.total.at[self.at(chunk)],
            self.out.at[self.at(chunk), lax.axis_index("seq")],
            self.keep_sems.at[chunk],
        )

    def pass_on(self, way, chunk):
        rows = self.at(chunk)

        @pl.when(self.comes(way))
        def _():
            copy = self.copy(self.going.at[way, rows], way, chunk)
            copy.wait_recv()

            @pl.when(self.goes(way))
            def _():
                value = self.own[rows].astype(jnp.float32) + self.came[way, rows].astype(jnp.float32)
                self.going[way, rows] = value.astype(jnp.bfloat16)
                copy.start()

    def step(self, index):
        @pl.when(index < self.chunks)
        def _():
            self.pass_on(self.first, index)

        @pl.when(index >= LINE_LAG)
        def _():
            chunk = index - LINE_LAG
            rows = self.at(chunk)
            self.pass_on(1 - self.first, chunk)
            value = self.own[rows].astype(jnp.float32)
            value = value + self.came[0, rows].astype(jnp.float32)
            value = value + self.came[1, rows].astype(jnp.float32)
            self.total[rows] = value.astype(jnp.bfloat16)
            if self.share:
                self.keep_copy(chunk).start()
                self.twin_copy(chunk).start()

    def steps(self, count=None):
        last = self.chunks + LINE_LAG
        stop = last if count is None else min(self.done + count, last)

        def one(index, carry):
            self.step(index)
            return carry

        lax.fori_loop(self.done, stop, one, 0)
        self.done = stop

    def end(self):
        def one(chunk, carry):
            for way in range(2):

                @pl.when(self.goes(way))
                def _():
                    self.copy(self.going.at[way, self.at(chunk)], way, chunk).wait_send()

            if self.share:
                self.keep_copy(chunk).wait()
                self.twin_copy(chunk).wait()
            return carry

        lax.fori_loop(0, self.chunks, one, 0)


def reduce_all(terms, collective_id, line=None):
    _, tensors, groups, count, _ = terms.shape
    half = count // 2

    def kernel(*refs):
        refs = list(refs)
        terms_ref = refs.pop(0)
        source_refs = [refs.pop(0) for _ in line.operands] if line else []
        out_ref = refs.pop(0)
        joined_ref = refs.pop(0) if line else None
        (
            near, own, mid, sums, mid_in, far, far_in,
            own_sems, near_send, near_recv, mid_send, mid_recv, far_send, far_recv,
        ) = refs[:14]
        if line:
            line.bind(source_refs, joined_ref, refs[14:])
            line.load()
        group, part, side = lax.axis_index("dp"), lax.axis_index("tensor"), lax.axis_index("seq")
        twin = 1 - side
        parts = others("tensor")
        order = others("dp") + [group]
        meet(
            [{"seq": twin}]
            + [{"tensor": peer} for peer in parts]
            + [{"dp": peer} for peer in order[:-1]]
        )
        waits, near_copies, own_copies = [], [], []
        for place, target in enumerate(order):
            near_copies.append(
                send(
                    terms_ref.at[twin, :, target],
                    near.at[place],
                    near_send.at[place],
                    near_recv.at[place],
                    {"seq": twin},
                )
            )
            copy = pltpu.make_async_copy(
                terms_ref.at[side, :, target], own.at[place], own_sems.at[place]
            )
            copy.start()
            own_copies.append(copy)
        if line:
            line.begin()
        beside = lax.rem(part + 1, 2) + part - lax.rem(part, 2)
        across = lax.rem(part + 2, 4)
        corner = 3 - part
        upper, lower = pl.ds(0, half), pl.ds(half, half)
        first_copies, second_copies = [], []

        def hand(place, index, source, target):
            return send(
                source,
                mid_in.at[place, index],
                mid_send.at[place, index],
                mid_recv.at[place, index],
                {"tensor": target},
            )

        for place in range(groups):
            near_copies[place].wait_recv()
            own_copies[place].wait()
            for slot in range(tensors):
                mid[place, slot] = (
                    own[place, slot].astype(jnp.float32) + near[place, slot].astype(jnp.float32)
                ).astype(jnp.bfloat16)
            first_copies.append(
                [
                    hand(place, 0, mid.at[place, corner, upper], beside),
                    hand(place, 1, mid.at[place, corner, lower], across),
                    hand(place, 2, mid.at[place, beside, upper], beside),
                    hand(place, 3, mid.at[place, across, lower], across),
                ]
            )
        for place in range(groups):
            if line and 0 < place < 4:
                line.steps(2)
            copies = []
            for index, slot, rows, target in ((0, across, upper, across), (1, beside, lower, beside)):
                first_copies[place][index].wait_recv()
                value = mid[place, slot, rows].astype(jnp.float32)
                value = value + mid_in[place, index].astype(jnp.float32)
                sums[place, index] = value.astype(jnp.bfloat16)
                copies.append(hand(place, 4 + index, sums.at[place, index], target))
            second_copies.append(copies)
        far_copies = []
        for place, target in enumerate(order):
            if line and place < 4:
                line.steps(2)
            copies = first_copies[place][2:] + second_copies[place]
            for copy in copies:
                copy.wait_recv()

            def joined(index):
                return mid_in[place, index].astype(jnp.float32)

            halves = [joined(2) + joined(4), joined(3) + joined(5)]
            total = mid[place, part].astype(jnp.float32) + jnp.concatenate(halves, axis=0)
            if place < groups - 1:
                far[place] = total.astype(jnp.bfloat16)
                far_copies.append(
                    send(
                        far.at[place],
                        far_in.at[place],
                        far_send.at[place],
                        far_recv.at[place],
                        {"dp": target},
                    )
                )
        if line:
            line.steps()
        for place, copy in enumerate(far_copies):
            copy.wait_recv()
            total = total + far_in[place].astype(jnp.float32)
        out_ref[...] = total
        for copy in near_copies + far_copies + [
            copy for row in first_copies + second_copies for copy in row
        ]:
            copy.wait_send()
        if line:
            line.end()

    block = (count, D)
    dma = pltpu.SemaphoreType.DMA
    return pl.pallas_call(
        kernel,
        name="reduce_all",
        out_shape=[jax.ShapeDtypeStruct(block, jnp.float32)] + ([line.out_shape] if line else []),
        in_specs=[pl.BlockSpec(memory_space=pl.ANY)] + (line.in_specs if line else []),
        out_specs=[pl.BlockSpec(memory_space=pltpu.VMEM)] + ([line.out_spec] if line else []),
        scratch_shapes=[pltpu.VMEM((groups, tensors) + block, jnp.bfloat16)] * 3
        + [
            pltpu.VMEM((groups, 2, half, D), jnp.bfloat16),
            pltpu.VMEM((groups, 6, half, D), jnp.bfloat16),
            pltpu.VMEM((groups,) + block, jnp.bfloat16),
            pltpu.VMEM((groups,) + block, jnp.bfloat16),
            dma((groups,)),
            dma((groups,)),
            dma((groups,)),
            dma((groups, 6)),
            dma((groups, 6)),
            dma((groups,)),
            dma((groups,)),
        ]
        + (line.scratch if line else []),
        cost_estimate=SHORT,
        compiler_params=pltpu.CompilerParams(
            collective_id=collective_id, has_side_effects=True, vmem_limit_bytes=56 << 20
        ),
    )(terms, *(line.operands if line else []))


def gather_all(block, collective_id, line=None):
    tensors, groups = lax.axis_size("tensor"), lax.axis_size("dp")
    half = block.shape[0] // 2

    def kernel(*refs):
        refs = list(refs)
        block_ref = refs.pop(0)
        source_refs = [refs.pop(0) for _ in line.operands] if line else []
        out = refs.pop(0)
        summed_ref = refs.pop(0) if line else None
        own_sem, far_send, far_recv, mid_send, mid_recv, near_send, near_recv = refs[:7]
        if line:
            line.bind(source_refs, summed_ref, refs[7:])
            line.load()
        group, part, side = lax.axis_index("dp"), lax.axis_index("tensor"), lax.axis_index("seq")
        twin = 1 - side
        meet(
            [{"seq": twin}]
            + [{"tensor": peer} for peer in others("tensor")]
            + [{"dp": peer} for peer in others("dp")]
        )
        far_copies = [
            send(
                block_ref,
                out.at[side, part, group],
                far_send.at[step],
                far_recv.at[step],
                {"dp": peer},
            )
            for step, peer in enumerate(others("dp"))
        ]
        own = pltpu.make_async_copy(block_ref, out.at[side, part, group], own_sem)
        own.start()
        if line:
            line.begin()
        beside = lax.rem(part + 1, 2) + part - lax.rem(part, 2)
        across = lax.rem(part + 2, 4)
        corner = 3 - part
        upper, lower = pl.ds(0, half), pl.ds(half, half)
        first_copies, second_copies, near_copies = [], [], []
        for place in range(groups):
            source = behind("dp", place)
            if place:
                far_copies[place - 1].wait_recv()
            held = out.at[side, part, source] if place else block_ref

            def hand(index, piece, slot, rows, target):
                return send(
                    piece,
                    out.at[side, slot, source, rows],
                    mid_send.at[place, index],
                    mid_recv.at[place, index],
                    {"tensor": target},
                )

            first = [
                hand(0, held.at[upper], part, upper, beside),
                hand(1, held.at[lower], part, lower, across),
                hand(2, held.at[lower], part, lower, beside),
                hand(3, held.at[upper], part, upper, across),
            ]
            near_copies.append(
                send(
                    held,
                    out.at[side, part, source],
                    near_send.at[place, 0],
                    near_recv.at[place, 0],
                    {"seq": twin},
                )
            )
            first[0].wait_recv()
            second = [hand(4, out.at[side, beside, source, upper], beside, upper, across)]
            first[1].wait_recv()
            second.append(hand(5, out.at[side, across, source, lower], across, lower, beside))
            first_copies.append(first)
            second_copies.append(second)
        for place in range(groups):
            if line and place < 4:
                line.steps(2)
            source = behind("dp", place)
            ready = [
                (beside, first_copies[place][2:3]),
                (across, first_copies[place][3:4]),
                (corner, second_copies[place]),
            ]
            for step, (slot, copies) in enumerate(ready):
                for copy in copies:
                    copy.wait_recv()
                held = out.at[side, slot, source]
                near_copies.append(
                    send(
                        held,
                        held,
                        near_send.at[place, step + 1],
                        near_recv.at[place, step + 1],
                        {"seq": twin},
                    )
                )
        if line:
            line.steps()
        for copy in near_copies:
            copy.wait_recv()
        for copy in near_copies + far_copies + [
            copy for row in first_copies + second_copies for copy in row
        ]:
            copy.wait_send()
        own.wait()
        if line:
            line.end()

    dma = pltpu.SemaphoreType.DMA
    anywhere = pl.BlockSpec(memory_space=pl.ANY)
    return pl.pallas_call(
        kernel,
        name="gather_all",
        out_shape=[jax.ShapeDtypeStruct((2, tensors, groups) + block.shape, block.dtype)]
        + ([line.out_shape] if line else []),
        in_specs=[VMEM_SPEC] + (line.in_specs if line else []),
        out_specs=[pl.BlockSpec(memory_space=pltpu.HBM)] + ([line.out_spec] if line else []),
        scratch_shapes=[
            dma,
            dma((groups - 1,)),
            dma((groups - 1,)),
            dma((groups, 6)),
            dma((groups, 6)),
            dma((groups, tensors)),
            dma((groups, tensors)),
        ]
        + (line.scratch if line else []),
        cost_estimate=SHORT,
        compiler_params=pltpu.CompilerParams(
            collective_id=collective_id, has_side_effects=True, vmem_limit_bytes=40 << 20
        ),
    )(block, *(line.operands if line else []))


def reduce_rows(terms, ids, line=None):
    count, groups = terms.shape[3], terms.shape[2]
    pieces = max(1, groups // 4)
    part = count // pieces
    sums, joined = [], None
    for i in range(pieces):
        piece = terms[:, :, :, i * part : (i + 1) * part] if pieces > 1 else terms
        if i == 0 and line:
            total, joined = reduce_all(piece, ids[1], line)
        else:
            (total,) = reduce_all(piece, ids[0])
        sums.append(total)
    return jnp.concatenate(sums, axis=0) if pieces > 1 else sums[0], joined


def join_stats(stats, collective_id):
    _, tensors, groups, _, _ = stats.shape

    def join(left, right):
        top = jnp.maximum(left[..., 0:1, :], right[..., 0:1, :])
        total = left[..., 1:2, :] * jnp.exp(left[..., 0:1, :] - top) + right[..., 1:2, :] * jnp.exp(
            right[..., 0:1, :] - top
        )
        return jnp.concatenate(
            [top, total, left[..., 2:3, :] + right[..., 2:3, :], left[..., 3:, :]], axis=-2
        )

    def kernel(
        stats_ref, home, full, near, mid, mid_in, far, far_in,
        near_send, near_recv, mid_send, mid_recv, far_send, far_recv,
    ):
        group, part, side = lax.axis_index("dp"), lax.axis_index("tensor"), lax.axis_index("seq")
        twin = 1 - side
        parts, groups_else = others("tensor"), others("dp")
        meet(
            [{"seq": twin}]
            + [{"tensor": peer} for peer in parts]
            + [{"dp": peer} for peer in groups_else]
        )
        copy = send(stats_ref.at[twin], near, near_send.at[0], near_recv.at[0], {"seq": twin})
        copy.wait()
        for slot in range(tensors):
            for spot in range(groups):
                mid[slot, spot] = join(stats_ref[side, slot, spot], near[slot, spot])
        copies = [
            send(mid.at[peer], mid_in.at[step], mid_send.at[0, step], mid_recv.at[0, step], {"tensor": peer})
            for step, peer in enumerate(parts)
        ]
        for copy in copies:
            copy.wait()
        for spot in range(groups):
            total = mid[part, spot]
            for step in range(tensors - 1):
                total = join(total, mid_in[step, spot])
            far[spot] = total
        copies = [
            send(far.at[peer], far_in.at[step], far_send.at[0, step], far_recv.at[0, step], {"dp": peer})
            for step, peer in enumerate(groups_else)
        ]
        total = far[group]
        for step, copy in enumerate(copies):
            copy.wait()
            total = join(total, far_in[step])
        log_total = total[0:1] + jnp.log(total[1:2])
        home[...] = jnp.concatenate([log_total, total[2:3], total[2:]], axis=0)
        full[side, part, group] = jnp.broadcast_to(log_total, (8, LANES))
        held = full.at[side, part, group]
        copies = [
            send(held, held, far_send.at[1, step], far_recv.at[1, step], {"dp": peer})
            for step, peer in enumerate(groups_else)
        ]
        for copy in copies:
            copy.wait()
        held = full.at[side, part]
        copies = [
            send(held, held, mid_send.at[1, step], mid_recv.at[1, step], {"tensor": peer})
            for step, peer in enumerate(parts)
        ]
        for copy in copies:
            copy.wait()
        held = full.at[side]
        send(held, held, near_send.at[1], near_recv.at[1], {"seq": twin}).wait()

    tile = (8, LANES)
    dma = pltpu.SemaphoreType.DMA
    vmem = pl.BlockSpec(memory_space=pltpu.VMEM)
    return pl.pallas_call(
        kernel,
        name="join_stats",
        out_shape=[
            jax.ShapeDtypeStruct(tile, jnp.float32),
            jax.ShapeDtypeStruct(stats.shape, jnp.float32),
        ],
        in_specs=[vmem],
        out_specs=[vmem, vmem],
        scratch_shapes=[
            pltpu.VMEM((tensors, groups) + tile, jnp.float32),
            pltpu.VMEM((tensors, groups) + tile, jnp.float32),
            pltpu.VMEM((tensors - 1, groups) + tile, jnp.float32),
            pltpu.VMEM((groups,) + tile, jnp.float32),
            pltpu.VMEM((groups - 1,) + tile, jnp.float32),
            dma((2,)),
            dma((2,)),
            dma((2, tensors - 1)),
            dma((2, tensors - 1)),
            dma((2, groups - 1)),
            dma((2, groups - 1)),
        ],
        cost_estimate=SHORT,
        compiler_params=pltpu.CompilerParams(collective_id=collective_id, has_side_effects=True),
    )(stats)


def spread_tokens(block, collective_id):
    tensors, groups = lax.axis_size("tensor"), lax.axis_size("dp")
    rows = 2 * tensors * groups

    def kernel(block_ref, ids, targets, kept, count, held, own_sem, send_sems, recv_sems):
        group, side = lax.axis_index("dp"), lax.axis_index("seq")
        peers = [
            {"dp": lax.rem(group + step // 2, groups), "seq": lax.rem(side + step % 2, 2)}
            for step in range(1, 2 * groups)
        ]
        meet(peers)
        copies = [
            send(block_ref, held.at[group, side], send_sems.at[step], recv_sems.at[step], peer)
            for step, peer in enumerate(peers)
        ]
        own = pltpu.make_async_copy(block_ref, held.at[group, side], own_sem)
        own.start()
        own.wait()
        for copy in copies:
            copy.wait()
        lane = lax.broadcasted_iota(jnp.int32, (1, LANES), 1)
        total = jnp.zeros((1, LANES), jnp.int32)
        for half in range(2):
            for source in range(groups):
                limit = held[source, half, 2 * tensors : 2 * tensors + 1, :]
                total = total + limit
                for part in range(tensors):
                    row = (half * tensors + part) * groups + source
                    ids[row] = held[source, half, part : part + 1, :]
                    targets[row] = held[source, half, tensors + part : tensors + part + 1, :]
                    kept[row] = jnp.where(lane + part * LANES < limit, 1.0, 0.0)
        count[...] = total.astype(jnp.float32)

    dma = pltpu.SemaphoreType.DMA
    vmem = pl.BlockSpec(memory_space=pltpu.VMEM)
    shape = (rows, 1, LANES)
    return pl.pallas_call(
        kernel,
        name="spread_tokens",
        out_shape=[
            jax.ShapeDtypeStruct(shape, jnp.int32),
            jax.ShapeDtypeStruct(shape, jnp.int32),
            jax.ShapeDtypeStruct(shape, jnp.float32),
            jax.ShapeDtypeStruct((1, LANES), jnp.float32),
        ],
        in_specs=[vmem],
        out_specs=[vmem] * 4,
        scratch_shapes=[
            pltpu.VMEM((groups, 2) + block.shape, jnp.int32),
            dma,
            dma((2 * groups - 1,)),
            dma((2 * groups - 1,)),
        ],
        cost_estimate=SHORT,
        compiler_params=pltpu.CompilerParams(collective_id=collective_id, has_side_effects=True),
    )(block)


def finish(gain_grads, states, grad_ys, home, keep, table_squares, layer_squares, count, smalls, collective_id):
    tensors, groups = lax.axis_size("tensor"), lax.axis_size("dp")
    block = (8, D)
    gain_rows = 2 * LAYERS + 1
    operands = list(gain_grads) + list(states) + list(grad_ys) + [
        home, keep, table_squares, layer_squares, count
    ] + list(smalls)

    def kernel(*refs):
        refs = list(refs)
        gain_refs = [refs.pop(0) for _ in gain_grads]
        state_refs = [refs.pop(0) for _ in states]
        grad_refs = [refs.pop(0) for _ in grad_ys]
        home_ref, keep_ref, table_ref, layer_ref, count_ref = [refs.pop(0) for _ in range(5)]
        small_refs = [refs.pop(0) for _ in smalls]
        out_refs = [refs.pop(0) for _ in range(8)]
        near, mid, far, near_send, near_recv, mid_send, mid_recv, far_send, far_recv = refs
        group, part, side = lax.axis_index("dp"), lax.axis_index("tensor"), lax.axis_index("seq")
        parts, groups_else = others("tensor"), others("dp")
        meet(
            [{"seq": 1 - side}]
            + [{"tensor": peer} for peer in parts]
            + [{"dp": peer} for peer in groups_else]
        )
        values = []
        for later in range(1, LAYERS + 1):
            grad = grad_refs[later - 1][...]
            for level in range(later + 1):
                values.append(jnp.sum(grad * state_refs[level][...], keepdims=True))
        loss = jnp.where(keep_ref[...] > 0.0, home_ref[0:1, :] - home_ref[1:2, :], 0.0)
        values.append(jnp.sum(loss, keepdims=True))
        values.append(jnp.sum(table_ref[...], keepdims=True) + layer_ref[...])
        lane = lax.broadcasted_iota(jnp.int32, (1, D), 1)
        row = jnp.zeros((1, D), jnp.float32)
        for place, value in enumerate(values):
            row = jnp.where(lane == place, value, row)
        blank = jnp.zeros((8 - gain_rows - 1, D), jnp.float32)
        total = jnp.concatenate([ref[...] for ref in gain_refs] + [row, blank], axis=0)
        stages = [
            ("seq", near, side, [1 - side], near_send, near_recv),
            ("tensor", mid, part, parts, mid_send, mid_recv),
            ("dp", far, group, groups_else, far_send, far_recv),
        ]
        for axis, slots, me, peers, send_sems, recv_sems in stages:
            slots[me] = total
            copies = [
                send(slots.at[me], slots.at[me], send_sems.at[step], recv_sems.at[step], {axis: peer})
                for step, peer in enumerate(peers)
            ]
            for copy in copies:
                copy.wait()
            total = slots[0]
            for index in range(1, slots.shape[0]):
                total = total + slots[index]
        gain_total = total[:gain_rows]
        row = total[gain_rows : gain_rows + 1]

        def pick(place):
            return jnp.sum(jnp.where(lane == place, row, 0.0), axis=1, keepdims=True)

        mix_squares = jnp.sum(jnp.where(lane < MIX_WEIGHTS, row * row, 0.0), axis=1, keepdims=True)
        gain_squares = jnp.sum(gain_total * gain_total, keepdims=True)
        tokens = count_ref[:, 0:1]
        clip_norm = jnp.sqrt(pick(MIX_WEIGHTS + 1) + gain_squares + mix_squares) / tokens
        factor = jnp.minimum(1.0, CLIP_NORM / clip_norm) / tokens
        gain_news = adam_update(
            *[ref[...] for ref in small_refs[:3]], gain_total * factor, RATE_SMALL, 0.0
        )
        mix_news = adam_update(
            *[ref[...] for ref in small_refs[3:]], row[:, :MIX_WEIGHTS] * factor, RATE_SMALL, 0.0
        )
        for ref, value in zip(out_refs[:6], gain_news + mix_news):
            ref[...] = value
        ends = jnp.where(lane == 0, pick(MIX_WEIGHTS), jnp.where(lane == 1, clip_norm, factor))
        out_refs[6][...] = ends[:, :LANES]
        out_refs[7][...] = jnp.broadcast_to(factor, (8, LANES))

    dma = pltpu.SemaphoreType.DMA
    vmem = pl.BlockSpec(memory_space=pltpu.VMEM)
    return pl.pallas_call(
        kernel,
        name="finish",
        out_shape=[jax.ShapeDtypeStruct(value.shape, jnp.float32) for value in smalls]
        + [
            jax.ShapeDtypeStruct((1, LANES), jnp.float32),
            jax.ShapeDtypeStruct((8, LANES), jnp.float32),
        ],
        in_specs=[vmem] * len(operands),
        out_specs=[vmem] * 8,
        scratch_shapes=[
            pltpu.VMEM((2,) + block, jnp.float32),
            pltpu.VMEM((tensors,) + block, jnp.float32),
            pltpu.VMEM((groups,) + block, jnp.float32),
            dma((1,)),
            dma((1,)),
            dma((tensors - 1,)),
            dma((tensors - 1,)),
            dma((groups - 1,)),
            dma((groups - 1,)),
        ],
        cost_estimate=SHORT,
        compiler_params=pltpu.CompilerParams(collective_id=collective_id, has_side_effects=True),
    )(*operands)


SLOT_STEP = 4


def update_slots(plan, factor, master, first, second, layer_grads, grad_table):
    slots, half_rows, _ = master.shape
    steps = -(-slots // SLOT_STEP)
    plan = jnp.pad(plan, ((0, 0), (0, steps * SLOT_STEP - slots)))

    def kernel(plan_ref, factor_ref, master_ref, first_ref, second_ref, *rest):
        layer_refs = rest[:SLOT_STEP]
        table_ref, new_master, new_first, new_second = rest[SLOT_STEP:]
        for place in range(SLOT_STEP):
            kind = plan_ref[0, pl.program_id(0) * SLOT_STEP + place]
            grad = table_ref[place * half_rows : (place + 1) * half_rows, :]
            grad = jnp.where(kind == 0, layer_refs[place][0].astype(jnp.float32), grad)
            grad = jnp.where(kind >= 0, grad * factor_ref[0:1, 0:1], 0.0)
            values = adam_update(
                master_ref[place],
                first_ref[place],
                second_ref[place],
                grad,
                RATE_MATRIX,
                DECAY_MATRIX,
            )
            for ref, value in zip((new_master, new_first, new_second), values):
                ref[place] = value

    slot = pl.BlockSpec((SLOT_STEP, half_rows, D), lambda step, plan: (step, 0, 0))
    return pl.pallas_call(
        kernel,
        name="update_slots",
        grid_spec=pltpu.PrefetchScalarGridSpec(
            num_scalar_prefetch=1,
            grid=(steps,),
            in_specs=[pl.BlockSpec((8, LANES), lambda step, plan: (0, 0)), slot, slot, slot]
            + [
                pl.BlockSpec(
                    (1, half_rows, D),
                    lambda step, plan, place=place: (plan[1, step * SLOT_STEP + place], 0, 0),
                )
                for place in range(SLOT_STEP)
            ]
            + [pl.BlockSpec((SLOT_STEP * half_rows, D), lambda step, plan: (step, 0))],
            out_specs=[slot] * 3,
        ),
        out_shape=[jax.ShapeDtypeStruct(master.shape, jnp.float32)] * 3,
        cost_estimate=SHORT,
        compiler_params=pltpu.CompilerParams(vmem_limit_bytes=48 << 20),
    )(
        plan,
        factor,
        master,
        first,
        second,
        *[layer_grads] * SLOT_STEP,
        grad_table,
    )


TILE = TILE_GROUPS * LANES
PICKED = 768


def row_of(values_ref, groups, place=0):
    rows = [values_ref[group, place : place + 1, :] for group in groups]
    return jnp.concatenate(rows, axis=1)


def tile_row(values_ref, tile):
    start = tile * TILE_GROUPS
    return row_of(values_ref, [start + place for place in range(TILE_GROUPS)])


PLAN_GROUPS = 4


def chunk_of(plan_ref, step):
    return pl.ds(pl.multiple_of(plan_ref[0] + step * ROW_STEP, 16), ROW_STEP)


def chunks_of(plan_ref):
    return (plan_ref[1] - plan_ref[0] + ROW_STEP - 1) // ROW_STEP


def whole(shape):
    return pl.BlockSpec(shape, lambda step, plan: (0,) * len(shape), pipeline_mode=pl.Buffered(1))


def last_tile(plan):
    return (plan[2] - 1) // TILE_GROUPS


def group_specs():
    return [
        pl.BlockSpec(
            (LANES, D),
            lambda step, plan, place=place: (
                plan[PLAN_GROUPS + jnp.minimum(step, last_tile(plan)) * TILE_GROUPS + place],
                0,
            ),
        )
        for place in range(TILE_GROUPS)
    ]


def powers_spec(rows):
    return pl.BlockSpec((rows, TILE), lambda step, plan: (0, jnp.minimum(step, last_tile(plan))))


def groups_of(plan_ref):
    start = PLAN_GROUPS + pl.program_id(0) * TILE_GROUPS
    return [plan_ref[start + place] for place in range(TILE_GROUPS)]


ROWS_SPEC = pl.BlockSpec((TILE, D), lambda step, plan: (step, 0))


def local_call(name, kernel, steps, plan, operands, in_specs, out_shape, out_specs, scratch):
    return pl.pallas_call(
        kernel,
        name=name,
        grid_spec=pltpu.PrefetchScalarGridSpec(
            num_scalar_prefetch=1,
            grid=(steps,),
            in_specs=in_specs,
            out_specs=out_specs,
            scratch_shapes=scratch,
        ),
        out_shape=out_shape,
        cost_estimate=SHORT,
        compiler_params=pltpu.CompilerParams(vmem_limit_bytes=60 << 20),
    )(plan, *operands)


def ones_where(condition):
    return jnp.where(condition, 1.0, 0.0).astype(jnp.bfloat16)


def picks(rank_row):
    return ones_where(lax.broadcasted_iota(jnp.int32, (PICKED, TILE), 0) == rank_row)


def rows_picked(plan_ref, step, place_row):
    start = plan_ref[0] + step * ROW_STEP
    row = lax.broadcasted_iota(jnp.int32, (ROW_STEP, PICKED), 0) + start
    return ones_where(row == place_row)


def look_up(plan, row_ids, tokens, places, table):
    rows, groups = table.shape[0], tokens.shape[0]
    steps = groups // TILE_GROUPS

    def kernel(
        plan_ref, ids_ref, tokens_ref, places_ref, table_ref, out_ref, ranks_ref, picked_ref, acc, picked
    ):
        tile = pl.program_id(0)
        few = plan_ref[3] <= PICKED

        @pl.when(tile == 0)
        def _():
            held = places_ref[...].reshape(groups, LANES) >= 0
            ones = ones_where(held)
            lane = (LANES, LANES)
            before = ones_where(
                lax.broadcasted_iota(jnp.int32, lane, 0) < lax.broadcasted_iota(jnp.int32, lane, 1)
            )
            group = (groups, groups)
            above = ones_where(
                lax.broadcasted_iota(jnp.int32, group, 1) < lax.broadcasted_iota(jnp.int32, group, 0)
            )
            totals = jnp.sum(ones.astype(jnp.float32), axis=1, keepdims=True)
            totals = jnp.broadcast_to(totals, (groups, LANES)).astype(jnp.bfloat16)
            ranks = (times(ones, before) + times(above, totals)).astype(jnp.int32)
            ranks_ref[...] = jnp.where(held, ranks, -1).reshape(groups, 1, LANES)

        @pl.when((tile == 0) & few)
        def _():
            def digits_of(step, total):
                place = tile_row(places_ref, step)
                high = lax.shift_right_arithmetic(place, 6)
                digits = jnp.concatenate([high, place - high * 64] * 4, axis=0)
                digits = digits.astype(jnp.float32).astype(jnp.bfloat16)
                return total + contract_last(digits, picks(tile_row(ranks_ref, step)))

            digits = lax.fori_loop(0, steps, digits_of, jnp.zeros((8, PICKED), jnp.float32))
            place = (digits[0:1] * 64.0 + digits[1:2]).astype(jnp.int32)
            index = lax.broadcasted_iota(jnp.int32, (1, PICKED), 1)
            place = jnp.where(index < plan_ref[3], place, -1)
            picked_ref[...] = jnp.broadcast_to(place, (8, PICKED))
            acc[:PICKED, :] = jnp.zeros((PICKED, D), jnp.float32)

            def one(step, carry):
                hits = rows_picked(plan_ref, step, place)
                acc[:PICKED, :] += contract_first(hits, table_ref[chunk_of(plan_ref, step), :])
                return carry

            lax.fori_loop(0, chunks_of(plan_ref), one, 0)
            picked[...] = acc[:PICKED, :].astype(jnp.bfloat16)

        @pl.when(few)
        def _():
            hits = picks(tile_row(ranks_ref, tile))
            out_ref[...] = contract_first(hits, picked[...]).astype(jnp.bfloat16)

        @pl.when(jnp.logical_not(few))
        def _():
            acc[...] = jnp.zeros_like(acc)
            wanted = tile_row(tokens_ref, tile)

            def one(step, carry):
                chunk = chunk_of(plan_ref, step)
                hits = ones_where(ids_ref[chunk, :] == wanted)
                acc[...] += contract_first(hits, table_ref[chunk, :])
                return carry

            lax.fori_loop(0, chunks_of(plan_ref), one, 0)
            out_ref[...] = acc[...].astype(jnp.bfloat16)

    lanes = (groups, 1, LANES)
    return local_call(
        "look_up",
        kernel,
        steps,
        plan,
        (row_ids, tokens, places, table),
        [whole((rows, 1)), whole(lanes), whole(lanes), whole((rows, D))],
        [
            jax.ShapeDtypeStruct((groups * LANES, D), jnp.bfloat16),
            jax.ShapeDtypeStruct(lanes, jnp.int32),
            jax.ShapeDtypeStruct((8, PICKED), jnp.int32),
        ],
        [ROWS_SPEC, whole(lanes), whole((8, PICKED))],
        [pltpu.VMEM((TILE, D), jnp.float32), pltpu.VMEM((PICKED, D), jnp.bfloat16)],
    )


def head_forward(plan, row_ids, labels, table, final):
    rows, groups = table.shape[0], labels.shape[0]
    steps = groups // TILE_GROUPS

    def kernel(plan_ref, ids_ref, labels_ref, table_ref, *rest):
        final_refs, (powers_ref, stats_ref, scores, hidden) = rest[:TILE_GROUPS], rest[TILE_GROUPS:]
        blank = jnp.zeros((1, TILE), jnp.float32)
        active = pl.program_id(0) <= last_tile(plan_ref)

        def put(top, total, target):
            pad = jnp.zeros((5, LANES), jnp.float32)
            for place in range(TILE_GROUPS):
                lanes = slice(place * LANES, (place + 1) * LANES)
                stats_ref[place] = jnp.concatenate(
                    [top[:, lanes], total[:, lanes], target[:, lanes], pad], axis=0
                )

        @pl.when(jnp.logical_not(active))
        def _():
            put(blank - 1e30, blank, blank)

        @pl.when(active)
        def _():
            wanted = row_of(labels_ref, groups_of(plan_ref))
            for place, ref in enumerate(final_refs):
                hidden[place * LANES : (place + 1) * LANES, :] = ref[...]

            def first(step, carry):
                top, target = carry
                chunk = chunk_of(plan_ref, step)
                ids = ids_ref[chunk, :]
                raw = contract_last(table_ref[chunk, :], hidden[...])
                raw = jnp.where(ids >= 0, raw, -1e30)
                scores[chunk, :] = raw
                top = jnp.maximum(top, jnp.max(raw, axis=0, keepdims=True))
                target = target + jnp.sum(
                    jnp.where(ids == wanted, raw, 0.0), axis=0, keepdims=True
                )
                return (top, target)

            top, target = lax.fori_loop(0, chunks_of(plan_ref), first, (blank - 1e30, blank))

            def second(step, total):
                chunk = chunk_of(plan_ref, step)
                powers = jnp.exp(scores[chunk, :] - top)
                powers_ref[chunk, :] = powers.astype(jnp.bfloat16)
                return total + jnp.sum(powers, axis=0, keepdims=True)

            put(top, lax.fori_loop(0, chunks_of(plan_ref), second, blank), target)

    return local_call(
        "head_forward",
        kernel,
        steps,
        plan,
        (row_ids, labels, table) + (final,) * TILE_GROUPS,
        [whole((rows, 1)), whole((groups, 1, LANES)), whole((rows, D))] + group_specs(),
        [
            jax.ShapeDtypeStruct((rows, groups * LANES), jnp.bfloat16),
            jax.ShapeDtypeStruct((groups, 8, LANES), jnp.float32),
        ],
        [
            powers_spec(rows),
            pl.BlockSpec((TILE_GROUPS, 8, LANES), lambda step, plan: (step, 0, 0)),
        ],
        [pltpu.VMEM((rows, TILE), jnp.float32), pltpu.VMEM((TILE, D), jnp.bfloat16)],
    )


def head_backward(plan, row_ids, labels, keep, stats, log_totals, table, final, powers):
    rows, groups = table.shape[0], labels.shape[0]
    steps = groups // TILE_GROUPS

    def kernel(plan_ref, ids_ref, labels_ref, keep_ref, stats_ref, logs_ref, table_ref, powers_ref, *rest):
        final_refs = rest[:TILE_GROUPS]
        grad_final_ref, grad_table_ref, acc, hidden, low, sems = rest[TILE_GROUPS:]
        tile = pl.program_id(0)
        slot = lax.rem(tile, 2)
        active = tile <= last_tile(plan_ref)

        def copies(step):
            start, side = PLAN_GROUPS + step * TILE_GROUPS, lax.rem(step, 2)
            return [
                pltpu.make_async_copy(
                    low.at[side, place],
                    grad_final_ref.at[plan_ref[start + place]],
                    sems.at[side, place],
                )
                for place in range(TILE_GROUPS)
            ]

        @pl.when(tile == 0)
        def _():
            grad_table_ref[...] = jnp.zeros_like(grad_table_ref)

        @pl.when(tile >= 2)
        def _():
            for copy in copies(tile - 2):
                copy.wait()

        acc[...] = jnp.zeros_like(acc)

        @pl.when(active)
        def _():
            own = groups_of(plan_ref)
            wanted, kept = row_of(labels_ref, own), row_of(keep_ref, own)
            tops = row_of(stats_ref, range(TILE_GROUPS))
            scale = jnp.exp(tops - row_of(logs_ref, own)) * kept
            for place, ref in enumerate(final_refs):
                hidden[place * LANES : (place + 1) * LANES, :] = ref[...]

            def one(step, carry):
                chunk = chunk_of(plan_ref, step)
                grads = powers_ref[chunk, :].astype(jnp.float32) * scale
                grads = grads - jnp.where(ids_ref[chunk, :] == wanted, kept, 0.0)
                grads = grads.astype(jnp.bfloat16)
                grad_table_ref[chunk, :] += times(grads, hidden[...])
                acc[...] += contract_first(grads, table_ref[chunk, :])
                return carry

            lax.fori_loop(0, chunks_of(plan_ref), one, 0)

        low[slot] = acc[...].astype(jnp.bfloat16).reshape(TILE_GROUPS, LANES, D)
        for copy in copies(tile):
            copy.start()

        @pl.when(tile == steps - 1)
        def _():
            for step in range(max(0, steps - 2), steps):
                for copy in copies(step):
                    copy.wait()

    lanes = (groups, 1, LANES)
    return local_call(
        "head_backward",
        kernel,
        steps,
        plan,
        (row_ids, labels, keep, stats, log_totals, table, powers) + (final,) * TILE_GROUPS,
        [
            whole((rows, 1)),
            whole(lanes),
            whole(lanes),
            pl.BlockSpec((TILE_GROUPS, 8, LANES), lambda step, plan: (step, 0, 0)),
            whole((groups, 8, LANES)),
            whole((rows, D)),
            powers_spec(rows),
        ]
        + group_specs(),
        [
            jax.ShapeDtypeStruct((groups, LANES, D), jnp.bfloat16),
            jax.ShapeDtypeStruct((rows, D), jnp.float32),
        ],
        [pl.BlockSpec(memory_space=pl.ANY), whole((rows, D))],
        [
            pltpu.VMEM((TILE, D), jnp.float32),
            pltpu.VMEM((TILE, D), jnp.bfloat16),
            pltpu.VMEM((2, TILE_GROUPS, LANES, D), jnp.bfloat16),
            pltpu.SemaphoreType.DMA((2, TILE_GROUPS)),
        ],
    )


def look_back(plan, row_ids, tokens, ranks, picked, grad_start, grad_table):
    rows, groups = grad_table.shape[0], tokens.shape[0]
    steps = groups // TILE_GROUPS

    def kernel(
        plan_ref, ids_ref, tokens_ref, ranks_ref, picked_ref, grad_ref, table_ref, out_ref, squares_ref, acc
    ):
        tile = pl.program_id(0)
        few = plan_ref[3] <= PICKED

        @pl.when(tile == 0)
        def _():
            acc[...] = jnp.zeros_like(acc)
            out_ref[...] = table_ref[...]

        @pl.when(few)
        def _():
            acc[...] += times(picks(tile_row(ranks_ref, tile)), grad_ref[...])

        @pl.when(jnp.logical_not(few))
        def _():
            wanted = tile_row(tokens_ref, tile)
            grads = grad_ref[...]

            def one(step, carry):
                chunk = chunk_of(plan_ref, step)
                out_ref[chunk, :] += times(ones_where(ids_ref[chunk, :] == wanted), grads)
                return carry

            lax.fori_loop(0, chunks_of(plan_ref), one, 0)

        @pl.when(few & (tile == steps - 1))
        def _():
            grads = acc[...].astype(jnp.bfloat16)
            place = picked_ref[0:1, :]

            def one(step, carry):
                out_ref[chunk_of(plan_ref, step), :] += times(
                    rows_picked(plan_ref, step, place), grads
                )
                return carry

            lax.fori_loop(0, chunks_of(plan_ref), one, 0)

        @pl.when(tile == steps - 1)
        def _():
            def square(step, total):
                values = out_ref[chunk_of(plan_ref, step), :]
                values = (values * values).reshape(ROW_STEP // 8, 8, D).sum(axis=0)
                return total + values

            squares_ref[...] = lax.fori_loop(
                0, chunks_of(plan_ref), square, jnp.zeros((8, D), jnp.float32)
            )

    lanes = (groups, 1, LANES)
    return local_call(
        "look_back",
        kernel,
        steps,
        plan,
        (row_ids, tokens, ranks, picked, grad_start, grad_table),
        [
            whole((rows, 1)),
            whole(lanes),
            whole(lanes),
            whole((8, PICKED)),
            ROWS_SPEC,
            whole((rows, D)),
        ],
        [
            jax.ShapeDtypeStruct((rows, D), jnp.float32),
            jax.ShapeDtypeStruct((8, D), jnp.float32),
        ],
        [whole((rows, D)), whole((8, D))],
        [pltpu.VMEM((PICKED, D), jnp.float32)],
    )


def body(
    token_ids,
    labels,
    real_counts,
    owners,
    master,
    first_moment,
    second_moment,
    gains,
    gains_first,
    gains_second,
    mix,
    mix_first,
    mix_second,
):
    tensors = lax.axis_size("tensor")
    groups = lax.axis_size("dp")
    group = lax.axis_index("dp")
    tensor_part = lax.axis_index("tensor")
    seq_part = lax.axis_index("seq")
    slots, half_rows, _ = master.shape
    seq_count, half_len = token_ids.shape
    row_count = seq_count * half_len
    share = row_count // tensors
    head_rows = 3 * D // tensors
    out_rows = D // tensors
    unit_rows = FF // tensors
    layer_rows = head_rows + out_rows + 2 * unit_rows
    layer_blocks = layer_rows // (2 * half_rows)
    blocks = LAYERS * layer_blocks
    vocab_rows = VOCAB // tensors
    local_heads = HEADS // tensors

    slot_rank = slot_table(owners)
    block_ids = jnp.arange(owners.shape[0], dtype=jnp.int32)
    mine = owners == group
    match = (jnp.arange(slots)[:, None] == slot_rank[None, :]) & mine[None, :]
    slot_block = jnp.sum(jnp.where(match, block_ids[None, :] + 1, 0), axis=1) - 1
    row_ids = (
        tensor_part * vocab_rows
        + (slot_block[:, None] - blocks) * (2 * half_rows)
        + seq_part * half_rows
        + jnp.arange(half_rows, dtype=jnp.int32)[None, :]
    )
    row_ids = jnp.where(slot_block[:, None] >= blocks, row_ids, -1).reshape(-1, 1)
    spare = -(-ROW_STEP // half_rows)
    row_ids = jnp.pad(row_ids, ((0, spare * half_rows), (0, 0)), constant_values=-1)
    held = jnp.sum(jnp.where(mine, 1, 0)) * half_rows
    first_held = jnp.sum(jnp.where(mine & (block_ids < blocks), 1, 0)) * half_rows
    slot_plan = jnp.stack(
        [
            jnp.where(slot_block < 0, -1, jnp.where(slot_block < blocks, 0, 1)),
            jnp.where(slot_block < blocks, jnp.maximum(slot_block, 0), 0),
        ]
    ).astype(jnp.int32)

    packed = jnp.concatenate(
        [
            token_ids.reshape(tensors, LANES),
            labels.reshape(tensors, LANES),
            jnp.broadcast_to(real_counts[:, None], (16 - 2 * tensors, LANES)),
        ],
        axis=0,
    )
    ids_all, labels_all, keep_all, count = spread_tokens(packed, 15)
    order = (2, tensors, groups, share)
    local_ids = ids_all - tensor_part * vocab_rows
    inside = (local_ids >= 0) & (local_ids < vocab_rows)
    block_of, within = local_ids // (2 * half_rows) + blocks, local_ids % (2 * half_rows)
    inside = inside & (within // half_rows == seq_part)
    same = block_of.reshape(1, -1) == jnp.where(slot_block < 0, -1, slot_block)[:, None]
    slot_of = jnp.sum(jnp.where(same, jnp.arange(1, slots + 1)[:, None], 0), axis=0)
    slot_of = slot_of.reshape(ids_all.shape) - 1
    places = jnp.where(inside & (slot_of >= 0), slot_of * half_rows + within % half_rows, -1)
    active = keep_all[:, 0, 0] > 0.0
    group_ids = jnp.arange(active.shape[0])
    earlier = group_ids[None, :] < group_ids[:, None]
    turn_of = jnp.where(
        active,
        jnp.sum(jnp.where(earlier & active[None, :], 1, 0), axis=1),
        jnp.sum(jnp.where(active, 1, 0))
        + jnp.sum(jnp.where(earlier & ~active[None, :], 1, 0), axis=1),
    )
    group_order = jnp.sum(
        jnp.where(turn_of[None, :] == group_ids[:, None], group_ids[None, :], 0), axis=1
    )
    plan = jnp.concatenate(
        [
            jnp.stack(
                [
                    first_held,
                    held,
                    jnp.sum(jnp.where(active, 1, 0)),
                    jnp.sum(jnp.where(places >= 0, 1, 0)),
                ]
            ),
            group_order,
        ]
    ).astype(jnp.int32)

    table_slots = jnp.pad(master.astype(jnp.bfloat16), ((0, spare), (0, 0), (0, 0)))
    table = table_slots.reshape(-1, D)

    halves = jnp.where(
        mine[:blocks][:, None, None], jnp.take(table_slots, slot_rank[:blocks], axis=0), 0.0
    ).astype(jnp.bfloat16)
    third = layer_blocks // 3

    def weights_line(*starts):
        return Line([(halves, start * third, third) for start in starts], True)

    def as_table(joined):
        return joined.reshape(-1, D)

    positions = seq_part * half_len + jnp.arange(row_count) % half_len
    steps_half = jnp.arange(HEAD_DIM // 2).astype(jnp.float32)
    freqs = 10000.0 ** (-2.0 * steps_half / HEAD_DIM)
    angles = freqs[:, None] * positions.astype(jnp.float32)[None, :]
    cosine, sine = jnp.cos(angles), jnp.sin(angles)

    looked, ranks, picked = look_up(plan, row_ids, ids_all, places, table)
    looked = looked.reshape(order + (D,))
    start, joined = reduce_rows(looked, (0, 14), weights_line(0, 1))
    table_one = as_table(joined)
    attention_table, up = table_one, (table_one, 1)
    tables = []
    gain = [gains[i : i + 1] for i in range(2 * LAYERS + 1)]
    piece = ((share, D), jnp.float32)

    def normed_of(total, stream, gain_row):
        return (layer_norm_parts(stream)[0] * gain_row,)

    def inner_of(total, stream, gain_row):
        inner = stream + total
        return (inner, layer_norm_parts(inner)[0] * gain_row)

    def outcome_of(base, total, inner, gain_row, *rest):
        states, scalars = rest[:-1], rest[-1]
        outcome = inner + total
        stream = scalars[base + len(states)] * outcome
        for source, state in enumerate(states):
            stream = stream + scalars[base + source] * state
        return (outcome, stream, layer_norm_parts(stream)[0] * gain_row)

    (normed,) = tensor_step("normed", normed_of, None, (start, gain[0]), (), [], True, 1)
    states, streams, inners, kept_all = [start], [start], [], []
    for level in range(LAYERS):
        here, last = 3 * level, level == LAYERS - 1
        carried = [] if last else [here + 3]
        carried += [here + 1, here + 2] if level else [here + 2]
        inner, normed_two, queries, both, logs, attended, joined = tensor_step(
            f"inner_{level}",
            inner_of,
            attention_work(normed, attention_table, cosine, sine),
            (streams[level], gain[2 * level + 1]),
            (),
            [piece],
            True,
            2 if level == 0 else 15 + level,
            weights_line(*carried),
        )
        kept = (queries, both, logs, attended)
        joined = as_table(joined)
        down = (joined, len(carried) - 1)
        up = (joined, len(carried) - 2) if level else up
        tables.append((attention_table, up, down))
        attention_table = joined
        outcome, stream, normed_next, hidden, activated = tensor_step(
            f"outcome_{level}",
            partial(outcome_of, (level + 1) * (level + 2) // 2 - 1),
            unit_work(normed_two, up, down),
            [inner, gain[2 * level + 2]] + states,
            (mix,),
            [piece, piece] + ([((share, D), jnp.bfloat16)] if last else []),
            not last,
            3 + level,
        )
        inners.append(inner)
        kept_all.append((normed, kept, normed_two, (hidden, activated)))
        states.append(outcome)
        streams.append(stream)
        normed = normed_next

    final_all = gather_all(normed, 3 + LAYERS)[0].reshape(-1, D)
    powers, stats = head_forward(plan, row_ids, labels_all, table, final_all)
    home, log_totals = join_stats(
        jnp.take(stats, turn_of, axis=0).reshape((2, tensors, groups, 8, LANES)), 4 + LAYERS
    )
    grad_final, grad_table = head_backward(
        plan,
        row_ids,
        labels_all,
        keep_all,
        stats,
        log_totals.reshape(-1, 8, LANES),
        table,
        final_all,
        powers,
    )
    grad_final, _ = reduce_rows(grad_final.reshape(order + (D,)), (0, 14))

    row = ((1, D), jnp.float32)

    def top_of(total, grad, stream, gain_row, scalars):
        grad_top, grad_gain = norm_pull(grad, gain_row, stream)
        grad_state = scalars[MIX_WEIGHTS - 1] * grad_top
        return (grad_top, grad_state, grad_gain, grad_state)

    def inner_back(total, grad_out, inner, gain_row):
        grad, grad_gain = norm_pull(total, gain_row, inner)
        grad = grad_out + grad
        return (grad, grad_gain, grad)

    def stream_back(block, total, grad_inner, stream, gain_row, *rest):
        grad_ys, scalars = rest[:-1], rest[-1]
        grad, grad_gain = norm_pull(total, gain_row, stream)
        grad = grad_inner + grad
        state = grad if block == 0 else scalars[block * (block + 1) // 2 - 1 + block] * grad
        for offset, grad_y in enumerate(grad_ys):
            later = block + 1 + offset
            state = state + scalars[later * (later + 1) // 2 - 1 + block] * grad_y
        return (grad, state, grad_gain, state)

    grad_ys = [None] * (LAYERS + 1)
    gain_grads = [None] * (2 * LAYERS + 1)
    layer_grads, attention_grads = [None] * (3 * LAYERS), None
    grad_ys[LAYERS], grad_state, gain_grads[2 * LAYERS], grad_branch = tensor_step(
        "top_back",
        top_of,
        None,
        (grad_final, streams[LAYERS], gain[2 * LAYERS]),
        (mix,),
        [piece, piece, row],
        True,
        5 + LAYERS,
    )
    for level in reversed(range(LAYERS)):
        normed, kept, normed_two, unit_kept = kept_all[level]
        attention_table, up, down = tables[level]
        grad_inner, gain_grads[2 * level + 1], grad_attn, unit_grads, *summed = tensor_step(
            f"inner_back_{level}",
            inner_back,
            unit_back_work(grad_branch, normed_two, up, down, unit_kept, half_rows),
            (grad_state, inners[level], gain[2 * level + 1]),
            (),
            [piece, row],
            True,
            6 + LAYERS if level == 0 else 19 + level,
            None if attention_grads is None else Line([(attention_grads, 0, third)], False),
        )
        if summed:
            layer_grads[3 * (level + 1)] = summed[0]
        grad_ys[level], grad_state, gain_grads[2 * level], grad_branch, attention_grads, summed = (
            tensor_step(
                f"stream_back_{level}",
                partial(stream_back, level),
                attention_back_work(
                    grad_attn, normed, attention_table, kept, cosine, sine, half_rows
                ),
                [grad_inner, streams[level], gain[2 * level]] + grad_ys[level + 1 :],
                (mix,),
                [piece, piece, row] + ([] if level else [((share, D), jnp.bfloat16)]),
                level > 0,
                7 + LAYERS + level,
                Line([(unit_grads, 0, 2 * third)], False),
            )
        )
        layer_grads[3 * level + 1] = summed

    grad_start_all, layer_grads[0] = gather_all(
        grad_branch, 13, Line([(attention_grads, 0, third)], False)
    )
    layer_grads = jnp.concatenate([grads for grads in layer_grads if grads is not None], axis=0)
    grad_start_all = grad_start_all.reshape(-1, D)
    grad_table, table_squares = look_back(
        plan, row_ids, ids_all, ranks, picked, grad_start_all, grad_table
    )
    values = layer_grads.astype(jnp.float32)
    layer_squares = jnp.sum(jnp.where(mine[:blocks][:, None, None], values * values, 0.0))
    keep = jnp.where(
        tensor_part * share + jnp.arange(share) < real_counts[0], 1.0, 0.0
    ).astype(jnp.float32)
    news = finish(
        gain_grads,
        states,
        grad_ys[1:],
        home,
        keep[None],
        table_squares,
        layer_squares.reshape(1, 1),
        count,
        (gains, gains_first, gains_second, mix[None], mix_first[None], mix_second[None]),
        7 + 2 * LAYERS,
    )
    new_gains, new_gains_first, new_gains_second = news[:3]
    new_mix, new_mix_first, new_mix_second = [value[0] for value in news[3:6]]
    loss_sum, clip_norm = news[6][0, 0], news[6][0, 1]
    token_count = count[0, 0]
    new_master, new_first, new_second = update_slots(
        slot_plan, news[7], master, first_moment, second_moment, layer_grads, grad_table
    )
    return (
        new_master,
        new_first,
        new_second,
        new_gains,
        new_gains_first,
        new_gains_second,
        new_mix,
        new_mix_first,
        new_mix_second,
        loss_sum,
        token_count,
        clip_norm,
    )


def solution(mesh):
    return jax.shard_map(
        body,
        mesh=mesh,
        in_specs=(
            P("dp", "seq"),
            P("dp", "seq"),
            P(("dp", "seq")),
            P(),
            P("dp", ("tensor", "seq"), None),
            P("dp", ("tensor", "seq"), None),
            P("dp", ("tensor", "seq"), None),
            P(),
            P(),
            P(),
            P(),
            P(),
            P(),
        ),
        out_specs=(
            P("dp", ("tensor", "seq"), None),
            P("dp", ("tensor", "seq"), None),
            P("dp", ("tensor", "seq"), None),
            P(),
            P(),
            P(),
            P(),
            P(),
            P(),
            P(),
            P(),
            P(),
        ),
        check_vma=False,
    )
```

```python
from functools import partial

import jax
import jax.numpy as jnp
from jax import lax
from jax.experimental import pallas as pl
from jax.experimental.pallas import tpu as pltpu
from jax.sharding import PartitionSpec as P

D = 768
HEADS = 12
HEAD_DIM = 64
FF = 3072
VOCAB = 50304
LAYERS = 2
STEP_COUNT = 10
MIX_WEIGHTS = 5


EPS_NORM = 1e-05
CLIP_NORM = 0.01
BETA_ONE = 0.9
BETA_TWO = 0.95
ADAM_EPS = 1e-08
RATE_MATRIX = 0.04
RATE_SMALL = 0.4
DECAY_MATRIX = 0.1


def contract_last(left, right):
    return lax.dot_general(
        left, right, (((1,), (1,)), ((), ())), preferred_element_type=jnp.float32
    )


def contract_first(left, right):
    return lax.dot_general(
        left, right, (((0,), (0,)), ((), ())), preferred_element_type=jnp.float32
    )


def slot_table(owners):
    ranks = jnp.arange(owners.shape[0])
    same = (owners[None, :] == owners[:, None]) & (ranks[None, :] < ranks[:, None])
    return jnp.sum(jnp.where(same, 1, 0), axis=1).astype(jnp.int32)


def adam_update(weight, first, second, grad, rate, decay):
    first = BETA_ONE * first + (1.0 - BETA_ONE) * grad
    second = BETA_TWO * second + (1.0 - BETA_TWO) * grad * grad
    first_hat = first / (1.0 - BETA_ONE**STEP_COUNT)
    second_hat = second / (1.0 - BETA_TWO**STEP_COUNT)
    weight = weight - rate * (first_hat / (jnp.sqrt(second_hat) + ADAM_EPS) + decay * weight)
    return (weight, first, second)


MESH = pl.DeviceIdType.MESH
ROW_STEP = 400
TILE_GROUPS = 8
LANES = 128
SHORT = pl.CostEstimate(flops=1000, bytes_accessed=1000, transcendentals=0)


def meet(peers):
    gate = pltpu.get_barrier_semaphore()
    for peer in peers:
        pl.semaphore_signal(gate, inc=1, device_id=peer, device_id_type=MESH)
    pl.semaphore_wait(gate, len(peers))


def others(axis):
    count, me = lax.axis_size(axis), lax.axis_index(axis)
    return [lax.rem(me + step, count) for step in range(1, count)]


def behind(axis, step):
    count, me = lax.axis_size(axis), lax.axis_index(axis)
    return lax.rem(me + count - step, count)


def send(source, target, send_sem, recv_sem, device):
    copy = pltpu.make_async_remote_copy(
        src_ref=source,
        dst_ref=target,
        send_sem=send_sem,
        recv_sem=recv_sem,
        device_id=device,
        device_id_type=MESH,
    )
    copy.start()
    return copy


def layer_norm_parts(stream):
    center = stream - jnp.mean(stream, -1, keepdims=True)
    inverse = lax.rsqrt(jnp.mean(center * center, -1, keepdims=True) + EPS_NORM)
    return center * inverse, inverse


def norm_pull(grad_normed, gain, stream):
    scaled, inverse = layer_norm_parts(stream)
    grad_scaled = grad_normed * gain
    grad_stream = inverse * (
        grad_scaled
        - jnp.mean(grad_scaled, -1, keepdims=True)
        - scaled * jnp.mean(grad_scaled * scaled, -1, keepdims=True)
    )
    return grad_stream, jnp.sum(grad_normed * scaled, axis=0, keepdims=True)


class Work:
    def __init__(self, before, during, operands, specs, outs, scratch, after=None, twins=False):
        self.before, self.during, self.after, self.twins = before, during, after, twins
        self.operands, self.specs, self.outs, self.scratch = operands, specs, outs, scratch


def tensor_step(name, function, work, extras, scalars, outs, gather, collective_id, line=None):
    parts = lax.axis_size("tensor")
    share = extras[0].shape[0]
    reduce = work is not None
    work = work or Work(None, None, [], [], [], [])

    def kernel(*refs):
        refs = list(refs)

        def take(count):
            return [refs.pop(0) for _ in range(count)]

        work_refs = take(len(work.operands))
        extra_refs = take(len(extras))
        scalar_refs = take(len(scalars))
        source_refs = take(len(line.operands)) if line else []
        out_refs = take(len(outs))
        (full,) = take(1) if gather else [None]
        work_outs = take(len(work.outs))
        (joined,) = take(1) if line else [None]
        send_sems, recv_sems = take(2)
        partial_ref, outgoing, arrived = take(3) if reduce else [None] * 3
        if line:
            line.bind(source_refs, joined, take(len(line.scratch)))
            line.load()

        def tick(count=1):
            if line:
                line.steps(count)

        me, side = lax.axis_index("tensor"), lax.axis_index("seq")
        peers = others("tensor")
        twin = {"seq": 1 - side}
        twins = work.twins or (line and line.share)
        meet(
            [{"tensor": peer} for peer in peers]
            + [twin] * bool(twins)
            + ([{"dp": peer} for peer in others("dp")] if line else [])
        )
        if line:
            line.begin()
        total = None
        if reduce:
            work.before(work_refs, work_outs, refs, partial_ref, tick)
            copies = []
            for step, peer in enumerate(peers):
                rows = pl.ds(pl.multiple_of(peer * share, share), share)
                outgoing[step] = partial_ref[rows, :].astype(jnp.bfloat16)
                copies.append(
                    send(
                        outgoing.at[step],
                        arrived.at[step],
                        send_sems.at[0, step],
                        recv_sems.at[0, step],
                        {"tensor": peer},
                    )
                )
            if work.during:
                work.during(work_refs, work_outs, refs)
            tick(6)
            total = partial_ref[pl.ds(pl.multiple_of(me * share, share), share), :]
            for step, copy in enumerate(copies):
                copy.wait()
                total = total + arrived[step].astype(jnp.float32)
        results = function(total, *[ref[...] for ref in extra_refs], *scalar_refs)
        for ref, value in zip(out_refs, results):
            ref[...] = value.astype(ref.dtype)
        if gather:
            full[me] = results[len(outs)].astype(jnp.bfloat16)
            copies = [
                send(
                    full.at[me],
                    full.at[me],
                    send_sems.at[1, step],
                    recv_sems.at[1, step],
                    {"tensor": peer},
                )
                for step, peer in enumerate(peers)
            ]
        if work.after:
            work.after(work_refs, work_outs, refs)
        tick(None)
        if gather:
            for copy in copies:
                copy.wait()
        if line:
            line.end()

    vmem = pl.BlockSpec(memory_space=pltpu.VMEM)
    smem = pl.BlockSpec(memory_space=pltpu.SMEM)
    shapes = [jax.ShapeDtypeStruct(shape, dtype) for shape, dtype in outs]
    if gather:
        shapes.append(jax.ShapeDtypeStruct((parts, share, D), jnp.bfloat16))
    shapes += [jax.ShapeDtypeStruct(shape, dtype) for shape, dtype in work.outs]
    out_specs = [vmem] * len(shapes)
    operands = list(work.operands) + list(extras) + list(scalars)
    in_specs = list(work.specs) + [vmem] * len(extras) + [smem] * len(scalars)
    dma = pltpu.SemaphoreType.DMA
    buffers = [dma((2, parts - 1))] * 2
    if reduce:
        buffers += [pltpu.VMEM((parts * share, D), jnp.float32)]
        buffers += [pltpu.VMEM((parts - 1, share, D), jnp.bfloat16)] * 2
    if line:
        operands += line.operands
        in_specs += line.in_specs
        shapes.append(line.out_shape)
        out_specs.append(line.out_spec)
        buffers += line.scratch
    return pl.pallas_call(
        kernel,
        name=name,
        grid=(1,),
        out_shape=shapes,
        in_specs=in_specs,
        out_specs=out_specs,
        scratch_shapes=buffers + list(work.scratch),
        cost_estimate=SHORT,
        compiler_params=pltpu.CompilerParams(
            collective_id=collective_id, has_side_effects=True, vmem_limit_bytes=50 << 20
        ),
    )(*operands)


VMEM_SPEC = pl.BlockSpec(memory_space=pltpu.VMEM)


def part_spec(rows, index):
    return pl.BlockSpec((rows, D), lambda step: (index, 0), pipeline_mode=pl.Buffered(1))


def turn(block, cosine, sine):
    half = HEAD_DIM // 2
    first, second = block[:half], block[half:]
    return jnp.concatenate(
        [first * cosine - second * sine, second * cosine + first * sine], axis=0
    )


def times(left, right):
    return jnp.dot(left, right, preferred_element_type=jnp.float32)


def scores_of(keys_values, head, queries, side):
    span = slice(head * HEAD_DIM, (head + 1) * HEAD_DIM)
    count = queries.shape[1]
    scale = HEAD_DIM ** (-0.5)
    far = contract_first(keys_values[0, 0, span, :], queries) * scale
    own = contract_first(keys_values[1, 0, span, :], queries) * scale
    key = lax.broadcasted_iota(jnp.int32, (count, count), 0)
    query = lax.broadcasted_iota(jnp.int32, (count, count), 1)
    own = jnp.where(key <= query, own, -1e30)
    far = jnp.where(query + side * (2 * count) >= 2 * count, far, -1e30)
    return far, own


def attention_work(normed, table, cosine, sine):
    parts, share, _ = normed.shape
    count = parts * share
    width = D // parts
    heads = width // HEAD_DIM

    def before(ins, outs, scratch, partial_ref, tick):
        normed_ref, qkv_ref, out_ref, cosine_ref, sine_ref = ins
        queries_ref, both, logs_ref, attended_ref = outs
        send_sem, recv_sem = scratch
        side = lax.axis_index("seq")
        cosine, sine = cosine_ref[...], sine_ref[...]
        rows = normed_ref[...].reshape(count, D)
        joined = contract_last(qkv_ref[...], rows)
        for head in range(heads):
            span = slice(head * HEAD_DIM, (head + 1) * HEAD_DIM)
            keys = joined[width + head * HEAD_DIM : width + (head + 1) * HEAD_DIM]
            both[1, 0, span, :] = turn(keys, cosine, sine).astype(jnp.bfloat16)
        both[1, 1] = joined[2 * width :].astype(jnp.bfloat16)
        copy = pltpu.make_async_remote_copy(
            src_ref=both.at[1],
            dst_ref=both.at[0],
            send_sem=send_sem,
            recv_sem=recv_sem,
            device_id={"seq": 1 - side},
            device_id_type=MESH,
        )

        copy.start()
        for head in range(heads):
            span = slice(head * HEAD_DIM, (head + 1) * HEAD_DIM)
            queries_ref[span, :] = turn(joined[span], cosine, sine).astype(jnp.bfloat16)

        copy.wait()
        for head in range(heads):
            span = slice(head * HEAD_DIM, (head + 1) * HEAD_DIM)
            far, own = scores_of(both, head, queries_ref[span, :], side)
            peak = jnp.maximum(
                jnp.max(far, axis=0, keepdims=True), jnp.max(own, axis=0, keepdims=True)
            )
            far, own = jnp.exp(far - peak), jnp.exp(own - peak)
            total = jnp.sum(far, axis=0, keepdims=True) + jnp.sum(own, axis=0, keepdims=True)
            logs_ref[head] = peak + jnp.log(total)
            inverse = 1.0 / total
            attended = times(both[0, 1, span, :], (far * inverse).astype(jnp.bfloat16))
            attended += times(both[1, 1, span, :], (own * inverse).astype(jnp.bfloat16))
            attended_ref[span, :] = attended.astype(jnp.bfloat16)
            tick(2)
        partial_ref[...] = contract_first(attended_ref[...], out_ref[...])

    low = jnp.bfloat16
    return Work(
        before,
        None,
        [normed, table, table, cosine, sine],
        [VMEM_SPEC, part_spec(3 * width, 0), part_spec(width, 3), VMEM_SPEC, VMEM_SPEC],
        [
            ((width, count), low),
            ((2, 2, width, count), low),
            ((heads, 1, count), jnp.float32),
            ((width, count), low),
        ],
        [pltpu.SemaphoreType.DMA, pltpu.SemaphoreType.DMA],
        twins=True,
    )


def fold_copy(own, near, send_sems, recv_sems, index):
    side = lax.axis_index("seq")
    return pltpu.make_async_remote_copy(
        src_ref=own.at[index, :, 1 - side],
        dst_ref=near.at[index],
        send_sem=send_sems.at[index],
        recv_sem=recv_sems.at[index],
        device_id={"seq": 1 - side},
        device_id_type=MESH,
    )


def add_halves(own, near, out, start):
    side = lax.axis_index("seq")

    def one(block, carry):
        value = own[block, side].astype(jnp.float32) + near[block].astype(jnp.float32)
        out[start + block] = value.astype(jnp.bfloat16)
        return carry

    lax.fori_loop(0, near.shape[0], one, 0)


def attention_back_work(grad, normed, table, kept, cosine, sine, half_rows):
    parts, share, _ = normed.shape
    count = parts * share
    width = D // parts
    heads = width // HEAD_DIM
    queries, both, logs, attended = kept
    blocks = 4 * width // (2 * half_rows)

    def before(ins, outs, scratch, partial_ref, tick):
        grad_ref, _, qkv_ref, out_ref, queries_ref, both, logs_ref, _, cosine_ref, sine_ref = ins
        back, came, grad_joined, send_sem, recv_sem = scratch[:5]
        side = lax.axis_index("seq")
        cosine, sine = cosine_ref[...], -sine_ref[...]
        scale = HEAD_DIM ** (-0.5)
        grads = contract_last(out_ref[...], grad_ref[...].reshape(count, D)).astype(jnp.bfloat16)
        own_grads = []
        for head in range(heads):
            span = slice(head * HEAD_DIM, (head + 1) * HEAD_DIM)
            head_queries, head_grads = queries_ref[span, :], grads[span]
            far, own = scores_of(both, head, head_queries, side)
            far, own = jnp.exp(far - logs_ref[head]), jnp.exp(own - logs_ref[head])
            far_grad = contract_first(both[0, 1, span, :], head_grads)
            own_grad = contract_first(both[1, 1, span, :], head_grads)
            mean = jnp.sum(far * far_grad, axis=0, keepdims=True)
            mean += jnp.sum(own * own_grad, axis=0, keepdims=True)
            far_grad = (far * (far_grad - mean)).astype(jnp.bfloat16)
            own_grad = (own * (own_grad - mean)).astype(jnp.bfloat16)
            far, own = far.astype(jnp.bfloat16), own.astype(jnp.bfloat16)
            back[0, span, :] = (contract_last(head_queries, far_grad) * scale).astype(jnp.bfloat16)
            back[1, span, :] = contract_last(head_grads, far).astype(jnp.bfloat16)
            query_grad = times(both[0, 0, span, :], far_grad) + times(both[1, 0, span, :], own_grad)
            grad_joined[span, :] = turn(query_grad * scale, cosine, sine).astype(jnp.bfloat16)
            own_grads.append(
                (contract_last(head_queries, own_grad) * scale, contract_last(head_grads, own))
            )
            tick(2)
        copy = send(back, came, send_sem, recv_sem, {"seq": 1 - side})
        copy.wait()
        for head, (key_grad, value_grad) in enumerate(own_grads):
            span = slice(head * HEAD_DIM, (head + 1) * HEAD_DIM)
            key_grad = key_grad + came[0, span, :].astype(jnp.float32)
            value_grad = value_grad + came[1, span, :].astype(jnp.float32)
            start = width + head * HEAD_DIM
            grad_joined[start : start + HEAD_DIM, :] = turn(key_grad, cosine, sine).astype(
                jnp.bfloat16
            )
            start += width
            grad_joined[start : start + HEAD_DIM, :] = value_grad.astype(jnp.bfloat16)
        partial_ref[...] = contract_first(grad_joined[...], qkv_ref[...])

    def during(ins, outs, scratch):
        grad_ref, normed_ref, attended_ref = ins[0], ins[1], ins[7]
        grad_joined = scratch[2]
        own, near, fold_send, fold_recv = scratch[5:]
        value = times(grad_joined[...], normed_ref[...].reshape(count, D)).astype(jnp.bfloat16)
        part = 3 * blocks // 4
        own[0, :part] = value.reshape(part, 2, half_rows, D)
        value = times(attended_ref[...], grad_ref[...].reshape(count, D)).astype(jnp.bfloat16)
        own[0, part:] = value.reshape(blocks - part, 2, half_rows, D)
        fold_copy(own, near, fold_send, fold_recv, 0).start()

    def after(ins, outs, scratch):
        own, near, fold_send, fold_recv = scratch[5:]
        fold_copy(own, near, fold_send, fold_recv, 0).wait()
        add_halves(own.at[0], near.at[0], outs[0], 0)

    low = jnp.bfloat16
    dma = pltpu.SemaphoreType.DMA
    return Work(
        before,
        during,
        [grad, normed, table, table, queries, both, logs, attended, cosine, sine],
        [VMEM_SPEC, VMEM_SPEC, part_spec(3 * width, 0), part_spec(width, 3)] + [VMEM_SPEC] * 6,
        [((blocks, half_rows, D), low)],
        [
            pltpu.VMEM((2, width, count), low),
            pltpu.VMEM((2, width, count), low),
            pltpu.VMEM((3 * width, count), low),
            dma,
            dma,
            pltpu.VMEM((1, blocks, 2, half_rows, D), low),
            pltpu.VMEM((1, blocks, half_rows, D), low),
            dma((1,)),
            dma((1,)),
        ],
        after,
        True,
    )


def gelu(hidden):
    return jax.nn.gelu(hidden, approximate=True)


def unit_work(normed, up, down):
    parts, share, _ = normed.shape
    count = parts * share
    units = FF // parts

    def before(ins, outs, scratch, partial_ref, tick):
        normed_ref, up_ref, down_ref = ins
        hidden_ref, activated_ref = outs
        hidden = contract_last(up_ref[...], normed_ref[...].reshape(count, D))
        hidden_ref[...] = hidden
        activated_ref[...] = gelu(hidden).astype(jnp.bfloat16)
        tick(2)
        partial_ref[...] = contract_first(activated_ref[...], down_ref[...])

    return Work(
        before,
        None,
        [normed, up[0], down[0]],
        [VMEM_SPEC, part_spec(units, up[1]), part_spec(units, down[1])],
        [((units, count), jnp.float32), ((units, count), jnp.bfloat16)],
        [],
    )


def unit_back_work(grad, normed, up, down, kept, half_rows):
    parts, share, _ = normed.shape
    count = parts * share
    units = FF // parts
    hidden, activated = kept
    blocks = units // (2 * half_rows)

    def before(ins, outs, scratch, partial_ref, tick):
        grad_ref, _, up_ref, down_ref, hidden_ref, _ = ins
        grad_hidden = scratch[0]
        grad_act = contract_last(down_ref[...], grad_ref[...].reshape(count, D))
        _, pull = jax.vjp(gelu, hidden_ref[...])
        grad_hidden[...] = pull(grad_act)[0].astype(jnp.bfloat16)
        tick(2)
        partial_ref[...] = contract_first(grad_hidden[...], up_ref[...])

    def during(ins, outs, scratch):
        grad_ref, normed_ref, _, _, _, activated_ref = ins
        grad_hidden, own, near, fold_send, fold_recv = scratch
        value = times(grad_hidden[...], normed_ref[...].reshape(count, D))
        own[0] = value.astype(jnp.bfloat16).reshape(own.shape[1:])
        fold_copy(own, near, fold_send, fold_recv, 0).start()
        value = times(activated_ref[...], grad_ref[...].reshape(count, D))
        own[1] = value.astype(jnp.bfloat16).reshape(own.shape[1:])
        fold_copy(own, near, fold_send, fold_recv, 1).start()

    def after(ins, outs, scratch):
        _, own, near, fold_send, fold_recv = scratch
        for index in range(2):
            fold_copy(own, near, fold_send, fold_recv, index).wait()
            add_halves(own.at[index], near.at[index], outs[0], index * blocks)

    low, dma = jnp.bfloat16, pltpu.SemaphoreType.DMA
    return Work(
        before,
        during,
        [grad, normed, up[0], down[0], hidden, activated],
        [VMEM_SPEC, VMEM_SPEC, part_spec(units, up[1]), part_spec(units, down[1])]
        + [VMEM_SPEC] * 2,
        [((2 * blocks, half_rows, D), low)],
        [
            pltpu.VMEM((units, count), low),
            pltpu.VMEM((2, blocks, 2, half_rows, D), low),
            pltpu.VMEM((2, blocks, half_rows, D), low),
            dma((2,)),
            dma((2,)),
        ],
        after,
        True,
    )


LINE_BLOCKS = 1
LINE_LAG = 3


class Line:
    def __init__(self, sources, share):
        self.groups = lax.axis_size("dp")
        self.sources, self.share = sources, share
        count = sum(size for _, _, size in sources)
        _, half_rows, _ = sources[0][0].shape
        self.half = (count, half_rows, D)
        self.chunks = count // LINE_BLOCKS
        self.operands = [array for array, _, _ in sources]
        self.in_specs = [pl.BlockSpec(memory_space=pl.ANY)] * len(sources)
        dma = pltpu.SemaphoreType.DMA
        out = (count, 2, half_rows, D) if share else self.half
        self.out_shape = jax.ShapeDtypeStruct(out, jnp.bfloat16)
        self.out_spec = pl.BlockSpec(memory_space=pl.ANY if share else pltpu.VMEM)
        self.scratch = [
            pltpu.VMEM(self.half, jnp.bfloat16),
            pltpu.VMEM((2,) + self.half, jnp.bfloat16),
            pltpu.VMEM((2,) + self.half, jnp.bfloat16),
            dma((len(sources),)),
            dma((2, self.chunks)),
            dma((2, self.chunks)),
        ]
        if share:
            self.scratch += [pltpu.VMEM(self.half, jnp.bfloat16)] + [dma((self.chunks,))] * 3

    def bind(self, source_refs, out_ref, refs):
        self.source_refs, self.out = source_refs, out_ref
        self.own, self.came, self.going, self.own_sems, self.send_sems, self.recv_sems = refs[:6]
        self.total = out_ref
        if self.share:
            self.total, self.keep_sems, self.twin_send, self.twin_recv = refs[6:]
        self.done = 0
        self.group = lax.axis_index("dp")
        self.first = jnp.where(self.group < self.groups // 2, 0, 1)

    def at(self, chunk):
        return pl.ds(chunk * LINE_BLOCKS, LINE_BLOCKS)

    def comes(self, way):
        return jnp.where(way == 0, self.group > 0, self.group < self.groups - 1)

    def goes(self, way):
        return jnp.where(way == 0, self.group < self.groups - 1, self.group > 0)

    def copy(self, source, way, chunk):
        target = jnp.where(way == 0, self.group + 1, self.group - 1)
        return pltpu.make_async_remote_copy(
            src_ref=source,
            dst_ref=self.came.at[way, self.at(chunk)],
            send_sem=self.send_sems.at[way, chunk],
            recv_sem=self.recv_sems.at[way, chunk],
            device_id={"dp": target},
            device_id_type=MESH,
        )

    def load(self):
        self.loads, place = [], 0
        for index, (ref, (_, start, size)) in enumerate(zip(self.source_refs, self.sources)):
            copy = pltpu.make_async_copy(
                ref.at[pl.ds(start, size)], self.own.at[pl.ds(place, size)], self.own_sems.at[index]
            )
            copy.start()
            self.loads.append(copy)
            place += size

    def begin(self):
        for copy in self.loads:
            copy.wait()
        for way in range(2):

            @pl.when(jnp.logical_not(self.comes(way)))
            def _():
                self.came[way] = jnp.zeros(self.half, jnp.bfloat16)

                def start(chunk, carry):
                    self.copy(self.own.at[self.at(chunk)], way, chunk).start()
                    return carry

                lax.fori_loop(0, self.chunks, start, 0)

    def twin_copy(self, chunk):
        side = lax.axis_index("seq")
        return pltpu.make_async_remote_copy(
            src_ref=self.total.at[self.at(chunk)],
            dst_ref=self.out.at[self.at(chunk), side],
            send_sem=self.twin_send.at[chunk],
            recv_sem=self.twin_recv.at[chunk],
            device_id={"seq": 1 - side},
            device_id_type=MESH,
        )

    def keep_copy(self, chunk):
        return pltpu.make_async_copy(
            self.total.at[self.at(chunk)],
            self.out.at[self.at(chunk), lax.axis_index("seq")],
            self.keep_sems.at[chunk],
        )

    def pass_on(self, way, chunk):
        rows = self.at(chunk)

        @pl.when(self.comes(way))
        def _():
            copy = self.copy(self.going.at[way, rows], way, chunk)
            copy.wait_recv()

            @pl.when(self.goes(way))
            def _():
                value = self.own[rows].astype(jnp.float32) + self.came[way, rows].astype(jnp.float32)
                self.going[way, rows] = value.astype(jnp.bfloat16)
                copy.start()

    def step(self, index):
        @pl.when(index < self.chunks)
        def _():
            self.pass_on(self.first, index)

        @pl.when(index >= LINE_LAG)
        def _():
            chunk = index - LINE_LAG
            rows = self.at(chunk)
            self.pass_on(1 - self.first, chunk)
            value = self.own[rows].astype(jnp.float32)
            value = value + self.came[0, rows].astype(jnp.float32)
            value = value + self.came[1, rows].astype(jnp.float32)
            self.total[rows] = value.astype(jnp.bfloat16)
            if self.share:
                self.keep_copy(chunk).start()
                self.twin_copy(chunk).start()

    def steps(self, count=None):
        last = self.chunks + LINE_LAG
        stop = last if count is None else min(self.done + count, last)

        def one(index, carry):
            self.step(index)
            return carry

        lax.fori_loop(self.done, stop, one, 0)
        self.done = stop

    def end(self):
        def one(chunk, carry):
            for way in range(2):

                @pl.when(self.goes(way))
                def _():
                    self.copy(self.going.at[way, self.at(chunk)], way, chunk).wait_send()

            if self.share:
                self.keep_copy(chunk).wait()
                self.twin_copy(chunk).wait()
            return carry

        lax.fori_loop(0, self.chunks, one, 0)


def reduce_all(terms, collective_id, line=None, tail=None):
    _, tensors, groups, count, _ = terms.shape
    half = count // 2
    function, extras, scalars, outs = tail or (None, [], [], [])
    extra_specs = [VMEM_SPEC] * len(extras)
    extra_specs += [pl.BlockSpec(memory_space=pltpu.SMEM)] * len(scalars)
    extras = list(extras) + list(scalars)

    def kernel(*refs):
        refs = list(refs)
        terms_ref = refs.pop(0)
        source_refs = [refs.pop(0) for _ in line.operands] if line else []
        extra_refs = [refs.pop(0) for _ in extras]
        out_refs = [refs.pop(0) for _ in range(len(outs) or 1)]
        full = refs.pop(0) if tail else None
        joined_ref = refs.pop(0) if line else None
        tail_sems = [refs.pop(0) for _ in range(2)] if tail else None
        (
            near, own, mid, sums, mid_in, far, far_in,
            own_sems, near_send, near_recv, mid_send, mid_recv, far_send, far_recv,
        ) = refs[:14]
        if line:
            line.bind(source_refs, joined_ref, refs[14:])
            line.load()
        group, part, side = lax.axis_index("dp"), lax.axis_index("tensor"), lax.axis_index("seq")
        twin = 1 - side
        parts = others("tensor")
        order = others("dp") + [group]
        meet(
            [{"seq": twin}]
            + [{"tensor": peer} for peer in parts]
            + [{"dp": peer} for peer in order[:-1]]
        )
        waits, near_copies, own_copies = [], [], []
        for place, target in enumerate(order):
            near_copies.append(
                send(
                    terms_ref.at[twin, :, target],
                    near.at[place],
                    near_send.at[place],
                    near_recv.at[place],
                    {"seq": twin},
                )
            )
            copy = pltpu.make_async_copy(
                terms_ref.at[side, :, target], own.at[place], own_sems.at[place]
            )
            copy.start()
            own_copies.append(copy)
        if line:
            line.begin()
        beside = lax.rem(part + 1, 2) + part - lax.rem(part, 2)
        across = lax.rem(part + 2, 4)
        corner = 3 - part
        upper, lower = pl.ds(0, half), pl.ds(half, half)
        first_copies, second_copies = [], []

        def hand(place, index, source, target):
            return send(
                source,
                mid_in.at[place, index],
                mid_send.at[place, index],
                mid_recv.at[place, index],
                {"tensor": target},
            )

        for place in range(groups):
            near_copies[place].wait_recv()
            own_copies[place].wait()
            for slot in range(tensors):
                mid[place, slot] = (
                    own[place, slot].astype(jnp.float32) + near[place, slot].astype(jnp.float32)
                ).astype(jnp.bfloat16)
            first_copies.append(
                [
                    hand(place, 0, mid.at[place, corner, upper], beside),
                    hand(place, 1, mid.at[place, corner, lower], across),
                    hand(place, 2, mid.at[place, beside, upper], beside),
                    hand(place, 3, mid.at[place, across, lower], across),
                ]
            )
        for place in range(groups):
            if line and 0 < place < 4:
                line.steps(2)
            copies = []
            for index, slot, rows, target in ((0, across, upper, across), (1, beside, lower, beside)):
                first_copies[place][index].wait_recv()
                value = mid[place, slot, rows].astype(jnp.float32)
                value = value + mid_in[place, index].astype(jnp.float32)
                sums[place, index] = value.astype(jnp.bfloat16)
                copies.append(hand(place, 4 + index, sums.at[place, index], target))
            second_copies.append(copies)
        far_copies = []
        for place, target in enumerate(order):
            if line and place < 4:
                line.steps(2)
            copies = first_copies[place][2:] + second_copies[place]
            for copy in copies:
                copy.wait_recv()

            def joined(index):
                return mid_in[place, index].astype(jnp.float32)

            halves = [joined(2) + joined(4), joined(3) + joined(5)]
            total = mid[place, part].astype(jnp.float32) + jnp.concatenate(halves, axis=0)
            if place < groups - 1:
                far[place] = total.astype(jnp.bfloat16)
                far_copies.append(
                    send(
                        far.at[place],
                        far_in.at[place],
                        far_send.at[place],
                        far_recv.at[place],
                        {"dp": target},
                    )
                )
        if line:
            line.steps()
        for place, copy in enumerate(far_copies):
            copy.wait_recv()
            total = total + far_in[place].astype(jnp.float32)
        if tail:
            results = function(total, *extra_refs)
            for ref, value in zip(out_refs, results):
                ref[...] = value
            full[part] = results[len(outs)].astype(jnp.bfloat16)
            last_copies = [
                send(
                    full.at[part],
                    full.at[part],
                    tail_sems[0].at[step],
                    tail_sems[1].at[step],
                    {"tensor": peer},
                )
                for step, peer in enumerate(parts)
            ]
            for copy in last_copies:
                copy.wait()
        else:
            out_refs[0][...] = total
        for copy in near_copies + far_copies + [
            copy for row in first_copies + second_copies for copy in row
        ]:
            copy.wait_send()
        if line:
            line.end()

    block = (count, D)
    dma = pltpu.SemaphoreType.DMA
    results = [jax.ShapeDtypeStruct(*out) for out in outs]
    if tail:
        results.append(jax.ShapeDtypeStruct((tensors,) + block, jnp.bfloat16))
    else:
        results.append(jax.ShapeDtypeStruct(block, jnp.float32))
    return pl.pallas_call(
        kernel,
        name="reduce_all",
        out_shape=results + ([line.out_shape] if line else []),
        in_specs=[pl.BlockSpec(memory_space=pl.ANY)] + (line.in_specs if line else []) + extra_specs,
        out_specs=[VMEM_SPEC] * len(results) + ([line.out_spec] if line else []),
        scratch_shapes=[dma((tensors - 1,))] * (2 if tail else 0)
        + [pltpu.VMEM((groups, tensors) + block, jnp.bfloat16)] * 3
        + [
            pltpu.VMEM((groups, 2, half, D), jnp.bfloat16),
            pltpu.VMEM((groups, 6, half, D), jnp.bfloat16),
            pltpu.VMEM((groups,) + block, jnp.bfloat16),
            pltpu.VMEM((groups,) + block, jnp.bfloat16),
            dma((groups,)),
            dma((groups,)),
            dma((groups,)),
            dma((groups, 6)),
            dma((groups, 6)),
            dma((groups,)),
            dma((groups,)),
        ]
        + (line.scratch if line else []),
        cost_estimate=SHORT,
        compiler_params=pltpu.CompilerParams(
            collective_id=collective_id, has_side_effects=True, vmem_limit_bytes=56 << 20
        ),
    )(terms, *(line.operands if line else []), *extras)


def gather_all(block, collective_id, line=None):
    tensors, groups = lax.axis_size("tensor"), lax.axis_size("dp")
    half = block.shape[0] // 2

    def kernel(*refs):
        refs = list(refs)
        block_ref = refs.pop(0)
        source_refs = [refs.pop(0) for _ in line.operands] if line else []
        out = refs.pop(0)
        summed_ref = refs.pop(0) if line else None
        own_sem, far_send, far_recv, mid_send, mid_recv, near_send, near_recv = refs[:7]
        if line:
            line.bind(source_refs, summed_ref, refs[7:])
            line.load()
        group, part, side = lax.axis_index("dp"), lax.axis_index("tensor"), lax.axis_index("seq")
        twin = 1 - side
        meet(
            [{"seq": twin}]
            + [{"tensor": peer} for peer in others("tensor")]
            + [{"dp": peer} for peer in others("dp")]
        )
        far_copies = [
            send(
                block_ref,
                out.at[side, part, group],
                far_send.at[step],
                far_recv.at[step],
                {"dp": peer},
            )
            for step, peer in enumerate(others("dp"))
        ]
        own = pltpu.make_async_copy(block_ref, out.at[side, part, group], own_sem)
        own.start()
        if line:
            line.begin()
        beside = lax.rem(part + 1, 2) + part - lax.rem(part, 2)
        across = lax.rem(part + 2, 4)
        corner = 3 - part
        upper, lower = pl.ds(0, half), pl.ds(half, half)
        first_copies, second_copies, near_copies = [], [], []
        for place in range(groups):
            source = behind("dp", place)
            if place:
                far_copies[place - 1].wait_recv()
            held = out.at[side, part, source] if place else block_ref

            def hand(index, piece, slot, rows, target):
                return send(
                    piece,
                    out.at[side, slot, source, rows],
                    mid_send.at[place, index],
                    mid_recv.at[place, index],
                    {"tensor": target},
                )

            first = [
                hand(0, held.at[upper], part, upper, beside),
                hand(1, held.at[lower], part, lower, across),
                hand(2, held.at[lower], part, lower, beside),
                hand(3, held.at[upper], part, upper, across),
            ]
            near_copies.append(
                send(
                    held,
                    out.at[side, part, source],
                    near_send.at[place, 0],
                    near_recv.at[place, 0],
                    {"seq": twin},
                )
            )
            first[0].wait_recv()
            second = [hand(4, out.at[side, beside, source, upper], beside, upper, across)]
            first[1].wait_recv()
            second.append(hand(5, out.at[side, across, source, lower], across, lower, beside))
            first_copies.append(first)
            second_copies.append(second)
        for place in range(groups):
            if line and place < 4:
                line.steps(2)
            source = behind("dp", place)
            ready = [
                (beside, first_copies[place][2:3]),
                (across, first_copies[place][3:4]),
                (corner, second_copies[place]),
            ]
            for step, (slot, copies) in enumerate(ready):
                for copy in copies:
                    copy.wait_recv()
                held = out.at[side, slot, source]
                near_copies.append(
                    send(
                        held,
                        held,
                        near_send.at[place, step + 1],
                        near_recv.at[place, step + 1],
                        {"seq": twin},
                    )
                )
        if line:
            line.steps()
        for copy in near_copies:
            copy.wait_recv()
        for copy in near_copies + far_copies + [
            copy for row in first_copies + second_copies for copy in row
        ]:
            copy.wait_send()
        own.wait()
        if line:
            line.end()

    dma = pltpu.SemaphoreType.DMA
    anywhere = pl.BlockSpec(memory_space=pl.ANY)
    return pl.pallas_call(
        kernel,
        name="gather_all",
        out_shape=[jax.ShapeDtypeStruct((2, tensors, groups) + block.shape, block.dtype)]
        + ([line.out_shape] if line else []),
        in_specs=[VMEM_SPEC] + (line.in_specs if line else []),
        out_specs=[pl.BlockSpec(memory_space=pltpu.HBM)] + ([line.out_spec] if line else []),
        scratch_shapes=[
            dma,
            dma((groups - 1,)),
            dma((groups - 1,)),
            dma((groups, 6)),
            dma((groups, 6)),
            dma((groups, tensors)),
            dma((groups, tensors)),
        ]
        + (line.scratch if line else []),
        cost_estimate=SHORT,
        compiler_params=pltpu.CompilerParams(
            collective_id=collective_id, has_side_effects=True, vmem_limit_bytes=60 << 20
        ),
    )(block, *(line.operands if line else []))


def reduce_rows(name, terms, ids, line, function, extras, scalars, outs):
    count, groups = terms.shape[3], terms.shape[2]
    pieces = max(1, groups // 4)
    if pieces == 1:
        return reduce_all(terms, ids[0], line, (function, extras, scalars, outs))
    part = count // pieces
    sums, joined = [], []
    for i in range(pieces):
        piece = terms[:, :, :, i * part : (i + 1) * part]
        total, *joined_now = reduce_all(piece, ids[1 if i and line else 0], None if i else line)
        sums.append(total)
        joined += joined_now
    total = jnp.concatenate(sums, axis=0)
    results = tensor_step(
        name,
        lambda _, total_ref, *refs: function(total_ref, *refs),
        None,
        [total] + list(extras),
        scalars,
        outs,
        True,
        ids[2],
    )
    return list(results) + joined


def join_stats(stats, collective_id):
    _, tensors, groups, _, _ = stats.shape

    def join(left, right):
        top = jnp.maximum(left[..., 0:1, :], right[..., 0:1, :])
        total = left[..., 1:2, :] * jnp.exp(left[..., 0:1, :] - top) + right[..., 1:2, :] * jnp.exp(
            right[..., 0:1, :] - top
        )
        return jnp.concatenate(
            [top, total, left[..., 2:3, :] + right[..., 2:3, :], left[..., 3:, :]], axis=-2
        )

    def kernel(
        stats_ref, home, full, near, mid, mid_in, far, far_in,
        near_send, near_recv, mid_send, mid_recv, far_send, far_recv,
    ):
        group, part, side = lax.axis_index("dp"), lax.axis_index("tensor"), lax.axis_index("seq")
        twin = 1 - side
        parts, groups_else = others("tensor"), others("dp")
        meet(
            [{"seq": twin}]
            + [{"tensor": peer} for peer in parts]
            + [{"dp": peer} for peer in groups_else]
        )
        copy = send(stats_ref.at[twin], near, near_send.at[0], near_recv.at[0], {"seq": twin})
        copy.wait()
        for slot in range(tensors):
            for spot in range(groups):
                mid[slot, spot] = join(stats_ref[side, slot, spot], near[slot, spot])
        copies = [
            send(mid.at[peer], mid_in.at[step], mid_send.at[0, step], mid_recv.at[0, step], {"tensor": peer})
            for step, peer in enumerate(parts)
        ]
        for copy in copies:
            copy.wait()
        for spot in range(groups):
            total = mid[part, spot]
            for step in range(tensors - 1):
                total = join(total, mid_in[step, spot])
            far[spot] = total
        copies = [
            send(far.at[peer], far_in.at[step], far_send.at[0, step], far_recv.at[0, step], {"dp": peer})
            for step, peer in enumerate(groups_else)
        ]
        total = far[group]
        for step, copy in enumerate(copies):
            copy.wait()
            total = join(total, far_in[step])
        log_total = total[0:1] + jnp.log(total[1:2])
        home[...] = jnp.concatenate([log_total, total[2:3], total[2:]], axis=0)
        full[side, part, group] = jnp.broadcast_to(log_total, (8, LANES))
        held = full.at[side, part, group]
        copies = [
            send(held, held, far_send.at[1, step], far_recv.at[1, step], {"dp": peer})
            for step, peer in enumerate(groups_else)
        ]
        for copy in copies:
            copy.wait()
        held = full.at[side, part]
        copies = [
            send(held, held, mid_send.at[1, step], mid_recv.at[1, step], {"tensor": peer})
            for step, peer in enumerate(parts)
        ]
        for copy in copies:
            copy.wait()
        held = full.at[side]
        send(held, held, near_send.at[1], near_recv.at[1], {"seq": twin}).wait()

    tile = (8, LANES)
    dma = pltpu.SemaphoreType.DMA
    vmem = pl.BlockSpec(memory_space=pltpu.VMEM)
    return pl.pallas_call(
        kernel,
        name="join_stats",
        out_shape=[
            jax.ShapeDtypeStruct(tile, jnp.float32),
            jax.ShapeDtypeStruct(stats.shape, jnp.float32),
        ],
        in_specs=[vmem],
        out_specs=[vmem, vmem],
        scratch_shapes=[
            pltpu.VMEM((tensors, groups) + tile, jnp.float32),
            pltpu.VMEM((tensors, groups) + tile, jnp.float32),
            pltpu.VMEM((tensors - 1, groups) + tile, jnp.float32),
            pltpu.VMEM((groups,) + tile, jnp.float32),
            pltpu.VMEM((groups - 1,) + tile, jnp.float32),
            dma((2,)),
            dma((2,)),
            dma((2, tensors - 1)),
            dma((2, tensors - 1)),
            dma((2, groups - 1)),
            dma((2, groups - 1)),
        ],
        cost_estimate=SHORT,
        compiler_params=pltpu.CompilerParams(collective_id=collective_id, has_side_effects=True),
    )(stats)


def spread_tokens(block, collective_id):
    tensors, groups = lax.axis_size("tensor"), lax.axis_size("dp")
    rows = 2 * tensors * groups

    def kernel(block_ref, ids, targets, kept, count, held, own_sem, send_sems, recv_sems):
        group, side = lax.axis_index("dp"), lax.axis_index("seq")
        peers = [
            {"dp": lax.rem(group + step // 2, groups), "seq": lax.rem(side + step % 2, 2)}
            for step in range(1, 2 * groups)
        ]
        meet(peers)
        copies = [
            send(block_ref, held.at[group, side], send_sems.at[step], recv_sems.at[step], peer)
            for step, peer in enumerate(peers)
        ]
        own = pltpu.make_async_copy(block_ref, held.at[group, side], own_sem)
        own.start()
        own.wait()
        for copy in copies:
            copy.wait()
        lane = lax.broadcasted_iota(jnp.int32, (1, LANES), 1)
        total = jnp.zeros((1, LANES), jnp.int32)
        for half in range(2):
            for source in range(groups):
                limit = held[source, half, 2 * tensors : 2 * tensors + 1, :]
                total = total + limit
                for part in range(tensors):
                    row = (half * tensors + part) * groups + source
                    ids[row] = held[source, half, part : part + 1, :]
                    targets[row] = held[source, half, tensors + part : tensors + part + 1, :]
                    kept[row] = jnp.where(lane + part * LANES < limit, 1.0, 0.0)
        count[...] = total.astype(jnp.float32)

    dma = pltpu.SemaphoreType.DMA
    vmem = pl.BlockSpec(memory_space=pltpu.VMEM)
    shape = (rows, 1, LANES)
    return pl.pallas_call(
        kernel,
        name="spread_tokens",
        out_shape=[
            jax.ShapeDtypeStruct(shape, jnp.int32),
            jax.ShapeDtypeStruct(shape, jnp.int32),
            jax.ShapeDtypeStruct(shape, jnp.float32),
            jax.ShapeDtypeStruct((1, LANES), jnp.float32),
        ],
        in_specs=[vmem],
        out_specs=[vmem] * 4,
        scratch_shapes=[
            pltpu.VMEM((groups, 2) + block.shape, jnp.int32),
            dma,
            dma((2 * groups - 1,)),
            dma((2 * groups - 1,)),
        ],
        cost_estimate=SHORT,
        compiler_params=pltpu.CompilerParams(collective_id=collective_id, has_side_effects=True),
    )(block)


def finish(gain_grads, states, grad_ys, home, keep, table_squares, count, smalls, collective_id):
    tensors, groups = lax.axis_size("tensor"), lax.axis_size("dp")
    block = (8, D)
    gain_rows = 2 * LAYERS + 1
    operands = list(gain_grads) + list(states) + list(grad_ys) + [
        home, keep, table_squares, count
    ] + list(smalls)

    def kernel(*refs):
        refs = list(refs)
        gain_refs = [refs.pop(0) for _ in gain_grads]
        state_refs = [refs.pop(0) for _ in states]
        grad_refs = [refs.pop(0) for _ in grad_ys]
        home_ref, keep_ref, table_ref, count_ref = [refs.pop(0) for _ in range(4)]
        small_refs = [refs.pop(0) for _ in smalls]
        out_refs = [refs.pop(0) for _ in range(8)]
        near, mid, far, near_send, near_recv, mid_send, mid_recv, far_send, far_recv = refs
        group, part, side = lax.axis_index("dp"), lax.axis_index("tensor"), lax.axis_index("seq")
        parts, groups_else = others("tensor"), others("dp")
        meet(
            [{"seq": 1 - side}]
            + [{"tensor": peer} for peer in parts]
            + [{"dp": peer} for peer in groups_else]
        )
        values = []
        for later in range(1, LAYERS + 1):
            grad = grad_refs[later - 1][...]
            for level in range(later + 1):
                values.append(jnp.sum(grad * state_refs[level][...], keepdims=True))
        loss = jnp.where(keep_ref[...] > 0.0, home_ref[0:1, :] - home_ref[1:2, :], 0.0)
        values.append(jnp.sum(loss, keepdims=True))
        values.append(jnp.sum(table_ref[...], keepdims=True))
        lane = lax.broadcasted_iota(jnp.int32, (1, D), 1)
        row = jnp.zeros((1, D), jnp.float32)
        for place, value in enumerate(values):
            row = jnp.where(lane == place, value, row)
        blank = jnp.zeros((8 - gain_rows - 1, D), jnp.float32)
        total = jnp.concatenate([ref[...] for ref in gain_refs] + [row, blank], axis=0)
        stages = [
            ("seq", near, side, [1 - side], near_send, near_recv),
            ("tensor", mid, part, parts, mid_send, mid_recv),
            ("dp", far, group, groups_else, far_send, far_recv),
        ]
        for axis, slots, me, peers, send_sems, recv_sems in stages:
            slots[me] = total
            copies = [
                send(slots.at[me], slots.at[me], send_sems.at[step], recv_sems.at[step], {axis: peer})
                for step, peer in enumerate(peers)
            ]
            for copy in copies:
                copy.wait()
            total = slots[0]
            for index in range(1, slots.shape[0]):
                total = total + slots[index]
        gain_total = total[:gain_rows]
        row = total[gain_rows : gain_rows + 1]

        def pick(place):
            return jnp.sum(jnp.where(lane == place, row, 0.0), axis=1, keepdims=True)

        mix_squares = jnp.sum(jnp.where(lane < MIX_WEIGHTS, row * row, 0.0), axis=1, keepdims=True)
        gain_squares = jnp.sum(gain_total * gain_total, keepdims=True)
        tokens = count_ref[:, 0:1]
        clip_norm = jnp.sqrt(pick(MIX_WEIGHTS + 1) + gain_squares + mix_squares) / tokens
        factor = jnp.minimum(1.0, CLIP_NORM / clip_norm) / tokens
        gain_news = adam_update(
            *[ref[...] for ref in small_refs[:3]], gain_total * factor, RATE_SMALL, 0.0
        )
        mix_news = adam_update(
            *[ref[...] for ref in small_refs[3:]], row[:, :MIX_WEIGHTS] * factor, RATE_SMALL, 0.0
        )
        for ref, value in zip(out_refs[:6], gain_news + mix_news):
            ref[...] = value
        ends = jnp.where(lane == 0, pick(MIX_WEIGHTS), jnp.where(lane == 1, clip_norm, factor))
        out_refs[6][...] = ends[:, :LANES]
        out_refs[7][...] = jnp.broadcast_to(factor, (8, LANES))

    dma = pltpu.SemaphoreType.DMA
    vmem = pl.BlockSpec(memory_space=pltpu.VMEM)
    return pl.pallas_call(
        kernel,
        name="finish",
        out_shape=[jax.ShapeDtypeStruct(value.shape, jnp.float32) for value in smalls]
        + [
            jax.ShapeDtypeStruct((1, LANES), jnp.float32),
            jax.ShapeDtypeStruct((8, LANES), jnp.float32),
        ],
        in_specs=[vmem] * len(operands),
        out_specs=[vmem] * 8,
        scratch_shapes=[
            pltpu.VMEM((2,) + block, jnp.float32),
            pltpu.VMEM((tensors,) + block, jnp.float32),
            pltpu.VMEM((groups,) + block, jnp.float32),
            dma((1,)),
            dma((1,)),
            dma((tensors - 1,)),
            dma((tensors - 1,)),
            dma((groups - 1,)),
            dma((groups - 1,)),
        ],
        cost_estimate=SHORT,
        compiler_params=pltpu.CompilerParams(collective_id=collective_id, has_side_effects=True),
    )(*operands)


SLOT_STEP = 8
PREPARE_STEP = 20


def prepare(slot_block, master, blocks):
    slots, half_rows, _ = master.shape
    total = slot_block.shape[0]
    steps = -(-total // PREPARE_STEP)
    slot_block = jnp.pad(slot_block, (0, steps * PREPARE_STEP - total), constant_values=-1)
    rows = PREPARE_STEP * half_rows

    def kernel(plan_ref, master_ref, table_ref, halves_ref):
        @pl.when(pl.program_id(0) == 0)
        def _():
            halves_ref[...] = jnp.zeros_like(halves_ref)

        for place in range(PREPARE_STEP):
            slot = pl.program_id(0) * PREPARE_STEP + place
            value = jnp.where(slot < slots, master_ref[place], 0.0).astype(jnp.bfloat16)
            table_ref[place * half_rows : (place + 1) * half_rows, :] = value

            block = plan_ref[slot]

            @pl.when((block >= 0) & (block < blocks))
            def _():
                halves_ref[block] = value

    last = (slots - 1) // PREPARE_STEP
    return pl.pallas_call(
        kernel,
        name="prepare",
        grid_spec=pltpu.PrefetchScalarGridSpec(
            num_scalar_prefetch=1,
            grid=(steps,),
            in_specs=[
                pl.BlockSpec(
                    (PREPARE_STEP, half_rows, D), lambda step, plan: (jnp.minimum(step, last), 0, 0)
                )
            ],
            out_specs=[
                pl.BlockSpec((rows, D), lambda step, plan: (step, 0)),
                pl.BlockSpec((blocks, half_rows, D), lambda step, plan: (0, 0, 0)),
            ],
        ),
        out_shape=[
            jax.ShapeDtypeStruct((total * half_rows, D), jnp.bfloat16),
            jax.ShapeDtypeStruct((blocks, half_rows, D), jnp.bfloat16),
        ],
        cost_estimate=SHORT,
        compiler_params=pltpu.CompilerParams(vmem_limit_bytes=60 << 20),
    )(slot_block, master)


TILE = TILE_GROUPS * LANES
PICKED = 768


def row_of(values_ref, groups, place=0):
    rows = [values_ref[group, place : place + 1, :] for group in groups]
    return jnp.concatenate(rows, axis=1)


def tile_row(values_ref, tile):
    start = tile * TILE_GROUPS
    return row_of(values_ref, [start + place for place in range(TILE_GROUPS)])


PLAN_GROUPS = 4


def chunk_of(plan_ref, step):
    return pl.ds(pl.multiple_of(plan_ref[0] + step * ROW_STEP, 16), ROW_STEP)


def chunks_of(plan_ref):
    return (plan_ref[1] - plan_ref[0] + ROW_STEP - 1) // ROW_STEP


def whole(shape):
    return pl.BlockSpec(shape, lambda step, plan: (0,) * len(shape), pipeline_mode=pl.Buffered(1))


def last_tile(plan):
    return (plan[2] - 1) // TILE_GROUPS


def group_specs():
    return [
        pl.BlockSpec(
            (LANES, D),
            lambda step, plan, place=place: (
                plan[PLAN_GROUPS + jnp.minimum(step, last_tile(plan)) * TILE_GROUPS + place],
                0,
            ),
        )
        for place in range(TILE_GROUPS)
    ]


def powers_spec(rows):
    return pl.BlockSpec((rows, TILE), lambda step, plan: (0, jnp.minimum(step, last_tile(plan))))


def groups_of(plan_ref):
    start = PLAN_GROUPS + pl.program_id(0) * TILE_GROUPS
    return [plan_ref[start + place] for place in range(TILE_GROUPS)]


ROWS_SPEC = pl.BlockSpec((TILE, D), lambda step, plan: (step, 0))


def local_call(name, kernel, steps, plan, operands, in_specs, out_shape, out_specs, scratch):
    return pl.pallas_call(
        kernel,
        name=name,
        grid_spec=pltpu.PrefetchScalarGridSpec(
            num_scalar_prefetch=1,
            grid=(steps,),
            in_specs=in_specs,
            out_specs=out_specs,
            scratch_shapes=scratch,
        ),
        out_shape=out_shape,
        cost_estimate=SHORT,
        compiler_params=pltpu.CompilerParams(vmem_limit_bytes=60 << 20),
    )(plan, *operands)


def ones_where(condition):
    return jnp.where(condition, 1.0, 0.0).astype(jnp.bfloat16)


def picks(rank_row):
    return ones_where(lax.broadcasted_iota(jnp.int32, (PICKED, TILE), 0) == rank_row)


def rows_picked(plan_ref, step, place_row):
    start = plan_ref[0] + step * ROW_STEP
    row = lax.broadcasted_iota(jnp.int32, (ROW_STEP, PICKED), 0) + start
    return ones_where(row == place_row)


def look_up(plan, row_ids, tokens, places, table):
    rows, groups = table.shape[0], tokens.shape[0]
    steps = groups // TILE_GROUPS

    def kernel(
        plan_ref, ids_ref, tokens_ref, places_ref, table_ref, out_ref, ranks_ref, picked_ref, acc, picked
    ):
        tile = pl.program_id(0)
        few = plan_ref[3] <= PICKED

        @pl.when(tile == 0)
        def _():
            held = places_ref[...].reshape(groups, LANES) >= 0
            ones = ones_where(held)
            lane = (LANES, LANES)
            before = ones_where(
                lax.broadcasted_iota(jnp.int32, lane, 0) < lax.broadcasted_iota(jnp.int32, lane, 1)
            )
            group = (groups, groups)
            above = ones_where(
                lax.broadcasted_iota(jnp.int32, group, 1) < lax.broadcasted_iota(jnp.int32, group, 0)
            )
            totals = jnp.sum(ones.astype(jnp.float32), axis=1, keepdims=True)
            totals = jnp.broadcast_to(totals, (groups, LANES)).astype(jnp.bfloat16)
            ranks = (times(ones, before) + times(above, totals)).astype(jnp.int32)
            ranks_ref[...] = jnp.where(held, ranks, -1).reshape(groups, 1, LANES)

        @pl.when((tile == 0) & few)
        def _():
            def digits_of(step, total):
                place = tile_row(places_ref, step)
                high = lax.shift_right_arithmetic(place, 6)
                digits = jnp.concatenate([high, place - high * 64] * 4, axis=0)
                digits = digits.astype(jnp.float32).astype(jnp.bfloat16)
                return total + contract_last(digits, picks(tile_row(ranks_ref, step)))

            digits = lax.fori_loop(0, steps, digits_of, jnp.zeros((8, PICKED), jnp.float32))
            place = (digits[0:1] * 64.0 + digits[1:2]).astype(jnp.int32)
            index = lax.broadcasted_iota(jnp.int32, (1, PICKED), 1)
            place = jnp.where(index < plan_ref[3], place, -1)
            picked_ref[...] = jnp.broadcast_to(place, (8, PICKED))
            acc[:PICKED, :] = jnp.zeros((PICKED, D), jnp.float32)

            def one(step, carry):
                hits = rows_picked(plan_ref, step, place)
                acc[:PICKED, :] += contract_first(hits, table_ref[chunk_of(plan_ref, step), :])
                return carry

            lax.fori_loop(0, chunks_of(plan_ref), one, 0)
            picked[...] = acc[:PICKED, :].astype(jnp.bfloat16)

        @pl.when(few)
        def _():
            hits = picks(tile_row(ranks_ref, tile))
            out_ref[...] = contract_first(hits, picked[...]).astype(jnp.bfloat16)

        @pl.when(jnp.logical_not(few))
        def _():
            acc[...] = jnp.zeros_like(acc)
            wanted = tile_row(tokens_ref, tile)

            def one(step, carry):
                chunk = chunk_of(plan_ref, step)
                hits = ones_where(ids_ref[chunk, :] == wanted)
                acc[...] += contract_first(hits, table_ref[chunk, :])
                return carry

            lax.fori_loop(0, chunks_of(plan_ref), one, 0)
            out_ref[...] = acc[...].astype(jnp.bfloat16)

    lanes = (groups, 1, LANES)
    return local_call(
        "look_up",
        kernel,
        steps,
        plan,
        (row_ids, tokens, places, table),
        [whole((rows, 1)), whole(lanes), whole(lanes), whole((rows, D))],
        [
            jax.ShapeDtypeStruct((groups * LANES, D), jnp.bfloat16),
            jax.ShapeDtypeStruct(lanes, jnp.int32),
            jax.ShapeDtypeStruct((8, PICKED), jnp.int32),
        ],
        [ROWS_SPEC, whole(lanes), whole((8, PICKED))],
        [pltpu.VMEM((TILE, D), jnp.float32), pltpu.VMEM((PICKED, D), jnp.bfloat16)],
    )


def head_forward(plan, row_ids, labels, table, final):
    rows, groups = table.shape[0], labels.shape[0]
    steps = groups // TILE_GROUPS

    def kernel(plan_ref, ids_ref, labels_ref, table_ref, *rest):
        final_refs, (powers_ref, stats_ref, scores, hidden) = rest[:TILE_GROUPS], rest[TILE_GROUPS:]
        blank = jnp.zeros((1, TILE), jnp.float32)
        active = pl.program_id(0) <= last_tile(plan_ref)

        def put(top, total, target):
            pad = jnp.zeros((5, LANES), jnp.float32)
            for place in range(TILE_GROUPS):
                lanes = slice(place * LANES, (place + 1) * LANES)
                stats_ref[place] = jnp.concatenate(
                    [top[:, lanes], total[:, lanes], target[:, lanes], pad], axis=0
                )

        @pl.when(jnp.logical_not(active))
        def _():
            put(blank - 1e30, blank, blank)

        @pl.when(active)
        def _():
            wanted = row_of(labels_ref, groups_of(plan_ref))
            for place, ref in enumerate(final_refs):
                hidden[place * LANES : (place + 1) * LANES, :] = ref[...]

            def first(step, carry):
                top, target = carry
                chunk = chunk_of(plan_ref, step)
                ids = ids_ref[chunk, :]
                raw = contract_last(table_ref[chunk, :], hidden[...])
                raw = jnp.where(ids >= 0, raw, -1e30)
                scores[chunk, :] = raw
                top = jnp.maximum(top, jnp.max(raw, axis=0, keepdims=True))
                target = target + jnp.sum(
                    jnp.where(ids == wanted, raw, 0.0), axis=0, keepdims=True
                )
                return (top, target)

            top, target = lax.fori_loop(0, chunks_of(plan_ref), first, (blank - 1e30, blank))

            def second(step, total):
                chunk = chunk_of(plan_ref, step)
                powers = jnp.exp(scores[chunk, :] - top)
                powers_ref[chunk, :] = powers.astype(jnp.bfloat16)
                return total + jnp.sum(powers, axis=0, keepdims=True)

            put(top, lax.fori_loop(0, chunks_of(plan_ref), second, blank), target)

    return local_call(
        "head_forward",
        kernel,
        steps,
        plan,
        (row_ids, labels, table) + (final,) * TILE_GROUPS,
        [whole((rows, 1)), whole((groups, 1, LANES)), whole((rows, D))] + group_specs(),
        [
            jax.ShapeDtypeStruct((rows, groups * LANES), jnp.bfloat16),
            jax.ShapeDtypeStruct((groups, 8, LANES), jnp.float32),
        ],
        [
            powers_spec(rows),
            pl.BlockSpec((TILE_GROUPS, 8, LANES), lambda step, plan: (step, 0, 0)),
        ],
        [pltpu.VMEM((rows, TILE), jnp.float32), pltpu.VMEM((TILE, D), jnp.bfloat16)],
    )


def head_backward(plan, row_ids, labels, keep, stats, log_totals, table, final, powers):
    rows, groups = table.shape[0], labels.shape[0]
    steps = groups // TILE_GROUPS

    def kernel(plan_ref, ids_ref, labels_ref, keep_ref, stats_ref, logs_ref, table_ref, powers_ref, *rest):
        final_refs = rest[:TILE_GROUPS]
        grad_final_ref, grad_table_ref, acc, hidden, low, sems = rest[TILE_GROUPS:]
        tile = pl.program_id(0)
        slot = lax.rem(tile, 2)
        active = tile <= last_tile(plan_ref)

        def copies(step):
            start, side = PLAN_GROUPS + step * TILE_GROUPS, lax.rem(step, 2)
            return [
                pltpu.make_async_copy(
                    low.at[side, place],
                    grad_final_ref.at[plan_ref[start + place]],
                    sems.at[side, place],
                )
                for place in range(TILE_GROUPS)
            ]

        @pl.when(tile == 0)
        def _():
            grad_table_ref[...] = jnp.zeros_like(grad_table_ref)

        @pl.when(tile >= 2)
        def _():
            for copy in copies(tile - 2):
                copy.wait()

        acc[...] = jnp.zeros_like(acc)

        @pl.when(active)
        def _():
            own = groups_of(plan_ref)
            wanted, kept = row_of(labels_ref, own), row_of(keep_ref, own)
            tops = row_of(stats_ref, range(TILE_GROUPS))
            scale = jnp.exp(tops - row_of(logs_ref, own)) * kept
            for place, ref in enumerate(final_refs):
                hidden[place * LANES : (place + 1) * LANES, :] = ref[...]

            def one(step, carry):
                chunk = chunk_of(plan_ref, step)
                grads = powers_ref[chunk, :].astype(jnp.float32) * scale
                grads = grads - jnp.where(ids_ref[chunk, :] == wanted, kept, 0.0)
                grads = grads.astype(jnp.bfloat16)
                grad_table_ref[chunk, :] += times(grads, hidden[...])
                acc[...] += contract_first(grads, table_ref[chunk, :])
                return carry

            lax.fori_loop(0, chunks_of(plan_ref), one, 0)

        low[slot] = acc[...].astype(jnp.bfloat16).reshape(TILE_GROUPS, LANES, D)
        for copy in copies(tile):
            copy.start()

        @pl.when(tile == steps - 1)
        def _():
            for step in range(max(0, steps - 2), steps):
                for copy in copies(step):
                    copy.wait()

    lanes = (groups, 1, LANES)
    return local_call(
        "head_backward",
        kernel,
        steps,
        plan,
        (row_ids, labels, keep, stats, log_totals, table, powers) + (final,) * TILE_GROUPS,
        [
            whole((rows, 1)),
            whole(lanes),
            whole(lanes),
            pl.BlockSpec((TILE_GROUPS, 8, LANES), lambda step, plan: (step, 0, 0)),
            whole((groups, 8, LANES)),
            whole((rows, D)),
            powers_spec(rows),
        ]
        + group_specs(),
        [
            jax.ShapeDtypeStruct((groups, LANES, D), jnp.bfloat16),
            jax.ShapeDtypeStruct((rows, D), jnp.float32),
        ],
        [pl.BlockSpec(memory_space=pl.ANY), whole((rows, D))],
        [
            pltpu.VMEM((TILE, D), jnp.float32),
            pltpu.VMEM((TILE, D), jnp.bfloat16),
            pltpu.VMEM((2, TILE_GROUPS, LANES, D), jnp.bfloat16),
            pltpu.SemaphoreType.DMA((2, TILE_GROUPS)),
        ],
    )


def look_back(
    plan, slot_plan, slots, row_ids, tokens, ranks, picked, grad_start, grad_table, layer_grads
):
    rows, groups = grad_table.shape[0], tokens.shape[0]
    steps = groups // TILE_GROUPS
    half_rows = layer_grads[0].shape[1]
    block = SLOT_STEP * half_rows
    kinds = len(layer_grads)

    def kernel(plan_ref, slot_ref, ids_ref, tokens_ref, ranks_ref, picked_ref, grad_ref, table_ref, *rest):
        layer_refs = rest[:kinds]
        slots_ref, squares_ref, acc, held, out_ref = rest[kinds:]
        step = pl.program_id(0)
        few = plan_ref[3] <= PICKED

        @pl.when(step == 0)
        def _():
            acc[...] = jnp.zeros_like(acc)
            squares_ref[...] = jnp.zeros_like(squares_ref)

        @pl.when((step < steps) & few)
        def _():
            acc[...] += times(picks(tile_row(ranks_ref, step)), grad_ref[...])

        @pl.when((step < steps) & jnp.logical_not(few))
        def _():
            held[step] = grad_ref[...]

        @pl.when(step >= steps)
        def _():
            start = (step - steps) * block

            @pl.when(few)
            def _():
                row = lax.broadcasted_iota(jnp.int32, (block, PICKED), 0) + start
                hits = ones_where(row == picked_ref[0:1, :])
                out_ref[...] = table_ref[...] + times(hits, acc[...].astype(jnp.bfloat16))

            @pl.when(jnp.logical_not(few))
            def _():
                out_ref[...] = table_ref[...]
                ids = ids_ref[pl.ds(pl.multiple_of(start, 16), block), :]

                def one(tile, carry):
                    hits = ones_where(ids == tile_row(tokens_ref, tile))
                    out_ref[...] += times(hits, held[tile])
                    return carry

                lax.fori_loop(0, steps, one, 0)

            for place in range(SLOT_STEP):
                slot = (step - steps) * SLOT_STEP + place
                kind = slot_ref[0, slot]
                part = slice(place * half_rows, (place + 1) * half_rows)

                for index in range(kinds):

                    @pl.when(kind == index)
                    def _():
                        layer = layer_refs[index][slot_ref[1 + index, slot]]
                        out_ref[part, :] = layer.astype(jnp.float32)

                @pl.when(kind < 0)
                def _():
                    out_ref[part, :] = jnp.zeros((half_rows, D), jnp.float32)

                slots_ref[place] = out_ref[part, :]

            values = out_ref[...]
            squares_ref[...] += (values * values).reshape(block // 8, 8, D).sum(axis=0)

    def fixed(shape):
        return pl.BlockSpec(
            shape, lambda step, plan, slot: (0,) * len(shape), pipeline_mode=pl.Buffered(1)
        )

    lanes = (groups, 1, LANES)
    row_spec = pl.BlockSpec((block, D), lambda step, plan, slot: (jnp.maximum(step - steps, 0), 0))
    return pl.pallas_call(
        kernel,
        name="look_back",
        grid_spec=pltpu.PrefetchScalarGridSpec(
            num_scalar_prefetch=2,
            grid=(steps + -(-slots // SLOT_STEP),),
            in_specs=[
                fixed((rows, 1)),
                fixed(lanes),
                fixed(lanes),
                fixed((8, PICKED)),
                pl.BlockSpec((TILE, D), lambda step, plan, slot: (jnp.minimum(step, steps - 1), 0)),
                row_spec,
            ]
            + [fixed(grads.shape) for grads in layer_grads],
            out_specs=[
                pl.BlockSpec(
                    (SLOT_STEP, half_rows, D),
                    lambda step, plan, slot: (jnp.maximum(step - steps, 0), 0, 0),
                ),
                fixed((8, D)),
            ],
            scratch_shapes=[
                pltpu.VMEM((PICKED, D), jnp.float32),
                pltpu.VMEM((steps, TILE, D), jnp.bfloat16),
                pltpu.VMEM((block, D), jnp.float32),
            ],
        ),
        out_shape=[
            jax.ShapeDtypeStruct((slots, half_rows, D), jnp.float32),
            jax.ShapeDtypeStruct((8, D), jnp.float32),
        ],
        cost_estimate=SHORT,
        compiler_params=pltpu.CompilerParams(vmem_limit_bytes=60 << 20),
    )(
        plan,
        slot_plan,
        row_ids,
        tokens,
        ranks,
        picked,
        grad_start,
        grad_table,
        *layer_grads,
    )


def grads_home(level):
    if level == 0:
        return [(0, 1), (1, 0), (0, 0)]
    return [(2 * level, 0), (2 * level + 1, 0), (2 * level + 1, 1)]


def body(
    token_ids,
    labels,
    real_counts,
    owners,
    master,
    first_moment,
    second_moment,
    gains,
    gains_first,
    gains_second,
    mix,
    mix_first,
    mix_second,
):
    tensors = lax.axis_size("tensor")
    groups = lax.axis_size("dp")
    group = lax.axis_index("dp")
    tensor_part = lax.axis_index("tensor")
    seq_part = lax.axis_index("seq")
    slots, half_rows, _ = master.shape
    seq_count, half_len = token_ids.shape
    row_count = seq_count * half_len
    share = row_count // tensors
    head_rows = 3 * D // tensors
    out_rows = D // tensors
    unit_rows = FF // tensors
    layer_rows = head_rows + out_rows + 2 * unit_rows
    layer_blocks = layer_rows // (2 * half_rows)
    blocks = LAYERS * layer_blocks
    vocab_rows = VOCAB // tensors
    local_heads = HEADS // tensors

    slot_rank = slot_table(owners)
    block_ids = jnp.arange(owners.shape[0], dtype=jnp.int32)
    mine = owners == group
    match = (jnp.arange(slots)[:, None] == slot_rank[None, :]) & mine[None, :]
    slot_block = jnp.sum(jnp.where(match, block_ids[None, :] + 1, 0), axis=1) - 1
    row_ids = (
        tensor_part * vocab_rows
        + (slot_block[:, None] - blocks) * (2 * half_rows)
        + seq_part * half_rows
        + jnp.arange(half_rows, dtype=jnp.int32)[None, :]
    )
    row_ids = jnp.where(slot_block[:, None] >= blocks, row_ids, -1).reshape(-1, 1)
    spare = -(-ROW_STEP // half_rows)
    spare += -(slots + spare) % SLOT_STEP
    row_ids = jnp.pad(row_ids, ((0, spare * half_rows), (0, 0)), constant_values=-1)
    held = jnp.sum(jnp.where(mine, 1, 0)) * half_rows
    first_held = jnp.sum(jnp.where(mine & (block_ids < blocks), 1, 0)) * half_rows
    slot_block_all = jnp.pad(slot_block, (0, spare), constant_values=-1).astype(jnp.int32)
    third = layer_blocks // 3
    which, within = slot_block_all // third, slot_block_all % third
    homes = [home for level in range(LAYERS) for home in grads_home(level)]
    arrays = 1 + max(array for array, _ in homes)
    kind, index = jnp.full(which.shape, -1), jnp.zeros_like(which)
    for place, (array, part) in enumerate(homes):
        kind = jnp.where(which == place, array, kind)
        index = jnp.where(which == place, within + part * third, index)
    kind = jnp.where(slot_block_all >= blocks, arrays, jnp.where(slot_block_all < 0, -1, kind))
    slot_plan = jnp.stack(
        [kind] + [jnp.where(kind == array, index, 0) for array in range(arrays)]
    ).astype(jnp.int32)

    packed = jnp.concatenate(
        [
            token_ids.reshape(tensors, LANES),
            labels.reshape(tensors, LANES),
            jnp.broadcast_to(real_counts[:, None], (16 - 2 * tensors, LANES)),
        ],
        axis=0,
    )
    ids_all, labels_all, keep_all, count = spread_tokens(packed, 15)
    order = (2, tensors, groups, share)
    local_ids = ids_all - tensor_part * vocab_rows
    inside = (local_ids >= 0) & (local_ids < vocab_rows)
    block_of, within = local_ids // (2 * half_rows) + blocks, local_ids % (2 * half_rows)
    inside = inside & (within // half_rows == seq_part)
    same = block_of.reshape(1, -1) == jnp.where(slot_block < 0, -1, slot_block)[:, None]
    slot_of = jnp.sum(jnp.where(same, jnp.arange(1, slots + 1)[:, None], 0), axis=0)
    slot_of = slot_of.reshape(ids_all.shape) - 1
    places = jnp.where(inside & (slot_of >= 0), slot_of * half_rows + within % half_rows, -1)
    active = keep_all[:, 0, 0] > 0.0
    group_ids = jnp.arange(active.shape[0])
    earlier = group_ids[None, :] < group_ids[:, None]
    turn_of = jnp.where(
        active,
        jnp.sum(jnp.where(earlier & active[None, :], 1, 0), axis=1),
        jnp.sum(jnp.where(active, 1, 0))
        + jnp.sum(jnp.where(earlier & ~active[None, :], 1, 0), axis=1),
    )
    group_order = jnp.sum(
        jnp.where(turn_of[None, :] == group_ids[:, None], group_ids[None, :], 0), axis=1
    )
    plan = jnp.concatenate(
        [
            jnp.stack(
                [
                    first_held,
                    held,
                    jnp.sum(jnp.where(active, 1, 0)),
                    jnp.sum(jnp.where(places >= 0, 1, 0)),
                ]
            ),
            group_order,
        ]
    ).astype(jnp.int32)

    table, halves = prepare(slot_block_all, master, blocks)

    def weights_line(*starts):
        return Line([(halves, start * third, third) for start in starts], True)

    def as_table(joined):
        return joined.reshape(-1, D)

    positions = seq_part * half_len + jnp.arange(row_count) % half_len
    steps_half = jnp.arange(HEAD_DIM // 2).astype(jnp.float32)
    freqs = 10000.0 ** (-2.0 * steps_half / HEAD_DIM)
    angles = freqs[:, None] * positions.astype(jnp.float32)[None, :]
    cosine, sine = jnp.cos(angles), jnp.sin(angles)

    looked, ranks, picked = look_up(plan, row_ids, ids_all, places, table)
    looked = looked.reshape(order + (D,))
    gain = [gains[i : i + 1] for i in range(2 * LAYERS + 1)]
    piece = ((share, D), jnp.float32)

    def normed_of(total, gain_row):
        return (total[...], layer_norm_parts(total[...])[0] * gain_row[...])

    def inner_of(total, stream, gain_row):
        inner = stream + total
        return (inner, layer_norm_parts(inner)[0] * gain_row)

    def outcome_of(base, total, inner, gain_row, *rest):
        states, scalars = rest[:-1], rest[-1]
        outcome = inner + total
        stream = scalars[base + len(states)] * outcome
        for source, state in enumerate(states):
            stream = stream + scalars[base + source] * state
        return (outcome, stream, layer_norm_parts(stream)[0] * gain_row)

    start, normed, joined = reduce_rows(
        "normed", looked, (14, 18, 1), weights_line(0, 1), normed_of, [gain[0]], [], [piece]
    )
    table_one = as_table(joined)
    attention_table, up = table_one, (table_one, 1)
    tables = []
    states, streams, inners, kept_all = [start], [start], [], []
    for level in range(LAYERS):
        here, last = 3 * level, level == LAYERS - 1
        carried = [here + 1, here + 2] if level else [here + 2]
        inner, normed_two, queries, both, logs, attended, joined = tensor_step(
            f"inner_{level}",
            inner_of,
            attention_work(normed, attention_table, cosine, sine),
            (streams[level], gain[2 * level + 1]),
            (),
            [piece],
            True,
            2 if level == 0 else 15 + level,
            weights_line(*carried),
        )
        kept = (queries, both, logs, attended)
        joined = as_table(joined)
        down = (joined, len(carried) - 1)
        up = (joined, len(carried) - 2) if level else up
        tables.append((attention_table, up, down))
        outcome, stream, normed_next, hidden, activated, *joined = tensor_step(
            f"outcome_{level}",
            partial(outcome_of, (level + 1) * (level + 2) // 2 - 1),
            unit_work(normed_two, up, down),
            [inner, gain[2 * level + 2]] + states,
            (mix,),
            [piece, piece] + ([((share, D), jnp.bfloat16)] if last else []),
            not last,
            3 + level,
            None if last else weights_line(here + 3),
        )
        attention_table = None if last else as_table(joined[0])
        inners.append(inner)
        kept_all.append((normed, kept, normed_two, (hidden, activated)))
        states.append(outcome)
        streams.append(stream)
        normed = normed_next

    final_all = gather_all(normed, 3 + LAYERS)[0].reshape(-1, D)
    powers, stats = head_forward(plan, row_ids, labels_all, table, final_all)
    home, log_totals = join_stats(
        jnp.take(stats, turn_of, axis=0).reshape((2, tensors, groups, 8, LANES)), 4 + LAYERS
    )
    grad_final, grad_table = head_backward(
        plan,
        row_ids,
        labels_all,
        keep_all,
        stats,
        log_totals.reshape(-1, 8, LANES),
        table,
        final_all,
        powers,
    )
    grad_final = grad_final.reshape(order + (D,))

    row = ((1, D), jnp.float32)

    def top_of(total, stream, gain_row, scalars):
        grad_top, grad_gain = norm_pull(total[...], gain_row[...], stream[...])
        grad_state = scalars[MIX_WEIGHTS - 1] * grad_top
        return (grad_top, grad_state, grad_gain, grad_state)

    def inner_back(total, grad_out, inner, gain_row):
        grad, grad_gain = norm_pull(total, gain_row, inner)
        grad = grad_out + grad
        return (grad, grad_gain, grad)

    def stream_back(block, total, grad_inner, stream, gain_row, *rest):
        grad_ys, scalars = rest[:-1], rest[-1]
        grad, grad_gain = norm_pull(total, gain_row, stream)
        grad = grad_inner + grad
        state = grad if block == 0 else scalars[block * (block + 1) // 2 - 1 + block] * grad
        for offset, grad_y in enumerate(grad_ys):
            later = block + 1 + offset
            state = state + scalars[later * (later + 1) // 2 - 1 + block] * grad_y
        return (grad, state, grad_gain, state)

    grad_ys = [None] * (LAYERS + 1)
    gain_grads = [None] * (2 * LAYERS + 1)
    layer_grads, attention_grads = [None] * (2 * LAYERS), None
    grad_ys[LAYERS], grad_state, gain_grads[2 * LAYERS], grad_branch = reduce_rows(
        "top_back",
        grad_final,
        (0, 0, 5 + LAYERS),
        None,
        top_of,
        [streams[LAYERS], gain[2 * LAYERS]],
        [mix],
        [piece, piece, row],
    )
    for level in reversed(range(LAYERS)):
        normed, kept, normed_two, unit_kept = kept_all[level]
        attention_table, up, down = tables[level]
        grad_inner, gain_grads[2 * level + 1], grad_attn, unit_grads, *summed = tensor_step(
            f"inner_back_{level}",
            inner_back,
            unit_back_work(grad_branch, normed_two, up, down, unit_kept, half_rows),
            (grad_state, inners[level], gain[2 * level + 1]),
            (),
            [piece, row],
            True,
            6 + LAYERS if level == 0 else 19 + level,
            None if attention_grads is None else Line([(attention_grads, 0, third)], False),
        )
        if summed:
            layer_grads[2 * (level + 1)] = summed[0]
        grad_ys[level], grad_state, gain_grads[2 * level], grad_branch, attention_grads, summed = (
            tensor_step(
                f"stream_back_{level}",
                partial(stream_back, level),
                attention_back_work(
                    grad_attn, normed, attention_table, kept, cosine, sine, half_rows
                ),
                [grad_inner, streams[level], gain[2 * level]] + grad_ys[level + 1 :],
                (mix,),
                [piece, piece, row] + ([] if level else [((share, D), jnp.bfloat16)]),
                level > 0,
                7 + LAYERS + level,
                Line([(unit_grads, 0, 2 * third if level else third)], False),
            )
        )
        layer_grads[2 * level + 1] = summed

    grad_start_all, layer_grads[0] = gather_all(
        grad_branch, 13, Line([(unit_grads, third, third), (attention_grads, 0, third)], False)
    )
    grad_start_all = grad_start_all.reshape(-1, D)
    owned, table_squares = look_back(
        plan,
        slot_plan,
        slots,
        row_ids,
        ids_all,
        ranks,
        picked,
        grad_start_all,
        grad_table,
        layer_grads,
    )
    keep = jnp.where(
        tensor_part * share + jnp.arange(share) < real_counts[0], 1.0, 0.0
    ).astype(jnp.float32)
    news = finish(
        gain_grads,
        states,
        grad_ys[1:],
        home,
        keep[None],
        table_squares,
        count,
        (gains, gains_first, gains_second, mix[None], mix_first[None], mix_second[None]),
        7 + 2 * LAYERS,
    )
    new_gains, new_gains_first, new_gains_second = news[:3]
    new_mix, new_mix_first, new_mix_second = [value[0] for value in news[3:6]]
    loss_sum, clip_norm = news[6][0, 0], news[6][0, 1]
    token_count = count[0, 0]
    owned = owned * news[7][0, 0]
    new_master, new_first, new_second = adam_update(
        master, first_moment, second_moment, owned, RATE_MATRIX, DECAY_MATRIX
    )
    return (
        new_master,
        new_first,
        new_second,
        new_gains,
        new_gains_first,
        new_gains_second,
        new_mix,
        new_mix_first,
        new_mix_second,
        loss_sum,
        token_count,
        clip_norm,
    )


def solution(mesh):
    return jax.shard_map(
        body,
        mesh=mesh,
        in_specs=(
            P("dp", "seq"),
            P("dp", "seq"),
            P(("dp", "seq")),
            P(),
            P("dp", ("tensor", "seq"), None),
            P("dp", ("tensor", "seq"), None),
            P("dp", ("tensor", "seq"), None),
            P(),
            P(),
            P(),
            P(),
            P(),
            P(),
        ),
        out_specs=(
            P("dp", ("tensor", "seq"), None),
            P("dp", ("tensor", "seq"), None),
            P("dp", ("tensor", "seq"), None),
            P(),
            P(),
            P(),
            P(),
            P(),
            P(),
            P(),
            P(),
            P(),
        ),
        check_vma=False,
    )
```

```python
from functools import partial

import jax
import jax.numpy as jnp
from jax import lax
from jax.experimental import pallas as pl
from jax.experimental.pallas import tpu as pltpu
from jax.sharding import PartitionSpec as P

D = 768
HEADS = 12
HEAD_DIM = 64
FF = 3072
VOCAB = 50304
LAYERS = 2
STEP_COUNT = 10
MIX_WEIGHTS = 5


EPS_NORM = 1e-05
CLIP_NORM = 0.01
BETA_ONE = 0.9
BETA_TWO = 0.95
ADAM_EPS = 1e-08
RATE_MATRIX = 0.04
RATE_SMALL = 0.4
DECAY_MATRIX = 0.1


def contract_last(left, right):
    return lax.dot_general(
        left, right, (((1,), (1,)), ((), ())), preferred_element_type=jnp.float32
    )


def contract_first(left, right):
    return lax.dot_general(
        left, right, (((0,), (0,)), ((), ())), preferred_element_type=jnp.float32
    )


def slot_table(owners):
    ranks = jnp.arange(owners.shape[0])
    same = (owners[None, :] == owners[:, None]) & (ranks[None, :] < ranks[:, None])
    return jnp.sum(jnp.where(same, 1, 0), axis=1).astype(jnp.int32)


def adam_update(weight, first, second, grad, rate, decay):
    first = BETA_ONE * first + (1.0 - BETA_ONE) * grad
    second = BETA_TWO * second + (1.0 - BETA_TWO) * grad * grad
    first_hat = first / (1.0 - BETA_ONE**STEP_COUNT)
    second_hat = second / (1.0 - BETA_TWO**STEP_COUNT)
    weight = weight - rate * (first_hat / (jnp.sqrt(second_hat) + ADAM_EPS) + decay * weight)
    return (weight, first, second)


MESH = pl.DeviceIdType.MESH
ROW_STEP = 400
TILE_GROUPS = 8
LANES = 128
SHORT = pl.CostEstimate(flops=1000, bytes_accessed=1000, transcendentals=0)


def meet(peers):
    gate = pltpu.get_barrier_semaphore()
    for peer in peers:
        pl.semaphore_signal(gate, inc=1, device_id=peer, device_id_type=MESH)
    pl.semaphore_wait(gate, len(peers))


def others(axis):
    count, me = lax.axis_size(axis), lax.axis_index(axis)
    return [lax.rem(me + step, count) for step in range(1, count)]


def behind(axis, step):
    count, me = lax.axis_size(axis), lax.axis_index(axis)
    return lax.rem(me + count - step, count)


def send(source, target, send_sem, recv_sem, device):
    copy = pltpu.make_async_remote_copy(
        src_ref=source,
        dst_ref=target,
        send_sem=send_sem,
        recv_sem=recv_sem,
        device_id=device,
        device_id_type=MESH,
    )
    copy.start()
    return copy


def layer_norm_parts(stream):
    center = stream - jnp.mean(stream, -1, keepdims=True)
    inverse = lax.rsqrt(jnp.mean(center * center, -1, keepdims=True) + EPS_NORM)
    return center * inverse, inverse


def norm_pull(grad_normed, gain, stream):
    scaled, inverse = layer_norm_parts(stream)
    grad_scaled = grad_normed * gain
    grad_stream = inverse * (
        grad_scaled
        - jnp.mean(grad_scaled, -1, keepdims=True)
        - scaled * jnp.mean(grad_scaled * scaled, -1, keepdims=True)
    )
    return grad_stream, jnp.sum(grad_normed * scaled, axis=0, keepdims=True)


class Work:
    def __init__(self, before, during, operands, specs, outs, scratch, after=None, twins=False):
        self.before, self.during, self.after, self.twins = before, during, after, twins
        self.operands, self.specs, self.outs, self.scratch = operands, specs, outs, scratch


def tensor_step(name, function, work, extras, scalars, outs, gather, collective_id, line=None):
    parts = lax.axis_size("tensor")
    share = extras[0].shape[0]
    reduce = work is not None
    work = work or Work(None, None, [], [], [], [])

    def kernel(*refs):
        refs = list(refs)

        def take(count):
            return [refs.pop(0) for _ in range(count)]

        work_refs = take(len(work.operands))
        extra_refs = take(len(extras))
        scalar_refs = take(len(scalars))
        source_refs = take(len(line.operands)) if line else []
        out_refs = take(len(outs))
        (full,) = take(1) if gather else [None]
        work_outs = take(len(work.outs))
        (joined,) = take(1) if line else [None]
        send_sems, recv_sems = take(2)
        partial_ref, outgoing, arrived = take(3) if reduce else [None] * 3
        if line:
            line.bind(source_refs, joined, take(len(line.scratch)))
            line.load()

        def tick(count=1):
            if line:
                line.steps(count)

        me, side = lax.axis_index("tensor"), lax.axis_index("seq")
        peers = others("tensor")
        twin = {"seq": 1 - side}
        twins = work.twins or (line and line.share)
        meet(
            [{"tensor": peer} for peer in peers]
            + [twin] * bool(twins)
            + ([{"dp": peer} for peer in others("dp")] if line else [])
        )
        if line:
            line.begin()
        total = None
        if reduce:
            work.before(work_refs, work_outs, refs, partial_ref, tick)
            copies = []
            for step, peer in enumerate(peers):
                rows = pl.ds(pl.multiple_of(peer * share, share), share)
                outgoing[step] = partial_ref[rows, :].astype(jnp.bfloat16)
                copies.append(
                    send(
                        outgoing.at[step],
                        arrived.at[step],
                        send_sems.at[0, step],
                        recv_sems.at[0, step],
                        {"tensor": peer},
                    )
                )
            if work.during:
                work.during(work_refs, work_outs, refs)
            tick(6)
            total = partial_ref[pl.ds(pl.multiple_of(me * share, share), share), :]
            for step, copy in enumerate(copies):
                copy.wait()
                total = total + arrived[step].astype(jnp.float32)
        results = function(total, *[ref[...] for ref in extra_refs], *scalar_refs)
        for ref, value in zip(out_refs, results):
            ref[...] = value.astype(ref.dtype)
        if gather:
            full[me] = results[len(outs)].astype(jnp.bfloat16)
            copies = [
                send(
                    full.at[me],
                    full.at[me],
                    send_sems.at[1, step],
                    recv_sems.at[1, step],
                    {"tensor": peer},
                )
                for step, peer in enumerate(peers)
            ]
        if work.after:
            work.after(work_refs, work_outs, refs)
        tick(None)
        if gather:
            for copy in copies:
                copy.wait()
        if line:
            line.end()

    vmem = pl.BlockSpec(memory_space=pltpu.VMEM)
    smem = pl.BlockSpec(memory_space=pltpu.SMEM)
    shapes = [jax.ShapeDtypeStruct(shape, dtype) for shape, dtype in outs]
    if gather:
        shapes.append(jax.ShapeDtypeStruct((parts, share, D), jnp.bfloat16))
    shapes += [jax.ShapeDtypeStruct(shape, dtype) for shape, dtype in work.outs]
    out_specs = [vmem] * len(shapes)
    operands = list(work.operands) + list(extras) + list(scalars)
    in_specs = list(work.specs) + [vmem] * len(extras) + [smem] * len(scalars)
    dma = pltpu.SemaphoreType.DMA
    buffers = [dma((2, parts - 1))] * 2
    if reduce:
        buffers += [pltpu.VMEM((parts * share, D), jnp.float32)]
        buffers += [pltpu.VMEM((parts - 1, share, D), jnp.bfloat16)] * 2
    if line:
        operands += line.operands
        in_specs += line.in_specs
        shapes.append(line.out_shape)
        out_specs.append(line.out_spec)
        buffers += line.scratch
    return pl.pallas_call(
        kernel,
        name=name,
        grid=(1,),
        out_shape=shapes,
        in_specs=in_specs,
        out_specs=out_specs,
        scratch_shapes=buffers + list(work.scratch),
        cost_estimate=SHORT,
        compiler_params=pltpu.CompilerParams(
            collective_id=collective_id, has_side_effects=True, vmem_limit_bytes=60 << 20
        ),
    )(*operands)


VMEM_SPEC = pl.BlockSpec(memory_space=pltpu.VMEM)


def part_spec(rows, index):
    return pl.BlockSpec((rows, D), lambda step: (index, 0), pipeline_mode=pl.Buffered(1))


def turn(block, cosine, sine):
    half = HEAD_DIM // 2
    first, second = block[:half], block[half:]
    return jnp.concatenate(
        [first * cosine - second * sine, second * cosine + first * sine], axis=0
    )


def times(left, right):
    return jnp.dot(left, right, preferred_element_type=jnp.float32)


def masks_of(count, side):
    key = lax.broadcasted_iota(jnp.int32, (count, count), 0)
    query = lax.broadcasted_iota(jnp.int32, (count, count), 1)
    far = jnp.where(side == 0, -1e30, 0.0).astype(jnp.float32)
    return far, jnp.where(key <= query, 0.0, -1e30)


def scores_of(keys_values, head, queries, masks):
    span = slice(head * HEAD_DIM, (head + 1) * HEAD_DIM)
    scale = HEAD_DIM ** (-0.5)
    far = contract_first(keys_values[0, 0, span, :], queries) * scale + masks[0]
    own = contract_first(keys_values[1, 0, span, :], queries) * scale + masks[1]
    return far, own


def attention_work(normed, table, cosine, sine):
    parts, share, _ = normed.shape
    count = parts * share
    width = D // parts
    heads = width // HEAD_DIM

    def before(ins, outs, scratch, partial_ref, tick):
        normed_ref, qkv_ref, out_ref, cosine_ref, sine_ref = ins
        queries_ref, both, logs_ref, attended_ref = outs
        send_sem, recv_sem = scratch
        side = lax.axis_index("seq")
        cosine, sine = cosine_ref[...], sine_ref[...]
        rows = normed_ref[...].reshape(count, D)
        joined = contract_last(qkv_ref[...], rows)
        for head in range(heads):
            span = slice(head * HEAD_DIM, (head + 1) * HEAD_DIM)
            keys = joined[width + head * HEAD_DIM : width + (head + 1) * HEAD_DIM]
            both[1, 0, span, :] = turn(keys, cosine, sine).astype(jnp.bfloat16)
        both[1, 1] = joined[2 * width :].astype(jnp.bfloat16)
        copy = pltpu.make_async_remote_copy(
            src_ref=both.at[1],
            dst_ref=both.at[0],
            send_sem=send_sem,
            recv_sem=recv_sem,
            device_id={"seq": 1 - side},
            device_id_type=MESH,
        )

        copy.start()
        for head in range(heads):
            span = slice(head * HEAD_DIM, (head + 1) * HEAD_DIM)
            queries_ref[span, :] = turn(joined[span], cosine, sine).astype(jnp.bfloat16)

        copy.wait()
        masks = masks_of(count, side)
        for head in range(heads):
            span = slice(head * HEAD_DIM, (head + 1) * HEAD_DIM)
            far, own = scores_of(both, head, queries_ref[span, :], masks)
            peak = jnp.maximum(
                jnp.max(far, axis=0, keepdims=True), jnp.max(own, axis=0, keepdims=True)
            )
            far, own = jnp.exp(far - peak), jnp.exp(own - peak)
            total = jnp.sum(far, axis=0, keepdims=True) + jnp.sum(own, axis=0, keepdims=True)
            logs_ref[head] = peak + jnp.log(total)
            inverse = 1.0 / total
            attended = times(both[0, 1, span, :], (far * inverse).astype(jnp.bfloat16))
            attended += times(both[1, 1, span, :], (own * inverse).astype(jnp.bfloat16))
            attended_ref[span, :] = attended.astype(jnp.bfloat16)
            tick(2)
        partial_ref[...] = contract_first(attended_ref[...], out_ref[...])

    low = jnp.bfloat16
    return Work(
        before,
        None,
        [normed, table, table, cosine, sine],
        [VMEM_SPEC, part_spec(3 * width, 0), part_spec(width, 3), VMEM_SPEC, VMEM_SPEC],
        [
            ((width, count), low),
            ((2, 2, width, count), low),
            ((heads, 1, count), jnp.float32),
            ((width, count), low),
        ],
        [pltpu.SemaphoreType.DMA, pltpu.SemaphoreType.DMA],
        twins=True,
    )


def fold_copy(own, near, send_sems, recv_sems, index):
    side = lax.axis_index("seq")
    return pltpu.make_async_remote_copy(
        src_ref=own.at[index, :, 1 - side],
        dst_ref=near.at[index],
        send_sem=send_sems.at[index],
        recv_sem=recv_sems.at[index],
        device_id={"seq": 1 - side},
        device_id_type=MESH,
    )


def add_halves(own, near, out, start):
    side = lax.axis_index("seq")

    def one(block, carry):
        value = own[block, side].astype(jnp.float32) + near[block].astype(jnp.float32)
        out[start + block] = value.astype(jnp.bfloat16)
        return carry

    lax.fori_loop(0, near.shape[0], one, 0)


def attention_back_work(grad, normed, table, kept, cosine, sine, half_rows):
    parts, share, _ = normed.shape
    count = parts * share
    width = D // parts
    heads = width // HEAD_DIM
    queries, both, logs, attended = kept
    blocks = 4 * width // (2 * half_rows)

    def before(ins, outs, scratch, partial_ref, tick):
        grad_ref, _, qkv_ref, out_ref, queries_ref, both, logs_ref, _, cosine_ref, sine_ref = ins
        back, came, grad_joined, send_sem, recv_sem = scratch[:5]
        side = lax.axis_index("seq")
        cosine, sine = cosine_ref[...], -sine_ref[...]
        scale = HEAD_DIM ** (-0.5)
        grads = contract_last(out_ref[...], grad_ref[...].reshape(count, D)).astype(jnp.bfloat16)
        own_grads = []
        masks = masks_of(count, side)
        for head in range(heads):
            span = slice(head * HEAD_DIM, (head + 1) * HEAD_DIM)
            head_queries, head_grads = queries_ref[span, :], grads[span]
            far, own = scores_of(both, head, head_queries, masks)
            far, own = jnp.exp(far - logs_ref[head]), jnp.exp(own - logs_ref[head])
            far_grad = contract_first(both[0, 1, span, :], head_grads)
            own_grad = contract_first(both[1, 1, span, :], head_grads)
            mean = jnp.sum(far * far_grad, axis=0, keepdims=True)
            mean += jnp.sum(own * own_grad, axis=0, keepdims=True)
            far_grad = (far * (far_grad - mean)).astype(jnp.bfloat16)
            own_grad = (own * (own_grad - mean)).astype(jnp.bfloat16)
            far, own = far.astype(jnp.bfloat16), own.astype(jnp.bfloat16)
            back[0, span, :] = (contract_last(head_queries, far_grad) * scale).astype(jnp.bfloat16)
            back[1, span, :] = contract_last(head_grads, far).astype(jnp.bfloat16)
            query_grad = times(both[0, 0, span, :], far_grad) + times(both[1, 0, span, :], own_grad)
            grad_joined[span, :] = turn(query_grad * scale, cosine, sine).astype(jnp.bfloat16)
            own_grads.append(
                (contract_last(head_queries, own_grad) * scale, contract_last(head_grads, own))
            )
            tick(2)
        copy = send(back, came, send_sem, recv_sem, {"seq": 1 - side})
        copy.wait()
        for head, (key_grad, value_grad) in enumerate(own_grads):
            span = slice(head * HEAD_DIM, (head + 1) * HEAD_DIM)
            key_grad = key_grad + came[0, span, :].astype(jnp.float32)
            value_grad = value_grad + came[1, span, :].astype(jnp.float32)
            start = width + head * HEAD_DIM
            grad_joined[start : start + HEAD_DIM, :] = turn(key_grad, cosine, sine).astype(
                jnp.bfloat16
            )
            start += width
            grad_joined[start : start + HEAD_DIM, :] = value_grad.astype(jnp.bfloat16)
        partial_ref[...] = contract_first(grad_joined[...], qkv_ref[...])

    def during(ins, outs, scratch):
        grad_ref, normed_ref, attended_ref = ins[0], ins[1], ins[7]
        grad_joined = scratch[2]
        own, near, fold_send, fold_recv = scratch[5:]
        value = times(grad_joined[...], normed_ref[...].reshape(count, D)).astype(jnp.bfloat16)
        part = 3 * blocks // 4
        own[0, :part] = value.reshape(part, 2, half_rows, D)
        value = times(attended_ref[...], grad_ref[...].reshape(count, D)).astype(jnp.bfloat16)
        own[0, part:] = value.reshape(blocks - part, 2, half_rows, D)
        fold_copy(own, near, fold_send, fold_recv, 0).start()

    def after(ins, outs, scratch):
        own, near, fold_send, fold_recv = scratch[5:]
        fold_copy(own, near, fold_send, fold_recv, 0).wait()
        add_halves(own.at[0], near.at[0], outs[0], 0)

    low = jnp.bfloat16
    dma = pltpu.SemaphoreType.DMA
    return Work(
        before,
        during,
        [grad, normed, table, table, queries, both, logs, attended, cosine, sine],
        [VMEM_SPEC, VMEM_SPEC, part_spec(3 * width, 0), part_spec(width, 3)] + [VMEM_SPEC] * 6,
        [((blocks, half_rows, D), low)],
        [
            pltpu.VMEM((2, width, count), low),
            pltpu.VMEM((2, width, count), low),
            pltpu.VMEM((3 * width, count), low),
            dma,
            dma,
            pltpu.VMEM((1, blocks, 2, half_rows, D), low),
            pltpu.VMEM((1, blocks, half_rows, D), low),
            dma((1,)),
            dma((1,)),
        ],
        after,
        True,
    )


def gelu(hidden):
    return jax.nn.gelu(hidden, approximate=True)


def unit_work(normed, up, down):
    parts, share, _ = normed.shape
    count = parts * share
    units = FF // parts

    def before(ins, outs, scratch, partial_ref, tick):
        normed_ref, up_ref, down_ref = ins
        hidden_ref, activated_ref = outs
        hidden = contract_last(up_ref[...], normed_ref[...].reshape(count, D))
        hidden_ref[...] = hidden
        activated_ref[...] = gelu(hidden).astype(jnp.bfloat16)
        tick(2)
        partial_ref[...] = contract_first(activated_ref[...], down_ref[...])

    return Work(
        before,
        None,
        [normed, up[0], down[0]],
        [VMEM_SPEC, part_spec(units, up[1]), part_spec(units, down[1])],
        [((units, count), jnp.float32), ((units, count), jnp.bfloat16)],
        [],
    )


def unit_back_work(grad, normed, up, down, kept, half_rows):
    parts, share, _ = normed.shape
    count = parts * share
    units = FF // parts
    hidden, activated = kept
    blocks = units // (2 * half_rows)

    def before(ins, outs, scratch, partial_ref, tick):
        grad_ref, _, up_ref, down_ref, hidden_ref, _ = ins
        grad_hidden = scratch[0]
        grad_act = contract_last(down_ref[...], grad_ref[...].reshape(count, D))
        _, pull = jax.vjp(gelu, hidden_ref[...])
        grad_hidden[...] = pull(grad_act)[0].astype(jnp.bfloat16)
        tick(2)
        partial_ref[...] = contract_first(grad_hidden[...], up_ref[...])

    def during(ins, outs, scratch):
        grad_ref, normed_ref, _, _, _, activated_ref = ins
        grad_hidden, own, near, fold_send, fold_recv = scratch
        value = times(grad_hidden[...], normed_ref[...].reshape(count, D))
        own[0] = value.astype(jnp.bfloat16).reshape(own.shape[1:])
        fold_copy(own, near, fold_send, fold_recv, 0).start()
        value = times(activated_ref[...], grad_ref[...].reshape(count, D))
        own[1] = value.astype(jnp.bfloat16).reshape(own.shape[1:])
        fold_copy(own, near, fold_send, fold_recv, 1).start()

    def after(ins, outs, scratch):
        _, own, near, fold_send, fold_recv = scratch
        for index in range(2):
            fold_copy(own, near, fold_send, fold_recv, index).wait()
            add_halves(own.at[index], near.at[index], outs[0], index * blocks)

    low, dma = jnp.bfloat16, pltpu.SemaphoreType.DMA
    return Work(
        before,
        during,
        [grad, normed, up[0], down[0], hidden, activated],
        [VMEM_SPEC, VMEM_SPEC, part_spec(units, up[1]), part_spec(units, down[1])]
        + [VMEM_SPEC] * 2,
        [((2 * blocks, half_rows, D), low)],
        [
            pltpu.VMEM((units, count), low),
            pltpu.VMEM((2, blocks, 2, half_rows, D), low),
            pltpu.VMEM((2, blocks, half_rows, D), low),
            dma((2,)),
            dma((2,)),
        ],
        after,
        True,
    )


LINE_BLOCKS = 1
LINE_LAG = 3


class Line:
    def __init__(self, sources, share):
        self.groups = lax.axis_size("dp")
        self.sources, self.share = sources, share
        count = sum(size for _, _, size in sources)
        _, half_rows, _ = sources[0][0].shape
        self.half = (count, half_rows, D)
        self.chunks = count // LINE_BLOCKS
        self.operands = [array for array, _, _ in sources]
        self.in_specs = [pl.BlockSpec(memory_space=pl.ANY)] * len(sources)
        dma = pltpu.SemaphoreType.DMA
        out = (count, 2, half_rows, D) if share else self.half
        self.out_shape = jax.ShapeDtypeStruct(out, jnp.bfloat16)
        self.out_spec = pl.BlockSpec(memory_space=pl.ANY if share else pltpu.VMEM)
        self.scratch = [
            pltpu.VMEM(self.half, jnp.bfloat16),
            pltpu.VMEM((2,) + self.half, jnp.bfloat16),
            pltpu.VMEM((2,) + self.half, jnp.bfloat16),
            dma((len(sources),)),
            dma((2, self.chunks)),
            dma((2, self.chunks)),
        ]
        if share:
            self.scratch += [pltpu.VMEM(self.half, jnp.bfloat16)] + [dma((self.chunks,))] * 3

    def bind(self, source_refs, out_ref, refs):
        self.source_refs, self.out = source_refs, out_ref
        self.own, self.came, self.going, self.own_sems, self.send_sems, self.recv_sems = refs[:6]
        self.total = out_ref
        if self.share:
            self.total, self.keep_sems, self.twin_send, self.twin_recv = refs[6:]
        self.done = 0
        self.group = lax.axis_index("dp")
        self.first = jnp.where(self.group < self.groups // 2, 0, 1)

    def at(self, chunk):
        return pl.ds(chunk * LINE_BLOCKS, LINE_BLOCKS)

    def comes(self, way):
        return jnp.where(way == 0, self.group > 0, self.group < self.groups - 1)

    def goes(self, way):
        return jnp.where(way == 0, self.group < self.groups - 1, self.group > 0)

    def copy(self, source, way, chunk):
        target = jnp.where(way == 0, self.group + 1, self.group - 1)
        return pltpu.make_async_remote_copy(
            src_ref=source,
            dst_ref=self.came.at[way, self.at(chunk)],
            send_sem=self.send_sems.at[way, chunk],
            recv_sem=self.recv_sems.at[way, chunk],
            device_id={"dp": target},
            device_id_type=MESH,
        )

    def load(self):
        self.loads, place = [], 0
        for index, (ref, (_, start, size)) in enumerate(zip(self.source_refs, self.sources)):
            copy = pltpu.make_async_copy(
                ref.at[pl.ds(start, size)], self.own.at[pl.ds(place, size)], self.own_sems.at[index]
            )
            copy.start()
            self.loads.append(copy)
            place += size

    def begin(self):
        for copy in self.loads:
            copy.wait()
        for way in range(2):

            @pl.when(jnp.logical_not(self.comes(way)))
            def _():
                self.came[way] = jnp.zeros(self.half, jnp.bfloat16)

                def start(chunk, carry):
                    self.copy(self.own.at[self.at(chunk)], way, chunk).start()
                    return carry

                lax.fori_loop(0, self.chunks, start, 0)

    def twin_copy(self, chunk):
        side = lax.axis_index("seq")
        return pltpu.make_async_remote_copy(
            src_ref=self.total.at[self.at(chunk)],
            dst_ref=self.out.at[self.at(chunk), side],
            send_sem=self.twin_send.at[chunk],
            recv_sem=self.twin_recv.at[chunk],
            device_id={"seq": 1 - side},
            device_id_type=MESH,
        )

    def keep_copy(self, chunk):
        return pltpu.make_async_copy(
            self.total.at[self.at(chunk)],
            self.out.at[self.at(chunk), lax.axis_index("seq")],
            self.keep_sems.at[chunk],
        )

    def pass_on(self, way, chunk):
        rows = self.at(chunk)

        @pl.when(self.comes(way))
        def _():
            copy = self.copy(self.going.at[way, rows], way, chunk)
            copy.wait_recv()

            @pl.when(self.goes(way))
            def _():
                value = self.own[rows].astype(jnp.float32) + self.came[way, rows].astype(jnp.float32)
                self.going[way, rows] = value.astype(jnp.bfloat16)
                copy.start()

    def step(self, index):
        @pl.when(index < self.chunks)
        def _():
            self.pass_on(self.first, index)

        @pl.when(index >= LINE_LAG)
        def _():
            chunk = index - LINE_LAG
            rows = self.at(chunk)
            self.pass_on(1 - self.first, chunk)
            value = self.own[rows].astype(jnp.float32)
            value = value + self.came[0, rows].astype(jnp.float32)
            value = value + self.came[1, rows].astype(jnp.float32)
            self.total[rows] = value.astype(jnp.bfloat16)
            if self.share:
                self.keep_copy(chunk).start()
                self.twin_copy(chunk).start()

    def steps(self, count=None):
        last = self.chunks + LINE_LAG
        stop = last if count is None else min(self.done + count, last)

        def one(index, carry):
            self.step(index)
            return carry

        lax.fori_loop(self.done, stop, one, 0)
        self.done = stop

    def end(self):
        def one(chunk, carry):
            for way in range(2):

                @pl.when(self.goes(way))
                def _():
                    self.copy(self.going.at[way, self.at(chunk)], way, chunk).wait_send()

            if self.share:
                self.keep_copy(chunk).wait()
                self.twin_copy(chunk).wait()
            return carry

        lax.fori_loop(0, self.chunks, one, 0)


def reduce_all(terms, collective_id, line=None, tail=None):
    _, tensors, groups, count, _ = terms.shape
    half = count // 2
    function, extras, scalars, outs = tail or (None, [], [], [])
    extra_specs = [VMEM_SPEC] * len(extras)
    extra_specs += [pl.BlockSpec(memory_space=pltpu.SMEM)] * len(scalars)
    extras = list(extras) + list(scalars)

    def kernel(*refs):
        refs = list(refs)
        terms_ref = refs.pop(0)
        source_refs = [refs.pop(0) for _ in line.operands] if line else []
        extra_refs = [refs.pop(0) for _ in extras]
        out_refs = [refs.pop(0) for _ in range(len(outs) or 1)]
        full = refs.pop(0) if tail else None
        joined_ref = refs.pop(0) if line else None
        tail_sems = [refs.pop(0) for _ in range(2)] if tail else None
        (
            near, own, mid, sums, mid_in, far, far_in,
            own_sems, near_send, near_recv, mid_send, mid_recv, far_send, far_recv,
        ) = refs[:14]
        if line:
            line.bind(source_refs, joined_ref, refs[14:])
            line.load()
        group, part, side = lax.axis_index("dp"), lax.axis_index("tensor"), lax.axis_index("seq")
        twin = 1 - side
        parts = others("tensor")
        order = others("dp") + [group]
        meet(
            [{"seq": twin}]
            + [{"tensor": peer} for peer in parts]
            + [{"dp": peer} for peer in order[:-1]]
        )
        waits, near_copies, own_copies = [], [], []
        for place, target in enumerate(order):
            near_copies.append(
                send(
                    terms_ref.at[twin, :, target],
                    near.at[place],
                    near_send.at[place],
                    near_recv.at[place],
                    {"seq": twin},
                )
            )
            copy = pltpu.make_async_copy(
                terms_ref.at[side, :, target], own.at[place], own_sems.at[place]
            )
            copy.start()
            own_copies.append(copy)
        if line:
            line.begin()
        beside = lax.rem(part + 1, 2) + part - lax.rem(part, 2)
        across = lax.rem(part + 2, 4)
        corner = 3 - part
        upper, lower = pl.ds(0, half), pl.ds(half, half)
        first_copies, second_copies = [], []

        def hand(place, index, source, target):
            return send(
                source,
                mid_in.at[place, index],
                mid_send.at[place, index],
                mid_recv.at[place, index],
                {"tensor": target},
            )

        for place in range(groups):
            near_copies[place].wait_recv()
            own_copies[place].wait()
            for slot in range(tensors):
                mid[place, slot] = (
                    own[place, slot].astype(jnp.float32) + near[place, slot].astype(jnp.float32)
                ).astype(jnp.bfloat16)
            first_copies.append(
                [
                    hand(place, 0, mid.at[place, corner, upper], beside),
                    hand(place, 1, mid.at[place, corner, lower], across),
                    hand(place, 2, mid.at[place, beside, upper], beside),
                    hand(place, 3, mid.at[place, across, lower], across),
                ]
            )
        for place in range(groups):
            if line and place < 4:
                line.steps(3)
            copies = []
            for index, slot, rows, target in ((0, across, upper, across), (1, beside, lower, beside)):
                first_copies[place][index].wait_recv()
                value = mid[place, slot, rows].astype(jnp.float32)
                value = value + mid_in[place, index].astype(jnp.float32)
                sums[place, index] = value.astype(jnp.bfloat16)
                copies.append(hand(place, 4 + index, sums.at[place, index], target))
            second_copies.append(copies)
        far_copies = []
        for place, target in enumerate(order):
            copies = first_copies[place][2:] + second_copies[place]
            for copy in copies:
                copy.wait_recv()

            def joined(index):
                return mid_in[place, index].astype(jnp.float32)

            halves = [joined(2) + joined(4), joined(3) + joined(5)]
            total = mid[place, part].astype(jnp.float32) + jnp.concatenate(halves, axis=0)
            if place < groups - 1:
                far[place] = total.astype(jnp.bfloat16)
                far_copies.append(
                    send(
                        far.at[place],
                        far_in.at[place],
                        far_send.at[place],
                        far_recv.at[place],
                        {"dp": target},
                    )
                )
        if line:
            line.steps()
        for place, copy in enumerate(far_copies):
            copy.wait_recv()
            total = total + far_in[place].astype(jnp.float32)
        if tail:
            results = function(total, *extra_refs)
            for ref, value in zip(out_refs, results):
                ref[...] = value
            full[part] = results[len(outs)].astype(jnp.bfloat16)
            last_copies = [
                send(
                    full.at[part],
                    full.at[part],
                    tail_sems[0].at[step],
                    tail_sems[1].at[step],
                    {"tensor": peer},
                )
                for step, peer in enumerate(parts)
            ]
            for copy in last_copies:
                copy.wait()
        else:
            out_refs[0][...] = total
        for copy in near_copies + far_copies + [
            copy for row in first_copies + second_copies for copy in row
        ]:
            copy.wait_send()
        if line:
            line.end()

    block = (count, D)
    dma = pltpu.SemaphoreType.DMA
    results = [jax.ShapeDtypeStruct(*out) for out in outs]
    if tail:
        results.append(jax.ShapeDtypeStruct((tensors,) + block, jnp.bfloat16))
    else:
        results.append(jax.ShapeDtypeStruct(block, jnp.float32))
    return pl.pallas_call(
        kernel,
        name="reduce_all",
        out_shape=results + ([line.out_shape] if line else []),
        in_specs=[pl.BlockSpec(memory_space=pl.ANY)] + (line.in_specs if line else []) + extra_specs,
        out_specs=[VMEM_SPEC] * len(results) + ([line.out_spec] if line else []),
        scratch_shapes=[dma((tensors - 1,))] * (2 if tail else 0)
        + [pltpu.VMEM((groups, tensors) + block, jnp.bfloat16)] * 3
        + [
            pltpu.VMEM((groups, 2, half, D), jnp.bfloat16),
            pltpu.VMEM((groups, 6, half, D), jnp.bfloat16),
            pltpu.VMEM((groups,) + block, jnp.bfloat16),
            pltpu.VMEM((groups,) + block, jnp.bfloat16),
            dma((groups,)),
            dma((groups,)),
            dma((groups,)),
            dma((groups, 6)),
            dma((groups, 6)),
            dma((groups,)),
            dma((groups,)),
        ]
        + (line.scratch if line else []),
        cost_estimate=SHORT,
        compiler_params=pltpu.CompilerParams(
            collective_id=collective_id, has_side_effects=True, vmem_limit_bytes=56 << 20
        ),
    )(terms, *(line.operands if line else []), *extras)


def gather_all(block, collective_id, line=None):
    tensors, groups = lax.axis_size("tensor"), lax.axis_size("dp")
    half = block.shape[0] // 2

    def kernel(*refs):
        refs = list(refs)
        block_ref = refs.pop(0)
        source_refs = [refs.pop(0) for _ in line.operands] if line else []
        out = refs.pop(0)
        summed_ref = refs.pop(0) if line else None
        own_sem, far_send, far_recv, mid_send, mid_recv, near_send, near_recv = refs[:7]
        if line:
            line.bind(source_refs, summed_ref, refs[7:])
            line.load()
        group, part, side = lax.axis_index("dp"), lax.axis_index("tensor"), lax.axis_index("seq")
        twin = 1 - side
        meet(
            [{"seq": twin}]
            + [{"tensor": peer} for peer in others("tensor")]
            + [{"dp": peer} for peer in others("dp")]
        )
        far_copies = [
            send(
                block_ref,
                out.at[side, part, group],
                far_send.at[step],
                far_recv.at[step],
                {"dp": peer},
            )
            for step, peer in enumerate(others("dp"))
        ]
        own = pltpu.make_async_copy(block_ref, out.at[side, part, group], own_sem)
        own.start()
        if line:
            line.begin()
        beside = lax.rem(part + 1, 2) + part - lax.rem(part, 2)
        across = lax.rem(part + 2, 4)
        corner = 3 - part
        upper, lower = pl.ds(0, half), pl.ds(half, half)
        first_copies, second_copies, near_copies = [], [], []
        for place in range(groups):
            source = behind("dp", place)
            if place:
                far_copies[place - 1].wait_recv()
            held = out.at[side, part, source] if place else block_ref

            def hand(index, piece, slot, rows, target):
                return send(
                    piece,
                    out.at[side, slot, source, rows],
                    mid_send.at[place, index],
                    mid_recv.at[place, index],
                    {"tensor": target},
                )

            first = [
                hand(0, held.at[upper], part, upper, beside),
                hand(1, held.at[lower], part, lower, across),
                hand(2, held.at[lower], part, lower, beside),
                hand(3, held.at[upper], part, upper, across),
            ]
            near_copies.append(
                send(
                    held,
                    out.at[side, part, source],
                    near_send.at[place, 0],
                    near_recv.at[place, 0],
                    {"seq": twin},
                )
            )
            first[0].wait_recv()
            second = [hand(4, out.at[side, beside, source, upper], beside, upper, across)]
            first[1].wait_recv()
            second.append(hand(5, out.at[side, across, source, lower], across, lower, beside))
            first_copies.append(first)
            second_copies.append(second)
        for place in range(groups):
            if line and place < 4:
                line.steps(2)
            source = behind("dp", place)
            ready = [
                (beside, first_copies[place][2:3]),
                (across, first_copies[place][3:4]),
                (corner, second_copies[place]),
            ]
            for step, (slot, copies) in enumerate(ready):
                for copy in copies:
                    copy.wait_recv()
                held = out.at[side, slot, source]
                near_copies.append(
                    send(
                        held,
                        held,
                        near_send.at[place, step + 1],
                        near_recv.at[place, step + 1],
                        {"seq": twin},
                    )
                )
        if line:
            line.steps()
        for copy in near_copies:
            copy.wait_recv()
        for copy in near_copies + far_copies + [
            copy for row in first_copies + second_copies for copy in row
        ]:
            copy.wait_send()
        own.wait()
        if line:
            line.end()

    dma = pltpu.SemaphoreType.DMA
    anywhere = pl.BlockSpec(memory_space=pl.ANY)
    return pl.pallas_call(
        kernel,
        name="gather_all",
        out_shape=[jax.ShapeDtypeStruct((2, tensors, groups) + block.shape, block.dtype)]
        + ([line.out_shape] if line else []),
        in_specs=[VMEM_SPEC] + (line.in_specs if line else []),
        out_specs=[pl.BlockSpec(memory_space=pltpu.HBM)] + ([line.out_spec] if line else []),
        scratch_shapes=[
            dma,
            dma((groups - 1,)),
            dma((groups - 1,)),
            dma((groups, 6)),
            dma((groups, 6)),
            dma((groups, tensors)),
            dma((groups, tensors)),
        ]
        + (line.scratch if line else []),
        cost_estimate=SHORT,
        compiler_params=pltpu.CompilerParams(
            collective_id=collective_id, has_side_effects=True, vmem_limit_bytes=60 << 20
        ),
    )(block, *(line.operands if line else []))


def reduce_rows(name, terms, ids, line, function, extras, scalars, outs):
    count, groups = terms.shape[3], terms.shape[2]
    pieces = max(1, groups // 4)
    if pieces == 1:
        return reduce_all(terms, ids[0], line, (function, extras, scalars, outs))
    part = count // pieces
    sums, joined = [], []
    for i in range(pieces):
        piece = terms[:, :, :, i * part : (i + 1) * part]
        total, *joined_now = reduce_all(piece, ids[1 if i and line else 0], None if i else line)
        sums.append(total)
        joined += joined_now
    total = jnp.concatenate(sums, axis=0)
    results = tensor_step(
        name,
        lambda _, total_ref, *refs: function(total_ref, *refs),
        None,
        [total] + list(extras),
        scalars,
        outs,
        True,
        ids[2],
    )
    return list(results) + joined


def join_stats(stats, collective_id):
    _, tensors, groups, _, _ = stats.shape

    def join(left, right):
        top = jnp.maximum(left[..., 0:1, :], right[..., 0:1, :])
        total = left[..., 1:2, :] * jnp.exp(left[..., 0:1, :] - top) + right[..., 1:2, :] * jnp.exp(
            right[..., 0:1, :] - top
        )
        return jnp.concatenate(
            [top, total, left[..., 2:3, :] + right[..., 2:3, :], left[..., 3:, :]], axis=-2
        )

    def kernel(
        stats_ref, home, full, near, mid, mid_in, far, far_in,
        near_send, near_recv, mid_send, mid_recv, far_send, far_recv,
    ):
        group, part, side = lax.axis_index("dp"), lax.axis_index("tensor"), lax.axis_index("seq")
        twin = 1 - side
        parts, groups_else = others("tensor"), others("dp")
        meet(
            [{"seq": twin}]
            + [{"tensor": peer} for peer in parts]
            + [{"dp": peer} for peer in groups_else]
        )
        copy = send(stats_ref.at[twin], near, near_send.at[0], near_recv.at[0], {"seq": twin})
        copy.wait()
        for slot in range(tensors):
            for spot in range(groups):
                mid[slot, spot] = join(stats_ref[side, slot, spot], near[slot, spot])
        copies = [
            send(mid.at[peer], mid_in.at[step], mid_send.at[0, step], mid_recv.at[0, step], {"tensor": peer})
            for step, peer in enumerate(parts)
        ]
        for copy in copies:
            copy.wait()
        for spot in range(groups):
            total = mid[part, spot]
            for step in range(tensors - 1):
                total = join(total, mid_in[step, spot])
            far[spot] = total
        copies = [
            send(far.at[peer], far_in.at[step], far_send.at[0, step], far_recv.at[0, step], {"dp": peer})
            for step, peer in enumerate(groups_else)
        ]
        total = far[group]
        for step, copy in enumerate(copies):
            copy.wait()
            total = join(total, far_in[step])
        log_total = total[0:1] + jnp.log(total[1:2])
        home[...] = jnp.concatenate([log_total, total[2:3], total[2:]], axis=0)
        full[side, part, group] = jnp.broadcast_to(log_total, (8, LANES))
        held = full.at[side, part, group]
        copies = [
            send(held, held, far_send.at[1, step], far_recv.at[1, step], {"dp": peer})
            for step, peer in enumerate(groups_else)
        ]
        for copy in copies:
            copy.wait()
        held = full.at[side, part]
        copies = [
            send(held, held, mid_send.at[1, step], mid_recv.at[1, step], {"tensor": peer})
            for step, peer in enumerate(parts)
        ]
        for copy in copies:
            copy.wait()
        held = full.at[side]
        send(held, held, near_send.at[1], near_recv.at[1], {"seq": twin}).wait()

    tile = (8, LANES)
    dma = pltpu.SemaphoreType.DMA
    vmem = pl.BlockSpec(memory_space=pltpu.VMEM)
    return pl.pallas_call(
        kernel,
        name="join_stats",
        out_shape=[
            jax.ShapeDtypeStruct(tile, jnp.float32),
            jax.ShapeDtypeStruct(stats.shape, jnp.float32),
        ],
        in_specs=[vmem],
        out_specs=[vmem, vmem],
        scratch_shapes=[
            pltpu.VMEM((tensors, groups) + tile, jnp.float32),
            pltpu.VMEM((tensors, groups) + tile, jnp.float32),
            pltpu.VMEM((tensors - 1, groups) + tile, jnp.float32),
            pltpu.VMEM((groups,) + tile, jnp.float32),
            pltpu.VMEM((groups - 1,) + tile, jnp.float32),
            dma((2,)),
            dma((2,)),
            dma((2, tensors - 1)),
            dma((2, tensors - 1)),
            dma((2, groups - 1)),
            dma((2, groups - 1)),
        ],
        cost_estimate=SHORT,
        compiler_params=pltpu.CompilerParams(collective_id=collective_id, has_side_effects=True),
    )(stats)


def spread_tokens(block, slot_block, ends, blocks, half_rows, collective_id):
    tensors, groups = lax.axis_size("tensor"), lax.axis_size("dp")
    rows = 2 * tensors * groups
    width = ends.shape[1]
    vocab_rows = VOCAB // tensors
    slots = slot_block.shape[0]

    def kernel(
        block_ref, slot_ref, ends_ref, ids, targets, kept, places, plan, count,
        held, firsts, own_sem, send_sems, recv_sems,
    ):
        group, side = lax.axis_index("dp"), lax.axis_index("seq")
        first_id = lax.axis_index("tensor") * vocab_rows
        peers = [
            {"dp": lax.rem(group + step // 2, groups), "seq": lax.rem(side + step % 2, 2)}
            for step in range(1, 2 * groups)
        ]
        meet(peers)
        copies = [
            send(block_ref, held.at[group, side], send_sems.at[step], recv_sems.at[step], peer)
            for step, peer in enumerate(peers)
        ]
        own = pltpu.make_async_copy(block_ref, held.at[group, side], own_sem)
        own.start()
        own.wait()
        for copy in copies:
            copy.wait()
        lane = lax.broadcasted_iota(jnp.int32, (1, LANES), 1)
        slot_ids = lax.broadcasted_iota(jnp.int32, (slots, LANES), 0)
        slot_blocks = jnp.broadcast_to(slot_ref[...], (slots, LANES))
        total = jnp.zeros((1, LANES), jnp.int32)
        hits = jnp.zeros((1, LANES), jnp.float32)
        for half in range(2):
            for source in range(groups):
                limit = held[source, half, 2 * tensors : 2 * tensors + 1, :]
                total = total + limit
                for part in range(tensors):
                    row = (half * tensors + part) * groups + source
                    token = held[source, half, part : part + 1, :]
                    ids[row] = token
                    targets[row] = held[source, half, tensors + part : tensors + part + 1, :]
                    kept[row] = jnp.where(lane + part * LANES < limit, 1.0, 0.0)
                    firsts[row : row + 1, :] = jnp.where(part * LANES < limit, 1.0, 0.0)
                    local = token - first_id
                    inside = (local >= 0) & (local < vocab_rows)
                    local = jnp.where(inside, local, 0).astype(jnp.float32)
                    block_of = jnp.floor((local + 0.5) * (0.5 / half_rows))
                    within = local - block_of * (2.0 * half_rows)
                    lower = within >= half_rows
                    inside = inside & (jnp.where(lower, 1, 0) == side)
                    within = (within - jnp.where(lower, 1.0 * half_rows, 0.0)).astype(jnp.int32)
                    same = slot_blocks == block_of.astype(jnp.int32) + blocks
                    slot = jnp.sum(jnp.where(same, slot_ids + 1, 0), axis=0, keepdims=True) - 1
                    inside = inside & (slot >= 0)
                    places[row] = jnp.where(inside, slot * half_rows + within, -1)
                    hits = hits + jnp.where(inside, 1.0, 0.0)
        count[...] = total.astype(jnp.float32)
        shape = (rows, width)
        active = jnp.concatenate([firsts[...]] * (width // LANES), axis=1)
        square = (rows, rows)
        above = jnp.where(
            lax.broadcasted_iota(jnp.int32, square, 1) < lax.broadcasted_iota(jnp.int32, square, 0),
            1.0,
            0.0,
        )
        earlier = times(above.astype(jnp.bfloat16), active.astype(jnp.bfloat16))
        number = jnp.sum(active, axis=0, keepdims=True)
        index = lax.broadcasted_iota(jnp.int32, shape, 0).astype(jnp.float32)
        turns = jnp.where(active > 0.0, earlier, number + index - earlier)
        spot = lax.broadcasted_iota(jnp.int32, shape, 1).astype(jnp.float32) - PLAN_GROUPS
        order = jnp.sum(jnp.where(turns == spot, index, 0.0), axis=0, keepdims=True)
        spot = lax.broadcasted_iota(jnp.int32, (1, width), 1)
        order = jnp.where(spot == 2, number, order)
        order = jnp.where(spot == 3, jnp.sum(hits, axis=1, keepdims=True), order)
        plan[...] = jnp.where(spot < 2, ends_ref[...], order.astype(jnp.int32))

    dma = pltpu.SemaphoreType.DMA
    vmem = pl.BlockSpec(memory_space=pltpu.VMEM)
    shape = (rows, 1, LANES)
    return pl.pallas_call(
        kernel,
        name="spread_tokens",
        out_shape=[
            jax.ShapeDtypeStruct(shape, jnp.int32),
            jax.ShapeDtypeStruct(shape, jnp.int32),
            jax.ShapeDtypeStruct(shape, jnp.float32),
            jax.ShapeDtypeStruct(shape, jnp.int32),
            jax.ShapeDtypeStruct((1, width), jnp.int32),
            jax.ShapeDtypeStruct((1, LANES), jnp.float32),
        ],
        in_specs=[vmem] * 3,
        out_specs=[vmem] * 6,
        scratch_shapes=[
            pltpu.VMEM((groups, 2) + block.shape, jnp.int32),
            pltpu.VMEM((rows, LANES), jnp.float32),
            dma,
            dma((2 * groups - 1,)),
            dma((2 * groups - 1,)),
        ],
        cost_estimate=SHORT,
        compiler_params=pltpu.CompilerParams(collective_id=collective_id, has_side_effects=True),
    )(block, slot_block, ends)


def finish(gain_grads, states, grad_ys, home, keep, table_squares, count, smalls, collective_id):
    tensors, groups = lax.axis_size("tensor"), lax.axis_size("dp")
    block = (8, D)
    gain_rows = 2 * LAYERS + 1
    operands = list(gain_grads) + list(states) + list(grad_ys) + [
        home, keep, table_squares, count
    ] + list(smalls)

    def kernel(*refs):
        refs = list(refs)
        gain_refs = [refs.pop(0) for _ in gain_grads]
        state_refs = [refs.pop(0) for _ in states]
        grad_refs = [refs.pop(0) for _ in grad_ys]
        home_ref, keep_ref, table_ref, count_ref = [refs.pop(0) for _ in range(4)]
        small_refs = [refs.pop(0) for _ in smalls]
        out_refs = [refs.pop(0) for _ in range(8)]
        near, mid, far, near_send, near_recv, mid_send, mid_recv, far_send, far_recv = refs
        group, part, side = lax.axis_index("dp"), lax.axis_index("tensor"), lax.axis_index("seq")
        parts, groups_else = others("tensor"), others("dp")
        meet(
            [{"seq": 1 - side}]
            + [{"tensor": peer} for peer in parts]
            + [{"dp": peer} for peer in groups_else]
        )
        values = []
        for later in range(1, LAYERS + 1):
            grad = grad_refs[later - 1][...]
            for level in range(later + 1):
                values.append(jnp.sum(grad * state_refs[level][...], keepdims=True))
        loss = jnp.where(keep_ref[...] > 0.0, home_ref[0:1, :] - home_ref[1:2, :], 0.0)
        values.append(jnp.sum(loss, keepdims=True))
        values.append(jnp.sum(table_ref[...], keepdims=True))
        lane = lax.broadcasted_iota(jnp.int32, (1, D), 1)
        row = jnp.zeros((1, D), jnp.float32)
        for place, value in enumerate(values):
            row = jnp.where(lane == place, value, row)
        blank = jnp.zeros((8 - gain_rows - 1, D), jnp.float32)
        total = jnp.concatenate([ref[...] for ref in gain_refs] + [row, blank], axis=0)
        stages = [
            ("seq", near, side, [1 - side], near_send, near_recv),
            ("tensor", mid, part, parts, mid_send, mid_recv),
            ("dp", far, group, groups_else, far_send, far_recv),
        ]
        for axis, slots, me, peers, send_sems, recv_sems in stages:
            slots[me] = total
            copies = [
                send(slots.at[me], slots.at[me], send_sems.at[step], recv_sems.at[step], {axis: peer})
                for step, peer in enumerate(peers)
            ]
            for copy in copies:
                copy.wait()
            total = slots[0]
            for index in range(1, slots.shape[0]):
                total = total + slots[index]
        gain_total = total[:gain_rows]
        row = total[gain_rows : gain_rows + 1]

        def pick(place):
            return jnp.sum(jnp.where(lane == place, row, 0.0), axis=1, keepdims=True)

        mix_squares = jnp.sum(jnp.where(lane < MIX_WEIGHTS, row * row, 0.0), axis=1, keepdims=True)
        gain_squares = jnp.sum(gain_total * gain_total, keepdims=True)
        tokens = count_ref[:, 0:1]
        clip_norm = jnp.sqrt(pick(MIX_WEIGHTS + 1) + gain_squares + mix_squares) / tokens
        factor = jnp.minimum(1.0, CLIP_NORM / clip_norm) / tokens
        gain_news = adam_update(
            *[ref[...] for ref in small_refs[:3]], gain_total * factor, RATE_SMALL, 0.0
        )
        mix_news = adam_update(
            *[ref[...] for ref in small_refs[3:]], row[:, :MIX_WEIGHTS] * factor, RATE_SMALL, 0.0
        )
        for ref, value in zip(out_refs[:6], gain_news + mix_news):
            ref[...] = value
        ends = jnp.where(lane == 0, pick(MIX_WEIGHTS), jnp.where(lane == 1, clip_norm, factor))
        out_refs[6][...] = ends[:, :LANES]
        out_refs[7][...] = jnp.broadcast_to(factor, (8, LANES))

    dma = pltpu.SemaphoreType.DMA
    vmem = pl.BlockSpec(memory_space=pltpu.VMEM)
    return pl.pallas_call(
        kernel,
        name="finish",
        out_shape=[jax.ShapeDtypeStruct(value.shape, jnp.float32) for value in smalls]
        + [
            jax.ShapeDtypeStruct((1, LANES), jnp.float32),
            jax.ShapeDtypeStruct((8, LANES), jnp.float32),
        ],
        in_specs=[vmem] * len(operands),
        out_specs=[vmem] * 8,
        scratch_shapes=[
            pltpu.VMEM((2,) + block, jnp.float32),
            pltpu.VMEM((tensors,) + block, jnp.float32),
            pltpu.VMEM((groups,) + block, jnp.float32),
            dma((1,)),
            dma((1,)),
            dma((tensors - 1,)),
            dma((tensors - 1,)),
            dma((groups - 1,)),
            dma((groups - 1,)),
        ],
        cost_estimate=SHORT,
        compiler_params=pltpu.CompilerParams(collective_id=collective_id, has_side_effects=True),
    )(*operands)


SLOT_STEP = 8
PREPARE_STEP = 20


def prepare(slot_block, first_id, master, blocks):
    slots, half_rows, _ = master.shape
    total = slot_block.shape[0]
    steps = -(-total // PREPARE_STEP)
    spare = steps * PREPARE_STEP - total
    slot_block = jnp.pad(slot_block, (0, spare), constant_values=-1)
    slot_block = jnp.concatenate([slot_block, first_id[None]])
    rows = PREPARE_STEP * half_rows

    def kernel(plan_ref, master_ref, table_ref, halves_ref, ids_ref):
        @pl.when(pl.program_id(0) == 0)
        def _():
            halves_ref[...] = jnp.zeros_like(halves_ref)

        for place in range(PREPARE_STEP):
            slot = pl.program_id(0) * PREPARE_STEP + place
            value = jnp.where(slot < slots, master_ref[place], 0.0).astype(jnp.bfloat16)
            table_ref[place * half_rows : (place + 1) * half_rows, :] = value

            block = plan_ref[slot]
            ids = plan_ref[steps * PREPARE_STEP] + (block - blocks) * (2 * half_rows)
            ids = ids + lax.broadcasted_iota(jnp.int32, (half_rows, 1), 0)
            ids_ref[place * half_rows : (place + 1) * half_rows, :] = jnp.where(
                block >= blocks, ids, -1
            )

            @pl.when((block >= 0) & (block < blocks))
            def _():
                halves_ref[block] = value

    last = (slots - 1) // PREPARE_STEP
    return pl.pallas_call(
        kernel,
        name="prepare",
        grid_spec=pltpu.PrefetchScalarGridSpec(
            num_scalar_prefetch=1,
            grid=(steps,),
            in_specs=[
                pl.BlockSpec(
                    (PREPARE_STEP, half_rows, D), lambda step, plan: (jnp.minimum(step, last), 0, 0)
                )
            ],
            out_specs=[
                pl.BlockSpec((rows, D), lambda step, plan: (step, 0)),
                pl.BlockSpec((blocks, half_rows, D), lambda step, plan: (0, 0, 0)),
                pl.BlockSpec((rows, 1), lambda step, plan: (step, 0)),
            ],
        ),
        out_shape=[
            jax.ShapeDtypeStruct((total * half_rows, D), jnp.bfloat16),
            jax.ShapeDtypeStruct((blocks, half_rows, D), jnp.bfloat16),
            jax.ShapeDtypeStruct((total * half_rows, 1), jnp.int32),
        ],
        cost_estimate=SHORT,
        compiler_params=pltpu.CompilerParams(vmem_limit_bytes=60 << 20),
    )(slot_block, master)


TILE = TILE_GROUPS * LANES
PICKED = 768


def row_of(values_ref, groups, place=0):
    rows = [values_ref[group, place : place + 1, :] for group in groups]
    return jnp.concatenate(rows, axis=1)


def tile_row(values_ref, tile):
    start = tile * TILE_GROUPS
    return row_of(values_ref, [start + place for place in range(TILE_GROUPS)])


PLAN_GROUPS = 4


def chunk_of(plan_ref, step):
    return pl.ds(pl.multiple_of(plan_ref[0] + step * ROW_STEP, 16), ROW_STEP)


def chunks_of(plan_ref):
    return (plan_ref[1] - plan_ref[0] + ROW_STEP - 1) // ROW_STEP


def whole(shape):
    return pl.BlockSpec(shape, lambda step, plan: (0,) * len(shape), pipeline_mode=pl.Buffered(1))


def last_tile(plan):
    return (plan[2] - 1) // TILE_GROUPS


def group_specs():
    return [
        pl.BlockSpec(
            (LANES, D),
            lambda step, plan, place=place: (
                plan[PLAN_GROUPS + jnp.minimum(step, last_tile(plan)) * TILE_GROUPS + place],
                0,
            ),
        )
        for place in range(TILE_GROUPS)
    ]


def powers_spec(rows):
    return pl.BlockSpec((rows, TILE), lambda step, plan: (0, jnp.minimum(step, last_tile(plan))))


def groups_of(plan_ref):
    start = PLAN_GROUPS + pl.program_id(0) * TILE_GROUPS
    return [plan_ref[start + place] for place in range(TILE_GROUPS)]


ROWS_SPEC = pl.BlockSpec((TILE, D), lambda step, plan: (step, 0))


def local_call(name, kernel, steps, plan, operands, in_specs, out_shape, out_specs, scratch):
    return pl.pallas_call(
        kernel,
        name=name,
        grid_spec=pltpu.PrefetchScalarGridSpec(
            num_scalar_prefetch=1,
            grid=(steps,),
            in_specs=in_specs,
            out_specs=out_specs,
            scratch_shapes=scratch,
        ),
        out_shape=out_shape,
        cost_estimate=SHORT,
        compiler_params=pltpu.CompilerParams(vmem_limit_bytes=60 << 20),
    )(plan, *operands)


def ones_where(condition):
    return jnp.where(condition, 1.0, 0.0).astype(jnp.bfloat16)


def picks(rank_row):
    return ones_where(lax.broadcasted_iota(jnp.int32, (PICKED, TILE), 0) == rank_row)


def rows_picked(plan_ref, step, place_row):
    start = plan_ref[0] + step * ROW_STEP
    row = lax.broadcasted_iota(jnp.int32, (ROW_STEP, PICKED), 0) + start
    return ones_where(row == place_row)


def look_up(plan, row_ids, tokens, places, table):
    rows, groups = table.shape[0], tokens.shape[0]
    steps = groups // TILE_GROUPS

    def kernel(
        plan_ref, ids_ref, tokens_ref, places_ref, table_ref, out_ref, ranks_ref, picked_ref, acc, picked
    ):
        tile = pl.program_id(0)
        few = plan_ref[3] <= PICKED

        @pl.when(tile == 0)
        def _():
            held = places_ref[...].reshape(groups, LANES) >= 0
            ones = ones_where(held)
            lane = (LANES, LANES)
            before = ones_where(
                lax.broadcasted_iota(jnp.int32, lane, 0) < lax.broadcasted_iota(jnp.int32, lane, 1)
            )
            group = (groups, groups)
            above = ones_where(
                lax.broadcasted_iota(jnp.int32, group, 1) < lax.broadcasted_iota(jnp.int32, group, 0)
            )
            totals = jnp.sum(ones.astype(jnp.float32), axis=1, keepdims=True)
            totals = jnp.broadcast_to(totals, (groups, LANES)).astype(jnp.bfloat16)
            ranks = (times(ones, before) + times(above, totals)).astype(jnp.int32)
            ranks_ref[...] = jnp.where(held, ranks, -1).reshape(groups, 1, LANES)

        @pl.when((tile == 0) & few)
        def _():
            def digits_of(step, total):
                place = tile_row(places_ref, step)
                high = lax.shift_right_arithmetic(place, 6)
                digits = jnp.concatenate([high, place - high * 64] * 4, axis=0)
                digits = digits.astype(jnp.float32).astype(jnp.bfloat16)
                return total + contract_last(digits, picks(tile_row(ranks_ref, step)))

            digits = lax.fori_loop(0, steps, digits_of, jnp.zeros((8, PICKED), jnp.float32))
            place = (digits[0:1] * 64.0 + digits[1:2]).astype(jnp.int32)
            index = lax.broadcasted_iota(jnp.int32, (1, PICKED), 1)
            place = jnp.where(index < plan_ref[3], place, -1)
            picked_ref[...] = jnp.broadcast_to(place, (8, PICKED))
            acc[:PICKED, :] = jnp.zeros((PICKED, D), jnp.float32)

            def one(step, carry):
                hits = rows_picked(plan_ref, step, place)
                acc[:PICKED, :] += contract_first(hits, table_ref[chunk_of(plan_ref, step), :])
                return carry

            lax.fori_loop(0, chunks_of(plan_ref), one, 0)
            picked[...] = acc[:PICKED, :].astype(jnp.bfloat16)

        @pl.when(few)
        def _():
            hits = picks(tile_row(ranks_ref, tile))
            out_ref[...] = contract_first(hits, picked[...]).astype(jnp.bfloat16)

        @pl.when(jnp.logical_not(few))
        def _():
            acc[...] = jnp.zeros_like(acc)
            wanted = tile_row(tokens_ref, tile)

            def one(step, carry):
                chunk = chunk_of(plan_ref, step)
                hits = ones_where(ids_ref[chunk, :] == wanted)
                acc[...] += contract_first(hits, table_ref[chunk, :])
                return carry

            lax.fori_loop(0, chunks_of(plan_ref), one, 0)
            out_ref[...] = acc[...].astype(jnp.bfloat16)

    lanes = (groups, 1, LANES)
    return local_call(
        "look_up",
        kernel,
        steps,
        plan,
        (row_ids, tokens, places, table),
        [whole((rows, 1)), whole(lanes), whole(lanes), whole((rows, D))],
        [
            jax.ShapeDtypeStruct((groups * LANES, D), jnp.bfloat16),
            jax.ShapeDtypeStruct(lanes, jnp.int32),
            jax.ShapeDtypeStruct((8, PICKED), jnp.int32),
        ],
        [ROWS_SPEC, whole(lanes), whole((8, PICKED))],
        [pltpu.VMEM((TILE, D), jnp.float32), pltpu.VMEM((PICKED, D), jnp.bfloat16)],
    )


def head_forward(plan, row_ids, labels, table, final):
    rows, groups = table.shape[0], labels.shape[0]
    steps = groups // TILE_GROUPS

    def kernel(plan_ref, ids_ref, labels_ref, table_ref, *rest):
        final_refs, (powers_ref, stats_ref, scores, hidden) = rest[:TILE_GROUPS], rest[TILE_GROUPS:]
        blank = jnp.zeros((1, TILE), jnp.float32)
        active = pl.program_id(0) <= last_tile(plan_ref)
        own = groups_of(plan_ref)

        def put(top, total, target):
            pad = jnp.zeros((5, LANES), jnp.float32)
            for place in range(TILE_GROUPS):
                lanes = slice(place * LANES, (place + 1) * LANES)
                stats_ref[own[place]] = jnp.concatenate(
                    [top[:, lanes], total[:, lanes], target[:, lanes], pad], axis=0
                )

        @pl.when(jnp.logical_not(active))
        def _():
            put(blank - 1e30, blank, blank)

        @pl.when(active)
        def _():
            wanted = row_of(labels_ref, own)
            for place, ref in enumerate(final_refs):
                hidden[place * LANES : (place + 1) * LANES, :] = ref[...]

            def first(step, carry):
                top, target = carry
                chunk = chunk_of(plan_ref, step)
                ids = ids_ref[chunk, :]
                raw = contract_last(table_ref[chunk, :], hidden[...])
                raw = jnp.where(ids >= 0, raw, -1e30)
                scores[chunk, :] = raw
                top = jnp.maximum(top, jnp.max(raw, axis=0, keepdims=True))
                target = target + jnp.sum(
                    jnp.where(ids == wanted, raw, 0.0), axis=0, keepdims=True
                )
                return (top, target)

            top, target = lax.fori_loop(0, chunks_of(plan_ref), first, (blank - 1e30, blank))

            def second(step, total):
                chunk = chunk_of(plan_ref, step)
                powers = jnp.exp(scores[chunk, :] - top)
                powers_ref[chunk, :] = powers.astype(jnp.bfloat16)
                return total + jnp.sum(powers, axis=0, keepdims=True)

            put(top, lax.fori_loop(0, chunks_of(plan_ref), second, blank), target)

    return local_call(
        "head_forward",
        kernel,
        steps,
        plan,
        (row_ids, labels, table) + (final,) * TILE_GROUPS,
        [whole((rows, 1)), whole((groups, 1, LANES)), whole((rows, D))] + group_specs(),
        [
            jax.ShapeDtypeStruct((rows, groups * LANES), jnp.bfloat16),
            jax.ShapeDtypeStruct((groups, 8, LANES), jnp.float32),
        ],
        [powers_spec(rows), whole((groups, 8, LANES))],
        [pltpu.VMEM((rows, TILE), jnp.float32), pltpu.VMEM((TILE, D), jnp.bfloat16)],
    )


def head_backward(plan, row_ids, labels, keep, stats, log_totals, table, final, powers):
    rows, groups = table.shape[0], labels.shape[0]
    steps = groups // TILE_GROUPS

    def kernel(plan_ref, ids_ref, labels_ref, keep_ref, stats_ref, logs_ref, table_ref, powers_ref, *rest):
        final_refs = rest[:TILE_GROUPS]
        grad_final_ref, grad_table_ref, acc, hidden, low, sems = rest[TILE_GROUPS:]
        tile = pl.program_id(0)
        slot = lax.rem(tile, 2)
        active = tile <= last_tile(plan_ref)

        def copies(step):
            start, side = PLAN_GROUPS + step * TILE_GROUPS, lax.rem(step, 2)
            return [
                pltpu.make_async_copy(
                    low.at[side, place],
                    grad_final_ref.at[plan_ref[start + place]],
                    sems.at[side, place],
                )
                for place in range(TILE_GROUPS)
            ]

        @pl.when(tile == 0)
        def _():
            grad_table_ref[...] = jnp.zeros_like(grad_table_ref)

        @pl.when(tile >= 2)
        def _():
            for copy in copies(tile - 2):
                copy.wait()

        acc[...] = jnp.zeros_like(acc)

        @pl.when(active)
        def _():
            own = groups_of(plan_ref)
            wanted, kept = row_of(labels_ref, own), row_of(keep_ref, own)
            tops = row_of(stats_ref, own)
            scale = jnp.exp(tops - row_of(logs_ref, own)) * kept
            for place, ref in enumerate(final_refs):
                hidden[place * LANES : (place + 1) * LANES, :] = ref[...]

            def one(step, carry):
                chunk = chunk_of(plan_ref, step)
                grads = powers_ref[chunk, :].astype(jnp.float32) * scale
                grads = grads - jnp.where(ids_ref[chunk, :] == wanted, kept, 0.0)
                grads = grads.astype(jnp.bfloat16)
                grad_table_ref[chunk, :] += times(grads, hidden[...])
                acc[...] += contract_first(grads, table_ref[chunk, :])
                return carry

            lax.fori_loop(0, chunks_of(plan_ref), one, 0)

        low[slot] = acc[...].astype(jnp.bfloat16).reshape(TILE_GROUPS, LANES, D)
        for copy in copies(tile):
            copy.start()

        @pl.when(tile == steps - 1)
        def _():
            for step in range(max(0, steps - 2), steps):
                for copy in copies(step):
                    copy.wait()

    lanes = (groups, 1, LANES)
    return local_call(
        "head_backward",
        kernel,
        steps,
        plan,
        (row_ids, labels, keep, stats, log_totals, table, powers) + (final,) * TILE_GROUPS,
        [
            whole((rows, 1)),
            whole(lanes),
            whole(lanes),
            whole((groups, 8, LANES)),
            whole((groups, 8, LANES)),
            whole((rows, D)),
            powers_spec(rows),
        ]
        + group_specs(),
        [
            jax.ShapeDtypeStruct((groups, LANES, D), jnp.bfloat16),
            jax.ShapeDtypeStruct((rows, D), jnp.float32),
        ],
        [pl.BlockSpec(memory_space=pl.ANY), whole((rows, D))],
        [
            pltpu.VMEM((TILE, D), jnp.float32),
            pltpu.VMEM((TILE, D), jnp.bfloat16),
            pltpu.VMEM((2, TILE_GROUPS, LANES, D), jnp.bfloat16),
            pltpu.SemaphoreType.DMA((2, TILE_GROUPS)),
        ],
    )


def look_back(
    plan, slot_plan, slots, row_ids, tokens, ranks, picked, grad_start, grad_table, layer_grads
):
    rows, groups = grad_table.shape[0], tokens.shape[0]
    steps = groups // TILE_GROUPS
    half_rows = layer_grads[0].shape[1]
    block = SLOT_STEP * half_rows
    kinds = len(layer_grads)

    def kernel(plan_ref, slot_ref, ids_ref, tokens_ref, ranks_ref, picked_ref, grad_ref, table_ref, *rest):
        layer_refs = rest[:kinds]
        slots_ref, squares_ref, acc, held, out_ref = rest[kinds:]
        step = pl.program_id(0)
        few = plan_ref[3] <= PICKED

        @pl.when(step == 0)
        def _():
            acc[...] = jnp.zeros_like(acc)
            squares_ref[...] = jnp.zeros_like(squares_ref)

        @pl.when((step < steps) & few)
        def _():
            acc[...] += times(picks(tile_row(ranks_ref, step)), grad_ref[...])

        @pl.when((step < steps) & jnp.logical_not(few))
        def _():
            held[step] = grad_ref[...]

        @pl.when(step >= steps)
        def _():
            start = (step - steps) * block

            @pl.when(few)
            def _():
                row = lax.broadcasted_iota(jnp.int32, (block, PICKED), 0) + start
                hits = ones_where(row == picked_ref[0:1, :])
                out_ref[...] = table_ref[...] + times(hits, acc[...].astype(jnp.bfloat16))

            @pl.when(jnp.logical_not(few))
            def _():
                out_ref[...] = table_ref[...]
                ids = ids_ref[pl.ds(pl.multiple_of(start, 16), block), :]

                def one(tile, carry):
                    hits = ones_where(ids == tile_row(tokens_ref, tile))
                    out_ref[...] += times(hits, held[tile])
                    return carry

                lax.fori_loop(0, steps, one, 0)

            for place in range(SLOT_STEP):
                slot = (step - steps) * SLOT_STEP + place
                kind = slot_ref[0, slot]
                part = slice(place * half_rows, (place + 1) * half_rows)

                for index in range(kinds):

                    @pl.when(kind == index)
                    def _():
                        layer = layer_refs[index][slot_ref[1 + index, slot]]
                        out_ref[part, :] = layer.astype(jnp.float32)

                @pl.when(kind < 0)
                def _():
                    out_ref[part, :] = jnp.zeros((half_rows, D), jnp.float32)

                slots_ref[place] = out_ref[part, :]

            values = out_ref[...]
            squares_ref[...] += (values * values).reshape(block // 8, 8, D).sum(axis=0)

    def fixed(shape):
        return pl.BlockSpec(
            shape, lambda step, plan, slot: (0,) * len(shape), pipeline_mode=pl.Buffered(1)
        )

    lanes = (groups, 1, LANES)
    row_spec = pl.BlockSpec((block, D), lambda step, plan, slot: (jnp.maximum(step - steps, 0), 0))
    return pl.pallas_call(
        kernel,
        name="look_back",
        grid_spec=pltpu.PrefetchScalarGridSpec(
            num_scalar_prefetch=2,
            grid=(steps + -(-slots // SLOT_STEP),),
            in_specs=[
                fixed((rows, 1)),
                fixed(lanes),
                fixed(lanes),
                fixed((8, PICKED)),
                pl.BlockSpec((TILE, D), lambda step, plan, slot: (jnp.minimum(step, steps - 1), 0)),
                row_spec,
            ]
            + [fixed(grads.shape) for grads in layer_grads],
            out_specs=[
                pl.BlockSpec(
                    (SLOT_STEP, half_rows, D),
                    lambda step, plan, slot: (jnp.maximum(step - steps, 0), 0, 0),
                ),
                fixed((8, D)),
            ],
            scratch_shapes=[
                pltpu.VMEM((PICKED, D), jnp.float32),
                pltpu.VMEM((steps, TILE, D), jnp.bfloat16),
                pltpu.VMEM((block, D), jnp.float32),
            ],
        ),
        out_shape=[
            jax.ShapeDtypeStruct((slots, half_rows, D), jnp.float32),
            jax.ShapeDtypeStruct((8, D), jnp.float32),
        ],
        cost_estimate=SHORT,
        compiler_params=pltpu.CompilerParams(vmem_limit_bytes=60 << 20),
    )(
        plan,
        slot_plan,
        row_ids,
        tokens,
        ranks,
        picked,
        grad_start,
        grad_table,
        *layer_grads,
    )


def grads_home(level):
    return [(2 * level, 0), (2 * level + 1, 0), (2 * level + 1, 1)]


def body(
    token_ids,
    labels,
    real_counts,
    owners,
    master,
    first_moment,
    second_moment,
    gains,
    gains_first,
    gains_second,
    mix,
    mix_first,
    mix_second,
):
    tensors = lax.axis_size("tensor")
    groups = lax.axis_size("dp")
    group = lax.axis_index("dp")
    tensor_part = lax.axis_index("tensor")
    seq_part = lax.axis_index("seq")
    slots, half_rows, _ = master.shape
    seq_count, half_len = token_ids.shape
    row_count = seq_count * half_len
    share = row_count // tensors
    head_rows = 3 * D // tensors
    out_rows = D // tensors
    unit_rows = FF // tensors
    layer_rows = head_rows + out_rows + 2 * unit_rows
    layer_blocks = layer_rows // (2 * half_rows)
    blocks = LAYERS * layer_blocks
    vocab_rows = VOCAB // tensors
    local_heads = HEADS // tensors

    slot_rank = slot_table(owners)
    block_ids = jnp.arange(owners.shape[0], dtype=jnp.int32)
    mine = owners == group
    match = (jnp.arange(slots)[:, None] == slot_rank[None, :]) & mine[None, :]
    slot_block = jnp.sum(jnp.where(match, block_ids[None, :] + 1, 0), axis=1) - 1
    spare = -(-ROW_STEP // half_rows)
    spare += -(slots + spare) % SLOT_STEP
    held = jnp.sum(jnp.where(mine, 1, 0)) * half_rows
    first_held = jnp.sum(jnp.where(mine & (block_ids < blocks), 1, 0)) * half_rows
    slot_block_all = jnp.pad(slot_block, (0, spare), constant_values=-1).astype(jnp.int32)
    third = layer_blocks // 3
    which, within = slot_block_all // third, slot_block_all % third
    homes = [home for level in range(LAYERS) for home in grads_home(level)]
    arrays = 1 + max(array for array, _ in homes)
    kind, index = jnp.full(which.shape, -1), jnp.zeros_like(which)
    for place, (array, part) in enumerate(homes):
        kind = jnp.where(which == place, array, kind)
        index = jnp.where(which == place, within + part * third, index)
    kind = jnp.where(slot_block_all >= blocks, arrays, jnp.where(slot_block_all < 0, -1, kind))
    slot_plan = jnp.stack(
        [kind] + [jnp.where(kind == array, index, 0) for array in range(arrays)]
    ).astype(jnp.int32)

    packed = jnp.concatenate(
        [
            token_ids.reshape(tensors, LANES),
            labels.reshape(tensors, LANES),
            jnp.broadcast_to(real_counts[:, None], (16 - 2 * tensors, LANES)),
        ],
        axis=0,
    )
    width = -(-(2 * tensors * groups + PLAN_GROUPS) // LANES) * LANES
    lane = jnp.arange(width)[None, :]
    ends = jnp.where(lane == 0, first_held, jnp.where(lane == 1, held, 0)).astype(jnp.int32)
    ids_all, labels_all, keep_all, places, plan, count = spread_tokens(
        packed, slot_block_all[:, None], ends, blocks, half_rows, 15
    )
    plan = plan.reshape(-1)
    order = (2, tensors, groups, share)

    first_id = (tensor_part * vocab_rows + seq_part * half_rows).astype(jnp.int32)
    table, halves, row_ids = prepare(slot_block_all, first_id, master, blocks)

    def weights_line(*starts):
        return Line([(halves, start * third, third) for start in starts], True)

    def as_table(joined):
        return joined.reshape(-1, D)

    positions = seq_part * half_len + jnp.arange(row_count) % half_len
    steps_half = jnp.arange(HEAD_DIM // 2).astype(jnp.float32)
    freqs = 10000.0 ** (-2.0 * steps_half / HEAD_DIM)
    angles = freqs[:, None] * positions.astype(jnp.float32)[None, :]
    cosine, sine = jnp.cos(angles), jnp.sin(angles)

    looked, ranks, picked = look_up(plan, row_ids, ids_all, places, table)
    looked = looked.reshape(order + (D,))
    gain = [gains[i : i + 1] for i in range(2 * LAYERS + 1)]
    piece = ((share, D), jnp.float32)

    def normed_of(total, gain_row):
        return (total[...], layer_norm_parts(total[...])[0] * gain_row[...])

    def inner_of(total, stream, gain_row):
        inner = stream + total
        return (inner, layer_norm_parts(inner)[0] * gain_row)

    def outcome_of(base, total, inner, gain_row, *rest):
        states, scalars = rest[:-1], rest[-1]
        outcome = inner + total
        stream = scalars[base + len(states)] * outcome
        for source, state in enumerate(states):
            stream = stream + scalars[base + source] * state
        return (outcome, stream, layer_norm_parts(stream)[0] * gain_row)

    start, normed, joined = reduce_rows(
        "normed", looked, (14, 18, 1), weights_line(0, 1), normed_of, [gain[0]], [], [piece]
    )
    table_one = as_table(joined)
    attention_table, up = table_one, (table_one, 1)
    tables = []
    states, streams, inners, kept_all = [start], [start], [], []
    for level in range(LAYERS):
        here, last = 3 * level, level == LAYERS - 1
        carried = [] if last else [here + 3]
        carried += [here + 1, here + 2] if level else [here + 2]
        inner, normed_two, queries, both, logs, attended, joined = tensor_step(
            f"inner_{level}",
            inner_of,
            attention_work(normed, attention_table, cosine, sine),
            (streams[level], gain[2 * level + 1]),
            (),
            [piece],
            True,
            2 if level == 0 else 15 + level,
            weights_line(*carried),
        )
        kept = (queries, both, logs, attended)
        joined = as_table(joined)
        down = (joined, len(carried) - 1)
        up = (joined, len(carried) - 2) if level else up
        tables.append((attention_table, up, down))
        attention_table = joined
        outcome, stream, normed_next, hidden, activated = tensor_step(
            f"outcome_{level}",
            partial(outcome_of, (level + 1) * (level + 2) // 2 - 1),
            unit_work(normed_two, up, down),
            [inner, gain[2 * level + 2]] + states,
            (mix,),
            [piece, piece] + ([((share, D), jnp.bfloat16)] if last else []),
            not last,
            3 + level,
        )
        inners.append(inner)
        kept_all.append((normed, kept, normed_two, (hidden, activated)))
        states.append(outcome)
        streams.append(stream)
        normed = normed_next

    final_all = gather_all(normed, 3 + LAYERS)[0].reshape(-1, D)
    powers, stats = head_forward(plan, row_ids, labels_all, table, final_all)
    home, log_totals = join_stats(
        stats.reshape((2, tensors, groups, 8, LANES)), 4 + LAYERS
    )
    grad_final, grad_table = head_backward(
        plan,
        row_ids,
        labels_all,
        keep_all,
        stats,
        log_totals.reshape(-1, 8, LANES),
        table,
        final_all,
        powers,
    )
    grad_final = grad_final.reshape(order + (D,))

    row = ((1, D), jnp.float32)

    def top_of(total, stream, gain_row, scalars):
        grad_top, grad_gain = norm_pull(total[...], gain_row[...], stream[...])
        grad_state = scalars[MIX_WEIGHTS - 1] * grad_top
        return (grad_top, grad_state, grad_gain, grad_state)

    def inner_back(total, grad_out, inner, gain_row):
        grad, grad_gain = norm_pull(total, gain_row, inner)
        grad = grad_out + grad
        return (grad, grad_gain, grad)

    def stream_back(block, total, grad_inner, stream, gain_row, *rest):
        grad_ys, scalars = rest[:-1], rest[-1]
        grad, grad_gain = norm_pull(total, gain_row, stream)
        grad = grad_inner + grad
        state = grad if block == 0 else scalars[block * (block + 1) // 2 - 1 + block] * grad
        for offset, grad_y in enumerate(grad_ys):
            later = block + 1 + offset
            state = state + scalars[later * (later + 1) // 2 - 1 + block] * grad_y
        return (grad, state, grad_gain, state)

    grad_ys = [None] * (LAYERS + 1)
    gain_grads = [None] * (2 * LAYERS + 1)
    layer_grads, attention_grads = [None] * (2 * LAYERS), None
    grad_ys[LAYERS], grad_state, gain_grads[2 * LAYERS], grad_branch = reduce_rows(
        "top_back",
        grad_final,
        (0, 0, 5 + LAYERS),
        None,
        top_of,
        [streams[LAYERS], gain[2 * LAYERS]],
        [mix],
        [piece, piece, row],
    )
    for level in reversed(range(LAYERS)):
        normed, kept, normed_two, unit_kept = kept_all[level]
        attention_table, up, down = tables[level]
        grad_inner, gain_grads[2 * level + 1], grad_attn, unit_grads, *summed = tensor_step(
            f"inner_back_{level}",
            inner_back,
            unit_back_work(grad_branch, normed_two, up, down, unit_kept, half_rows),
            (grad_state, inners[level], gain[2 * level + 1]),
            (),
            [piece, row],
            True,
            6 + LAYERS if level == 0 else 19 + level,
            None if attention_grads is None else Line([(attention_grads, 0, third)], False),
        )
        if summed:
            layer_grads[2 * (level + 1)] = summed[0]
        grad_ys[level], grad_state, gain_grads[2 * level], grad_branch, attention_grads, summed = (
            tensor_step(
                f"stream_back_{level}",
                partial(stream_back, level),
                attention_back_work(
                    grad_attn, normed, attention_table, kept, cosine, sine, half_rows
                ),
                [grad_inner, streams[level], gain[2 * level]] + grad_ys[level + 1 :],
                (mix,),
                [piece, piece, row] + ([] if level else [((share, D), jnp.bfloat16)]),
                level > 0,
                7 + LAYERS + level,
                Line([(unit_grads, 0, 2 * third)], False),
            )
        )
        layer_grads[2 * level + 1] = summed

    grad_start_all, layer_grads[0] = gather_all(
        grad_branch, 13, Line([(attention_grads, 0, third)], False)
    )
    grad_start_all = grad_start_all.reshape(-1, D)
    owned, table_squares = look_back(
        plan,
        slot_plan,
        slots,
        row_ids,
        ids_all,
        ranks,
        picked,
        grad_start_all,
        grad_table,
        layer_grads,
    )
    keep = jnp.where(
        tensor_part * share + jnp.arange(share) < real_counts[0], 1.0, 0.0
    ).astype(jnp.float32)
    news = finish(
        gain_grads,
        states,
        grad_ys[1:],
        home,
        keep[None],
        table_squares,
        count,
        (gains, gains_first, gains_second, mix[None], mix_first[None], mix_second[None]),
        7 + 2 * LAYERS,
    )
    new_gains, new_gains_first, new_gains_second = news[:3]
    new_mix, new_mix_first, new_mix_second = [value[0] for value in news[3:6]]
    loss_sum, clip_norm = news[6][0, 0], news[6][0, 1]
    token_count = count[0, 0]
    owned = owned * news[7][0, 0]
    new_master, new_first, new_second = adam_update(
        master, first_moment, second_moment, owned, RATE_MATRIX, DECAY_MATRIX
    )
    return (
        new_master,
        new_first,
        new_second,
        new_gains,
        new_gains_first,
        new_gains_second,
        new_mix,
        new_mix_first,
        new_mix_second,
        loss_sum,
        token_count,
        clip_norm,
    )


def solution(mesh):
    return jax.shard_map(
        body,
        mesh=mesh,
        in_specs=(
            P("dp", "seq"),
            P("dp", "seq"),
            P(("dp", "seq")),
            P(),
            P("dp", ("tensor", "seq"), None),
            P("dp", ("tensor", "seq"), None),
            P("dp", ("tensor", "seq"), None),
            P(),
            P(),
            P(),
            P(),
            P(),
            P(),
        ),
        out_specs=(
            P("dp", ("tensor", "seq"), None),
            P("dp", ("tensor", "seq"), None),
            P("dp", ("tensor", "seq"), None),
            P(),
            P(),
            P(),
            P(),
            P(),
            P(),
            P(),
            P(),
            P(),
        ),
        check_vma=False,
    )
```

```python
from functools import partial

import jax
import jax.numpy as jnp
from jax import lax
from jax.experimental import pallas as pl
from jax.experimental.pallas import tpu as pltpu
from jax.sharding import PartitionSpec as P

D = 768
HEADS = 12
HEAD_DIM = 64
FF = 3072
VOCAB = 50304
LAYERS = 2
STEP_COUNT = 10
MIX_WEIGHTS = 5


EPS_NORM = 1e-05
CLIP_NORM = 0.01
BETA_ONE = 0.9
BETA_TWO = 0.95
ADAM_EPS = 1e-08
RATE_MATRIX = 0.04
RATE_SMALL = 0.4
DECAY_MATRIX = 0.1


def contract_last(left, right):
    return lax.dot_general(
        left, right, (((1,), (1,)), ((), ())), preferred_element_type=jnp.float32
    )


def contract_first(left, right):
    return lax.dot_general(
        left, right, (((0,), (0,)), ((), ())), preferred_element_type=jnp.float32
    )


def slot_table(owners):
    ranks = jnp.arange(owners.shape[0])
    same = (owners[None, :] == owners[:, None]) & (ranks[None, :] < ranks[:, None])
    return jnp.sum(jnp.where(same, 1, 0), axis=1).astype(jnp.int32)


def adam_update(weight, first, second, grad, rate, decay):
    first = BETA_ONE * first + (1.0 - BETA_ONE) * grad
    second = BETA_TWO * second + (1.0 - BETA_TWO) * grad * grad
    first_hat = first / (1.0 - BETA_ONE**STEP_COUNT)
    second_hat = second / (1.0 - BETA_TWO**STEP_COUNT)
    weight = weight - rate * (first_hat / (jnp.sqrt(second_hat) + ADAM_EPS) + decay * weight)
    return (weight, first, second)


MESH = pl.DeviceIdType.MESH
ROW_STEP = 400
TILE_GROUPS = 8
LANES = 128
SHORT = pl.CostEstimate(flops=1000, bytes_accessed=1000, transcendentals=0)


def meet(peers):
    gate = pltpu.get_barrier_semaphore()
    for peer in peers:
        pl.semaphore_signal(gate, inc=1, device_id=peer, device_id_type=MESH)
    pl.semaphore_wait(gate, len(peers))


def others(axis):
    count, me = lax.axis_size(axis), lax.axis_index(axis)
    return [lax.rem(me + step, count) for step in range(1, count)]


def behind(axis, step):
    count, me = lax.axis_size(axis), lax.axis_index(axis)
    return lax.rem(me + count - step, count)


def send(source, target, send_sem, recv_sem, device):
    copy = pltpu.make_async_remote_copy(
        src_ref=source,
        dst_ref=target,
        send_sem=send_sem,
        recv_sem=recv_sem,
        device_id=device,
        device_id_type=MESH,
    )
    copy.start()
    return copy


def layer_norm_parts(stream):
    center = stream - jnp.mean(stream, -1, keepdims=True)
    inverse = lax.rsqrt(jnp.mean(center * center, -1, keepdims=True) + EPS_NORM)
    return center * inverse, inverse


def norm_pull(grad_normed, gain, stream):
    scaled, inverse = layer_norm_parts(stream)
    grad_scaled = grad_normed * gain
    grad_stream = inverse * (
        grad_scaled
        - jnp.mean(grad_scaled, -1, keepdims=True)
        - scaled * jnp.mean(grad_scaled * scaled, -1, keepdims=True)
    )
    return grad_stream, jnp.sum(grad_normed * scaled, axis=0, keepdims=True)


class Work:
    def __init__(self, before, during, operands, specs, outs, scratch, after=None, twins=False):
        self.before, self.during, self.after, self.twins = before, during, after, twins
        self.operands, self.specs, self.outs, self.scratch = operands, specs, outs, scratch


def tensor_step(name, function, work, extras, scalars, outs, gather, collective_id, line=None):
    parts = lax.axis_size("tensor")
    share = extras[0].shape[0]
    reduce = work is not None
    work = work or Work(None, None, [], [], [], [])

    def kernel(*refs):
        refs = list(refs)

        def take(count):
            return [refs.pop(0) for _ in range(count)]

        work_refs = take(len(work.operands))
        extra_refs = take(len(extras))
        scalar_refs = take(len(scalars))
        source_refs = take(len(line.operands)) if line else []
        out_refs = take(len(outs))
        (full,) = take(1) if gather else [None]
        work_outs = take(len(work.outs))
        (joined,) = take(1) if line else [None]
        send_sems, recv_sems = take(2)
        partial_ref, outgoing, arrived = take(3) if reduce else [None] * 3
        if line:
            line.bind(source_refs, joined, take(len(line.scratch)))
            line.load()

        def tick(count=1):
            if line:
                line.steps(count)

        me, side = lax.axis_index("tensor"), lax.axis_index("seq")
        peers = others("tensor")
        twin = {"seq": 1 - side}
        twins = work.twins or (line and line.share)
        meet(
            [{"tensor": peer} for peer in peers]
            + [twin] * bool(twins)
            + ([{"dp": peer} for peer in others("dp")] if line else [])
        )
        if line:
            line.begin()
        total = None
        if reduce:
            work.before(work_refs, work_outs, refs, partial_ref, tick)
            copies = []
            for step, peer in enumerate(peers):
                rows = pl.ds(pl.multiple_of(peer * share, share), share)
                outgoing[step] = partial_ref[rows, :].astype(jnp.bfloat16)
                copies.append(
                    send(
                        outgoing.at[step],
                        arrived.at[step],
                        send_sems.at[0, step],
                        recv_sems.at[0, step],
                        {"tensor": peer},
                    )
                )
            if work.during:
                work.during(work_refs, work_outs, refs)
            tick(6)
            total = partial_ref[pl.ds(pl.multiple_of(me * share, share), share), :]
            for step, copy in enumerate(copies):
                copy.wait()
                total = total + arrived[step].astype(jnp.float32)
        results = function(total, *[ref[...] for ref in extra_refs], *scalar_refs)
        for ref, value in zip(out_refs, results):
            ref[...] = value.astype(ref.dtype)
        if gather:
            full[me] = results[len(outs)].astype(jnp.bfloat16)
            copies = [
                send(
                    full.at[me],
                    full.at[me],
                    send_sems.at[1, step],
                    recv_sems.at[1, step],
                    {"tensor": peer},
                )
                for step, peer in enumerate(peers)
            ]
        if work.after:
            work.after(work_refs, work_outs, refs)
        tick(None)
        if gather:
            for copy in copies:
                copy.wait()
        if line:
            line.end()

    vmem = pl.BlockSpec(memory_space=pltpu.VMEM)
    smem = pl.BlockSpec(memory_space=pltpu.SMEM)
    shapes = [jax.ShapeDtypeStruct(shape, dtype) for shape, dtype in outs]
    if gather:
        shapes.append(jax.ShapeDtypeStruct((parts, share, D), jnp.bfloat16))
    shapes += [jax.ShapeDtypeStruct(shape, dtype) for shape, dtype in work.outs]
    out_specs = [vmem] * len(shapes)
    operands = list(work.operands) + list(extras) + list(scalars)
    in_specs = list(work.specs) + [vmem] * len(extras) + [smem] * len(scalars)
    dma = pltpu.SemaphoreType.DMA
    buffers = [dma((2, parts - 1))] * 2
    if reduce:
        buffers += [pltpu.VMEM((parts * share, D), jnp.float32)]
        buffers += [pltpu.VMEM((parts - 1, share, D), jnp.bfloat16)] * 2
    if line:
        operands += line.operands
        in_specs += line.in_specs
        shapes.append(line.out_shape)
        out_specs.append(line.out_spec)
        buffers += line.scratch
    return pl.pallas_call(
        kernel,
        name=name,
        grid=(1,),
        out_shape=shapes,
        in_specs=in_specs,
        out_specs=out_specs,
        scratch_shapes=buffers + list(work.scratch),
        cost_estimate=SHORT,
        compiler_params=pltpu.CompilerParams(
            collective_id=collective_id, has_side_effects=True, vmem_limit_bytes=60 << 20
        ),
    )(*operands)


VMEM_SPEC = pl.BlockSpec(memory_space=pltpu.VMEM)


def part_spec(rows, index):
    return pl.BlockSpec((rows, D), lambda step: (index, 0), pipeline_mode=pl.Buffered(1))


def turn(block, cosine, sine):
    half = HEAD_DIM // 2
    first, second = block[:half], block[half:]
    return jnp.concatenate(
        [first * cosine - second * sine, second * cosine + first * sine], axis=0
    )


def times(left, right):
    return jnp.dot(left, right, preferred_element_type=jnp.float32)


def masks_of(count, side):
    key = lax.broadcasted_iota(jnp.int32, (count, count), 0)
    query = lax.broadcasted_iota(jnp.int32, (count, count), 1)
    far = jnp.where(side == 0, -1e30, 0.0).astype(jnp.float32)
    return far, jnp.where(key <= query, 0.0, -1e30)


def scores_of(keys_values, head, queries, masks):
    span = slice(head * HEAD_DIM, (head + 1) * HEAD_DIM)
    scale = HEAD_DIM ** (-0.5)
    far = contract_first(keys_values[0, 0, span, :], queries) * scale + masks[0]
    own = contract_first(keys_values[1, 0, span, :], queries) * scale + masks[1]
    return far, own


def attention_work(normed, table, cosine, sine):
    parts, share, _ = normed.shape
    count = parts * share
    width = D // parts
    heads = width // HEAD_DIM

    def before(ins, outs, scratch, partial_ref, tick):
        normed_ref, qkv_ref, out_ref, cosine_ref, sine_ref = ins
        queries_ref, both, logs_ref, attended_ref = outs
        send_sem, recv_sem = scratch
        side = lax.axis_index("seq")
        cosine, sine = cosine_ref[...], sine_ref[...]
        rows = normed_ref[...].reshape(count, D)
        joined = contract_last(qkv_ref[...], rows)
        for head in range(heads):
            span = slice(head * HEAD_DIM, (head + 1) * HEAD_DIM)
            keys = joined[width + head * HEAD_DIM : width + (head + 1) * HEAD_DIM]
            both[1, 0, span, :] = turn(keys, cosine, sine).astype(jnp.bfloat16)
        both[1, 1] = joined[2 * width :].astype(jnp.bfloat16)
        copy = pltpu.make_async_remote_copy(
            src_ref=both.at[1],
            dst_ref=both.at[0],
            send_sem=send_sem,
            recv_sem=recv_sem,
            device_id={"seq": 1 - side},
            device_id_type=MESH,
        )

        copy.start()
        for head in range(heads):
            span = slice(head * HEAD_DIM, (head + 1) * HEAD_DIM)
            queries_ref[span, :] = turn(joined[span], cosine, sine).astype(jnp.bfloat16)

        copy.wait()
        masks = masks_of(count, side)
        for head in range(heads):
            span = slice(head * HEAD_DIM, (head + 1) * HEAD_DIM)
            far, own = scores_of(both, head, queries_ref[span, :], masks)
            peak = jnp.maximum(
                jnp.max(far, axis=0, keepdims=True), jnp.max(own, axis=0, keepdims=True)
            )
            far, own = jnp.exp(far - peak), jnp.exp(own - peak)
            total = jnp.sum(far, axis=0, keepdims=True) + jnp.sum(own, axis=0, keepdims=True)
            logs_ref[head] = peak + jnp.log(total)
            inverse = 1.0 / total
            attended = times(both[0, 1, span, :], (far * inverse).astype(jnp.bfloat16))
            attended += times(both[1, 1, span, :], (own * inverse).astype(jnp.bfloat16))
            attended_ref[span, :] = attended.astype(jnp.bfloat16)
            tick(2)
        partial_ref[...] = contract_first(attended_ref[...], out_ref[...])

    low = jnp.bfloat16
    return Work(
        before,
        None,
        [normed, table, table, cosine, sine],
        [VMEM_SPEC, part_spec(3 * width, 0), part_spec(width, 3), VMEM_SPEC, VMEM_SPEC],
        [
            ((width, count), low),
            ((2, 2, width, count), low),
            ((heads, 1, count), jnp.float32),
            ((width, count), low),
        ],
        [pltpu.SemaphoreType.DMA, pltpu.SemaphoreType.DMA],
        twins=True,
    )


def fold_copy(own, near, send_sems, recv_sems, index):
    side = lax.axis_index("seq")
    return pltpu.make_async_remote_copy(
        src_ref=own.at[index, :, 1 - side],
        dst_ref=near.at[index],
        send_sem=send_sems.at[index],
        recv_sem=recv_sems.at[index],
        device_id={"seq": 1 - side},
        device_id_type=MESH,
    )


def add_halves(own, near, out, start):
    side = lax.axis_index("seq")

    def one(block, carry):
        value = own[block, side].astype(jnp.float32) + near[block].astype(jnp.float32)
        out[start + block] = value.astype(jnp.bfloat16)
        return carry

    lax.fori_loop(0, near.shape[0], one, 0)


def attention_back_work(grad, normed, table, kept, cosine, sine, half_rows):
    parts, share, _ = normed.shape
    count = parts * share
    width = D // parts
    heads = width // HEAD_DIM
    queries, both, logs, attended = kept
    blocks = 4 * width // (2 * half_rows)

    def before(ins, outs, scratch, partial_ref, tick):
        grad_ref, _, qkv_ref, out_ref, queries_ref, both, logs_ref, _, cosine_ref, sine_ref = ins
        back, came, grad_joined, send_sem, recv_sem = scratch[:5]
        side = lax.axis_index("seq")
        cosine, sine = cosine_ref[...], -sine_ref[...]
        scale = HEAD_DIM ** (-0.5)
        grads = contract_last(out_ref[...], grad_ref[...].reshape(count, D)).astype(jnp.bfloat16)
        own_grads = []
        masks = masks_of(count, side)
        for head in range(heads):
            span = slice(head * HEAD_DIM, (head + 1) * HEAD_DIM)
            head_queries, head_grads = queries_ref[span, :], grads[span]
            far, own = scores_of(both, head, head_queries, masks)
            far, own = jnp.exp(far - logs_ref[head]), jnp.exp(own - logs_ref[head])
            far_grad = contract_first(both[0, 1, span, :], head_grads)
            own_grad = contract_first(both[1, 1, span, :], head_grads)
            mean = jnp.sum(far * far_grad, axis=0, keepdims=True)
            mean += jnp.sum(own * own_grad, axis=0, keepdims=True)
            far_grad = (far * (far_grad - mean)).astype(jnp.bfloat16)
            own_grad = (own * (own_grad - mean)).astype(jnp.bfloat16)
            far, own = far.astype(jnp.bfloat16), own.astype(jnp.bfloat16)
            back[0, span, :] = (contract_last(head_queries, far_grad) * scale).astype(jnp.bfloat16)
            back[1, span, :] = contract_last(head_grads, far).astype(jnp.bfloat16)
            query_grad = times(both[0, 0, span, :], far_grad) + times(both[1, 0, span, :], own_grad)
            grad_joined[span, :] = turn(query_grad * scale, cosine, sine).astype(jnp.bfloat16)
            own_grads.append(
                (contract_last(head_queries, own_grad) * scale, contract_last(head_grads, own))
            )
            tick(2)
        copy = send(back, came, send_sem, recv_sem, {"seq": 1 - side})
        copy.wait()
        for head, (key_grad, value_grad) in enumerate(own_grads):
            span = slice(head * HEAD_DIM, (head + 1) * HEAD_DIM)
            key_grad = key_grad + came[0, span, :].astype(jnp.float32)
            value_grad = value_grad + came[1, span, :].astype(jnp.float32)
            start = width + head * HEAD_DIM
            grad_joined[start : start + HEAD_DIM, :] = turn(key_grad, cosine, sine).astype(
                jnp.bfloat16
            )
            start += width
            grad_joined[start : start + HEAD_DIM, :] = value_grad.astype(jnp.bfloat16)
        partial_ref[...] = contract_first(grad_joined[...], qkv_ref[...])

    def during(ins, outs, scratch):
        grad_ref, normed_ref, attended_ref = ins[0], ins[1], ins[7]
        grad_joined = scratch[2]
        own, near, fold_send, fold_recv = scratch[5:]
        value = times(grad_joined[...], normed_ref[...].reshape(count, D)).astype(jnp.bfloat16)
        part = 3 * blocks // 4
        own[0, :part] = value.reshape(part, 2, half_rows, D)
        value = times(attended_ref[...], grad_ref[...].reshape(count, D)).astype(jnp.bfloat16)
        own[0, part:] = value.reshape(blocks - part, 2, half_rows, D)
        fold_copy(own, near, fold_send, fold_recv, 0).start()

    def after(ins, outs, scratch):
        own, near, fold_send, fold_recv = scratch[5:]
        fold_copy(own, near, fold_send, fold_recv, 0).wait()
        add_halves(own.at[0], near.at[0], outs[0], 0)

    low = jnp.bfloat16
    dma = pltpu.SemaphoreType.DMA
    return Work(
        before,
        during,
        [grad, normed, table, table, queries, both, logs, attended, cosine, sine],
        [VMEM_SPEC, VMEM_SPEC, part_spec(3 * width, 0), part_spec(width, 3)] + [VMEM_SPEC] * 6,
        [((blocks, half_rows, D), low)],
        [
            pltpu.VMEM((2, width, count), low),
            pltpu.VMEM((2, width, count), low),
            pltpu.VMEM((3 * width, count), low),
            dma,
            dma,
            pltpu.VMEM((1, blocks, 2, half_rows, D), low),
            pltpu.VMEM((1, blocks, half_rows, D), low),
            dma((1,)),
            dma((1,)),
        ],
        after,
        True,
    )


def gelu(hidden):
    return jax.nn.gelu(hidden, approximate=True)


def unit_work(normed, up, down):
    parts, share, _ = normed.shape
    count = parts * share
    units = FF // parts

    def before(ins, outs, scratch, partial_ref, tick):
        normed_ref, up_ref, down_ref = ins
        hidden_ref, activated_ref = outs
        hidden = contract_last(up_ref[...], normed_ref[...].reshape(count, D))
        hidden_ref[...] = hidden
        activated_ref[...] = gelu(hidden).astype(jnp.bfloat16)
        tick(2)
        partial_ref[...] = contract_first(activated_ref[...], down_ref[...])

    return Work(
        before,
        None,
        [normed, up[0], down[0]],
        [VMEM_SPEC, part_spec(units, up[1]), part_spec(units, down[1])],
        [((units, count), jnp.float32), ((units, count), jnp.bfloat16)],
        [],
    )


def unit_back_work(grad, normed, up, down, kept, half_rows):
    parts, share, _ = normed.shape
    count = parts * share
    units = FF // parts
    hidden, activated = kept
    blocks = units // (2 * half_rows)

    def before(ins, outs, scratch, partial_ref, tick):
        grad_ref, _, up_ref, down_ref, hidden_ref, _ = ins
        grad_hidden = scratch[0]
        grad_act = contract_last(down_ref[...], grad_ref[...].reshape(count, D))
        _, pull = jax.vjp(gelu, hidden_ref[...])
        grad_hidden[...] = pull(grad_act)[0].astype(jnp.bfloat16)
        tick(2)
        partial_ref[...] = contract_first(grad_hidden[...], up_ref[...])

    def during(ins, outs, scratch):
        grad_ref, normed_ref, _, _, _, activated_ref = ins
        grad_hidden, own, near, fold_send, fold_recv = scratch
        value = times(grad_hidden[...], normed_ref[...].reshape(count, D))
        own[0] = value.astype(jnp.bfloat16).reshape(own.shape[1:])
        fold_copy(own, near, fold_send, fold_recv, 0).start()
        value = times(activated_ref[...], grad_ref[...].reshape(count, D))
        own[1] = value.astype(jnp.bfloat16).reshape(own.shape[1:])
        fold_copy(own, near, fold_send, fold_recv, 1).start()

    def after(ins, outs, scratch):
        _, own, near, fold_send, fold_recv = scratch
        for index in range(2):
            fold_copy(own, near, fold_send, fold_recv, index).wait()
            add_halves(own.at[index], near.at[index], outs[0], index * blocks)

    low, dma = jnp.bfloat16, pltpu.SemaphoreType.DMA
    return Work(
        before,
        during,
        [grad, normed, up[0], down[0], hidden, activated],
        [VMEM_SPEC, VMEM_SPEC, part_spec(units, up[1]), part_spec(units, down[1])]
        + [VMEM_SPEC] * 2,
        [((2 * blocks, half_rows, D), low)],
        [
            pltpu.VMEM((units, count), low),
            pltpu.VMEM((2, blocks, 2, half_rows, D), low),
            pltpu.VMEM((2, blocks, half_rows, D), low),
            dma((2,)),
            dma((2,)),
        ],
        after,
        True,
    )


LINE_BLOCKS = 1
LINE_LAG = 3
LINE_SHARE = 4


class Line:
    def __init__(self, sources, share):
        self.groups = lax.axis_size("dp")
        self.sources, self.share = sources, share
        count = sum(size for _, _, size in sources)
        _, half_rows, _ = sources[0][0].shape
        self.half = (count, half_rows, D)
        self.chunks = count // LINE_BLOCKS
        self.operands = [array for array, _, _ in sources]
        self.in_specs = [pl.BlockSpec(memory_space=pl.ANY)] * len(sources)
        dma = pltpu.SemaphoreType.DMA
        out = (count, 2, half_rows, D) if share else self.half
        self.out_shape = jax.ShapeDtypeStruct(out, jnp.bfloat16)
        self.out_spec = pl.BlockSpec(memory_space=pl.ANY if share else pltpu.VMEM)
        self.scratch = [
            pltpu.VMEM(self.half, jnp.bfloat16),
            pltpu.VMEM((2,) + self.half, jnp.bfloat16),
            pltpu.VMEM((2,) + self.half, jnp.bfloat16),
            dma((len(sources),)),
            dma((2,)),
            dma((2, self.chunks)),
        ]
        if share:
            self.scratch += [pltpu.VMEM(self.half, jnp.bfloat16)] + [dma] * 3

    def bind(self, source_refs, out_ref, refs):
        self.source_refs, self.out = source_refs, out_ref
        self.own, self.came, self.going, self.own_sems, self.send_sems, self.recv_sems = refs[:6]
        self.total = out_ref
        if self.share:
            self.total, self.keep_sem, self.twin_send, self.twin_recv = refs[6:]
        self.done = 0
        self.group = lax.axis_index("dp")
        self.first = jnp.where(self.group < self.groups // 2, 0, 1)

    def at(self, chunk):
        return pl.ds(chunk * LINE_BLOCKS, LINE_BLOCKS)

    def comes(self, way):
        return jnp.where(way == 0, self.group > 0, self.group < self.groups - 1)

    def goes(self, way):
        return jnp.where(way == 0, self.group < self.groups - 1, self.group > 0)

    def copy(self, source, way, chunk):
        target = jnp.where(way == 0, self.group + 1, self.group - 1)
        return pltpu.make_async_remote_copy(
            src_ref=source,
            dst_ref=self.came.at[way, self.at(chunk)],
            send_sem=self.send_sems.at[way],
            recv_sem=self.recv_sems.at[way, chunk],
            device_id={"dp": target},
            device_id_type=MESH,
        )

    def load(self):
        self.loads, place = [], 0
        for index, (ref, (_, start, size)) in enumerate(zip(self.source_refs, self.sources)):
            copy = pltpu.make_async_copy(
                ref.at[pl.ds(start, size)], self.own.at[pl.ds(place, size)], self.own_sems.at[index]
            )
            copy.start()
            self.loads.append(copy)
            place += size

    def begin(self):
        for copy in self.loads:
            copy.wait()
        for way in range(2):

            @pl.when(jnp.logical_not(self.comes(way)))
            def _():
                self.came[way] = jnp.zeros(self.half, jnp.bfloat16)

                def start(chunk, carry):
                    self.copy(self.own.at[self.at(chunk)], way, chunk).start()
                    return carry

                lax.fori_loop(0, self.chunks, start, 0)

    def twin_copy(self, rows):
        side = lax.axis_index("seq")
        return pltpu.make_async_remote_copy(
            src_ref=self.total.at[rows],
            dst_ref=self.out.at[rows, side],
            send_sem=self.twin_send,
            recv_sem=self.twin_recv,
            device_id={"seq": 1 - side},
            device_id_type=MESH,
        )

    def keep_copy(self, rows):
        return pltpu.make_async_copy(
            self.total.at[rows], self.out.at[rows, lax.axis_index("seq")], self.keep_sem
        )

    def pass_on(self, way, chunk):
        rows = self.at(chunk)

        @pl.when(self.comes(way))
        def _():
            copy = self.copy(self.going.at[way, rows], way, chunk)
            copy.wait_recv()

            @pl.when(self.goes(way))
            def _():
                value = self.own[rows].astype(jnp.float32) + self.came[way, rows].astype(jnp.float32)
                self.going[way, rows] = value.astype(jnp.bfloat16)
                copy.start()

    def step(self, index):
        @pl.when(index < self.chunks)
        def _():
            self.pass_on(self.first, index)

        @pl.when(index >= LINE_LAG)
        def _():
            chunk = index - LINE_LAG
            rows = self.at(chunk)
            self.pass_on(1 - self.first, chunk)
            value = self.own[rows].astype(jnp.float32)
            value = value + self.came[0, rows].astype(jnp.float32)
            value = value + self.came[1, rows].astype(jnp.float32)
            self.total[rows] = value.astype(jnp.bfloat16)
            if self.share:

                @pl.when(lax.rem(chunk, LINE_SHARE) == LINE_SHARE - 1)
                def _():
                    done = pl.ds(chunk - (LINE_SHARE - 1), LINE_SHARE)
                    self.keep_copy(done).start()
                    self.twin_copy(done).start()

    def steps(self, count=None):
        last = self.chunks + LINE_LAG
        stop = last if count is None else min(self.done + count, last)

        def one(index, carry):
            self.step(index)
            return carry

        lax.fori_loop(self.done, stop, one, 0)
        self.done = stop

    def end(self):
        for way in range(2):

            @pl.when(self.goes(way))
            def _():
                whole_copy = pltpu.make_async_remote_copy(
                    src_ref=self.going.at[way],
                    dst_ref=self.came.at[way],
                    send_sem=self.send_sems.at[way],
                    recv_sem=self.recv_sems.at[way, 0],
                    device_id={"dp": self.group},
                    device_id_type=MESH,
                )
                whole_copy.wait_send()

        if self.share:
            everything = pl.ds(0, self.half[0])
            self.keep_copy(everything).wait()
            self.twin_copy(everything).wait()


def reduce_all(terms, collective_id, line=None, tail=None):
    _, tensors, groups, count, _ = terms.shape
    half = count // 2
    function, extras, scalars, outs = tail or (None, [], [], [])
    extra_specs = [VMEM_SPEC] * len(extras)
    extra_specs += [pl.BlockSpec(memory_space=pltpu.SMEM)] * len(scalars)
    extras = list(extras) + list(scalars)

    def kernel(*refs):
        refs = list(refs)
        terms_ref = refs.pop(0)
        source_refs = [refs.pop(0) for _ in line.operands] if line else []
        extra_refs = [refs.pop(0) for _ in extras]
        out_refs = [refs.pop(0) for _ in range(len(outs) or 1)]
        full = refs.pop(0) if tail else None
        joined_ref = refs.pop(0) if line else None
        tail_sems = [refs.pop(0) for _ in range(2)] if tail else None
        (
            near, own, mid, sums, mid_in, far, far_in,
            own_sems, near_send, near_recv, mid_send, mid_recv, far_send, far_recv,
        ) = refs[:14]
        if line:
            line.bind(source_refs, joined_ref, refs[14:])
            line.load()
        group, part, side = lax.axis_index("dp"), lax.axis_index("tensor"), lax.axis_index("seq")
        twin = 1 - side
        parts = others("tensor")
        order = others("dp") + [group]
        meet(
            [{"seq": twin}]
            + [{"tensor": peer} for peer in parts]
            + [{"dp": peer} for peer in order[:-1]]
        )
        waits, near_copies, own_copies = [], [], []
        for place, target in enumerate(order):
            near_copies.append(
                send(
                    terms_ref.at[twin, :, target],
                    near.at[place],
                    near_send.at[place],
                    near_recv.at[place],
                    {"seq": twin},
                )
            )
            copy = pltpu.make_async_copy(
                terms_ref.at[side, :, target], own.at[place], own_sems.at[place]
            )
            copy.start()
            own_copies.append(copy)
        if line:
            line.begin()
        beside = lax.rem(part + 1, 2) + part - lax.rem(part, 2)
        across = lax.rem(part + 2, 4)
        corner = 3 - part
        upper, lower = pl.ds(0, half), pl.ds(half, half)
        first_copies, second_copies = [], []

        def hand(place, index, source, target):
            return send(
                source,
                mid_in.at[place, index],
                mid_send.at[place, index],
                mid_recv.at[place, index],
                {"tensor": target},
            )

        for place in range(groups):
            near_copies[place].wait_recv()
            own_copies[place].wait()
            for slot in range(tensors):
                mid[place, slot] = (
                    own[place, slot].astype(jnp.float32) + near[place, slot].astype(jnp.float32)
                ).astype(jnp.bfloat16)
            first_copies.append(
                [
                    hand(place, 0, mid.at[place, corner, upper], beside),
                    hand(place, 1, mid.at[place, corner, lower], across),
                    hand(place, 2, mid.at[place, beside, upper], beside),
                    hand(place, 3, mid.at[place, across, lower], across),
                ]
            )
        for place in range(groups):
            if line and place < 4:
                line.steps(3)
            copies = []
            for index, slot, rows, target in ((0, across, upper, across), (1, beside, lower, beside)):
                first_copies[place][index].wait_recv()
                value = mid[place, slot, rows].astype(jnp.float32)
                value = value + mid_in[place, index].astype(jnp.float32)
                sums[place, index] = value.astype(jnp.bfloat16)
                copies.append(hand(place, 4 + index, sums.at[place, index], target))
            second_copies.append(copies)
        far_copies = []
        for place, target in enumerate(order):
            copies = first_copies[place][2:] + second_copies[place]
            for copy in copies:
                copy.wait_recv()

            def joined(index):
                return mid_in[place, index].astype(jnp.float32)

            halves = [joined(2) + joined(4), joined(3) + joined(5)]
            total = mid[place, part].astype(jnp.float32) + jnp.concatenate(halves, axis=0)
            if place < groups - 1:
                far[place] = total.astype(jnp.bfloat16)
                far_copies.append(
                    send(
                        far.at[place],
                        far_in.at[place],
                        far_send.at[place],
                        far_recv.at[place],
                        {"dp": target},
                    )
                )
        if line:
            line.steps()
        for place, copy in enumerate(far_copies):
            copy.wait_recv()
            total = total + far_in[place].astype(jnp.float32)
        if tail:
            results = function(total, *extra_refs)
            for ref, value in zip(out_refs, results):
                ref[...] = value
            full[part] = results[len(outs)].astype(jnp.bfloat16)
            last_copies = [
                send(
                    full.at[part],
                    full.at[part],
                    tail_sems[0].at[step],
                    tail_sems[1].at[step],
                    {"tensor": peer},
                )
                for step, peer in enumerate(parts)
            ]
            for copy in last_copies:
                copy.wait()
        else:
            out_refs[0][...] = total
        for copy in near_copies + far_copies + [
            copy for row in first_copies + second_copies for copy in row
        ]:
            copy.wait_send()
        if line:
            line.end()

    block = (count, D)
    dma = pltpu.SemaphoreType.DMA
    results = [jax.ShapeDtypeStruct(*out) for out in outs]
    if tail:
        results.append(jax.ShapeDtypeStruct((tensors,) + block, jnp.bfloat16))
    else:
        results.append(jax.ShapeDtypeStruct(block, jnp.float32))
    return pl.pallas_call(
        kernel,
        name="reduce_all",
        out_shape=results + ([line.out_shape] if line else []),
        in_specs=[pl.BlockSpec(memory_space=pl.ANY)] + (line.in_specs if line else []) + extra_specs,
        out_specs=[VMEM_SPEC] * len(results) + ([line.out_spec] if line else []),
        scratch_shapes=[dma((tensors - 1,))] * (2 if tail else 0)
        + [pltpu.VMEM((groups, tensors) + block, jnp.bfloat16)] * 3
        + [
            pltpu.VMEM((groups, 2, half, D), jnp.bfloat16),
            pltpu.VMEM((groups, 6, half, D), jnp.bfloat16),
            pltpu.VMEM((groups,) + block, jnp.bfloat16),
            pltpu.VMEM((groups,) + block, jnp.bfloat16),
            dma((groups,)),
            dma((groups,)),
            dma((groups,)),
            dma((groups, 6)),
            dma((groups, 6)),
            dma((groups,)),
            dma((groups,)),
        ]
        + (line.scratch if line else []),
        cost_estimate=SHORT,
        compiler_params=pltpu.CompilerParams(
            collective_id=collective_id, has_side_effects=True, vmem_limit_bytes=56 << 20
        ),
    )(terms, *(line.operands if line else []), *extras)


def gather_all(block, collective_id, line=None):
    tensors, groups = lax.axis_size("tensor"), lax.axis_size("dp")
    half = block.shape[0] // 2

    def kernel(*refs):
        refs = list(refs)
        block_ref = refs.pop(0)
        source_refs = [refs.pop(0) for _ in line.operands] if line else []
        out = refs.pop(0)
        summed_ref = refs.pop(0) if line else None
        own_sem, far_send, far_recv, mid_send, mid_recv, near_send, near_recv = refs[:7]
        if line:
            line.bind(source_refs, summed_ref, refs[7:])
            line.load()
        group, part, side = lax.axis_index("dp"), lax.axis_index("tensor"), lax.axis_index("seq")
        twin = 1 - side
        meet(
            [{"seq": twin}]
            + [{"tensor": peer} for peer in others("tensor")]
            + [{"dp": peer} for peer in others("dp")]
        )
        far_copies = [
            send(
                block_ref,
                out.at[side, part, group],
                far_send.at[step],
                far_recv.at[step],
                {"dp": peer},
            )
            for step, peer in enumerate(others("dp"))
        ]
        own = pltpu.make_async_copy(block_ref, out.at[side, part, group], own_sem)
        own.start()
        if line:
            line.begin()
        beside = lax.rem(part + 1, 2) + part - lax.rem(part, 2)
        across = lax.rem(part + 2, 4)
        corner = 3 - part
        upper, lower = pl.ds(0, half), pl.ds(half, half)
        first_copies, second_copies, near_copies = [], [], []
        for place in range(groups):
            source = behind("dp", place)
            if place:
                far_copies[place - 1].wait_recv()
            held = out.at[side, part, source] if place else block_ref

            def hand(index, piece, slot, rows, target):
                return send(
                    piece,
                    out.at[side, slot, source, rows],
                    mid_send.at[place, index],
                    mid_recv.at[place, index],
                    {"tensor": target},
                )

            first = [
                hand(0, held.at[upper], part, upper, beside),
                hand(1, held.at[lower], part, lower, across),
                hand(2, held.at[lower], part, lower, beside),
                hand(3, held.at[upper], part, upper, across),
            ]
            near_copies.append(
                send(
                    held,
                    out.at[side, part, source],
                    near_send.at[place, 0],
                    near_recv.at[place, 0],
                    {"seq": twin},
                )
            )
            first[0].wait_recv()
            second = [hand(4, out.at[side, beside, source, upper], beside, upper, across)]
            first[1].wait_recv()
            second.append(hand(5, out.at[side, across, source, lower], across, lower, beside))
            first_copies.append(first)
            second_copies.append(second)
        for place in range(groups):
            if line and place < 4:
                line.steps(2)
            source = behind("dp", place)
            ready = [
                (beside, first_copies[place][2:3]),
                (across, first_copies[place][3:4]),
                (corner, second_copies[place]),
            ]
            for step, (slot, copies) in enumerate(ready):
                for copy in copies:
                    copy.wait_recv()
                held = out.at[side, slot, source]
                near_copies.append(
                    send(
                        held,
                        held,
                        near_send.at[place, step + 1],
                        near_recv.at[place, step + 1],
                        {"seq": twin},
                    )
                )
        if line:
            line.steps()
        for copy in near_copies:
            copy.wait_recv()
        for copy in near_copies + far_copies + [
            copy for row in first_copies + second_copies for copy in row
        ]:
            copy.wait_send()
        own.wait()
        if line:
            line.end()

    dma = pltpu.SemaphoreType.DMA
    anywhere = pl.BlockSpec(memory_space=pl.ANY)
    return pl.pallas_call(
        kernel,
        name="gather_all",
        out_shape=[jax.ShapeDtypeStruct((2, tensors, groups) + block.shape, block.dtype)]
        + ([line.out_shape] if line else []),
        in_specs=[VMEM_SPEC] + (line.in_specs if line else []),
        out_specs=[pl.BlockSpec(memory_space=pltpu.HBM)] + ([line.out_spec] if line else []),
        scratch_shapes=[
            dma,
            dma((groups - 1,)),
            dma((groups - 1,)),
            dma((groups, 6)),
            dma((groups, 6)),
            dma((groups, tensors)),
            dma((groups, tensors)),
        ]
        + (line.scratch if line else []),
        cost_estimate=SHORT,
        compiler_params=pltpu.CompilerParams(
            collective_id=collective_id, has_side_effects=True, vmem_limit_bytes=60 << 20
        ),
    )(block, *(line.operands if line else []))


def reduce_rows(name, terms, ids, line, function, extras, scalars, outs):
    count, groups = terms.shape[3], terms.shape[2]
    pieces = max(1, groups // 4)
    if pieces == 1:
        return reduce_all(terms, ids[0], line, (function, extras, scalars, outs))
    part = count // pieces
    sums, joined = [], []
    for i in range(pieces):
        piece = terms[:, :, :, i * part : (i + 1) * part]
        total, *joined_now = reduce_all(piece, ids[1 if i and line else 0], None if i else line)
        sums.append(total)
        joined += joined_now
    total = jnp.concatenate(sums, axis=0)
    results = tensor_step(
        name,
        lambda _, total_ref, *refs: function(total_ref, *refs),
        None,
        [total] + list(extras),
        scalars,
        outs,
        True,
        ids[2],
    )
    return list(results) + joined


def plane_steps(tensors):
    return [(step, turn_by) for step in range(tensors) for turn_by in range(2)][1:]


def plane_peers(steps):
    count, part = lax.axis_size("tensor"), lax.axis_index("tensor")
    side = lax.axis_index("seq")
    return [
        (lax.rem(part + step, count), lax.rem(side + turn_by, 2)) for step, turn_by in steps
    ]


def join_stats(stats, collective_id):
    _, tensors, groups, _, _ = stats.shape

    def join(left, right):
        top = jnp.maximum(left[..., 0:1, :], right[..., 0:1, :])
        total = left[..., 1:2, :] * jnp.exp(left[..., 0:1, :] - top) + right[..., 1:2, :] * jnp.exp(
            right[..., 0:1, :] - top
        )
        return jnp.concatenate(
            [top, total, left[..., 2:3, :] + right[..., 2:3, :], left[..., 3:, :]], axis=-2
        )

    plane = plane_steps(tensors)

    def kernel(
        stats_ref, home, full, mid_in, far, far_in, mid_send, mid_recv, far_send, far_recv
    ):
        group, part, side = lax.axis_index("dp"), lax.axis_index("tensor"), lax.axis_index("seq")
        peers, groups_else = plane_peers(plane), others("dp")
        meet(
            [{"tensor": peer, "seq": other} for peer, other in peers]
            + [{"dp": peer} for peer in groups_else]
        )
        copies = [
            send(
                stats_ref.at[other, peer],
                mid_in.at[step],
                mid_send.at[0, step],
                mid_recv.at[0, step],
                {"tensor": peer, "seq": other},
            )
            for step, (peer, other) in enumerate(peers)
        ]
        for copy in copies:
            copy.wait()
        for spot in range(groups):
            total = stats_ref[side, part, spot]
            for step in range(len(plane)):
                total = join(total, mid_in[step, spot])
            far[spot] = total
        copies = [
            send(far.at[peer], far_in.at[step], far_send.at[0, step], far_recv.at[0, step], {"dp": peer})
            for step, peer in enumerate(groups_else)
        ]
        total = far[group]
        for step, copy in enumerate(copies):
            copy.wait()
            total = join(total, far_in[step])
        log_total = total[0:1] + jnp.log(total[1:2])
        home[...] = jnp.concatenate([log_total, total[2:3], total[2:]], axis=0)
        full[side, part, group] = jnp.broadcast_to(log_total, (8, LANES))
        held = full.at[side, part, group]
        copies = [
            send(held, held, far_send.at[1, step], far_recv.at[1, step], {"dp": peer})
            for step, peer in enumerate(groups_else)
        ]
        for copy in copies:
            copy.wait()
        held = full.at[side, part]
        copies = [
            send(
                held,
                held,
                mid_send.at[1, step],
                mid_recv.at[1, step],
                {"tensor": peer, "seq": other},
            )
            for step, (peer, other) in enumerate(peers)
        ]
        for copy in copies:
            copy.wait()

    tile = (8, LANES)
    dma = pltpu.SemaphoreType.DMA
    vmem = pl.BlockSpec(memory_space=pltpu.VMEM)
    return pl.pallas_call(
        kernel,
        name="join_stats",
        out_shape=[
            jax.ShapeDtypeStruct(tile, jnp.float32),
            jax.ShapeDtypeStruct(stats.shape, jnp.float32),
        ],
        in_specs=[vmem],
        out_specs=[vmem, vmem],
        scratch_shapes=[
            pltpu.VMEM((len(plane), groups) + tile, jnp.float32),
            pltpu.VMEM((groups,) + tile, jnp.float32),
            pltpu.VMEM((groups - 1,) + tile, jnp.float32),
            dma((2, len(plane))),
            dma((2, len(plane))),
            dma((2, groups - 1)),
            dma((2, groups - 1)),
        ],
        cost_estimate=SHORT,
        compiler_params=pltpu.CompilerParams(collective_id=collective_id, has_side_effects=True),
    )(stats)


def spread_tokens(block, slot_block, ends, blocks, half_rows, collective_id):
    tensors, groups = lax.axis_size("tensor"), lax.axis_size("dp")
    rows = 2 * tensors * groups
    width = ends.shape[1]
    vocab_rows = VOCAB // tensors
    slots = slot_block.shape[0]

    def kernel(
        block_ref, slot_ref, ends_ref, ids, targets, kept, places, plan, count,
        held, firsts, own_sem, send_sems, recv_sems,
    ):
        group, side = lax.axis_index("dp"), lax.axis_index("seq")
        first_id = lax.axis_index("tensor") * vocab_rows
        peers = [
            {"dp": lax.rem(group + step // 2, groups), "seq": lax.rem(side + step % 2, 2)}
            for step in range(1, 2 * groups)
        ]
        meet(peers)
        copies = [
            send(block_ref, held.at[group, side], send_sems.at[step], recv_sems.at[step], peer)
            for step, peer in enumerate(peers)
        ]
        own = pltpu.make_async_copy(block_ref, held.at[group, side], own_sem)
        own.start()
        own.wait()
        for copy in copies:
            copy.wait()
        lane = lax.broadcasted_iota(jnp.int32, (1, LANES), 1)
        slot_ids = lax.broadcasted_iota(jnp.int32, (slots, LANES), 0)
        slot_blocks = jnp.broadcast_to(slot_ref[...], (slots, LANES))
        total = jnp.zeros((1, LANES), jnp.int32)
        hits = jnp.zeros((1, LANES), jnp.float32)
        for half in range(2):
            for source in range(groups):
                limit = held[source, half, 2 * tensors : 2 * tensors + 1, :]
                total = total + limit
                for part in range(tensors):
                    row = (half * tensors + part) * groups + source
                    token = held[source, half, part : part + 1, :]
                    ids[row] = token
                    targets[row] = held[source, half, tensors + part : tensors + part + 1, :]
                    kept[row] = jnp.where(lane + part * LANES < limit, 1.0, 0.0)
                    firsts[row : row + 1, :] = jnp.where(part * LANES < limit, 1.0, 0.0)
                    local = token - first_id
                    inside = (local >= 0) & (local < vocab_rows)
                    local = jnp.where(inside, local, 0).astype(jnp.float32)
                    block_of = jnp.floor((local + 0.5) * (0.5 / half_rows))
                    within = local - block_of * (2.0 * half_rows)
                    lower = within >= half_rows
                    inside = inside & (jnp.where(lower, 1, 0) == side)
                    within = (within - jnp.where(lower, 1.0 * half_rows, 0.0)).astype(jnp.int32)
                    same = slot_blocks == block_of.astype(jnp.int32) + blocks
                    slot = jnp.sum(jnp.where(same, slot_ids + 1, 0), axis=0, keepdims=True) - 1
                    inside = inside & (slot >= 0)
                    places[row] = jnp.where(inside, slot * half_rows + within, -1)
                    hits = hits + jnp.where(inside, 1.0, 0.0)
        count[...] = total.astype(jnp.float32)
        shape = (rows, width)
        active = jnp.concatenate([firsts[...]] * (width // LANES), axis=1)
        square = (rows, rows)
        above = jnp.where(
            lax.broadcasted_iota(jnp.int32, square, 1) < lax.broadcasted_iota(jnp.int32, square, 0),
            1.0,
            0.0,
        )
        earlier = times(above.astype(jnp.bfloat16), active.astype(jnp.bfloat16))
        number = jnp.sum(active, axis=0, keepdims=True)
        index = lax.broadcasted_iota(jnp.int32, shape, 0).astype(jnp.float32)
        turns = jnp.where(active > 0.0, earlier, number + index - earlier)
        spot = lax.broadcasted_iota(jnp.int32, shape, 1).astype(jnp.float32) - PLAN_GROUPS
        order = jnp.sum(jnp.where(turns == spot, index, 0.0), axis=0, keepdims=True)
        spot = lax.broadcasted_iota(jnp.int32, (1, width), 1)
        order = jnp.where(spot == 2, number, order)
        order = jnp.where(spot == 3, jnp.sum(hits, axis=1, keepdims=True), order)
        plan[...] = jnp.where(spot < 2, ends_ref[...], order.astype(jnp.int32))

    dma = pltpu.SemaphoreType.DMA
    vmem = pl.BlockSpec(memory_space=pltpu.VMEM)
    shape = (rows, 1, LANES)
    return pl.pallas_call(
        kernel,
        name="spread_tokens",
        out_shape=[
            jax.ShapeDtypeStruct(shape, jnp.int32),
            jax.ShapeDtypeStruct(shape, jnp.int32),
            jax.ShapeDtypeStruct(shape, jnp.float32),
            jax.ShapeDtypeStruct(shape, jnp.int32),
            jax.ShapeDtypeStruct((1, width), jnp.int32),
            jax.ShapeDtypeStruct((1, LANES), jnp.float32),
        ],
        in_specs=[vmem] * 3,
        out_specs=[vmem] * 6,
        scratch_shapes=[
            pltpu.VMEM((groups, 2) + block.shape, jnp.int32),
            pltpu.VMEM((rows, LANES), jnp.float32),
            dma,
            dma((2 * groups - 1,)),
            dma((2 * groups - 1,)),
        ],
        cost_estimate=SHORT,
        compiler_params=pltpu.CompilerParams(collective_id=collective_id, has_side_effects=True),
    )(block, slot_block, ends)


def finish(gain_grads, states, grad_ys, home, keep, table_squares, count, smalls, collective_id):
    tensors, groups = lax.axis_size("tensor"), lax.axis_size("dp")
    block = (8, D)
    plane = plane_steps(tensors)
    gain_rows = 2 * LAYERS + 1
    operands = list(gain_grads) + list(states) + list(grad_ys) + [
        home, keep, table_squares, count
    ] + list(smalls)

    def kernel(*refs):
        refs = list(refs)
        gain_refs = [refs.pop(0) for _ in gain_grads]
        state_refs = [refs.pop(0) for _ in states]
        grad_refs = [refs.pop(0) for _ in grad_ys]
        home_ref, keep_ref, table_ref, count_ref = [refs.pop(0) for _ in range(4)]
        small_refs = [refs.pop(0) for _ in smalls]
        out_refs = [refs.pop(0) for _ in range(8)]
        mid, far, mid_send, mid_recv, far_send, far_recv = refs
        group, part, side = lax.axis_index("dp"), lax.axis_index("tensor"), lax.axis_index("seq")
        peers, groups_else = plane_peers(plane), others("dp")
        meet(
            [{"tensor": peer, "seq": other} for peer, other in peers]
            + [{"dp": peer} for peer in groups_else]
        )
        values = []
        for later in range(1, LAYERS + 1):
            grad = grad_refs[later - 1][...]
            for level in range(later + 1):
                values.append(jnp.sum(grad * state_refs[level][...], keepdims=True))
        loss = jnp.where(keep_ref[...] > 0.0, home_ref[0:1, :] - home_ref[1:2, :], 0.0)
        values.append(jnp.sum(loss, keepdims=True))
        values.append(jnp.sum(table_ref[...], keepdims=True))
        lane = lax.broadcasted_iota(jnp.int32, (1, D), 1)
        row = jnp.zeros((1, D), jnp.float32)
        for place, value in enumerate(values):
            row = jnp.where(lane == place, value, row)
        blank = jnp.zeros((8 - gain_rows - 1, D), jnp.float32)
        total = jnp.concatenate([ref[...] for ref in gain_refs] + [row, blank], axis=0)
        stages = [
            (
                mid,
                2 * part + side,
                [{"tensor": peer, "seq": other} for peer, other in peers],
                mid_send,
                mid_recv,
            ),
            (far, group, [{"dp": peer} for peer in groups_else], far_send, far_recv),
        ]
        for slots, me, targets, send_sems, recv_sems in stages:
            slots[me] = total
            copies = [
                send(slots.at[me], slots.at[me], send_sems.at[step], recv_sems.at[step], target)
                for step, target in enumerate(targets)
            ]
            for copy in copies:
                copy.wait()
            total = slots[0]
            for index in range(1, slots.shape[0]):
                total = total + slots[index]
        gain_total = total[:gain_rows]
        row = total[gain_rows : gain_rows + 1]

        def pick(place):
            return jnp.sum(jnp.where(lane == place, row, 0.0), axis=1, keepdims=True)

        mix_squares = jnp.sum(jnp.where(lane < MIX_WEIGHTS, row * row, 0.0), axis=1, keepdims=True)
        gain_squares = jnp.sum(gain_total * gain_total, keepdims=True)
        tokens = count_ref[:, 0:1]
        clip_norm = jnp.sqrt(pick(MIX_WEIGHTS + 1) + gain_squares + mix_squares) / tokens
        factor = jnp.minimum(1.0, CLIP_NORM / clip_norm) / tokens
        gain_news = adam_update(
            *[ref[...] for ref in small_refs[:3]], gain_total * factor, RATE_SMALL, 0.0
        )
        mix_news = adam_update(
            *[ref[...] for ref in small_refs[3:]], row[:, :MIX_WEIGHTS] * factor, RATE_SMALL, 0.0
        )
        for ref, value in zip(out_refs[:6], gain_news + mix_news):
            ref[...] = value
        ends = jnp.where(lane == 0, pick(MIX_WEIGHTS), jnp.where(lane == 1, clip_norm, factor))
        out_refs[6][...] = ends[:, :LANES]
        out_refs[7][...] = jnp.broadcast_to(factor, (8, LANES))

    dma = pltpu.SemaphoreType.DMA
    vmem = pl.BlockSpec(memory_space=pltpu.VMEM)
    return pl.pallas_call(
        kernel,
        name="finish",
        out_shape=[jax.ShapeDtypeStruct(value.shape, jnp.float32) for value in smalls]
        + [
            jax.ShapeDtypeStruct((1, LANES), jnp.float32),
            jax.ShapeDtypeStruct((8, LANES), jnp.float32),
        ],
        in_specs=[vmem] * len(operands),
        out_specs=[vmem] * 8,
        scratch_shapes=[
            pltpu.VMEM((2 * tensors,) + block, jnp.float32),
            pltpu.VMEM((groups,) + block, jnp.float32),
            dma((len(plane),)),
            dma((len(plane),)),
            dma((groups - 1,)),
            dma((groups - 1,)),
        ],
        cost_estimate=SHORT,
        compiler_params=pltpu.CompilerParams(collective_id=collective_id, has_side_effects=True),
    )(*operands)


SLOT_STEP = 8
PREPARE_STEP = 20


def prepare(slot_block, first_id, master, blocks):
    slots, half_rows, _ = master.shape
    total = slot_block.shape[0]
    steps = -(-total // PREPARE_STEP)
    spare = steps * PREPARE_STEP - total
    slot_block = jnp.pad(slot_block, (0, spare), constant_values=-1)
    slot_block = jnp.concatenate([slot_block, first_id[None]])
    rows = PREPARE_STEP * half_rows

    def kernel(plan_ref, master_ref, table_ref, halves_ref, ids_ref):
        @pl.when(pl.program_id(0) == 0)
        def _():
            halves_ref[...] = jnp.zeros_like(halves_ref)

        for place in range(PREPARE_STEP):
            slot = pl.program_id(0) * PREPARE_STEP + place
            value = jnp.where(slot < slots, master_ref[place], 0.0).astype(jnp.bfloat16)
            table_ref[place * half_rows : (place + 1) * half_rows, :] = value

            block = plan_ref[slot]
            ids = plan_ref[steps * PREPARE_STEP] + (block - blocks) * (2 * half_rows)
            ids = ids + lax.broadcasted_iota(jnp.int32, (half_rows, 1), 0)
            ids_ref[place * half_rows : (place + 1) * half_rows, :] = jnp.where(
                block >= blocks, ids, -1
            )

            @pl.when((block >= 0) & (block < blocks))
            def _():
                halves_ref[block] = value

    last = (slots - 1) // PREPARE_STEP
    return pl.pallas_call(
        kernel,
        name="prepare",
        grid_spec=pltpu.PrefetchScalarGridSpec(
            num_scalar_prefetch=1,
            grid=(steps,),
            in_specs=[
                pl.BlockSpec(
                    (PREPARE_STEP, half_rows, D), lambda step, plan: (jnp.minimum(step, last), 0, 0)
                )
            ],
            out_specs=[
                pl.BlockSpec((rows, D), lambda step, plan: (step, 0)),
                pl.BlockSpec((blocks, half_rows, D), lambda step, plan: (0, 0, 0)),
                pl.BlockSpec((rows, 1), lambda step, plan: (step, 0)),
            ],
        ),
        out_shape=[
            jax.ShapeDtypeStruct((total * half_rows, D), jnp.bfloat16),
            jax.ShapeDtypeStruct((blocks, half_rows, D), jnp.bfloat16),
            jax.ShapeDtypeStruct((total * half_rows, 1), jnp.int32),
        ],
        cost_estimate=SHORT,
        compiler_params=pltpu.CompilerParams(vmem_limit_bytes=60 << 20),
    )(slot_block, master)


TILE = TILE_GROUPS * LANES
PICKED = 768


def row_of(values_ref, groups, place=0):
    rows = [values_ref[group, place : place + 1, :] for group in groups]
    return jnp.concatenate(rows, axis=1)


def tile_row(values_ref, tile):
    start = tile * TILE_GROUPS
    return row_of(values_ref, [start + place for place in range(TILE_GROUPS)])


PLAN_GROUPS = 4


def chunk_of(plan_ref, step):
    return pl.ds(pl.multiple_of(plan_ref[0] + step * ROW_STEP, 16), ROW_STEP)


def chunks_of(plan_ref):
    return (plan_ref[1] - plan_ref[0] + ROW_STEP - 1) // ROW_STEP


def whole(shape):
    return pl.BlockSpec(shape, lambda step, plan: (0,) * len(shape), pipeline_mode=pl.Buffered(1))


def last_tile(plan):
    return (plan[2] - 1) // TILE_GROUPS


def group_specs():
    return [
        pl.BlockSpec(
            (LANES, D),
            lambda step, plan, place=place: (
                plan[PLAN_GROUPS + jnp.minimum(step, last_tile(plan)) * TILE_GROUPS + place],
                0,
            ),
        )
        for place in range(TILE_GROUPS)
    ]


def powers_spec(rows):
    return pl.BlockSpec((rows, TILE), lambda step, plan: (0, jnp.minimum(step, last_tile(plan))))


def groups_of(plan_ref):
    start = PLAN_GROUPS + pl.program_id(0) * TILE_GROUPS
    return [plan_ref[start + place] for place in range(TILE_GROUPS)]


ROWS_SPEC = pl.BlockSpec((TILE, D), lambda step, plan: (step, 0))


def local_call(name, kernel, steps, plan, operands, in_specs, out_shape, out_specs, scratch):
    return pl.pallas_call(
        kernel,
        name=name,
        grid_spec=pltpu.PrefetchScalarGridSpec(
            num_scalar_prefetch=1,
            grid=(steps,),
            in_specs=in_specs,
            out_specs=out_specs,
            scratch_shapes=scratch,
        ),
        out_shape=out_shape,
        cost_estimate=SHORT,
        compiler_params=pltpu.CompilerParams(vmem_limit_bytes=60 << 20),
    )(plan, *operands)


def ones_where(condition):
    return jnp.where(condition, 1.0, 0.0).astype(jnp.bfloat16)


def picks(rank_row):
    return ones_where(lax.broadcasted_iota(jnp.int32, (PICKED, TILE), 0) == rank_row)


def rows_picked(plan_ref, step, place_row):
    start = plan_ref[0] + step * ROW_STEP
    row = lax.broadcasted_iota(jnp.int32, (ROW_STEP, PICKED), 0) + start
    return ones_where(row == place_row)


def look_up(plan, row_ids, tokens, places, table):
    rows, groups = table.shape[0], tokens.shape[0]
    steps = groups // TILE_GROUPS

    def kernel(
        plan_ref, ids_ref, tokens_ref, places_ref, table_ref, out_ref, ranks_ref, picked_ref, acc, picked
    ):
        tile = pl.program_id(0)
        few = plan_ref[3] <= PICKED

        @pl.when(tile == 0)
        def _():
            held = places_ref[...].reshape(groups, LANES) >= 0
            ones = ones_where(held)
            lane = (LANES, LANES)
            before = ones_where(
                lax.broadcasted_iota(jnp.int32, lane, 0) < lax.broadcasted_iota(jnp.int32, lane, 1)
            )
            group = (groups, groups)
            above = ones_where(
                lax.broadcasted_iota(jnp.int32, group, 1) < lax.broadcasted_iota(jnp.int32, group, 0)
            )
            totals = jnp.sum(ones.astype(jnp.float32), axis=1, keepdims=True)
            totals = jnp.broadcast_to(totals, (groups, LANES)).astype(jnp.bfloat16)
            ranks = (times(ones, before) + times(above, totals)).astype(jnp.int32)
            ranks_ref[...] = jnp.where(held, ranks, -1).reshape(groups, 1, LANES)

        @pl.when((tile == 0) & few)
        def _():
            def digits_of(step, total):
                place = tile_row(places_ref, step)
                high = lax.shift_right_arithmetic(place, 6)
                digits = jnp.concatenate([high, place - high * 64] * 4, axis=0)
                digits = digits.astype(jnp.float32).astype(jnp.bfloat16)
                return total + contract_last(digits, picks(tile_row(ranks_ref, step)))

            digits = lax.fori_loop(0, steps, digits_of, jnp.zeros((8, PICKED), jnp.float32))
            place = (digits[0:1] * 64.0 + digits[1:2]).astype(jnp.int32)
            index = lax.broadcasted_iota(jnp.int32, (1, PICKED), 1)
            place = jnp.where(index < plan_ref[3], place, -1)
            picked_ref[...] = jnp.broadcast_to(place, (8, PICKED))
            acc[:PICKED, :] = jnp.zeros((PICKED, D), jnp.float32)

            def one(step, carry):
                hits = rows_picked(plan_ref, step, place)
                acc[:PICKED, :] += contract_first(hits, table_ref[chunk_of(plan_ref, step), :])
                return carry

            lax.fori_loop(0, chunks_of(plan_ref), one, 0)
            picked[...] = acc[:PICKED, :].astype(jnp.bfloat16)

        @pl.when(few)
        def _():
            hits = picks(tile_row(ranks_ref, tile))
            out_ref[...] = contract_first(hits, picked[...]).astype(jnp.bfloat16)

        @pl.when(jnp.logical_not(few))
        def _():
            acc[...] = jnp.zeros_like(acc)
            wanted = tile_row(tokens_ref, tile)

            def one(step, carry):
                chunk = chunk_of(plan_ref, step)
                hits = ones_where(ids_ref[chunk, :] == wanted)
                acc[...] += contract_first(hits, table_ref[chunk, :])
                return carry

            lax.fori_loop(0, chunks_of(plan_ref), one, 0)
            out_ref[...] = acc[...].astype(jnp.bfloat16)

    lanes = (groups, 1, LANES)
    return local_call(
        "look_up",
        kernel,
        steps,
        plan,
        (row_ids, tokens, places, table),
        [whole((rows, 1)), whole(lanes), whole(lanes), whole((rows, D))],
        [
            jax.ShapeDtypeStruct((groups * LANES, D), jnp.bfloat16),
            jax.ShapeDtypeStruct(lanes, jnp.int32),
            jax.ShapeDtypeStruct((8, PICKED), jnp.int32),
        ],
        [ROWS_SPEC, whole(lanes), whole((8, PICKED))],
        [pltpu.VMEM((TILE, D), jnp.float32), pltpu.VMEM((PICKED, D), jnp.bfloat16)],
    )


def head_forward(plan, row_ids, labels, table, final):
    rows, groups = table.shape[0], labels.shape[0]
    steps = groups // TILE_GROUPS

    def kernel(plan_ref, ids_ref, labels_ref, table_ref, *rest):
        final_refs, (powers_ref, stats_ref, scores, hidden) = rest[:TILE_GROUPS], rest[TILE_GROUPS:]
        blank = jnp.zeros((1, TILE), jnp.float32)
        active = pl.program_id(0) <= last_tile(plan_ref)
        own = groups_of(plan_ref)

        def put(top, total, target):
            pad = jnp.zeros((5, LANES), jnp.float32)
            for place in range(TILE_GROUPS):
                lanes = slice(place * LANES, (place + 1) * LANES)
                stats_ref[own[place]] = jnp.concatenate(
                    [top[:, lanes], total[:, lanes], target[:, lanes], pad], axis=0
                )

        @pl.when(jnp.logical_not(active))
        def _():
            put(blank - 1e30, blank, blank)

        @pl.when(active)
        def _():
            wanted = row_of(labels_ref, own)
            for place, ref in enumerate(final_refs):
                hidden[place * LANES : (place + 1) * LANES, :] = ref[...]

            def first(step, carry):
                top, target = carry
                chunk = chunk_of(plan_ref, step)
                ids = ids_ref[chunk, :]
                raw = contract_last(table_ref[chunk, :], hidden[...])
                raw = jnp.where(ids >= 0, raw, -1e30)
                scores[chunk, :] = raw
                top = jnp.maximum(top, jnp.max(raw, axis=0, keepdims=True))
                target = target + jnp.sum(
                    jnp.where(ids == wanted, raw, 0.0), axis=0, keepdims=True
                )
                return (top, target)

            top, target = lax.fori_loop(0, chunks_of(plan_ref), first, (blank - 1e30, blank))

            def second(step, total):
                chunk = chunk_of(plan_ref, step)
                powers = jnp.exp(scores[chunk, :] - top)
                powers_ref[chunk, :] = powers.astype(jnp.bfloat16)
                return total + jnp.sum(powers, axis=0, keepdims=True)

            put(top, lax.fori_loop(0, chunks_of(plan_ref), second, blank), target)

    return local_call(
        "head_forward",
        kernel,
        steps,
        plan,
        (row_ids, labels, table) + (final,) * TILE_GROUPS,
        [whole((rows, 1)), whole((groups, 1, LANES)), whole((rows, D))] + group_specs(),
        [
            jax.ShapeDtypeStruct((rows, groups * LANES), jnp.bfloat16),
            jax.ShapeDtypeStruct((groups, 8, LANES), jnp.float32),
        ],
        [powers_spec(rows), whole((groups, 8, LANES))],
        [pltpu.VMEM((rows, TILE), jnp.float32), pltpu.VMEM((TILE, D), jnp.bfloat16)],
    )


def head_backward(plan, row_ids, labels, keep, stats, log_totals, table, final, powers):
    rows, groups = table.shape[0], labels.shape[0]
    steps = groups // TILE_GROUPS

    def kernel(plan_ref, ids_ref, labels_ref, keep_ref, stats_ref, logs_ref, table_ref, powers_ref, *rest):
        final_refs = rest[:TILE_GROUPS]
        grad_final_ref, grad_table_ref, acc, hidden, low, sems = rest[TILE_GROUPS:]
        tile = pl.program_id(0)
        slot = lax.rem(tile, 2)
        active = tile <= last_tile(plan_ref)

        def copies(step):
            start, side = PLAN_GROUPS + step * TILE_GROUPS, lax.rem(step, 2)
            return [
                pltpu.make_async_copy(
                    low.at[side, place],
                    grad_final_ref.at[plan_ref[start + place]],
                    sems.at[side, place],
                )
                for place in range(TILE_GROUPS)
            ]

        @pl.when(tile == 0)
        def _():
            grad_table_ref[...] = jnp.zeros_like(grad_table_ref)

        @pl.when(tile >= 2)
        def _():
            for copy in copies(tile - 2):
                copy.wait()

        acc[...] = jnp.zeros_like(acc)

        @pl.when(active)
        def _():
            own = groups_of(plan_ref)
            wanted, kept = row_of(labels_ref, own), row_of(keep_ref, own)
            tops = row_of(stats_ref, own)
            scale = jnp.exp(tops - row_of(logs_ref, own)) * kept
            for place, ref in enumerate(final_refs):
                hidden[place * LANES : (place + 1) * LANES, :] = ref[...]

            def one(step, carry):
                chunk = chunk_of(plan_ref, step)
                grads = powers_ref[chunk, :].astype(jnp.float32) * scale
                grads = grads - jnp.where(ids_ref[chunk, :] == wanted, kept, 0.0)
                grads = grads.astype(jnp.bfloat16)
                grad_table_ref[chunk, :] += times(grads, hidden[...])
                acc[...] += contract_first(grads, table_ref[chunk, :])
                return carry

            lax.fori_loop(0, chunks_of(plan_ref), one, 0)

        low[slot] = acc[...].astype(jnp.bfloat16).reshape(TILE_GROUPS, LANES, D)
        for copy in copies(tile):
            copy.start()

        @pl.when(tile == steps - 1)
        def _():
            for step in range(max(0, steps - 2), steps):
                for copy in copies(step):
                    copy.wait()

    lanes = (groups, 1, LANES)
    return local_call(
        "head_backward",
        kernel,
        steps,
        plan,
        (row_ids, labels, keep, stats, log_totals, table, powers) + (final,) * TILE_GROUPS,
        [
            whole((rows, 1)),
            whole(lanes),
            whole(lanes),
            whole((groups, 8, LANES)),
            whole((groups, 8, LANES)),
            whole((rows, D)),
            powers_spec(rows),
        ]
        + group_specs(),
        [
            jax.ShapeDtypeStruct((groups, LANES, D), jnp.bfloat16),
            jax.ShapeDtypeStruct((rows, D), jnp.float32),
        ],
        [pl.BlockSpec(memory_space=pl.ANY), whole((rows, D))],
        [
            pltpu.VMEM((TILE, D), jnp.float32),
            pltpu.VMEM((TILE, D), jnp.bfloat16),
            pltpu.VMEM((2, TILE_GROUPS, LANES, D), jnp.bfloat16),
            pltpu.SemaphoreType.DMA((2, TILE_GROUPS)),
        ],
    )


def look_back(
    plan, slot_plan, slots, row_ids, tokens, ranks, picked, grad_start, grad_table, layer_grads
):
    rows, groups = grad_table.shape[0], tokens.shape[0]
    steps = groups // TILE_GROUPS
    half_rows = layer_grads[0].shape[1]
    block = SLOT_STEP * half_rows
    kinds = len(layer_grads)

    def kernel(plan_ref, slot_ref, ids_ref, tokens_ref, ranks_ref, picked_ref, grad_ref, table_ref, *rest):
        layer_refs = rest[:kinds]
        slots_ref, squares_ref, acc, held, out_ref = rest[kinds:]
        step = pl.program_id(0)
        few = plan_ref[3] <= PICKED

        @pl.when(step == 0)
        def _():
            acc[...] = jnp.zeros_like(acc)
            squares_ref[...] = jnp.zeros_like(squares_ref)

        @pl.when((step < steps) & few)
        def _():
            acc[...] += times(picks(tile_row(ranks_ref, step)), grad_ref[...])

        @pl.when((step < steps) & jnp.logical_not(few))
        def _():
            held[step] = grad_ref[...]

        @pl.when(step >= steps)
        def _():
            start = (step - steps) * block

            @pl.when(few)
            def _():
                row = lax.broadcasted_iota(jnp.int32, (block, PICKED), 0) + start
                hits = ones_where(row == picked_ref[0:1, :])
                out_ref[...] = table_ref[...] + times(hits, acc[...].astype(jnp.bfloat16))

            @pl.when(jnp.logical_not(few))
            def _():
                out_ref[...] = table_ref[...]
                ids = ids_ref[pl.ds(pl.multiple_of(start, 16), block), :]

                def one(tile, carry):
                    hits = ones_where(ids == tile_row(tokens_ref, tile))
                    out_ref[...] += times(hits, held[tile])
                    return carry

                lax.fori_loop(0, steps, one, 0)

            for place in range(SLOT_STEP):
                slot = (step - steps) * SLOT_STEP + place
                kind = slot_ref[0, slot]
                part = slice(place * half_rows, (place + 1) * half_rows)

                for index in range(kinds):

                    @pl.when(kind == index)
                    def _():
                        layer = layer_refs[index][slot_ref[1 + index, slot]]
                        out_ref[part, :] = layer.astype(jnp.float32)

                @pl.when(kind < 0)
                def _():
                    out_ref[part, :] = jnp.zeros((half_rows, D), jnp.float32)

                slots_ref[place] = out_ref[part, :]

            values = out_ref[...]
            squares_ref[...] += (values * values).reshape(block // 8, 8, D).sum(axis=0)

    def fixed(shape):
        return pl.BlockSpec(
            shape, lambda step, plan, slot: (0,) * len(shape), pipeline_mode=pl.Buffered(1)
        )

    lanes = (groups, 1, LANES)
    row_spec = pl.BlockSpec((block, D), lambda step, plan, slot: (jnp.maximum(step - steps, 0), 0))
    return pl.pallas_call(
        kernel,
        name="look_back",
        grid_spec=pltpu.PrefetchScalarGridSpec(
            num_scalar_prefetch=2,
            grid=(steps + -(-slots // SLOT_STEP),),
            in_specs=[
                fixed((rows, 1)),
                fixed(lanes),
                fixed(lanes),
                fixed((8, PICKED)),
                pl.BlockSpec((TILE, D), lambda step, plan, slot: (jnp.minimum(step, steps - 1), 0)),
                row_spec,
            ]
            + [fixed(grads.shape) for grads in layer_grads],
            out_specs=[
                pl.BlockSpec(
                    (SLOT_STEP, half_rows, D),
                    lambda step, plan, slot: (jnp.maximum(step - steps, 0), 0, 0),
                ),
                fixed((8, D)),
            ],
            scratch_shapes=[
                pltpu.VMEM((PICKED, D), jnp.float32),
                pltpu.VMEM((steps, TILE, D), jnp.bfloat16),
                pltpu.VMEM((block, D), jnp.float32),
            ],
        ),
        out_shape=[
            jax.ShapeDtypeStruct((slots, half_rows, D), jnp.float32),
            jax.ShapeDtypeStruct((8, D), jnp.float32),
        ],
        cost_estimate=SHORT,
        compiler_params=pltpu.CompilerParams(vmem_limit_bytes=60 << 20),
    )(
        plan,
        slot_plan,
        row_ids,
        tokens,
        ranks,
        picked,
        grad_start,
        grad_table,
        *layer_grads,
    )


def grads_home(level):
    return [(2 * level, 0), (2 * level + 1, 0), (2 * level + 1, 1)]


def body(
    token_ids,
    labels,
    real_counts,
    owners,
    master,
    first_moment,
    second_moment,
    gains,
    gains_first,
    gains_second,
    mix,
    mix_first,
    mix_second,
):
    tensors = lax.axis_size("tensor")
    groups = lax.axis_size("dp")
    group = lax.axis_index("dp")
    tensor_part = lax.axis_index("tensor")
    seq_part = lax.axis_index("seq")
    slots, half_rows, _ = master.shape
    seq_count, half_len = token_ids.shape
    row_count = seq_count * half_len
    share = row_count // tensors
    head_rows = 3 * D // tensors
    out_rows = D // tensors
    unit_rows = FF // tensors
    layer_rows = head_rows + out_rows + 2 * unit_rows
    layer_blocks = layer_rows // (2 * half_rows)
    blocks = LAYERS * layer_blocks
    vocab_rows = VOCAB // tensors
    local_heads = HEADS // tensors

    slot_rank = slot_table(owners)
    block_ids = jnp.arange(owners.shape[0], dtype=jnp.int32)
    mine = owners == group
    match = (jnp.arange(slots)[:, None] == slot_rank[None, :]) & mine[None, :]
    slot_block = jnp.sum(jnp.where(match, block_ids[None, :] + 1, 0), axis=1) - 1
    spare = -(-ROW_STEP // half_rows)
    spare += -(slots + spare) % SLOT_STEP
    held = jnp.sum(jnp.where(mine, 1, 0)) * half_rows
    first_held = jnp.sum(jnp.where(mine & (block_ids < blocks), 1, 0)) * half_rows
    slot_block_all = jnp.pad(slot_block, (0, spare), constant_values=-1).astype(jnp.int32)
    third = layer_blocks // 3
    which, within = slot_block_all // third, slot_block_all % third
    homes = [home for level in range(LAYERS) for home in grads_home(level)]
    arrays = 1 + max(array for array, _ in homes)
    kind, index = jnp.full(which.shape, -1), jnp.zeros_like(which)
    for place, (array, part) in enumerate(homes):
        kind = jnp.where(which == place, array, kind)
        index = jnp.where(which == place, within + part * third, index)
    kind = jnp.where(slot_block_all >= blocks, arrays, jnp.where(slot_block_all < 0, -1, kind))
    slot_plan = jnp.stack(
        [kind] + [jnp.where(kind == array, index, 0) for array in range(arrays)]
    ).astype(jnp.int32)

    packed = jnp.concatenate(
        [
            token_ids.reshape(tensors, LANES),
            labels.reshape(tensors, LANES),
            jnp.broadcast_to(real_counts[:, None], (16 - 2 * tensors, LANES)),
        ],
        axis=0,
    )
    width = -(-(2 * tensors * groups + PLAN_GROUPS) // LANES) * LANES
    lane = jnp.arange(width)[None, :]
    ends = jnp.where(lane == 0, first_held, jnp.where(lane == 1, held, 0)).astype(jnp.int32)
    ids_all, labels_all, keep_all, places, plan, count = spread_tokens(
        packed, slot_block_all[:, None], ends, blocks, half_rows, 15
    )
    plan = plan.reshape(-1)
    order = (2, tensors, groups, share)

    first_id = (tensor_part * vocab_rows + seq_part * half_rows).astype(jnp.int32)
    table, halves, row_ids = prepare(slot_block_all, first_id, master, blocks)

    def weights_line(*starts):
        return Line([(halves, start * third, third) for start in starts], True)

    def as_table(joined):
        return joined.reshape(-1, D)

    positions = seq_part * half_len + jnp.arange(row_count) % half_len
    steps_half = jnp.arange(HEAD_DIM // 2).astype(jnp.float32)
    freqs = 10000.0 ** (-2.0 * steps_half / HEAD_DIM)
    angles = freqs[:, None] * positions.astype(jnp.float32)[None, :]
    cosine, sine = jnp.cos(angles), jnp.sin(angles)

    looked, ranks, picked = look_up(plan, row_ids, ids_all, places, table)
    looked = looked.reshape(order + (D,))
    gain = [gains[i : i + 1] for i in range(2 * LAYERS + 1)]
    piece = ((share, D), jnp.float32)

    def normed_of(total, gain_row):
        return (total[...], layer_norm_parts(total[...])[0] * gain_row[...])

    def inner_of(total, stream, gain_row):
        inner = stream + total
        return (inner, layer_norm_parts(inner)[0] * gain_row)

    def outcome_of(base, total, inner, gain_row, *rest):
        states, scalars = rest[:-1], rest[-1]
        outcome = inner + total
        stream = scalars[base + len(states)] * outcome
        for source, state in enumerate(states):
            stream = stream + scalars[base + source] * state
        return (outcome, stream, layer_norm_parts(stream)[0] * gain_row)

    start, normed, joined = reduce_rows(
        "normed", looked, (14, 18, 1), weights_line(0, 1), normed_of, [gain[0]], [], [piece]
    )
    table_one = as_table(joined)
    attention_table, up = table_one, (table_one, 1)
    tables = []
    states, streams, inners, kept_all = [start], [start], [], []
    for level in range(LAYERS):
        here, last = 3 * level, level == LAYERS - 1
        carried = [] if last else [here + 3]
        carried += [here + 1, here + 2] if level else [here + 2]
        inner, normed_two, queries, both, logs, attended, joined = tensor_step(
            f"inner_{level}",
            inner_of,
            attention_work(normed, attention_table, cosine, sine),
            (streams[level], gain[2 * level + 1]),
            (),
            [piece],
            True,
            2 if level == 0 else 15 + level,
            weights_line(*carried),
        )
        kept = (queries, both, logs, attended)
        joined = as_table(joined)
        down = (joined, len(carried) - 1)
        up = (joined, len(carried) - 2) if level else up
        tables.append((attention_table, up, down))
        attention_table = joined
        outcome, stream, normed_next, hidden, activated = tensor_step(
            f"outcome_{level}",
            partial(outcome_of, (level + 1) * (level + 2) // 2 - 1),
            unit_work(normed_two, up, down),
            [inner, gain[2 * level + 2]] + states,
            (mix,),
            [piece, piece] + ([((share, D), jnp.bfloat16)] if last else []),
            not last,
            3 + level,
        )
        inners.append(inner)
        kept_all.append((normed, kept, normed_two, (hidden, activated)))
        states.append(outcome)
        streams.append(stream)
        normed = normed_next

    final_all = gather_all(normed, 3 + LAYERS)[0].reshape(-1, D)
    powers, stats = head_forward(plan, row_ids, labels_all, table, final_all)
    home, log_totals = join_stats(
        stats.reshape((2, tensors, groups, 8, LANES)), 4 + LAYERS
    )
    grad_final, grad_table = head_backward(
        plan,
        row_ids,
        labels_all,
        keep_all,
        stats,
        log_totals.reshape(-1, 8, LANES),
        table,
        final_all,
        powers,
    )
    grad_final = grad_final.reshape(order + (D,))

    row = ((1, D), jnp.float32)

    def top_of(total, stream, gain_row, scalars):
        grad_top, grad_gain = norm_pull(total[...], gain_row[...], stream[...])
        grad_state = scalars[MIX_WEIGHTS - 1] * grad_top
        return (grad_top, grad_state, grad_gain, grad_state)

    def inner_back(total, grad_out, inner, gain_row):
        grad, grad_gain = norm_pull(total, gain_row, inner)
        grad = grad_out + grad
        return (grad, grad_gain, grad)

    def stream_back(block, total, grad_inner, stream, gain_row, *rest):
        grad_ys, scalars = rest[:-1], rest[-1]
        grad, grad_gain = norm_pull(total, gain_row, stream)
        grad = grad_inner + grad
        state = grad if block == 0 else scalars[block * (block + 1) // 2 - 1 + block] * grad
        for offset, grad_y in enumerate(grad_ys):
            later = block + 1 + offset
            state = state + scalars[later * (later + 1) // 2 - 1 + block] * grad_y
        return (grad, state, grad_gain, state)

    grad_ys = [None] * (LAYERS + 1)
    gain_grads = [None] * (2 * LAYERS + 1)
    layer_grads, attention_grads = [None] * (2 * LAYERS), None
    grad_ys[LAYERS], grad_state, gain_grads[2 * LAYERS], grad_branch = reduce_rows(
        "top_back",
        grad_final,
        (0, 0, 5 + LAYERS),
        None,
        top_of,
        [streams[LAYERS], gain[2 * LAYERS]],
        [mix],
        [piece, piece, row],
    )
    for level in reversed(range(LAYERS)):
        normed, kept, normed_two, unit_kept = kept_all[level]
        attention_table, up, down = tables[level]
        grad_inner, gain_grads[2 * level + 1], grad_attn, unit_grads, *summed = tensor_step(
            f"inner_back_{level}",
            inner_back,
            unit_back_work(grad_branch, normed_two, up, down, unit_kept, half_rows),
            (grad_state, inners[level], gain[2 * level + 1]),
            (),
            [piece, row],
            True,
            6 + LAYERS if level == 0 else 19 + level,
            None if attention_grads is None else Line([(attention_grads, 0, third)], False),
        )
        if summed:
            layer_grads[2 * (level + 1)] = summed[0]
        grad_ys[level], grad_state, gain_grads[2 * level], grad_branch, attention_grads, summed = (
            tensor_step(
                f"stream_back_{level}",
                partial(stream_back, level),
                attention_back_work(
                    grad_attn, normed, attention_table, kept, cosine, sine, half_rows
                ),
                [grad_inner, streams[level], gain[2 * level]] + grad_ys[level + 1 :],
                (mix,),
                [piece, piece, row] + ([] if level else [((share, D), jnp.bfloat16)]),
                level > 0,
                7 + LAYERS + level,
                Line([(unit_grads, 0, 2 * third)], False),
            )
        )
        layer_grads[2 * level + 1] = summed

    grad_start_all, layer_grads[0] = gather_all(
        grad_branch, 13, Line([(attention_grads, 0, third)], False)
    )
    grad_start_all = grad_start_all.reshape(-1, D)
    owned, table_squares = look_back(
        plan,
        slot_plan,
        slots,
        row_ids,
        ids_all,
        ranks,
        picked,
        grad_start_all,
        grad_table,
        layer_grads,
    )
    keep = jnp.where(
        tensor_part * share + jnp.arange(share) < real_counts[0], 1.0, 0.0
    ).astype(jnp.float32)
    news = finish(
        gain_grads,
        states,
        grad_ys[1:],
        home,
        keep[None],
        table_squares,
        count,
        (gains, gains_first, gains_second, mix[None], mix_first[None], mix_second[None]),
        7 + 2 * LAYERS,
    )
    new_gains, new_gains_first, new_gains_second = news[:3]
    new_mix, new_mix_first, new_mix_second = [value[0] for value in news[3:6]]
    loss_sum, clip_norm = news[6][0, 0], news[6][0, 1]
    token_count = count[0, 0]
    owned = owned * news[7][0, 0]
    new_master, new_first, new_second = adam_update(
        master, first_moment, second_moment, owned, RATE_MATRIX, DECAY_MATRIX
    )
    return (
        new_master,
        new_first,
        new_second,
        new_gains,
        new_gains_first,
        new_gains_second,
        new_mix,
        new_mix_first,
        new_mix_second,
        loss_sum,
        token_count,
        clip_norm,
    )


def solution(mesh):
    return jax.shard_map(
        body,
        mesh=mesh,
        in_specs=(
            P("dp", "seq"),
            P("dp", "seq"),
            P(("dp", "seq")),
            P(),
            P("dp", ("tensor", "seq"), None),
            P("dp", ("tensor", "seq"), None),
            P("dp", ("tensor", "seq"), None),
            P(),
            P(),
            P(),
            P(),
            P(),
            P(),
        ),
        out_specs=(
            P("dp", ("tensor", "seq"), None),
            P("dp", ("tensor", "seq"), None),
            P("dp", ("tensor", "seq"), None),
            P(),
            P(),
            P(),
            P(),
            P(),
            P(),
            P(),
            P(),
            P(),
        ),
        check_vma=False,
    )
```

```python
from functools import partial

import jax
import jax.numpy as jnp
from jax import lax
from jax.experimental import pallas as pl
from jax.experimental.pallas import tpu as pltpu
from jax.sharding import PartitionSpec as P

D = 768
HEADS = 12
HEAD_DIM = 64
FF = 3072
VOCAB = 50304
LAYERS = 2
STEP_COUNT = 10
MIX_WEIGHTS = 5


EPS_NORM = 1e-05
CLIP_NORM = 0.01
BETA_ONE = 0.9
BETA_TWO = 0.95
ADAM_EPS = 1e-08
RATE_MATRIX = 0.04
RATE_SMALL = 0.4
DECAY_MATRIX = 0.1


def contract_last(left, right):
    return lax.dot_general(
        left, right, (((1,), (1,)), ((), ())), preferred_element_type=jnp.float32
    )


def contract_first(left, right):
    return lax.dot_general(
        left, right, (((0,), (0,)), ((), ())), preferred_element_type=jnp.float32
    )


def slot_table(owners):
    ranks = jnp.arange(owners.shape[0])
    same = (owners[None, :] == owners[:, None]) & (ranks[None, :] < ranks[:, None])
    return jnp.sum(jnp.where(same, 1, 0), axis=1).astype(jnp.int32)


def adam_update(weight, first, second, grad, rate, decay):
    first = BETA_ONE * first + (1.0 - BETA_ONE) * grad
    second = BETA_TWO * second + (1.0 - BETA_TWO) * grad * grad
    first_hat = first / (1.0 - BETA_ONE**STEP_COUNT)
    second_hat = second / (1.0 - BETA_TWO**STEP_COUNT)
    weight = weight - rate * (first_hat / (jnp.sqrt(second_hat) + ADAM_EPS) + decay * weight)
    return (weight, first, second)


MESH = pl.DeviceIdType.MESH
ROW_STEP = 400
TILE_GROUPS = 8
LANES = 128
SHORT = pl.CostEstimate(flops=1000, bytes_accessed=1000, transcendentals=0)


def meet(peers):
    gate = pltpu.get_barrier_semaphore()
    for peer in peers:
        pl.semaphore_signal(gate, inc=1, device_id=peer, device_id_type=MESH)
    pl.semaphore_wait(gate, len(peers))


def others(axis):
    count, me = lax.axis_size(axis), lax.axis_index(axis)
    return [lax.rem(me + step, count) for step in range(1, count)]


def behind(axis, step):
    count, me = lax.axis_size(axis), lax.axis_index(axis)
    return lax.rem(me + count - step, count)


def send(source, target, send_sem, recv_sem, device):
    copy = pltpu.make_async_remote_copy(
        src_ref=source,
        dst_ref=target,
        send_sem=send_sem,
        recv_sem=recv_sem,
        device_id=device,
        device_id_type=MESH,
    )
    copy.start()
    return copy


def layer_norm_parts(stream):
    center = stream - jnp.mean(stream, -1, keepdims=True)
    inverse = lax.rsqrt(jnp.mean(center * center, -1, keepdims=True) + EPS_NORM)
    return center * inverse, inverse


def norm_pull(grad_normed, gain, stream):
    scaled, inverse = layer_norm_parts(stream)
    grad_scaled = grad_normed * gain
    grad_stream = inverse * (
        grad_scaled
        - jnp.mean(grad_scaled, -1, keepdims=True)
        - scaled * jnp.mean(grad_scaled * scaled, -1, keepdims=True)
    )
    return grad_stream, jnp.sum(grad_normed * scaled, axis=0, keepdims=True)


class Work:
    def __init__(self, before, during, operands, specs, outs, scratch, after=None, twins=False):
        self.before, self.during, self.after, self.twins = before, during, after, twins
        self.operands, self.specs, self.outs, self.scratch = operands, specs, outs, scratch


def tensor_step(name, function, work, extras, scalars, outs, gather, collective_id, line=None):
    parts = lax.axis_size("tensor")
    share = extras[0].shape[0]
    reduce = work is not None
    work = work or Work(None, None, [], [], [], [])

    def kernel(*refs):
        refs = list(refs)

        def take(count):
            return [refs.pop(0) for _ in range(count)]

        work_refs = take(len(work.operands))
        extra_refs = take(len(extras))
        scalar_refs = take(len(scalars))
        source_refs = take(len(line.operands)) if line else []
        out_refs = take(len(outs))
        (full,) = take(1) if gather else [None]
        work_outs = take(len(work.outs))
        (joined,) = take(1) if line else [None]
        send_sems, recv_sems = take(2)
        partial_ref, outgoing, arrived = take(3) if reduce else [None] * 3
        if line:
            line.bind(source_refs, joined, take(len(line.scratch)))
            line.load()

        def tick(count=1):
            if line:
                line.steps(count)

        me, side = lax.axis_index("tensor"), lax.axis_index("seq")
        peers = others("tensor")
        twin = {"seq": 1 - side}
        twins = work.twins or (line and line.share)
        meet(
            [{"tensor": peer} for peer in peers]
            + [twin] * bool(twins)
            + ([{"dp": peer} for peer in others("dp")] if line else [])
        )
        if line:
            line.begin()
        total = None
        if reduce:
            work.before(work_refs, work_outs, refs, partial_ref, tick)
            copies = []
            for step, peer in enumerate(peers):
                rows = pl.ds(pl.multiple_of(peer * share, share), share)
                outgoing[step] = partial_ref[rows, :].astype(jnp.bfloat16)
                copies.append(
                    send(
                        outgoing.at[step],
                        arrived.at[step],
                        send_sems.at[0, step],
                        recv_sems.at[0, step],
                        {"tensor": peer},
                    )
                )
            if work.during:
                work.during(work_refs, work_outs, refs)
            tick(6)
            total = partial_ref[pl.ds(pl.multiple_of(me * share, share), share), :]
            for step, copy in enumerate(copies):
                copy.wait()
                total = total + arrived[step].astype(jnp.float32)
        results = function(total, *[ref[...] for ref in extra_refs], *scalar_refs)
        for ref, value in zip(out_refs, results):
            ref[...] = value.astype(ref.dtype)
        if gather:
            full[me] = results[len(outs)].astype(jnp.bfloat16)
            copies = [
                send(
                    full.at[me],
                    full.at[me],
                    send_sems.at[1, step],
                    recv_sems.at[1, step],
                    {"tensor": peer},
                )
                for step, peer in enumerate(peers)
            ]
        if work.after:
            work.after(work_refs, work_outs, refs)
        tick(None)
        if gather:
            for copy in copies:
                copy.wait()
        if line:
            line.end()

    vmem = pl.BlockSpec(memory_space=pltpu.VMEM)
    smem = pl.BlockSpec(memory_space=pltpu.SMEM)
    shapes = [jax.ShapeDtypeStruct(shape, dtype) for shape, dtype in outs]
    if gather:
        shapes.append(jax.ShapeDtypeStruct((parts, share, D), jnp.bfloat16))
    shapes += [jax.ShapeDtypeStruct(shape, dtype) for shape, dtype in work.outs]
    out_specs = [vmem] * len(shapes)
    operands = list(work.operands) + list(extras) + list(scalars)
    in_specs = list(work.specs) + [vmem] * len(extras) + [smem] * len(scalars)
    dma = pltpu.SemaphoreType.DMA
    buffers = [dma((2, parts - 1))] * 2
    if reduce:
        buffers += [pltpu.VMEM((parts * share, D), jnp.float32)]
        buffers += [pltpu.VMEM((parts - 1, share, D), jnp.bfloat16)] * 2
    if line:
        operands += line.operands
        in_specs += line.in_specs
        shapes.append(line.out_shape)
        out_specs.append(line.out_spec)
        buffers += line.scratch
    return pl.pallas_call(
        kernel,
        name=name,
        grid=(1,),
        out_shape=shapes,
        in_specs=in_specs,
        out_specs=out_specs,
        scratch_shapes=buffers + list(work.scratch),
        cost_estimate=SHORT,
        compiler_params=pltpu.CompilerParams(
            collective_id=collective_id, has_side_effects=True, vmem_limit_bytes=60 << 20
        ),
    )(*operands)


VMEM_SPEC = pl.BlockSpec(memory_space=pltpu.VMEM)


def part_spec(rows, index):
    return pl.BlockSpec((rows, D), lambda step: (index, 0), pipeline_mode=pl.Buffered(1))


def turn(block, cosine, sine):
    half = HEAD_DIM // 2
    first, second = block[:half], block[half:]
    return jnp.concatenate(
        [first * cosine - second * sine, second * cosine + first * sine], axis=0
    )


def times(left, right):
    return jnp.dot(left, right, preferred_element_type=jnp.float32)


def masks_of(count, side):
    key = lax.broadcasted_iota(jnp.int32, (count, count), 0)
    query = lax.broadcasted_iota(jnp.int32, (count, count), 1)
    far = jnp.where(side == 0, -1e30, 0.0).astype(jnp.float32)
    return far, jnp.where(key <= query, 0.0, -1e30)


def scores_of(keys_values, head, queries, masks):
    span = slice(head * HEAD_DIM, (head + 1) * HEAD_DIM)
    scale = HEAD_DIM ** (-0.5)
    far = contract_first(keys_values[0, 0, span, :], queries) * scale + masks[0]
    own = contract_first(keys_values[1, 0, span, :], queries) * scale + masks[1]
    return far, own


def attention_work(normed, table, cosine, sine):
    parts, share, _ = normed.shape
    count = parts * share
    width = D // parts
    heads = width // HEAD_DIM

    def before(ins, outs, scratch, partial_ref, tick):
        normed_ref, qkv_ref, out_ref, cosine_ref, sine_ref = ins
        queries_ref, both, logs_ref, attended_ref = outs
        send_sem, recv_sem = scratch
        side = lax.axis_index("seq")
        cosine, sine = cosine_ref[...], sine_ref[...]
        rows = normed_ref[...].reshape(count, D)
        joined = contract_last(qkv_ref[...], rows)
        tick()
        for head in range(heads):
            span = slice(head * HEAD_DIM, (head + 1) * HEAD_DIM)
            keys = joined[width + head * HEAD_DIM : width + (head + 1) * HEAD_DIM]
            both[1, 0, span, :] = turn(keys, cosine, sine).astype(jnp.bfloat16)
        both[1, 1] = joined[2 * width :].astype(jnp.bfloat16)
        copy = pltpu.make_async_remote_copy(
            src_ref=both.at[1],
            dst_ref=both.at[0],
            send_sem=send_sem,
            recv_sem=recv_sem,
            device_id={"seq": 1 - side},
            device_id_type=MESH,
        )

        copy.start()
        for head in range(heads):
            span = slice(head * HEAD_DIM, (head + 1) * HEAD_DIM)
            queries_ref[span, :] = turn(joined[span], cosine, sine).astype(jnp.bfloat16)

        copy.wait()
        masks = masks_of(count, side)
        for head in range(heads):
            span = slice(head * HEAD_DIM, (head + 1) * HEAD_DIM)
            far, own = scores_of(both, head, queries_ref[span, :], masks)
            peak = jnp.maximum(
                jnp.max(far, axis=0, keepdims=True), jnp.max(own, axis=0, keepdims=True)
            )
            far, own = jnp.exp(far - peak), jnp.exp(own - peak)
            total = jnp.sum(far, axis=0, keepdims=True) + jnp.sum(own, axis=0, keepdims=True)
            logs_ref[head] = peak + jnp.log(total)
            inverse = 1.0 / total
            attended = times(both[0, 1, span, :], (far * inverse).astype(jnp.bfloat16))
            attended += times(both[1, 1, span, :], (own * inverse).astype(jnp.bfloat16))
            attended_ref[span, :] = attended.astype(jnp.bfloat16)
            tick(2)
        partial_ref[...] = contract_first(attended_ref[...], out_ref[...])

    low = jnp.bfloat16
    return Work(
        before,
        None,
        [normed, table, table, cosine, sine],
        [VMEM_SPEC, part_spec(3 * width, 0), part_spec(width, 3), VMEM_SPEC, VMEM_SPEC],
        [
            ((width, count), low),
            ((2, 2, width, count), low),
            ((heads, 1, count), jnp.float32),
            ((width, count), low),
        ],
        [pltpu.SemaphoreType.DMA, pltpu.SemaphoreType.DMA],
        twins=True,
    )


def fold_copy(own, near, send_sems, recv_sems, index):
    side = lax.axis_index("seq")
    return pltpu.make_async_remote_copy(
        src_ref=own.at[index, :, 1 - side],
        dst_ref=near.at[index],
        send_sem=send_sems.at[index],
        recv_sem=recv_sems.at[index],
        device_id={"seq": 1 - side},
        device_id_type=MESH,
    )


def add_halves(own, near, out, start):
    side = lax.axis_index("seq")

    def one(block, carry):
        value = own[block, side].astype(jnp.float32) + near[block].astype(jnp.float32)
        out[start + block] = value.astype(jnp.bfloat16)
        return carry

    lax.fori_loop(0, near.shape[0], one, 0)


def attention_back_work(grad, normed, table, kept, cosine, sine, half_rows):
    parts, share, _ = normed.shape
    count = parts * share
    width = D // parts
    heads = width // HEAD_DIM
    queries, both, logs, attended = kept
    blocks = 4 * width // (2 * half_rows)

    def before(ins, outs, scratch, partial_ref, tick):
        grad_ref, _, qkv_ref, out_ref, queries_ref, both, logs_ref, _, cosine_ref, sine_ref = ins
        back, came, grad_joined, send_sem, recv_sem = scratch[:5]
        side = lax.axis_index("seq")
        cosine, sine = cosine_ref[...], -sine_ref[...]
        scale = HEAD_DIM ** (-0.5)
        grads = contract_last(out_ref[...], grad_ref[...].reshape(count, D)).astype(jnp.bfloat16)
        tick()
        own_grads = []
        masks = masks_of(count, side)
        for head in range(heads):
            span = slice(head * HEAD_DIM, (head + 1) * HEAD_DIM)
            head_queries, head_grads = queries_ref[span, :], grads[span]
            far, own = scores_of(both, head, head_queries, masks)
            far, own = jnp.exp(far - logs_ref[head]), jnp.exp(own - logs_ref[head])
            far_grad = contract_first(both[0, 1, span, :], head_grads)
            own_grad = contract_first(both[1, 1, span, :], head_grads)
            mean = jnp.sum(far * far_grad, axis=0, keepdims=True)
            mean += jnp.sum(own * own_grad, axis=0, keepdims=True)
            far_grad = (far * (far_grad - mean)).astype(jnp.bfloat16)
            own_grad = (own * (own_grad - mean)).astype(jnp.bfloat16)
            far, own = far.astype(jnp.bfloat16), own.astype(jnp.bfloat16)
            back[0, span, :] = (contract_last(head_queries, far_grad) * scale).astype(jnp.bfloat16)
            back[1, span, :] = contract_last(head_grads, far).astype(jnp.bfloat16)
            query_grad = times(both[0, 0, span, :], far_grad) + times(both[1, 0, span, :], own_grad)
            grad_joined[span, :] = turn(query_grad * scale, cosine, sine).astype(jnp.bfloat16)
            own_grads.append(
                (contract_last(head_queries, own_grad) * scale, contract_last(head_grads, own))
            )
            tick(2)
        copy = send(back, came, send_sem, recv_sem, {"seq": 1 - side})
        copy.wait()
        for head, (key_grad, value_grad) in enumerate(own_grads):
            span = slice(head * HEAD_DIM, (head + 1) * HEAD_DIM)
            key_grad = key_grad + came[0, span, :].astype(jnp.float32)
            value_grad = value_grad + came[1, span, :].astype(jnp.float32)
            start = width + head * HEAD_DIM
            grad_joined[start : start + HEAD_DIM, :] = turn(key_grad, cosine, sine).astype(
                jnp.bfloat16
            )
            start += width
            grad_joined[start : start + HEAD_DIM, :] = value_grad.astype(jnp.bfloat16)
        partial_ref[...] = contract_first(grad_joined[...], qkv_ref[...])

    def during(ins, outs, scratch):
        grad_ref, normed_ref, attended_ref = ins[0], ins[1], ins[7]
        grad_joined = scratch[2]
        own, near, fold_send, fold_recv = scratch[5:]
        value = times(grad_joined[...], normed_ref[...].reshape(count, D)).astype(jnp.bfloat16)
        part = 3 * blocks // 4
        own[0, :part] = value.reshape(part, 2, half_rows, D)
        value = times(attended_ref[...], grad_ref[...].reshape(count, D)).astype(jnp.bfloat16)
        own[0, part:] = value.reshape(blocks - part, 2, half_rows, D)
        fold_copy(own, near, fold_send, fold_recv, 0).start()

    def after(ins, outs, scratch):
        own, near, fold_send, fold_recv = scratch[5:]
        fold_copy(own, near, fold_send, fold_recv, 0).wait()
        add_halves(own.at[0], near.at[0], outs[0], 0)

    low = jnp.bfloat16
    dma = pltpu.SemaphoreType.DMA
    return Work(
        before,
        during,
        [grad, normed, table, table, queries, both, logs, attended, cosine, sine],
        [VMEM_SPEC, VMEM_SPEC, part_spec(3 * width, 0), part_spec(width, 3)] + [VMEM_SPEC] * 6,
        [((blocks, half_rows, D), low)],
        [
            pltpu.VMEM((2, width, count), low),
            pltpu.VMEM((2, width, count), low),
            pltpu.VMEM((3 * width, count), low),
            dma,
            dma,
            pltpu.VMEM((1, blocks, 2, half_rows, D), low),
            pltpu.VMEM((1, blocks, half_rows, D), low),
            dma((1,)),
            dma((1,)),
        ],
        after,
        True,
    )


def gelu(hidden):
    return jax.nn.gelu(hidden, approximate=True)


def unit_work(normed, up, down):
    parts, share, _ = normed.shape
    count = parts * share
    units = FF // parts

    def before(ins, outs, scratch, partial_ref, tick):
        normed_ref, up_ref, down_ref = ins
        hidden_ref, activated_ref = outs
        hidden = contract_last(up_ref[...], normed_ref[...].reshape(count, D))
        hidden_ref[...] = hidden
        activated_ref[...] = gelu(hidden).astype(jnp.bfloat16)
        tick(2)
        partial_ref[...] = contract_first(activated_ref[...], down_ref[...])

    return Work(
        before,
        None,
        [normed, up[0], down[0]],
        [VMEM_SPEC, part_spec(units, up[1]), part_spec(units, down[1])],
        [((units, count), jnp.float32), ((units, count), jnp.bfloat16)],
        [],
    )


def unit_back_work(grad, normed, up, down, kept, half_rows):
    parts, share, _ = normed.shape
    count = parts * share
    units = FF // parts
    hidden, activated = kept
    blocks = units // (2 * half_rows)

    def before(ins, outs, scratch, partial_ref, tick):
        grad_ref, _, up_ref, down_ref, hidden_ref, _ = ins
        grad_hidden = scratch[0]
        grad_act = contract_last(down_ref[...], grad_ref[...].reshape(count, D))
        _, pull = jax.vjp(gelu, hidden_ref[...])
        grad_hidden[...] = pull(grad_act)[0].astype(jnp.bfloat16)
        tick(2)
        partial_ref[...] = contract_first(grad_hidden[...], up_ref[...])

    def during(ins, outs, scratch):
        grad_ref, normed_ref, _, _, _, activated_ref = ins
        grad_hidden, own, near, fold_send, fold_recv = scratch
        value = times(grad_hidden[...], normed_ref[...].reshape(count, D))
        own[0] = value.astype(jnp.bfloat16).reshape(own.shape[1:])
        fold_copy(own, near, fold_send, fold_recv, 0).start()
        value = times(activated_ref[...], grad_ref[...].reshape(count, D))
        own[1] = value.astype(jnp.bfloat16).reshape(own.shape[1:])
        fold_copy(own, near, fold_send, fold_recv, 1).start()

    def after(ins, outs, scratch):
        _, own, near, fold_send, fold_recv = scratch
        for index in range(2):
            fold_copy(own, near, fold_send, fold_recv, index).wait()
            add_halves(own.at[index], near.at[index], outs[0], index * blocks)

    low, dma = jnp.bfloat16, pltpu.SemaphoreType.DMA
    return Work(
        before,
        during,
        [grad, normed, up[0], down[0], hidden, activated],
        [VMEM_SPEC, VMEM_SPEC, part_spec(units, up[1]), part_spec(units, down[1])]
        + [VMEM_SPEC] * 2,
        [((2 * blocks, half_rows, D), low)],
        [
            pltpu.VMEM((units, count), low),
            pltpu.VMEM((2, blocks, 2, half_rows, D), low),
            pltpu.VMEM((2, blocks, half_rows, D), low),
            dma((2,)),
            dma((2,)),
        ],
        after,
        True,
    )


LINE_BLOCKS = 1
LINE_LAG = 3
LINE_SHARE = 4


class Line:
    def __init__(self, sources, share):
        self.groups = lax.axis_size("dp")
        self.sources, self.share = sources, share
        count = sum(size for _, _, size in sources)
        _, half_rows, _ = sources[0][0].shape
        self.half = (count, half_rows, D)
        self.chunks = count // LINE_BLOCKS
        self.operands = [array for array, _, _ in sources]
        self.in_specs = [pl.BlockSpec(memory_space=pl.ANY)] * len(sources)
        dma = pltpu.SemaphoreType.DMA
        out = (count, 2, half_rows, D) if share else self.half
        self.out_shape = jax.ShapeDtypeStruct(out, jnp.bfloat16)
        self.out_spec = pl.BlockSpec(memory_space=pl.ANY if share else pltpu.VMEM)
        self.scratch = [
            pltpu.VMEM(self.half, jnp.bfloat16),
            pltpu.VMEM((2,) + self.half, jnp.bfloat16),
            pltpu.VMEM((2,) + self.half, jnp.bfloat16),
            dma((len(sources),)),
            dma((2,)),
            dma((2, self.chunks)),
        ]
        if share:
            self.scratch += [pltpu.VMEM(self.half, jnp.bfloat16)] + [dma] * 3

    def bind(self, source_refs, out_ref, refs):
        self.source_refs, self.out = source_refs, out_ref
        self.own, self.came, self.going, self.own_sems, self.send_sems, self.recv_sems = refs[:6]
        self.total = out_ref
        if self.share:
            self.total, self.keep_sem, self.twin_send, self.twin_recv = refs[6:]
        self.done = 0
        self.group = lax.axis_index("dp")
        self.first = jnp.where(self.group < self.groups // 2, 0, 1)

    def at(self, chunk):
        return pl.ds(chunk * LINE_BLOCKS, LINE_BLOCKS)

    def comes(self, way):
        return jnp.where(way == 0, self.group > 0, self.group < self.groups - 1)

    def goes(self, way):
        return jnp.where(way == 0, self.group < self.groups - 1, self.group > 0)

    def copy(self, source, way, chunk):
        target = jnp.where(way == 0, self.group + 1, self.group - 1)
        return pltpu.make_async_remote_copy(
            src_ref=source,
            dst_ref=self.came.at[way, self.at(chunk)],
            send_sem=self.send_sems.at[way],
            recv_sem=self.recv_sems.at[way, chunk],
            device_id={"dp": target},
            device_id_type=MESH,
        )

    def load(self):
        self.loads, place = [], 0
        for index, (ref, (_, start, size)) in enumerate(zip(self.source_refs, self.sources)):
            copy = pltpu.make_async_copy(
                ref.at[pl.ds(start, size)], self.own.at[pl.ds(place, size)], self.own_sems.at[index]
            )
            copy.start()
            self.loads.append(copy)
            place += size

    def begin(self):
        for copy in self.loads:
            copy.wait()
        for way in range(2):

            @pl.when(jnp.logical_not(self.comes(way)))
            def _():
                self.came[way] = jnp.zeros(self.half, jnp.bfloat16)

                def start(chunk, carry):
                    self.copy(self.own.at[self.at(chunk)], way, chunk).start()
                    return carry

                lax.fori_loop(0, self.chunks, start, 0)

    def twin_copy(self, rows):
        side = lax.axis_index("seq")
        return pltpu.make_async_remote_copy(
            src_ref=self.total.at[rows],
            dst_ref=self.out.at[rows, side],
            send_sem=self.twin_send,
            recv_sem=self.twin_recv,
            device_id={"seq": 1 - side},
            device_id_type=MESH,
        )

    def keep_copy(self, rows):
        return pltpu.make_async_copy(
            self.total.at[rows], self.out.at[rows, lax.axis_index("seq")], self.keep_sem
        )

    def pass_on(self, way, chunk):
        rows = self.at(chunk)

        @pl.when(self.comes(way))
        def _():
            copy = self.copy(self.going.at[way, rows], way, chunk)
            copy.wait_recv()

            @pl.when(self.goes(way))
            def _():
                value = self.own[rows].astype(jnp.float32) + self.came[way, rows].astype(jnp.float32)
                self.going[way, rows] = value.astype(jnp.bfloat16)
                copy.start()

    def step(self, index):
        @pl.when(index < self.chunks)
        def _():
            self.pass_on(self.first, index)

        @pl.when(index >= LINE_LAG)
        def _():
            chunk = index - LINE_LAG
            rows = self.at(chunk)
            self.pass_on(1 - self.first, chunk)
            value = self.own[rows].astype(jnp.float32)
            value = value + self.came[0, rows].astype(jnp.float32)
            value = value + self.came[1, rows].astype(jnp.float32)
            self.total[rows] = value.astype(jnp.bfloat16)
            if self.share:

                @pl.when(lax.rem(chunk, LINE_SHARE) == LINE_SHARE - 1)
                def _():
                    done = pl.ds(chunk - (LINE_SHARE - 1), LINE_SHARE)
                    self.keep_copy(done).start()
                    self.twin_copy(done).start()

    def steps(self, count=None):
        last = self.chunks + LINE_LAG
        stop = last if count is None else min(self.done + count, last)

        def one(index, carry):
            self.step(index)
            return carry

        lax.fori_loop(self.done, stop, one, 0)
        self.done = stop

    def end(self):
        for way in range(2):

            @pl.when(self.goes(way))
            def _():
                whole_copy = pltpu.make_async_remote_copy(
                    src_ref=self.going.at[way],
                    dst_ref=self.came.at[way],
                    send_sem=self.send_sems.at[way],
                    recv_sem=self.recv_sems.at[way, 0],
                    device_id={"dp": self.group},
                    device_id_type=MESH,
                )
                whole_copy.wait_send()

        if self.share:
            everything = pl.ds(0, self.half[0])
            self.keep_copy(everything).wait()
            self.twin_copy(everything).wait()


def reduce_all(terms, collective_id, line=None, tail=None):
    _, tensors, groups, count, _ = terms.shape
    half = count // 2
    function, extras, scalars, outs = tail or (None, [], [], [])
    extra_specs = [VMEM_SPEC] * len(extras)
    extra_specs += [pl.BlockSpec(memory_space=pltpu.SMEM)] * len(scalars)
    extras = list(extras) + list(scalars)

    def kernel(*refs):
        refs = list(refs)
        terms_ref = refs.pop(0)
        source_refs = [refs.pop(0) for _ in line.operands] if line else []
        extra_refs = [refs.pop(0) for _ in extras]
        out_refs = [refs.pop(0) for _ in range(len(outs) or 1)]
        full = refs.pop(0) if tail else None
        joined_ref = refs.pop(0) if line else None
        tail_sems = [refs.pop(0) for _ in range(2)] if tail else None
        (
            near, own, mid, sums, mid_in, far, far_in,
            own_sems, near_send, near_recv, mid_send, mid_recv, far_send, far_recv,
        ) = refs[:14]
        if line:
            line.bind(source_refs, joined_ref, refs[14:])
            line.load()
        group, part, side = lax.axis_index("dp"), lax.axis_index("tensor"), lax.axis_index("seq")
        twin = 1 - side
        parts = others("tensor")
        order = others("dp") + [group]
        meet(
            [{"seq": twin}]
            + [{"tensor": peer} for peer in parts]
            + [{"dp": peer} for peer in order[:-1]]
        )
        waits, near_copies, own_copies = [], [], []
        for place, target in enumerate(order):
            near_copies.append(
                send(
                    terms_ref.at[twin, :, target],
                    near.at[place],
                    near_send.at[place],
                    near_recv.at[place],
                    {"seq": twin},
                )
            )
            copy = pltpu.make_async_copy(
                terms_ref.at[side, :, target], own.at[place], own_sems.at[place]
            )
            copy.start()
            own_copies.append(copy)
        if line:
            line.begin()
        beside = lax.rem(part + 1, 2) + part - lax.rem(part, 2)
        across = lax.rem(part + 2, 4)
        corner = 3 - part
        upper, lower = pl.ds(0, half), pl.ds(half, half)
        first_copies, second_copies = [], []

        def hand(place, index, source, target):
            return send(
                source,
                mid_in.at[place, index],
                mid_send.at[place, index],
                mid_recv.at[place, index],
                {"tensor": target},
            )

        for place in range(groups):
            near_copies[place].wait_recv()
            own_copies[place].wait()
            if line and place == 2:
                line.steps(1)
            for slot in range(tensors):
                mid[place, slot] = (
                    own[place, slot].astype(jnp.float32) + near[place, slot].astype(jnp.float32)
                ).astype(jnp.bfloat16)
            first_copies.append(
                [
                    hand(place, 0, mid.at[place, corner, upper], beside),
                    hand(place, 1, mid.at[place, corner, lower], across),
                    hand(place, 2, mid.at[place, beside, upper], beside),
                    hand(place, 3, mid.at[place, across, lower], across),
                ]
            )
        for place in range(groups):
            if line and place < 4:
                line.steps(3)
            copies = []
            for index, slot, rows, target in ((0, across, upper, across), (1, beside, lower, beside)):
                first_copies[place][index].wait_recv()
                value = mid[place, slot, rows].astype(jnp.float32)
                value = value + mid_in[place, index].astype(jnp.float32)
                sums[place, index] = value.astype(jnp.bfloat16)
                copies.append(hand(place, 4 + index, sums.at[place, index], target))
            second_copies.append(copies)
        far_copies = []
        for place, target in enumerate(order):
            copies = first_copies[place][2:] + second_copies[place]
            for copy in copies:
                copy.wait_recv()

            def joined(index):
                return mid_in[place, index].astype(jnp.float32)

            halves = [joined(2) + joined(4), joined(3) + joined(5)]
            total = mid[place, part].astype(jnp.float32) + jnp.concatenate(halves, axis=0)
            if place < groups - 1:
                far[place] = total.astype(jnp.bfloat16)
                far_copies.append(
                    send(
                        far.at[place],
                        far_in.at[place],
                        far_send.at[place],
                        far_recv.at[place],
                        {"dp": target},
                    )
                )
        if line:
            line.steps()
        for place, copy in enumerate(far_copies):
            copy.wait_recv()
            total = total + far_in[place].astype(jnp.float32)
        if tail:
            results = function(total, *extra_refs)
            for ref, value in zip(out_refs, results):
                ref[...] = value
            full[part] = results[len(outs)].astype(jnp.bfloat16)
            last_copies = [
                send(
                    full.at[part],
                    full.at[part],
                    tail_sems[0].at[step],
                    tail_sems[1].at[step],
                    {"tensor": peer},
                )
                for step, peer in enumerate(parts)
            ]
            for copy in last_copies:
                copy.wait()
        else:
            out_refs[0][...] = total
        for copy in near_copies + far_copies + [
            copy for row in first_copies + second_copies for copy in row
        ]:
            copy.wait_send()
        if line:
            line.end()

    block = (count, D)
    dma = pltpu.SemaphoreType.DMA
    results = [jax.ShapeDtypeStruct(*out) for out in outs]
    if tail:
        results.append(jax.ShapeDtypeStruct((tensors,) + block, jnp.bfloat16))
    else:
        results.append(jax.ShapeDtypeStruct(block, jnp.float32))
    return pl.pallas_call(
        kernel,
        name="reduce_all",
        out_shape=results + ([line.out_shape] if line else []),
        in_specs=[pl.BlockSpec(memory_space=pl.ANY)] + (line.in_specs if line else []) + extra_specs,
        out_specs=[VMEM_SPEC] * len(results) + ([line.out_spec] if line else []),
        scratch_shapes=[dma((tensors - 1,))] * (2 if tail else 0)
        + [pltpu.VMEM((groups, tensors) + block, jnp.bfloat16)] * 3
        + [
            pltpu.VMEM((groups, 2, half, D), jnp.bfloat16),
            pltpu.VMEM((groups, 6, half, D), jnp.bfloat16),
            pltpu.VMEM((groups,) + block, jnp.bfloat16),
            pltpu.VMEM((groups,) + block, jnp.bfloat16),
            dma((groups,)),
            dma((groups,)),
            dma((groups,)),
            dma((groups, 6)),
            dma((groups, 6)),
            dma((groups,)),
            dma((groups,)),
        ]
        + (line.scratch if line else []),
        cost_estimate=SHORT,
        compiler_params=pltpu.CompilerParams(
            collective_id=collective_id, has_side_effects=True, vmem_limit_bytes=56 << 20
        ),
    )(terms, *(line.operands if line else []), *extras)


def gather_all(block, collective_id, line=None):
    tensors, groups = lax.axis_size("tensor"), lax.axis_size("dp")
    half = block.shape[0] // 2

    def kernel(*refs):
        refs = list(refs)
        block_ref = refs.pop(0)
        source_refs = [refs.pop(0) for _ in line.operands] if line else []
        out = refs.pop(0)
        summed_ref = refs.pop(0) if line else None
        own_sem, far_send, far_recv, mid_send, mid_recv, near_send, near_recv = refs[:7]
        if line:
            line.bind(source_refs, summed_ref, refs[7:])
            line.load()
        group, part, side = lax.axis_index("dp"), lax.axis_index("tensor"), lax.axis_index("seq")
        twin = 1 - side
        meet(
            [{"seq": twin}]
            + [{"tensor": peer} for peer in others("tensor")]
            + [{"dp": peer} for peer in others("dp")]
        )
        far_copies = [
            send(
                block_ref,
                out.at[side, part, group],
                far_send.at[step],
                far_recv.at[step],
                {"dp": peer},
            )
            for step, peer in enumerate(others("dp"))
        ]
        own = pltpu.make_async_copy(block_ref, out.at[side, part, group], own_sem)
        own.start()
        if line:
            line.begin()
        beside = lax.rem(part + 1, 2) + part - lax.rem(part, 2)
        across = lax.rem(part + 2, 4)
        corner = 3 - part
        upper, lower = pl.ds(0, half), pl.ds(half, half)
        first_copies, second_copies, near_copies = [], [], []
        for place in range(groups):
            source = behind("dp", place)
            if place:
                far_copies[place - 1].wait_recv()
            held = out.at[side, part, source] if place else block_ref

            def hand(index, piece, slot, rows, target):
                return send(
                    piece,
                    out.at[side, slot, source, rows],
                    mid_send.at[place, index],
                    mid_recv.at[place, index],
                    {"tensor": target},
                )

            first = [
                hand(0, held.at[upper], part, upper, beside),
                hand(1, held.at[lower], part, lower, across),
                hand(2, held.at[lower], part, lower, beside),
                hand(3, held.at[upper], part, upper, across),
            ]
            near_copies.append(
                send(
                    held,
                    out.at[side, part, source],
                    near_send.at[place, 0],
                    near_recv.at[place, 0],
                    {"seq": twin},
                )
            )
            first[0].wait_recv()
            second = [hand(4, out.at[side, beside, source, upper], beside, upper, across)]
            first[1].wait_recv()
            second.append(hand(5, out.at[side, across, source, lower], across, lower, beside))
            first_copies.append(first)
            second_copies.append(second)
        for place in range(groups):
            if line and place < 4:
                line.steps(2)
            source = behind("dp", place)
            ready = [
                (beside, first_copies[place][2:3]),
                (across, first_copies[place][3:4]),
                (corner, second_copies[place]),
            ]
            for step, (slot, copies) in enumerate(ready):
                for copy in copies:
                    copy.wait_recv()
                held = out.at[side, slot, source]
                near_copies.append(
                    send(
                        held,
                        held,
                        near_send.at[place, step + 1],
                        near_recv.at[place, step + 1],
                        {"seq": twin},
                    )
                )
        if line:
            line.steps()
        for copy in near_copies:
            copy.wait_recv()
        for copy in near_copies + far_copies + [
            copy for row in first_copies + second_copies for copy in row
        ]:
            copy.wait_send()
        own.wait()
        if line:
            line.end()

    dma = pltpu.SemaphoreType.DMA
    anywhere = pl.BlockSpec(memory_space=pl.ANY)
    return pl.pallas_call(
        kernel,
        name="gather_all",
        out_shape=[jax.ShapeDtypeStruct((2, tensors, groups) + block.shape, block.dtype)]
        + ([line.out_shape] if line else []),
        in_specs=[VMEM_SPEC] + (line.in_specs if line else []),
        out_specs=[pl.BlockSpec(memory_space=pltpu.HBM)] + ([line.out_spec] if line else []),
        scratch_shapes=[
            dma,
            dma((groups - 1,)),
            dma((groups - 1,)),
            dma((groups, 6)),
            dma((groups, 6)),
            dma((groups, tensors)),
            dma((groups, tensors)),
        ]
        + (line.scratch if line else []),
        cost_estimate=SHORT,
        compiler_params=pltpu.CompilerParams(
            collective_id=collective_id, has_side_effects=True, vmem_limit_bytes=60 << 20
        ),
    )(block, *(line.operands if line else []))


def reduce_rows(name, terms, ids, line, function, extras, scalars, outs):
    count, groups = terms.shape[3], terms.shape[2]
    pieces = max(1, groups // 4)
    if pieces == 1:
        return reduce_all(terms, ids[0], line, (function, extras, scalars, outs))
    part = count // pieces
    sums, joined = [], []
    for i in range(pieces):
        piece = terms[:, :, :, i * part : (i + 1) * part]
        total, *joined_now = reduce_all(piece, ids[1 if i and line else 0], None if i else line)
        sums.append(total)
        joined += joined_now
    total = jnp.concatenate(sums, axis=0)
    results = tensor_step(
        name,
        lambda _, total_ref, *refs: function(total_ref, *refs),
        None,
        [total] + list(extras),
        scalars,
        outs,
        True,
        ids[2],
    )
    return list(results) + joined


def plane_steps(tensors):
    return [(step, turn_by) for step in range(tensors) for turn_by in range(2)][1:]


def plane_peers(steps):
    count, part = lax.axis_size("tensor"), lax.axis_index("tensor")
    side = lax.axis_index("seq")
    return [
        (lax.rem(part + step, count), lax.rem(side + turn_by, 2)) for step, turn_by in steps
    ]


def join_stats(stats, collective_id):
    _, tensors, groups, _, _ = stats.shape

    def join(left, right):
        top = jnp.maximum(left[..., 0:1, :], right[..., 0:1, :])
        total = left[..., 1:2, :] * jnp.exp(left[..., 0:1, :] - top) + right[..., 1:2, :] * jnp.exp(
            right[..., 0:1, :] - top
        )
        return jnp.concatenate(
            [top, total, left[..., 2:3, :] + right[..., 2:3, :], left[..., 3:, :]], axis=-2
        )

    plane = plane_steps(tensors)

    def kernel(
        stats_ref, home, full, mid_in, far, far_in, mid_send, mid_recv, far_send, far_recv
    ):
        group, part, side = lax.axis_index("dp"), lax.axis_index("tensor"), lax.axis_index("seq")
        peers, groups_else = plane_peers(plane), others("dp")
        meet(
            [{"tensor": peer, "seq": other} for peer, other in peers]
            + [{"dp": peer} for peer in groups_else]
        )
        copies = [
            send(
                stats_ref.at[other, peer],
                mid_in.at[step],
                mid_send.at[0, step],
                mid_recv.at[0, step],
                {"tensor": peer, "seq": other},
            )
            for step, (peer, other) in enumerate(peers)
        ]
        for copy in copies:
            copy.wait()
        for spot in range(groups):
            total = stats_ref[side, part, spot]
            for step in range(len(plane)):
                total = join(total, mid_in[step, spot])
            far[spot] = total
        copies = [
            send(far.at[peer], far_in.at[step], far_send.at[0, step], far_recv.at[0, step], {"dp": peer})
            for step, peer in enumerate(groups_else)
        ]
        total = far[group]
        for step, copy in enumerate(copies):
            copy.wait()
            total = join(total, far_in[step])
        log_total = total[0:1] + jnp.log(total[1:2])
        home[...] = jnp.concatenate([log_total, total[2:3], total[2:]], axis=0)
        full[side, part, group] = jnp.broadcast_to(log_total, (8, LANES))
        held = full.at[side, part, group]
        copies = [
            send(held, held, far_send.at[1, step], far_recv.at[1, step], {"dp": peer})
            for step, peer in enumerate(groups_else)
        ]
        for copy in copies:
            copy.wait()
        held = full.at[side, part]
        copies = [
            send(
                held,
                held,
                mid_send.at[1, step],
                mid_recv.at[1, step],
                {"tensor": peer, "seq": other},
            )
            for step, (peer, other) in enumerate(peers)
        ]
        for copy in copies:
            copy.wait()

    tile = (8, LANES)
    dma = pltpu.SemaphoreType.DMA
    vmem = pl.BlockSpec(memory_space=pltpu.VMEM)
    return pl.pallas_call(
        kernel,
        name="join_stats",
        out_shape=[
            jax.ShapeDtypeStruct(tile, jnp.float32),
            jax.ShapeDtypeStruct(stats.shape, jnp.float32),
        ],
        in_specs=[vmem],
        out_specs=[vmem, vmem],
        scratch_shapes=[
            pltpu.VMEM((len(plane), groups) + tile, jnp.float32),
            pltpu.VMEM((groups,) + tile, jnp.float32),
            pltpu.VMEM((groups - 1,) + tile, jnp.float32),
            dma((2, len(plane))),
            dma((2, len(plane))),
            dma((2, groups - 1)),
            dma((2, groups - 1)),
        ],
        cost_estimate=SHORT,
        compiler_params=pltpu.CompilerParams(collective_id=collective_id, has_side_effects=True),
    )(stats)


def spread_tokens(block, slot_block, ends, blocks, half_rows, collective_id):
    tensors, groups = lax.axis_size("tensor"), lax.axis_size("dp")
    rows = 2 * tensors * groups
    width = ends.shape[1]
    vocab_rows = VOCAB // tensors
    slots = slot_block.shape[0]

    def kernel(
        block_ref, slot_ref, ends_ref, ids, targets, kept, places, plan, count,
        held, firsts, own_sem, send_sems, recv_sems,
    ):
        group, side = lax.axis_index("dp"), lax.axis_index("seq")
        first_id = lax.axis_index("tensor") * vocab_rows
        peers = [
            {"dp": lax.rem(group + step // 2, groups), "seq": lax.rem(side + step % 2, 2)}
            for step in range(1, 2 * groups)
        ]
        meet(peers)
        copies = [
            send(block_ref, held.at[group, side], send_sems.at[step], recv_sems.at[step], peer)
            for step, peer in enumerate(peers)
        ]
        own = pltpu.make_async_copy(block_ref, held.at[group, side], own_sem)
        own.start()
        own.wait()
        for copy in copies:
            copy.wait()
        lane = lax.broadcasted_iota(jnp.int32, (1, LANES), 1)
        slot_ids = lax.broadcasted_iota(jnp.int32, (slots, LANES), 0)
        slot_blocks = jnp.broadcast_to(slot_ref[...], (slots, LANES))
        total = jnp.zeros((1, LANES), jnp.int32)
        hits = jnp.zeros((1, LANES), jnp.float32)
        for half in range(2):
            for source in range(groups):
                limit = held[source, half, 2 * tensors : 2 * tensors + 1, :]
                total = total + limit
                for part in range(tensors):
                    row = (half * tensors + part) * groups + source
                    token = held[source, half, part : part + 1, :]
                    ids[row] = token
                    targets[row] = held[source, half, tensors + part : tensors + part + 1, :]
                    kept[row] = jnp.where(lane + part * LANES < limit, 1.0, 0.0)
                    firsts[row : row + 1, :] = jnp.where(part * LANES < limit, 1.0, 0.0)
                    local = token - first_id
                    inside = (local >= 0) & (local < vocab_rows)
                    local = jnp.where(inside, local, 0).astype(jnp.float32)
                    block_of = jnp.floor((local + 0.5) * (0.5 / half_rows))
                    within = local - block_of * (2.0 * half_rows)
                    lower = within >= half_rows
                    inside = inside & (jnp.where(lower, 1, 0) == side)
                    within = (within - jnp.where(lower, 1.0 * half_rows, 0.0)).astype(jnp.int32)
                    same = slot_blocks == block_of.astype(jnp.int32) + blocks
                    slot = jnp.sum(jnp.where(same, slot_ids + 1, 0), axis=0, keepdims=True) - 1
                    inside = inside & (slot >= 0)
                    places[row] = jnp.where(inside, slot * half_rows + within, -1)
                    hits = hits + jnp.where(inside, 1.0, 0.0)
        count[...] = total.astype(jnp.float32)
        shape = (rows, width)
        active = jnp.concatenate([firsts[...]] * (width // LANES), axis=1)
        square = (rows, rows)
        above = jnp.where(
            lax.broadcasted_iota(jnp.int32, square, 1) < lax.broadcasted_iota(jnp.int32, square, 0),
            1.0,
            0.0,
        )
        earlier = times(above.astype(jnp.bfloat16), active.astype(jnp.bfloat16))
        number = jnp.sum(active, axis=0, keepdims=True)
        index = lax.broadcasted_iota(jnp.int32, shape, 0).astype(jnp.float32)
        turns = jnp.where(active > 0.0, earlier, number + index - earlier)
        spot = lax.broadcasted_iota(jnp.int32, shape, 1).astype(jnp.float32) - PLAN_GROUPS
        order = jnp.sum(jnp.where(turns == spot, index, 0.0), axis=0, keepdims=True)
        spot = lax.broadcasted_iota(jnp.int32, (1, width), 1)
        order = jnp.where(spot == 2, number, order)
        order = jnp.where(spot == 3, jnp.sum(hits, axis=1, keepdims=True), order)
        plan[...] = jnp.where(spot < 2, ends_ref[...], order.astype(jnp.int32))

    dma = pltpu.SemaphoreType.DMA
    vmem = pl.BlockSpec(memory_space=pltpu.VMEM)
    shape = (rows, 1, LANES)
    return pl.pallas_call(
        kernel,
        name="spread_tokens",
        out_shape=[
            jax.ShapeDtypeStruct(shape, jnp.int32),
            jax.ShapeDtypeStruct(shape, jnp.int32),
            jax.ShapeDtypeStruct(shape, jnp.float32),
            jax.ShapeDtypeStruct(shape, jnp.int32),
            jax.ShapeDtypeStruct((1, width), jnp.int32),
            jax.ShapeDtypeStruct((1, LANES), jnp.float32),
        ],
        in_specs=[vmem] * 3,
        out_specs=[vmem] * 6,
        scratch_shapes=[
            pltpu.VMEM((groups, 2) + block.shape, jnp.int32),
            pltpu.VMEM((rows, LANES), jnp.float32),
            dma,
            dma((2 * groups - 1,)),
            dma((2 * groups - 1,)),
        ],
        cost_estimate=SHORT,
        compiler_params=pltpu.CompilerParams(collective_id=collective_id, has_side_effects=True),
    )(block, slot_block, ends)


def finish(gain_grads, states, grad_ys, home, keep, table_squares, count, smalls, collective_id):
    tensors, groups = lax.axis_size("tensor"), lax.axis_size("dp")
    block = (8, D)
    plane = plane_steps(tensors)
    gain_rows = 2 * LAYERS + 1
    operands = list(gain_grads) + list(states) + list(grad_ys) + [
        home, keep, table_squares, count
    ] + list(smalls)

    def kernel(*refs):
        refs = list(refs)
        gain_refs = [refs.pop(0) for _ in gain_grads]
        state_refs = [refs.pop(0) for _ in states]
        grad_refs = [refs.pop(0) for _ in grad_ys]
        home_ref, keep_ref, table_ref, count_ref = [refs.pop(0) for _ in range(4)]
        small_refs = [refs.pop(0) for _ in smalls]
        out_refs = [refs.pop(0) for _ in range(8)]
        mid, far, mid_send, mid_recv, far_send, far_recv = refs
        group, part, side = lax.axis_index("dp"), lax.axis_index("tensor"), lax.axis_index("seq")
        peers, groups_else = plane_peers(plane), others("dp")
        meet(
            [{"tensor": peer, "seq": other} for peer, other in peers]
            + [{"dp": peer} for peer in groups_else]
        )
        values = []
        for later in range(1, LAYERS + 1):
            grad = grad_refs[later - 1][...]
            for level in range(later + 1):
                values.append(jnp.sum(grad * state_refs[level][...], keepdims=True))
        loss = jnp.where(keep_ref[...] > 0.0, home_ref[0:1, :] - home_ref[1:2, :], 0.0)
        values.append(jnp.sum(loss, keepdims=True))
        values.append(jnp.sum(table_ref[...], keepdims=True))
        lane = lax.broadcasted_iota(jnp.int32, (1, D), 1)
        row = jnp.zeros((1, D), jnp.float32)
        for place, value in enumerate(values):
            row = jnp.where(lane == place, value, row)
        blank = jnp.zeros((8 - gain_rows - 1, D), jnp.float32)
        total = jnp.concatenate([ref[...] for ref in gain_refs] + [row, blank], axis=0)
        stages = [
            (
                mid,
                2 * part + side,
                [{"tensor": peer, "seq": other} for peer, other in peers],
                mid_send,
                mid_recv,
            ),
            (far, group, [{"dp": peer} for peer in groups_else], far_send, far_recv),
        ]
        for slots, me, targets, send_sems, recv_sems in stages:
            slots[me] = total
            copies = [
                send(slots.at[me], slots.at[me], send_sems.at[step], recv_sems.at[step], target)
                for step, target in enumerate(targets)
            ]
            for copy in copies:
                copy.wait()
            total = slots[0]
            for index in range(1, slots.shape[0]):
                total = total + slots[index]
        gain_total = total[:gain_rows]
        row = total[gain_rows : gain_rows + 1]

        def pick(place):
            return jnp.sum(jnp.where(lane == place, row, 0.0), axis=1, keepdims=True)

        mix_squares = jnp.sum(jnp.where(lane < MIX_WEIGHTS, row * row, 0.0), axis=1, keepdims=True)
        gain_squares = jnp.sum(gain_total * gain_total, keepdims=True)
        tokens = count_ref[:, 0:1]
        clip_norm = jnp.sqrt(pick(MIX_WEIGHTS + 1) + gain_squares + mix_squares) / tokens
        factor = jnp.minimum(1.0, CLIP_NORM / clip_norm) / tokens
        gain_news = adam_update(
            *[ref[...] for ref in small_refs[:3]], gain_total * factor, RATE_SMALL, 0.0
        )
        mix_news = adam_update(
            *[ref[...] for ref in small_refs[3:]], row[:, :MIX_WEIGHTS] * factor, RATE_SMALL, 0.0
        )
        for ref, value in zip(out_refs[:6], gain_news + mix_news):
            ref[...] = value
        ends = jnp.where(lane == 0, pick(MIX_WEIGHTS), jnp.where(lane == 1, clip_norm, factor))
        out_refs[6][...] = ends[:, :LANES]
        out_refs[7][...] = jnp.broadcast_to(factor, (8, LANES))

    dma = pltpu.SemaphoreType.DMA
    vmem = pl.BlockSpec(memory_space=pltpu.VMEM)
    return pl.pallas_call(
        kernel,
        name="finish",
        out_shape=[jax.ShapeDtypeStruct(value.shape, jnp.float32) for value in smalls]
        + [
            jax.ShapeDtypeStruct((1, LANES), jnp.float32),
            jax.ShapeDtypeStruct((8, LANES), jnp.float32),
        ],
        in_specs=[vmem] * len(operands),
        out_specs=[vmem] * 8,
        scratch_shapes=[
            pltpu.VMEM((2 * tensors,) + block, jnp.float32),
            pltpu.VMEM((groups,) + block, jnp.float32),
            dma((len(plane),)),
            dma((len(plane),)),
            dma((groups - 1,)),
            dma((groups - 1,)),
        ],
        cost_estimate=SHORT,
        compiler_params=pltpu.CompilerParams(collective_id=collective_id, has_side_effects=True),
    )(*operands)


SLOT_STEP = 8
PREPARE_STEP = 20


def prepare(slot_block, first_id, master, blocks):
    slots, half_rows, _ = master.shape
    total = slot_block.shape[0]
    steps = -(-total // PREPARE_STEP)
    spare = steps * PREPARE_STEP - total
    slot_block = jnp.pad(slot_block, (0, spare), constant_values=-1)
    slot_block = jnp.concatenate([slot_block, first_id[None]])
    rows = PREPARE_STEP * half_rows

    def kernel(plan_ref, master_ref, table_ref, halves_ref, ids_ref):
        @pl.when(pl.program_id(0) == 0)
        def _():
            halves_ref[...] = jnp.zeros_like(halves_ref)

        for place in range(PREPARE_STEP):
            slot = pl.program_id(0) * PREPARE_STEP + place
            value = jnp.where(slot < slots, master_ref[place], 0.0).astype(jnp.bfloat16)
            table_ref[place * half_rows : (place + 1) * half_rows, :] = value

            block = plan_ref[slot]
            ids = plan_ref[steps * PREPARE_STEP] + (block - blocks) * (2 * half_rows)
            ids = ids + lax.broadcasted_iota(jnp.int32, (half_rows, 1), 0)
            ids_ref[place * half_rows : (place + 1) * half_rows, :] = jnp.where(
                block >= blocks, ids, -1
            )

            @pl.when((block >= 0) & (block < blocks))
            def _():
                halves_ref[block] = value

    last = (slots - 1) // PREPARE_STEP
    return pl.pallas_call(
        kernel,
        name="prepare",
        grid_spec=pltpu.PrefetchScalarGridSpec(
            num_scalar_prefetch=1,
            grid=(steps,),
            in_specs=[
                pl.BlockSpec(
                    (PREPARE_STEP, half_rows, D), lambda step, plan: (jnp.minimum(step, last), 0, 0)
                )
            ],
            out_specs=[
                pl.BlockSpec((rows, D), lambda step, plan: (step, 0)),
                pl.BlockSpec((blocks, half_rows, D), lambda step, plan: (0, 0, 0)),
                pl.BlockSpec((rows, 1), lambda step, plan: (step, 0)),
            ],
        ),
        out_shape=[
            jax.ShapeDtypeStruct((total * half_rows, D), jnp.bfloat16),
            jax.ShapeDtypeStruct((blocks, half_rows, D), jnp.bfloat16),
            jax.ShapeDtypeStruct((total * half_rows, 1), jnp.int32),
        ],
        cost_estimate=SHORT,
        compiler_params=pltpu.CompilerParams(vmem_limit_bytes=60 << 20),
    )(slot_block, master)


TILE = TILE_GROUPS * LANES
PICKED = 768


def row_of(values_ref, groups, place=0):
    rows = [values_ref[group, place : place + 1, :] for group in groups]
    return jnp.concatenate(rows, axis=1)


def tile_row(values_ref, tile):
    start = tile * TILE_GROUPS
    return row_of(values_ref, [start + place for place in range(TILE_GROUPS)])


PLAN_GROUPS = 4


def chunk_of(plan_ref, step):
    return pl.ds(pl.multiple_of(plan_ref[0] + step * ROW_STEP, 16), ROW_STEP)


def chunks_of(plan_ref):
    return (plan_ref[1] - plan_ref[0] + ROW_STEP - 1) // ROW_STEP


def whole(shape):
    return pl.BlockSpec(shape, lambda step, plan: (0,) * len(shape), pipeline_mode=pl.Buffered(1))


def last_tile(plan):
    return (plan[2] - 1) // TILE_GROUPS


def group_specs():
    return [
        pl.BlockSpec(
            (LANES, D),
            lambda step, plan, place=place: (
                plan[PLAN_GROUPS + jnp.minimum(step, last_tile(plan)) * TILE_GROUPS + place],
                0,
            ),
        )
        for place in range(TILE_GROUPS)
    ]


def powers_spec(rows):
    return pl.BlockSpec((rows, TILE), lambda step, plan: (0, jnp.minimum(step, last_tile(plan))))


def groups_of(plan_ref):
    start = PLAN_GROUPS + pl.program_id(0) * TILE_GROUPS
    return [plan_ref[start + place] for place in range(TILE_GROUPS)]


ROWS_SPEC = pl.BlockSpec((TILE, D), lambda step, plan: (step, 0))


def local_call(name, kernel, steps, plan, operands, in_specs, out_shape, out_specs, scratch):
    return pl.pallas_call(
        kernel,
        name=name,
        grid_spec=pltpu.PrefetchScalarGridSpec(
            num_scalar_prefetch=1,
            grid=(steps,),
            in_specs=in_specs,
            out_specs=out_specs,
            scratch_shapes=scratch,
        ),
        out_shape=out_shape,
        cost_estimate=SHORT,
        compiler_params=pltpu.CompilerParams(vmem_limit_bytes=60 << 20),
    )(plan, *operands)


def ones_where(condition):
    return jnp.where(condition, 1.0, 0.0).astype(jnp.bfloat16)


def picks(rank_row):
    return ones_where(lax.broadcasted_iota(jnp.int32, (PICKED, TILE), 0) == rank_row)


def rows_picked(plan_ref, step, place_row):
    start = plan_ref[0] + step * ROW_STEP
    row = lax.broadcasted_iota(jnp.int32, (ROW_STEP, PICKED), 0) + start
    return ones_where(row == place_row)


def look_up(plan, row_ids, tokens, places, table):
    rows, groups = table.shape[0], tokens.shape[0]
    steps = groups // TILE_GROUPS

    def kernel(
        plan_ref, ids_ref, tokens_ref, places_ref, table_ref, out_ref, ranks_ref, picked_ref, acc, picked
    ):
        tile = pl.program_id(0)
        few = plan_ref[3] <= PICKED

        @pl.when(tile == 0)
        def _():
            held = places_ref[...].reshape(groups, LANES) >= 0
            ones = ones_where(held)
            lane = (LANES, LANES)
            before = ones_where(
                lax.broadcasted_iota(jnp.int32, lane, 0) < lax.broadcasted_iota(jnp.int32, lane, 1)
            )
            group = (groups, groups)
            above = ones_where(
                lax.broadcasted_iota(jnp.int32, group, 1) < lax.broadcasted_iota(jnp.int32, group, 0)
            )
            totals = jnp.sum(ones.astype(jnp.float32), axis=1, keepdims=True)
            totals = jnp.broadcast_to(totals, (groups, LANES)).astype(jnp.bfloat16)
            ranks = (times(ones, before) + times(above, totals)).astype(jnp.int32)
            ranks_ref[...] = jnp.where(held, ranks, -1).reshape(groups, 1, LANES)

        @pl.when((tile == 0) & few)
        def _():
            def digits_of(step, total):
                place = tile_row(places_ref, step)
                high = lax.shift_right_arithmetic(place, 6)
                digits = jnp.concatenate([high, place - high * 64] * 4, axis=0)
                digits = digits.astype(jnp.float32).astype(jnp.bfloat16)
                return total + contract_last(digits, picks(tile_row(ranks_ref, step)))

            digits = lax.fori_loop(0, steps, digits_of, jnp.zeros((8, PICKED), jnp.float32))
            place = (digits[0:1] * 64.0 + digits[1:2]).astype(jnp.int32)
            index = lax.broadcasted_iota(jnp.int32, (1, PICKED), 1)
            place = jnp.where(index < plan_ref[3], place, -1)
            picked_ref[...] = jnp.broadcast_to(place, (8, PICKED))
            acc[:PICKED, :] = jnp.zeros((PICKED, D), jnp.float32)

            def one(step, carry):
                hits = rows_picked(plan_ref, step, place)
                acc[:PICKED, :] += contract_first(hits, table_ref[chunk_of(plan_ref, step), :])
                return carry

            lax.fori_loop(0, chunks_of(plan_ref), one, 0)
            picked[...] = acc[:PICKED, :].astype(jnp.bfloat16)

        @pl.when(few)
        def _():
            hits = picks(tile_row(ranks_ref, tile))
            out_ref[...] = contract_first(hits, picked[...]).astype(jnp.bfloat16)

        @pl.when(jnp.logical_not(few))
        def _():
            acc[...] = jnp.zeros_like(acc)
            wanted = tile_row(tokens_ref, tile)

            def one(step, carry):
                chunk = chunk_of(plan_ref, step)
                hits = ones_where(ids_ref[chunk, :] == wanted)
                acc[...] += contract_first(hits, table_ref[chunk, :])
                return carry

            lax.fori_loop(0, chunks_of(plan_ref), one, 0)
            out_ref[...] = acc[...].astype(jnp.bfloat16)

    lanes = (groups, 1, LANES)
    return local_call(
        "look_up",
        kernel,
        steps,
        plan,
        (row_ids, tokens, places, table),
        [whole((rows, 1)), whole(lanes), whole(lanes), whole((rows, D))],
        [
            jax.ShapeDtypeStruct((groups * LANES, D), jnp.bfloat16),
            jax.ShapeDtypeStruct(lanes, jnp.int32),
            jax.ShapeDtypeStruct((8, PICKED), jnp.int32),
        ],
        [ROWS_SPEC, whole(lanes), whole((8, PICKED))],
        [pltpu.VMEM((TILE, D), jnp.float32), pltpu.VMEM((PICKED, D), jnp.bfloat16)],
    )


def head_forward(plan, row_ids, labels, table, final):
    rows, groups = table.shape[0], labels.shape[0]
    steps = groups // TILE_GROUPS

    def kernel(plan_ref, ids_ref, labels_ref, table_ref, *rest):
        final_refs, (powers_ref, stats_ref, scores, hidden) = rest[:TILE_GROUPS], rest[TILE_GROUPS:]
        blank = jnp.zeros((1, TILE), jnp.float32)
        active = pl.program_id(0) <= last_tile(plan_ref)
        own = groups_of(plan_ref)

        def put(top, total, target):
            pad = jnp.zeros((5, LANES), jnp.float32)
            for place in range(TILE_GROUPS):
                lanes = slice(place * LANES, (place + 1) * LANES)
                stats_ref[own[place]] = jnp.concatenate(
                    [top[:, lanes], total[:, lanes], target[:, lanes], pad], axis=0
                )

        @pl.when(jnp.logical_not(active))
        def _():
            put(blank - 1e30, blank, blank)

        @pl.when(active)
        def _():
            wanted = row_of(labels_ref, own)
            for place, ref in enumerate(final_refs):
                hidden[place * LANES : (place + 1) * LANES, :] = ref[...]

            def first(step, carry):
                top, target = carry
                chunk = chunk_of(plan_ref, step)
                ids = ids_ref[chunk, :]
                raw = contract_last(table_ref[chunk, :], hidden[...])
                raw = jnp.where(ids >= 0, raw, -1e30)
                scores[chunk, :] = raw
                top = jnp.maximum(top, jnp.max(raw, axis=0, keepdims=True))
                target = target + jnp.sum(
                    jnp.where(ids == wanted, raw, 0.0), axis=0, keepdims=True
                )
                return (top, target)

            top, target = lax.fori_loop(0, chunks_of(plan_ref), first, (blank - 1e30, blank))

            def second(step, total):
                chunk = chunk_of(plan_ref, step)
                powers = jnp.exp(scores[chunk, :] - top)
                powers_ref[chunk, :] = powers.astype(jnp.bfloat16)
                return total + jnp.sum(powers, axis=0, keepdims=True)

            put(top, lax.fori_loop(0, chunks_of(plan_ref), second, blank), target)

    return local_call(
        "head_forward",
        kernel,
        steps,
        plan,
        (row_ids, labels, table) + (final,) * TILE_GROUPS,
        [whole((rows, 1)), whole((groups, 1, LANES)), whole((rows, D))] + group_specs(),
        [
            jax.ShapeDtypeStruct((rows, groups * LANES), jnp.bfloat16),
            jax.ShapeDtypeStruct((groups, 8, LANES), jnp.float32),
        ],
        [powers_spec(rows), whole((groups, 8, LANES))],
        [pltpu.VMEM((rows, TILE), jnp.float32), pltpu.VMEM((TILE, D), jnp.bfloat16)],
    )


def head_backward(plan, row_ids, labels, keep, stats, log_totals, table, final, powers):
    rows, groups = table.shape[0], labels.shape[0]
    steps = groups // TILE_GROUPS

    def kernel(plan_ref, ids_ref, labels_ref, keep_ref, stats_ref, logs_ref, table_ref, powers_ref, *rest):
        final_refs = rest[:TILE_GROUPS]
        grad_final_ref, grad_table_ref, acc, hidden, low, sems = rest[TILE_GROUPS:]
        tile = pl.program_id(0)
        slot = lax.rem(tile, 2)
        active = tile <= last_tile(plan_ref)

        def copies(step):
            start, side = PLAN_GROUPS + step * TILE_GROUPS, lax.rem(step, 2)
            return [
                pltpu.make_async_copy(
                    low.at[side, place],
                    grad_final_ref.at[plan_ref[start + place]],
                    sems.at[side, place],
                )
                for place in range(TILE_GROUPS)
            ]

        @pl.when(tile == 0)
        def _():
            grad_table_ref[...] = jnp.zeros_like(grad_table_ref)

        @pl.when(tile >= 2)
        def _():
            for copy in copies(tile - 2):
                copy.wait()

        acc[...] = jnp.zeros_like(acc)

        @pl.when(active)
        def _():
            own = groups_of(plan_ref)
            wanted, kept = row_of(labels_ref, own), row_of(keep_ref, own)
            tops = row_of(stats_ref, own)
            scale = jnp.exp(tops - row_of(logs_ref, own)) * kept
            for place, ref in enumerate(final_refs):
                hidden[place * LANES : (place + 1) * LANES, :] = ref[...]

            def one(step, carry):
                chunk = chunk_of(plan_ref, step)
                grads = powers_ref[chunk, :].astype(jnp.float32) * scale
                grads = grads - jnp.where(ids_ref[chunk, :] == wanted, kept, 0.0)
                grads = grads.astype(jnp.bfloat16)
                grad_table_ref[chunk, :] += times(grads, hidden[...])
                acc[...] += contract_first(grads, table_ref[chunk, :])
                return carry

            lax.fori_loop(0, chunks_of(plan_ref), one, 0)

        low[slot] = acc[...].astype(jnp.bfloat16).reshape(TILE_GROUPS, LANES, D)
        for copy in copies(tile):
            copy.start()

        @pl.when(tile == steps - 1)
        def _():
            for step in range(max(0, steps - 2), steps):
                for copy in copies(step):
                    copy.wait()

    lanes = (groups, 1, LANES)
    return local_call(
        "head_backward",
        kernel,
        steps,
        plan,
        (row_ids, labels, keep, stats, log_totals, table, powers) + (final,) * TILE_GROUPS,
        [
            whole((rows, 1)),
            whole(lanes),
            whole(lanes),
            whole((groups, 8, LANES)),
            whole((groups, 8, LANES)),
            whole((rows, D)),
            powers_spec(rows),
        ]
        + group_specs(),
        [
            jax.ShapeDtypeStruct((groups, LANES, D), jnp.bfloat16),
            jax.ShapeDtypeStruct((rows, D), jnp.float32),
        ],
        [pl.BlockSpec(memory_space=pl.ANY), whole((rows, D))],
        [
            pltpu.VMEM((TILE, D), jnp.float32),
            pltpu.VMEM((TILE, D), jnp.bfloat16),
            pltpu.VMEM((2, TILE_GROUPS, LANES, D), jnp.bfloat16),
            pltpu.SemaphoreType.DMA((2, TILE_GROUPS)),
        ],
    )


def look_back(
    plan, slot_plan, slots, row_ids, tokens, ranks, picked, grad_start, grad_table, layer_grads
):
    rows, groups = grad_table.shape[0], tokens.shape[0]
    steps = groups // TILE_GROUPS
    half_rows = layer_grads[0].shape[1]
    block = SLOT_STEP * half_rows
    kinds = len(layer_grads)

    def kernel(plan_ref, slot_ref, ids_ref, tokens_ref, ranks_ref, picked_ref, grad_ref, table_ref, *rest):
        layer_refs = rest[:kinds]
        slots_ref, squares_ref, acc, held, out_ref = rest[kinds:]
        step = pl.program_id(0)
        few = plan_ref[3] <= PICKED

        @pl.when(step == 0)
        def _():
            acc[...] = jnp.zeros_like(acc)
            squares_ref[...] = jnp.zeros_like(squares_ref)

        @pl.when((step < steps) & few)
        def _():
            acc[...] += times(picks(tile_row(ranks_ref, step)), grad_ref[...])

        @pl.when((step < steps) & jnp.logical_not(few))
        def _():
            held[step] = grad_ref[...]

        @pl.when(step >= steps)
        def _():
            start = (step - steps) * block

            @pl.when(few)
            def _():
                row = lax.broadcasted_iota(jnp.int32, (block, PICKED), 0) + start
                hits = ones_where(row == picked_ref[0:1, :])
                out_ref[...] = table_ref[...] + times(hits, acc[...].astype(jnp.bfloat16))

            @pl.when(jnp.logical_not(few))
            def _():
                out_ref[...] = table_ref[...]
                ids = ids_ref[pl.ds(pl.multiple_of(start, 16), block), :]

                def one(tile, carry):
                    hits = ones_where(ids == tile_row(tokens_ref, tile))
                    out_ref[...] += times(hits, held[tile])
                    return carry

                lax.fori_loop(0, steps, one, 0)

            for place in range(SLOT_STEP):
                slot = (step - steps) * SLOT_STEP + place
                kind = slot_ref[0, slot]
                part = slice(place * half_rows, (place + 1) * half_rows)

                for index in range(kinds):

                    @pl.when(kind == index)
                    def _():
                        layer = layer_refs[index][slot_ref[1 + index, slot]]
                        out_ref[part, :] = layer.astype(jnp.float32)

                @pl.when(kind < 0)
                def _():
                    out_ref[part, :] = jnp.zeros((half_rows, D), jnp.float32)

                slots_ref[place] = out_ref[part, :].astype(jnp.bfloat16)

            values = out_ref[...]
            squares_ref[...] += (values * values).reshape(block // 8, 8, D).sum(axis=0)

    def fixed(shape):
        return pl.BlockSpec(
            shape, lambda step, plan, slot: (0,) * len(shape), pipeline_mode=pl.Buffered(1)
        )

    lanes = (groups, 1, LANES)
    row_spec = pl.BlockSpec((block, D), lambda step, plan, slot: (jnp.maximum(step - steps, 0), 0))
    return pl.pallas_call(
        kernel,
        name="look_back",
        grid_spec=pltpu.PrefetchScalarGridSpec(
            num_scalar_prefetch=2,
            grid=(steps + -(-slots // SLOT_STEP),),
            in_specs=[
                fixed((rows, 1)),
                fixed(lanes),
                fixed(lanes),
                fixed((8, PICKED)),
                pl.BlockSpec((TILE, D), lambda step, plan, slot: (jnp.minimum(step, steps - 1), 0)),
                row_spec,
            ]
            + [fixed(grads.shape) for grads in layer_grads],
            out_specs=[
                pl.BlockSpec(
                    (SLOT_STEP, half_rows, D),
                    lambda step, plan, slot: (jnp.maximum(step - steps, 0), 0, 0),
                ),
                fixed((8, D)),
            ],
            scratch_shapes=[
                pltpu.VMEM((PICKED, D), jnp.float32),
                pltpu.VMEM((steps, TILE, D), jnp.bfloat16),
                pltpu.VMEM((block, D), jnp.float32),
            ],
        ),
        out_shape=[
            jax.ShapeDtypeStruct((slots, half_rows, D), jnp.bfloat16),
            jax.ShapeDtypeStruct((8, D), jnp.float32),
        ],
        cost_estimate=SHORT,
        compiler_params=pltpu.CompilerParams(vmem_limit_bytes=60 << 20),
    )(
        plan,
        slot_plan,
        row_ids,
        tokens,
        ranks,
        picked,
        grad_start,
        grad_table,
        *layer_grads,
    )


def grads_home(level):
    return [(2 * level, 0), (2 * level + 1, 0), (2 * level + 1, 1)]


def body(
    token_ids,
    labels,
    real_counts,
    owners,
    master,
    first_moment,
    second_moment,
    gains,
    gains_first,
    gains_second,
    mix,
    mix_first,
    mix_second,
):
    tensors = lax.axis_size("tensor")
    groups = lax.axis_size("dp")
    group = lax.axis_index("dp")
    tensor_part = lax.axis_index("tensor")
    seq_part = lax.axis_index("seq")
    slots, half_rows, _ = master.shape
    seq_count, half_len = token_ids.shape
    row_count = seq_count * half_len
    share = row_count // tensors
    head_rows = 3 * D // tensors
    out_rows = D // tensors
    unit_rows = FF // tensors
    layer_rows = head_rows + out_rows + 2 * unit_rows
    layer_blocks = layer_rows // (2 * half_rows)
    blocks = LAYERS * layer_blocks
    vocab_rows = VOCAB // tensors
    local_heads = HEADS // tensors

    slot_rank = slot_table(owners)
    block_ids = jnp.arange(owners.shape[0], dtype=jnp.int32)
    mine = owners == group
    match = (jnp.arange(slots)[:, None] == slot_rank[None, :]) & mine[None, :]
    slot_block = jnp.sum(jnp.where(match, block_ids[None, :] + 1, 0), axis=1) - 1
    spare = -(-ROW_STEP // half_rows)
    spare += -(slots + spare) % SLOT_STEP
    held = jnp.sum(jnp.where(mine, 1, 0)) * half_rows
    first_held = jnp.sum(jnp.where(mine & (block_ids < blocks), 1, 0)) * half_rows
    slot_block_all = jnp.pad(slot_block, (0, spare), constant_values=-1).astype(jnp.int32)
    third = layer_blocks // 3
    which, within = slot_block_all // third, slot_block_all % third
    homes = [home for level in range(LAYERS) for home in grads_home(level)]
    arrays = 1 + max(array for array, _ in homes)
    kind, index = jnp.full(which.shape, -1), jnp.zeros_like(which)
    for place, (array, part) in enumerate(homes):
        kind = jnp.where(which == place, array, kind)
        index = jnp.where(which == place, within + part * third, index)
    kind = jnp.where(slot_block_all >= blocks, arrays, jnp.where(slot_block_all < 0, -1, kind))
    slot_plan = jnp.stack(
        [kind] + [jnp.where(kind == array, index, 0) for array in range(arrays)]
    ).astype(jnp.int32)

    packed = jnp.concatenate(
        [
            token_ids.reshape(tensors, LANES),
            labels.reshape(tensors, LANES),
            jnp.broadcast_to(real_counts[:, None], (16 - 2 * tensors, LANES)),
        ],
        axis=0,
    )
    width = -(-(2 * tensors * groups + PLAN_GROUPS) // LANES) * LANES
    lane = jnp.arange(width)[None, :]
    ends = jnp.where(lane == 0, first_held, jnp.where(lane == 1, held, 0)).astype(jnp.int32)
    ids_all, labels_all, keep_all, places, plan, count = spread_tokens(
        packed, slot_block_all[:, None], ends, blocks, half_rows, 15
    )
    plan = plan.reshape(-1)
    order = (2, tensors, groups, share)

    first_id = (tensor_part * vocab_rows + seq_part * half_rows).astype(jnp.int32)
    table, halves, row_ids = prepare(slot_block_all, first_id, master, blocks)

    def weights_line(*starts):
        return Line([(halves, start * third, third) for start in starts], True)

    def as_table(joined):
        return joined.reshape(-1, D)

    positions = seq_part * half_len + jnp.arange(row_count) % half_len
    steps_half = jnp.arange(HEAD_DIM // 2).astype(jnp.float32)
    freqs = 10000.0 ** (-2.0 * steps_half / HEAD_DIM)
    angles = freqs[:, None] * positions.astype(jnp.float32)[None, :]
    cosine, sine = jnp.cos(angles), jnp.sin(angles)

    looked, ranks, picked = look_up(plan, row_ids, ids_all, places, table)
    looked = looked.reshape(order + (D,))
    gain = [gains[i : i + 1] for i in range(2 * LAYERS + 1)]
    piece = ((share, D), jnp.float32)

    def normed_of(total, gain_row):
        return (total[...], layer_norm_parts(total[...])[0] * gain_row[...])

    def inner_of(total, stream, gain_row):
        inner = stream + total
        return (inner, layer_norm_parts(inner)[0] * gain_row)

    def outcome_of(base, total, inner, gain_row, *rest):
        states, scalars = rest[:-1], rest[-1]
        outcome = inner + total
        stream = scalars[base + len(states)] * outcome
        for source, state in enumerate(states):
            stream = stream + scalars[base + source] * state
        return (outcome, stream, layer_norm_parts(stream)[0] * gain_row)

    start, normed, joined = reduce_rows(
        "normed", looked, (14, 18, 1), weights_line(0, 1), normed_of, [gain[0]], [], [piece]
    )
    table_one = as_table(joined)
    attention_table, up = table_one, (table_one, 1)
    tables = []
    states, streams, inners, kept_all = [start], [start], [], []
    for level in range(LAYERS):
        here, last = 3 * level, level == LAYERS - 1
        carried = [] if last else [here + 3]
        carried += [here + 1, here + 2] if level else [here + 2]
        inner, normed_two, queries, both, logs, attended, joined = tensor_step(
            f"inner_{level}",
            inner_of,
            attention_work(normed, attention_table, cosine, sine),
            (streams[level], gain[2 * level + 1]),
            (),
            [piece],
            True,
            2 if level == 0 else 15 + level,
            weights_line(*carried),
        )
        kept = (queries, both, logs, attended)
        joined = as_table(joined)
        down = (joined, len(carried) - 1)
        up = (joined, len(carried) - 2) if level else up
        tables.append((attention_table, up, down))
        attention_table = joined
        outcome, stream, normed_next, hidden, activated = tensor_step(
            f"outcome_{level}",
            partial(outcome_of, (level + 1) * (level + 2) // 2 - 1),
            unit_work(normed_two, up, down),
            [inner, gain[2 * level + 2]] + states,
            (mix,),
            [piece, piece] + ([((share, D), jnp.bfloat16)] if last else []),
            not last,
            3 + level,
        )
        inners.append(inner)
        kept_all.append((normed, kept, normed_two, (hidden, activated)))
        states.append(outcome)
        streams.append(stream)
        normed = normed_next

    final_all = gather_all(normed, 3 + LAYERS)[0].reshape(-1, D)
    powers, stats = head_forward(plan, row_ids, labels_all, table, final_all)
    home, log_totals = join_stats(
        stats.reshape((2, tensors, groups, 8, LANES)), 4 + LAYERS
    )
    grad_final, grad_table = head_backward(
        plan,
        row_ids,
        labels_all,
        keep_all,
        stats,
        log_totals.reshape(-1, 8, LANES),
        table,
        final_all,
        powers,
    )
    grad_final = grad_final.reshape(order + (D,))

    row = ((1, D), jnp.float32)

    def top_of(total, stream, gain_row, scalars):
        grad_top, grad_gain = norm_pull(total[...], gain_row[...], stream[...])
        grad_state = scalars[MIX_WEIGHTS - 1] * grad_top
        return (grad_top, grad_state, grad_gain, grad_state)

    def inner_back(total, grad_out, inner, gain_row):
        grad, grad_gain = norm_pull(total, gain_row, inner)
        grad = grad_out + grad
        return (grad, grad_gain, grad)

    def stream_back(block, total, grad_inner, stream, gain_row, *rest):
        grad_ys, scalars = rest[:-1], rest[-1]
        grad, grad_gain = norm_pull(total, gain_row, stream)
        grad = grad_inner + grad
        state = grad if block == 0 else scalars[block * (block + 1) // 2 - 1 + block] * grad
        for offset, grad_y in enumerate(grad_ys):
            later = block + 1 + offset
            state = state + scalars[later * (later + 1) // 2 - 1 + block] * grad_y
        return (grad, state, grad_gain, state)

    grad_ys = [None] * (LAYERS + 1)
    gain_grads = [None] * (2 * LAYERS + 1)
    layer_grads, attention_grads = [None] * (2 * LAYERS), None
    grad_ys[LAYERS], grad_state, gain_grads[2 * LAYERS], grad_branch = reduce_rows(
        "top_back",
        grad_final,
        (0, 0, 5 + LAYERS),
        None,
        top_of,
        [streams[LAYERS], gain[2 * LAYERS]],
        [mix],
        [piece, piece, row],
    )
    for level in reversed(range(LAYERS)):
        normed, kept, normed_two, unit_kept = kept_all[level]
        attention_table, up, down = tables[level]
        grad_inner, gain_grads[2 * level + 1], grad_attn, unit_grads, *summed = tensor_step(
            f"inner_back_{level}",
            inner_back,
            unit_back_work(grad_branch, normed_two, up, down, unit_kept, half_rows),
            (grad_state, inners[level], gain[2 * level + 1]),
            (),
            [piece, row],
            True,
            6 + LAYERS if level == 0 else 19 + level,
            None if attention_grads is None else Line([(attention_grads, 0, third)], False),
        )
        if summed:
            layer_grads[2 * (level + 1)] = summed[0]
        grad_ys[level], grad_state, gain_grads[2 * level], grad_branch, attention_grads, summed = (
            tensor_step(
                f"stream_back_{level}",
                partial(stream_back, level),
                attention_back_work(
                    grad_attn, normed, attention_table, kept, cosine, sine, half_rows
                ),
                [grad_inner, streams[level], gain[2 * level]] + grad_ys[level + 1 :],
                (mix,),
                [piece, piece, row] + ([] if level else [((share, D), jnp.bfloat16)]),
                level > 0,
                7 + LAYERS + level,
                Line([(unit_grads, 0, 2 * third)], False),
            )
        )
        layer_grads[2 * level + 1] = summed

    grad_start_all, layer_grads[0] = gather_all(
        grad_branch, 13, Line([(attention_grads, 0, third)], False)
    )
    grad_start_all = grad_start_all.reshape(-1, D)
    owned, table_squares = look_back(
        plan,
        slot_plan,
        slots,
        row_ids,
        ids_all,
        ranks,
        picked,
        grad_start_all,
        grad_table,
        layer_grads,
    )
    keep = jnp.where(
        tensor_part * share + jnp.arange(share) < real_counts[0], 1.0, 0.0
    ).astype(jnp.float32)
    news = finish(
        gain_grads,
        states,
        grad_ys[1:],
        home,
        keep[None],
        table_squares,
        count,
        (gains, gains_first, gains_second, mix[None], mix_first[None], mix_second[None]),
        7 + 2 * LAYERS,
    )
    new_gains, new_gains_first, new_gains_second = news[:3]
    new_mix, new_mix_first, new_mix_second = [value[0] for value in news[3:6]]
    loss_sum, clip_norm = news[6][0, 0], news[6][0, 1]
    token_count = count[0, 0]
    owned = owned.astype(jnp.float32) * news[7][0, 0]
    new_master, new_first, new_second = adam_update(
        master, first_moment, second_moment, owned, RATE_MATRIX, DECAY_MATRIX
    )
    return (
        new_master,
        new_first,
        new_second,
        new_gains,
        new_gains_first,
        new_gains_second,
        new_mix,
        new_mix_first,
        new_mix_second,
        loss_sum,
        token_count,
        clip_norm,
    )


def solution(mesh):
    return jax.shard_map(
        body,
        mesh=mesh,
        in_specs=(
            P("dp", "seq"),
            P("dp", "seq"),
            P(("dp", "seq")),
            P(),
            P("dp", ("tensor", "seq"), None),
            P("dp", ("tensor", "seq"), None),
            P("dp", ("tensor", "seq"), None),
            P(),
            P(),
            P(),
            P(),
            P(),
            P(),
        ),
        out_specs=(
            P("dp", ("tensor", "seq"), None),
            P("dp", ("tensor", "seq"), None),
            P("dp", ("tensor", "seq"), None),
            P(),
            P(),
            P(),
            P(),
            P(),
            P(),
            P(),
            P(),
            P(),
        ),
        check_vma=False,
    )
```

```python
from functools import partial

import jax
import jax.numpy as jnp
from jax import lax
from jax.experimental import pallas as pl
from jax.experimental.pallas import tpu as pltpu
from jax.sharding import PartitionSpec as P

D = 768
HEADS = 12
HEAD_DIM = 64
FF = 3072
VOCAB = 50304
LAYERS = 2
STEP_COUNT = 10
MIX_WEIGHTS = 5


EPS_NORM = 1e-05
CLIP_NORM = 0.01
BETA_ONE = 0.9
BETA_TWO = 0.95
ADAM_EPS = 1e-08
RATE_MATRIX = 0.04
RATE_SMALL = 0.4
DECAY_MATRIX = 0.1


def contract_last(left, right):
    return lax.dot_general(
        left, right, (((1,), (1,)), ((), ())), preferred_element_type=jnp.float32
    )


def contract_first(left, right):
    return lax.dot_general(
        left, right, (((0,), (0,)), ((), ())), preferred_element_type=jnp.float32
    )


def slot_table(owners):
    ranks = jnp.arange(owners.shape[0])
    same = (owners[None, :] == owners[:, None]) & (ranks[None, :] < ranks[:, None])
    return jnp.sum(jnp.where(same, 1, 0), axis=1).astype(jnp.int32)


def adam_update(weight, first, second, grad, rate, decay):
    first = BETA_ONE * first + (1.0 - BETA_ONE) * grad
    second = BETA_TWO * second + (1.0 - BETA_TWO) * grad * grad
    first_hat = first / (1.0 - BETA_ONE**STEP_COUNT)
    second_hat = second / (1.0 - BETA_TWO**STEP_COUNT)
    weight = weight - rate * (first_hat / (jnp.sqrt(second_hat) + ADAM_EPS) + decay * weight)
    return (weight, first, second)


MESH = pl.DeviceIdType.MESH
ROW_STEP = 400
TILE_GROUPS = 8
LANES = 128
SHORT = pl.CostEstimate(flops=1000, bytes_accessed=1000, transcendentals=0)


def meet(peers):
    gate = pltpu.get_barrier_semaphore()
    for peer in peers:
        pl.semaphore_signal(gate, inc=1, device_id=peer, device_id_type=MESH)
    pl.semaphore_wait(gate, len(peers))


def others(axis):
    count, me = lax.axis_size(axis), lax.axis_index(axis)
    return [lax.rem(me + step, count) for step in range(1, count)]


def behind(axis, step):
    count, me = lax.axis_size(axis), lax.axis_index(axis)
    return lax.rem(me + count - step, count)


def send(source, target, send_sem, recv_sem, device):
    copy = pltpu.make_async_remote_copy(
        src_ref=source,
        dst_ref=target,
        send_sem=send_sem,
        recv_sem=recv_sem,
        device_id=device,
        device_id_type=MESH,
    )
    copy.start()
    return copy


def layer_norm_parts(stream):
    center = stream - jnp.mean(stream, -1, keepdims=True)
    inverse = lax.rsqrt(jnp.mean(center * center, -1, keepdims=True) + EPS_NORM)
    return center * inverse, inverse


def norm_pull(grad_normed, gain, stream):
    scaled, inverse = layer_norm_parts(stream)
    grad_scaled = grad_normed * gain
    grad_stream = inverse * (
        grad_scaled
        - jnp.mean(grad_scaled, -1, keepdims=True)
        - scaled * jnp.mean(grad_scaled * scaled, -1, keepdims=True)
    )
    return grad_stream, jnp.sum(grad_normed * scaled, axis=0, keepdims=True)


class Work:
    def __init__(self, before, during, operands, specs, outs, scratch, after=None, twins=False):
        self.before, self.during, self.after, self.twins = before, during, after, twins
        self.operands, self.specs, self.outs, self.scratch = operands, specs, outs, scratch


def tensor_step(name, function, work, extras, scalars, outs, gather, collective_id, line=None):
    parts = lax.axis_size("tensor")
    share = extras[0].shape[0]
    reduce = work is not None
    work = work or Work(None, None, [], [], [], [])
    arrays = list(work.operands) + list(extras)
    parts_of = list(work.specs) + [None] * len(extras)

    def kernel(*refs):
        refs = list(refs)

        def take(count):
            return [refs.pop(0) for _ in range(count)]

        array_refs = take(len(arrays))
        scalar_refs = take(len(scalars))
        source_refs = take(len(line.operands)) if line else []
        out_refs = take(len(outs))
        (full,) = take(1) if gather else [None]
        work_outs = take(len(work.outs))
        (joined,) = take(1) if line else [None]
        held = take(len(arrays))
        (load_sems,) = take(1)
        loads = []
        for index, (ref, part, target) in enumerate(zip(array_refs, parts_of, held)):
            if part:
                ref = ref.at[pl.ds(part[0] * part[1], part[0])]
            loads.append(pltpu.make_async_copy(ref, target, load_sems.at[index]))
            loads[-1].start()
        work_refs, extra_refs = held[: len(work.operands)], held[len(work.operands) :]
        send_sems, recv_sems = take(2)
        partial_ref, outgoing, arrived = take(3) if reduce else [None] * 3
        if line:
            line.bind(source_refs, joined, take(len(line.scratch)))
            line.load()

        def tick(count=1):
            if line:
                line.steps(count)

        me, side = lax.axis_index("tensor"), lax.axis_index("seq")
        peers = others("tensor")
        twin = {"seq": 1 - side}
        twins = work.twins or (line and line.share)
        meet(
            [{"tensor": peer} for peer in peers]
            + [twin] * bool(twins)
            + ([{"dp": peer} for peer in others("dp")] if line else [])
        )
        if line:
            line.begin()
        for load in loads:
            load.wait()
        total = None
        if reduce:
            work.before(work_refs, work_outs, refs, partial_ref, tick)
            copies = []
            for step, peer in enumerate(peers):
                rows = pl.ds(pl.multiple_of(peer * share, share), share)
                outgoing[step] = partial_ref[rows, :].astype(jnp.bfloat16)
                copies.append(
                    send(
                        outgoing.at[step],
                        arrived.at[step],
                        send_sems.at[0, step],
                        recv_sems.at[0, step],
                        {"tensor": peer},
                    )
                )
            if work.during:
                work.during(work_refs, work_outs, refs)
            tick(6)
            total = partial_ref[pl.ds(pl.multiple_of(me * share, share), share), :]
            for step, copy in enumerate(copies):
                copy.wait()
                total = total + arrived[step].astype(jnp.float32)
        results = function(total, *[ref[...] for ref in extra_refs], *scalar_refs)
        for ref, value in zip(out_refs, results):
            ref[...] = value.astype(ref.dtype)
        if gather:
            full[me] = results[len(outs)].astype(jnp.bfloat16)
            copies = [
                send(
                    full.at[me],
                    full.at[me],
                    send_sems.at[1, step],
                    recv_sems.at[1, step],
                    {"tensor": peer},
                )
                for step, peer in enumerate(peers)
            ]
        if work.after:
            work.after(work_refs, work_outs, refs)
        tick(None)
        if gather:
            for copy in copies:
                copy.wait()
        if line:
            line.end()

    vmem = pl.BlockSpec(memory_space=pltpu.VMEM)
    smem = pl.BlockSpec(memory_space=pltpu.SMEM)
    shapes = [jax.ShapeDtypeStruct(shape, dtype) for shape, dtype in outs]
    if gather:
        shapes.append(jax.ShapeDtypeStruct((parts, share, D), jnp.bfloat16))
    shapes += [jax.ShapeDtypeStruct(shape, dtype) for shape, dtype in work.outs]
    out_specs = [vmem] * len(shapes)
    operands = arrays + list(scalars)
    in_specs = [pl.BlockSpec(memory_space=pl.ANY)] * len(arrays) + [smem] * len(scalars)
    dma = pltpu.SemaphoreType.DMA
    buffers = [
        pltpu.VMEM((part[0], D) if part else array.shape, array.dtype)
        for array, part in zip(arrays, parts_of)
    ]
    buffers += [dma((len(arrays),))] + [dma((2, parts - 1))] * 2
    if reduce:
        buffers += [pltpu.VMEM((parts * share, D), jnp.float32)]
        buffers += [pltpu.VMEM((parts - 1, share, D), jnp.bfloat16)] * 2
    if line:
        operands += line.operands
        in_specs += line.in_specs
        shapes.append(line.out_shape)
        out_specs.append(line.out_spec)
        buffers += line.scratch
    return pl.pallas_call(
        kernel,
        name=name,
        grid=(1,),
        out_shape=shapes,
        in_specs=in_specs,
        out_specs=out_specs,
        scratch_shapes=buffers + list(work.scratch),
        cost_estimate=SHORT,
        compiler_params=pltpu.CompilerParams(
            collective_id=collective_id, has_side_effects=True, vmem_limit_bytes=60 << 20
        ),
    )(*operands)


VMEM_SPEC = pl.BlockSpec(memory_space=pltpu.VMEM)


def part_spec(rows, index):
    return rows, index


def turn(block, cosine, sine):
    half = HEAD_DIM // 2
    first, second = block[:half], block[half:]
    return jnp.concatenate(
        [first * cosine - second * sine, second * cosine + first * sine], axis=0
    )


def times(left, right):
    return jnp.dot(left, right, preferred_element_type=jnp.float32)


def masks_of(count, side):
    key = lax.broadcasted_iota(jnp.int32, (count, count), 0)
    query = lax.broadcasted_iota(jnp.int32, (count, count), 1)
    far = jnp.where(side == 0, -1e30, 0.0).astype(jnp.float32)
    return far, jnp.where(key <= query, 0.0, -1e30)


def scores_of(keys_values, head, queries, masks):
    span = slice(head * HEAD_DIM, (head + 1) * HEAD_DIM)
    scale = HEAD_DIM ** (-0.5)
    far = contract_first(keys_values[0, 0, span, :], queries) * scale + masks[0]
    own = contract_first(keys_values[1, 0, span, :], queries) * scale + masks[1]
    return far, own


def attention_work(normed, table, cosine, sine):
    parts, share, _ = normed.shape
    count = parts * share
    width = D // parts
    heads = width // HEAD_DIM

    def before(ins, outs, scratch, partial_ref, tick):
        normed_ref, qkv_ref, out_ref, cosine_ref, sine_ref = ins
        queries_ref, both, logs_ref, attended_ref = outs
        send_sem, recv_sem = scratch
        side = lax.axis_index("seq")
        cosine, sine = cosine_ref[...], sine_ref[...]
        rows = normed_ref[...].reshape(count, D)
        joined = contract_last(qkv_ref[...], rows)
        for head in range(heads):
            span = slice(head * HEAD_DIM, (head + 1) * HEAD_DIM)
            keys = joined[width + head * HEAD_DIM : width + (head + 1) * HEAD_DIM]
            both[1, 0, span, :] = turn(keys, cosine, sine).astype(jnp.bfloat16)
        both[1, 1] = joined[2 * width :].astype(jnp.bfloat16)
        copy = pltpu.make_async_remote_copy(
            src_ref=both.at[1],
            dst_ref=both.at[0],
            send_sem=send_sem,
            recv_sem=recv_sem,
            device_id={"seq": 1 - side},
            device_id_type=MESH,
        )

        copy.start()
        for head in range(heads):
            span = slice(head * HEAD_DIM, (head + 1) * HEAD_DIM)
            queries_ref[span, :] = turn(joined[span], cosine, sine).astype(jnp.bfloat16)

        copy.wait()
        masks = masks_of(count, side)
        for head in range(heads):
            span = slice(head * HEAD_DIM, (head + 1) * HEAD_DIM)
            far, own = scores_of(both, head, queries_ref[span, :], masks)
            peak = jnp.maximum(
                jnp.max(far, axis=0, keepdims=True), jnp.max(own, axis=0, keepdims=True)
            )
            far, own = jnp.exp(far - peak), jnp.exp(own - peak)
            total = jnp.sum(far, axis=0, keepdims=True) + jnp.sum(own, axis=0, keepdims=True)
            logs_ref[head] = peak + jnp.log(total)
            inverse = 1.0 / total
            attended = times(both[0, 1, span, :], (far * inverse).astype(jnp.bfloat16))
            attended += times(both[1, 1, span, :], (own * inverse).astype(jnp.bfloat16))
            attended_ref[span, :] = attended.astype(jnp.bfloat16)
            tick(2)
        partial_ref[...] = contract_first(attended_ref[...], out_ref[...])

    low = jnp.bfloat16
    return Work(
        before,
        None,
        [normed, table, table, cosine, sine],
        [None, part_spec(3 * width, 0), part_spec(width, 3), None, None],
        [
            ((width, count), low),
            ((2, 2, width, count), low),
            ((heads, 1, count), jnp.float32),
            ((width, count), low),
        ],
        [pltpu.SemaphoreType.DMA, pltpu.SemaphoreType.DMA],
        twins=True,
    )


def fold_copy(own, near, send_sems, recv_sems, index):
    side = lax.axis_index("seq")
    return pltpu.make_async_remote_copy(
        src_ref=own.at[index, :, 1 - side],
        dst_ref=near.at[index],
        send_sem=send_sems.at[index],
        recv_sem=recv_sems.at[index],
        device_id={"seq": 1 - side},
        device_id_type=MESH,
    )


def add_halves(own, near, out, start):
    side = lax.axis_index("seq")

    def one(block, carry):
        value = own[block, side].astype(jnp.float32) + near[block].astype(jnp.float32)
        out[start + block] = value.astype(jnp.bfloat16)
        return carry

    lax.fori_loop(0, near.shape[0], one, 0)


def attention_back_work(grad, normed, table, kept, cosine, sine, half_rows):
    parts, share, _ = normed.shape
    count = parts * share
    width = D // parts
    heads = width // HEAD_DIM
    queries, both, logs, attended = kept
    blocks = 4 * width // (2 * half_rows)

    def before(ins, outs, scratch, partial_ref, tick):
        grad_ref, _, qkv_ref, out_ref, queries_ref, both, logs_ref, _, cosine_ref, sine_ref = ins
        back, came, grad_joined, send_sem, recv_sem = scratch[:5]
        side = lax.axis_index("seq")
        cosine, sine = cosine_ref[...], -sine_ref[...]
        scale = HEAD_DIM ** (-0.5)
        grads = contract_last(out_ref[...], grad_ref[...].reshape(count, D)).astype(jnp.bfloat16)
        own_grads = []
        masks = masks_of(count, side)
        for head in range(heads):
            span = slice(head * HEAD_DIM, (head + 1) * HEAD_DIM)
            head_queries, head_grads = queries_ref[span, :], grads[span]
            far, own = scores_of(both, head, head_queries, masks)
            far, own = jnp.exp(far - logs_ref[head]), jnp.exp(own - logs_ref[head])
            far_grad = contract_first(both[0, 1, span, :], head_grads)
            own_grad = contract_first(both[1, 1, span, :], head_grads)
            mean = jnp.sum(far * far_grad, axis=0, keepdims=True)
            mean += jnp.sum(own * own_grad, axis=0, keepdims=True)
            far_grad = (far * (far_grad - mean)).astype(jnp.bfloat16)
            own_grad = (own * (own_grad - mean)).astype(jnp.bfloat16)
            far, own = far.astype(jnp.bfloat16), own.astype(jnp.bfloat16)
            back[0, span, :] = (contract_last(head_queries, far_grad) * scale).astype(jnp.bfloat16)
            back[1, span, :] = contract_last(head_grads, far).astype(jnp.bfloat16)
            query_grad = times(both[0, 0, span, :], far_grad) + times(both[1, 0, span, :], own_grad)
            grad_joined[span, :] = turn(query_grad * scale, cosine, sine).astype(jnp.bfloat16)
            own_grads.append(
                (contract_last(head_queries, own_grad) * scale, contract_last(head_grads, own))
            )
            tick(2)
        copy = send(back, came, send_sem, recv_sem, {"seq": 1 - side})
        copy.wait()
        for head, (key_grad, value_grad) in enumerate(own_grads):
            span = slice(head * HEAD_DIM, (head + 1) * HEAD_DIM)
            key_grad = key_grad + came[0, span, :].astype(jnp.float32)
            value_grad = value_grad + came[1, span, :].astype(jnp.float32)
            start = width + head * HEAD_DIM
            grad_joined[start : start + HEAD_DIM, :] = turn(key_grad, cosine, sine).astype(
                jnp.bfloat16
            )
            start += width
            grad_joined[start : start + HEAD_DIM, :] = value_grad.astype(jnp.bfloat16)
        partial_ref[...] = contract_first(grad_joined[...], qkv_ref[...])

    def during(ins, outs, scratch):
        grad_ref, normed_ref, attended_ref = ins[0], ins[1], ins[7]
        grad_joined = scratch[2]
        own, near, fold_send, fold_recv = scratch[5:]
        value = times(grad_joined[...], normed_ref[...].reshape(count, D)).astype(jnp.bfloat16)
        part = 3 * blocks // 4
        own[0, :part] = value.reshape(part, 2, half_rows, D)
        value = times(attended_ref[...], grad_ref[...].reshape(count, D)).astype(jnp.bfloat16)
        own[0, part:] = value.reshape(blocks - part, 2, half_rows, D)
        fold_copy(own, near, fold_send, fold_recv, 0).start()

    def after(ins, outs, scratch):
        own, near, fold_send, fold_recv = scratch[5:]
        fold_copy(own, near, fold_send, fold_recv, 0).wait()
        add_halves(own.at[0], near.at[0], outs[0], 0)

    low = jnp.bfloat16
    dma = pltpu.SemaphoreType.DMA
    return Work(
        before,
        during,
        [grad, normed, table, table, queries, both, logs, attended, cosine, sine],
        [None, None, part_spec(3 * width, 0), part_spec(width, 3)] + [None] * 6,
        [((blocks, half_rows, D), low)],
        [
            pltpu.VMEM((2, width, count), low),
            pltpu.VMEM((2, width, count), low),
            pltpu.VMEM((3 * width, count), low),
            dma,
            dma,
            pltpu.VMEM((1, blocks, 2, half_rows, D), low),
            pltpu.VMEM((1, blocks, half_rows, D), low),
            dma((1,)),
            dma((1,)),
        ],
        after,
        True,
    )


def gelu(hidden):
    return jax.nn.gelu(hidden, approximate=True)


def unit_work(normed, up, down):
    parts, share, _ = normed.shape
    count = parts * share
    units = FF // parts

    def before(ins, outs, scratch, partial_ref, tick):
        normed_ref, up_ref, down_ref = ins
        hidden_ref, activated_ref = outs
        hidden = contract_last(up_ref[...], normed_ref[...].reshape(count, D))
        hidden_ref[...] = hidden
        activated_ref[...] = gelu(hidden).astype(jnp.bfloat16)
        tick(2)
        partial_ref[...] = contract_first(activated_ref[...], down_ref[...])

    return Work(
        before,
        None,
        [normed, up[0], down[0]],
        [None, part_spec(units, up[1]), part_spec(units, down[1])],
        [((units, count), jnp.float32), ((units, count), jnp.bfloat16)],
        [],
    )


def unit_back_work(grad, normed, up, down, kept, half_rows):
    parts, share, _ = normed.shape
    count = parts * share
    units = FF // parts
    hidden, activated = kept
    blocks = units // (2 * half_rows)

    def before(ins, outs, scratch, partial_ref, tick):
        grad_ref, _, up_ref, down_ref, hidden_ref, _ = ins
        grad_hidden = scratch[0]
        grad_act = contract_last(down_ref[...], grad_ref[...].reshape(count, D))
        _, pull = jax.vjp(gelu, hidden_ref[...])
        grad_hidden[...] = pull(grad_act)[0].astype(jnp.bfloat16)
        tick(2)
        partial_ref[...] = contract_first(grad_hidden[...], up_ref[...])

    def during(ins, outs, scratch):
        grad_ref, normed_ref, _, _, _, activated_ref = ins
        grad_hidden, own, near, fold_send, fold_recv = scratch
        value = times(grad_hidden[...], normed_ref[...].reshape(count, D))
        own[0] = value.astype(jnp.bfloat16).reshape(own.shape[1:])
        fold_copy(own, near, fold_send, fold_recv, 0).start()
        value = times(activated_ref[...], grad_ref[...].reshape(count, D))
        own[1] = value.astype(jnp.bfloat16).reshape(own.shape[1:])
        fold_copy(own, near, fold_send, fold_recv, 1).start()

    def after(ins, outs, scratch):
        _, own, near, fold_send, fold_recv = scratch
        for index in range(2):
            fold_copy(own, near, fold_send, fold_recv, index).wait()
            add_halves(own.at[index], near.at[index], outs[0], index * blocks)

    low, dma = jnp.bfloat16, pltpu.SemaphoreType.DMA
    return Work(
        before,
        during,
        [grad, normed, up[0], down[0], hidden, activated],
        [None, None, part_spec(units, up[1]), part_spec(units, down[1])]
        + [None] * 2,
        [((2 * blocks, half_rows, D), low)],
        [
            pltpu.VMEM((units, count), low),
            pltpu.VMEM((2, blocks, 2, half_rows, D), low),
            pltpu.VMEM((2, blocks, half_rows, D), low),
            dma((2,)),
            dma((2,)),
        ],
        after,
        True,
    )


LINE_BLOCKS = 1
LINE_LAG = 3
LINE_SHARE = 4


class Line:
    def __init__(self, sources, share):
        self.groups = lax.axis_size("dp")
        self.sources, self.share = sources, share
        count = sum(size for _, _, size in sources)
        _, half_rows, _ = sources[0][0].shape
        self.half = (count, half_rows, D)
        self.chunks = count // LINE_BLOCKS
        self.operands = [array for array, _, _ in sources]
        self.in_specs = [pl.BlockSpec(memory_space=pl.ANY)] * len(sources)
        dma = pltpu.SemaphoreType.DMA
        out = (count, 2, half_rows, D) if share else self.half
        self.out_shape = jax.ShapeDtypeStruct(out, jnp.bfloat16)
        self.out_spec = pl.BlockSpec(memory_space=pl.ANY if share else pltpu.VMEM)
        self.scratch = [
            pltpu.VMEM(self.half, jnp.bfloat16),
            pltpu.VMEM((2,) + self.half, jnp.bfloat16),
            pltpu.VMEM((2,) + self.half, jnp.bfloat16),
            dma((len(sources),)),
            dma((2,)),
            dma((2, self.chunks)),
        ]
        if share:
            self.scratch += [pltpu.VMEM(self.half, jnp.bfloat16)] + [dma] * 3

    def bind(self, source_refs, out_ref, refs):
        self.source_refs, self.out = source_refs, out_ref
        self.own, self.came, self.going, self.own_sems, self.send_sems, self.recv_sems = refs[:6]
        self.total = out_ref
        if self.share:
            self.total, self.keep_sem, self.twin_send, self.twin_recv = refs[6:]
        self.done = 0
        self.group = lax.axis_index("dp")
        self.first = jnp.where(self.group < self.groups // 2, 0, 1)

    def at(self, chunk):
        return pl.ds(chunk * LINE_BLOCKS, LINE_BLOCKS)

    def comes(self, way):
        return jnp.where(way == 0, self.group > 0, self.group < self.groups - 1)

    def goes(self, way):
        return jnp.where(way == 0, self.group < self.groups - 1, self.group > 0)

    def copy(self, source, way, chunk):
        target = jnp.where(way == 0, self.group + 1, self.group - 1)
        return pltpu.make_async_remote_copy(
            src_ref=source,
            dst_ref=self.came.at[way, self.at(chunk)],
            send_sem=self.send_sems.at[way],
            recv_sem=self.recv_sems.at[way, chunk],
            device_id={"dp": target},
            device_id_type=MESH,
        )

    def load(self):
        self.loads, place = [], 0
        for index, (ref, (_, start, size)) in enumerate(zip(self.source_refs, self.sources)):
            copy = pltpu.make_async_copy(
                ref.at[pl.ds(start, size)], self.own.at[pl.ds(place, size)], self.own_sems.at[index]
            )
            copy.start()
            self.loads.append(copy)
            place += size

    def begin(self):
        for copy in self.loads:
            copy.wait()
        for way in range(2):

            @pl.when(jnp.logical_not(self.comes(way)))
            def _():
                self.came[way] = jnp.zeros(self.half, jnp.bfloat16)

                def start(chunk, carry):
                    self.copy(self.own.at[self.at(chunk)], way, chunk).start()
                    return carry

                lax.fori_loop(0, self.chunks, start, 0)

    def twin_copy(self, rows):
        side = lax.axis_index("seq")
        return pltpu.make_async_remote_copy(
            src_ref=self.total.at[rows],
            dst_ref=self.out.at[rows, side],
            send_sem=self.twin_send,
            recv_sem=self.twin_recv,
            device_id={"seq": 1 - side},
            device_id_type=MESH,
        )

    def keep_copy(self, rows):
        return pltpu.make_async_copy(
            self.total.at[rows], self.out.at[rows, lax.axis_index("seq")], self.keep_sem
        )

    def pass_on(self, way, chunk):
        rows = self.at(chunk)

        @pl.when(self.comes(way))
        def _():
            copy = self.copy(self.going.at[way, rows], way, chunk)
            copy.wait_recv()

            @pl.when(self.goes(way))
            def _():
                value = self.own[rows].astype(jnp.float32) + self.came[way, rows].astype(jnp.float32)
                self.going[way, rows] = value.astype(jnp.bfloat16)
                copy.start()

    def step(self, index):
        @pl.when(index < self.chunks)
        def _():
            self.pass_on(self.first, index)

        @pl.when(index >= LINE_LAG)
        def _():
            chunk = index - LINE_LAG
            rows = self.at(chunk)
            self.pass_on(1 - self.first, chunk)
            value = self.own[rows].astype(jnp.float32)
            value = value + self.came[0, rows].astype(jnp.float32)
            value = value + self.came[1, rows].astype(jnp.float32)
            self.total[rows] = value.astype(jnp.bfloat16)
            if self.share:

                @pl.when(lax.rem(chunk, LINE_SHARE) == LINE_SHARE - 1)
                def _():
                    done = pl.ds(chunk - (LINE_SHARE - 1), LINE_SHARE)
                    self.keep_copy(done).start()
                    self.twin_copy(done).start()

    def steps(self, count=None):
        last = self.chunks + LINE_LAG
        stop = last if count is None else min(self.done + count, last)

        def one(index, carry):
            self.step(index)
            return carry

        lax.fori_loop(self.done, stop, one, 0)
        self.done = stop

    def end(self):
        for way in range(2):

            @pl.when(self.goes(way))
            def _():
                whole_copy = pltpu.make_async_remote_copy(
                    src_ref=self.going.at[way],
                    dst_ref=self.came.at[way],
                    send_sem=self.send_sems.at[way],
                    recv_sem=self.recv_sems.at[way, 0],
                    device_id={"dp": self.group},
                    device_id_type=MESH,
                )
                whole_copy.wait_send()

        if self.share:
            everything = pl.ds(0, self.half[0])
            self.keep_copy(everything).wait()
            self.twin_copy(everything).wait()


def reduce_all(terms, collective_id, line=None, tail=None):
    _, tensors, groups, count, _ = terms.shape
    half = count // 2
    function, extras, scalars, outs = tail or (None, [], [], [])
    extra_specs = [VMEM_SPEC] * len(extras)
    extra_specs += [pl.BlockSpec(memory_space=pltpu.SMEM)] * len(scalars)
    extras = list(extras) + list(scalars)

    def kernel(*refs):
        refs = list(refs)
        terms_ref = refs.pop(0)
        source_refs = [refs.pop(0) for _ in line.operands] if line else []
        extra_refs = [refs.pop(0) for _ in extras]
        out_refs = [refs.pop(0) for _ in range(len(outs) or 1)]
        full = refs.pop(0) if tail else None
        joined_ref = refs.pop(0) if line else None
        tail_sems = [refs.pop(0) for _ in range(2)] if tail else None
        (
            near, own, mid, sums, mid_in, far, far_in,
            own_sems, near_send, near_recv, mid_send, mid_recv, far_send, far_recv,
        ) = refs[:14]
        if line:
            line.bind(source_refs, joined_ref, refs[14:])
            line.load()
        group, part, side = lax.axis_index("dp"), lax.axis_index("tensor"), lax.axis_index("seq")
        twin = 1 - side
        parts = others("tensor")
        order = others("dp") + [group]
        meet(
            [{"seq": twin}]
            + [{"tensor": peer} for peer in parts]
            + [{"dp": peer} for peer in order[:-1]]
        )
        waits, near_copies, own_copies = [], [], []
        for place, target in enumerate(order):
            near_copies.append(
                send(
                    terms_ref.at[twin, :, target],
                    near.at[place],
                    near_send.at[place],
                    near_recv.at[place],
                    {"seq": twin},
                )
            )
            copy = pltpu.make_async_copy(
                terms_ref.at[side, :, target], own.at[place], own_sems.at[place]
            )
            copy.start()
            own_copies.append(copy)
        if line:
            line.begin()
        beside = lax.rem(part + 1, 2) + part - lax.rem(part, 2)
        across = lax.rem(part + 2, 4)
        corner = 3 - part
        upper, lower = pl.ds(0, half), pl.ds(half, half)
        first_copies, second_copies = [], []

        def hand(place, index, source, target):
            return send(
                source,
                mid_in.at[place, index],
                mid_send.at[place, index],
                mid_recv.at[place, index],
                {"tensor": target},
            )

        for place in range(groups):
            near_copies[place].wait_recv()
            own_copies[place].wait()
            if line and place == 2:
                line.steps(1)
            for slot in range(tensors):
                mid[place, slot] = (
                    own[place, slot].astype(jnp.float32) + near[place, slot].astype(jnp.float32)
                ).astype(jnp.bfloat16)
            first_copies.append(
                [
                    hand(place, 0, mid.at[place, corner, upper], beside),
                    hand(place, 1, mid.at[place, corner, lower], across),
                    hand(place, 2, mid.at[place, beside, upper], beside),
                    hand(place, 3, mid.at[place, across, lower], across),
                ]
            )
        for place in range(groups):
            if line and place < 4:
                line.steps(3)
            copies = []
            for index, slot, rows, target in ((0, across, upper, across), (1, beside, lower, beside)):
                first_copies[place][index].wait_recv()
                value = mid[place, slot, rows].astype(jnp.float32)
                value = value + mid_in[place, index].astype(jnp.float32)
                sums[place, index] = value.astype(jnp.bfloat16)
                copies.append(hand(place, 4 + index, sums.at[place, index], target))
            second_copies.append(copies)
        far_copies = []
        for place, target in enumerate(order):
            copies = first_copies[place][2:] + second_copies[place]
            for copy in copies:
                copy.wait_recv()

            def joined(index):
                return mid_in[place, index].astype(jnp.float32)

            halves = [joined(2) + joined(4), joined(3) + joined(5)]
            total = mid[place, part].astype(jnp.float32) + jnp.concatenate(halves, axis=0)
            if place < groups - 1:
                far[place] = total.astype(jnp.bfloat16)
                far_copies.append(
                    send(
                        far.at[place],
                        far_in.at[place],
                        far_send.at[place],
                        far_recv.at[place],
                        {"dp": target},
                    )
                )
        if line:
            line.steps()
        for place, copy in enumerate(far_copies):
            copy.wait_recv()
            total = total + far_in[place].astype(jnp.float32)
        if tail:
            results = function(total, *extra_refs)
            for ref, value in zip(out_refs, results):
                ref[...] = value
            full[part] = results[len(outs)].astype(jnp.bfloat16)
            last_copies = [
                send(
                    full.at[part],
                    full.at[part],
                    tail_sems[0].at[step],
                    tail_sems[1].at[step],
                    {"tensor": peer},
                )
                for step, peer in enumerate(parts)
            ]
            for copy in last_copies:
                copy.wait()
        else:
            out_refs[0][...] = total
        for copy in near_copies + far_copies + [
            copy for row in first_copies + second_copies for copy in row
        ]:
            copy.wait_send()
        if line:
            line.end()

    block = (count, D)
    dma = pltpu.SemaphoreType.DMA
    results = [jax.ShapeDtypeStruct(*out) for out in outs]
    if tail:
        results.append(jax.ShapeDtypeStruct((tensors,) + block, jnp.bfloat16))
    else:
        results.append(jax.ShapeDtypeStruct(block, jnp.float32))
    return pl.pallas_call(
        kernel,
        name="reduce_all",
        out_shape=results + ([line.out_shape] if line else []),
        in_specs=[pl.BlockSpec(memory_space=pl.ANY)] + (line.in_specs if line else []) + extra_specs,
        out_specs=[VMEM_SPEC] * len(results) + ([line.out_spec] if line else []),
        scratch_shapes=[dma((tensors - 1,))] * (2 if tail else 0)
        + [pltpu.VMEM((groups, tensors) + block, jnp.bfloat16)] * 3
        + [
            pltpu.VMEM((groups, 2, half, D), jnp.bfloat16),
            pltpu.VMEM((groups, 6, half, D), jnp.bfloat16),
            pltpu.VMEM((groups,) + block, jnp.bfloat16),
            pltpu.VMEM((groups,) + block, jnp.bfloat16),
            dma((groups,)),
            dma((groups,)),
            dma((groups,)),
            dma((groups, 6)),
            dma((groups, 6)),
            dma((groups,)),
            dma((groups,)),
        ]
        + (line.scratch if line else []),
        cost_estimate=SHORT,
        compiler_params=pltpu.CompilerParams(
            collective_id=collective_id, has_side_effects=True, vmem_limit_bytes=56 << 20
        ),
    )(terms, *(line.operands if line else []), *extras)


def gather_all(block, collective_id, line=None):
    tensors, groups = lax.axis_size("tensor"), lax.axis_size("dp")
    half = block.shape[0] // 2

    def kernel(*refs):
        refs = list(refs)
        block_ref = refs.pop(0)
        source_refs = [refs.pop(0) for _ in line.operands] if line else []
        out = refs.pop(0)
        summed_ref = refs.pop(0) if line else None
        own_sem, far_send, far_recv, mid_send, mid_recv, near_send, near_recv = refs[:7]
        if line:
            line.bind(source_refs, summed_ref, refs[7:])
            line.load()
        group, part, side = lax.axis_index("dp"), lax.axis_index("tensor"), lax.axis_index("seq")
        twin = 1 - side
        meet(
            [{"seq": twin}]
            + [{"tensor": peer} for peer in others("tensor")]
            + [{"dp": peer} for peer in others("dp")]
        )
        far_copies = [
            send(
                block_ref,
                out.at[side, part, group],
                far_send.at[step],
                far_recv.at[step],
                {"dp": peer},
            )
            for step, peer in enumerate(others("dp"))
        ]
        own = pltpu.make_async_copy(block_ref, out.at[side, part, group], own_sem)
        own.start()
        if line:
            line.begin()
        beside = lax.rem(part + 1, 2) + part - lax.rem(part, 2)
        across = lax.rem(part + 2, 4)
        corner = 3 - part
        upper, lower = pl.ds(0, half), pl.ds(half, half)
        first_copies, second_copies, near_copies = [], [], []
        for place in range(groups):
            source = behind("dp", place)
            if place:
                far_copies[place - 1].wait_recv()
            held = out.at[side, part, source] if place else block_ref

            def hand(index, piece, slot, rows, target):
                return send(
                    piece,
                    out.at[side, slot, source, rows],
                    mid_send.at[place, index],
                    mid_recv.at[place, index],
                    {"tensor": target},
                )

            first = [
                hand(0, held.at[upper], part, upper, beside),
                hand(1, held.at[lower], part, lower, across),
                hand(2, held.at[lower], part, lower, beside),
                hand(3, held.at[upper], part, upper, across),
            ]
            near_copies.append(
                send(
                    held,
                    out.at[side, part, source],
                    near_send.at[place, 0],
                    near_recv.at[place, 0],
                    {"seq": twin},
                )
            )
            first[0].wait_recv()
            second = [hand(4, out.at[side, beside, source, upper], beside, upper, across)]
            first[1].wait_recv()
            second.append(hand(5, out.at[side, across, source, lower], across, lower, beside))
            first_copies.append(first)
            second_copies.append(second)
        for place in range(groups):
            if line and place < 4:
                line.steps(2)
            source = behind("dp", place)
            ready = [
                (beside, first_copies[place][2:3]),
                (across, first_copies[place][3:4]),
                (corner, second_copies[place]),
            ]
            for step, (slot, copies) in enumerate(ready):
                for copy in copies:
                    copy.wait_recv()
                held = out.at[side, slot, source]
                near_copies.append(
                    send(
                        held,
                        held,
                        near_send.at[place, step + 1],
                        near_recv.at[place, step + 1],
                        {"seq": twin},
                    )
                )
        if line:
            line.steps()
        for copy in near_copies:
            copy.wait_recv()
        for copy in near_copies + far_copies + [
            copy for row in first_copies + second_copies for copy in row
        ]:
            copy.wait_send()
        own.wait()
        if line:
            line.end()

    dma = pltpu.SemaphoreType.DMA
    anywhere = pl.BlockSpec(memory_space=pl.ANY)
    return pl.pallas_call(
        kernel,
        name="gather_all",
        out_shape=[jax.ShapeDtypeStruct((2, tensors, groups) + block.shape, block.dtype)]
        + ([line.out_shape] if line else []),
        in_specs=[VMEM_SPEC] + (line.in_specs if line else []),
        out_specs=[pl.BlockSpec(memory_space=pltpu.HBM)] + ([line.out_spec] if line else []),
        scratch_shapes=[
            dma,
            dma((groups - 1,)),
            dma((groups - 1,)),
            dma((groups, 6)),
            dma((groups, 6)),
            dma((groups, tensors)),
            dma((groups, tensors)),
        ]
        + (line.scratch if line else []),
        cost_estimate=SHORT,
        compiler_params=pltpu.CompilerParams(
            collective_id=collective_id, has_side_effects=True, vmem_limit_bytes=60 << 20
        ),
    )(block, *(line.operands if line else []))


def reduce_rows(name, terms, ids, line, function, extras, scalars, outs):
    count, groups = terms.shape[3], terms.shape[2]
    pieces = max(1, groups // 4)
    if pieces == 1:
        return reduce_all(terms, ids[0], line, (function, extras, scalars, outs))
    part = count // pieces
    sums, joined = [], []
    for i in range(pieces):
        piece = terms[:, :, :, i * part : (i + 1) * part]
        total, *joined_now = reduce_all(piece, ids[1 if i and line else 0], None if i else line)
        sums.append(total)
        joined += joined_now
    total = jnp.concatenate(sums, axis=0)
    results = tensor_step(
        name,
        lambda _, total_ref, *refs: function(total_ref, *refs),
        None,
        [total] + list(extras),
        scalars,
        outs,
        True,
        ids[2],
    )
    return list(results) + joined


def plane_steps(tensors):
    return [(step, turn_by) for step in range(tensors) for turn_by in range(2)][1:]


def plane_peers(steps):
    count, part = lax.axis_size("tensor"), lax.axis_index("tensor")
    side = lax.axis_index("seq")
    return [
        (lax.rem(part + step, count), lax.rem(side + turn_by, 2)) for step, turn_by in steps
    ]


def join_stats(stats, collective_id):
    _, tensors, groups, _, _ = stats.shape

    def join(left, right):
        top = jnp.maximum(left[..., 0:1, :], right[..., 0:1, :])
        total = left[..., 1:2, :] * jnp.exp(left[..., 0:1, :] - top) + right[..., 1:2, :] * jnp.exp(
            right[..., 0:1, :] - top
        )
        return jnp.concatenate(
            [top, total, left[..., 2:3, :] + right[..., 2:3, :], left[..., 3:, :]], axis=-2
        )

    plane = plane_steps(tensors)

    def kernel(
        stats_ref, home, full, mid_in, far, far_in, mid_send, mid_recv, far_send, far_recv
    ):
        group, part, side = lax.axis_index("dp"), lax.axis_index("tensor"), lax.axis_index("seq")
        peers, groups_else = plane_peers(plane), others("dp")
        meet(
            [{"tensor": peer, "seq": other} for peer, other in peers]
            + [{"dp": peer} for peer in groups_else]
        )
        copies = [
            send(
                stats_ref.at[other, peer],
                mid_in.at[step],
                mid_send.at[0, step],
                mid_recv.at[0, step],
                {"tensor": peer, "seq": other},
            )
            for step, (peer, other) in enumerate(peers)
        ]
        for copy in copies:
            copy.wait()
        for spot in range(groups):
            total = stats_ref[side, part, spot]
            for step in range(len(plane)):
                total = join(total, mid_in[step, spot])
            far[spot] = total
        copies = [
            send(far.at[peer], far_in.at[step], far_send.at[0, step], far_recv.at[0, step], {"dp": peer})
            for step, peer in enumerate(groups_else)
        ]
        total = far[group]
        for step, copy in enumerate(copies):
            copy.wait()
            total = join(total, far_in[step])
        log_total = total[0:1] + jnp.log(total[1:2])
        home[...] = jnp.concatenate([log_total, total[2:3], total[2:]], axis=0)
        full[side, part, group] = jnp.broadcast_to(log_total, (8, LANES))
        held = full.at[side, part, group]
        copies = [
            send(held, held, far_send.at[1, step], far_recv.at[1, step], {"dp": peer})
            for step, peer in enumerate(groups_else)
        ]
        for copy in copies:
            copy.wait()
        held = full.at[side, part]
        copies = [
            send(
                held,
                held,
                mid_send.at[1, step],
                mid_recv.at[1, step],
                {"tensor": peer, "seq": other},
            )
            for step, (peer, other) in enumerate(peers)
        ]
        for copy in copies:
            copy.wait()

    tile = (8, LANES)
    dma = pltpu.SemaphoreType.DMA
    vmem = pl.BlockSpec(memory_space=pltpu.VMEM)
    return pl.pallas_call(
        kernel,
        name="join_stats",
        out_shape=[
            jax.ShapeDtypeStruct(tile, jnp.float32),
            jax.ShapeDtypeStruct(stats.shape, jnp.float32),
        ],
        in_specs=[vmem],
        out_specs=[vmem, vmem],
        scratch_shapes=[
            pltpu.VMEM((len(plane), groups) + tile, jnp.float32),
            pltpu.VMEM((groups,) + tile, jnp.float32),
            pltpu.VMEM((groups - 1,) + tile, jnp.float32),
            dma((2, len(plane))),
            dma((2, len(plane))),
            dma((2, groups - 1)),
            dma((2, groups - 1)),
        ],
        cost_estimate=SHORT,
        compiler_params=pltpu.CompilerParams(collective_id=collective_id, has_side_effects=True),
    )(stats)


def spread_tokens(block, slot_block, ends, blocks, half_rows, collective_id):
    tensors, groups = lax.axis_size("tensor"), lax.axis_size("dp")
    rows = 2 * tensors * groups
    width = ends.shape[1]
    vocab_rows = VOCAB // tensors
    slots = slot_block.shape[0]

    def kernel(
        block_ref, slot_ref, ends_ref, ids, targets, kept, places, plan, count,
        held, firsts, own_sem, send_sems, recv_sems,
    ):
        group, side = lax.axis_index("dp"), lax.axis_index("seq")
        first_id = lax.axis_index("tensor") * vocab_rows
        peers = [
            {"dp": lax.rem(group + step // 2, groups), "seq": lax.rem(side + step % 2, 2)}
            for step in range(1, 2 * groups)
        ]
        meet(peers)
        copies = [
            send(block_ref, held.at[group, side], send_sems.at[step], recv_sems.at[step], peer)
            for step, peer in enumerate(peers)
        ]
        own = pltpu.make_async_copy(block_ref, held.at[group, side], own_sem)
        own.start()
        own.wait()
        for copy in copies:
            copy.wait()
        lane = lax.broadcasted_iota(jnp.int32, (1, LANES), 1)
        slot_ids = lax.broadcasted_iota(jnp.int32, (slots, LANES), 0)
        slot_blocks = jnp.broadcast_to(slot_ref[...], (slots, LANES))
        total = jnp.zeros((1, LANES), jnp.int32)
        hits = jnp.zeros((1, LANES), jnp.float32)
        for half in range(2):
            for source in range(groups):
                limit = held[source, half, 2 * tensors : 2 * tensors + 1, :]
                total = total + limit
                for part in range(tensors):
                    row = (half * tensors + part) * groups + source
                    token = held[source, half, part : part + 1, :]
                    ids[row] = token
                    targets[row] = held[source, half, tensors + part : tensors + part + 1, :]
                    kept[row] = jnp.where(lane + part * LANES < limit, 1.0, 0.0)
                    firsts[row : row + 1, :] = jnp.where(part * LANES < limit, 1.0, 0.0)
                    local = token - first_id
                    inside = (local >= 0) & (local < vocab_rows)
                    local = jnp.where(inside, local, 0).astype(jnp.float32)
                    block_of = jnp.floor((local + 0.5) * (0.5 / half_rows))
                    within = local - block_of * (2.0 * half_rows)
                    lower = within >= half_rows
                    inside = inside & (jnp.where(lower, 1, 0) == side)
                    within = (within - jnp.where(lower, 1.0 * half_rows, 0.0)).astype(jnp.int32)
                    same = slot_blocks == block_of.astype(jnp.int32) + blocks
                    slot = jnp.sum(jnp.where(same, slot_ids + 1, 0), axis=0, keepdims=True) - 1
                    inside = inside & (slot >= 0)
                    places[row] = jnp.where(inside, slot * half_rows + within, -1)
                    hits = hits + jnp.where(inside, 1.0, 0.0)
        count[...] = total.astype(jnp.float32)
        shape = (rows, width)
        active = jnp.concatenate([firsts[...]] * (width // LANES), axis=1)
        square = (rows, rows)
        above = jnp.where(
            lax.broadcasted_iota(jnp.int32, square, 1) < lax.broadcasted_iota(jnp.int32, square, 0),
            1.0,
            0.0,
        )
        earlier = times(above.astype(jnp.bfloat16), active.astype(jnp.bfloat16))
        number = jnp.sum(active, axis=0, keepdims=True)
        index = lax.broadcasted_iota(jnp.int32, shape, 0).astype(jnp.float32)
        turns = jnp.where(active > 0.0, earlier, number + index - earlier)
        spot = lax.broadcasted_iota(jnp.int32, shape, 1).astype(jnp.float32) - PLAN_GROUPS
        order = jnp.sum(jnp.where(turns == spot, index, 0.0), axis=0, keepdims=True)
        spot = lax.broadcasted_iota(jnp.int32, (1, width), 1)
        order = jnp.where(spot == 2, number, order)
        order = jnp.where(spot == 3, jnp.sum(hits, axis=1, keepdims=True), order)
        plan[...] = jnp.where(spot < 2, ends_ref[...], order.astype(jnp.int32))

    dma = pltpu.SemaphoreType.DMA
    vmem = pl.BlockSpec(memory_space=pltpu.VMEM)
    shape = (rows, 1, LANES)
    return pl.pallas_call(
        kernel,
        name="spread_tokens",
        out_shape=[
            jax.ShapeDtypeStruct(shape, jnp.int32),
            jax.ShapeDtypeStruct(shape, jnp.int32),
            jax.ShapeDtypeStruct(shape, jnp.float32),
            jax.ShapeDtypeStruct(shape, jnp.int32),
            jax.ShapeDtypeStruct((1, width), jnp.int32),
            jax.ShapeDtypeStruct((1, LANES), jnp.float32),
        ],
        in_specs=[vmem] * 3,
        out_specs=[vmem] * 6,
        scratch_shapes=[
            pltpu.VMEM((groups, 2) + block.shape, jnp.int32),
            pltpu.VMEM((rows, LANES), jnp.float32),
            dma,
            dma((2 * groups - 1,)),
            dma((2 * groups - 1,)),
        ],
        cost_estimate=SHORT,
        compiler_params=pltpu.CompilerParams(collective_id=collective_id, has_side_effects=True),
    )(block, slot_block, ends)


def finish(gain_grads, states, grad_ys, home, keep, table_squares, count, smalls, collective_id):
    tensors, groups = lax.axis_size("tensor"), lax.axis_size("dp")
    block = (8, D)
    plane = plane_steps(tensors)
    gain_rows = 2 * LAYERS + 1
    operands = list(gain_grads) + list(states) + list(grad_ys) + [
        home, keep, table_squares, count
    ] + list(smalls)

    def kernel(*refs):
        refs = list(refs)
        gain_refs = [refs.pop(0) for _ in gain_grads]
        state_refs = [refs.pop(0) for _ in states]
        grad_refs = [refs.pop(0) for _ in grad_ys]
        home_ref, keep_ref, table_ref, count_ref = [refs.pop(0) for _ in range(4)]
        small_refs = [refs.pop(0) for _ in smalls]
        out_refs = [refs.pop(0) for _ in range(8)]
        mid, far, mid_send, mid_recv, far_send, far_recv = refs
        group, part, side = lax.axis_index("dp"), lax.axis_index("tensor"), lax.axis_index("seq")
        peers, groups_else = plane_peers(plane), others("dp")
        meet(
            [{"tensor": peer, "seq": other} for peer, other in peers]
            + [{"dp": peer} for peer in groups_else]
        )
        values = []
        for later in range(1, LAYERS + 1):
            grad = grad_refs[later - 1][...]
            for level in range(later + 1):
                values.append(jnp.sum(grad * state_refs[level][...], keepdims=True))
        loss = jnp.where(keep_ref[...] > 0.0, home_ref[0:1, :] - home_ref[1:2, :], 0.0)
        values.append(jnp.sum(loss, keepdims=True))
        values.append(jnp.sum(table_ref[...], keepdims=True))
        lane = lax.broadcasted_iota(jnp.int32, (1, D), 1)
        row = jnp.zeros((1, D), jnp.float32)
        for place, value in enumerate(values):
            row = jnp.where(lane == place, value, row)
        blank = jnp.zeros((8 - gain_rows - 1, D), jnp.float32)
        total = jnp.concatenate([ref[...] for ref in gain_refs] + [row, blank], axis=0)
        stages = [
            (
                mid,
                2 * part + side,
                [{"tensor": peer, "seq": other} for peer, other in peers],
                mid_send,
                mid_recv,
            ),
            (far, group, [{"dp": peer} for peer in groups_else], far_send, far_recv),
        ]
        for slots, me, targets, send_sems, recv_sems in stages:
            slots[me] = total
            copies = [
                send(slots.at[me], slots.at[me], send_sems.at[step], recv_sems.at[step], target)
                for step, target in enumerate(targets)
            ]
            for copy in copies:
                copy.wait()
            total = slots[0]
            for index in range(1, slots.shape[0]):
                total = total + slots[index]
        gain_total = total[:gain_rows]
        row = total[gain_rows : gain_rows + 1]

        def pick(place):
            return jnp.sum(jnp.where(lane == place, row, 0.0), axis=1, keepdims=True)

        mix_squares = jnp.sum(jnp.where(lane < MIX_WEIGHTS, row * row, 0.0), axis=1, keepdims=True)
        gain_squares = jnp.sum(gain_total * gain_total, keepdims=True)
        tokens = count_ref[:, 0:1]
        clip_norm = jnp.sqrt(pick(MIX_WEIGHTS + 1) + gain_squares + mix_squares) / tokens
        factor = jnp.minimum(1.0, CLIP_NORM / clip_norm) / tokens
        gain_news = adam_update(
            *[ref[...] for ref in small_refs[:3]], gain_total * factor, RATE_SMALL, 0.0
        )
        mix_news = adam_update(
            *[ref[...] for ref in small_refs[3:]], row[:, :MIX_WEIGHTS] * factor, RATE_SMALL, 0.0
        )
        for ref, value in zip(out_refs[:6], gain_news + mix_news):
            ref[...] = value
        ends = jnp.where(lane == 0, pick(MIX_WEIGHTS), jnp.where(lane == 1, clip_norm, factor))
        out_refs[6][...] = ends[:, :LANES]
        out_refs[7][...] = jnp.broadcast_to(factor, (8, LANES))

    dma = pltpu.SemaphoreType.DMA
    vmem = pl.BlockSpec(memory_space=pltpu.VMEM)
    return pl.pallas_call(
        kernel,
        name="finish",
        out_shape=[jax.ShapeDtypeStruct(value.shape, jnp.float32) for value in smalls]
        + [
            jax.ShapeDtypeStruct((1, LANES), jnp.float32),
            jax.ShapeDtypeStruct((8, LANES), jnp.float32),
        ],
        in_specs=[vmem] * len(operands),
        out_specs=[vmem] * 8,
        scratch_shapes=[
            pltpu.VMEM((2 * tensors,) + block, jnp.float32),
            pltpu.VMEM((groups,) + block, jnp.float32),
            dma((len(plane),)),
            dma((len(plane),)),
            dma((groups - 1,)),
            dma((groups - 1,)),
        ],
        cost_estimate=SHORT,
        compiler_params=pltpu.CompilerParams(collective_id=collective_id, has_side_effects=True),
    )(*operands)


SLOT_STEP = 8
PREPARE_STEP = 20


def prepare(slot_block, first_id, master, blocks):
    slots, half_rows, _ = master.shape
    total = slot_block.shape[0]
    steps = -(-total // PREPARE_STEP)
    spare = steps * PREPARE_STEP - total
    slot_block = jnp.pad(slot_block, (0, spare), constant_values=-1)
    slot_block = jnp.concatenate([slot_block, first_id[None]])
    rows = PREPARE_STEP * half_rows

    def kernel(plan_ref, master_ref, table_ref, halves_ref, ids_ref):
        @pl.when(pl.program_id(0) == 0)
        def _():
            halves_ref[...] = jnp.zeros_like(halves_ref)

        for place in range(PREPARE_STEP):
            slot = pl.program_id(0) * PREPARE_STEP + place
            value = jnp.where(slot < slots, master_ref[place], 0.0).astype(jnp.bfloat16)
            table_ref[place * half_rows : (place + 1) * half_rows, :] = value

            block = plan_ref[slot]
            ids = plan_ref[steps * PREPARE_STEP] + (block - blocks) * (2 * half_rows)
            ids = ids + lax.broadcasted_iota(jnp.int32, (half_rows, 1), 0)
            ids_ref[place * half_rows : (place + 1) * half_rows, :] = jnp.where(
                block >= blocks, ids, -1
            )

            @pl.when((block >= 0) & (block < blocks))
            def _():
                halves_ref[block] = value

    last = (slots - 1) // PREPARE_STEP
    return pl.pallas_call(
        kernel,
        name="prepare",
        grid_spec=pltpu.PrefetchScalarGridSpec(
            num_scalar_prefetch=1,
            grid=(steps,),
            in_specs=[
                pl.BlockSpec(
                    (PREPARE_STEP, half_rows, D), lambda step, plan: (jnp.minimum(step, last), 0, 0)
                )
            ],
            out_specs=[
                pl.BlockSpec((rows, D), lambda step, plan: (step, 0)),
                pl.BlockSpec((blocks, half_rows, D), lambda step, plan: (0, 0, 0)),
                pl.BlockSpec((rows, 1), lambda step, plan: (step, 0)),
            ],
        ),
        out_shape=[
            jax.ShapeDtypeStruct((total * half_rows, D), jnp.bfloat16),
            jax.ShapeDtypeStruct((blocks, half_rows, D), jnp.bfloat16),
            jax.ShapeDtypeStruct((total * half_rows, 1), jnp.int32),
        ],
        cost_estimate=SHORT,
        compiler_params=pltpu.CompilerParams(vmem_limit_bytes=60 << 20),
    )(slot_block, master)


TILE = TILE_GROUPS * LANES
PICKED = 768


def row_of(values_ref, groups, place=0):
    rows = [values_ref[group, place : place + 1, :] for group in groups]
    return jnp.concatenate(rows, axis=1)


def tile_row(values_ref, tile):
    start = tile * TILE_GROUPS
    return row_of(values_ref, [start + place for place in range(TILE_GROUPS)])


PLAN_GROUPS = 4


def chunk_of(plan_ref, step):
    return pl.ds(pl.multiple_of(plan_ref[0] + step * ROW_STEP, 16), ROW_STEP)


def chunks_of(plan_ref):
    return (plan_ref[1] - plan_ref[0] + ROW_STEP - 1) // ROW_STEP


def whole(shape):
    return pl.BlockSpec(shape, lambda step, plan: (0,) * len(shape), pipeline_mode=pl.Buffered(1))


def last_tile(plan):
    return (plan[2] - 1) // TILE_GROUPS


def group_specs():
    return [
        pl.BlockSpec(
            (LANES, D),
            lambda step, plan, place=place: (
                plan[PLAN_GROUPS + jnp.minimum(step, last_tile(plan)) * TILE_GROUPS + place],
                0,
            ),
        )
        for place in range(TILE_GROUPS)
    ]


def powers_spec(rows):
    return pl.BlockSpec((rows, TILE), lambda step, plan: (0, jnp.minimum(step, last_tile(plan))))


def groups_of(plan_ref):
    start = PLAN_GROUPS + pl.program_id(0) * TILE_GROUPS
    return [plan_ref[start + place] for place in range(TILE_GROUPS)]


ROWS_SPEC = pl.BlockSpec((TILE, D), lambda step, plan: (step, 0))


def local_call(name, kernel, steps, plan, operands, in_specs, out_shape, out_specs, scratch):
    return pl.pallas_call(
        kernel,
        name=name,
        grid_spec=pltpu.PrefetchScalarGridSpec(
            num_scalar_prefetch=1,
            grid=(steps,),
            in_specs=in_specs,
            out_specs=out_specs,
            scratch_shapes=scratch,
        ),
        out_shape=out_shape,
        cost_estimate=SHORT,
        compiler_params=pltpu.CompilerParams(vmem_limit_bytes=60 << 20),
    )(plan, *operands)


def ones_where(condition):
    return jnp.where(condition, 1.0, 0.0).astype(jnp.bfloat16)


def picks(rank_row):
    return ones_where(lax.broadcasted_iota(jnp.int32, (PICKED, TILE), 0) == rank_row)


def rows_picked(plan_ref, step, place_row):
    start = plan_ref[0] + step * ROW_STEP
    row = lax.broadcasted_iota(jnp.int32, (ROW_STEP, PICKED), 0) + start
    return ones_where(row == place_row)


def look_up(plan, row_ids, tokens, places, table):
    rows, groups = table.shape[0], tokens.shape[0]
    steps = groups // TILE_GROUPS

    def kernel(
        plan_ref, ids_ref, tokens_ref, places_ref, table_ref, out_ref, ranks_ref, picked_ref, acc, picked
    ):
        tile = pl.program_id(0)
        few = plan_ref[3] <= PICKED

        @pl.when(tile == 0)
        def _():
            held = places_ref[...].reshape(groups, LANES) >= 0
            ones = ones_where(held)
            lane = (LANES, LANES)
            before = ones_where(
                lax.broadcasted_iota(jnp.int32, lane, 0) < lax.broadcasted_iota(jnp.int32, lane, 1)
            )
            group = (groups, groups)
            above = ones_where(
                lax.broadcasted_iota(jnp.int32, group, 1) < lax.broadcasted_iota(jnp.int32, group, 0)
            )
            totals = jnp.sum(ones.astype(jnp.float32), axis=1, keepdims=True)
            totals = jnp.broadcast_to(totals, (groups, LANES)).astype(jnp.bfloat16)
            ranks = (times(ones, before) + times(above, totals)).astype(jnp.int32)
            ranks_ref[...] = jnp.where(held, ranks, -1).reshape(groups, 1, LANES)

        @pl.when((tile == 0) & few)
        def _():
            def digits_of(step, total):
                place = tile_row(places_ref, step)
                high = lax.shift_right_arithmetic(place, 6)
                digits = jnp.concatenate([high, place - high * 64] * 4, axis=0)
                digits = digits.astype(jnp.float32).astype(jnp.bfloat16)
                return total + contract_last(digits, picks(tile_row(ranks_ref, step)))

            digits = lax.fori_loop(0, steps, digits_of, jnp.zeros((8, PICKED), jnp.float32))
            place = (digits[0:1] * 64.0 + digits[1:2]).astype(jnp.int32)
            index = lax.broadcasted_iota(jnp.int32, (1, PICKED), 1)
            place = jnp.where(index < plan_ref[3], place, -1)
            picked_ref[...] = jnp.broadcast_to(place, (8, PICKED))
            acc[:PICKED, :] = jnp.zeros((PICKED, D), jnp.float32)

            def one(step, carry):
                hits = rows_picked(plan_ref, step, place)
                acc[:PICKED, :] += contract_first(hits, table_ref[chunk_of(plan_ref, step), :])
                return carry

            lax.fori_loop(0, chunks_of(plan_ref), one, 0)
            picked[...] = acc[:PICKED, :].astype(jnp.bfloat16)

        @pl.when(few)
        def _():
            hits = picks(tile_row(ranks_ref, tile))
            out_ref[...] = contract_first(hits, picked[...]).astype(jnp.bfloat16)

        @pl.when(jnp.logical_not(few))
        def _():
            acc[...] = jnp.zeros_like(acc)
            wanted = tile_row(tokens_ref, tile)

            def one(step, carry):
                chunk = chunk_of(plan_ref, step)
                hits = ones_where(ids_ref[chunk, :] == wanted)
                acc[...] += contract_first(hits, table_ref[chunk, :])
                return carry

            lax.fori_loop(0, chunks_of(plan_ref), one, 0)
            out_ref[...] = acc[...].astype(jnp.bfloat16)

    lanes = (groups, 1, LANES)
    return local_call(
        "look_up",
        kernel,
        steps,
        plan,
        (row_ids, tokens, places, table),
        [whole((rows, 1)), whole(lanes), whole(lanes), whole((rows, D))],
        [
            jax.ShapeDtypeStruct((groups * LANES, D), jnp.bfloat16),
            jax.ShapeDtypeStruct(lanes, jnp.int32),
            jax.ShapeDtypeStruct((8, PICKED), jnp.int32),
        ],
        [ROWS_SPEC, whole(lanes), whole((8, PICKED))],
        [pltpu.VMEM((TILE, D), jnp.float32), pltpu.VMEM((PICKED, D), jnp.bfloat16)],
    )


def head_forward(plan, row_ids, labels, table, final):
    rows, groups = table.shape[0], labels.shape[0]
    steps = groups // TILE_GROUPS

    def kernel(plan_ref, ids_ref, labels_ref, table_ref, *rest):
        final_refs, (powers_ref, stats_ref, scores, hidden) = rest[:TILE_GROUPS], rest[TILE_GROUPS:]
        blank = jnp.zeros((1, TILE), jnp.float32)
        active = pl.program_id(0) <= last_tile(plan_ref)
        own = groups_of(plan_ref)

        def put(top, total, target):
            pad = jnp.zeros((5, LANES), jnp.float32)
            for place in range(TILE_GROUPS):
                lanes = slice(place * LANES, (place + 1) * LANES)
                stats_ref[own[place]] = jnp.concatenate(
                    [top[:, lanes], total[:, lanes], target[:, lanes], pad], axis=0
                )

        @pl.when(jnp.logical_not(active))
        def _():
            put(blank - 1e30, blank, blank)

        @pl.when(active)
        def _():
            wanted = row_of(labels_ref, own)
            for place, ref in enumerate(final_refs):
                hidden[place * LANES : (place + 1) * LANES, :] = ref[...]

            def first(step, carry):
                top, target = carry
                chunk = chunk_of(plan_ref, step)
                ids = ids_ref[chunk, :]
                raw = contract_last(table_ref[chunk, :], hidden[...])
                raw = jnp.where(ids >= 0, raw, -1e30)
                scores[chunk, :] = raw
                top = jnp.maximum(top, jnp.max(raw, axis=0, keepdims=True))
                target = target + jnp.sum(
                    jnp.where(ids == wanted, raw, 0.0), axis=0, keepdims=True
                )
                return (top, target)

            top, target = lax.fori_loop(0, chunks_of(plan_ref), first, (blank - 1e30, blank))

            def second(step, total):
                chunk = chunk_of(plan_ref, step)
                powers = jnp.exp(scores[chunk, :] - top)
                powers_ref[chunk, :] = powers.astype(jnp.bfloat16)
                return total + jnp.sum(powers, axis=0, keepdims=True)

            put(top, lax.fori_loop(0, chunks_of(plan_ref), second, blank), target)

    return local_call(
        "head_forward",
        kernel,
        steps,
        plan,
        (row_ids, labels, table) + (final,) * TILE_GROUPS,
        [whole((rows, 1)), whole((groups, 1, LANES)), whole((rows, D))] + group_specs(),
        [
            jax.ShapeDtypeStruct((rows, groups * LANES), jnp.bfloat16),
            jax.ShapeDtypeStruct((groups, 8, LANES), jnp.float32),
        ],
        [powers_spec(rows), whole((groups, 8, LANES))],
        [pltpu.VMEM((rows, TILE), jnp.float32), pltpu.VMEM((TILE, D), jnp.bfloat16)],
    )


def head_backward(plan, row_ids, labels, keep, stats, log_totals, table, final, powers):
    rows, groups = table.shape[0], labels.shape[0]
    steps = groups // TILE_GROUPS

    def kernel(plan_ref, ids_ref, labels_ref, keep_ref, stats_ref, logs_ref, table_ref, powers_ref, *rest):
        final_refs = rest[:TILE_GROUPS]
        grad_final_ref, grad_table_ref, acc, hidden, low, sems = rest[TILE_GROUPS:]
        tile = pl.program_id(0)
        slot = lax.rem(tile, 2)
        active = tile <= last_tile(plan_ref)

        def copies(step):
            start, side = PLAN_GROUPS + step * TILE_GROUPS, lax.rem(step, 2)
            return [
                pltpu.make_async_copy(
                    low.at[side, place],
                    grad_final_ref.at[plan_ref[start + place]],
                    sems.at[side, place],
                )
                for place in range(TILE_GROUPS)
            ]

        @pl.when(tile == 0)
        def _():
            grad_table_ref[...] = jnp.zeros_like(grad_table_ref)

        @pl.when(tile >= 2)
        def _():
            for copy in copies(tile - 2):
                copy.wait()

        acc[...] = jnp.zeros_like(acc)

        @pl.when(active)
        def _():
            own = groups_of(plan_ref)
            wanted, kept = row_of(labels_ref, own), row_of(keep_ref, own)
            tops = row_of(stats_ref, own)
            scale = jnp.exp(tops - row_of(logs_ref, own)) * kept
            for place, ref in enumerate(final_refs):
                hidden[place * LANES : (place + 1) * LANES, :] = ref[...]

            def one(step, carry):
                chunk = chunk_of(plan_ref, step)
                grads = powers_ref[chunk, :].astype(jnp.float32) * scale
                grads = grads - jnp.where(ids_ref[chunk, :] == wanted, kept, 0.0)
                grads = grads.astype(jnp.bfloat16)
                grad_table_ref[chunk, :] += times(grads, hidden[...])
                acc[...] += contract_first(grads, table_ref[chunk, :])
                return carry

            lax.fori_loop(0, chunks_of(plan_ref), one, 0)

        low[slot] = acc[...].astype(jnp.bfloat16).reshape(TILE_GROUPS, LANES, D)
        for copy in copies(tile):
            copy.start()

        @pl.when(tile == steps - 1)
        def _():
            for step in range(max(0, steps - 2), steps):
                for copy in copies(step):
                    copy.wait()

    lanes = (groups, 1, LANES)
    return local_call(
        "head_backward",
        kernel,
        steps,
        plan,
        (row_ids, labels, keep, stats, log_totals, table, powers) + (final,) * TILE_GROUPS,
        [
            whole((rows, 1)),
            whole(lanes),
            whole(lanes),
            whole((groups, 8, LANES)),
            whole((groups, 8, LANES)),
            whole((rows, D)),
            powers_spec(rows),
        ]
        + group_specs(),
        [
            jax.ShapeDtypeStruct((groups, LANES, D), jnp.bfloat16),
            jax.ShapeDtypeStruct((rows, D), jnp.float32),
        ],
        [pl.BlockSpec(memory_space=pl.ANY), whole((rows, D))],
        [
            pltpu.VMEM((TILE, D), jnp.float32),
            pltpu.VMEM((TILE, D), jnp.bfloat16),
            pltpu.VMEM((2, TILE_GROUPS, LANES, D), jnp.bfloat16),
            pltpu.SemaphoreType.DMA((2, TILE_GROUPS)),
        ],
    )


def look_back(
    plan, slot_plan, slots, row_ids, tokens, ranks, picked, grad_start, grad_table, layer_grads
):
    rows, groups = grad_table.shape[0], tokens.shape[0]
    steps = groups // TILE_GROUPS
    half_rows = layer_grads[0].shape[1]
    block = SLOT_STEP * half_rows
    kinds = len(layer_grads)

    def kernel(plan_ref, slot_ref, ids_ref, tokens_ref, ranks_ref, picked_ref, grad_ref, table_ref, *rest):
        layer_refs = rest[:kinds]
        slots_ref, squares_ref, acc, held, out_ref = rest[kinds:]
        step = pl.program_id(0)
        few = plan_ref[3] <= PICKED

        @pl.when(step == 0)
        def _():
            acc[...] = jnp.zeros_like(acc)
            squares_ref[...] = jnp.zeros_like(squares_ref)

        @pl.when((step < steps) & few)
        def _():
            acc[...] += times(picks(tile_row(ranks_ref, step)), grad_ref[...])

        @pl.when((step < steps) & jnp.logical_not(few))
        def _():
            held[step] = grad_ref[...]

        @pl.when(step >= steps)
        def _():
            start = (step - steps) * block

            @pl.when(few)
            def _():
                row = lax.broadcasted_iota(jnp.int32, (block, PICKED), 0) + start
                hits = ones_where(row == picked_ref[0:1, :])
                out_ref[...] = table_ref[...] + times(hits, acc[...].astype(jnp.bfloat16))

            @pl.when(jnp.logical_not(few))
            def _():
                out_ref[...] = table_ref[...]
                ids = ids_ref[pl.ds(pl.multiple_of(start, 16), block), :]

                def one(tile, carry):
                    hits = ones_where(ids == tile_row(tokens_ref, tile))
                    out_ref[...] += times(hits, held[tile])
                    return carry

                lax.fori_loop(0, steps, one, 0)

            for place in range(SLOT_STEP):
                slot = (step - steps) * SLOT_STEP + place
                kind = slot_ref[0, slot]
                part = slice(place * half_rows, (place + 1) * half_rows)

                for index in range(kinds):

                    @pl.when(kind == index)
                    def _():
                        layer = layer_refs[index][slot_ref[1 + index, slot]]
                        out_ref[part, :] = layer.astype(jnp.float32)

                @pl.when(kind < 0)
                def _():
                    out_ref[part, :] = jnp.zeros((half_rows, D), jnp.float32)

                slots_ref[place] = out_ref[part, :].astype(jnp.bfloat16)

            values = out_ref[...]
            squares_ref[...] += (values * values).reshape(block // 8, 8, D).sum(axis=0)

    def fixed(shape):
        return pl.BlockSpec(
            shape, lambda step, plan, slot: (0,) * len(shape), pipeline_mode=pl.Buffered(1)
        )

    lanes = (groups, 1, LANES)
    row_spec = pl.BlockSpec((block, D), lambda step, plan, slot: (jnp.maximum(step - steps, 0), 0))
    return pl.pallas_call(
        kernel,
        name="look_back",
        grid_spec=pltpu.PrefetchScalarGridSpec(
            num_scalar_prefetch=2,
            grid=(steps + -(-slots // SLOT_STEP),),
            in_specs=[
                fixed((rows, 1)),
                fixed(lanes),
                fixed(lanes),
                fixed((8, PICKED)),
                pl.BlockSpec((TILE, D), lambda step, plan, slot: (jnp.minimum(step, steps - 1), 0)),
                row_spec,
            ]
            + [fixed(grads.shape) for grads in layer_grads],
            out_specs=[
                pl.BlockSpec(
                    (SLOT_STEP, half_rows, D),
                    lambda step, plan, slot: (jnp.maximum(step - steps, 0), 0, 0),
                ),
                fixed((8, D)),
            ],
            scratch_shapes=[
                pltpu.VMEM((PICKED, D), jnp.float32),
                pltpu.VMEM((steps, TILE, D), jnp.bfloat16),
                pltpu.VMEM((block, D), jnp.float32),
            ],
        ),
        out_shape=[
            jax.ShapeDtypeStruct((slots, half_rows, D), jnp.bfloat16),
            jax.ShapeDtypeStruct((8, D), jnp.float32),
        ],
        cost_estimate=SHORT,
        compiler_params=pltpu.CompilerParams(vmem_limit_bytes=60 << 20),
    )(
        plan,
        slot_plan,
        row_ids,
        tokens,
        ranks,
        picked,
        grad_start,
        grad_table,
        *layer_grads,
    )


def grads_home(level):
    return [(2 * level, 0), (2 * level + 1, 0), (2 * level + 1, 1)]


def body(
    token_ids,
    labels,
    real_counts,
    owners,
    master,
    first_moment,
    second_moment,
    gains,
    gains_first,
    gains_second,
    mix,
    mix_first,
    mix_second,
):
    tensors = lax.axis_size("tensor")
    groups = lax.axis_size("dp")
    group = lax.axis_index("dp")
    tensor_part = lax.axis_index("tensor")
    seq_part = lax.axis_index("seq")
    slots, half_rows, _ = master.shape
    seq_count, half_len = token_ids.shape
    row_count = seq_count * half_len
    share = row_count // tensors
    head_rows = 3 * D // tensors
    out_rows = D // tensors
    unit_rows = FF // tensors
    layer_rows = head_rows + out_rows + 2 * unit_rows
    layer_blocks = layer_rows // (2 * half_rows)
    blocks = LAYERS * layer_blocks
    vocab_rows = VOCAB // tensors
    local_heads = HEADS // tensors

    slot_rank = slot_table(owners)
    block_ids = jnp.arange(owners.shape[0], dtype=jnp.int32)
    mine = owners == group
    match = (jnp.arange(slots)[:, None] == slot_rank[None, :]) & mine[None, :]
    slot_block = jnp.sum(jnp.where(match, block_ids[None, :] + 1, 0), axis=1) - 1
    spare = -(-ROW_STEP // half_rows)
    spare += -(slots + spare) % SLOT_STEP
    held = jnp.sum(jnp.where(mine, 1, 0)) * half_rows
    first_held = jnp.sum(jnp.where(mine & (block_ids < blocks), 1, 0)) * half_rows
    slot_block_all = jnp.pad(slot_block, (0, spare), constant_values=-1).astype(jnp.int32)
    third = layer_blocks // 3
    which, within = slot_block_all // third, slot_block_all % third
    homes = [home for level in range(LAYERS) for home in grads_home(level)]
    arrays = 1 + max(array for array, _ in homes)
    kind, index = jnp.full(which.shape, -1), jnp.zeros_like(which)
    for place, (array, part) in enumerate(homes):
        kind = jnp.where(which == place, array, kind)
        index = jnp.where(which == place, within + part * third, index)
    kind = jnp.where(slot_block_all >= blocks, arrays, jnp.where(slot_block_all < 0, -1, kind))
    slot_plan = jnp.stack(
        [kind] + [jnp.where(kind == array, index, 0) for array in range(arrays)]
    ).astype(jnp.int32)

    packed = jnp.concatenate(
        [
            token_ids.reshape(tensors, LANES),
            labels.reshape(tensors, LANES),
            jnp.broadcast_to(real_counts[:, None], (16 - 2 * tensors, LANES)),
        ],
        axis=0,
    )
    width = -(-(2 * tensors * groups + PLAN_GROUPS) // LANES) * LANES
    lane = jnp.arange(width)[None, :]
    ends = jnp.where(lane == 0, first_held, jnp.where(lane == 1, held, 0)).astype(jnp.int32)
    ids_all, labels_all, keep_all, places, plan, count = spread_tokens(
        packed, slot_block_all[:, None], ends, blocks, half_rows, 15
    )
    plan = plan.reshape(-1)
    order = (2, tensors, groups, share)

    first_id = (tensor_part * vocab_rows + seq_part * half_rows).astype(jnp.int32)
    table, halves, row_ids = prepare(slot_block_all, first_id, master, blocks)

    def weights_line(*starts):
        return Line([(halves, start * third, third) for start in starts], True)

    def as_table(joined):
        return joined.reshape(-1, D)

    positions = seq_part * half_len + jnp.arange(row_count) % half_len
    steps_half = jnp.arange(HEAD_DIM // 2).astype(jnp.float32)
    freqs = 10000.0 ** (-2.0 * steps_half / HEAD_DIM)
    angles = freqs[:, None] * positions.astype(jnp.float32)[None, :]
    cosine, sine = jnp.cos(angles), jnp.sin(angles)

    looked, ranks, picked = look_up(plan, row_ids, ids_all, places, table)
    looked = looked.reshape(order + (D,))
    gain = [gains[i : i + 1] for i in range(2 * LAYERS + 1)]
    piece = ((share, D), jnp.float32)

    def normed_of(total, gain_row):
        return (total[...], layer_norm_parts(total[...])[0] * gain_row[...])

    def inner_of(total, stream, gain_row):
        inner = stream + total
        return (inner, layer_norm_parts(inner)[0] * gain_row)

    def outcome_of(base, total, inner, gain_row, *rest):
        states, scalars = rest[:-1], rest[-1]
        outcome = inner + total
        stream = scalars[base + len(states)] * outcome
        for source, state in enumerate(states):
            stream = stream + scalars[base + source] * state
        return (outcome, stream, layer_norm_parts(stream)[0] * gain_row)

    start, normed, joined = reduce_rows(
        "normed", looked, (14, 18, 1), weights_line(0, 1), normed_of, [gain[0]], [], [piece]
    )
    table_one = as_table(joined)
    attention_table, up = table_one, (table_one, 1)
    tables = []
    states, streams, inners, kept_all = [start], [start], [], []
    for level in range(LAYERS):
        here, last = 3 * level, level == LAYERS - 1
        carried = [] if last else [here + 3]
        carried += [here + 1, here + 2] if level else [here + 2]
        inner, normed_two, queries, both, logs, attended, joined = tensor_step(
            f"inner_{level}",
            inner_of,
            attention_work(normed, attention_table, cosine, sine),
            (streams[level], gain[2 * level + 1]),
            (),
            [piece],
            True,
            2 if level == 0 else 15 + level,
            weights_line(*carried),
        )
        kept = (queries, both, logs, attended)
        joined = as_table(joined)
        down = (joined, len(carried) - 1)
        up = (joined, len(carried) - 2) if level else up
        tables.append((attention_table, up, down))
        attention_table = joined
        outcome, stream, normed_next, hidden, activated = tensor_step(
            f"outcome_{level}",
            partial(outcome_of, (level + 1) * (level + 2) // 2 - 1),
            unit_work(normed_two, up, down),
            [inner, gain[2 * level + 2]] + states,
            (mix,),
            [piece, piece] + ([((share, D), jnp.bfloat16)] if last else []),
            not last,
            3 + level,
        )
        inners.append(inner)
        kept_all.append((normed, kept, normed_two, (hidden, activated)))
        states.append(outcome)
        streams.append(stream)
        normed = normed_next

    final_all = gather_all(normed, 3 + LAYERS)[0].reshape(-1, D)
    powers, stats = head_forward(plan, row_ids, labels_all, table, final_all)
    home, log_totals = join_stats(
        stats.reshape((2, tensors, groups, 8, LANES)), 4 + LAYERS
    )
    grad_final, grad_table = head_backward(
        plan,
        row_ids,
        labels_all,
        keep_all,
        stats,
        log_totals.reshape(-1, 8, LANES),
        table,
        final_all,
        powers,
    )
    grad_final = grad_final.reshape(order + (D,))

    row = ((1, D), jnp.float32)

    def top_of(total, stream, gain_row, scalars):
        grad_top, grad_gain = norm_pull(total[...], gain_row[...], stream[...])
        grad_state = scalars[MIX_WEIGHTS - 1] * grad_top
        return (grad_top, grad_state, grad_gain, grad_state)

    def inner_back(total, grad_out, inner, gain_row):
        grad, grad_gain = norm_pull(total, gain_row, inner)
        grad = grad_out + grad
        return (grad, grad_gain, grad)

    def stream_back(block, total, grad_inner, stream, gain_row, *rest):
        grad_ys, scalars = rest[:-1], rest[-1]
        grad, grad_gain = norm_pull(total, gain_row, stream)
        grad = grad_inner + grad
        state = grad if block == 0 else scalars[block * (block + 1) // 2 - 1 + block] * grad
        for offset, grad_y in enumerate(grad_ys):
            later = block + 1 + offset
            state = state + scalars[later * (later + 1) // 2 - 1 + block] * grad_y
        return (grad, state, grad_gain, state)

    grad_ys = [None] * (LAYERS + 1)
    gain_grads = [None] * (2 * LAYERS + 1)
    layer_grads, attention_grads = [None] * (2 * LAYERS), None
    grad_ys[LAYERS], grad_state, gain_grads[2 * LAYERS], grad_branch = reduce_rows(
        "top_back",
        grad_final,
        (0, 0, 5 + LAYERS),
        None,
        top_of,
        [streams[LAYERS], gain[2 * LAYERS]],
        [mix],
        [piece, piece, row],
    )
    for level in reversed(range(LAYERS)):
        normed, kept, normed_two, unit_kept = kept_all[level]
        attention_table, up, down = tables[level]
        grad_inner, gain_grads[2 * level + 1], grad_attn, unit_grads, *summed = tensor_step(
            f"inner_back_{level}",
            inner_back,
            unit_back_work(grad_branch, normed_two, up, down, unit_kept, half_rows),
            (grad_state, inners[level], gain[2 * level + 1]),
            (),
            [piece, row],
            True,
            6 + LAYERS if level == 0 else 19 + level,
            None if attention_grads is None else Line([(attention_grads, 0, third)], False),
        )
        if summed:
            layer_grads[2 * (level + 1)] = summed[0]
        grad_ys[level], grad_state, gain_grads[2 * level], grad_branch, attention_grads, summed = (
            tensor_step(
                f"stream_back_{level}",
                partial(stream_back, level),
                attention_back_work(
                    grad_attn, normed, attention_table, kept, cosine, sine, half_rows
                ),
                [grad_inner, streams[level], gain[2 * level]] + grad_ys[level + 1 :],
                (mix,),
                [piece, piece, row] + ([] if level else [((share, D), jnp.bfloat16)]),
                level > 0,
                7 + LAYERS + level,
                Line([(unit_grads, 0, 2 * third)], False),
            )
        )
        layer_grads[2 * level + 1] = summed

    grad_start_all, layer_grads[0] = gather_all(
        grad_branch, 13, Line([(attention_grads, 0, third)], False)
    )
    grad_start_all = grad_start_all.reshape(-1, D)
    owned, table_squares = look_back(
        plan,
        slot_plan,
        slots,
        row_ids,
        ids_all,
        ranks,
        picked,
        grad_start_all,
        grad_table,
        layer_grads,
    )
    keep = jnp.where(
        tensor_part * share + jnp.arange(share) < real_counts[0], 1.0, 0.0
    ).astype(jnp.float32)
    news = finish(
        gain_grads,
        states,
        grad_ys[1:],
        home,
        keep[None],
        table_squares,
        count,
        (gains, gains_first, gains_second, mix[None], mix_first[None], mix_second[None]),
        7 + 2 * LAYERS,
    )
    new_gains, new_gains_first, new_gains_second = news[:3]
    new_mix, new_mix_first, new_mix_second = [value[0] for value in news[3:6]]
    loss_sum, clip_norm = news[6][0, 0], news[6][0, 1]
    token_count = count[0, 0]
    owned = owned.astype(jnp.float32) * news[7][0, 0]
    new_master, new_first, new_second = adam_update(
        master, first_moment, second_moment, owned, RATE_MATRIX, DECAY_MATRIX
    )
    return (
        new_master,
        new_first,
        new_second,
        new_gains,
        new_gains_first,
        new_gains_second,
        new_mix,
        new_mix_first,
        new_mix_second,
        loss_sum,
        token_count,
        clip_norm,
    )


def solution(mesh):
    return jax.shard_map(
        body,
        mesh=mesh,
        in_specs=(
            P("dp", "seq"),
            P("dp", "seq"),
            P(("dp", "seq")),
            P(),
            P("dp", ("tensor", "seq"), None),
            P("dp", ("tensor", "seq"), None),
            P("dp", ("tensor", "seq"), None),
            P(),
            P(),
            P(),
            P(),
            P(),
            P(),
        ),
        out_specs=(
            P("dp", ("tensor", "seq"), None),
            P("dp", ("tensor", "seq"), None),
            P("dp", ("tensor", "seq"), None),
            P(),
            P(),
            P(),
            P(),
            P(),
            P(),
            P(),
            P(),
            P(),
        ),
        check_vma=False,
    )
```

```python
from functools import partial

import jax
import jax.numpy as jnp
from jax import lax
from jax.experimental import pallas as pl
from jax.experimental.pallas import tpu as pltpu
from jax.sharding import PartitionSpec as P

D = 768
HEADS = 12
HEAD_DIM = 64
FF = 3072
VOCAB = 50304
LAYERS = 2
STEP_COUNT = 10
MIX_WEIGHTS = 5


EPS_NORM = 1e-05
CLIP_NORM = 0.01
BETA_ONE = 0.9
BETA_TWO = 0.95
ADAM_EPS = 1e-08
RATE_MATRIX = 0.04
RATE_SMALL = 0.4
DECAY_MATRIX = 0.1


def contract_last(left, right):
    return lax.dot_general(
        left, right, (((1,), (1,)), ((), ())), preferred_element_type=jnp.float32
    )


def contract_first(left, right):
    return lax.dot_general(
        left, right, (((0,), (0,)), ((), ())), preferred_element_type=jnp.float32
    )


def slot_table(owners):
    ranks = jnp.arange(owners.shape[0])
    same = (owners[None, :] == owners[:, None]) & (ranks[None, :] < ranks[:, None])
    return jnp.sum(jnp.where(same, 1, 0), axis=1).astype(jnp.int32)


def adam_update(weight, first, second, grad, rate, decay):
    first = BETA_ONE * first + (1.0 - BETA_ONE) * grad
    second = BETA_TWO * second + (1.0 - BETA_TWO) * grad * grad
    first_hat = first / (1.0 - BETA_ONE**STEP_COUNT)
    second_hat = second / (1.0 - BETA_TWO**STEP_COUNT)
    weight = weight - rate * (first_hat / (jnp.sqrt(second_hat) + ADAM_EPS) + decay * weight)
    return (weight, first, second)


MESH = pl.DeviceIdType.MESH
ROW_STEP = 400
TILE_GROUPS = 8
LANES = 128
SHORT = pl.CostEstimate(flops=1000, bytes_accessed=1000, transcendentals=0)
LONG = pl.CostEstimate(flops=10**12, bytes_accessed=1 << 30, transcendentals=0)


def meet(peers):
    gate = pltpu.get_barrier_semaphore()
    for peer in peers:
        pl.semaphore_signal(gate, inc=1, device_id=peer, device_id_type=MESH)
    pl.semaphore_wait(gate, len(peers))


def others(axis):
    count, me = lax.axis_size(axis), lax.axis_index(axis)
    return [lax.rem(me + step, count) for step in range(1, count)]


def behind(axis, step):
    count, me = lax.axis_size(axis), lax.axis_index(axis)
    return lax.rem(me + count - step, count)


def send(source, target, send_sem, recv_sem, device):
    copy = pltpu.make_async_remote_copy(
        src_ref=source,
        dst_ref=target,
        send_sem=send_sem,
        recv_sem=recv_sem,
        device_id=device,
        device_id_type=MESH,
    )
    copy.start()
    return copy


def layer_norm_parts(stream):
    center = stream - jnp.mean(stream, -1, keepdims=True)
    inverse = lax.rsqrt(jnp.mean(center * center, -1, keepdims=True) + EPS_NORM)
    return center * inverse, inverse


def norm_pull(grad_normed, gain, stream):
    scaled, inverse = layer_norm_parts(stream)
    grad_scaled = grad_normed * gain
    grad_stream = inverse * (
        grad_scaled
        - jnp.mean(grad_scaled, -1, keepdims=True)
        - scaled * jnp.mean(grad_scaled * scaled, -1, keepdims=True)
    )
    return grad_stream, jnp.sum(grad_normed * scaled, axis=0, keepdims=True)


class Work:
    def __init__(self, before, during, operands, specs, outs, scratch, after=None, twins=False):
        self.before, self.during, self.after, self.twins = before, during, after, twins
        self.operands, self.specs, self.outs, self.scratch = operands, specs, outs, scratch


def tensor_step(name, function, work, extras, scalars, outs, gather, collective_id, line=None):
    parts = lax.axis_size("tensor")
    share = extras[0].shape[0]
    reduce = work is not None
    work = work or Work(None, None, [], [], [], [])
    arrays = list(work.operands) + list(extras)
    parts_of = list(work.specs) + [None] * len(extras)

    def kernel(*refs):
        refs = list(refs)

        def take(count):
            return [refs.pop(0) for _ in range(count)]

        array_refs = take(len(arrays))
        scalar_refs = take(len(scalars))
        source_refs = take(len(line.operands)) if line else []
        out_refs = take(len(outs))
        (full,) = take(1) if gather else [None]
        work_outs = take(len(work.outs))
        (joined,) = take(1) if line else [None]
        held = take(len(arrays))
        (load_sems,) = take(1)
        loads = []
        for index, (ref, part, target) in enumerate(zip(array_refs, parts_of, held)):
            if part:
                ref = ref.at[pl.ds(part[0] * part[1], part[0])]
            loads.append(pltpu.make_async_copy(ref, target, load_sems.at[index]))
            loads[-1].start()
        work_refs, extra_refs = held[: len(work.operands)], held[len(work.operands) :]
        send_sems, recv_sems = take(2)
        partial_ref, outgoing, arrived = take(3) if reduce else [None] * 3
        if line:
            line.bind(source_refs, joined, take(len(line.scratch)))
            line.load()

        def tick(count=1):
            if line:
                line.steps(count)

        me, side = lax.axis_index("tensor"), lax.axis_index("seq")
        peers = others("tensor")
        twin = {"seq": 1 - side}
        twins = work.twins or (line and line.share)
        meet(
            [{"tensor": peer} for peer in peers]
            + [twin] * bool(twins)
            + ([{"dp": peer} for peer in others("dp")] if line else [])
        )
        if line:
            line.begin()
        for load in loads:
            load.wait()
        total = None
        if reduce:
            work.before(work_refs, work_outs, refs, partial_ref, tick)
            copies = []
            for step, peer in enumerate(peers):
                rows = pl.ds(pl.multiple_of(peer * share, share), share)
                outgoing[step] = partial_ref[rows, :].astype(jnp.bfloat16)
                copies.append(
                    send(
                        outgoing.at[step],
                        arrived.at[step],
                        send_sems.at[0, step],
                        recv_sems.at[0, step],
                        {"tensor": peer},
                    )
                )
            if work.during:
                work.during(work_refs, work_outs, refs)
            tick(6)
            total = partial_ref[pl.ds(pl.multiple_of(me * share, share), share), :]
            for step, copy in enumerate(copies):
                copy.wait()
                total = total + arrived[step].astype(jnp.float32)
        results = function(total, *[ref[...] for ref in extra_refs], *scalar_refs)
        for ref, value in zip(out_refs, results):
            ref[...] = value.astype(ref.dtype)
        if gather:
            full[me] = results[len(outs)].astype(jnp.bfloat16)
            copies = [
                send(
                    full.at[me],
                    full.at[me],
                    send_sems.at[1, step],
                    recv_sems.at[1, step],
                    {"tensor": peer},
                )
                for step, peer in enumerate(peers)
            ]
        if work.after:
            work.after(work_refs, work_outs, refs)
        tick(None)
        if gather:
            for copy in copies:
                copy.wait()
        if line:
            line.end()

    vmem = pl.BlockSpec(memory_space=pltpu.VMEM)
    smem = pl.BlockSpec(memory_space=pltpu.SMEM)
    shapes = [jax.ShapeDtypeStruct(shape, dtype) for shape, dtype in outs]
    if gather:
        shapes.append(jax.ShapeDtypeStruct((parts, share, D), jnp.bfloat16))
    shapes += [jax.ShapeDtypeStruct(shape, dtype) for shape, dtype in work.outs]
    out_specs = [vmem] * len(shapes)
    operands = arrays + list(scalars)
    in_specs = [pl.BlockSpec(memory_space=pl.ANY)] * len(arrays) + [smem] * len(scalars)
    dma = pltpu.SemaphoreType.DMA
    buffers = [
        pltpu.VMEM((part[0], D) if part else array.shape, array.dtype)
        for array, part in zip(arrays, parts_of)
    ]
    buffers += [dma((len(arrays),))] + [dma((2, parts - 1))] * 2
    if reduce:
        buffers += [pltpu.VMEM((parts * share, D), jnp.float32)]
        buffers += [pltpu.VMEM((parts - 1, share, D), jnp.bfloat16)] * 2
    if line:
        operands += line.operands
        in_specs += line.in_specs
        shapes.append(line.out_shape)
        out_specs.append(line.out_spec)
        buffers += line.scratch
    return pl.pallas_call(
        kernel,
        name=name,
        grid=(1,),
        out_shape=shapes,
        in_specs=in_specs,
        out_specs=out_specs,
        scratch_shapes=buffers + list(work.scratch),
        cost_estimate=SHORT,
        compiler_params=pltpu.CompilerParams(
            collective_id=collective_id, has_side_effects=True, vmem_limit_bytes=60 << 20
        ),
    )(*operands)


VMEM_SPEC = pl.BlockSpec(memory_space=pltpu.VMEM)


def part_spec(rows, index):
    return rows, index


def turn(block, cosine, sine):
    half = HEAD_DIM // 2
    first, second = block[:half], block[half:]
    return jnp.concatenate(
        [first * cosine - second * sine, second * cosine + first * sine], axis=0
    )


def times(left, right):
    return jnp.dot(left, right, preferred_element_type=jnp.float32)


def masks_of(count, side):
    key = lax.broadcasted_iota(jnp.int32, (count, count), 0)
    query = lax.broadcasted_iota(jnp.int32, (count, count), 1)
    far = jnp.where(side == 0, -1e30, 0.0).astype(jnp.float32)
    return far, jnp.where(key <= query, 0.0, -1e30)


def scores_of(keys_values, head, queries, masks):
    span = slice(head * HEAD_DIM, (head + 1) * HEAD_DIM)
    scale = HEAD_DIM ** (-0.5)
    far = contract_first(keys_values[0, 0, span, :], queries) * scale + masks[0]
    own = contract_first(keys_values[1, 0, span, :], queries) * scale + masks[1]
    return far, own


def attention_work(normed, table, cosine, sine):
    parts, share, _ = normed.shape
    count = parts * share
    width = D // parts
    heads = width // HEAD_DIM

    def before(ins, outs, scratch, partial_ref, tick):
        normed_ref, qkv_ref, out_ref, cosine_ref, sine_ref = ins
        queries_ref, both, logs_ref, attended_ref = outs
        send_sem, recv_sem = scratch
        side = lax.axis_index("seq")
        cosine, sine = cosine_ref[...], sine_ref[...]
        rows = normed_ref[...].reshape(count, D)
        joined = contract_last(qkv_ref[...], rows)
        for head in range(heads):
            span = slice(head * HEAD_DIM, (head + 1) * HEAD_DIM)
            keys = joined[width + head * HEAD_DIM : width + (head + 1) * HEAD_DIM]
            both[1, 0, span, :] = turn(keys, cosine, sine).astype(jnp.bfloat16)
        both[1, 1] = joined[2 * width :].astype(jnp.bfloat16)
        copy = pltpu.make_async_remote_copy(
            src_ref=both.at[1],
            dst_ref=both.at[0],
            send_sem=send_sem,
            recv_sem=recv_sem,
            device_id={"seq": 1 - side},
            device_id_type=MESH,
        )

        copy.start()
        for head in range(heads):
            span = slice(head * HEAD_DIM, (head + 1) * HEAD_DIM)
            queries_ref[span, :] = turn(joined[span], cosine, sine).astype(jnp.bfloat16)

        copy.wait()
        masks = masks_of(count, side)
        for head in range(heads):
            span = slice(head * HEAD_DIM, (head + 1) * HEAD_DIM)
            far, own = scores_of(both, head, queries_ref[span, :], masks)
            peak = jnp.maximum(
                jnp.max(far, axis=0, keepdims=True), jnp.max(own, axis=0, keepdims=True)
            )
            far, own = jnp.exp(far - peak), jnp.exp(own - peak)
            total = jnp.sum(far, axis=0, keepdims=True) + jnp.sum(own, axis=0, keepdims=True)
            logs_ref[head] = peak + jnp.log(total)
            inverse = 1.0 / total
            attended = times(both[0, 1, span, :], (far * inverse).astype(jnp.bfloat16))
            attended += times(both[1, 1, span, :], (own * inverse).astype(jnp.bfloat16))
            attended_ref[span, :] = attended.astype(jnp.bfloat16)
            tick(2)
        partial_ref[...] = contract_first(attended_ref[...], out_ref[...])

    low = jnp.bfloat16
    return Work(
        before,
        None,
        [normed, table, table, cosine, sine],
        [None, part_spec(3 * width, 0), part_spec(width, 3), None, None],
        [
            ((width, count), low),
            ((2, 2, width, count), low),
            ((heads, 1, count), jnp.float32),
            ((width, count), low),
        ],
        [pltpu.SemaphoreType.DMA, pltpu.SemaphoreType.DMA],
        twins=True,
    )


def fold_copy(own, near, send_sems, recv_sems, index):
    side = lax.axis_index("seq")
    return pltpu.make_async_remote_copy(
        src_ref=own.at[index, :, 1 - side],
        dst_ref=near.at[index],
        send_sem=send_sems.at[index],
        recv_sem=recv_sems.at[index],
        device_id={"seq": 1 - side},
        device_id_type=MESH,
    )


def add_halves(own, near, out, start):
    side = lax.axis_index("seq")

    def one(block, carry):
        value = own[block, side].astype(jnp.float32) + near[block].astype(jnp.float32)
        out[start + block] = value.astype(jnp.bfloat16)
        return carry

    lax.fori_loop(0, near.shape[0], one, 0)


def attention_back_work(grad, normed, table, kept, cosine, sine, half_rows):
    parts, share, _ = normed.shape
    count = parts * share
    width = D // parts
    heads = width // HEAD_DIM
    queries, both, logs, attended = kept
    blocks = 4 * width // (2 * half_rows)

    def before(ins, outs, scratch, partial_ref, tick):
        grad_ref, _, qkv_ref, out_ref, queries_ref, both, logs_ref, _, cosine_ref, sine_ref = ins
        back, came, grad_joined, send_sem, recv_sem = scratch[:5]
        side = lax.axis_index("seq")
        cosine, sine = cosine_ref[...], -sine_ref[...]
        scale = HEAD_DIM ** (-0.5)
        grads = contract_last(out_ref[...], grad_ref[...].reshape(count, D)).astype(jnp.bfloat16)
        own_grads = []
        masks = masks_of(count, side)
        for head in range(heads):
            span = slice(head * HEAD_DIM, (head + 1) * HEAD_DIM)
            head_queries, head_grads = queries_ref[span, :], grads[span]
            far, own = scores_of(both, head, head_queries, masks)
            far, own = jnp.exp(far - logs_ref[head]), jnp.exp(own - logs_ref[head])
            far_grad = contract_first(both[0, 1, span, :], head_grads)
            own_grad = contract_first(both[1, 1, span, :], head_grads)
            mean = jnp.sum(far * far_grad, axis=0, keepdims=True)
            mean += jnp.sum(own * own_grad, axis=0, keepdims=True)
            far_grad = (far * (far_grad - mean)).astype(jnp.bfloat16)
            own_grad = (own * (own_grad - mean)).astype(jnp.bfloat16)
            far, own = far.astype(jnp.bfloat16), own.astype(jnp.bfloat16)
            back[0, span, :] = (contract_last(head_queries, far_grad) * scale).astype(jnp.bfloat16)
            back[1, span, :] = contract_last(head_grads, far).astype(jnp.bfloat16)
            query_grad = times(both[0, 0, span, :], far_grad) + times(both[1, 0, span, :], own_grad)
            grad_joined[span, :] = turn(query_grad * scale, cosine, sine).astype(jnp.bfloat16)
            own_grads.append(
                (contract_last(head_queries, own_grad) * scale, contract_last(head_grads, own))
            )
            tick(2)
        copy = send(back, came, send_sem, recv_sem, {"seq": 1 - side})
        copy.wait()
        for head, (key_grad, value_grad) in enumerate(own_grads):
            span = slice(head * HEAD_DIM, (head + 1) * HEAD_DIM)
            key_grad = key_grad + came[0, span, :].astype(jnp.float32)
            value_grad = value_grad + came[1, span, :].astype(jnp.float32)
            start = width + head * HEAD_DIM
            grad_joined[start : start + HEAD_DIM, :] = turn(key_grad, cosine, sine).astype(
                jnp.bfloat16
            )
            start += width
            grad_joined[start : start + HEAD_DIM, :] = value_grad.astype(jnp.bfloat16)
        partial_ref[...] = contract_first(grad_joined[...], qkv_ref[...])

    def during(ins, outs, scratch):
        grad_ref, normed_ref, attended_ref = ins[0], ins[1], ins[7]
        grad_joined = scratch[2]
        own, near, fold_send, fold_recv = scratch[5:]
        value = times(grad_joined[...], normed_ref[...].reshape(count, D)).astype(jnp.bfloat16)
        part = 3 * blocks // 4
        own[0, :part] = value.reshape(part, 2, half_rows, D)
        value = times(attended_ref[...], grad_ref[...].reshape(count, D)).astype(jnp.bfloat16)
        own[0, part:] = value.reshape(blocks - part, 2, half_rows, D)
        fold_copy(own, near, fold_send, fold_recv, 0).start()

    def after(ins, outs, scratch):
        own, near, fold_send, fold_recv = scratch[5:]
        fold_copy(own, near, fold_send, fold_recv, 0).wait()
        add_halves(own.at[0], near.at[0], outs[0], 0)

    low = jnp.bfloat16
    dma = pltpu.SemaphoreType.DMA
    return Work(
        before,
        during,
        [grad, normed, table, table, queries, both, logs, attended, cosine, sine],
        [None, None, part_spec(3 * width, 0), part_spec(width, 3)] + [None] * 6,
        [((blocks, half_rows, D), low)],
        [
            pltpu.VMEM((2, width, count), low),
            pltpu.VMEM((2, width, count), low),
            pltpu.VMEM((3 * width, count), low),
            dma,
            dma,
            pltpu.VMEM((1, blocks, 2, half_rows, D), low),
            pltpu.VMEM((1, blocks, half_rows, D), low),
            dma((1,)),
            dma((1,)),
        ],
        after,
        True,
    )


def gelu(hidden):
    return jax.nn.gelu(hidden, approximate=True)


def unit_work(normed, up, down):
    parts, share, _ = normed.shape
    count = parts * share
    units = FF // parts

    def before(ins, outs, scratch, partial_ref, tick):
        normed_ref, up_ref, down_ref = ins
        hidden_ref, activated_ref = outs
        hidden = contract_last(up_ref[...], normed_ref[...].reshape(count, D))
        hidden_ref[...] = hidden
        activated_ref[...] = gelu(hidden).astype(jnp.bfloat16)
        tick(2)
        partial_ref[...] = contract_first(activated_ref[...], down_ref[...])

    return Work(
        before,
        None,
        [normed, up[0], down[0]],
        [None, part_spec(units, up[1]), part_spec(units, down[1])],
        [((units, count), jnp.float32), ((units, count), jnp.bfloat16)],
        [],
    )


def unit_back_work(grad, normed, up, down, kept, half_rows):
    parts, share, _ = normed.shape
    count = parts * share
    units = FF // parts
    hidden, activated = kept
    blocks = units // (2 * half_rows)

    def before(ins, outs, scratch, partial_ref, tick):
        grad_ref, _, up_ref, down_ref, hidden_ref, _ = ins
        grad_hidden = scratch[0]
        grad_act = contract_last(down_ref[...], grad_ref[...].reshape(count, D))
        _, pull = jax.vjp(gelu, hidden_ref[...])
        grad_hidden[...] = pull(grad_act)[0].astype(jnp.bfloat16)
        tick(2)
        partial_ref[...] = contract_first(grad_hidden[...], up_ref[...])

    def during(ins, outs, scratch):
        grad_ref, normed_ref, _, _, _, activated_ref = ins
        grad_hidden, own, near, fold_send, fold_recv = scratch
        value = times(grad_hidden[...], normed_ref[...].reshape(count, D))
        own[0] = value.astype(jnp.bfloat16).reshape(own.shape[1:])
        fold_copy(own, near, fold_send, fold_recv, 0).start()
        value = times(activated_ref[...], grad_ref[...].reshape(count, D))
        own[1] = value.astype(jnp.bfloat16).reshape(own.shape[1:])
        fold_copy(own, near, fold_send, fold_recv, 1).start()

    def after(ins, outs, scratch):
        _, own, near, fold_send, fold_recv = scratch
        for index in range(2):
            fold_copy(own, near, fold_send, fold_recv, index).wait()
            add_halves(own.at[index], near.at[index], outs[0], index * blocks)

    low, dma = jnp.bfloat16, pltpu.SemaphoreType.DMA
    return Work(
        before,
        during,
        [grad, normed, up[0], down[0], hidden, activated],
        [None, None, part_spec(units, up[1]), part_spec(units, down[1])]
        + [None] * 2,
        [((2 * blocks, half_rows, D), low)],
        [
            pltpu.VMEM((units, count), low),
            pltpu.VMEM((2, blocks, 2, half_rows, D), low),
            pltpu.VMEM((2, blocks, half_rows, D), low),
            dma((2,)),
            dma((2,)),
        ],
        after,
        True,
    )


LINE_BLOCKS = 1
LINE_LAG = 3
LINE_SHARE = 4


class Line:
    def __init__(self, sources, share):
        self.groups = lax.axis_size("dp")
        self.sources, self.share = sources, share
        count = sum(size for _, _, size in sources)
        _, half_rows, _ = sources[0][0].shape
        self.half = (count, half_rows, D)
        self.chunks = count // LINE_BLOCKS
        self.operands = [array for array, _, _ in sources]
        self.in_specs = [pl.BlockSpec(memory_space=pl.ANY)] * len(sources)
        dma = pltpu.SemaphoreType.DMA
        out = (count, 2, half_rows, D) if share else self.half
        self.out_shape = jax.ShapeDtypeStruct(out, jnp.bfloat16)
        self.out_spec = pl.BlockSpec(memory_space=pl.ANY if share else pltpu.VMEM)
        self.scratch = [
            pltpu.VMEM(self.half, jnp.bfloat16),
            pltpu.VMEM((2,) + self.half, jnp.bfloat16),
            pltpu.VMEM((2,) + self.half, jnp.bfloat16),
            dma((len(sources),)),
            dma((2,)),
            dma((2, self.chunks)),
        ]
        if share:
            self.scratch += [pltpu.VMEM(self.half, jnp.bfloat16)] + [dma] * 3

    def bind(self, source_refs, out_ref, refs):
        self.source_refs, self.out = source_refs, out_ref
        self.own, self.came, self.going, self.own_sems, self.send_sems, self.recv_sems = refs[:6]
        self.total = out_ref
        if self.share:
            self.total, self.keep_sem, self.twin_send, self.twin_recv = refs[6:]
        self.done = 0
        self.group = lax.axis_index("dp")
        self.first = jnp.where(self.group < self.groups // 2, 0, 1)

    def at(self, chunk):
        return pl.ds(chunk * LINE_BLOCKS, LINE_BLOCKS)

    def comes(self, way):
        return jnp.where(way == 0, self.group > 0, self.group < self.groups - 1)

    def goes(self, way):
        return jnp.where(way == 0, self.group < self.groups - 1, self.group > 0)

    def copy(self, source, way, chunk):
        target = jnp.where(way == 0, self.group + 1, self.group - 1)
        return pltpu.make_async_remote_copy(
            src_ref=source,
            dst_ref=self.came.at[way, self.at(chunk)],
            send_sem=self.send_sems.at[way],
            recv_sem=self.recv_sems.at[way, chunk],
            device_id={"dp": target},
            device_id_type=MESH,
        )

    def load(self):
        self.loads, place = [], 0
        for index, (ref, (_, start, size)) in enumerate(zip(self.source_refs, self.sources)):
            copy = pltpu.make_async_copy(
                ref.at[pl.ds(start, size)], self.own.at[pl.ds(place, size)], self.own_sems.at[index]
            )
            copy.start()
            self.loads.append(copy)
            place += size

    def begin(self):
        for copy in self.loads:
            copy.wait()
        for way in range(2):

            @pl.when(jnp.logical_not(self.comes(way)))
            def _():
                self.came[way] = jnp.zeros(self.half, jnp.bfloat16)

                def start(chunk, carry):
                    self.copy(self.own.at[self.at(chunk)], way, chunk).start()
                    return carry

                lax.fori_loop(0, self.chunks, start, 0)

    def twin_copy(self, rows):
        side = lax.axis_index("seq")
        return pltpu.make_async_remote_copy(
            src_ref=self.total.at[rows],
            dst_ref=self.out.at[rows, side],
            send_sem=self.twin_send,
            recv_sem=self.twin_recv,
            device_id={"seq": 1 - side},
            device_id_type=MESH,
        )

    def keep_copy(self, rows):
        return pltpu.make_async_copy(
            self.total.at[rows], self.out.at[rows, lax.axis_index("seq")], self.keep_sem
        )

    def pass_on(self, way, chunk):
        rows = self.at(chunk)

        @pl.when(self.comes(way))
        def _():
            copy = self.copy(self.going.at[way, rows], way, chunk)
            copy.wait_recv()

            @pl.when(self.goes(way))
            def _():
                value = self.own[rows].astype(jnp.float32) + self.came[way, rows].astype(jnp.float32)
                self.going[way, rows] = value.astype(jnp.bfloat16)
                copy.start()

    def step(self, index):
        @pl.when(index < self.chunks)
        def _():
            self.pass_on(self.first, index)

        @pl.when(index >= LINE_LAG)
        def _():
            chunk = index - LINE_LAG
            rows = self.at(chunk)
            self.pass_on(1 - self.first, chunk)
            value = self.own[rows].astype(jnp.float32)
            value = value + self.came[0, rows].astype(jnp.float32)
            value = value + self.came[1, rows].astype(jnp.float32)
            self.total[rows] = value.astype(jnp.bfloat16)
            if self.share:

                @pl.when(lax.rem(chunk, LINE_SHARE) == LINE_SHARE - 1)
                def _():
                    done = pl.ds(chunk - (LINE_SHARE - 1), LINE_SHARE)
                    self.keep_copy(done).start()
                    self.twin_copy(done).start()

    def steps(self, count=None):
        last = self.chunks + LINE_LAG
        stop = last if count is None else min(self.done + count, last)

        def one(index, carry):
            self.step(index)
            return carry

        lax.fori_loop(self.done, stop, one, 0)
        self.done = stop

    def end(self):
        for way in range(2):

            @pl.when(self.goes(way))
            def _():
                whole_copy = pltpu.make_async_remote_copy(
                    src_ref=self.going.at[way],
                    dst_ref=self.came.at[way],
                    send_sem=self.send_sems.at[way],
                    recv_sem=self.recv_sems.at[way, 0],
                    device_id={"dp": self.group},
                    device_id_type=MESH,
                )
                whole_copy.wait_send()

        if self.share:
            everything = pl.ds(0, self.half[0])
            self.keep_copy(everything).wait()
            self.twin_copy(everything).wait()


def reduce_all(terms, collective_id, line=None, tail=None):
    _, tensors, groups, count, _ = terms.shape
    half = count // 2
    function, extras, scalars, outs = tail or (None, [], [], [])
    extra_specs = [VMEM_SPEC] * len(extras)
    extra_specs += [pl.BlockSpec(memory_space=pltpu.SMEM)] * len(scalars)
    extras = list(extras) + list(scalars)

    def kernel(*refs):
        refs = list(refs)
        terms_ref = refs.pop(0)
        source_refs = [refs.pop(0) for _ in line.operands] if line else []
        extra_refs = [refs.pop(0) for _ in extras]
        out_refs = [refs.pop(0) for _ in range(len(outs) or 1)]
        full = refs.pop(0) if tail else None
        joined_ref = refs.pop(0) if line else None
        tail_sems = [refs.pop(0) for _ in range(2)] if tail else None
        (
            near, own, mid, sums, mid_in, far, far_in,
            own_sems, near_send, near_recv, mid_send, mid_recv, far_send, far_recv,
        ) = refs[:14]
        if line:
            line.bind(source_refs, joined_ref, refs[14:])
            line.load()
        group, part, side = lax.axis_index("dp"), lax.axis_index("tensor"), lax.axis_index("seq")
        twin = 1 - side
        parts = others("tensor")
        order = others("dp") + [group]
        meet(
            [{"seq": twin}]
            + [{"tensor": peer} for peer in parts]
            + [{"dp": peer} for peer in order[:-1]]
        )
        waits, near_copies, own_copies = [], [], []
        for place, target in enumerate(order):
            near_copies.append(
                send(
                    terms_ref.at[twin, :, target],
                    near.at[place],
                    near_send.at[place],
                    near_recv.at[place],
                    {"seq": twin},
                )
            )
            copy = pltpu.make_async_copy(
                terms_ref.at[side, :, target], own.at[place], own_sems.at[place]
            )
            copy.start()
            own_copies.append(copy)
        if line:
            line.begin()
        beside = lax.rem(part + 1, 2) + part - lax.rem(part, 2)
        across = lax.rem(part + 2, 4)
        corner = 3 - part
        upper, lower = pl.ds(0, half), pl.ds(half, half)
        first_copies, second_copies = [], []

        def hand(place, index, source, target):
            return send(
                source,
                mid_in.at[place, index],
                mid_send.at[place, index],
                mid_recv.at[place, index],
                {"tensor": target},
            )

        for place in range(groups):
            near_copies[place].wait_recv()
            own_copies[place].wait()
            if line and place == 2:
                line.steps(1)
            for slot in range(tensors):
                mid[place, slot] = (
                    own[place, slot].astype(jnp.float32) + near[place, slot].astype(jnp.float32)
                ).astype(jnp.bfloat16)
            first_copies.append(
                [
                    hand(place, 0, mid.at[place, corner, upper], beside),
                    hand(place, 1, mid.at[place, corner, lower], across),
                    hand(place, 2, mid.at[place, beside, upper], beside),
                    hand(place, 3, mid.at[place, across, lower], across),
                ]
            )
        for place in range(groups):
            if line and place < 4:
                line.steps(3)
            copies = []
            for index, slot, rows, target in ((0, across, upper, across), (1, beside, lower, beside)):
                first_copies[place][index].wait_recv()
                value = mid[place, slot, rows].astype(jnp.float32)
                value = value + mid_in[place, index].astype(jnp.float32)
                sums[place, index] = value.astype(jnp.bfloat16)
                copies.append(hand(place, 4 + index, sums.at[place, index], target))
            second_copies.append(copies)
        far_copies = []
        for place, target in enumerate(order):
            copies = first_copies[place][2:] + second_copies[place]
            for copy in copies:
                copy.wait_recv()

            def joined(index):
                return mid_in[place, index].astype(jnp.float32)

            halves = [joined(2) + joined(4), joined(3) + joined(5)]
            total = mid[place, part].astype(jnp.float32) + jnp.concatenate(halves, axis=0)
            if place < groups - 1:
                far[place] = total.astype(jnp.bfloat16)
                far_copies.append(
                    send(
                        far.at[place],
                        far_in.at[place],
                        far_send.at[place],
                        far_recv.at[place],
                        {"dp": target},
                    )
                )
        if line:
            line.steps()
        for place, copy in enumerate(far_copies):
            copy.wait_recv()
            total = total + far_in[place].astype(jnp.float32)
        if tail:
            results = function(total, *extra_refs)
            for ref, value in zip(out_refs, results):
                ref[...] = value
            full[part] = results[len(outs)].astype(jnp.bfloat16)
            last_copies = [
                send(
                    full.at[part],
                    full.at[part],
                    tail_sems[0].at[step],
                    tail_sems[1].at[step],
                    {"tensor": peer},
                )
                for step, peer in enumerate(parts)
            ]
            for copy in last_copies:
                copy.wait()
        else:
            out_refs[0][...] = total
        for copy in near_copies + far_copies + [
            copy for row in first_copies + second_copies for copy in row
        ]:
            copy.wait_send()
        if line:
            line.end()

    block = (count, D)
    dma = pltpu.SemaphoreType.DMA
    results = [jax.ShapeDtypeStruct(*out) for out in outs]
    if tail:
        results.append(jax.ShapeDtypeStruct((tensors,) + block, jnp.bfloat16))
    else:
        results.append(jax.ShapeDtypeStruct(block, jnp.float32))
    return pl.pallas_call(
        kernel,
        name="reduce_all",
        out_shape=results + ([line.out_shape] if line else []),
        in_specs=[pl.BlockSpec(memory_space=pl.ANY)] + (line.in_specs if line else []) + extra_specs,
        out_specs=[VMEM_SPEC] * len(results) + ([line.out_spec] if line else []),
        scratch_shapes=[dma((tensors - 1,))] * (2 if tail else 0)
        + [pltpu.VMEM((groups, tensors) + block, jnp.bfloat16)] * 3
        + [
            pltpu.VMEM((groups, 2, half, D), jnp.bfloat16),
            pltpu.VMEM((groups, 6, half, D), jnp.bfloat16),
            pltpu.VMEM((groups,) + block, jnp.bfloat16),
            pltpu.VMEM((groups,) + block, jnp.bfloat16),
            dma((groups,)),
            dma((groups,)),
            dma((groups,)),
            dma((groups, 6)),
            dma((groups, 6)),
            dma((groups,)),
            dma((groups,)),
        ]
        + (line.scratch if line else []),
        cost_estimate=SHORT,
        compiler_params=pltpu.CompilerParams(
            collective_id=collective_id, has_side_effects=True, vmem_limit_bytes=56 << 20
        ),
    )(terms, *(line.operands if line else []), *extras)


def gather_all(block, collective_id, line=None):
    tensors, groups = lax.axis_size("tensor"), lax.axis_size("dp")
    half = block.shape[0] // 2

    def kernel(*refs):
        refs = list(refs)
        block_ref = refs.pop(0)
        source_refs = [refs.pop(0) for _ in line.operands] if line else []
        out = refs.pop(0)
        summed_ref = refs.pop(0) if line else None
        own_sem, far_send, far_recv, mid_send, mid_recv, near_send, near_recv = refs[:7]
        if line:
            line.bind(source_refs, summed_ref, refs[7:])
            line.load()
        group, part, side = lax.axis_index("dp"), lax.axis_index("tensor"), lax.axis_index("seq")
        twin = 1 - side
        meet(
            [{"seq": twin}]
            + [{"tensor": peer} for peer in others("tensor")]
            + [{"dp": peer} for peer in others("dp")]
        )
        far_copies = [
            send(
                block_ref,
                out.at[side, part, group],
                far_send.at[step],
                far_recv.at[step],
                {"dp": peer},
            )
            for step, peer in enumerate(others("dp"))
        ]
        own = pltpu.make_async_copy(block_ref, out.at[side, part, group], own_sem)
        own.start()
        if line:
            line.begin()
        beside = lax.rem(part + 1, 2) + part - lax.rem(part, 2)
        across = lax.rem(part + 2, 4)
        corner = 3 - part
        upper, lower = pl.ds(0, half), pl.ds(half, half)
        first_copies, second_copies, near_copies = [], [], []
        for place in range(groups):
            source = behind("dp", place)
            if place:
                far_copies[place - 1].wait_recv()
            held = out.at[side, part, source] if place else block_ref

            def hand(index, piece, slot, rows, target):
                return send(
                    piece,
                    out.at[side, slot, source, rows],
                    mid_send.at[place, index],
                    mid_recv.at[place, index],
                    {"tensor": target},
                )

            first = [
                hand(0, held.at[upper], part, upper, beside),
                hand(1, held.at[lower], part, lower, across),
                hand(2, held.at[lower], part, lower, beside),
                hand(3, held.at[upper], part, upper, across),
            ]
            near_copies.append(
                send(
                    held,
                    out.at[side, part, source],
                    near_send.at[place, 0],
                    near_recv.at[place, 0],
                    {"seq": twin},
                )
            )
            first[0].wait_recv()
            second = [hand(4, out.at[side, beside, source, upper], beside, upper, across)]
            first[1].wait_recv()
            second.append(hand(5, out.at[side, across, source, lower], across, lower, beside))
            first_copies.append(first)
            second_copies.append(second)
        for place in range(groups):
            if line and place < 4:
                line.steps(2)
            source = behind("dp", place)
            ready = [
                (beside, first_copies[place][2:3]),
                (across, first_copies[place][3:4]),
                (corner, second_copies[place]),
            ]
            for step, (slot, copies) in enumerate(ready):
                for copy in copies:
                    copy.wait_recv()
                held = out.at[side, slot, source]
                near_copies.append(
                    send(
                        held,
                        held,
                        near_send.at[place, step + 1],
                        near_recv.at[place, step + 1],
                        {"seq": twin},
                    )
                )
        if line:
            line.steps()
        for copy in near_copies:
            copy.wait_recv()
        for copy in near_copies + far_copies + [
            copy for row in first_copies + second_copies for copy in row
        ]:
            copy.wait_send()
        own.wait()
        if line:
            line.end()

    dma = pltpu.SemaphoreType.DMA
    anywhere = pl.BlockSpec(memory_space=pl.ANY)
    return pl.pallas_call(
        kernel,
        name="gather_all",
        out_shape=[jax.ShapeDtypeStruct((2, tensors, groups) + block.shape, block.dtype)]
        + ([line.out_shape] if line else []),
        in_specs=[VMEM_SPEC] + (line.in_specs if line else []),
        out_specs=[pl.BlockSpec(memory_space=pltpu.HBM)] + ([line.out_spec] if line else []),
        scratch_shapes=[
            dma,
            dma((groups - 1,)),
            dma((groups - 1,)),
            dma((groups, 6)),
            dma((groups, 6)),
            dma((groups, tensors)),
            dma((groups, tensors)),
        ]
        + (line.scratch if line else []),
        cost_estimate=SHORT,
        compiler_params=pltpu.CompilerParams(
            collective_id=collective_id, has_side_effects=True, vmem_limit_bytes=60 << 20
        ),
    )(block, *(line.operands if line else []))


def reduce_rows(name, terms, ids, line, function, extras, scalars, outs):
    count, groups = terms.shape[3], terms.shape[2]
    pieces = max(1, groups // 4)
    if pieces == 1:
        return reduce_all(terms, ids[0], line, (function, extras, scalars, outs))
    part = count // pieces
    sums, joined = [], []
    for i in range(pieces):
        piece = terms[:, :, :, i * part : (i + 1) * part]
        total, *joined_now = reduce_all(piece, ids[1 if i and line else 0], None if i else line)
        sums.append(total)
        joined += joined_now
    total = jnp.concatenate(sums, axis=0)
    results = tensor_step(
        name,
        lambda _, total_ref, *refs: function(total_ref, *refs),
        None,
        [total] + list(extras),
        scalars,
        outs,
        True,
        ids[2],
    )
    return list(results) + joined


def plane_steps(tensors):
    return [(step, turn_by) for step in range(tensors) for turn_by in range(2)][1:]


def plane_peers(steps):
    count, part = lax.axis_size("tensor"), lax.axis_index("tensor")
    side = lax.axis_index("seq")
    return [
        (lax.rem(part + step, count), lax.rem(side + turn_by, 2)) for step, turn_by in steps
    ]


def join_stats(stats, collective_id):
    _, tensors, groups, _, _ = stats.shape

    def join(left, right):
        top = jnp.maximum(left[..., 0:1, :], right[..., 0:1, :])
        total = left[..., 1:2, :] * jnp.exp(left[..., 0:1, :] - top) + right[..., 1:2, :] * jnp.exp(
            right[..., 0:1, :] - top
        )
        return jnp.concatenate(
            [top, total, left[..., 2:3, :] + right[..., 2:3, :], left[..., 3:, :]], axis=-2
        )

    plane = plane_steps(tensors)

    def kernel(
        stats_ref, home, full, mid_in, far, far_in, mid_send, mid_recv, far_send, far_recv
    ):
        group, part, side = lax.axis_index("dp"), lax.axis_index("tensor"), lax.axis_index("seq")
        peers, groups_else = plane_peers(plane), others("dp")
        meet(
            [{"tensor": peer, "seq": other} for peer, other in peers]
            + [{"dp": peer} for peer in groups_else]
        )
        copies = [
            send(
                stats_ref.at[other, peer],
                mid_in.at[step],
                mid_send.at[0, step],
                mid_recv.at[0, step],
                {"tensor": peer, "seq": other},
            )
            for step, (peer, other) in enumerate(peers)
        ]
        for copy in copies:
            copy.wait()
        for spot in range(groups):
            total = stats_ref[side, part, spot]
            for step in range(len(plane)):
                total = join(total, mid_in[step, spot])
            far[spot] = total
        copies = [
            send(far.at[peer], far_in.at[step], far_send.at[0, step], far_recv.at[0, step], {"dp": peer})
            for step, peer in enumerate(groups_else)
        ]
        total = far[group]
        for step, copy in enumerate(copies):
            copy.wait()
            total = join(total, far_in[step])
        log_total = total[0:1] + jnp.log(total[1:2])
        home[...] = jnp.concatenate([log_total, total[2:3], total[2:]], axis=0)
        full[side, part, group] = jnp.broadcast_to(log_total, (8, LANES))
        held = full.at[side, part, group]
        copies = [
            send(held, held, far_send.at[1, step], far_recv.at[1, step], {"dp": peer})
            for step, peer in enumerate(groups_else)
        ]
        for copy in copies:
            copy.wait()
        held = full.at[side, part]
        copies = [
            send(
                held,
                held,
                mid_send.at[1, step],
                mid_recv.at[1, step],
                {"tensor": peer, "seq": other},
            )
            for step, (peer, other) in enumerate(peers)
        ]
        for copy in copies:
            copy.wait()

    tile = (8, LANES)
    dma = pltpu.SemaphoreType.DMA
    vmem = pl.BlockSpec(memory_space=pltpu.VMEM)
    return pl.pallas_call(
        kernel,
        name="join_stats",
        out_shape=[
            jax.ShapeDtypeStruct(tile, jnp.float32),
            jax.ShapeDtypeStruct(stats.shape, jnp.float32),
        ],
        in_specs=[vmem],
        out_specs=[vmem, vmem],
        scratch_shapes=[
            pltpu.VMEM((len(plane), groups) + tile, jnp.float32),
            pltpu.VMEM((groups,) + tile, jnp.float32),
            pltpu.VMEM((groups - 1,) + tile, jnp.float32),
            dma((2, len(plane))),
            dma((2, len(plane))),
            dma((2, groups - 1)),
            dma((2, groups - 1)),
        ],
        cost_estimate=SHORT,
        compiler_params=pltpu.CompilerParams(collective_id=collective_id, has_side_effects=True),
    )(stats)


def spread_tokens(block, slot_block, ends, blocks, half_rows, collective_id):
    tensors, groups = lax.axis_size("tensor"), lax.axis_size("dp")
    rows = 2 * tensors * groups
    width = ends.shape[1]
    vocab_rows = VOCAB // tensors
    slots = slot_block.shape[0]

    def kernel(
        block_ref, slot_ref, ends_ref, ids, targets, kept, places, plan, count,
        held, firsts, own_sem, send_sems, recv_sems,
    ):
        group, side = lax.axis_index("dp"), lax.axis_index("seq")
        first_id = lax.axis_index("tensor") * vocab_rows
        peers = [
            {"dp": lax.rem(group + step // 2, groups), "seq": lax.rem(side + step % 2, 2)}
            for step in range(1, 2 * groups)
        ]
        meet(peers)
        copies = [
            send(block_ref, held.at[group, side], send_sems.at[step], recv_sems.at[step], peer)
            for step, peer in enumerate(peers)
        ]
        own = pltpu.make_async_copy(block_ref, held.at[group, side], own_sem)
        own.start()
        own.wait()
        for copy in copies:
            copy.wait()
        lane = lax.broadcasted_iota(jnp.int32, (1, LANES), 1)
        slot_ids = lax.broadcasted_iota(jnp.int32, (slots, LANES), 0)
        slot_blocks = jnp.broadcast_to(slot_ref[...], (slots, LANES))
        total = jnp.zeros((1, LANES), jnp.int32)
        hits = jnp.zeros((1, LANES), jnp.float32)
        for half in range(2):
            for source in range(groups):
                limit = held[source, half, 2 * tensors : 2 * tensors + 1, :]
                total = total + limit
                for part in range(tensors):
                    row = (half * tensors + part) * groups + source
                    token = held[source, half, part : part + 1, :]
                    ids[row] = token
                    targets[row] = held[source, half, tensors + part : tensors + part + 1, :]
                    kept[row] = jnp.where(lane + part * LANES < limit, 1.0, 0.0)
                    firsts[row : row + 1, :] = jnp.where(part * LANES < limit, 1.0, 0.0)
                    local = token - first_id
                    inside = (local >= 0) & (local < vocab_rows)
                    local = jnp.where(inside, local, 0).astype(jnp.float32)
                    block_of = jnp.floor((local + 0.5) * (0.5 / half_rows))
                    within = local - block_of * (2.0 * half_rows)
                    lower = within >= half_rows
                    inside = inside & (jnp.where(lower, 1, 0) == side)
                    within = (within - jnp.where(lower, 1.0 * half_rows, 0.0)).astype(jnp.int32)
                    same = slot_blocks == block_of.astype(jnp.int32) + blocks
                    slot = jnp.sum(jnp.where(same, slot_ids + 1, 0), axis=0, keepdims=True) - 1
                    inside = inside & (slot >= 0)
                    places[row] = jnp.where(inside, slot * half_rows + within, -1)
                    hits = hits + jnp.where(inside, 1.0, 0.0)
        count[...] = total.astype(jnp.float32)
        shape = (rows, width)
        active = jnp.concatenate([firsts[...]] * (width // LANES), axis=1)
        square = (rows, rows)
        above = jnp.where(
            lax.broadcasted_iota(jnp.int32, square, 1) < lax.broadcasted_iota(jnp.int32, square, 0),
            1.0,
            0.0,
        )
        earlier = times(above.astype(jnp.bfloat16), active.astype(jnp.bfloat16))
        number = jnp.sum(active, axis=0, keepdims=True)
        index = lax.broadcasted_iota(jnp.int32, shape, 0).astype(jnp.float32)
        turns = jnp.where(active > 0.0, earlier, number + index - earlier)
        spot = lax.broadcasted_iota(jnp.int32, shape, 1).astype(jnp.float32) - PLAN_GROUPS
        order = jnp.sum(jnp.where(turns == spot, index, 0.0), axis=0, keepdims=True)
        spot = lax.broadcasted_iota(jnp.int32, (1, width), 1)
        order = jnp.where(spot == 2, number, order)
        order = jnp.where(spot == 3, jnp.sum(hits, axis=1, keepdims=True), order)
        plan[...] = jnp.where(spot < 2, ends_ref[...], order.astype(jnp.int32))

    dma = pltpu.SemaphoreType.DMA
    vmem = pl.BlockSpec(memory_space=pltpu.VMEM)
    shape = (rows, 1, LANES)
    return pl.pallas_call(
        kernel,
        name="spread_tokens",
        out_shape=[
            jax.ShapeDtypeStruct(shape, jnp.int32),
            jax.ShapeDtypeStruct(shape, jnp.int32),
            jax.ShapeDtypeStruct(shape, jnp.float32),
            jax.ShapeDtypeStruct(shape, jnp.int32),
            jax.ShapeDtypeStruct((1, width), jnp.int32),
            jax.ShapeDtypeStruct((1, LANES), jnp.float32),
        ],
        in_specs=[vmem] * 3,
        out_specs=[vmem] * 6,
        scratch_shapes=[
            pltpu.VMEM((groups, 2) + block.shape, jnp.int32),
            pltpu.VMEM((rows, LANES), jnp.float32),
            dma,
            dma((2 * groups - 1,)),
            dma((2 * groups - 1,)),
        ],
        cost_estimate=SHORT,
        compiler_params=pltpu.CompilerParams(collective_id=collective_id, has_side_effects=True),
    )(block, slot_block, ends)


def finish(gain_grads, states, grad_ys, home, keep, table_squares, count, smalls, collective_id):
    tensors, groups = lax.axis_size("tensor"), lax.axis_size("dp")
    block = (8, D)
    plane = plane_steps(tensors)
    gain_rows = 2 * LAYERS + 1
    operands = list(gain_grads) + list(states) + list(grad_ys) + [
        home, keep, table_squares, count
    ] + list(smalls)

    def kernel(*refs):
        refs = list(refs)
        gain_refs = [refs.pop(0) for _ in gain_grads]
        state_refs = [refs.pop(0) for _ in states]
        grad_refs = [refs.pop(0) for _ in grad_ys]
        home_ref, keep_ref, table_ref, count_ref = [refs.pop(0) for _ in range(4)]
        small_refs = [refs.pop(0) for _ in smalls]
        out_refs = [refs.pop(0) for _ in range(8)]
        mid, far, mid_send, mid_recv, far_send, far_recv = refs
        group, part, side = lax.axis_index("dp"), lax.axis_index("tensor"), lax.axis_index("seq")
        peers, groups_else = plane_peers(plane), others("dp")
        meet(
            [{"tensor": peer, "seq": other} for peer, other in peers]
            + [{"dp": peer} for peer in groups_else]
        )
        values = []
        for later in range(1, LAYERS + 1):
            grad = grad_refs[later - 1][...]
            for level in range(later + 1):
                values.append(jnp.sum(grad * state_refs[level][...], keepdims=True))
        loss = jnp.where(keep_ref[...] > 0.0, home_ref[0:1, :] - home_ref[1:2, :], 0.0)
        values.append(jnp.sum(loss, keepdims=True))
        values.append(jnp.sum(table_ref[...], keepdims=True))
        lane = lax.broadcasted_iota(jnp.int32, (1, D), 1)
        row = jnp.zeros((1, D), jnp.float32)
        for place, value in enumerate(values):
            row = jnp.where(lane == place, value, row)
        blank = jnp.zeros((8 - gain_rows - 1, D), jnp.float32)
        total = jnp.concatenate([ref[...] for ref in gain_refs] + [row, blank], axis=0)
        stages = [
            (
                mid,
                2 * part + side,
                [{"tensor": peer, "seq": other} for peer, other in peers],
                mid_send,
                mid_recv,
            ),
            (far, group, [{"dp": peer} for peer in groups_else], far_send, far_recv),
        ]
        for slots, me, targets, send_sems, recv_sems in stages:
            slots[me] = total
            copies = [
                send(slots.at[me], slots.at[me], send_sems.at[step], recv_sems.at[step], target)
                for step, target in enumerate(targets)
            ]
            for copy in copies:
                copy.wait()
            total = slots[0]
            for index in range(1, slots.shape[0]):
                total = total + slots[index]
        gain_total = total[:gain_rows]
        row = total[gain_rows : gain_rows + 1]

        def pick(place):
            return jnp.sum(jnp.where(lane == place, row, 0.0), axis=1, keepdims=True)

        mix_squares = jnp.sum(jnp.where(lane < MIX_WEIGHTS, row * row, 0.0), axis=1, keepdims=True)
        gain_squares = jnp.sum(gain_total * gain_total, keepdims=True)
        tokens = count_ref[:, 0:1]
        clip_norm = jnp.sqrt(pick(MIX_WEIGHTS + 1) + gain_squares + mix_squares) / tokens
        factor = jnp.minimum(1.0, CLIP_NORM / clip_norm) / tokens
        gain_news = adam_update(
            *[ref[...] for ref in small_refs[:3]], gain_total * factor, RATE_SMALL, 0.0
        )
        mix_news = adam_update(
            *[ref[...] for ref in small_refs[3:]], row[:, :MIX_WEIGHTS] * factor, RATE_SMALL, 0.0
        )
        for ref, value in zip(out_refs[:6], gain_news + mix_news):
            ref[...] = value
        ends = jnp.where(lane == 0, pick(MIX_WEIGHTS), jnp.where(lane == 1, clip_norm, factor))
        out_refs[6][...] = ends[:, :LANES]
        out_refs[7][...] = jnp.broadcast_to(factor, (8, LANES))

    dma = pltpu.SemaphoreType.DMA
    vmem = pl.BlockSpec(memory_space=pltpu.VMEM)
    return pl.pallas_call(
        kernel,
        name="finish",
        out_shape=[jax.ShapeDtypeStruct(value.shape, jnp.float32) for value in smalls]
        + [
            jax.ShapeDtypeStruct((1, LANES), jnp.float32),
            jax.ShapeDtypeStruct((8, LANES), jnp.float32),
        ],
        in_specs=[vmem] * len(operands),
        out_specs=[vmem] * 8,
        scratch_shapes=[
            pltpu.VMEM((2 * tensors,) + block, jnp.float32),
            pltpu.VMEM((groups,) + block, jnp.float32),
            dma((len(plane),)),
            dma((len(plane),)),
            dma((groups - 1,)),
            dma((groups - 1,)),
        ],
        cost_estimate=LONG,
        compiler_params=pltpu.CompilerParams(
            collective_id=collective_id, has_side_effects=True, vmem_limit_bytes=8 << 20
        ),
    )(*operands)


SLOT_STEP = 8
PREPARE_STEP = 20


def prepare(slot_block, first_id, master, blocks):
    slots, half_rows, _ = master.shape
    total = slot_block.shape[0]
    steps = -(-total // PREPARE_STEP)
    spare = steps * PREPARE_STEP - total
    slot_block = jnp.pad(slot_block, (0, spare), constant_values=-1)
    slot_block = jnp.concatenate([slot_block, first_id[None]])
    rows = PREPARE_STEP * half_rows

    def kernel(plan_ref, master_ref, table_ref, halves_ref, ids_ref):
        @pl.when(pl.program_id(0) == 0)
        def _():
            halves_ref[...] = jnp.zeros_like(halves_ref)

        for place in range(PREPARE_STEP):
            slot = pl.program_id(0) * PREPARE_STEP + place
            value = jnp.where(slot < slots, master_ref[place], 0.0).astype(jnp.bfloat16)
            table_ref[place * half_rows : (place + 1) * half_rows, :] = value

            block = plan_ref[slot]
            ids = plan_ref[steps * PREPARE_STEP] + (block - blocks) * (2 * half_rows)
            ids = ids + lax.broadcasted_iota(jnp.int32, (half_rows, 1), 0)
            ids_ref[place * half_rows : (place + 1) * half_rows, :] = jnp.where(
                block >= blocks, ids, -1
            )

            @pl.when((block >= 0) & (block < blocks))
            def _():
                halves_ref[block] = value

    last = (slots - 1) // PREPARE_STEP
    return pl.pallas_call(
        kernel,
        name="prepare",
        grid_spec=pltpu.PrefetchScalarGridSpec(
            num_scalar_prefetch=1,
            grid=(steps,),
            in_specs=[
                pl.BlockSpec(
                    (PREPARE_STEP, half_rows, D), lambda step, plan: (jnp.minimum(step, last), 0, 0)
                )
            ],
            out_specs=[
                pl.BlockSpec((rows, D), lambda step, plan: (step, 0)),
                pl.BlockSpec((blocks, half_rows, D), lambda step, plan: (0, 0, 0)),
                pl.BlockSpec((rows, 1), lambda step, plan: (step, 0)),
            ],
        ),
        out_shape=[
            jax.ShapeDtypeStruct((total * half_rows, D), jnp.bfloat16),
            jax.ShapeDtypeStruct((blocks, half_rows, D), jnp.bfloat16),
            jax.ShapeDtypeStruct((total * half_rows, 1), jnp.int32),
        ],
        cost_estimate=SHORT,
        compiler_params=pltpu.CompilerParams(vmem_limit_bytes=60 << 20),
    )(slot_block, master)


TILE = TILE_GROUPS * LANES
PICKED = 768


def row_of(values_ref, groups, place=0):
    rows = [values_ref[group, place : place + 1, :] for group in groups]
    return jnp.concatenate(rows, axis=1)


def tile_row(values_ref, tile):
    start = tile * TILE_GROUPS
    return row_of(values_ref, [start + place for place in range(TILE_GROUPS)])


PLAN_GROUPS = 4


def chunk_of(plan_ref, step):
    return pl.ds(pl.multiple_of(plan_ref[0] + step * ROW_STEP, 16), ROW_STEP)


def chunks_of(plan_ref):
    return (plan_ref[1] - plan_ref[0] + ROW_STEP - 1) // ROW_STEP


def whole(shape):
    return pl.BlockSpec(shape, lambda step, plan: (0,) * len(shape), pipeline_mode=pl.Buffered(1))


def last_tile(plan):
    return (plan[2] - 1) // TILE_GROUPS


def group_specs():
    return [
        pl.BlockSpec(
            (LANES, D),
            lambda step, plan, place=place: (
                plan[PLAN_GROUPS + jnp.minimum(step, last_tile(plan)) * TILE_GROUPS + place],
                0,
            ),
        )
        for place in range(TILE_GROUPS)
    ]


def powers_spec(rows):
    return pl.BlockSpec((rows, TILE), lambda step, plan: (0, jnp.minimum(step, last_tile(plan))))


def groups_of(plan_ref):
    start = PLAN_GROUPS + pl.program_id(0) * TILE_GROUPS
    return [plan_ref[start + place] for place in range(TILE_GROUPS)]


ROWS_SPEC = pl.BlockSpec((TILE, D), lambda step, plan: (step, 0))


def local_call(name, kernel, steps, plan, operands, in_specs, out_shape, out_specs, scratch):
    return pl.pallas_call(
        kernel,
        name=name,
        grid_spec=pltpu.PrefetchScalarGridSpec(
            num_scalar_prefetch=1,
            grid=(steps,),
            in_specs=in_specs,
            out_specs=out_specs,
            scratch_shapes=scratch,
        ),
        out_shape=out_shape,
        cost_estimate=SHORT,
        compiler_params=pltpu.CompilerParams(vmem_limit_bytes=60 << 20),
    )(plan, *operands)


def ones_where(condition):
    return jnp.where(condition, 1.0, 0.0).astype(jnp.bfloat16)


def picks(rank_row):
    return ones_where(lax.broadcasted_iota(jnp.int32, (PICKED, TILE), 0) == rank_row)


def rows_picked(plan_ref, step, place_row):
    start = plan_ref[0] + step * ROW_STEP
    row = lax.broadcasted_iota(jnp.int32, (ROW_STEP, PICKED), 0) + start
    return ones_where(row == place_row)


def look_up(plan, row_ids, tokens, places, table):
    rows, groups = table.shape[0], tokens.shape[0]
    steps = groups // TILE_GROUPS

    def kernel(
        plan_ref, ids_ref, tokens_ref, places_ref, table_ref, out_ref, ranks_ref, picked_ref, acc, picked
    ):
        tile = pl.program_id(0)
        few = plan_ref[3] <= PICKED

        @pl.when(tile == 0)
        def _():
            held = places_ref[...].reshape(groups, LANES) >= 0
            ones = ones_where(held)
            lane = (LANES, LANES)
            before = ones_where(
                lax.broadcasted_iota(jnp.int32, lane, 0) < lax.broadcasted_iota(jnp.int32, lane, 1)
            )
            group = (groups, groups)
            above = ones_where(
                lax.broadcasted_iota(jnp.int32, group, 1) < lax.broadcasted_iota(jnp.int32, group, 0)
            )
            totals = jnp.sum(ones.astype(jnp.float32), axis=1, keepdims=True)
            totals = jnp.broadcast_to(totals, (groups, LANES)).astype(jnp.bfloat16)
            ranks = (times(ones, before) + times(above, totals)).astype(jnp.int32)
            ranks_ref[...] = jnp.where(held, ranks, -1).reshape(groups, 1, LANES)

        @pl.when((tile == 0) & few)
        def _():
            def digits_of(step, total):
                place = tile_row(places_ref, step)
                high = lax.shift_right_arithmetic(place, 6)
                digits = jnp.concatenate([high, place - high * 64] * 4, axis=0)
                digits = digits.astype(jnp.float32).astype(jnp.bfloat16)
                return total + contract_last(digits, picks(tile_row(ranks_ref, step)))

            digits = lax.fori_loop(0, steps, digits_of, jnp.zeros((8, PICKED), jnp.float32))
            place = (digits[0:1] * 64.0 + digits[1:2]).astype(jnp.int32)
            index = lax.broadcasted_iota(jnp.int32, (1, PICKED), 1)
            place = jnp.where(index < plan_ref[3], place, -1)
            picked_ref[...] = jnp.broadcast_to(place, (8, PICKED))
            acc[:PICKED, :] = jnp.zeros((PICKED, D), jnp.float32)

            def one(step, carry):
                hits = rows_picked(plan_ref, step, place)
                acc[:PICKED, :] += contract_first(hits, table_ref[chunk_of(plan_ref, step), :])
                return carry

            lax.fori_loop(0, chunks_of(plan_ref), one, 0)
            picked[...] = acc[:PICKED, :].astype(jnp.bfloat16)

        @pl.when(few)
        def _():
            hits = picks(tile_row(ranks_ref, tile))
            out_ref[...] = contract_first(hits, picked[...]).astype(jnp.bfloat16)

        @pl.when(jnp.logical_not(few))
        def _():
            acc[...] = jnp.zeros_like(acc)
            wanted = tile_row(tokens_ref, tile)

            def one(step, carry):
                chunk = chunk_of(plan_ref, step)
                hits = ones_where(ids_ref[chunk, :] == wanted)
                acc[...] += contract_first(hits, table_ref[chunk, :])
                return carry

            lax.fori_loop(0, chunks_of(plan_ref), one, 0)
            out_ref[...] = acc[...].astype(jnp.bfloat16)

    lanes = (groups, 1, LANES)
    return local_call(
        "look_up",
        kernel,
        steps,
        plan,
        (row_ids, tokens, places, table),
        [whole((rows, 1)), whole(lanes), whole(lanes), whole((rows, D))],
        [
            jax.ShapeDtypeStruct((groups * LANES, D), jnp.bfloat16),
            jax.ShapeDtypeStruct(lanes, jnp.int32),
            jax.ShapeDtypeStruct((8, PICKED), jnp.int32),
        ],
        [ROWS_SPEC, whole(lanes), whole((8, PICKED))],
        [pltpu.VMEM((TILE, D), jnp.float32), pltpu.VMEM((PICKED, D), jnp.bfloat16)],
    )


def head_forward(plan, row_ids, labels, table, final):
    rows, groups = table.shape[0], labels.shape[0]
    steps = groups // TILE_GROUPS

    def kernel(plan_ref, ids_ref, labels_ref, table_ref, *rest):
        final_refs, (powers_ref, stats_ref, scores, hidden) = rest[:TILE_GROUPS], rest[TILE_GROUPS:]
        blank = jnp.zeros((1, TILE), jnp.float32)
        active = pl.program_id(0) <= last_tile(plan_ref)
        own = groups_of(plan_ref)

        def put(top, total, target):
            pad = jnp.zeros((5, LANES), jnp.float32)
            for place in range(TILE_GROUPS):
                lanes = slice(place * LANES, (place + 1) * LANES)
                stats_ref[own[place]] = jnp.concatenate(
                    [top[:, lanes], total[:, lanes], target[:, lanes], pad], axis=0
                )

        @pl.when(jnp.logical_not(active))
        def _():
            put(blank - 1e30, blank, blank)

        @pl.when(active)
        def _():
            wanted = row_of(labels_ref, own)
            for place, ref in enumerate(final_refs):
                hidden[place * LANES : (place + 1) * LANES, :] = ref[...]

            def first(step, carry):
                top, target = carry
                chunk = chunk_of(plan_ref, step)
                ids = ids_ref[chunk, :]
                raw = contract_last(table_ref[chunk, :], hidden[...])
                raw = jnp.where(ids >= 0, raw, -1e30)
                scores[chunk, :] = raw
                top = jnp.maximum(top, jnp.max(raw, axis=0, keepdims=True))
                target = target + jnp.sum(
                    jnp.where(ids == wanted, raw, 0.0), axis=0, keepdims=True
                )
                return (top, target)

            top, target = lax.fori_loop(0, chunks_of(plan_ref), first, (blank - 1e30, blank))

            def second(step, total):
                chunk = chunk_of(plan_ref, step)
                powers = jnp.exp(scores[chunk, :] - top)
                powers_ref[chunk, :] = powers.astype(jnp.bfloat16)
                return total + jnp.sum(powers, axis=0, keepdims=True)

            put(top, lax.fori_loop(0, chunks_of(plan_ref), second, blank), target)

    return local_call(
        "head_forward",
        kernel,
        steps,
        plan,
        (row_ids, labels, table) + (final,) * TILE_GROUPS,
        [whole((rows, 1)), whole((groups, 1, LANES)), whole((rows, D))] + group_specs(),
        [
            jax.ShapeDtypeStruct((rows, groups * LANES), jnp.bfloat16),
            jax.ShapeDtypeStruct((groups, 8, LANES), jnp.float32),
        ],
        [powers_spec(rows), whole((groups, 8, LANES))],
        [pltpu.VMEM((rows, TILE), jnp.float32), pltpu.VMEM((TILE, D), jnp.bfloat16)],
    )


def head_backward(plan, row_ids, labels, keep, stats, log_totals, table, final, powers):
    rows, groups = table.shape[0], labels.shape[0]
    steps = groups // TILE_GROUPS

    def kernel(plan_ref, ids_ref, labels_ref, keep_ref, stats_ref, logs_ref, table_ref, powers_ref, *rest):
        final_refs = rest[:TILE_GROUPS]
        grad_final_ref, grad_table_ref, acc, hidden, low, sems = rest[TILE_GROUPS:]
        tile = pl.program_id(0)
        slot = lax.rem(tile, 2)
        active = tile <= last_tile(plan_ref)

        def copies(step):
            start, side = PLAN_GROUPS + step * TILE_GROUPS, lax.rem(step, 2)
            return [
                pltpu.make_async_copy(
                    low.at[side, place],
                    grad_final_ref.at[plan_ref[start + place]],
                    sems.at[side, place],
                )
                for place in range(TILE_GROUPS)
            ]

        @pl.when(tile == 0)
        def _():
            grad_table_ref[...] = jnp.zeros_like(grad_table_ref)

        @pl.when(tile >= 2)
        def _():
            for copy in copies(tile - 2):
                copy.wait()

        acc[...] = jnp.zeros_like(acc)

        @pl.when(active)
        def _():
            own = groups_of(plan_ref)
            wanted, kept = row_of(labels_ref, own), row_of(keep_ref, own)
            tops = row_of(stats_ref, own)
            scale = jnp.exp(tops - row_of(logs_ref, own)) * kept
            for place, ref in enumerate(final_refs):
                hidden[place * LANES : (place + 1) * LANES, :] = ref[...]

            def one(step, carry):
                chunk = chunk_of(plan_ref, step)
                grads = powers_ref[chunk, :].astype(jnp.float32) * scale
                grads = grads - jnp.where(ids_ref[chunk, :] == wanted, kept, 0.0)
                grads = grads.astype(jnp.bfloat16)
                grad_table_ref[chunk, :] += times(grads, hidden[...])
                acc[...] += contract_first(grads, table_ref[chunk, :])
                return carry

            lax.fori_loop(0, chunks_of(plan_ref), one, 0)

        low[slot] = acc[...].astype(jnp.bfloat16).reshape(TILE_GROUPS, LANES, D)
        for copy in copies(tile):
            copy.start()

        @pl.when(tile == steps - 1)
        def _():
            for step in range(max(0, steps - 2), steps):
                for copy in copies(step):
                    copy.wait()

    lanes = (groups, 1, LANES)
    return local_call(
        "head_backward",
        kernel,
        steps,
        plan,
        (row_ids, labels, keep, stats, log_totals, table, powers) + (final,) * TILE_GROUPS,
        [
            whole((rows, 1)),
            whole(lanes),
            whole(lanes),
            whole((groups, 8, LANES)),
            whole((groups, 8, LANES)),
            whole((rows, D)),
            powers_spec(rows),
        ]
        + group_specs(),
        [
            jax.ShapeDtypeStruct((groups, LANES, D), jnp.bfloat16),
            jax.ShapeDtypeStruct((rows, D), jnp.float32),
        ],
        [pl.BlockSpec(memory_space=pl.ANY), whole((rows, D))],
        [
            pltpu.VMEM((TILE, D), jnp.float32),
            pltpu.VMEM((TILE, D), jnp.bfloat16),
            pltpu.VMEM((2, TILE_GROUPS, LANES, D), jnp.bfloat16),
            pltpu.SemaphoreType.DMA((2, TILE_GROUPS)),
        ],
    )


def look_back(
    plan, slot_plan, slots, row_ids, tokens, ranks, picked, grad_start, grad_table, layer_grads
):
    rows, groups = grad_table.shape[0], tokens.shape[0]
    steps = groups // TILE_GROUPS
    half_rows = layer_grads[0].shape[1]
    block = SLOT_STEP * half_rows
    kinds = len(layer_grads)

    def kernel(plan_ref, slot_ref, ids_ref, tokens_ref, ranks_ref, picked_ref, grad_ref, table_ref, *rest):
        layer_refs = rest[:kinds]
        slots_ref, squares_ref, acc, held, out_ref = rest[kinds:]
        step = pl.program_id(0)
        few = plan_ref[3] <= PICKED

        @pl.when(step == 0)
        def _():
            acc[...] = jnp.zeros_like(acc)
            squares_ref[...] = jnp.zeros_like(squares_ref)

        @pl.when((step < steps) & few)
        def _():
            acc[...] += times(picks(tile_row(ranks_ref, step)), grad_ref[...])

        @pl.when((step < steps) & jnp.logical_not(few))
        def _():
            held[step] = grad_ref[...]

        @pl.when(step >= steps)
        def _():
            start = (step - steps) * block

            @pl.when(few)
            def _():
                row = lax.broadcasted_iota(jnp.int32, (block, PICKED), 0) + start
                hits = ones_where(row == picked_ref[0:1, :])
                out_ref[...] = table_ref[...] + times(hits, acc[...].astype(jnp.bfloat16))

            @pl.when(jnp.logical_not(few))
            def _():
                out_ref[...] = table_ref[...]
                ids = ids_ref[pl.ds(pl.multiple_of(start, 16), block), :]

                def one(tile, carry):
                    hits = ones_where(ids == tile_row(tokens_ref, tile))
                    out_ref[...] += times(hits, held[tile])
                    return carry

                lax.fori_loop(0, steps, one, 0)

            for place in range(SLOT_STEP):
                slot = (step - steps) * SLOT_STEP + place
                kind = slot_ref[0, slot]
                part = slice(place * half_rows, (place + 1) * half_rows)

                for index in range(kinds):

                    @pl.when(kind == index)
                    def _():
                        layer = layer_refs[index][slot_ref[1 + index, slot]]
                        out_ref[part, :] = layer.astype(jnp.float32)

                @pl.when(kind < 0)
                def _():
                    out_ref[part, :] = jnp.zeros((half_rows, D), jnp.float32)

                slots_ref[place] = out_ref[part, :].astype(jnp.bfloat16)

            values = out_ref[...]
            squares_ref[...] += (values * values).reshape(block // 8, 8, D).sum(axis=0)

    def fixed(shape):
        return pl.BlockSpec(
            shape, lambda step, plan, slot: (0,) * len(shape), pipeline_mode=pl.Buffered(1)
        )

    lanes = (groups, 1, LANES)
    row_spec = pl.BlockSpec((block, D), lambda step, plan, slot: (jnp.maximum(step - steps, 0), 0))
    return pl.pallas_call(
        kernel,
        name="look_back",
        grid_spec=pltpu.PrefetchScalarGridSpec(
            num_scalar_prefetch=2,
            grid=(steps + -(-slots // SLOT_STEP),),
            in_specs=[
                fixed((rows, 1)),
                fixed(lanes),
                fixed(lanes),
                fixed((8, PICKED)),
                pl.BlockSpec((TILE, D), lambda step, plan, slot: (jnp.minimum(step, steps - 1), 0)),
                row_spec,
            ]
            + [fixed(grads.shape) for grads in layer_grads],
            out_specs=[
                pl.BlockSpec(
                    (SLOT_STEP, half_rows, D),
                    lambda step, plan, slot: (jnp.maximum(step - steps, 0), 0, 0),
                ),
                fixed((8, D)),
            ],
            scratch_shapes=[
                pltpu.VMEM((PICKED, D), jnp.float32),
                pltpu.VMEM((steps, TILE, D), jnp.bfloat16),
                pltpu.VMEM((block, D), jnp.float32),
            ],
        ),
        out_shape=[
            jax.ShapeDtypeStruct((slots, half_rows, D), jnp.bfloat16),
            jax.ShapeDtypeStruct((8, D), jnp.float32),
        ],
        cost_estimate=SHORT,
        compiler_params=pltpu.CompilerParams(vmem_limit_bytes=60 << 20),
    )(
        plan,
        slot_plan,
        row_ids,
        tokens,
        ranks,
        picked,
        grad_start,
        grad_table,
        *layer_grads,
    )


def grads_home(level):
    return [(2 * level, 0), (2 * level + 1, 0), (2 * level + 1, 1)]


def body(
    token_ids,
    labels,
    real_counts,
    owners,
    master,
    first_moment,
    second_moment,
    gains,
    gains_first,
    gains_second,
    mix,
    mix_first,
    mix_second,
):
    tensors = lax.axis_size("tensor")
    groups = lax.axis_size("dp")
    group = lax.axis_index("dp")
    tensor_part = lax.axis_index("tensor")
    seq_part = lax.axis_index("seq")
    slots, half_rows, _ = master.shape
    seq_count, half_len = token_ids.shape
    row_count = seq_count * half_len
    share = row_count // tensors
    head_rows = 3 * D // tensors
    out_rows = D // tensors
    unit_rows = FF // tensors
    layer_rows = head_rows + out_rows + 2 * unit_rows
    layer_blocks = layer_rows // (2 * half_rows)
    blocks = LAYERS * layer_blocks
    vocab_rows = VOCAB // tensors
    local_heads = HEADS // tensors

    slot_rank = slot_table(owners)
    block_ids = jnp.arange(owners.shape[0], dtype=jnp.int32)
    mine = owners == group
    match = (jnp.arange(slots)[:, None] == slot_rank[None, :]) & mine[None, :]
    slot_block = jnp.sum(jnp.where(match, block_ids[None, :] + 1, 0), axis=1) - 1
    spare = -(-ROW_STEP // half_rows)
    spare += -(slots + spare) % SLOT_STEP
    held = jnp.sum(jnp.where(mine, 1, 0)) * half_rows
    first_held = jnp.sum(jnp.where(mine & (block_ids < blocks), 1, 0)) * half_rows
    slot_block_all = jnp.pad(slot_block, (0, spare), constant_values=-1).astype(jnp.int32)
    third = layer_blocks // 3
    which, within = slot_block_all // third, slot_block_all % third
    homes = [home for level in range(LAYERS) for home in grads_home(level)]
    arrays = 1 + max(array for array, _ in homes)
    kind, index = jnp.full(which.shape, -1), jnp.zeros_like(which)
    for place, (array, part) in enumerate(homes):
        kind = jnp.where(which == place, array, kind)
        index = jnp.where(which == place, within + part * third, index)
    kind = jnp.where(slot_block_all >= blocks, arrays, jnp.where(slot_block_all < 0, -1, kind))
    slot_plan = jnp.stack(
        [kind] + [jnp.where(kind == array, index, 0) for array in range(arrays)]
    ).astype(jnp.int32)

    packed = jnp.concatenate(
        [
            token_ids.reshape(tensors, LANES),
            labels.reshape(tensors, LANES),
            jnp.broadcast_to(real_counts[:, None], (16 - 2 * tensors, LANES)),
        ],
        axis=0,
    )
    width = -(-(2 * tensors * groups + PLAN_GROUPS) // LANES) * LANES
    lane = jnp.arange(width)[None, :]
    ends = jnp.where(lane == 0, first_held, jnp.where(lane == 1, held, 0)).astype(jnp.int32)
    ids_all, labels_all, keep_all, places, plan, count = spread_tokens(
        packed, slot_block_all[:, None], ends, blocks, half_rows, 15
    )
    plan = plan.reshape(-1)
    order = (2, tensors, groups, share)

    first_id = (tensor_part * vocab_rows + seq_part * half_rows).astype(jnp.int32)
    table, halves, row_ids = prepare(slot_block_all, first_id, master, blocks)

    def weights_line(*starts):
        return Line([(halves, start * third, third) for start in starts], True)

    def as_table(joined):
        return joined.reshape(-1, D)

    positions = seq_part * half_len + jnp.arange(row_count) % half_len
    steps_half = jnp.arange(HEAD_DIM // 2).astype(jnp.float32)
    freqs = 10000.0 ** (-2.0 * steps_half / HEAD_DIM)
    angles = freqs[:, None] * positions.astype(jnp.float32)[None, :]
    cosine, sine = jnp.cos(angles), jnp.sin(angles)

    looked, ranks, picked = look_up(plan, row_ids, ids_all, places, table)
    looked = looked.reshape(order + (D,))
    gain = [gains[i : i + 1] for i in range(2 * LAYERS + 1)]
    piece = ((share, D), jnp.float32)

    def normed_of(total, gain_row):
        return (total[...], layer_norm_parts(total[...])[0] * gain_row[...])

    def inner_of(total, stream, gain_row):
        inner = stream + total
        return (inner, layer_norm_parts(inner)[0] * gain_row)

    def outcome_of(base, total, inner, gain_row, *rest):
        states, scalars = rest[:-1], rest[-1]
        outcome = inner + total
        stream = scalars[base + len(states)] * outcome
        for source, state in enumerate(states):
            stream = stream + scalars[base + source] * state
        return (outcome, stream, layer_norm_parts(stream)[0] * gain_row)

    start, normed, joined = reduce_rows(
        "normed", looked, (14, 18, 1), weights_line(0, 1), normed_of, [gain[0]], [], [piece]
    )
    table_one = as_table(joined)
    attention_table, up = table_one, (table_one, 1)
    tables = []
    states, streams, inners, kept_all = [start], [start], [], []
    for level in range(LAYERS):
        here, last = 3 * level, level == LAYERS - 1
        carried = [] if last else [here + 3]
        carried += [here + 1, here + 2] if level else [here + 2]
        inner, normed_two, queries, both, logs, attended, joined = tensor_step(
            f"inner_{level}",
            inner_of,
            attention_work(normed, attention_table, cosine, sine),
            (streams[level], gain[2 * level + 1]),
            (),
            [piece],
            True,
            2 if level == 0 else 15 + level,
            weights_line(*carried),
        )
        kept = (queries, both, logs, attended)
        joined = as_table(joined)
        down = (joined, len(carried) - 1)
        up = (joined, len(carried) - 2) if level else up
        tables.append((attention_table, up, down))
        attention_table = joined
        outcome, stream, normed_next, hidden, activated = tensor_step(
            f"outcome_{level}",
            partial(outcome_of, (level + 1) * (level + 2) // 2 - 1),
            unit_work(normed_two, up, down),
            [inner, gain[2 * level + 2]] + states,
            (mix,),
            [piece, piece] + ([((share, D), jnp.bfloat16)] if last else []),
            not last,
            3 + level,
        )
        inners.append(inner)
        kept_all.append((normed, kept, normed_two, (hidden, activated)))
        states.append(outcome)
        streams.append(stream)
        normed = normed_next

    final_all = gather_all(normed, 3 + LAYERS)[0].reshape(-1, D)
    powers, stats = head_forward(plan, row_ids, labels_all, table, final_all)
    home, log_totals = join_stats(
        stats.reshape((2, tensors, groups, 8, LANES)), 4 + LAYERS
    )
    grad_final, grad_table = head_backward(
        plan,
        row_ids,
        labels_all,
        keep_all,
        stats,
        log_totals.reshape(-1, 8, LANES),
        table,
        final_all,
        powers,
    )
    grad_final = grad_final.reshape(order + (D,))

    row = ((1, D), jnp.float32)

    def top_of(total, stream, gain_row, scalars):
        grad_top, grad_gain = norm_pull(total[...], gain_row[...], stream[...])
        grad_state = scalars[MIX_WEIGHTS - 1] * grad_top
        return (grad_top, grad_state, grad_gain, grad_state)

    def inner_back(total, grad_out, inner, gain_row):
        grad, grad_gain = norm_pull(total, gain_row, inner)
        grad = grad_out + grad
        return (grad, grad_gain, grad)

    def stream_back(block, total, grad_inner, stream, gain_row, *rest):
        grad_ys, scalars = rest[:-1], rest[-1]
        grad, grad_gain = norm_pull(total, gain_row, stream)
        grad = grad_inner + grad
        state = grad if block == 0 else scalars[block * (block + 1) // 2 - 1 + block] * grad
        for offset, grad_y in enumerate(grad_ys):
            later = block + 1 + offset
            state = state + scalars[later * (later + 1) // 2 - 1 + block] * grad_y
        return (grad, state, grad_gain, state)

    grad_ys = [None] * (LAYERS + 1)
    gain_grads = [None] * (2 * LAYERS + 1)
    layer_grads, attention_grads = [None] * (2 * LAYERS), None
    grad_ys[LAYERS], grad_state, gain_grads[2 * LAYERS], grad_branch = reduce_rows(
        "top_back",
        grad_final,
        (0, 0, 5 + LAYERS),
        None,
        top_of,
        [streams[LAYERS], gain[2 * LAYERS]],
        [mix],
        [piece, piece, row],
    )
    for level in reversed(range(LAYERS)):
        normed, kept, normed_two, unit_kept = kept_all[level]
        attention_table, up, down = tables[level]
        grad_inner, gain_grads[2 * level + 1], grad_attn, unit_grads, *summed = tensor_step(
            f"inner_back_{level}",
            inner_back,
            unit_back_work(grad_branch, normed_two, up, down, unit_kept, half_rows),
            (grad_state, inners[level], gain[2 * level + 1]),
            (),
            [piece, row],
            True,
            6 + LAYERS if level == 0 else 19 + level,
            None if attention_grads is None else Line([(attention_grads, 0, third)], False),
        )
        if summed:
            layer_grads[2 * (level + 1)] = summed[0]
        grad_ys[level], grad_state, gain_grads[2 * level], grad_branch, attention_grads, summed = (
            tensor_step(
                f"stream_back_{level}",
                partial(stream_back, level),
                attention_back_work(
                    grad_attn, normed, attention_table, kept, cosine, sine, half_rows
                ),
                [grad_inner, streams[level], gain[2 * level]] + grad_ys[level + 1 :],
                (mix,),
                [piece, piece, row] + ([] if level else [((share, D), jnp.bfloat16)]),
                level > 0,
                7 + LAYERS + level,
                Line([(unit_grads, 0, 2 * third)], False),
            )
        )
        layer_grads[2 * level + 1] = summed

    grad_start_all, layer_grads[0] = gather_all(
        grad_branch, 13, Line([(attention_grads, 0, third)], False)
    )
    grad_start_all = grad_start_all.reshape(-1, D)
    owned, table_squares = look_back(
        plan,
        slot_plan,
        slots,
        row_ids,
        ids_all,
        ranks,
        picked,
        grad_start_all,
        grad_table,
        layer_grads,
    )
    keep = jnp.where(
        tensor_part * share + jnp.arange(share) < real_counts[0], 1.0, 0.0
    ).astype(jnp.float32)
    news = finish(
        gain_grads,
        states,
        grad_ys[1:],
        home,
        keep[None],
        table_squares,
        count,
        (gains, gains_first, gains_second, mix[None], mix_first[None], mix_second[None]),
        7 + 2 * LAYERS,
    )
    new_gains, new_gains_first, new_gains_second = news[:3]
    new_mix, new_mix_first, new_mix_second = [value[0] for value in news[3:6]]
    loss_sum, clip_norm = news[6][0, 0], news[6][0, 1]
    token_count = count[0, 0]
    owned = owned.astype(jnp.float32) * news[7][0, 0]
    new_master, new_first, new_second = adam_update(
        master, first_moment, second_moment, owned, RATE_MATRIX, DECAY_MATRIX
    )
    return (
        new_master,
        new_first,
        new_second,
        new_gains,
        new_gains_first,
        new_gains_second,
        new_mix,
        new_mix_first,
        new_mix_second,
        loss_sum,
        token_count,
        clip_norm,
    )


def solution(mesh):
    return jax.shard_map(
        body,
        mesh=mesh,
        in_specs=(
            P("dp", "seq"),
            P("dp", "seq"),
            P(("dp", "seq")),
            P(),
            P("dp", ("tensor", "seq"), None),
            P("dp", ("tensor", "seq"), None),
            P("dp", ("tensor", "seq"), None),
            P(),
            P(),
            P(),
            P(),
            P(),
            P(),
        ),
        out_specs=(
            P("dp", ("tensor", "seq"), None),
            P("dp", ("tensor", "seq"), None),
            P("dp", ("tensor", "seq"), None),
            P(),
            P(),
            P(),
            P(),
            P(),
            P(),
            P(),
            P(),
            P(),
        ),
        check_vma=False,
    )
```

```python
from functools import partial

import jax
import jax.numpy as jnp
from jax import lax
from jax.experimental import pallas as pl
from jax.experimental.pallas import tpu as pltpu
from jax.sharding import PartitionSpec as P

D = 768
HEADS = 12
HEAD_DIM = 64
FF = 3072
VOCAB = 50304
LAYERS = 2
STEP_COUNT = 10
MIX_WEIGHTS = 5


EPS_NORM = 1e-05
CLIP_NORM = 0.01
BETA_ONE = 0.9
BETA_TWO = 0.95
ADAM_EPS = 1e-08
RATE_MATRIX = 0.04
RATE_SMALL = 0.4
DECAY_MATRIX = 0.1


def contract_last(left, right):
    return lax.dot_general(
        left, right, (((1,), (1,)), ((), ())), preferred_element_type=jnp.float32
    )


def contract_first(left, right):
    return lax.dot_general(
        left, right, (((0,), (0,)), ((), ())), preferred_element_type=jnp.float32
    )


def slot_table(owners):
    ranks = jnp.arange(owners.shape[0])
    same = (owners[None, :] == owners[:, None]) & (ranks[None, :] < ranks[:, None])
    return jnp.sum(jnp.where(same, 1, 0), axis=1).astype(jnp.int32)


def adam_update(weight, first, second, grad, rate, decay):
    first = BETA_ONE * first + (1.0 - BETA_ONE) * grad
    second = BETA_TWO * second + (1.0 - BETA_TWO) * grad * grad
    first_hat = first / (1.0 - BETA_ONE**STEP_COUNT)
    second_hat = second / (1.0 - BETA_TWO**STEP_COUNT)
    weight = weight - rate * (first_hat / (jnp.sqrt(second_hat) + ADAM_EPS) + decay * weight)
    return (weight, first, second)


MESH = pl.DeviceIdType.MESH
ROW_STEP = 400
TILE_GROUPS = 8
LANES = 128
SHORT = pl.CostEstimate(flops=1000, bytes_accessed=1000, transcendentals=0)
LONG = pl.CostEstimate(flops=10**12, bytes_accessed=1 << 30, transcendentals=0)


def meet(peers):
    gate = pltpu.get_barrier_semaphore()
    for peer in peers:
        pl.semaphore_signal(gate, inc=1, device_id=peer, device_id_type=MESH)
    pl.semaphore_wait(gate, len(peers))


def others(axis):
    count, me = lax.axis_size(axis), lax.axis_index(axis)
    return [lax.rem(me + step, count) for step in range(1, count)]


def behind(axis, step):
    count, me = lax.axis_size(axis), lax.axis_index(axis)
    return lax.rem(me + count - step, count)


def send(source, target, send_sem, recv_sem, device):
    copy = pltpu.make_async_remote_copy(
        src_ref=source,
        dst_ref=target,
        send_sem=send_sem,
        recv_sem=recv_sem,
        device_id=device,
        device_id_type=MESH,
    )
    copy.start()
    return copy


def layer_norm_parts(stream):
    center = stream - jnp.mean(stream, -1, keepdims=True)
    inverse = lax.rsqrt(jnp.mean(center * center, -1, keepdims=True) + EPS_NORM)
    return center * inverse, inverse


def norm_pull(grad_normed, gain, stream):
    scaled, inverse = layer_norm_parts(stream)
    grad_scaled = grad_normed * gain
    grad_stream = inverse * (
        grad_scaled
        - jnp.mean(grad_scaled, -1, keepdims=True)
        - scaled * jnp.mean(grad_scaled * scaled, -1, keepdims=True)
    )
    return grad_stream, jnp.sum(grad_normed * scaled, axis=0, keepdims=True)


class Work:
    def __init__(self, before, during, operands, specs, outs, scratch, after=None, twins=False):
        self.before, self.during, self.after, self.twins = before, during, after, twins
        self.operands, self.specs, self.outs, self.scratch = operands, specs, outs, scratch


def tensor_step(name, function, work, extras, scalars, outs, gather, collective_id, line=None):
    parts = lax.axis_size("tensor")
    share = extras[0].shape[0]
    reduce = work is not None
    work = work or Work(None, None, [], [], [], [])
    arrays = list(work.operands) + list(extras)
    parts_of = list(work.specs) + [None] * len(extras)

    def kernel(*refs):
        refs = list(refs)

        def take(count):
            return [refs.pop(0) for _ in range(count)]

        array_refs = take(len(arrays))
        scalar_refs = take(len(scalars))
        source_refs = take(len(line.operands)) if line else []
        out_refs = take(len(outs))
        (full,) = take(1) if gather else [None]
        work_outs = take(len(work.outs))
        (joined,) = take(1) if line else [None]
        held = take(len(arrays))
        (load_sems,) = take(1)
        loads = []
        for index, (ref, part, target) in enumerate(zip(array_refs, parts_of, held)):
            if part:
                ref = ref.at[pl.ds(part[0] * part[1], part[0])]
            loads.append(pltpu.make_async_copy(ref, target, load_sems.at[index]))
            loads[-1].start()
        work_refs, extra_refs = held[: len(work.operands)], held[len(work.operands) :]
        send_sems, recv_sems = take(2)
        partial_ref, outgoing, arrived = take(3) if reduce else [None] * 3
        if line:
            line.bind(source_refs, joined, take(len(line.scratch)))
            line.load()

        def tick(count=1):
            if line:
                line.steps(count)

        me, side = lax.axis_index("tensor"), lax.axis_index("seq")
        peers = others("tensor")
        twin = {"seq": 1 - side}
        twins = work.twins or (line and line.share)
        meet(
            [{"tensor": peer} for peer in peers]
            + [twin] * bool(twins)
            + ([{"dp": peer} for peer in others("dp")] if line else [])
        )
        if line:
            line.begin()
        for load in loads:
            load.wait()
        total = None
        if reduce:
            work.before(work_refs, work_outs, refs, partial_ref, tick)
            copies = []
            for step, peer in enumerate(peers):
                rows = pl.ds(pl.multiple_of(peer * share, share), share)
                outgoing[step] = partial_ref[rows, :].astype(jnp.bfloat16)
                copies.append(
                    send(
                        outgoing.at[step],
                        arrived.at[step],
                        send_sems.at[0, step],
                        recv_sems.at[0, step],
                        {"tensor": peer},
                    )
                )
            if work.during:
                work.during(work_refs, work_outs, refs)
            tick(4)
            total = partial_ref[pl.ds(pl.multiple_of(me * share, share), share), :]
            for step, copy in enumerate(copies):
                copy.wait()
                total = total + arrived[step].astype(jnp.float32)
        results = function(total, *[ref[...] for ref in extra_refs], *scalar_refs)
        for ref, value in zip(out_refs, results):
            ref[...] = value.astype(ref.dtype)
        if gather:
            full[me] = results[len(outs)].astype(jnp.bfloat16)
            copies = [
                send(
                    full.at[me],
                    full.at[me],
                    send_sems.at[1, step],
                    recv_sems.at[1, step],
                    {"tensor": peer},
                )
                for step, peer in enumerate(peers)
            ]
        if work.after:
            work.after(work_refs, work_outs, refs)
        tick(None)
        if gather:
            for copy in copies:
                copy.wait()
        if line:
            line.end()

    vmem = pl.BlockSpec(memory_space=pltpu.VMEM)
    smem = pl.BlockSpec(memory_space=pltpu.SMEM)
    shapes = [jax.ShapeDtypeStruct(shape, dtype) for shape, dtype in outs]
    if gather:
        shapes.append(jax.ShapeDtypeStruct((parts, share, D), jnp.bfloat16))
    shapes += [jax.ShapeDtypeStruct(shape, dtype) for shape, dtype in work.outs]
    out_specs = [vmem] * len(shapes)
    operands = arrays + list(scalars)
    in_specs = [pl.BlockSpec(memory_space=pl.ANY)] * len(arrays) + [smem] * len(scalars)
    dma = pltpu.SemaphoreType.DMA
    buffers = [
        pltpu.VMEM((part[0], D) if part else array.shape, array.dtype)
        for array, part in zip(arrays, parts_of)
    ]
    buffers += [dma((len(arrays),))] + [dma((2, parts - 1))] * 2
    if reduce:
        buffers += [pltpu.VMEM((parts * share, D), jnp.float32)]
        buffers += [pltpu.VMEM((parts - 1, share, D), jnp.bfloat16)] * 2
    if line:
        operands += line.operands
        in_specs += line.in_specs
        shapes.append(line.out_shape)
        out_specs.append(line.out_spec)
        buffers += line.scratch
    return pl.pallas_call(
        kernel,
        name=name,
        grid=(1,),
        out_shape=shapes,
        in_specs=in_specs,
        out_specs=out_specs,
        scratch_shapes=buffers + list(work.scratch),
        cost_estimate=SHORT,
        compiler_params=pltpu.CompilerParams(
            collective_id=collective_id, has_side_effects=True, vmem_limit_bytes=60 << 20
        ),
    )(*operands)


VMEM_SPEC = pl.BlockSpec(memory_space=pltpu.VMEM)


def part_spec(rows, index):
    return rows, index


def turn(block, cosine, sine):
    half = HEAD_DIM // 2
    first, second = block[:half], block[half:]
    return jnp.concatenate(
        [first * cosine - second * sine, second * cosine + first * sine], axis=0
    )


def times(left, right):
    return jnp.dot(left, right, preferred_element_type=jnp.float32)


def masks_of(count, side):
    key = lax.broadcasted_iota(jnp.int32, (count, count), 0)
    query = lax.broadcasted_iota(jnp.int32, (count, count), 1)
    far = jnp.where(side == 0, -1e30, 0.0).astype(jnp.float32)
    return far, jnp.where(key <= query, 0.0, -1e30)


def scores_of(keys_values, head, queries, masks):
    span = slice(head * HEAD_DIM, (head + 1) * HEAD_DIM)
    scale = HEAD_DIM ** (-0.5)
    far = contract_first(keys_values[0, 0, span, :], queries) * scale + masks[0]
    own = contract_first(keys_values[1, 0, span, :], queries) * scale + masks[1]
    return far, own


def attention_work(normed, table, cosine, sine):
    parts, share, _ = normed.shape
    count = parts * share
    width = D // parts
    heads = width // HEAD_DIM

    def before(ins, outs, scratch, partial_ref, tick):
        normed_ref, qkv_ref, out_ref, cosine_ref, sine_ref = ins
        queries_ref, both, logs_ref, attended_ref = outs
        send_sem, recv_sem = scratch
        side = lax.axis_index("seq")
        cosine, sine = cosine_ref[...], sine_ref[...]
        rows = normed_ref[...].reshape(count, D)
        joined = contract_last(qkv_ref[...], rows)
        for head in range(heads):
            span = slice(head * HEAD_DIM, (head + 1) * HEAD_DIM)
            keys = joined[width + head * HEAD_DIM : width + (head + 1) * HEAD_DIM]
            both[1, 0, span, :] = turn(keys, cosine, sine).astype(jnp.bfloat16)
        both[1, 1] = joined[2 * width :].astype(jnp.bfloat16)
        copy = pltpu.make_async_remote_copy(
            src_ref=both.at[1],
            dst_ref=both.at[0],
            send_sem=send_sem,
            recv_sem=recv_sem,
            device_id={"seq": 1 - side},
            device_id_type=MESH,
        )

        copy.start()
        for head in range(heads):
            span = slice(head * HEAD_DIM, (head + 1) * HEAD_DIM)
            queries_ref[span, :] = turn(joined[span], cosine, sine).astype(jnp.bfloat16)

        copy.wait()
        masks = masks_of(count, side)
        for head in range(heads):
            span = slice(head * HEAD_DIM, (head + 1) * HEAD_DIM)
            far, own = scores_of(both, head, queries_ref[span, :], masks)
            peak = jnp.maximum(
                jnp.max(far, axis=0, keepdims=True), jnp.max(own, axis=0, keepdims=True)
            )
            far, own = jnp.exp(far - peak), jnp.exp(own - peak)
            total = jnp.sum(far, axis=0, keepdims=True) + jnp.sum(own, axis=0, keepdims=True)
            logs_ref[head] = peak + jnp.log(total)
            inverse = 1.0 / total
            attended = times(both[0, 1, span, :], (far * inverse).astype(jnp.bfloat16))
            attended += times(both[1, 1, span, :], (own * inverse).astype(jnp.bfloat16))
            attended_ref[span, :] = attended.astype(jnp.bfloat16)
            tick(2)
        partial_ref[...] = contract_first(attended_ref[...], out_ref[...])

    low = jnp.bfloat16
    return Work(
        before,
        None,
        [normed, table, table, cosine, sine],
        [None, part_spec(3 * width, 0), part_spec(width, 3), None, None],
        [
            ((width, count), low),
            ((2, 2, width, count), low),
            ((heads, 1, count), jnp.float32),
            ((width, count), low),
        ],
        [pltpu.SemaphoreType.DMA, pltpu.SemaphoreType.DMA],
        twins=True,
    )


def fold_copy(own, near, send_sems, recv_sems, index):
    side = lax.axis_index("seq")
    return pltpu.make_async_remote_copy(
        src_ref=own.at[index, :, 1 - side],
        dst_ref=near.at[index],
        send_sem=send_sems.at[index],
        recv_sem=recv_sems.at[index],
        device_id={"seq": 1 - side},
        device_id_type=MESH,
    )


def add_halves(own, near, out, start):
    side = lax.axis_index("seq")

    def one(block, carry):
        value = own[block, side].astype(jnp.float32) + near[block].astype(jnp.float32)
        out[start + block] = value.astype(jnp.bfloat16)
        return carry

    lax.fori_loop(0, near.shape[0], one, 0)


def attention_back_work(grad, normed, table, kept, cosine, sine, half_rows):
    parts, share, _ = normed.shape
    count = parts * share
    width = D // parts
    heads = width // HEAD_DIM
    queries, both, logs, attended = kept
    blocks = 4 * width // (2 * half_rows)

    def before(ins, outs, scratch, partial_ref, tick):
        grad_ref, _, qkv_ref, out_ref, queries_ref, both, logs_ref, _, cosine_ref, sine_ref = ins
        back, came, grad_joined, send_sem, recv_sem = scratch[:5]
        side = lax.axis_index("seq")
        cosine, sine = cosine_ref[...], -sine_ref[...]
        scale = HEAD_DIM ** (-0.5)
        grads = contract_last(out_ref[...], grad_ref[...].reshape(count, D)).astype(jnp.bfloat16)
        own_grads = []
        masks = masks_of(count, side)
        for head in range(heads):
            span = slice(head * HEAD_DIM, (head + 1) * HEAD_DIM)
            head_queries, head_grads = queries_ref[span, :], grads[span]
            far, own = scores_of(both, head, head_queries, masks)
            far, own = jnp.exp(far - logs_ref[head]), jnp.exp(own - logs_ref[head])
            far_grad = contract_first(both[0, 1, span, :], head_grads)
            own_grad = contract_first(both[1, 1, span, :], head_grads)
            mean = jnp.sum(far * far_grad, axis=0, keepdims=True)
            mean += jnp.sum(own * own_grad, axis=0, keepdims=True)
            far_grad = (far * (far_grad - mean)).astype(jnp.bfloat16)
            own_grad = (own * (own_grad - mean)).astype(jnp.bfloat16)
            far, own = far.astype(jnp.bfloat16), own.astype(jnp.bfloat16)
            back[0, span, :] = (contract_last(head_queries, far_grad) * scale).astype(jnp.bfloat16)
            back[1, span, :] = contract_last(head_grads, far).astype(jnp.bfloat16)
            query_grad = times(both[0, 0, span, :], far_grad) + times(both[1, 0, span, :], own_grad)
            grad_joined[span, :] = turn(query_grad * scale, cosine, sine).astype(jnp.bfloat16)
            own_grads.append(
                (contract_last(head_queries, own_grad) * scale, contract_last(head_grads, own))
            )
            tick(2)
        copy = send(back, came, send_sem, recv_sem, {"seq": 1 - side})
        copy.wait()
        for head, (key_grad, value_grad) in enumerate(own_grads):
            span = slice(head * HEAD_DIM, (head + 1) * HEAD_DIM)
            key_grad = key_grad + came[0, span, :].astype(jnp.float32)
            value_grad = value_grad + came[1, span, :].astype(jnp.float32)
            start = width + head * HEAD_DIM
            grad_joined[start : start + HEAD_DIM, :] = turn(key_grad, cosine, sine).astype(
                jnp.bfloat16
            )
            start += width
            grad_joined[start : start + HEAD_DIM, :] = value_grad.astype(jnp.bfloat16)
        partial_ref[...] = contract_first(grad_joined[...], qkv_ref[...])

    def during(ins, outs, scratch):
        grad_ref, normed_ref, attended_ref = ins[0], ins[1], ins[7]
        grad_joined = scratch[2]
        own, near, fold_send, fold_recv = scratch[5:]
        value = times(grad_joined[...], normed_ref[...].reshape(count, D)).astype(jnp.bfloat16)
        part = 3 * blocks // 4
        own[0, :part] = value.reshape(part, 2, half_rows, D)
        value = times(attended_ref[...], grad_ref[...].reshape(count, D)).astype(jnp.bfloat16)
        own[0, part:] = value.reshape(blocks - part, 2, half_rows, D)
        fold_copy(own, near, fold_send, fold_recv, 0).start()

    def after(ins, outs, scratch):
        own, near, fold_send, fold_recv = scratch[5:]
        fold_copy(own, near, fold_send, fold_recv, 0).wait()
        add_halves(own.at[0], near.at[0], outs[0], 0)

    low = jnp.bfloat16
    dma = pltpu.SemaphoreType.DMA
    return Work(
        before,
        during,
        [grad, normed, table, table, queries, both, logs, attended, cosine, sine],
        [None, None, part_spec(3 * width, 0), part_spec(width, 3)] + [None] * 6,
        [((blocks, half_rows, D), low)],
        [
            pltpu.VMEM((2, width, count), low),
            pltpu.VMEM((2, width, count), low),
            pltpu.VMEM((3 * width, count), low),
            dma,
            dma,
            pltpu.VMEM((1, blocks, 2, half_rows, D), low),
            pltpu.VMEM((1, blocks, half_rows, D), low),
            dma((1,)),
            dma((1,)),
        ],
        after,
        True,
    )


def gelu(hidden):
    return jax.nn.gelu(hidden, approximate=True)


def unit_work(normed, up, down):
    parts, share, _ = normed.shape
    count = parts * share
    units = FF // parts

    def before(ins, outs, scratch, partial_ref, tick):
        normed_ref, up_ref, down_ref = ins
        hidden_ref, activated_ref = outs
        hidden = contract_last(up_ref[...], normed_ref[...].reshape(count, D))
        hidden_ref[...] = hidden
        activated_ref[...] = gelu(hidden).astype(jnp.bfloat16)
        tick(2)
        partial_ref[...] = contract_first(activated_ref[...], down_ref[...])

    return Work(
        before,
        None,
        [normed, up[0], down[0]],
        [None, part_spec(units, up[1]), part_spec(units, down[1])],
        [((units, count), jnp.float32), ((units, count), jnp.bfloat16)],
        [],
    )


def unit_back_work(grad, normed, up, down, kept, half_rows):
    parts, share, _ = normed.shape
    count = parts * share
    units = FF // parts
    hidden, activated = kept
    blocks = units // (2 * half_rows)

    def before(ins, outs, scratch, partial_ref, tick):
        grad_ref, _, up_ref, down_ref, hidden_ref, _ = ins
        grad_hidden = scratch[0]
        grad_act = contract_last(down_ref[...], grad_ref[...].reshape(count, D))
        _, pull = jax.vjp(gelu, hidden_ref[...])
        grad_hidden[...] = pull(grad_act)[0].astype(jnp.bfloat16)
        tick(2)
        partial_ref[...] = contract_first(grad_hidden[...], up_ref[...])

    def during(ins, outs, scratch):
        grad_ref, normed_ref, _, _, _, activated_ref = ins
        grad_hidden, own, near, fold_send, fold_recv = scratch
        value = times(grad_hidden[...], normed_ref[...].reshape(count, D))
        own[0] = value.astype(jnp.bfloat16).reshape(own.shape[1:])
        fold_copy(own, near, fold_send, fold_recv, 0).start()
        value = times(activated_ref[...], grad_ref[...].reshape(count, D))
        own[1] = value.astype(jnp.bfloat16).reshape(own.shape[1:])
        fold_copy(own, near, fold_send, fold_recv, 1).start()

    def after(ins, outs, scratch):
        _, own, near, fold_send, fold_recv = scratch
        for index in range(2):
            fold_copy(own, near, fold_send, fold_recv, index).wait()
            add_halves(own.at[index], near.at[index], outs[0], index * blocks)

    low, dma = jnp.bfloat16, pltpu.SemaphoreType.DMA
    return Work(
        before,
        during,
        [grad, normed, up[0], down[0], hidden, activated],
        [None, None, part_spec(units, up[1]), part_spec(units, down[1])]
        + [None] * 2,
        [((2 * blocks, half_rows, D), low)],
        [
            pltpu.VMEM((units, count), low),
            pltpu.VMEM((2, blocks, 2, half_rows, D), low),
            pltpu.VMEM((2, blocks, half_rows, D), low),
            dma((2,)),
            dma((2,)),
        ],
        after,
        True,
    )


LINE_BLOCKS = 1
LINE_LAG = 3
LINE_SHARE = 4


class Line:
    def __init__(self, sources, share):
        self.groups = lax.axis_size("dp")
        self.sources, self.share = sources, share
        count = sum(size for _, _, size in sources)
        _, half_rows, _ = sources[0][0].shape
        self.half = (count, half_rows, D)
        self.chunks = count // LINE_BLOCKS
        self.operands = [array for array, _, _ in sources]
        self.in_specs = [pl.BlockSpec(memory_space=pl.ANY)] * len(sources)
        dma = pltpu.SemaphoreType.DMA
        out = (count, 2, half_rows, D) if share else self.half
        self.out_shape = jax.ShapeDtypeStruct(out, jnp.bfloat16)
        self.out_spec = pl.BlockSpec(memory_space=pl.ANY if share else pltpu.VMEM)
        self.scratch = [
            pltpu.VMEM(self.half, jnp.bfloat16),
            pltpu.VMEM((2,) + self.half, jnp.bfloat16),
            pltpu.VMEM((2,) + self.half, jnp.bfloat16),
            dma((len(sources),)),
            dma((2,)),
            dma((2, self.chunks)),
        ]
        if share:
            self.scratch += [pltpu.VMEM(self.half, jnp.bfloat16)] + [dma] * 3

    def bind(self, source_refs, out_ref, refs):
        self.source_refs, self.out = source_refs, out_ref
        self.own, self.came, self.going, self.own_sems, self.send_sems, self.recv_sems = refs[:6]
        self.total = out_ref
        if self.share:
            self.total, self.keep_sem, self.twin_send, self.twin_recv = refs[6:]
        self.done = 0
        self.group = lax.axis_index("dp")
        self.first = jnp.where(self.group < self.groups // 2, 0, 1)

    def at(self, chunk):
        return pl.ds(chunk * LINE_BLOCKS, LINE_BLOCKS)

    def comes(self, way):
        return jnp.where(way == 0, self.group > 0, self.group < self.groups - 1)

    def goes(self, way):
        return jnp.where(way == 0, self.group < self.groups - 1, self.group > 0)

    def copy(self, source, way, chunk):
        target = jnp.where(way == 0, self.group + 1, self.group - 1)
        return pltpu.make_async_remote_copy(
            src_ref=source,
            dst_ref=self.came.at[way, self.at(chunk)],
            send_sem=self.send_sems.at[way],
            recv_sem=self.recv_sems.at[way, chunk],
            device_id={"dp": target},
            device_id_type=MESH,
        )

    def load(self):
        self.loads, place = [], 0
        for index, (ref, (_, start, size)) in enumerate(zip(self.source_refs, self.sources)):
            copy = pltpu.make_async_copy(
                ref.at[pl.ds(start, size)], self.own.at[pl.ds(place, size)], self.own_sems.at[index]
            )
            copy.start()
            self.loads.append(copy)
            place += size

    def begin(self):
        for copy in self.loads:
            copy.wait()
        for way in range(2):

            @pl.when(jnp.logical_not(self.comes(way)))
            def _():
                self.came[way] = jnp.zeros(self.half, jnp.bfloat16)

                def start(chunk, carry):
                    self.copy(self.own.at[self.at(chunk)], way, chunk).start()
                    return carry

                lax.fori_loop(0, self.chunks, start, 0)

    def twin_copy(self, rows):
        side = lax.axis_index("seq")
        return pltpu.make_async_remote_copy(
            src_ref=self.total.at[rows],
            dst_ref=self.out.at[rows, side],
            send_sem=self.twin_send,
            recv_sem=self.twin_recv,
            device_id={"seq": 1 - side},
            device_id_type=MESH,
        )

    def keep_copy(self, rows):
        return pltpu.make_async_copy(
            self.total.at[rows], self.out.at[rows, lax.axis_index("seq")], self.keep_sem
        )

    def pass_on(self, way, chunk):
        rows = self.at(chunk)

        @pl.when(self.comes(way))
        def _():
            copy = self.copy(self.going.at[way, rows], way, chunk)
            copy.wait_recv()

            @pl.when(self.goes(way))
            def _():
                value = self.own[rows].astype(jnp.float32) + self.came[way, rows].astype(jnp.float32)
                self.going[way, rows] = value.astype(jnp.bfloat16)
                copy.start()

    def step(self, index):
        @pl.when(index < self.chunks)
        def _():
            self.pass_on(self.first, index)

        @pl.when(index >= LINE_LAG)
        def _():
            chunk = index - LINE_LAG
            rows = self.at(chunk)
            self.pass_on(1 - self.first, chunk)
            value = self.own[rows].astype(jnp.float32)
            value = value + self.came[0, rows].astype(jnp.float32)
            value = value + self.came[1, rows].astype(jnp.float32)
            self.total[rows] = value.astype(jnp.bfloat16)
            if self.share:

                @pl.when(lax.rem(chunk, LINE_SHARE) == LINE_SHARE - 1)
                def _():
                    done = pl.ds(chunk - (LINE_SHARE - 1), LINE_SHARE)
                    self.keep_copy(done).start()
                    self.twin_copy(done).start()

    def steps(self, count=None):
        last = self.chunks + LINE_LAG
        stop = last if count is None else min(self.done + count, last)

        def one(index, carry):
            self.step(index)
            return carry

        lax.fori_loop(self.done, stop, one, 0)
        self.done = stop

    def end(self):
        for way in range(2):

            @pl.when(self.goes(way))
            def _():
                whole_copy = pltpu.make_async_remote_copy(
                    src_ref=self.going.at[way],
                    dst_ref=self.came.at[way],
                    send_sem=self.send_sems.at[way],
                    recv_sem=self.recv_sems.at[way, 0],
                    device_id={"dp": self.group},
                    device_id_type=MESH,
                )
                whole_copy.wait_send()

        if self.share:
            everything = pl.ds(0, self.half[0])
            self.keep_copy(everything).wait()
            self.twin_copy(everything).wait()


def reduce_all(terms, collective_id, line=None, tail=None):
    _, tensors, groups, count, _ = terms.shape
    half = count // 2
    function, extras, scalars, outs = tail or (None, [], [], [])
    extra_specs = [VMEM_SPEC] * len(extras)
    extra_specs += [pl.BlockSpec(memory_space=pltpu.SMEM)] * len(scalars)
    extras = list(extras) + list(scalars)

    def kernel(*refs):
        refs = list(refs)
        terms_ref = refs.pop(0)
        source_refs = [refs.pop(0) for _ in line.operands] if line else []
        extra_refs = [refs.pop(0) for _ in extras]
        out_refs = [refs.pop(0) for _ in range(len(outs) or 1)]
        full = refs.pop(0) if tail else None
        joined_ref = refs.pop(0) if line else None
        tail_sems = [refs.pop(0) for _ in range(2)] if tail else None
        (
            near, own, mid, sums, mid_in, far, far_in,
            own_sems, near_send, near_recv, mid_send, mid_recv, far_send, far_recv,
        ) = refs[:14]
        if line:
            line.bind(source_refs, joined_ref, refs[14:])
            line.load()
        group, part, side = lax.axis_index("dp"), lax.axis_index("tensor"), lax.axis_index("seq")
        twin = 1 - side
        parts = others("tensor")
        order = others("dp") + [group]
        meet(
            [{"seq": twin}]
            + [{"tensor": peer} for peer in parts]
            + [{"dp": peer} for peer in order[:-1]]
        )
        waits, near_copies, own_copies = [], [], []
        for place, target in enumerate(order):
            near_copies.append(
                send(
                    terms_ref.at[twin, :, target],
                    near.at[place],
                    near_send.at[place],
                    near_recv.at[place],
                    {"seq": twin},
                )
            )
            copy = pltpu.make_async_copy(
                terms_ref.at[side, :, target], own.at[place], own_sems.at[place]
            )
            copy.start()
            own_copies.append(copy)
        if line:
            line.begin()
        beside = lax.rem(part + 1, 2) + part - lax.rem(part, 2)
        across = lax.rem(part + 2, 4)
        corner = 3 - part
        upper, lower = pl.ds(0, half), pl.ds(half, half)
        first_copies, second_copies = [], []

        def hand(place, index, source, target):
            return send(
                source,
                mid_in.at[place, index],
                mid_send.at[place, index],
                mid_recv.at[place, index],
                {"tensor": target},
            )

        for place in range(groups):
            near_copies[place].wait_recv()
            own_copies[place].wait()
            if line and place == 2:
                line.steps(1)
            for slot in range(tensors):
                mid[place, slot] = (
                    own[place, slot].astype(jnp.float32) + near[place, slot].astype(jnp.float32)
                ).astype(jnp.bfloat16)
            first_copies.append(
                [
                    hand(place, 0, mid.at[place, corner, upper], beside),
                    hand(place, 1, mid.at[place, corner, lower], across),
                    hand(place, 2, mid.at[place, beside, upper], beside),
                    hand(place, 3, mid.at[place, across, lower], across),
                ]
            )
        for place in range(groups):
            if line and place < 4:
                line.steps(3)
            copies = []
            for index, slot, rows, target in ((0, across, upper, across), (1, beside, lower, beside)):
                first_copies[place][index].wait_recv()
                value = mid[place, slot, rows].astype(jnp.float32)
                value = value + mid_in[place, index].astype(jnp.float32)
                sums[place, index] = value.astype(jnp.bfloat16)
                copies.append(hand(place, 4 + index, sums.at[place, index], target))
            second_copies.append(copies)
        far_copies = []
        for place, target in enumerate(order):
            copies = first_copies[place][2:] + second_copies[place]
            for copy in copies:
                copy.wait_recv()

            def joined(index):
                return mid_in[place, index].astype(jnp.float32)

            halves = [joined(2) + joined(4), joined(3) + joined(5)]
            total = mid[place, part].astype(jnp.float32) + jnp.concatenate(halves, axis=0)
            if place < groups - 1:
                far[place] = total.astype(jnp.bfloat16)
                far_copies.append(
                    send(
                        far.at[place],
                        far_in.at[place],
                        far_send.at[place],
                        far_recv.at[place],
                        {"dp": target},
                    )
                )
        if line:
            line.steps()
        for place, copy in enumerate(far_copies):
            copy.wait_recv()
            total = total + far_in[place].astype(jnp.float32)
        if tail:
            results = function(total, *extra_refs)
            for ref, value in zip(out_refs, results):
                ref[...] = value
            full[part] = results[len(outs)].astype(jnp.bfloat16)
            last_copies = [
                send(
                    full.at[part],
                    full.at[part],
                    tail_sems[0].at[step],
                    tail_sems[1].at[step],
                    {"tensor": peer},
                )
                for step, peer in enumerate(parts)
            ]
            for copy in last_copies:
                copy.wait()
        else:
            out_refs[0][...] = total
        for copy in near_copies + far_copies + [
            copy for row in first_copies + second_copies for copy in row
        ]:
            copy.wait_send()
        if line:
            line.end()

    block = (count, D)
    dma = pltpu.SemaphoreType.DMA
    results = [jax.ShapeDtypeStruct(*out) for out in outs]
    if tail:
        results.append(jax.ShapeDtypeStruct((tensors,) + block, jnp.bfloat16))
    else:
        results.append(jax.ShapeDtypeStruct(block, jnp.float32))
    return pl.pallas_call(
        kernel,
        name="reduce_all",
        out_shape=results + ([line.out_shape] if line else []),
        in_specs=[pl.BlockSpec(memory_space=pl.ANY)] + (line.in_specs if line else []) + extra_specs,
        out_specs=[VMEM_SPEC] * len(results) + ([line.out_spec] if line else []),
        scratch_shapes=[dma((tensors - 1,))] * (2 if tail else 0)
        + [pltpu.VMEM((groups, tensors) + block, jnp.bfloat16)] * 3
        + [
            pltpu.VMEM((groups, 2, half, D), jnp.bfloat16),
            pltpu.VMEM((groups, 6, half, D), jnp.bfloat16),
            pltpu.VMEM((groups,) + block, jnp.bfloat16),
            pltpu.VMEM((groups,) + block, jnp.bfloat16),
            dma((groups,)),
            dma((groups,)),
            dma((groups,)),
            dma((groups, 6)),
            dma((groups, 6)),
            dma((groups,)),
            dma((groups,)),
        ]
        + (line.scratch if line else []),
        cost_estimate=SHORT,
        compiler_params=pltpu.CompilerParams(
            collective_id=collective_id, has_side_effects=True, vmem_limit_bytes=56 << 20
        ),
    )(terms, *(line.operands if line else []), *extras)


def gather_all(block, collective_id, line=None):
    tensors, groups = lax.axis_size("tensor"), lax.axis_size("dp")
    half = block.shape[0] // 2

    def kernel(*refs):
        refs = list(refs)
        block_ref = refs.pop(0)
        source_refs = [refs.pop(0) for _ in line.operands] if line else []
        out = refs.pop(0)
        summed_ref = refs.pop(0) if line else None
        own_sem, far_send, far_recv, mid_send, mid_recv, near_send, near_recv = refs[:7]
        if line:
            line.bind(source_refs, summed_ref, refs[7:])
            line.load()
        group, part, side = lax.axis_index("dp"), lax.axis_index("tensor"), lax.axis_index("seq")
        twin = 1 - side
        meet(
            [{"seq": twin}]
            + [{"tensor": peer} for peer in others("tensor")]
            + [{"dp": peer} for peer in others("dp")]
        )
        far_copies = [
            send(
                block_ref,
                out.at[side, part, group],
                far_send.at[step],
                far_recv.at[step],
                {"dp": peer},
            )
            for step, peer in enumerate(others("dp"))
        ]
        own = pltpu.make_async_copy(block_ref, out.at[side, part, group], own_sem)
        own.start()
        if line:
            line.begin()
        beside = lax.rem(part + 1, 2) + part - lax.rem(part, 2)
        across = lax.rem(part + 2, 4)
        corner = 3 - part
        upper, lower = pl.ds(0, half), pl.ds(half, half)
        first_copies, second_copies, near_copies = [], [], []
        for place in range(groups):
            source = behind("dp", place)
            if place:
                far_copies[place - 1].wait_recv()
            held = out.at[side, part, source] if place else block_ref

            def hand(index, piece, slot, rows, target):
                return send(
                    piece,
                    out.at[side, slot, source, rows],
                    mid_send.at[place, index],
                    mid_recv.at[place, index],
                    {"tensor": target},
                )

            first = [
                hand(0, held.at[upper], part, upper, beside),
                hand(1, held.at[lower], part, lower, across),
                hand(2, held.at[lower], part, lower, beside),
                hand(3, held.at[upper], part, upper, across),
            ]
            near_copies.append(
                send(
                    held,
                    out.at[side, part, source],
                    near_send.at[place, 0],
                    near_recv.at[place, 0],
                    {"seq": twin},
                )
            )
            first[0].wait_recv()
            second = [hand(4, out.at[side, beside, source, upper], beside, upper, across)]
            first[1].wait_recv()
            second.append(hand(5, out.at[side, across, source, lower], across, lower, beside))
            first_copies.append(first)
            second_copies.append(second)
        for place in range(groups):
            if line and place < 4:
                line.steps(2)
            source = behind("dp", place)
            ready = [
                (beside, first_copies[place][2:3]),
                (across, first_copies[place][3:4]),
                (corner, second_copies[place]),
            ]
            for step, (slot, copies) in enumerate(ready):
                for copy in copies:
                    copy.wait_recv()
                held = out.at[side, slot, source]
                near_copies.append(
                    send(
                        held,
                        held,
                        near_send.at[place, step + 1],
                        near_recv.at[place, step + 1],
                        {"seq": twin},
                    )
                )
        if line:
            line.steps()
        for copy in near_copies:
            copy.wait_recv()
        for copy in near_copies + far_copies + [
            copy for row in first_copies + second_copies for copy in row
        ]:
            copy.wait_send()
        own.wait()
        if line:
            line.end()

    dma = pltpu.SemaphoreType.DMA
    anywhere = pl.BlockSpec(memory_space=pl.ANY)
    return pl.pallas_call(
        kernel,
        name="gather_all",
        out_shape=[jax.ShapeDtypeStruct((2, tensors, groups) + block.shape, block.dtype)]
        + ([line.out_shape] if line else []),
        in_specs=[VMEM_SPEC] + (line.in_specs if line else []),
        out_specs=[pl.BlockSpec(memory_space=pltpu.HBM)] + ([line.out_spec] if line else []),
        scratch_shapes=[
            dma,
            dma((groups - 1,)),
            dma((groups - 1,)),
            dma((groups, 6)),
            dma((groups, 6)),
            dma((groups, tensors)),
            dma((groups, tensors)),
        ]
        + (line.scratch if line else []),
        cost_estimate=SHORT,
        compiler_params=pltpu.CompilerParams(
            collective_id=collective_id, has_side_effects=True, vmem_limit_bytes=60 << 20
        ),
    )(block, *(line.operands if line else []))


def reduce_rows(name, terms, ids, line, function, extras, scalars, outs):
    count, groups = terms.shape[3], terms.shape[2]
    pieces = max(1, groups // 4)
    if pieces == 1:
        return reduce_all(terms, ids[0], line, (function, extras, scalars, outs))
    part = count // pieces
    sums, joined = [], []
    for i in range(pieces):
        piece = terms[:, :, :, i * part : (i + 1) * part]
        total, *joined_now = reduce_all(piece, ids[1 if i and line else 0], None if i else line)
        sums.append(total)
        joined += joined_now
    total = jnp.concatenate(sums, axis=0)
    results = tensor_step(
        name,
        lambda _, total_ref, *refs: function(total_ref, *refs),
        None,
        [total] + list(extras),
        scalars,
        outs,
        True,
        ids[2],
    )
    return list(results) + joined


def plane_steps(tensors):
    return [(step, turn_by) for step in range(tensors) for turn_by in range(2)][1:]


def plane_peers(steps):
    count, part = lax.axis_size("tensor"), lax.axis_index("tensor")
    side = lax.axis_index("seq")
    return [
        (lax.rem(part + step, count), lax.rem(side + turn_by, 2)) for step, turn_by in steps
    ]


def join_stats(stats, collective_id):
    _, tensors, groups, _, _ = stats.shape

    def join(left, right):
        top = jnp.maximum(left[..., 0:1, :], right[..., 0:1, :])
        total = left[..., 1:2, :] * jnp.exp(left[..., 0:1, :] - top) + right[..., 1:2, :] * jnp.exp(
            right[..., 0:1, :] - top
        )
        return jnp.concatenate(
            [top, total, left[..., 2:3, :] + right[..., 2:3, :], left[..., 3:, :]], axis=-2
        )

    plane = plane_steps(tensors)

    def kernel(
        stats_ref, home, full, mid_in, far, far_in, mid_send, mid_recv, far_send, far_recv
    ):
        group, part, side = lax.axis_index("dp"), lax.axis_index("tensor"), lax.axis_index("seq")
        peers, groups_else = plane_peers(plane), others("dp")
        meet(
            [{"tensor": peer, "seq": other} for peer, other in peers]
            + [{"dp": peer} for peer in groups_else]
        )
        copies = [
            send(
                stats_ref.at[other, peer],
                mid_in.at[step],
                mid_send.at[0, step],
                mid_recv.at[0, step],
                {"tensor": peer, "seq": other},
            )
            for step, (peer, other) in enumerate(peers)
        ]
        for copy in copies:
            copy.wait()
        for spot in range(groups):
            total = stats_ref[side, part, spot]
            for step in range(len(plane)):
                total = join(total, mid_in[step, spot])
            far[spot] = total
        copies = [
            send(far.at[peer], far_in.at[step], far_send.at[0, step], far_recv.at[0, step], {"dp": peer})
            for step, peer in enumerate(groups_else)
        ]
        total = far[group]
        for step, copy in enumerate(copies):
            copy.wait()
            total = join(total, far_in[step])
        log_total = total[0:1] + jnp.log(total[1:2])
        home[...] = jnp.concatenate([log_total, total[2:3], total[2:]], axis=0)
        full[side, part, group] = jnp.broadcast_to(log_total, (8, LANES))
        held = full.at[side, part, group]
        copies = [
            send(held, held, far_send.at[1, step], far_recv.at[1, step], {"dp": peer})
            for step, peer in enumerate(groups_else)
        ]
        for copy in copies:
            copy.wait()
        held = full.at[side, part]
        copies = [
            send(
                held,
                held,
                mid_send.at[1, step],
                mid_recv.at[1, step],
                {"tensor": peer, "seq": other},
            )
            for step, (peer, other) in enumerate(peers)
        ]
        for copy in copies:
            copy.wait()

    tile = (8, LANES)
    dma = pltpu.SemaphoreType.DMA
    vmem = pl.BlockSpec(memory_space=pltpu.VMEM)
    return pl.pallas_call(
        kernel,
        name="join_stats",
        out_shape=[
            jax.ShapeDtypeStruct(tile, jnp.float32),
            jax.ShapeDtypeStruct(stats.shape, jnp.float32),
        ],
        in_specs=[vmem],
        out_specs=[vmem, vmem],
        scratch_shapes=[
            pltpu.VMEM((len(plane), groups) + tile, jnp.float32),
            pltpu.VMEM((groups,) + tile, jnp.float32),
            pltpu.VMEM((groups - 1,) + tile, jnp.float32),
            dma((2, len(plane))),
            dma((2, len(plane))),
            dma((2, groups - 1)),
            dma((2, groups - 1)),
        ],
        cost_estimate=SHORT,
        compiler_params=pltpu.CompilerParams(collective_id=collective_id, has_side_effects=True),
    )(stats)


def spread_tokens(block, slot_block, ends, blocks, half_rows, collective_id):
    tensors, groups = lax.axis_size("tensor"), lax.axis_size("dp")
    rows = 2 * tensors * groups
    width = ends.shape[1]
    vocab_rows = VOCAB // tensors
    slots = slot_block.shape[0]

    def kernel(
        block_ref, slot_ref, ends_ref, ids, targets, kept, places, plan, count,
        held, firsts, own_sem, send_sems, recv_sems,
    ):
        group, side = lax.axis_index("dp"), lax.axis_index("seq")
        first_id = lax.axis_index("tensor") * vocab_rows
        peers = [
            {"dp": lax.rem(group + step // 2, groups), "seq": lax.rem(side + step % 2, 2)}
            for step in range(1, 2 * groups)
        ]
        meet(peers)
        copies = [
            send(block_ref, held.at[group, side], send_sems.at[step], recv_sems.at[step], peer)
            for step, peer in enumerate(peers)
        ]
        own = pltpu.make_async_copy(block_ref, held.at[group, side], own_sem)
        own.start()
        own.wait()
        for copy in copies:
            copy.wait()
        lane = lax.broadcasted_iota(jnp.int32, (1, LANES), 1)
        slot_ids = lax.broadcasted_iota(jnp.int32, (slots, LANES), 0)
        slot_blocks = jnp.broadcast_to(slot_ref[...], (slots, LANES))
        total = jnp.zeros((1, LANES), jnp.int32)
        hits = jnp.zeros((1, LANES), jnp.float32)
        for half in range(2):
            for source in range(groups):
                limit = held[source, half, 2 * tensors : 2 * tensors + 1, :]
                total = total + limit
                for part in range(tensors):
                    row = (half * tensors + part) * groups + source
                    token = held[source, half, part : part + 1, :]
                    ids[row] = token
                    targets[row] = held[source, half, tensors + part : tensors + part + 1, :]
                    kept[row] = jnp.where(lane + part * LANES < limit, 1.0, 0.0)
                    firsts[row : row + 1, :] = jnp.where(part * LANES < limit, 1.0, 0.0)
                    local = token - first_id
                    inside = (local >= 0) & (local < vocab_rows)
                    local = jnp.where(inside, local, 0).astype(jnp.float32)
                    block_of = jnp.floor((local + 0.5) * (0.5 / half_rows))
                    within = local - block_of * (2.0 * half_rows)
                    lower = within >= half_rows
                    inside = inside & (jnp.where(lower, 1, 0) == side)
                    within = (within - jnp.where(lower, 1.0 * half_rows, 0.0)).astype(jnp.int32)
                    same = slot_blocks == block_of.astype(jnp.int32) + blocks
                    slot = jnp.sum(jnp.where(same, slot_ids + 1, 0), axis=0, keepdims=True) - 1
                    inside = inside & (slot >= 0)
                    places[row] = jnp.where(inside, slot * half_rows + within, -1)
                    hits = hits + jnp.where(inside, 1.0, 0.0)
        count[...] = total.astype(jnp.float32)
        shape = (rows, width)
        active = jnp.concatenate([firsts[...]] * (width // LANES), axis=1)
        square = (rows, rows)
        above = jnp.where(
            lax.broadcasted_iota(jnp.int32, square, 1) < lax.broadcasted_iota(jnp.int32, square, 0),
            1.0,
            0.0,
        )
        earlier = times(above.astype(jnp.bfloat16), active.astype(jnp.bfloat16))
        number = jnp.sum(active, axis=0, keepdims=True)
        index = lax.broadcasted_iota(jnp.int32, shape, 0).astype(jnp.float32)
        turns = jnp.where(active > 0.0, earlier, number + index - earlier)
        spot = lax.broadcasted_iota(jnp.int32, shape, 1).astype(jnp.float32) - PLAN_GROUPS
        order = jnp.sum(jnp.where(turns == spot, index, 0.0), axis=0, keepdims=True)
        spot = lax.broadcasted_iota(jnp.int32, (1, width), 1)
        order = jnp.where(spot == 2, number, order)
        order = jnp.where(spot == 3, jnp.sum(hits, axis=1, keepdims=True), order)
        plan[...] = jnp.where(spot < 2, ends_ref[...], order.astype(jnp.int32))

    dma = pltpu.SemaphoreType.DMA
    vmem = pl.BlockSpec(memory_space=pltpu.VMEM)
    shape = (rows, 1, LANES)
    return pl.pallas_call(
        kernel,
        name="spread_tokens",
        out_shape=[
            jax.ShapeDtypeStruct(shape, jnp.int32),
            jax.ShapeDtypeStruct(shape, jnp.int32),
            jax.ShapeDtypeStruct(shape, jnp.float32),
            jax.ShapeDtypeStruct(shape, jnp.int32),
            jax.ShapeDtypeStruct((1, width), jnp.int32),
            jax.ShapeDtypeStruct((1, LANES), jnp.float32),
        ],
        in_specs=[vmem] * 3,
        out_specs=[vmem] * 6,
        scratch_shapes=[
            pltpu.VMEM((groups, 2) + block.shape, jnp.int32),
            pltpu.VMEM((rows, LANES), jnp.float32),
            dma,
            dma((2 * groups - 1,)),
            dma((2 * groups - 1,)),
        ],
        cost_estimate=SHORT,
        compiler_params=pltpu.CompilerParams(collective_id=collective_id, has_side_effects=True),
    )(block, slot_block, ends)


def finish(gain_grads, states, grad_ys, home, keep, table_squares, count, smalls, collective_id):
    tensors, groups = lax.axis_size("tensor"), lax.axis_size("dp")
    block = (8, D)
    plane = plane_steps(tensors)
    gain_rows = 2 * LAYERS + 1
    operands = list(gain_grads) + list(states) + list(grad_ys) + [
        home, keep, table_squares, count
    ] + list(smalls)

    def kernel(*refs):
        refs = list(refs)
        gain_refs = [refs.pop(0) for _ in gain_grads]
        state_refs = [refs.pop(0) for _ in states]
        grad_refs = [refs.pop(0) for _ in grad_ys]
        home_ref, keep_ref, table_ref, count_ref = [refs.pop(0) for _ in range(4)]
        small_refs = [refs.pop(0) for _ in smalls]
        out_refs = [refs.pop(0) for _ in range(8)]
        mid, far, mid_send, mid_recv, far_send, far_recv = refs
        group, part, side = lax.axis_index("dp"), lax.axis_index("tensor"), lax.axis_index("seq")
        peers, groups_else = plane_peers(plane), others("dp")
        meet(
            [{"tensor": peer, "seq": other} for peer, other in peers]
            + [{"dp": peer} for peer in groups_else]
        )
        values = []
        for later in range(1, LAYERS + 1):
            grad = grad_refs[later - 1][...]
            for level in range(later + 1):
                values.append(jnp.sum(grad * state_refs[level][...], keepdims=True))
        loss = jnp.where(keep_ref[...] > 0.0, home_ref[0:1, :] - home_ref[1:2, :], 0.0)
        values.append(jnp.sum(loss, keepdims=True))
        values.append(jnp.sum(table_ref[...], keepdims=True))
        lane = lax.broadcasted_iota(jnp.int32, (1, D), 1)
        row = jnp.zeros((1, D), jnp.float32)
        for place, value in enumerate(values):
            row = jnp.where(lane == place, value, row)
        blank = jnp.zeros((8 - gain_rows - 1, D), jnp.float32)
        total = jnp.concatenate([ref[...] for ref in gain_refs] + [row, blank], axis=0)
        stages = [
            (
                mid,
                2 * part + side,
                [{"tensor": peer, "seq": other} for peer, other in peers],
                mid_send,
                mid_recv,
            ),
            (far, group, [{"dp": peer} for peer in groups_else], far_send, far_recv),
        ]
        for slots, me, targets, send_sems, recv_sems in stages:
            slots[me] = total
            copies = [
                send(slots.at[me], slots.at[me], send_sems.at[step], recv_sems.at[step], target)
                for step, target in enumerate(targets)
            ]
            for copy in copies:
                copy.wait()
            total = slots[0]
            for index in range(1, slots.shape[0]):
                total = total + slots[index]
        gain_total = total[:gain_rows]
        row = total[gain_rows : gain_rows + 1]

        def pick(place):
            return jnp.sum(jnp.where(lane == place, row, 0.0), axis=1, keepdims=True)

        mix_squares = jnp.sum(jnp.where(lane < MIX_WEIGHTS, row * row, 0.0), axis=1, keepdims=True)
        gain_squares = jnp.sum(gain_total * gain_total, keepdims=True)
        tokens = count_ref[:, 0:1]
        clip_norm = jnp.sqrt(pick(MIX_WEIGHTS + 1) + gain_squares + mix_squares) / tokens
        factor = jnp.minimum(1.0, CLIP_NORM / clip_norm) / tokens
        gain_news = adam_update(
            *[ref[...] for ref in small_refs[:3]], gain_total * factor, RATE_SMALL, 0.0
        )
        mix_news = adam_update(
            *[ref[...] for ref in small_refs[3:]], row[:, :MIX_WEIGHTS] * factor, RATE_SMALL, 0.0
        )
        for ref, value in zip(out_refs[:6], gain_news + mix_news):
            ref[...] = value
        ends = jnp.where(lane == 0, pick(MIX_WEIGHTS), jnp.where(lane == 1, clip_norm, factor))
        out_refs[6][...] = ends[:, :LANES]
        out_refs[7][...] = jnp.broadcast_to(factor, (8, LANES))

    dma = pltpu.SemaphoreType.DMA
    vmem = pl.BlockSpec(memory_space=pltpu.VMEM)
    return pl.pallas_call(
        kernel,
        name="finish",
        out_shape=[jax.ShapeDtypeStruct(value.shape, jnp.float32) for value in smalls]
        + [
            jax.ShapeDtypeStruct((1, LANES), jnp.float32),
            jax.ShapeDtypeStruct((8, LANES), jnp.float32),
        ],
        in_specs=[vmem] * len(operands),
        out_specs=[vmem] * 8,
        scratch_shapes=[
            pltpu.VMEM((2 * tensors,) + block, jnp.float32),
            pltpu.VMEM((groups,) + block, jnp.float32),
            dma((len(plane),)),
            dma((len(plane),)),
            dma((groups - 1,)),
            dma((groups - 1,)),
        ],
        cost_estimate=LONG,
        compiler_params=pltpu.CompilerParams(
            collective_id=collective_id, has_side_effects=True, vmem_limit_bytes=8 << 20
        ),
    )(*operands)


SLOT_STEP = 8
PREPARE_STEP = 20


def prepare(slot_block, first_id, master, blocks):
    slots, half_rows, _ = master.shape
    total = slot_block.shape[0]
    steps = -(-total // PREPARE_STEP)
    spare = steps * PREPARE_STEP - total
    slot_block = jnp.pad(slot_block, (0, spare), constant_values=-1)
    slot_block = jnp.concatenate([slot_block, first_id[None]])
    rows = PREPARE_STEP * half_rows

    def kernel(plan_ref, master_ref, table_ref, halves_ref, ids_ref):
        @pl.when(pl.program_id(0) == 0)
        def _():
            halves_ref[...] = jnp.zeros_like(halves_ref)

        for place in range(PREPARE_STEP):
            slot = pl.program_id(0) * PREPARE_STEP + place
            value = jnp.where(slot < slots, master_ref[place], 0.0).astype(jnp.bfloat16)
            table_ref[place * half_rows : (place + 1) * half_rows, :] = value

            block = plan_ref[slot]
            ids = plan_ref[steps * PREPARE_STEP] + (block - blocks) * (2 * half_rows)
            ids = ids + lax.broadcasted_iota(jnp.int32, (half_rows, 1), 0)
            ids_ref[place * half_rows : (place + 1) * half_rows, :] = jnp.where(
                block >= blocks, ids, -1
            )

            @pl.when((block >= 0) & (block < blocks))
            def _():
                halves_ref[block] = value

    last = (slots - 1) // PREPARE_STEP
    return pl.pallas_call(
        kernel,
        name="prepare",
        grid_spec=pltpu.PrefetchScalarGridSpec(
            num_scalar_prefetch=1,
            grid=(steps,),
            in_specs=[
                pl.BlockSpec(
                    (PREPARE_STEP, half_rows, D), lambda step, plan: (jnp.minimum(step, last), 0, 0)
                )
            ],
            out_specs=[
                pl.BlockSpec((rows, D), lambda step, plan: (step, 0)),
                pl.BlockSpec((blocks, half_rows, D), lambda step, plan: (0, 0, 0)),
                pl.BlockSpec((rows, 1), lambda step, plan: (step, 0)),
            ],
        ),
        out_shape=[
            jax.ShapeDtypeStruct((total * half_rows, D), jnp.bfloat16),
            jax.ShapeDtypeStruct((blocks, half_rows, D), jnp.bfloat16),
            jax.ShapeDtypeStruct((total * half_rows, 1), jnp.int32),
        ],
        cost_estimate=SHORT,
        compiler_params=pltpu.CompilerParams(vmem_limit_bytes=60 << 20),
    )(slot_block, master)


TILE = TILE_GROUPS * LANES
PICKED = 768


def row_of(values_ref, groups, place=0):
    rows = [values_ref[group, place : place + 1, :] for group in groups]
    return jnp.concatenate(rows, axis=1)


def tile_row(values_ref, tile):
    start = tile * TILE_GROUPS
    return row_of(values_ref, [start + place for place in range(TILE_GROUPS)])


PLAN_GROUPS = 4


def chunk_of(plan_ref, step):
    return pl.ds(pl.multiple_of(plan_ref[0] + step * ROW_STEP, 16), ROW_STEP)


def chunks_of(plan_ref):
    return (plan_ref[1] - plan_ref[0] + ROW_STEP - 1) // ROW_STEP


def whole(shape):
    return pl.BlockSpec(shape, lambda step, plan: (0,) * len(shape), pipeline_mode=pl.Buffered(1))


def last_tile(plan):
    return (plan[2] - 1) // TILE_GROUPS


def group_specs():
    return [
        pl.BlockSpec(
            (LANES, D),
            lambda step, plan, place=place: (
                plan[PLAN_GROUPS + jnp.minimum(step, last_tile(plan)) * TILE_GROUPS + place],
                0,
            ),
        )
        for place in range(TILE_GROUPS)
    ]


def powers_spec(rows):
    return pl.BlockSpec((rows, TILE), lambda step, plan: (0, jnp.minimum(step, last_tile(plan))))


def groups_of(plan_ref):
    start = PLAN_GROUPS + pl.program_id(0) * TILE_GROUPS
    return [plan_ref[start + place] for place in range(TILE_GROUPS)]


ROWS_SPEC = pl.BlockSpec((TILE, D), lambda step, plan: (step, 0))


def local_call(name, kernel, steps, plan, operands, in_specs, out_shape, out_specs, scratch):
    return pl.pallas_call(
        kernel,
        name=name,
        grid_spec=pltpu.PrefetchScalarGridSpec(
            num_scalar_prefetch=1,
            grid=(steps,),
            in_specs=in_specs,
            out_specs=out_specs,
            scratch_shapes=scratch,
        ),
        out_shape=out_shape,
        cost_estimate=SHORT,
        compiler_params=pltpu.CompilerParams(vmem_limit_bytes=60 << 20),
    )(plan, *operands)


def ones_where(condition):
    return jnp.where(condition, 1.0, 0.0).astype(jnp.bfloat16)


def picks(rank_row):
    return ones_where(lax.broadcasted_iota(jnp.int32, (PICKED, TILE), 0) == rank_row)


def rows_picked(plan_ref, step, place_row):
    start = plan_ref[0] + step * ROW_STEP
    row = lax.broadcasted_iota(jnp.int32, (ROW_STEP, PICKED), 0) + start
    return ones_where(row == place_row)


def look_up(plan, row_ids, tokens, places, table):
    rows, groups = table.shape[0], tokens.shape[0]
    steps = groups // TILE_GROUPS

    def kernel(
        plan_ref, ids_ref, tokens_ref, places_ref, table_ref, out_ref, ranks_ref, picked_ref, acc, picked
    ):
        tile = pl.program_id(0)
        few = plan_ref[3] <= PICKED

        @pl.when(tile == 0)
        def _():
            held = places_ref[...].reshape(groups, LANES) >= 0
            ones = ones_where(held)
            lane = (LANES, LANES)
            before = ones_where(
                lax.broadcasted_iota(jnp.int32, lane, 0) < lax.broadcasted_iota(jnp.int32, lane, 1)
            )
            group = (groups, groups)
            above = ones_where(
                lax.broadcasted_iota(jnp.int32, group, 1) < lax.broadcasted_iota(jnp.int32, group, 0)
            )
            totals = jnp.sum(ones.astype(jnp.float32), axis=1, keepdims=True)
            totals = jnp.broadcast_to(totals, (groups, LANES)).astype(jnp.bfloat16)
            ranks = (times(ones, before) + times(above, totals)).astype(jnp.int32)
            ranks_ref[...] = jnp.where(held, ranks, -1).reshape(groups, 1, LANES)

        @pl.when((tile == 0) & few)
        def _():
            def digits_of(step, total):
                place = tile_row(places_ref, step)
                high = lax.shift_right_arithmetic(place, 6)
                digits = jnp.concatenate([high, place - high * 64] * 4, axis=0)
                digits = digits.astype(jnp.float32).astype(jnp.bfloat16)
                return total + contract_last(digits, picks(tile_row(ranks_ref, step)))

            digits = lax.fori_loop(0, steps, digits_of, jnp.zeros((8, PICKED), jnp.float32))
            place = (digits[0:1] * 64.0 + digits[1:2]).astype(jnp.int32)
            index = lax.broadcasted_iota(jnp.int32, (1, PICKED), 1)
            place = jnp.where(index < plan_ref[3], place, -1)
            picked_ref[...] = jnp.broadcast_to(place, (8, PICKED))
            acc[:PICKED, :] = jnp.zeros((PICKED, D), jnp.float32)

            def one(step, carry):
                hits = rows_picked(plan_ref, step, place)
                acc[:PICKED, :] += contract_first(hits, table_ref[chunk_of(plan_ref, step), :])
                return carry

            lax.fori_loop(0, chunks_of(plan_ref), one, 0)
            picked[...] = acc[:PICKED, :].astype(jnp.bfloat16)

        @pl.when(few)
        def _():
            hits = picks(tile_row(ranks_ref, tile))
            out_ref[...] = contract_first(hits, picked[...]).astype(jnp.bfloat16)

        @pl.when(jnp.logical_not(few))
        def _():
            acc[...] = jnp.zeros_like(acc)
            wanted = tile_row(tokens_ref, tile)

            def one(step, carry):
                chunk = chunk_of(plan_ref, step)
                hits = ones_where(ids_ref[chunk, :] == wanted)
                acc[...] += contract_first(hits, table_ref[chunk, :])
                return carry

            lax.fori_loop(0, chunks_of(plan_ref), one, 0)
            out_ref[...] = acc[...].astype(jnp.bfloat16)

    lanes = (groups, 1, LANES)
    return local_call(
        "look_up",
        kernel,
        steps,
        plan,
        (row_ids, tokens, places, table),
        [whole((rows, 1)), whole(lanes), whole(lanes), whole((rows, D))],
        [
            jax.ShapeDtypeStruct((groups * LANES, D), jnp.bfloat16),
            jax.ShapeDtypeStruct(lanes, jnp.int32),
            jax.ShapeDtypeStruct((8, PICKED), jnp.int32),
        ],
        [ROWS_SPEC, whole(lanes), whole((8, PICKED))],
        [pltpu.VMEM((TILE, D), jnp.float32), pltpu.VMEM((PICKED, D), jnp.bfloat16)],
    )


def head_forward(plan, row_ids, labels, table, final):
    rows, groups = table.shape[0], labels.shape[0]
    steps = groups // TILE_GROUPS

    def kernel(plan_ref, ids_ref, labels_ref, table_ref, *rest):
        final_refs, (powers_ref, stats_ref, scores, hidden) = rest[:TILE_GROUPS], rest[TILE_GROUPS:]
        blank = jnp.zeros((1, TILE), jnp.float32)
        active = pl.program_id(0) <= last_tile(plan_ref)
        own = groups_of(plan_ref)

        def put(top, total, target):
            pad = jnp.zeros((5, LANES), jnp.float32)
            for place in range(TILE_GROUPS):
                lanes = slice(place * LANES, (place + 1) * LANES)
                stats_ref[own[place]] = jnp.concatenate(
                    [top[:, lanes], total[:, lanes], target[:, lanes], pad], axis=0
                )

        @pl.when(jnp.logical_not(active))
        def _():
            put(blank - 1e30, blank, blank)

        @pl.when(active)
        def _():
            wanted = row_of(labels_ref, own)
            for place, ref in enumerate(final_refs):
                hidden[place * LANES : (place + 1) * LANES, :] = ref[...]

            def first(step, carry):
                top, target = carry
                chunk = chunk_of(plan_ref, step)
                ids = ids_ref[chunk, :]
                raw = contract_last(table_ref[chunk, :], hidden[...])
                raw = jnp.where(ids >= 0, raw, -1e30)
                scores[chunk, :] = raw
                top = jnp.maximum(top, jnp.max(raw, axis=0, keepdims=True))
                target = target + jnp.sum(
                    jnp.where(ids == wanted, raw, 0.0), axis=0, keepdims=True
                )
                return (top, target)

            top, target = lax.fori_loop(0, chunks_of(plan_ref), first, (blank - 1e30, blank))

            def second(step, total):
                chunk = chunk_of(plan_ref, step)
                powers = jnp.exp(scores[chunk, :] - top)
                powers_ref[chunk, :] = powers.astype(jnp.bfloat16)
                return total + jnp.sum(powers, axis=0, keepdims=True)

            put(top, lax.fori_loop(0, chunks_of(plan_ref), second, blank), target)

    return local_call(
        "head_forward",
        kernel,
        steps,
        plan,
        (row_ids, labels, table) + (final,) * TILE_GROUPS,
        [whole((rows, 1)), whole((groups, 1, LANES)), whole((rows, D))] + group_specs(),
        [
            jax.ShapeDtypeStruct((rows, groups * LANES), jnp.bfloat16),
            jax.ShapeDtypeStruct((groups, 8, LANES), jnp.float32),
        ],
        [powers_spec(rows), whole((groups, 8, LANES))],
        [pltpu.VMEM((rows, TILE), jnp.float32), pltpu.VMEM((TILE, D), jnp.bfloat16)],
    )


def head_backward(plan, row_ids, labels, keep, stats, log_totals, table, final, powers):
    rows, groups = table.shape[0], labels.shape[0]
    steps = groups // TILE_GROUPS

    def kernel(plan_ref, ids_ref, labels_ref, keep_ref, stats_ref, logs_ref, table_ref, powers_ref, *rest):
        final_refs = rest[:TILE_GROUPS]
        grad_final_ref, grad_table_ref, acc, hidden, low, sems = rest[TILE_GROUPS:]
        tile = pl.program_id(0)
        slot = lax.rem(tile, 2)
        active = tile <= last_tile(plan_ref)

        def copies(step):
            start, side = PLAN_GROUPS + step * TILE_GROUPS, lax.rem(step, 2)
            return [
                pltpu.make_async_copy(
                    low.at[side, place],
                    grad_final_ref.at[plan_ref[start + place]],
                    sems.at[side, place],
                )
                for place in range(TILE_GROUPS)
            ]

        @pl.when(tile == 0)
        def _():
            grad_table_ref[...] = jnp.zeros_like(grad_table_ref)

        @pl.when(tile >= 2)
        def _():
            for copy in copies(tile - 2):
                copy.wait()

        acc[...] = jnp.zeros_like(acc)

        @pl.when(active)
        def _():
            own = groups_of(plan_ref)
            wanted, kept = row_of(labels_ref, own), row_of(keep_ref, own)
            tops = row_of(stats_ref, own)
            scale = jnp.exp(tops - row_of(logs_ref, own)) * kept
            for place, ref in enumerate(final_refs):
                hidden[place * LANES : (place + 1) * LANES, :] = ref[...]

            def one(step, carry):
                chunk = chunk_of(plan_ref, step)
                grads = powers_ref[chunk, :].astype(jnp.float32) * scale
                grads = grads - jnp.where(ids_ref[chunk, :] == wanted, kept, 0.0)
                grads = grads.astype(jnp.bfloat16)
                grad_table_ref[chunk, :] += times(grads, hidden[...])
                acc[...] += contract_first(grads, table_ref[chunk, :])
                return carry

            lax.fori_loop(0, chunks_of(plan_ref), one, 0)

        low[slot] = acc[...].astype(jnp.bfloat16).reshape(TILE_GROUPS, LANES, D)
        for copy in copies(tile):
            copy.start()

        @pl.when(tile == steps - 1)
        def _():
            for step in range(max(0, steps - 2), steps):
                for copy in copies(step):
                    copy.wait()

    lanes = (groups, 1, LANES)
    return local_call(
        "head_backward",
        kernel,
        steps,
        plan,
        (row_ids, labels, keep, stats, log_totals, table, powers) + (final,) * TILE_GROUPS,
        [
            whole((rows, 1)),
            whole(lanes),
            whole(lanes),
            whole((groups, 8, LANES)),
            whole((groups, 8, LANES)),
            whole((rows, D)),
            powers_spec(rows),
        ]
        + group_specs(),
        [
            jax.ShapeDtypeStruct((groups, LANES, D), jnp.bfloat16),
            jax.ShapeDtypeStruct((rows, D), jnp.float32),
        ],
        [pl.BlockSpec(memory_space=pl.ANY), whole((rows, D))],
        [
            pltpu.VMEM((TILE, D), jnp.float32),
            pltpu.VMEM((TILE, D), jnp.bfloat16),
            pltpu.VMEM((2, TILE_GROUPS, LANES, D), jnp.bfloat16),
            pltpu.SemaphoreType.DMA((2, TILE_GROUPS)),
        ],
    )


def look_back(
    plan, slot_plan, slots, row_ids, tokens, ranks, picked, grad_start, grad_table, layer_grads
):
    rows, groups = grad_table.shape[0], tokens.shape[0]
    steps = groups // TILE_GROUPS
    half_rows = layer_grads[0].shape[1]
    block = SLOT_STEP * half_rows
    kinds = len(layer_grads)

    def kernel(plan_ref, slot_ref, ids_ref, tokens_ref, ranks_ref, picked_ref, grad_ref, table_ref, *rest):
        layer_refs = rest[:kinds]
        slots_ref, squares_ref, acc, held, out_ref = rest[kinds:]
        step = pl.program_id(0)
        few = plan_ref[3] <= PICKED

        @pl.when(step == 0)
        def _():
            acc[...] = jnp.zeros_like(acc)
            squares_ref[...] = jnp.zeros_like(squares_ref)

        @pl.when((step < steps) & few)
        def _():
            acc[...] += times(picks(tile_row(ranks_ref, step)), grad_ref[...])

        @pl.when((step < steps) & jnp.logical_not(few))
        def _():
            held[step] = grad_ref[...]

        @pl.when(step >= steps)
        def _():
            start = (step - steps) * block

            @pl.when(few)
            def _():
                row = lax.broadcasted_iota(jnp.int32, (block, PICKED), 0) + start
                hits = ones_where(row == picked_ref[0:1, :])
                out_ref[...] = table_ref[...] + times(hits, acc[...].astype(jnp.bfloat16))

            @pl.when(jnp.logical_not(few))
            def _():
                out_ref[...] = table_ref[...]
                ids = ids_ref[pl.ds(pl.multiple_of(start, 16), block), :]

                def one(tile, carry):
                    hits = ones_where(ids == tile_row(tokens_ref, tile))
                    out_ref[...] += times(hits, held[tile])
                    return carry

                lax.fori_loop(0, steps, one, 0)

            for place in range(SLOT_STEP):
                slot = (step - steps) * SLOT_STEP + place
                kind = slot_ref[0, slot]
                part = slice(place * half_rows, (place + 1) * half_rows)

                for index in range(kinds):

                    @pl.when(kind == index)
                    def _():
                        layer = layer_refs[index][slot_ref[1 + index, slot]]
                        out_ref[part, :] = layer.astype(jnp.float32)

                @pl.when(kind < 0)
                def _():
                    out_ref[part, :] = jnp.zeros((half_rows, D), jnp.float32)

                slots_ref[place] = out_ref[part, :].astype(jnp.bfloat16)

            values = out_ref[...]
            squares_ref[...] += (values * values).reshape(block // 8, 8, D).sum(axis=0)

    def fixed(shape):
        return pl.BlockSpec(
            shape, lambda step, plan, slot: (0,) * len(shape), pipeline_mode=pl.Buffered(1)
        )

    lanes = (groups, 1, LANES)
    row_spec = pl.BlockSpec((block, D), lambda step, plan, slot: (jnp.maximum(step - steps, 0), 0))
    return pl.pallas_call(
        kernel,
        name="look_back",
        grid_spec=pltpu.PrefetchScalarGridSpec(
            num_scalar_prefetch=2,
            grid=(steps + -(-slots // SLOT_STEP),),
            in_specs=[
                fixed((rows, 1)),
                fixed(lanes),
                fixed(lanes),
                fixed((8, PICKED)),
                pl.BlockSpec((TILE, D), lambda step, plan, slot: (jnp.minimum(step, steps - 1), 0)),
                row_spec,
            ]
            + [fixed(grads.shape) for grads in layer_grads],
            out_specs=[
                pl.BlockSpec(
                    (SLOT_STEP, half_rows, D),
                    lambda step, plan, slot: (jnp.maximum(step - steps, 0), 0, 0),
                ),
                fixed((8, D)),
            ],
            scratch_shapes=[
                pltpu.VMEM((PICKED, D), jnp.float32),
                pltpu.VMEM((steps, TILE, D), jnp.bfloat16),
                pltpu.VMEM((block, D), jnp.float32),
            ],
        ),
        out_shape=[
            jax.ShapeDtypeStruct((slots, half_rows, D), jnp.bfloat16),
            jax.ShapeDtypeStruct((8, D), jnp.float32),
        ],
        cost_estimate=SHORT,
        compiler_params=pltpu.CompilerParams(vmem_limit_bytes=60 << 20),
    )(
        plan,
        slot_plan,
        row_ids,
        tokens,
        ranks,
        picked,
        grad_start,
        grad_table,
        *layer_grads,
    )


def grads_home(level):
    return [(2 * level, 0), (2 * level + 1, 0), (2 * level + 1, 1)]


def body(
    token_ids,
    labels,
    real_counts,
    owners,
    master,
    first_moment,
    second_moment,
    gains,
    gains_first,
    gains_second,
    mix,
    mix_first,
    mix_second,
):
    tensors = lax.axis_size("tensor")
    groups = lax.axis_size("dp")
    group = lax.axis_index("dp")
    tensor_part = lax.axis_index("tensor")
    seq_part = lax.axis_index("seq")
    slots, half_rows, _ = master.shape
    seq_count, half_len = token_ids.shape
    row_count = seq_count * half_len
    share = row_count // tensors
    head_rows = 3 * D // tensors
    out_rows = D // tensors
    unit_rows = FF // tensors
    layer_rows = head_rows + out_rows + 2 * unit_rows
    layer_blocks = layer_rows // (2 * half_rows)
    blocks = LAYERS * layer_blocks
    vocab_rows = VOCAB // tensors
    local_heads = HEADS // tensors

    slot_rank = slot_table(owners)
    block_ids = jnp.arange(owners.shape[0], dtype=jnp.int32)
    mine = owners == group
    match = (jnp.arange(slots)[:, None] == slot_rank[None, :]) & mine[None, :]
    slot_block = jnp.sum(jnp.where(match, block_ids[None, :] + 1, 0), axis=1) - 1
    spare = -(-ROW_STEP // half_rows)
    spare += -(slots + spare) % SLOT_STEP
    held = jnp.sum(jnp.where(mine, 1, 0)) * half_rows
    first_held = jnp.sum(jnp.where(mine & (block_ids < blocks), 1, 0)) * half_rows
    slot_block_all = jnp.pad(slot_block, (0, spare), constant_values=-1).astype(jnp.int32)
    third = layer_blocks // 3
    which, within = slot_block_all // third, slot_block_all % third
    homes = [home for level in range(LAYERS) for home in grads_home(level)]
    arrays = 1 + max(array for array, _ in homes)
    kind, index = jnp.full(which.shape, -1), jnp.zeros_like(which)
    for place, (array, part) in enumerate(homes):
        kind = jnp.where(which == place, array, kind)
        index = jnp.where(which == place, within + part * third, index)
    kind = jnp.where(slot_block_all >= blocks, arrays, jnp.where(slot_block_all < 0, -1, kind))
    slot_plan = jnp.stack(
        [kind] + [jnp.where(kind == array, index, 0) for array in range(arrays)]
    ).astype(jnp.int32)

    packed = jnp.concatenate(
        [
            token_ids.reshape(tensors, LANES),
            labels.reshape(tensors, LANES),
            jnp.broadcast_to(real_counts[:, None], (16 - 2 * tensors, LANES)),
        ],
        axis=0,
    )
    width = -(-(2 * tensors * groups + PLAN_GROUPS) // LANES) * LANES
    lane = jnp.arange(width)[None, :]
    ends = jnp.where(lane == 0, first_held, jnp.where(lane == 1, held, 0)).astype(jnp.int32)
    ids_all, labels_all, keep_all, places, plan, count = spread_tokens(
        packed, slot_block_all[:, None], ends, blocks, half_rows, 15
    )
    plan = plan.reshape(-1)
    order = (2, tensors, groups, share)

    first_id = (tensor_part * vocab_rows + seq_part * half_rows).astype(jnp.int32)
    table, halves, row_ids = prepare(slot_block_all, first_id, master, blocks)

    def weights_line(*starts):
        return Line([(halves, start * third, third) for start in starts], True)

    def as_table(joined):
        return joined.reshape(-1, D)

    positions = seq_part * half_len + jnp.arange(row_count) % half_len
    steps_half = jnp.arange(HEAD_DIM // 2).astype(jnp.float32)
    freqs = 10000.0 ** (-2.0 * steps_half / HEAD_DIM)
    angles = freqs[:, None] * positions.astype(jnp.float32)[None, :]
    cosine, sine = jnp.cos(angles), jnp.sin(angles)

    looked, ranks, picked = look_up(plan, row_ids, ids_all, places, table)
    looked = looked.reshape(order + (D,))
    gain = [gains[i : i + 1] for i in range(2 * LAYERS + 1)]
    piece = ((share, D), jnp.float32)

    def normed_of(total, gain_row):
        return (total[...], layer_norm_parts(total[...])[0] * gain_row[...])

    def inner_of(total, stream, gain_row):
        inner = stream + total
        return (inner, layer_norm_parts(inner)[0] * gain_row)

    def outcome_of(base, total, inner, gain_row, *rest):
        states, scalars = rest[:-1], rest[-1]
        outcome = inner + total
        stream = scalars[base + len(states)] * outcome
        for source, state in enumerate(states):
            stream = stream + scalars[base + source] * state
        return (outcome, stream, layer_norm_parts(stream)[0] * gain_row)

    start, normed, joined = reduce_rows(
        "normed", looked, (14, 18, 1), weights_line(0, 1), normed_of, [gain[0]], [], [piece]
    )
    table_one = as_table(joined)
    attention_table, up = table_one, (table_one, 1)
    tables = []
    states, streams, inners, kept_all = [start], [start], [], []
    for level in range(LAYERS):
        here, last = 3 * level, level == LAYERS - 1
        carried = [] if last else [here + 3]
        carried += [here + 1, here + 2] if level else [here + 2]
        inner, normed_two, queries, both, logs, attended, joined = tensor_step(
            f"inner_{level}",
            inner_of,
            attention_work(normed, attention_table, cosine, sine),
            (streams[level], gain[2 * level + 1]),
            (),
            [piece],
            True,
            2 if level == 0 else 15 + level,
            weights_line(*carried),
        )
        kept = (queries, both, logs, attended)
        joined = as_table(joined)
        down = (joined, len(carried) - 1)
        up = (joined, len(carried) - 2) if level else up
        tables.append((attention_table, up, down))
        attention_table = joined
        outcome, stream, normed_next, hidden, activated = tensor_step(
            f"outcome_{level}",
            partial(outcome_of, (level + 1) * (level + 2) // 2 - 1),
            unit_work(normed_two, up, down),
            [inner, gain[2 * level + 2]] + states,
            (mix,),
            [piece, piece] + ([((share, D), jnp.bfloat16)] if last else []),
            not last,
            3 + level,
        )
        inners.append(inner)
        kept_all.append((normed, kept, normed_two, (hidden, activated)))
        states.append(outcome)
        streams.append(stream)
        normed = normed_next

    final_all = gather_all(normed, 3 + LAYERS)[0].reshape(-1, D)
    powers, stats = head_forward(plan, row_ids, labels_all, table, final_all)
    home, log_totals = join_stats(
        stats.reshape((2, tensors, groups, 8, LANES)), 4 + LAYERS
    )
    grad_final, grad_table = head_backward(
        plan,
        row_ids,
        labels_all,
        keep_all,
        stats,
        log_totals.reshape(-1, 8, LANES),
        table,
        final_all,
        powers,
    )
    grad_final = grad_final.reshape(order + (D,))

    row = ((1, D), jnp.float32)

    def top_of(total, stream, gain_row, scalars):
        grad_top, grad_gain = norm_pull(total[...], gain_row[...], stream[...])
        grad_state = scalars[MIX_WEIGHTS - 1] * grad_top
        return (grad_top, grad_state, grad_gain, grad_state)

    def inner_back(total, grad_out, inner, gain_row):
        grad, grad_gain = norm_pull(total, gain_row, inner)
        grad = grad_out + grad
        return (grad, grad_gain, grad)

    def stream_back(block, total, grad_inner, stream, gain_row, *rest):
        grad_ys, scalars = rest[:-1], rest[-1]
        grad, grad_gain = norm_pull(total, gain_row, stream)
        grad = grad_inner + grad
        state = grad if block == 0 else scalars[block * (block + 1) // 2 - 1 + block] * grad
        for offset, grad_y in enumerate(grad_ys):
            later = block + 1 + offset
            state = state + scalars[later * (later + 1) // 2 - 1 + block] * grad_y
        return (grad, state, grad_gain, state)

    grad_ys = [None] * (LAYERS + 1)
    gain_grads = [None] * (2 * LAYERS + 1)
    layer_grads, attention_grads = [None] * (2 * LAYERS), None
    grad_ys[LAYERS], grad_state, gain_grads[2 * LAYERS], grad_branch = reduce_rows(
        "top_back",
        grad_final,
        (0, 0, 5 + LAYERS),
        None,
        top_of,
        [streams[LAYERS], gain[2 * LAYERS]],
        [mix],
        [piece, piece, row],
    )
    for level in reversed(range(LAYERS)):
        normed, kept, normed_two, unit_kept = kept_all[level]
        attention_table, up, down = tables[level]
        grad_inner, gain_grads[2 * level + 1], grad_attn, unit_grads, *summed = tensor_step(
            f"inner_back_{level}",
            inner_back,
            unit_back_work(grad_branch, normed_two, up, down, unit_kept, half_rows),
            (grad_state, inners[level], gain[2 * level + 1]),
            (),
            [piece, row],
            True,
            6 + LAYERS if level == 0 else 19 + level,
            None if attention_grads is None else Line([(attention_grads, 0, third)], False),
        )
        if summed:
            layer_grads[2 * (level + 1)] = summed[0]
        grad_ys[level], grad_state, gain_grads[2 * level], grad_branch, attention_grads, summed = (
            tensor_step(
                f"stream_back_{level}",
                partial(stream_back, level),
                attention_back_work(
                    grad_attn, normed, attention_table, kept, cosine, sine, half_rows
                ),
                [grad_inner, streams[level], gain[2 * level]] + grad_ys[level + 1 :],
                (mix,),
                [piece, piece, row] + ([] if level else [((share, D), jnp.bfloat16)]),
                level > 0,
                7 + LAYERS + level,
                Line([(unit_grads, 0, 2 * third)], False),
            )
        )
        layer_grads[2 * level + 1] = summed

    grad_start_all, layer_grads[0] = gather_all(
        grad_branch, 13, Line([(attention_grads, 0, third)], False)
    )
    grad_start_all = grad_start_all.reshape(-1, D)
    owned, table_squares = look_back(
        plan,
        slot_plan,
        slots,
        row_ids,
        ids_all,
        ranks,
        picked,
        grad_start_all,
        grad_table,
        layer_grads,
    )
    keep = jnp.where(
        tensor_part * share + jnp.arange(share) < real_counts[0], 1.0, 0.0
    ).astype(jnp.float32)
    news = finish(
        gain_grads,
        states,
        grad_ys[1:],
        home,
        keep[None],
        table_squares,
        count,
        (gains, gains_first, gains_second, mix[None], mix_first[None], mix_second[None]),
        7 + 2 * LAYERS,
    )
    new_gains, new_gains_first, new_gains_second = news[:3]
    new_mix, new_mix_first, new_mix_second = [value[0] for value in news[3:6]]
    loss_sum, clip_norm = news[6][0, 0], news[6][0, 1]
    token_count = count[0, 0]
    owned = owned.astype(jnp.float32) * news[7][0, 0]
    new_master, new_first, new_second = adam_update(
        master, first_moment, second_moment, owned, RATE_MATRIX, DECAY_MATRIX
    )
    return (
        new_master,
        new_first,
        new_second,
        new_gains,
        new_gains_first,
        new_gains_second,
        new_mix,
        new_mix_first,
        new_mix_second,
        loss_sum,
        token_count,
        clip_norm,
    )


def solution(mesh):
    return jax.shard_map(
        body,
        mesh=mesh,
        in_specs=(
            P("dp", "seq"),
            P("dp", "seq"),
            P(("dp", "seq")),
            P(),
            P("dp", ("tensor", "seq"), None),
            P("dp", ("tensor", "seq"), None),
            P("dp", ("tensor", "seq"), None),
            P(),
            P(),
            P(),
            P(),
            P(),
            P(),
        ),
        out_specs=(
            P("dp", ("tensor", "seq"), None),
            P("dp", ("tensor", "seq"), None),
            P("dp", ("tensor", "seq"), None),
            P(),
            P(),
            P(),
            P(),
            P(),
            P(),
            P(),
            P(),
            P(),
        ),
        check_vma=False,
    )
```
